32 devices in a mesh: clip: 32 (over z, y, x, core).
Axes of the slice: x: 2, y: 2, z: 4, core: 2. Of those that a mesh axis runs over, the one named last changes fastest.
Arguments:
- frames: bfloat16 [128, 14, 14, 1024], P('clip'), may hold values from -6 to 6
- w_reduce: bfloat16 [1024, 256], replicated, may hold values from -0.1875 to 0.1875
- w_spatial: bfloat16 [3, 3, 256, 256], replicated, may hold values from -0.125 to 0.125
- w_expand: bfloat16 [256, 1024], replicated, may hold values from -0.375 to 0.375
- gain_a: float32 [256], replicated, may hold values from 0.5 to 1.5
- bias_a: float32 [256], replicated, may hold values from -3 to 3
- gain_b: float32 [256], replicated, may hold values from 0.5 to 1.5
- bias_b: float32 [256], replicated, may hold values from -3 to 3
- gain_c: float32 [1024], replicated, may hold values from 0.5 to 1.5
- bias_c: float32 [1024], replicated, may hold values from -3 to 3
- clip_ids: int32 [128], P('clip'), may hold values from 0 to 31, as said below
- segment_ids: int32 [128], P('clip'), may hold values from 0 to 2
- slot_valid: int32 [128], P('clip'), may hold values from 0 to 1, as said below
- segment_weight: float32 [3], replicated, may hold values from 0.5 to 2
- loss_weight: float32 [1024], replicated, may hold values from -3600 to 3600
Outputs:
- grad_frames: bfloat16 [128, 14, 14, 1024], P('clip')
- grad_reduce: float32 [1024, 256], replicated
- grad_spatial: float32 [3, 3, 256, 256], replicated
- grad_expand: float32 [256, 1024], replicated
- grad_gain_a: float32 [256], replicated
- grad_bias_a: float32 [256], replicated
- grad_gain_b: float32 [256], replicated
- grad_bias_b: float32 [256], replicated
- grad_gain_c: float32 [1024], replicated
- grad_bias_c: float32 [1024], replicated
The draws below stay inside these ranges and needn't reach their ends.
Inputs may be any that keep to these rules, and one draw needn't show every extreme that they name: `clip_ids`: every clip has exactly 3 slots, one of each segment index, on the devices d, d + 1 and d + D/2 (mod D, where D is the number of devices along `clip` in the mesh's order) for some d; which segment sits on which of those devices varies by draw. Each device holds exactly 3 such slots and its other slots are padding. `slot_valid`: segment 0 of every clip is valid; padding slots are not.
All inputs are finite; a program needn't handle non-finite values.
Results may differ from the reference program's by a relative error of at most 0.007.
Values sent between devices are 32-bit elements; how exact they have to be, the bound alone decides.
A program may use at most 128 MiB of HBM per device.

```python
import math
import jax
import jax.numpy as jnp
from jax import lax

F = 1024
MID = 256
H = 14
W = 14
SEGMENTS = 3
CLIP_DEV = 1
SLOT_DEV = 4
SLOTS = 128
CLIPS = 32


def slot_layout(key):
    devices = SLOTS // SLOT_DEV
    label_key, offset_key, slot_key, kept_key = jax.random.split(key, 4)
    offset_choices = jnp.array([0, 1, devices // 2], jnp.int32)
    offsets = jax.random.permutation(offset_key, offset_choices).astype(jnp.int32)
    device_index = jnp.arange(devices, dtype=jnp.int32)
    segment_index = jnp.arange(SEGMENTS, dtype=jnp.int32)
    clip_group = (device_index[:, None] - offsets[None, :]) % devices
    within = jnp.arange(CLIP_DEV, dtype=jnp.int32)
    raw_clip = clip_group[:, :, None] + devices * within[None, None, :]
    labels = jax.random.permutation(label_key, CLIPS).astype(jnp.int32)
    clip_table = labels[raw_clip]
    segment_table = jnp.broadcast_to(segment_index[None, :, None], clip_table.shape)
    live_slots = SEGMENTS * CLIP_DEV
    pad_slots = SLOT_DEV - live_slots
    kept_mask = (jax.random.randint(kept_key, (devices, live_slots), 0, 4) > 0).astype(jnp.int32)
    segment_flat = segment_table.reshape(devices, live_slots)
    kept_mask = jnp.maximum(kept_mask, (segment_flat == 0).astype(jnp.int32))
    filler = jnp.zeros((devices, pad_slots), jnp.int32)
    clips_flat = jnp.concatenate([clip_table.reshape(devices, live_slots), filler], axis=1)
    segments_flat = jnp.concatenate([segment_flat, filler], axis=1)
    valid_flat = jnp.concatenate([kept_mask, filler], axis=1)
    slot_keys = jax.random.split(slot_key, devices)
    places = jax.vmap(lambda single: jax.random.permutation(single, SLOT_DEV))(slot_keys).astype(jnp.int32)
    clips_flat = jnp.take_along_axis(clips_flat, places, axis=1)
    segments_flat = jnp.take_along_axis(segments_flat, places, axis=1)
    valid_flat = jnp.take_along_axis(valid_flat, places, axis=1)
    return (clips_flat.reshape(-1).astype(jnp.int32), segments_flat.reshape(-1).astype(jnp.int32), valid_flat.reshape(-1).astype(jnp.int32))


def draw_clip_ids(key, part):
    return slot_layout(key)[0]


def draw_segment_ids(key, part):
    return slot_layout(key)[1]


def draw_slot_valid(key, part):
    return slot_layout(key)[2]


def levels(key, extent, cuts, low, high):
    level, own = 1.0, jax.random.fold_in(key, 6)
    for axis_at, shards_of in cuts:
        draws = jnp.exp(jax.random.uniform(jax.random.fold_in(own, axis_at), (shards_of,), jnp.float32, low / len(cuts), high / len(cuts)))
        level = level * jnp.repeat(draws, extent[axis_at] // shards_of).reshape([-1 if axis == axis_at else 1 for axis in range(len(extent))])
    return level


def scatter_about(own_key, shape, width, bound, shards=(), kind=jnp.bfloat16):
    factor_of = levels(own_key, shape, shards, -0.22, 0.18) if shards else 1.0
    values = jax.random.normal(own_key, shape, jnp.float32) * width * factor_of
    return jnp.minimum(jnp.maximum(values, -bound), bound).astype(kind)


def setup_inputs(seed: int = 0) -> dict:
    key_list = jax.random.split(jax.random.key(seed), 16)
    frames = scatter_about(key_list[0], (SLOTS, H, W, F), 1.0, 6.0, ((0, 32),))
    w_reduce = scatter_about(key_list[1], (F, MID), F ** -0.5, 0.1875)
    w_spatial = scatter_about(key_list[2], (3, 3, MID, MID), (9 * MID) ** -0.5, 0.125)
    w_expand = scatter_about(key_list[3], (MID, F), MID ** -0.5, 0.375)
    gain_a = jnp.clip(1.0 + 0.1 * jax.random.normal(key_list[4], (MID,), jnp.float32), 0.5, 1.5)
    bias_a = scatter_about(key_list[5], (MID,), 0.5, 3.0, (), jnp.float32)
    gain_b = jnp.clip(1.0 + 0.1 * jax.random.normal(key_list[6], (MID,), jnp.float32), 0.5, 1.5)
    bias_b = scatter_about(key_list[7], (MID,), 0.5, 3.0, (), jnp.float32)
    gain_c = jnp.clip(1.0 + 0.1 * jax.random.normal(key_list[8], (F,), jnp.float32), 0.5, 1.5)
    bias_c = scatter_about(key_list[9], (F,), 0.5, 3.0, (), jnp.float32)
    clip_ids = draw_clip_ids(jax.random.fold_in(key_list[15], 71), 0)
    segment_ids = draw_segment_ids(jax.random.fold_in(key_list[15], 71), 0)
    slot_valid = draw_slot_valid(jax.random.fold_in(key_list[15], 71), 0)
    segment_weight = jnp.clip(jnp.exp(jax.random.uniform(key_list[13], (SEGMENTS,), jnp.float32, math.log(0.5), math.log(2.0))), 0.5, 2.0)
    loss_weight = scatter_about(key_list[14], (F,), 600.0, 3600.0, (), jnp.float32)
    return dict(frames=frames, w_reduce=w_reduce, w_spatial=w_spatial, w_expand=w_expand, gain_a=gain_a, bias_a=bias_a, gain_b=gain_b, bias_b=bias_b, gain_c=gain_c, bias_c=bias_c, clip_ids=clip_ids, segment_ids=segment_ids, slot_valid=slot_valid, segment_weight=segment_weight, loss_weight=loss_weight)


EPS = 1e-05

@jax.custom_vjp
def low(v):
    return lax.optimization_barrier(v.astype(jnp.bfloat16)).astype(jnp.float32)

@jax.custom_vjp
def low_back(v):
    return v

def low_keep(v):
    return (low(v), None)

def low_pass(kept, grad):
    return (grad,)

def back_keep(v):
    return (v, None)

def back_low(kept, grad):
    return (low(grad),)
low.defvjp(low_keep, low_pass)
low_back.defvjp(back_keep, back_low)

def sigmoid_linear(value):
    return value * jax.nn.sigmoid(value)

def batch_norm(pre_norm, valid_pixel, total_count, gain, shift):
    centre = lax.optimization_barrier(jnp.sum(pre_norm * valid_pixel, axis=0)) / total_count
    centred = pre_norm - centre
    spread = lax.optimization_barrier(jnp.sum(valid_pixel * centred * centred, axis=0)) / total_count
    return centred * lax.rsqrt(spread + EPS) * gain + shift

def reference(frames, w_reduce, w_spatial, w_expand, gain_a, bias_a, gain_b, bias_b, gain_c, bias_c, clip_ids, segment_ids, slot_valid, segment_weight, loss_weight):
    highest = lax.Precision.HIGHEST
    valid_slot = slot_valid.astype(jnp.float32)
    valid_pixel = jnp.repeat(valid_slot, H * W)[:, None]
    total_count = jnp.sum(valid_slot) * (H * W)
    slot_w = valid_slot * segment_weight[segment_ids]
    onehot = (clip_ids[:, None] == jnp.arange(CLIPS, dtype=jnp.int32)[None, :]).astype(jnp.float32) * slot_w[:, None]
    weight_total = lax.optimization_barrier(jnp.sum(onehot, axis=0))

    def forward(frames_value, reduce_value, spatial_value, expand_value, gain_one, bias_one, gain_two, bias_two, gain_three, bias_three):
        pixel_rows = frames_value.reshape(-1, F)
        pre_one = low_back(jnp.dot(pixel_rows, reduce_value, precision=highest))
        hidden_one = low(sigmoid_linear(batch_norm(pre_one, valid_pixel, total_count, gain_one, bias_one)))
        pre_two = lax.conv_general_dilated(hidden_one.reshape(SLOTS, H, W, MID), spatial_value, (1, 1), 'SAME', dimension_numbers=('NHWC', 'HWIO', 'NHWC'), precision=highest)
        pre_two = low_back(pre_two.reshape(-1, MID))
        hidden_two = low(sigmoid_linear(batch_norm(pre_two, valid_pixel, total_count, gain_two, bias_two)))
        pre_three = low_back(jnp.dot(hidden_two, expand_value, precision=highest))
        summed = batch_norm(pre_three, valid_pixel, total_count, gain_three, bias_three) + pixel_rows
        pooled = low(lax.optimization_barrier(jnp.mean(sigmoid_linear(summed).reshape(SLOTS, H * W, F), axis=1)))
        clip_mean = jnp.dot(onehot.T, pooled, precision=highest) / weight_total[:, None]
        unit_mean = clip_mean * lax.rsqrt(lax.optimization_barrier(jnp.mean(clip_mean * clip_mean, axis=1, keepdims=True)) + EPS)
        return jnp.sum(unit_mean * loss_weight[None, :])
    inputs = (frames.astype(jnp.float32), w_reduce.astype(jnp.float32), w_spatial.astype(jnp.float32), w_expand.astype(jnp.float32), gain_a, bias_a, gain_b, bias_b, gain_c, bias_c)
    loss_value, pullback = jax.vjp(forward, *inputs)
    gradients = pullback(jnp.ones_like(loss_value))
    return (gradients[0].astype(jnp.bfloat16), gradients[1], gradients[2], gradients[3], gradients[4], gradients[5], gradients[6], gradients[7], gradients[8], gradients[9])
```

```python
import functools
from types import SimpleNamespace

import jax
import jax.numpy as jnp
from jax import lax
from jax.experimental import pallas as pl
from jax.experimental.pallas import tpu as pltpu
from jax.sharding import PartitionSpec as P

MESH = pl.DeviceIdType.MESH
EPS = 1e-05
F32 = jnp.float32
BF16 = jnp.bfloat16
SIDE = 16
ROWS = SIDE * SIDE
NN = (((1,), (0,)), ((), ()))
NT = (((1,), (1,)), ((), ()))
E, S0, S1, S2, R = range(5)


def dot(a, b, dims=NN):
    return lax.dot_general(a, b, dims, preferred_element_type=F32)


def wait_bytes(ref, sem):
    pltpu.make_async_copy(ref, ref, sem).wait()


def kernel(cfg, *refs):
    names, n, slots, height, width, feat, mid = cfg
    r = SimpleNamespace(**dict(zip(names, refs, strict=True)))
    live = slots - 1
    rows = live * ROWS
    area = height * width
    inner = 8
    outer = n // inner
    quad = min(4, outer)
    far = outer // quad
    me = lax.axis_index("clip")
    low, high = me % inner, me // inner

    def send(src, dst, ssem, rsem, device):
        copy = pltpu.make_async_remote_copy(
            src_ref=src, dst_ref=dst, send_sem=ssem, recv_sem=rsem, device_id=(device,), device_id_type=MESH
        )
        copy.start()

    low_peers = [me - low + (low + o) % inner for o in range(1, inner)]
    high_peers = [low + inner * ((high + o) % outer) for o in range(1, outer)]
    clip_peers = [(me + o) % n for o in (1, n - 1, n // 2, n // 2 - 1, n // 2 + 1)]
    barrier = pltpu.get_barrier_semaphore()
    for device in low_peers + high_peers + clip_peers:
        pl.semaphore_signal(barrier, inc=1, device_id=(device,), device_id_type=MESH)

    load = r.load_sem
    f_load = pltpu.make_async_copy(r.frames, r.f4, load.at[0])
    wr_load = pltpu.make_async_copy(r.w_reduce, r.wr, load.at[1])
    ws_load = pltpu.make_async_copy(r.w_spatial, r.ws, load.at[2])
    we_load = pltpu.make_async_copy(r.w_expand, r.we, load.at[3])
    f_load.start()
    wr_load.start()
    ws_load.start()
    we_load.start()
    wc = r.wc
    for i in range(3):
        for j in range(3):
            pltpu.make_async_copy(
                r.w_spatial.at[i, j], wc.at[i, :, pl.ds(j * mid, mid)], load.at[4]
            ).start()

    for ref in (r.fp, r.xp, r.g3, r.hb, r.gpc, r.gpa):
        ref[...] = jnp.zeros(ref.shape, ref.dtype)

    valid, clip, segment = r.slot_valid, r.clip_ids, r.segment_ids
    later, alive = [], 1
    for k in range(live):
        alive = alive * valid[k]
        later.append(1 - alive)

    def kept(values, k):
        return values[k] + later[k] * (values[k + 1] - values[k])

    v = [kept(valid, k).astype(F32) for k in range(live)]
    key = [kept(clip, k).astype(F32) for k in range(live)]
    weight = []
    for k in range(live):
        at = kept(segment, k).astype(F32)
        w0, w1, w2 = (r.segment_weight[q] for q in range(3))
        weight.append(
            v[k] * (w0 * ((1.0 - at) * (2.0 - at) * 0.5) + w1 * (at * (2.0 - at)) + w2 * (at * (at - 1.0) * 0.5))
        )
    n_own = (v[0] + v[1] + v[2]) * float(area)

    def block(k, y):
        return pl.multiple_of(k * ROWS + y * SIDE, SIDE)

    mask = lax.broadcasted_iota(jnp.int32, (SIDE, 256), 0) < width

    def fold(value):
        return jnp.sum(jnp.where(mask, value, 0.0), axis=0, keepdims=True)

    def to_dense(ref, at, row0, value, first):
        for q in range(value.shape[1] // 128):
            ref[at, pl.ds(row0 + first + q, 1), :] = value[:, q * 128 : (q + 1) * 128]

    def row_form(ref, row, dense):
        d = r.dense
        count = dense.shape[0]
        d[0:count, :] = dense
        for q in range(count):
            ref[row : row + 1, q * 128 : (q + 1) * 128] = d[q : q + 1, :]

    def dense_of(ref1):
        d = r.dense
        count = ref1.shape[0] // 128
        for q in range(count):
            d[q : q + 1, :] = ref1[q * 128 : (q + 1) * 128].reshape(1, 128)
        return d[0:count, :]

    def vector_out(ref1, dense):
        for q in range(dense.shape[0]):
            ref1[q * 128 : (q + 1) * 128] = dense[q : q + 1, :].reshape(128)

    near_s, near_r, wide_s, wide_r = r.near_s, r.near_r, r.wide_s, r.wide_r

    def near_send(at):
        buf = r.near[at]
        for o in range(1, inner):
            send(buf.at[low], buf.at[low], near_s.at[at], near_r.at[at], low_peers[o - 1])

    def near_wait(at):
        wait_bytes(r.near[at].at[pl.ds(0, inner - 1)], near_r.at[at])

    def wide_send(at):
        buf = r.wide[at]
        for o in range(1, outer):
            send(buf.at[high], buf.at[high], wide_s.at[at], wide_r.at[at], high_peers[o - 1])

    def wide_wait(at):
        wait_bytes(r.wide[at].at[pl.ds(0, outer - 1)], wide_r.at[at])

    def combine(kind, at, group, count):
        buf, counts = kind[at], kind[0]
        n_part = [counts[q, 4:5, :] for q in range(group)]
        s_part = [buf[q, 0:count, :] for q in range(group)]
        n_all = sum(n_part[1:], n_part[0])
        s_all = sum(s_part[1:], s_part[0])
        mean = s_all / jnp.maximum(n_all, 1.0)
        spread = jnp.zeros((count, 128), F32)
        for q in range(group):
            gap = s_part[q] / jnp.maximum(n_part[q], 1.0) - mean
            spread = spread + (buf[q, count : 2 * count, :] + n_part[q] * gap * gap)
        return n_all, s_all, mean, spread

    def stats_near(at, count):
        near_wait(at)
        n_all, s_all, _, spread = combine(r.near, at, inner, count)
        buf = r.wide[at]
        buf[high, 0:count, :] = s_all
        buf[high, count : 2 * count, :] = spread
        if at == 0:
            buf[high, 4:5, :] = n_all
        wide_send(at)

    def stats_wide(at, count, table):
        wide_wait(at)
        n_all, _, mean, spread = combine(r.wide, at, outer, count)
        row_form(table, 0, mean)
        inverse = lax.rsqrt(spread / n_all + EPS)
        row_form(table, 1, inverse)
        return n_all, inverse

    def total(kind, at, group):
        buf = kind[at]
        out = buf[0]
        for q in range(1, group):
            out = out + buf[q]
        return out

    def sums_near(at):
        near_wait(at)
        r.wide[at][high] = total(r.near, at, inner)
        wide_send(at)

    def sums_wide(at):
        wide_wait(at)
        return total(r.wide, at, outer)

    def local_stats(at, ref, channels):
        count = channels // 128
        buf = r.near[at]
        for c in range(channels // 256):
            lanes = slice(c * 256, (c + 1) * 256)
            acc = jnp.zeros((SIDE, 256), F32)
            for k in range(live):
                part = lax.fori_loop(
                    0, height, lambda y, a: a + ref[pl.ds(block(k, y), SIDE), lanes],
                    jnp.zeros((SIDE, 256), F32), unroll=height,
                )
                acc = acc + part * v[k]
            s_own = fold(acc)
            mean = s_own / jnp.maximum(n_own, 1.0)
            acc = jnp.zeros((SIDE, 256), F32)
            for k in range(live):
                def square(y, a):
                    gap = ref[pl.ds(block(k, y), SIDE), lanes] - mean
                    return a + gap * gap

                part = lax.fori_loop(0, height, square, jnp.zeros((SIDE, 256), F32), unroll=height)
                acc = acc + part * v[k]
            to_dense(buf, low, 0, s_own, 2 * c)
            to_dense(buf, low, count, fold(acc), 2 * c)
        if at == 0:
            buf[low, 4:5, :] = jnp.full((1, 128), n_own, F32)

    def norm_silu(ref, slope_ref, table, gain, bias, write):
        centre, inverse = table[0:1, :], table[1:2, :]
        g, b = gain[...].reshape(1, mid), bias[...].reshape(1, mid)
        for k in range(live):
            def step(y, carry):
                at = block(k, y)
                hat = (ref[pl.ds(at, SIDE), :] - centre) * inverse
                u = hat * g + b
                s = 0.5 * jnp.tanh(0.5 * u) + 0.5
                h = u * s
                ref[pl.ds(at, SIDE), :] = hat
                slope_ref[pl.ds(at, SIDE), :] = jnp.where(mask, s + (h - h * s), 0.0)
                write(at, jnp.where(mask, h, 0.0))
                return carry

            lax.fori_loop(0, height, step, 0, unroll=2)

    f_load.wait()
    fp, f4 = r.fp, r.f4
    for k in range(live):
        first, second = ((alive).astype(F32).astype(BF16) for alive in (1 - later[k], later[k]))

        def copy_row(y, carry):
            fp[pl.ds(block(k, y), width), :] = f4[k, y] * first + f4[k + 1, y] * second
            return carry

        lax.fori_loop(0, height, copy_row, 0, unroll=2)
    wr_load.wait()
    wr = r.wr
    hat_a, slope_a = r.hat_a, r.slope_a
    hat_a[...] = dot(fp[...], wr[...])
    local_stats(0, hat_a, mid)
    pl.semaphore_wait(barrier, len(low_peers + high_peers + clip_peers))
    near_send(0)
    r.ft[...] = fp[...].T
    stats_near(0, mid // 128)
    ws_load.wait()
    we_load.wait()
    wait_bytes(wc, load.at[4])
    ws, we = r.ws, r.we
    table_a, table_b, table_c = r.table_a, r.table_b, r.table_c
    n_all, inv_a = stats_wide(0, mid // 128, table_a)
    xp = r.xp

    def three(ref, at, left, middle, right):
        here = pl.ds(at + SIDE, SIDE)
        ref[here, 0:mid] = left.astype(BF16)
        ref[here, mid : 2 * mid] = middle.astype(BF16)
        ref[here, 2 * mid : 3 * mid] = right.astype(BF16)

    def write_a(at, h):
        three(xp, at, pltpu.roll(h, 1, 0), h, pltpu.roll(h, SIDE - 1, 0))

    norm_silu(hat_a, slope_a, table_a, r.gain_a, r.bias_a, write_a)

    hat_b, slope_b, hb = r.hat_b, r.slope_b, r.hb
    acc = None
    for i in range(3):
        part = dot(xp[i * SIDE : i * SIDE + rows, :], ws[i].reshape(3 * mid, mid))
        acc = part if acc is None else acc + part
    hat_b[...] = acc
    local_stats(1, hat_b, mid)
    near_send(1)
    xt = r.xt
    xt[...] = xp[SIDE : SIDE + rows, mid : 2 * mid].T
    stats_near(1, mid // 128)
    _, inv_b = stats_wide(1, mid // 128, table_b)

    def write_b(at, h):
        hb[pl.ds(at, SIDE), :] = h.astype(BF16)

    norm_silu(hat_b, slope_b, table_b, r.gain_b, r.bias_b, write_b)

    hat_c, slope_c = r.hat_c, r.slope_c
    hat_c[...] = dot(hb[...], we[...])
    local_stats(2, hat_c, feat)
    near_send(2)
    hbt = r.hbt
    hbt[...] = hb[...].T
    stats_near(2, feat // 128)
    _, inv_c = stats_wide(2, feat // 128, table_c)

    pool, slope_sum, slope_hat = r.pool, r.slope_sum, r.slope_hat
    for c in range(feat // 256):
        lanes = slice(c * 256, (c + 1) * 256)
        centre, inverse = table_c[0:1, lanes], table_c[1:2, lanes]
        g = r.gain_c[lanes].reshape(1, 256)
        b = r.bias_c[lanes].reshape(1, 256)
        for k in range(live):
            def step(y, carry):
                a0, a1, a2 = carry
                at = block(k, y)
                hat = (hat_c[pl.ds(at, SIDE), lanes] - centre) * inverse
                u = hat * g + b + fp[pl.ds(at, SIDE), lanes].astype(F32)
                s = 0.5 * jnp.tanh(0.5 * u) + 0.5
                h = u * s
                slope = s + (h - h * s)
                hat_c[pl.ds(at, SIDE), lanes] = hat
                slope_c[pl.ds(at, SIDE), lanes] = slope
                return a0 + h, a1 + slope, a2 + slope * hat

            zero = jnp.zeros((SIDE, 256), F32)
            a0, a1, a2 = lax.fori_loop(0, height, step, (zero, zero, zero), unroll=2)
            p_row = (fold(a0) * (1.0 / area)).astype(BF16).astype(F32)
            to_dense(pool, 0, 8 * k, p_row, 2 * c)
            to_dense(slope_sum, k, 0, fold(a1), 2 * c)
            to_dense(slope_hat, k, 0, fold(a2), 2 * c)
    for k in range(live):
        pool[0, 24 + k : 25 + k, :] = jnp.full((1, 128), key[k], F32)
        pool[0, 28 + k : 29 + k, :] = jnp.full((1, 128), weight[k], F32)
    for q, device in enumerate(clip_peers):
        send(pool.at[0], pool.at[q + 1], r.pool_s.at[0], r.pool_r.at[0], device)
    wait_bytes(pool.at[pl.ds(1, len(clip_peers))], r.pool_r.at[0])

    lw = dense_of(r.loss_weight)
    grads = []
    for k in range(live):
        my_key = jnp.full((1, 128), key[k], F32)
        my_weight = jnp.full((1, 128), weight[k], F32)
        mean = jnp.zeros((8, 128), F32)
        den = jnp.zeros((1, 128), F32)
        for q in range(len(clip_peers) + 1):
            for m in range(live):
                match = jnp.where(pool[q, 24 + m : 25 + m, :] == my_key, pool[q, 28 + m : 29 + m, :], 0.0)
                den = den + match
                mean = mean + match * pool[q, 8 * m : 8 * m + 8, :]
        den = jnp.where(den == 0.0, 1.0, den)
        mean = mean / den
        power = jnp.sum(jnp.sum(mean * mean, axis=0, keepdims=True), axis=1, keepdims=True)
        scale = lax.rsqrt(power * (1.0 / feat) + EPS)
        unit = mean * scale
        along = jnp.sum(jnp.sum(unit * lw, axis=0, keepdims=True), axis=1, keepdims=True)
        mean_grad = scale * (lw - unit * (along * (1.0 / feat)))
        grads.append((my_weight / den) * mean_grad * (1.0 / area))

    near3 = r.near[3]
    shift = jnp.zeros((8, 128), F32)
    gain = jnp.zeros((8, 128), F32)
    for k in range(live):
        shift = shift + grads[k] * slope_sum[k]
        gain = gain + grads[k] * slope_hat[k]
    near3[low, 0:8, :] = shift
    near3[low, 8:16, :] = gain
    near_send(3)
    coef = r.coef
    scale_c = dense_of(r.gain_c) * inv_c
    for k in range(live):
        row_form(coef, k, grads[k])
        row_form(coef, 3 + k, grads[k] * scale_c)
    sums_near(3)
    both = sums_wide(3)
    vector_out(r.grad_bias_c, both[0:8])
    vector_out(r.grad_gain_c, both[8:16])
    row_form(coef, 6, both[0:8] * scale_c / n_all)
    row_form(coef, 7, both[8:16] * scale_c / n_all)
    gpc = r.gpc
    for k in range(live):
        for c in range(feat // 256):
            lanes = slice(c * 256, (c + 1) * 256)
            c0 = coef[3 + k : 4 + k, lanes]
            c1 = coef[6:7, lanes] * v[k]
            c2 = coef[7:8, lanes] * v[k]

            def step(y, carry):
                at = block(k, y)
                grad = slope_c[pl.ds(at, SIDE), lanes] * c0 - (c1 + hat_c[pl.ds(at, SIDE), lanes] * c2)
                gpc[pl.ds(at, SIDE), lanes] = grad.astype(BF16)
                return carry

            lax.fori_loop(0, height, step, 0, unroll=2)

    def back_sums(at, grad_ref, slope_ref, hat_ref):
        zero = jnp.zeros((SIDE, mid), F32)
        carry = (zero, zero)
        for k in range(live):
            def step(y, c):
                here = pl.ds(block(k, y), SIDE)
                grad = grad_ref[here, :] * slope_ref[here, :]
                grad_ref[here, :] = grad
                return c[0] + grad, c[1] + grad * hat_ref[here, :]

            carry = lax.fori_loop(0, height, step, carry, unroll=2)
        buf = r.near[at]
        to_dense(buf, low, 0, jnp.sum(carry[0], axis=0, keepdims=True), 0)
        to_dense(buf, low, 2, jnp.sum(carry[1], axis=0, keepdims=True), 0)

    def back_apply(at, table, gain_ref, inv, grad_ref, hat_ref, bias_out, gain_out, write):
        both = sums_wide(at)
        vector_out(bias_out, both[0:2])
        vector_out(gain_out, both[2:4])
        scale = dense_of(gain_ref) * inv
        row_form(table, 2, scale)
        row_form(table, 3, both[0:2] * scale / n_all)
        row_form(table, 4, both[2:4] * scale / n_all)
        for k in range(live):
            c0, c1, c2 = table[2:3, :], table[3:4, :] * v[k], table[4:5, :] * v[k]

            def step(y, carry):
                at_row = block(k, y)
                here = pl.ds(at_row, SIDE)
                write(at_row, grad_ref[here, :] * c0 - (c1 + hat_ref[here, :] * c2))
                return carry

            lax.fori_loop(0, height, step, 0, unroll=2)

    core, bit_x, bit_y, at_z = me % 2, (me // 2) % 2, (me // 4) % 2, (me // 8) % quad
    at_far = me // (8 * quad)
    bit1 = bit_x + core * (bit_y - bit_x)
    bit2 = bit_y + core * (bit_x - bit_y)
    sibling = me + 1 - 2 * core
    peer1 = me + (1 - 2 * bit1) * (2 + 2 * core)
    peer2 = me + (1 - 2 * bit2) * (4 - 2 * core)
    z_at = [(at_z + o) % quad for o in range(1, quad)]
    z_peer = [me + 8 * (q - at_z) for q in z_at]
    far_peer = [me + 8 * quad * ((at_far + o) % far - at_far) for o in range(1, far)]
    chunk_s, chunk_r, out_sem = r.chunk_s, r.chunk_r, r.out_sem
    waits = []

    def chunk(q, outs):
        part, whole = r.part[q], r.whole[q]
        size = part.shape[0]
        half, quarter, eighth, piece = size // 2, size // 4, size // 8, size // (8 * quad)
        m8 = lambda value: pl.multiple_of(value, 8)
        at_h = m8(core * half)
        at_q = m8(at_h + bit1 * quarter)
        at_e = m8(at_q + bit2 * eighth)
        at_p = m8(at_e + at_z * piece)

        def go(step, src, dst, device):
            send(src, dst, chunk_s.at[q, step], chunk_r.at[q, step], device)

        def finish(step, ref):
            wait_bytes(ref, chunk_r.at[q, step])
            waits.append((ref, chunk_s.at[q, step]))

        rb0, rb1, rb2, rb3 = r.rb0[q], r.rb1[q], r.rb2[q], r.rb3[q]
        go(0, part.at[pl.ds(m8((1 - core) * half), half)], rb0, sibling)
        yield
        finish(0, rb0)
        part[pl.ds(at_h, half), :] = part[pl.ds(at_h, half), :] + rb0[...]
        go(1, part.at[pl.ds(m8(at_h + (1 - bit1) * quarter), quarter)], rb1, peer1)
        yield
        finish(1, rb1)
        part[pl.ds(at_q, quarter), :] = part[pl.ds(at_q, quarter), :] + rb1[...]
        go(2, part.at[pl.ds(m8(at_q + (1 - bit2) * eighth), eighth)], rb2, peer2)
        yield
        finish(2, rb2)
        part[pl.ds(at_e, eighth), :] = part[pl.ds(at_e, eighth), :] + rb2[...]
        for o in range(quad - 1):
            go(3, part.at[pl.ds(m8(at_e + z_at[o] * piece), piece)], rb3.at[pl.ds(o * piece, piece)], z_peer[o])
        yield
        finish(3, rb3)
        own = part[pl.ds(at_p, piece), :]
        for o in range(quad - 1):
            own = own + rb3[o * piece : (o + 1) * piece, :]
        if far > 1:
            rb4 = r.rb4[q]
            rb4[at_far] = own
            for device in far_peer:
                go(8, rb4.at[at_far], rb4.at[at_far], device)
            yield
            finish(8, rb4.at[pl.ds(0, far - 1)])
            own = rb4[0]
            for o in range(1, far):
                own = own + rb4[o]
        whole[pl.ds(at_p, piece), :] = own
        for o in range(quad - 1):
            go(4, whole.at[pl.ds(at_p, piece)], whole.at[pl.ds(at_p, piece)], z_peer[o])
        yield
        finish(4, whole.at[pl.ds(0, (quad - 1) * piece)])
        go(5, whole.at[pl.ds(at_e, eighth)], whole.at[pl.ds(at_e, eighth)], peer2)
        yield
        finish(5, whole.at[pl.ds(0, eighth)])
        go(6, whole.at[pl.ds(at_q, quarter)], whole.at[pl.ds(at_q, quarter)], peer1)
        yield
        finish(6, whole.at[pl.ds(0, quarter)])
        go(7, whole.at[pl.ds(at_h, half)], whole.at[pl.ds(at_h, half)], sibling)
        yield
        finish(7, whole.at[pl.ds(0, half)])
        step = size // len(outs)
        for o, dst in enumerate(outs):
            pltpu.make_async_copy(whole.at[pl.ds(o * step, step)], dst, out_sem.at[q]).start()
        waits.append((whole, out_sem.at[q]))
        yield

    def lanes_of(ref, count):
        return [ref.at[:, pl.ds(128 * q, 128)] for q in range(count)]

    chunks = [chunk(E, lanes_of(r.grad_expand, feat // 128))]
    for i in range(3):
        outs = [
            r.grad_spatial.at[i, q // 2, :, pl.ds(128 * (q % 2), 128)] for q in range(3 * mid // 128)
        ]
        chunks.append(chunk(S0 + i, outs))
    chunks.append(chunk(R, lanes_of(r.grad_reduce, mid // 128)))

    def go_on(*which):
        for name in which:
            next(chunks[name], None)

    def spread_lanes(ref, value):
        height_of = value.shape[0]
        for q in range(value.shape[1] // 128):
            ref[q * height_of : (q + 1) * height_of, :] = value[:, q * 128 : (q + 1) * 128]

    grad_b, grad_a = r.grad_b, r.grad_a
    grad_b[...] = dot(gpc[...], we[...], NT)
    back_sums(4, grad_b, slope_b, hat_b)
    near_send(4)
    spread_lanes(r.part[E], dot(hbt[...], gpc[...]))
    go_on(E)
    sums_near(4)
    go_on(E)
    g3 = r.g3

    def write_gb(at, grad):
        grad = jnp.where(mask, grad, 0.0)
        three(g3, at, pltpu.roll(grad, SIDE - 1, 0), grad, pltpu.roll(grad, 1, 0))

    back_apply(4, table_b, r.gain_b, inv_b, grad_b, hat_b, r.grad_bias_b, r.grad_gain_b, write_gb)
    acc = None
    for i in range(3):
        part = dot(g3[(2 - i) * SIDE : (2 - i) * SIDE + rows, :], wc[i], NT)
        acc = part if acc is None else acc + part
    grad_a[...] = acc
    back_sums(5, grad_a, slope_a, hat_a)
    near_send(5)
    go_on(E)
    for i in range(3):
        spread_lanes(r.part[S0 + i], dot(xt[...], g3[(2 - i) * SIDE : (2 - i) * SIDE + rows, :]))
        go_on(S0 + i)
        if i == 0:
            sums_near(5)
    go_on(E, S0, S1)
    gpa = r.gpa

    def write_ga(at, grad):
        gpa[pl.ds(at, SIDE), :] = grad.astype(BF16)

    back_apply(5, table_a, r.gain_a, inv_a, grad_a, hat_a, r.grad_bias_a, r.grad_gain_a, write_ga)
    spread_lanes(r.part[R], dot(r.ft[...], gpa[...]))
    go_on(R)
    go_on(E, S0, S1, S2)

    hat_c[...] = dot(gpa[...], wr[...], NT)
    go_on(E, S0, S1, S2, R)
    gf = r.gf
    for s in range(slots):
        def step(y, carry):
            out = jnp.zeros((SIDE, feat), F32)
            for k, share in ((s, 1 - later[s] if s < live else 0), (s - 1, later[s - 1] if s else 0)):
                if 0 <= k < live:
                    at = block(k, y)
                    term = slope_c[pl.ds(at, SIDE), :] * coef[k : k + 1, :] + hat_c[pl.ds(at, SIDE), :]
                    out = out + term * share.astype(F32)
            gf[s, y] = out[0:width, :].astype(BF16)
            return carry

        lax.fori_loop(0, height, step, 0)
        pltpu.make_async_copy(gf.at[s], r.grad_frames.at[s], out_sem.at[5]).start()
        go_on(E, S0, S1, S2, R)
    waits.append((gf, out_sem.at[5]))

    for _ in range(12):
        go_on(E, S0, S1, S2, R)

    for at in range(6):
        wait_bytes(r.near[at].at[pl.ds(0, inner - 1)], near_s.at[at])
        wait_bytes(r.wide[at].at[pl.ds(0, outer - 1)], wide_s.at[at])
    wait_bytes(pool.at[pl.ds(1, len(clip_peers))], r.pool_s.at[0])
    for ref, sem in waits:
        wait_bytes(ref, sem)


def solution(mesh):
    n = mesh.shape["clip"]

    def shards(*args):
        slots, height, width, feat = args[0].shape
        mid = args[1].shape[1]
        live = slots - 1
        rows = live * ROWS
        outer = n // 8
        quad = min(4, outer)
        far = outer // quad
        any_spec = pl.BlockSpec(memory_space=pl.ANY)
        vmem = pl.BlockSpec(memory_space=pltpu.VMEM)
        smem = pl.BlockSpec(memory_space=pltpu.SMEM)
        dma = pltpu.SemaphoreType.DMA
        matrix, third = mid * feat // 128, 3 * mid * mid // 128
        sizes = [matrix, third, third, third, matrix]
        scratch = dict(
            f4=pltpu.VMEM((slots, height, width, feat), BF16),
            fp=pltpu.VMEM((rows, feat), BF16),
            ft=pltpu.VMEM((feat, rows), BF16),
            wr=pltpu.VMEM((feat, mid), BF16),
            ws=pltpu.VMEM((3, 3, mid, mid), BF16),
            wc=pltpu.VMEM((3, mid, 3 * mid), BF16),
            we=pltpu.VMEM((mid, feat), BF16),
            hat_a=pltpu.VMEM((rows, mid), F32),
            slope_a=pltpu.VMEM((rows, mid), F32),
            grad_a=pltpu.VMEM((rows, mid), F32),
            hat_b=pltpu.VMEM((rows, mid), F32),
            slope_b=pltpu.VMEM((rows, mid), F32),
            grad_b=pltpu.VMEM((rows, mid), F32),
            xp=pltpu.VMEM((rows + 2 * SIDE, 3 * mid), BF16),
            xt=pltpu.VMEM((mid, rows), BF16),
            hb=pltpu.VMEM((rows, mid), BF16),
            hbt=pltpu.VMEM((mid, rows), BF16),
            hat_c=pltpu.VMEM((rows, feat), F32),
            slope_c=pltpu.VMEM((rows, feat), F32),
            gpc=pltpu.VMEM((rows, feat), BF16),
            g3=pltpu.VMEM((rows + 2 * SIDE, 3 * mid), BF16),
            gpa=pltpu.VMEM((rows, mid), BF16),
            gf=pltpu.VMEM((slots, height, width, feat), BF16),
            table_a=pltpu.VMEM((8, mid), F32),
            table_b=pltpu.VMEM((8, mid), F32),
            table_c=pltpu.VMEM((8, feat), F32),
            coef=pltpu.VMEM((8, feat), F32),
            dense=pltpu.VMEM((8, 128), F32),
            pool=pltpu.VMEM((6, 32, 128), F32),
            slope_sum=pltpu.VMEM((live, 8, 128), F32),
            slope_hat=pltpu.VMEM((live, 8, 128), F32),
            near=[pltpu.VMEM((8, 16 if at in (2, 3) else 8, 128), F32) for at in range(6)],
            wide=[pltpu.VMEM((outer, 16 if at in (2, 3) else 8, 128), F32) for at in range(6)],
            part=[pltpu.VMEM((size, 128), F32) for size in sizes],
            whole=[pltpu.VMEM((size, 128), F32) for size in sizes],
            rb0=[pltpu.VMEM((size // 2, 128), F32) for size in sizes],
            rb1=[pltpu.VMEM((size // 4, 128), F32) for size in sizes],
            rb2=[pltpu.VMEM((size // 8, 128), F32) for size in sizes],
            rb3=[pltpu.VMEM(((quad - 1) * size // (8 * quad), 128), F32) for size in sizes],
            rb4=[pltpu.VMEM((far, size // (8 * quad), 128), F32) for size in sizes if far > 1],
            load_sem=dma((5,)),
            near_s=dma((6,)),
            near_r=dma((6,)),
            wide_s=dma((6,)),
            wide_r=dma((6,)),
            pool_s=dma((1,)),
            pool_r=dma((1,)),
            chunk_s=dma((5, 9)),
            chunk_r=dma((5, 9)),
            out_sem=dma((6,)),
        )
        ins = dict(
            frames=any_spec, w_reduce=any_spec, w_spatial=any_spec, w_expand=any_spec,
            gain_a=vmem, bias_a=vmem, gain_b=vmem, bias_b=vmem, gain_c=vmem, bias_c=vmem,
            clip_ids=smem, segment_ids=smem, slot_valid=smem, segment_weight=smem, loss_weight=vmem,
        )
        vector = jax.ShapeDtypeStruct((mid,), F32)
        wide_vector = jax.ShapeDtypeStruct((feat,), F32)
        outs = dict(
            grad_frames=jax.ShapeDtypeStruct(args[0].shape, BF16),
            grad_reduce=jax.ShapeDtypeStruct((feat, mid), F32),
            grad_spatial=jax.ShapeDtypeStruct((3, 3, mid, mid), F32),
            grad_expand=jax.ShapeDtypeStruct((mid, feat), F32),
            grad_gain_a=vector, grad_bias_a=vector, grad_gain_b=vector, grad_bias_b=vector,
            grad_gain_c=wide_vector, grad_bias_c=wide_vector,
        )
        names = (*ins, *outs, *scratch)
        return pl.pallas_call(
            functools.partial(kernel, (names, n, slots, height, width, feat, mid)),
            out_shape=list(outs.values()),
            in_specs=list(ins.values()),
            out_specs=[any_spec] * 4 + [vmem] * 6,
            scratch_shapes=list(scratch.values()),
            compiler_params=pltpu.CompilerParams(
                collective_id=0, has_side_effects=True, vmem_limit_bytes=60 * 1024 * 1024
            ),
            cost_estimate=pl.CostEstimate(flops=5_200_000_000, bytes_accessed=12_000_000, transcendentals=1_500_000),
        )(*args)

    split = P("clip")
    in_specs = (split,) + (P(),) * 9 + (split,) * 3 + (P(), P())
    out_specs = (split,) + (P(),) * 9
    return jax.shard_map(shards, mesh=mesh, in_specs=in_specs, out_specs=out_specs, check_vma=False)
```

```python
import functools
from types import SimpleNamespace

import jax
import jax.numpy as jnp
from jax import lax
from jax.experimental import pallas as pl
from jax.experimental.pallas import tpu as pltpu
from jax.sharding import PartitionSpec as P

MESH = pl.DeviceIdType.MESH
EPS = 1e-05
F32 = jnp.float32
BF16 = jnp.bfloat16
SIDE = 16
ROWS = SIDE * SIDE
NN = (((1,), (0,)), ((), ()))
NT = (((1,), (1,)), ((), ()))
E, S0, S1, S2, R = range(5)


def dot(a, b, dims=NN):
    return lax.dot_general(a, b, dims, preferred_element_type=F32)


def wait_bytes(ref, sem):
    pltpu.make_async_copy(ref, ref, sem).wait()


def kernel(cfg, *refs):
    names, arrays, n, slots, height, width, feat, mid = cfg
    r = SimpleNamespace(**dict(zip(names, refs[:arrays] + refs[arrays + 5 :], strict=True)), whole=refs[arrays : arrays + 5])
    live = slots - 1
    rows = live * ROWS
    area = height * width
    inner = 8
    outer = n // inner
    quad = min(4, outer)
    far = outer // quad
    me = lax.axis_index("clip")
    low, high = me % inner, me // inner

    def send(src, dst, ssem, rsem, device):
        copy = pltpu.make_async_remote_copy(
            src_ref=src, dst_ref=dst, send_sem=ssem, recv_sem=rsem, device_id=(device,), device_id_type=MESH
        )
        copy.start()

    low_peers = [me - low + (low + o) % inner for o in range(1, inner)]
    high_peers = [low + inner * ((high + o) % outer) for o in range(1, outer)]
    clip_peers = [(me + o) % n for o in (1, n - 1, n // 2, n // 2 - 1, n // 2 + 1)]
    barrier = pltpu.get_barrier_semaphore()
    for device in low_peers + high_peers + clip_peers:
        pl.semaphore_signal(barrier, inc=1, device_id=(device,), device_id_type=MESH)

    load = r.load_sem
    out = r.vectors
    f_load = pltpu.make_async_copy(r.frames, r.f4, load.at[0])
    wr_load = pltpu.make_async_copy(r.w_reduce, r.wr, load.at[1])
    ws_load = pltpu.make_async_copy(r.w_spatial, r.ws, load.at[2])
    we_load = pltpu.make_async_copy(r.w_expand, r.we, load.at[3])
    f_load.start()
    wr_load.start()
    ws_load.start()
    we_load.start()
    wc = r.wc
    for i in range(3):
        for j in range(3):
            pltpu.make_async_copy(
                r.w_spatial.at[i, j], wc.at[i, :, pl.ds(j * mid, mid)], load.at[4]
            ).start()

    for ref in (r.fp, r.xp, r.g3, r.hb, r.gpc, r.gpa):
        ref[...] = jnp.zeros(ref.shape, ref.dtype)

    valid, clip, segment = r.slot_valid, r.clip_ids, r.segment_ids
    later, alive = [], 1
    for k in range(live):
        alive = alive * valid[k]
        later.append(1 - alive)

    def kept(values, k):
        return values[k] + later[k] * (values[k + 1] - values[k])

    v = [kept(valid, k).astype(F32) for k in range(live)]
    key = [kept(clip, k).astype(F32) for k in range(live)]
    weight = []
    for k in range(live):
        at = kept(segment, k).astype(F32)
        w0, w1, w2 = (r.segment_weight[q] for q in range(3))
        weight.append(
            v[k] * (w0 * ((1.0 - at) * (2.0 - at) * 0.5) + w1 * (at * (2.0 - at)) + w2 * (at * (at - 1.0) * 0.5))
        )
    n_own = (v[0] + v[1] + v[2]) * float(area)

    def block(k, y):
        return pl.multiple_of(k * ROWS + y * SIDE, SIDE)

    mask = lax.broadcasted_iota(jnp.int32, (SIDE, 256), 0) < width

    def fold(value):
        return jnp.sum(jnp.where(mask, value, 0.0), axis=0, keepdims=True)

    def to_dense(ref, at, row0, value, first):
        for q in range(value.shape[1] // 128):
            ref[at, pl.ds(row0 + first + q, 1), :] = value[:, q * 128 : (q + 1) * 128]

    def row_form(ref, row, dense):
        d = r.dense
        count = dense.shape[0]
        d[0:count, :] = dense
        for q in range(count):
            ref[row : row + 1, q * 128 : (q + 1) * 128] = d[q : q + 1, :]

    def dense_of(ref1):
        d = r.dense
        count = ref1.shape[0] // 128
        for q in range(count):
            d[q : q + 1, :] = ref1[q * 128 : (q + 1) * 128].reshape(1, 128)
        return d[0:count, :]

    near_s, near_r, wide_s, wide_r = r.near_s, r.near_r, r.wide_s, r.wide_r

    def near_send(at):
        buf = r.near[at]
        for o in range(1, inner):
            send(buf.at[low], buf.at[low], near_s.at[at], near_r.at[at], low_peers[o - 1])

    def near_wait(at):
        wait_bytes(r.near[at].at[pl.ds(0, inner - 1)], near_r.at[at])

    def wide_send(at):
        buf = r.wide[at]
        for o in range(1, outer):
            send(buf.at[high], buf.at[high], wide_s.at[at], wide_r.at[at], high_peers[o - 1])

    def wide_wait(at):
        wait_bytes(r.wide[at].at[pl.ds(0, outer - 1)], wide_r.at[at])

    def combine(kind, at, group, count):
        buf, counts = kind[at], kind[0]
        n_part = [counts[q, 4:5, :] for q in range(group)]
        s_part = [buf[q, 0:count, :] for q in range(group)]
        n_all = sum(n_part[1:], n_part[0])
        s_all = sum(s_part[1:], s_part[0])
        mean = s_all / jnp.maximum(n_all, 1.0)
        spread = jnp.zeros((count, 128), F32)
        for q in range(group):
            gap = s_part[q] / jnp.maximum(n_part[q], 1.0) - mean
            spread = spread + (buf[q, count : 2 * count, :] + n_part[q] * gap * gap)
        return n_all, s_all, mean, spread

    def stats_near(at, count):
        near_wait(at)
        n_all, s_all, _, spread = combine(r.near, at, inner, count)
        buf = r.wide[at]
        buf[high, 0:count, :] = s_all
        buf[high, count : 2 * count, :] = spread
        if at == 0:
            buf[high, 4:5, :] = n_all
        wide_send(at)

    def stats_wide(at, count, table):
        wide_wait(at)
        n_all, _, mean, spread = combine(r.wide, at, outer, count)
        row_form(table, 0, mean)
        inverse = lax.rsqrt(spread / n_all + EPS)
        row_form(table, 1, inverse)
        return n_all, inverse

    def total(kind, at, group):
        buf = kind[at]
        out = buf[0]
        for q in range(1, group):
            out = out + buf[q]
        return out

    def sums_near(at):
        near_wait(at)
        r.wide[at][high] = total(r.near, at, inner)
        wide_send(at)

    def sums_wide(at):
        wide_wait(at)
        return total(r.wide, at, outer)

    def local_stats(at, ref, channels):
        count = channels // 128
        buf = r.near[at]
        for c in range(channels // 256):
            lanes = slice(c * 256, (c + 1) * 256)
            acc = jnp.zeros((SIDE, 256), F32)
            for k in range(live):
                part = lax.fori_loop(
                    0, height, lambda y, a: a + ref[pl.ds(block(k, y), SIDE), lanes],
                    jnp.zeros((SIDE, 256), F32), unroll=height,
                )
                acc = acc + part * v[k]
            s_own = fold(acc)
            mean = s_own / jnp.maximum(n_own, 1.0)
            acc = jnp.zeros((SIDE, 256), F32)
            for k in range(live):
                def square(y, a):
                    gap = ref[pl.ds(block(k, y), SIDE), lanes] - mean
                    return a + gap * gap

                part = lax.fori_loop(0, height, square, jnp.zeros((SIDE, 256), F32), unroll=height)
                acc = acc + part * v[k]
            to_dense(buf, low, 0, s_own, 2 * c)
            to_dense(buf, low, count, fold(acc), 2 * c)
        if at == 0:
            buf[low, 4:5, :] = jnp.full((1, 128), n_own, F32)

    def norm_silu(ref, slope_ref, table, gain, bias, write):
        centre, inverse = table[0:1, :], table[1:2, :]
        g, b = gain[...].reshape(1, mid), bias[...].reshape(1, mid)
        for k in range(live):
            def step(y, carry):
                at = block(k, y)
                hat = (ref[pl.ds(at, SIDE), :] - centre) * inverse
                u = hat * g + b
                s = 0.5 * jnp.tanh(0.5 * u) + 0.5
                h = u * s
                ref[pl.ds(at, SIDE), :] = hat
                slope_ref[pl.ds(at, SIDE), :] = jnp.where(mask, s + (h - h * s), 0.0)
                write(at, jnp.where(mask, h, 0.0))
                return carry

            lax.fori_loop(0, height, step, 0, unroll=2)

    f_load.wait()
    fp, f4, flat = r.fp, r.f4, r.flat
    tiles = feat // 128
    pitch = slots * tiles

    def widen(q, carry):
        here = pl.ds(pl.multiple_of(q * 128, 128), 128)
        flat[here, :] = f4[here, :].astype(F32)
        return carry

    lax.fori_loop(0, f4.shape[0] // 128, widen, 0, unroll=7)
    flat[area * pitch :, :] = jnp.zeros((flat.shape[0] - area * pitch, 128), F32)
    short = lax.broadcasted_iota(jnp.int32, (SIDE, 128), 0) < width
    for k in range(live):
        first, second = (1 - later[k]).astype(F32), later[k].astype(F32)

        def copy_row(y, carry):
            for q in range(tiles):
                at = y * (width * pitch) + (q * slots + k)
                one = flat[pl.ds(at, SIDE, stride=pitch), :]
                two = flat[pl.ds(at + 1, SIDE, stride=pitch), :]
                row = jnp.where(short, one * first + two * second, 0.0)
                fp[pl.ds(block(k, y), SIDE), q * 128 : (q + 1) * 128] = row.astype(BF16)
            return carry

        lax.fori_loop(0, height, copy_row, 0)
    wr_load.wait()
    wr = r.wr
    hat_a, slope_a = r.hat_a, r.slope_a
    hat_a[...] = dot(fp[...], wr[...])
    local_stats(0, hat_a, mid)
    pl.semaphore_wait(barrier, len(low_peers + high_peers + clip_peers))
    near_send(0)
    r.ft[...] = fp[...].T
    stats_near(0, mid // 128)
    ws_load.wait()
    we_load.wait()
    wait_bytes(wc, load.at[4])
    ws, we = r.ws, r.we
    table_a, table_b, table_c = r.table_a, r.table_b, r.table_c
    n_all, inv_a = stats_wide(0, mid // 128, table_a)
    xp = r.xp

    def three(ref, at, left, middle, right):
        here = pl.ds(at + SIDE, SIDE)
        ref[here, 0:mid] = left.astype(BF16)
        ref[here, mid : 2 * mid] = middle.astype(BF16)
        ref[here, 2 * mid : 3 * mid] = right.astype(BF16)

    def write_a(at, h):
        three(xp, at, pltpu.roll(h, 1, 0), h, pltpu.roll(h, SIDE - 1, 0))

    norm_silu(hat_a, slope_a, table_a, r.gain_a, r.bias_a, write_a)

    hat_b, slope_b, hb = r.hat_b, r.slope_b, r.hb
    acc = None
    for i in range(3):
        part = dot(xp[i * SIDE : i * SIDE + rows, :], ws[i].reshape(3 * mid, mid))
        acc = part if acc is None else acc + part
    hat_b[...] = acc
    local_stats(1, hat_b, mid)
    near_send(1)
    xt = r.xt
    xt[...] = xp[SIDE : SIDE + rows, mid : 2 * mid].T
    stats_near(1, mid // 128)
    _, inv_b = stats_wide(1, mid // 128, table_b)

    def write_b(at, h):
        hb[pl.ds(at, SIDE), :] = h.astype(BF16)

    norm_silu(hat_b, slope_b, table_b, r.gain_b, r.bias_b, write_b)

    hat_c, slope_c = r.hat_c, r.slope_c
    hat_c[...] = dot(hb[...], we[...])
    local_stats(2, hat_c, feat)
    near_send(2)
    hbt = r.hbt
    hbt[...] = hb[...].T
    stats_near(2, feat // 128)
    _, inv_c = stats_wide(2, feat // 128, table_c)

    pool, slope_sum, slope_hat = r.pool, r.slope_sum, r.slope_hat
    for c in range(feat // 256):
        lanes = slice(c * 256, (c + 1) * 256)
        centre, inverse = table_c[0:1, lanes], table_c[1:2, lanes]
        g = r.gain_c[lanes].reshape(1, 256)
        b = r.bias_c[lanes].reshape(1, 256)
        for k in range(live):
            def step(y, carry):
                a0, a1, a2 = carry
                at = block(k, y)
                hat = (hat_c[pl.ds(at, SIDE), lanes] - centre) * inverse
                u = hat * g + b + fp[pl.ds(at, SIDE), lanes].astype(F32)
                s = 0.5 * jnp.tanh(0.5 * u) + 0.5
                h = u * s
                slope = s + (h - h * s)
                hat_c[pl.ds(at, SIDE), lanes] = hat
                slope_c[pl.ds(at, SIDE), lanes] = slope
                return a0 + h, a1 + slope, a2 + slope * hat

            zero = jnp.zeros((SIDE, 256), F32)
            a0, a1, a2 = lax.fori_loop(0, height, step, (zero, zero, zero), unroll=2)
            p_row = (fold(a0) * (1.0 / area)).astype(BF16).astype(F32)
            to_dense(pool, 0, 8 * k, p_row, 2 * c)
            to_dense(slope_sum, k, 0, fold(a1), 2 * c)
            to_dense(slope_hat, k, 0, fold(a2), 2 * c)
    for k in range(live):
        pool[0, 24 + k : 25 + k, :] = jnp.full((1, 128), key[k], F32)
        pool[0, 28 + k : 29 + k, :] = jnp.full((1, 128), weight[k], F32)
    for q, device in enumerate(clip_peers):
        send(pool.at[0], pool.at[q + 1], r.pool_s.at[0], r.pool_r.at[0], device)
    wait_bytes(pool.at[pl.ds(1, len(clip_peers))], r.pool_r.at[0])

    lw = dense_of(r.loss_weight)
    grads = []
    for k in range(live):
        my_key = jnp.full((1, 128), key[k], F32)
        my_weight = jnp.full((1, 128), weight[k], F32)
        mean = jnp.zeros((8, 128), F32)
        den = jnp.zeros((1, 128), F32)
        for q in range(len(clip_peers) + 1):
            for m in range(live):
                match = jnp.where(pool[q, 24 + m : 25 + m, :] == my_key, pool[q, 28 + m : 29 + m, :], 0.0)
                den = den + match
                mean = mean + match * pool[q, 8 * m : 8 * m + 8, :]
        den = jnp.where(den == 0.0, 1.0, den)
        mean = mean / den
        power = jnp.sum(jnp.sum(mean * mean, axis=0, keepdims=True), axis=1, keepdims=True)
        scale = lax.rsqrt(power * (1.0 / feat) + EPS)
        unit = mean * scale
        along = jnp.sum(jnp.sum(unit * lw, axis=0, keepdims=True), axis=1, keepdims=True)
        mean_grad = scale * (lw - unit * (along * (1.0 / feat)))
        grads.append((my_weight / den) * mean_grad * (1.0 / area))

    near3 = r.near[3]
    shift = jnp.zeros((8, 128), F32)
    gain = jnp.zeros((8, 128), F32)
    for k in range(live):
        shift = shift + grads[k] * slope_sum[k]
        gain = gain + grads[k] * slope_hat[k]
    near3[low, 0:8, :] = shift
    near3[low, 8:16, :] = gain
    near_send(3)
    coef = r.coef
    scale_c = dense_of(r.gain_c) * inv_c
    for k in range(live):
        row_form(coef, k, grads[k])
        row_form(coef, 3 + k, grads[k] * scale_c)
    sums_near(3)
    both = sums_wide(3)
    out[0:16, :] = both
    row_form(coef, 6, both[0:8] * scale_c / n_all)
    row_form(coef, 7, both[8:16] * scale_c / n_all)
    gpc = r.gpc
    for k in range(live):
        for c in range(feat // 256):
            lanes = slice(c * 256, (c + 1) * 256)
            c0 = coef[3 + k : 4 + k, lanes]
            c1 = coef[6:7, lanes] * v[k]
            c2 = coef[7:8, lanes] * v[k]

            def step(y, carry):
                at = block(k, y)
                grad = slope_c[pl.ds(at, SIDE), lanes] * c0 - (c1 + hat_c[pl.ds(at, SIDE), lanes] * c2)
                gpc[pl.ds(at, SIDE), lanes] = grad.astype(BF16)
                return carry

            lax.fori_loop(0, height, step, 0, unroll=2)

    def back_sums(at, grad_ref, slope_ref, hat_ref):
        zero = jnp.zeros((SIDE, mid), F32)
        carry = (zero, zero)
        for k in range(live):
            def step(y, c):
                here = pl.ds(block(k, y), SIDE)
                grad = grad_ref[here, :] * slope_ref[here, :]
                grad_ref[here, :] = grad
                return c[0] + grad, c[1] + grad * hat_ref[here, :]

            carry = lax.fori_loop(0, height, step, carry, unroll=2)
        buf = r.near[at]
        to_dense(buf, low, 0, jnp.sum(carry[0], axis=0, keepdims=True), 0)
        to_dense(buf, low, 2, jnp.sum(carry[1], axis=0, keepdims=True), 0)

    def back_apply(at, table, gain_ref, inv, grad_ref, hat_ref, write):
        both = sums_wide(at)
        out[8 * at - 16 : 8 * at - 8, :] = both
        scale = dense_of(gain_ref) * inv
        row_form(table, 2, scale)
        row_form(table, 3, both[0:2] * scale / n_all)
        row_form(table, 4, both[2:4] * scale / n_all)
        for k in range(live):
            c0, c1, c2 = table[2:3, :], table[3:4, :] * v[k], table[4:5, :] * v[k]

            def step(y, carry):
                at_row = block(k, y)
                here = pl.ds(at_row, SIDE)
                write(at_row, grad_ref[here, :] * c0 - (c1 + hat_ref[here, :] * c2))
                return carry

            lax.fori_loop(0, height, step, 0, unroll=2)

    core, bit_x, bit_y, at_z = me % 2, (me // 2) % 2, (me // 4) % 2, (me // 8) % quad
    at_far = me // (8 * quad)
    bit1 = bit_x + core * (bit_y - bit_x)
    bit2 = bit_y + core * (bit_x - bit_y)
    sibling = me + 1 - 2 * core
    peer1 = me + (1 - 2 * bit1) * (2 + 2 * core)
    peer2 = me + (1 - 2 * bit2) * (4 - 2 * core)
    z_at = [(at_z + o) % quad for o in range(1, quad)]
    z_peer = [me + 8 * (q - at_z) for q in z_at]
    far_peer = [me + 8 * quad * ((at_far + o) % far - at_far) for o in range(1, far)]
    chunk_s, chunk_r = r.chunk_s, r.chunk_r
    waits = []

    def chunk(q):
        part, whole = r.part[q], r.whole[q]
        size = part.shape[0]
        half, quarter, eighth, piece = size // 2, size // 4, size // 8, size // (8 * quad)
        m8 = lambda value: pl.multiple_of(value, 8)
        at_h = m8(core * half)
        at_q = m8(at_h + bit1 * quarter)
        at_e = m8(at_q + bit2 * eighth)
        at_p = m8(at_e + at_z * piece)

        def go(step, src, dst, device):
            send(src, dst, chunk_s.at[q, step], chunk_r.at[q, step], device)

        def finish(step, ref):
            wait_bytes(ref, chunk_r.at[q, step])
            waits.append((ref, chunk_s.at[q, step]))

        rb0, rb1, rb2, rb3 = r.rb0[q], r.rb1[q], r.rb2[q], r.rb3[q]
        go(0, part.at[pl.ds(m8((1 - core) * half), half)], rb0, sibling)
        yield
        finish(0, rb0)
        part[pl.ds(at_h, half), :] = part[pl.ds(at_h, half), :] + rb0[...]
        go(1, part.at[pl.ds(m8(at_h + (1 - bit1) * quarter), quarter)], rb1, peer1)
        yield
        finish(1, rb1)
        part[pl.ds(at_q, quarter), :] = part[pl.ds(at_q, quarter), :] + rb1[...]
        go(2, part.at[pl.ds(m8(at_q + (1 - bit2) * eighth), eighth)], rb2, peer2)
        yield
        finish(2, rb2)
        part[pl.ds(at_e, eighth), :] = part[pl.ds(at_e, eighth), :] + rb2[...]
        for o in range(quad - 1):
            go(3, part.at[pl.ds(m8(at_e + z_at[o] * piece), piece)], rb3.at[pl.ds(o * piece, piece)], z_peer[o])
        yield
        finish(3, rb3)
        own = part[pl.ds(at_p, piece), :]
        for o in range(quad - 1):
            own = own + rb3[o * piece : (o + 1) * piece, :]
        if far > 1:
            rb4 = r.rb4[q]
            rb4[at_far] = own
            for device in far_peer:
                go(8, rb4.at[at_far], rb4.at[at_far], device)
            yield
            finish(8, rb4.at[pl.ds(0, far - 1)])
            own = rb4[0]
            for o in range(1, far):
                own = own + rb4[o]
        whole[pl.ds(at_p, piece), :] = own
        for o in range(quad - 1):
            go(4, whole.at[pl.ds(at_p, piece)], whole.at[pl.ds(at_p, piece)], z_peer[o])
        yield
        finish(4, whole.at[pl.ds(0, (quad - 1) * piece)])
        go(5, whole.at[pl.ds(at_e, eighth)], whole.at[pl.ds(at_e, eighth)], peer2)
        yield
        finish(5, whole.at[pl.ds(0, eighth)])
        go(6, whole.at[pl.ds(at_q, quarter)], whole.at[pl.ds(at_q, quarter)], peer1)
        yield
        finish(6, whole.at[pl.ds(0, quarter)])
        go(7, whole.at[pl.ds(at_h, half)], whole.at[pl.ds(at_h, half)], sibling)
        yield
        finish(7, whole.at[pl.ds(0, half)])
        yield

    chunks = [chunk(q) for q in range(5)]

    def go_on(*which):
        for name in which:
            next(chunks[name], None)

    def spread_lanes(ref, value):
        height_of = value.shape[0]
        for q in range(value.shape[1] // 128):
            ref[q * height_of : (q + 1) * height_of, :] = value[:, q * 128 : (q + 1) * 128]

    grad_b, grad_a = r.grad_b, r.grad_a
    grad_b[...] = dot(gpc[...], we[...], NT)
    back_sums(4, grad_b, slope_b, hat_b)
    near_send(4)
    spread_lanes(r.part[E], dot(hbt[...], gpc[...]))
    go_on(E)
    sums_near(4)
    go_on(E)
    g3 = r.g3

    def write_gb(at, grad):
        grad = jnp.where(mask, grad, 0.0)
        three(g3, at, pltpu.roll(grad, SIDE - 1, 0), grad, pltpu.roll(grad, 1, 0))

    back_apply(4, table_b, r.gain_b, inv_b, grad_b, hat_b, write_gb)
    go_on(E)
    for i in range(3):
        spread_lanes(r.part[S0 + i], dot(xt[...], g3[(2 - i) * SIDE : (2 - i) * SIDE + rows, :]))
        go_on(S0 + i)
    acc = None
    for i in range(3):
        part = dot(g3[(2 - i) * SIDE : (2 - i) * SIDE + rows, :], wc[i], NT)
        acc = part if acc is None else acc + part
    grad_a[...] = acc
    back_sums(5, grad_a, slope_a, hat_a)
    near_send(5)
    go_on(S0, S1, E, S2)
    sums_near(5)
    go_on(S0, S1, E, S2)
    gpa = r.gpa

    def write_ga(at, grad):
        gpa[pl.ds(at, SIDE), :] = grad.astype(BF16)

    back_apply(5, table_a, r.gain_a, inv_a, grad_a, hat_a, write_ga)
    spread_lanes(r.part[R], dot(r.ft[...], gpa[...]))
    go_on(R)
    go_on(E, S0, S1, S2)

    hat_c[...] = dot(gpa[...], wr[...], NT)
    go_on(E, S0, S1, S2, R)
    def blend(y, carry):
        for q in range(tiles):
            lanes = slice(q * 128, (q + 1) * 128)
            terms = [
                slope_c[pl.ds(block(k, y), SIDE), lanes] * coef[k : k + 1, lanes] + hat_c[pl.ds(block(k, y), SIDE), lanes]
                for k in range(live)
            ]
            for m in range(slots):
                if m == 0:
                    value = terms[0] * keep[0]
                elif m == live:
                    value = terms[m - 1] * moved[m - 1]
                else:
                    value = terms[m] * keep[m] + terms[m - 1] * moved[m - 1]
                at = y * (width * pitch) + (q * slots + m)
                flat[pl.ds(at, width, stride=pitch), :] = value[0:width, :]
        return carry

    keep = [(1 - later[k]).astype(F32) for k in range(live)]
    moved = [later[k].astype(F32) for k in range(live)]
    for part in range(2):
        lax.fori_loop(part * height // 2, (part + 1) * height // 2, blend, 0)
        go_on(E, S0, S1, S2, R)
    gf = r.gf

    def narrow(q, carry):
        here = pl.ds(pl.multiple_of(q * 128, 128), 128)
        gf[here, :] = flat[here, :].astype(BF16)
        return carry

    lax.fori_loop(0, gf.shape[0] // 128, narrow, 0, unroll=7)

    for _ in range(12):
        go_on(E, S0, S1, S2, R)

    for at in range(6):
        wait_bytes(r.near[at].at[pl.ds(0, inner - 1)], near_s.at[at])
        wait_bytes(r.wide[at].at[pl.ds(0, outer - 1)], wide_s.at[at])
    wait_bytes(pool.at[pl.ds(1, len(clip_peers))], r.pool_s.at[0])
    for ref, sem in waits:
        wait_bytes(ref, sem)


def store(gf, vectors, expand, s0, s1, s2, reduce, frames_out, reduce_out, spatial_out, expand_out, *rest):
    ga, ba, gb, bb, gc, bc, sem = rest
    pltpu.make_async_copy(gf, frames_out, sem.at[0]).start()
    depth, width = reduce_out.shape
    for q in range(width // 128):
        pltpu.make_async_copy(
            reduce.at[pl.ds(q * depth, depth)], reduce_out.at[:, pl.ds(q * 128, 128)], sem.at[1]
        ).start()
    depth, width = expand_out.shape
    for q in range(width // 128):
        pltpu.make_async_copy(
            expand.at[pl.ds(q * depth, depth)], expand_out.at[:, pl.ds(q * 128, 128)], sem.at[2]
        ).start()
    for i, part in enumerate((s0, s1, s2)):
        for q in range(part.shape[0] // depth):
            pltpu.make_async_copy(
                part.at[pl.ds(q * depth, depth)],
                spatial_out.at[i, q * 128 // depth, :, pl.ds(q * 128 % depth, 128)],
                sem.at[3 + i],
            ).start()
    for ref, first in ((bc, 0), (gc, 8), (bb, 16), (gb, 18), (ba, 24), (ga, 26)):
        for q in range(ref.shape[0] // 128):
            ref[q * 128 : (q + 1) * 128] = vectors[first + q : first + q + 1, :].reshape(128)
    wait_bytes(gf, sem.at[0])
    wait_bytes(reduce, sem.at[1])
    wait_bytes(expand, sem.at[2])
    for i, part in enumerate((s0, s1, s2)):
        wait_bytes(part, sem.at[3 + i])


def solution(mesh):
    n = mesh.shape["clip"]

    def shards(*args):
        slots, height, width, feat = args[0].shape
        mid = args[1].shape[1]
        live = slots - 1
        rows = live * ROWS
        outer = n // 8
        quad = min(4, outer)
        far = outer // quad
        flat_shape = (slots * height * width * feat // 128, 128)
        hbm = pl.BlockSpec(memory_space=pltpu.HBM)
        any_spec = pl.BlockSpec(memory_space=pl.ANY)
        vmem = pl.BlockSpec(memory_space=pltpu.VMEM)
        smem = pl.BlockSpec(memory_space=pltpu.SMEM)
        dma = pltpu.SemaphoreType.DMA
        matrix, third = mid * feat // 128, 3 * mid * mid // 128
        sizes = [matrix, third, third, third, matrix]
        scratch = dict(
            f4=pltpu.VMEM(flat_shape, BF16),
            flat=pltpu.VMEM((flat_shape[0] + 2 * flat_shape[0] // (height * width), 128), F32),
            fp=pltpu.VMEM((rows, feat), BF16),
            ft=pltpu.VMEM((feat, rows), BF16),
            wr=pltpu.VMEM((feat, mid), BF16),
            ws=pltpu.VMEM((3, 3, mid, mid), BF16),
            wc=pltpu.VMEM((3, mid, 3 * mid), BF16),
            we=pltpu.VMEM((mid, feat), BF16),
            hat_a=pltpu.VMEM((rows, mid), F32),
            slope_a=pltpu.VMEM((rows, mid), F32),
            grad_a=pltpu.VMEM((rows, mid), F32),
            hat_b=pltpu.VMEM((rows, mid), F32),
            slope_b=pltpu.VMEM((rows, mid), F32),
            grad_b=pltpu.VMEM((rows, mid), F32),
            xp=pltpu.VMEM((rows + 2 * SIDE, 3 * mid), BF16),
            xt=pltpu.VMEM((mid, rows), BF16),
            hb=pltpu.VMEM((rows, mid), BF16),
            hbt=pltpu.VMEM((mid, rows), BF16),
            hat_c=pltpu.VMEM((rows, feat), F32),
            slope_c=pltpu.VMEM((rows, feat), F32),
            gpc=pltpu.VMEM((rows, feat), BF16),
            g3=pltpu.VMEM((rows + 2 * SIDE, 3 * mid), BF16),
            gpa=pltpu.VMEM((rows, mid), BF16),
            table_a=pltpu.VMEM((8, mid), F32),
            table_b=pltpu.VMEM((8, mid), F32),
            table_c=pltpu.VMEM((8, feat), F32),
            coef=pltpu.VMEM((8, feat), F32),
            dense=pltpu.VMEM((8, 128), F32),
            pool=pltpu.VMEM((6, 32, 128), F32),
            slope_sum=pltpu.VMEM((live, 8, 128), F32),
            slope_hat=pltpu.VMEM((live, 8, 128), F32),
            near=[pltpu.VMEM((8, 16 if at in (2, 3) else 8, 128), F32) for at in range(6)],
            wide=[pltpu.VMEM((outer, 16 if at in (2, 3) else 8, 128), F32) for at in range(6)],
            part=[pltpu.VMEM((size, 128), F32) for size in sizes],
            rb0=[pltpu.VMEM((size // 2, 128), F32) for size in sizes],
            rb1=[pltpu.VMEM((size // 4, 128), F32) for size in sizes],
            rb2=[pltpu.VMEM((size // 8, 128), F32) for size in sizes],
            rb3=[pltpu.VMEM(((quad - 1) * size // (8 * quad), 128), F32) for size in sizes],
            rb4=[pltpu.VMEM((far, size // (8 * quad), 128), F32) for size in sizes if far > 1],
            load_sem=dma((5,)),
            near_s=dma((6,)),
            near_r=dma((6,)),
            wide_s=dma((6,)),
            wide_r=dma((6,)),
            pool_s=dma((1,)),
            pool_r=dma((1,)),
            chunk_s=dma((5, 9)),
            chunk_r=dma((5, 9)),
        )
        ins = dict(
            frames=hbm, w_reduce=hbm, w_spatial=hbm, w_expand=hbm,
            gain_a=vmem, bias_a=vmem, gain_b=vmem, bias_b=vmem, gain_c=vmem, bias_c=vmem,
            clip_ids=smem, segment_ids=smem, slot_valid=smem, segment_weight=smem, loss_weight=vmem,
        )
        outs = dict(gf=pltpu.VMEM(flat_shape, BF16), vectors=pltpu.VMEM((32, 128), F32))
        names = (*ins, *outs, *scratch)
        whole = [pltpu.VMEM((size, 128), F32) for size in sizes]
        tiled = args[0].transpose(1, 2, 0, 3).reshape(height, width, slots, feat // 128, 128)
        tiled = tiled.transpose(0, 1, 3, 2, 4).reshape(flat_shape)
        results = pl.pallas_call(
            functools.partial(kernel, (names, len(ins) + len(outs), n, slots, height, width, feat, mid)),
            out_shape=[*outs.values(), *whole],
            in_specs=list(ins.values()),
            out_specs=[vmem] * (len(outs) + len(whole)),
            scratch_shapes=list(scratch.values()),
            compiler_params=pltpu.CompilerParams(
                collective_id=0, has_side_effects=True, vmem_limit_bytes=52 * 1024 * 1024
            ),
            cost_estimate=pl.CostEstimate(flops=5_200_000_000, bytes_accessed=12_000_000, transcendentals=1_500_000),
        )(tiled, *args[1:])
        vector = jax.ShapeDtypeStruct((mid,), F32)
        wide_vector = jax.ShapeDtypeStruct((feat,), F32)
        flat_grad, *rest = pl.pallas_call(
            store,
            out_shape=[
                jax.ShapeDtypeStruct(flat_shape, BF16),
                jax.ShapeDtypeStruct((feat, mid), F32),
                jax.ShapeDtypeStruct((3, 3, mid, mid), F32),
                jax.ShapeDtypeStruct((mid, feat), F32),
                vector, vector, vector, vector, wide_vector, wide_vector,
            ],
            in_specs=[any_spec, vmem] + [any_spec] * 5,
            out_specs=[hbm] * 4 + [vmem] * 6,
            scratch_shapes=[dma((6,))],
        )(*results)
        grad_frames = flat_grad.reshape(height, width, feat // 128, slots, 128).transpose(0, 1, 3, 2, 4)
        return grad_frames.reshape(height, width, slots, feat).transpose(2, 0, 1, 3), *rest

    split = P("clip")
    in_specs = (split,) + (P(),) * 9 + (split,) * 3 + (P(), P())
    out_specs = (split,) + (P(),) * 9
    return jax.shard_map(shards, mesh=mesh, in_specs=in_specs, out_specs=out_specs, check_vma=False)
```

```python
import functools
from types import SimpleNamespace

import jax
import jax.numpy as jnp
from jax import lax
from jax.experimental import pallas as pl
from jax.experimental.pallas import tpu as pltpu
from jax.sharding import PartitionSpec as P

MESH = pl.DeviceIdType.MESH
EPS = 1e-05
F32 = jnp.float32
BF16 = jnp.bfloat16
SIDE = 16
ROWS = SIDE * SIDE
NN = (((1,), (0,)), ((), ()))
NT = (((1,), (1,)), ((), ()))
E, S0, S1, S2, R = range(5)


def dot(a, b, dims=NN):
    return lax.dot_general(a, b, dims, preferred_element_type=F32)


def wait_bytes(ref, sem):
    pltpu.make_async_copy(ref, ref, sem).wait()


def kernel(cfg, *refs):
    names, arrays, n, slots, height, width, feat, mid = cfg
    r = SimpleNamespace(**dict(zip(names, refs[:arrays] + refs[arrays + 5 :], strict=True)), whole=refs[arrays : arrays + 5])
    live = slots - 1
    rows = live * ROWS
    area = height * width
    inner = 8
    outer = n // inner
    quad = min(4, outer)
    far = outer // quad
    me = lax.axis_index("clip")
    low, high = me % inner, me // inner

    def send(src, dst, ssem, rsem, device):
        copy = pltpu.make_async_remote_copy(
            src_ref=src, dst_ref=dst, send_sem=ssem, recv_sem=rsem, device_id=(device,), device_id_type=MESH
        )
        copy.start()

    low_peers = [me - low + (low + o) % inner for o in range(1, inner)]
    high_peers = [low + inner * ((high + o) % outer) for o in range(1, outer)]
    clip_peers = [(me + o) % n for o in (1, n - 1, n // 2, n // 2 - 1, n // 2 + 1)]
    barrier = pltpu.get_barrier_semaphore()
    for device in low_peers + high_peers + clip_peers:
        pl.semaphore_signal(barrier, inc=1, device_id=(device,), device_id_type=MESH)

    load = r.load_sem
    out = r.vectors
    f_load = pltpu.make_async_copy(r.frames, r.f4.at[pl.ds(0, area)], load.at[0])
    wr_load = pltpu.make_async_copy(r.w_reduce, r.wr, load.at[1])
    ws_load = pltpu.make_async_copy(r.w_spatial, r.ws, load.at[2])
    we_load = pltpu.make_async_copy(r.w_expand, r.we, load.at[3])
    f_load.start()
    r.f4[area:] = jnp.zeros((r.f4.shape[0] - area, *r.f4.shape[1:]), BF16)
    wr_load.start()
    ws_load.start()
    we_load.start()
    wc = r.wc
    for i in range(3):
        for j in range(3):
            pltpu.make_async_copy(
                r.w_spatial.at[i, j], wc.at[i, :, pl.ds(j * mid, mid)], load.at[4]
            ).start()

    for ref in (r.fp, r.xp, r.g3, r.hb, r.gpc, r.gpa):
        ref[...] = jnp.zeros(ref.shape, ref.dtype)

    valid, clip, segment = r.slot_valid, r.clip_ids, r.segment_ids
    later, alive = [], 1
    for k in range(live):
        alive = alive * valid[k]
        later.append(1 - alive)

    def kept(values, k):
        return values[k] + later[k] * (values[k + 1] - values[k])

    v = [kept(valid, k).astype(F32) for k in range(live)]
    key = [kept(clip, k).astype(F32) for k in range(live)]
    weight = []
    for k in range(live):
        at = kept(segment, k).astype(F32)
        w0, w1, w2 = (r.segment_weight[q] for q in range(3))
        weight.append(
            v[k] * (w0 * ((1.0 - at) * (2.0 - at) * 0.5) + w1 * (at * (2.0 - at)) + w2 * (at * (at - 1.0) * 0.5))
        )
    n_own = (v[0] + v[1] + v[2]) * float(area)

    def block(k, y):
        return pl.multiple_of(k * ROWS + y * SIDE, SIDE)

    mask = lax.broadcasted_iota(jnp.int32, (SIDE, 256), 0) < width

    def fold(value):
        return jnp.sum(jnp.where(mask, value, 0.0), axis=0, keepdims=True)

    def to_dense(ref, at, row0, value, first):
        for q in range(value.shape[1] // 128):
            ref[at, pl.ds(row0 + first + q, 1), :] = value[:, q * 128 : (q + 1) * 128]

    def row_form(ref, row, dense):
        d = r.dense
        count = dense.shape[0]
        d[0:count, :] = dense
        for q in range(count):
            ref[row : row + 1, q * 128 : (q + 1) * 128] = d[q : q + 1, :]

    def dense_of(ref1):
        d = r.dense
        count = ref1.shape[0] // 128
        for q in range(count):
            d[q : q + 1, :] = ref1[q * 128 : (q + 1) * 128].reshape(1, 128)
        return d[0:count, :]

    near_s, near_r, wide_s, wide_r = r.near_s, r.near_r, r.wide_s, r.wide_r

    def near_send(at):
        buf = r.near[at]
        for o in range(1, inner):
            send(buf.at[low], buf.at[low], near_s.at[at], near_r.at[at], low_peers[o - 1])

    def near_wait(at):
        wait_bytes(r.near[at].at[pl.ds(0, inner - 1)], near_r.at[at])

    def wide_send(at):
        buf = r.wide[at]
        for o in range(1, outer):
            send(buf.at[high], buf.at[high], wide_s.at[at], wide_r.at[at], high_peers[o - 1])

    def wide_wait(at):
        wait_bytes(r.wide[at].at[pl.ds(0, outer - 1)], wide_r.at[at])

    def combine(kind, at, group, count):
        buf, counts = kind[at], kind[0]
        n_part = [counts[q, 4:5, :] for q in range(group)]
        s_part = [buf[q, 0:count, :] for q in range(group)]
        n_all = sum(n_part[1:], n_part[0])
        s_all = sum(s_part[1:], s_part[0])
        mean = s_all / jnp.maximum(n_all, 1.0)
        spread = jnp.zeros((count, 128), F32)
        for q in range(group):
            gap = s_part[q] / jnp.maximum(n_part[q], 1.0) - mean
            spread = spread + (buf[q, count : 2 * count, :] + n_part[q] * gap * gap)
        return n_all, s_all, mean, spread

    def stats_near(at, count):
        near_wait(at)
        n_all, s_all, _, spread = combine(r.near, at, inner, count)
        buf = r.wide[at]
        buf[high, 0:count, :] = s_all
        buf[high, count : 2 * count, :] = spread
        if at == 0:
            buf[high, 4:5, :] = n_all
        wide_send(at)

    def stats_wide(at, count, table):
        wide_wait(at)
        n_all, _, mean, spread = combine(r.wide, at, outer, count)
        row_form(table, 0, mean)
        inverse = lax.rsqrt(spread / n_all + EPS)
        row_form(table, 1, inverse)
        return n_all, inverse

    def total(kind, at, group):
        buf = kind[at]
        out = buf[0]
        for q in range(1, group):
            out = out + buf[q]
        return out

    def sums_near(at):
        near_wait(at)
        r.wide[at][high] = total(r.near, at, inner)
        wide_send(at)

    def sums_wide(at):
        wide_wait(at)
        return total(r.wide, at, outer)

    def local_stats(at, ref, channels):
        count = channels // 128
        buf = r.near[at]
        for c in range(channels // 256):
            lanes = slice(c * 256, (c + 1) * 256)
            acc = jnp.zeros((SIDE, 256), F32)
            for k in range(live):
                part = lax.fori_loop(
                    0, height, lambda y, a: a + ref[pl.ds(block(k, y), SIDE), lanes],
                    jnp.zeros((SIDE, 256), F32), unroll=height,
                )
                acc = acc + part * v[k]
            s_own = fold(acc)
            mean = s_own / jnp.maximum(n_own, 1.0)
            acc = jnp.zeros((SIDE, 256), F32)
            for k in range(live):
                def square(y, a):
                    gap = ref[pl.ds(block(k, y), SIDE), lanes] - mean
                    return a + gap * gap

                part = lax.fori_loop(0, height, square, jnp.zeros((SIDE, 256), F32), unroll=height)
                acc = acc + part * v[k]
            to_dense(buf, low, 0, s_own, 2 * c)
            to_dense(buf, low, count, fold(acc), 2 * c)
        if at == 0:
            buf[low, 4:5, :] = jnp.full((1, 128), n_own, F32)

    def norm_silu(ref, slope_ref, table, gain, bias, write):
        centre, inverse = table[0:1, :], table[1:2, :]
        g, b = gain[...].reshape(1, mid), bias[...].reshape(1, mid)
        for k in range(live):
            def step(y, carry):
                at = block(k, y)
                hat = (ref[pl.ds(at, SIDE), :] - centre) * inverse
                u = hat * g + b
                s = 0.5 * jnp.tanh(0.5 * u) + 0.5
                h = u * s
                ref[pl.ds(at, SIDE), :] = hat
                slope_ref[pl.ds(at, SIDE), :] = jnp.where(mask, s + (h - h * s), 0.0)
                write(at, jnp.where(mask, h, 0.0))
                return carry

            lax.fori_loop(0, height, step, 0, unroll=2)

    f_load.wait()
    fp, f4 = r.fp, r.f4
    tiles = feat // 128
    group = SIDE // slots
    short = lax.broadcasted_iota(jnp.int32, (SIDE, 128), 0) < width
    keep = [(1 - later[k]).astype(F32) for k in range(live)]
    moved = [later[k].astype(F32) for k in range(live)]

    def regroup(y, carry):
        for p in range(tiles // group):
            value = f4[pl.ds(y * width, SIDE), p * SIDE : (p + 1) * SIDE, :].astype(F32)
            value = jnp.swapaxes(value, 0, 1)
            for q in range(group):
                for k in range(live):
                    row = value[q * slots + k] * keep[k] + value[q * slots + k + 1] * moved[k]
                    lanes = slice((p * group + q) * 128, (p * group + q + 1) * 128)
                    fp[pl.ds(block(k, y), SIDE), lanes] = jnp.where(short, row, 0.0).astype(BF16)
        return carry

    lax.fori_loop(0, height, regroup, 0)
    wr_load.wait()
    wr = r.wr
    hat_a, slope_a = r.hat_a, r.slope_a
    hat_a[...] = dot(fp[...], wr[...])
    local_stats(0, hat_a, mid)
    pl.semaphore_wait(barrier, len(low_peers + high_peers + clip_peers))
    near_send(0)
    r.ft[...] = fp[...].T
    stats_near(0, mid // 128)
    ws_load.wait()
    we_load.wait()
    wait_bytes(wc, load.at[4])
    ws, we = r.ws, r.we
    table_a, table_b, table_c = r.table_a, r.table_b, r.table_c
    n_all, inv_a = stats_wide(0, mid // 128, table_a)
    xp = r.xp

    def three(ref, at, left, middle, right):
        here = pl.ds(at + SIDE, SIDE)
        ref[here, 0:mid] = left.astype(BF16)
        ref[here, mid : 2 * mid] = middle.astype(BF16)
        ref[here, 2 * mid : 3 * mid] = right.astype(BF16)

    def write_a(at, h):
        three(xp, at, pltpu.roll(h, 1, 0), h, pltpu.roll(h, SIDE - 1, 0))

    norm_silu(hat_a, slope_a, table_a, r.gain_a, r.bias_a, write_a)

    hat_b, slope_b, hb = r.hat_b, r.slope_b, r.hb
    acc = None
    for i in range(3):
        part = dot(xp[i * SIDE : i * SIDE + rows, :], ws[i].reshape(3 * mid, mid))
        acc = part if acc is None else acc + part
    hat_b[...] = acc
    local_stats(1, hat_b, mid)
    near_send(1)
    xt = r.xt
    xt[...] = xp[SIDE : SIDE + rows, mid : 2 * mid].T
    stats_near(1, mid // 128)
    _, inv_b = stats_wide(1, mid // 128, table_b)

    def write_b(at, h):
        hb[pl.ds(at, SIDE), :] = h.astype(BF16)

    norm_silu(hat_b, slope_b, table_b, r.gain_b, r.bias_b, write_b)

    hat_c, slope_c = r.hat_c, r.slope_c
    hat_c[...] = dot(hb[...], we[...])
    local_stats(2, hat_c, feat)
    near_send(2)
    hbt = r.hbt
    hbt[...] = hb[...].T
    stats_near(2, feat // 128)
    _, inv_c = stats_wide(2, feat // 128, table_c)

    pool, slope_sum, slope_hat = r.pool, r.slope_sum, r.slope_hat
    for c in range(feat // 256):
        lanes = slice(c * 256, (c + 1) * 256)
        centre, inverse = table_c[0:1, lanes], table_c[1:2, lanes]
        g = r.gain_c[lanes].reshape(1, 256)
        b = r.bias_c[lanes].reshape(1, 256)
        for k in range(live):
            def step(y, carry):
                a0, a1, a2 = carry
                at = block(k, y)
                hat = (hat_c[pl.ds(at, SIDE), lanes] - centre) * inverse
                u = hat * g + b + fp[pl.ds(at, SIDE), lanes].astype(F32)
                s = 0.5 * jnp.tanh(0.5 * u) + 0.5
                h = u * s
                slope = s + (h - h * s)
                hat_c[pl.ds(at, SIDE), lanes] = hat
                slope_c[pl.ds(at, SIDE), lanes] = slope
                return a0 + h, a1 + slope, a2 + slope * hat

            zero = jnp.zeros((SIDE, 256), F32)
            a0, a1, a2 = lax.fori_loop(0, height, step, (zero, zero, zero), unroll=2)
            p_row = (fold(a0) * (1.0 / area)).astype(BF16).astype(F32)
            to_dense(pool, 0, 8 * k, p_row, 2 * c)
            to_dense(slope_sum, k, 0, fold(a1), 2 * c)
            to_dense(slope_hat, k, 0, fold(a2), 2 * c)
    for k in range(live):
        pool[0, 24 + k : 25 + k, :] = jnp.full((1, 128), key[k], F32)
        pool[0, 28 + k : 29 + k, :] = jnp.full((1, 128), weight[k], F32)
    for q, device in enumerate(clip_peers):
        send(pool.at[0], pool.at[q + 1], r.pool_s.at[0], r.pool_r.at[0], device)
    wait_bytes(pool.at[pl.ds(1, len(clip_peers))], r.pool_r.at[0])

    lw = dense_of(r.loss_weight)
    grads = []
    for k in range(live):
        my_key = jnp.full((1, 128), key[k], F32)
        my_weight = jnp.full((1, 128), weight[k], F32)
        mean = jnp.zeros((8, 128), F32)
        den = jnp.zeros((1, 128), F32)
        for q in range(len(clip_peers) + 1):
            for m in range(live):
                match = jnp.where(pool[q, 24 + m : 25 + m, :] == my_key, pool[q, 28 + m : 29 + m, :], 0.0)
                den = den + match
                mean = mean + match * pool[q, 8 * m : 8 * m + 8, :]
        den = jnp.where(den == 0.0, 1.0, den)
        mean = mean / den
        power = jnp.sum(jnp.sum(mean * mean, axis=0, keepdims=True), axis=1, keepdims=True)
        scale = lax.rsqrt(power * (1.0 / feat) + EPS)
        unit = mean * scale
        along = jnp.sum(jnp.sum(unit * lw, axis=0, keepdims=True), axis=1, keepdims=True)
        mean_grad = scale * (lw - unit * (along * (1.0 / feat)))
        grads.append((my_weight / den) * mean_grad * (1.0 / area))

    near3 = r.near[3]
    shift = jnp.zeros((8, 128), F32)
    gain = jnp.zeros((8, 128), F32)
    for k in range(live):
        shift = shift + grads[k] * slope_sum[k]
        gain = gain + grads[k] * slope_hat[k]
    near3[low, 0:8, :] = shift
    near3[low, 8:16, :] = gain
    near_send(3)
    coef = r.coef
    scale_c = dense_of(r.gain_c) * inv_c
    for k in range(live):
        row_form(coef, k, grads[k])
        row_form(coef, 3 + k, grads[k] * scale_c)
    sums_near(3)
    both = sums_wide(3)
    out[0:16, :] = both
    row_form(coef, 6, both[0:8] * scale_c / n_all)
    row_form(coef, 7, both[8:16] * scale_c / n_all)
    gpc = r.gpc
    for k in range(live):
        for c in range(feat // 256):
            lanes = slice(c * 256, (c + 1) * 256)
            c0 = coef[3 + k : 4 + k, lanes]
            c1 = coef[6:7, lanes] * v[k]
            c2 = coef[7:8, lanes] * v[k]

            def step(y, carry):
                at = block(k, y)
                grad = slope_c[pl.ds(at, SIDE), lanes] * c0 - (c1 + hat_c[pl.ds(at, SIDE), lanes] * c2)
                gpc[pl.ds(at, SIDE), lanes] = grad.astype(BF16)
                return carry

            lax.fori_loop(0, height, step, 0, unroll=2)

    def back_sums(at, grad_ref, slope_ref, hat_ref):
        zero = jnp.zeros((SIDE, mid), F32)
        carry = (zero, zero)
        for k in range(live):
            def step(y, c):
                here = pl.ds(block(k, y), SIDE)
                grad = grad_ref[here, :] * slope_ref[here, :]
                grad_ref[here, :] = grad
                return c[0] + grad, c[1] + grad * hat_ref[here, :]

            carry = lax.fori_loop(0, height, step, carry, unroll=2)
        buf = r.near[at]
        to_dense(buf, low, 0, jnp.sum(carry[0], axis=0, keepdims=True), 0)
        to_dense(buf, low, 2, jnp.sum(carry[1], axis=0, keepdims=True), 0)

    def back_apply(at, table, gain_ref, inv, grad_ref, hat_ref, write):
        both = sums_wide(at)
        out[8 * at - 16 : 8 * at - 8, :] = both
        scale = dense_of(gain_ref) * inv
        row_form(table, 2, scale)
        row_form(table, 3, both[0:2] * scale / n_all)
        row_form(table, 4, both[2:4] * scale / n_all)
        for k in range(live):
            c0, c1, c2 = table[2:3, :], table[3:4, :] * v[k], table[4:5, :] * v[k]

            def step(y, carry):
                at_row = block(k, y)
                here = pl.ds(at_row, SIDE)
                write(at_row, grad_ref[here, :] * c0 - (c1 + hat_ref[here, :] * c2))
                return carry

            lax.fori_loop(0, height, step, 0, unroll=2)

    core, bit_x, bit_y, at_z = me % 2, (me // 2) % 2, (me // 4) % 2, (me // 8) % quad
    at_far = me // (8 * quad)
    bit1 = bit_x + core * (bit_y - bit_x)
    bit2 = bit_y + core * (bit_x - bit_y)
    sibling = me + 1 - 2 * core
    peer1 = me + (1 - 2 * bit1) * (2 + 2 * core)
    peer2 = me + (1 - 2 * bit2) * (4 - 2 * core)
    z_at = [(at_z + o) % quad for o in range(1, quad)]
    z_peer = [me + 8 * (q - at_z) for q in z_at]
    far_peer = [me + 8 * quad * ((at_far + o) % far - at_far) for o in range(1, far)]
    chunk_s, chunk_r = r.chunk_s, r.chunk_r
    waits = []

    def chunk(q):
        part, whole = r.part[q], r.whole[q]
        size = part.shape[0]
        half, quarter, eighth, piece = size // 2, size // 4, size // 8, size // (8 * quad)
        m8 = lambda value: pl.multiple_of(value, 8)
        at_h = m8(core * half)
        at_q = m8(at_h + bit1 * quarter)
        at_e = m8(at_q + bit2 * eighth)
        at_p = m8(at_e + at_z * piece)

        def go(step, src, dst, device):
            send(src, dst, chunk_s.at[q, step], chunk_r.at[q, step], device)

        def finish(step, ref):
            wait_bytes(ref, chunk_r.at[q, step])
            waits.append((ref, chunk_s.at[q, step]))

        rb0, rb1, rb2, rb3 = r.rb0[q], r.rb1[q], r.rb2[q], r.rb3[q]
        go(0, part.at[pl.ds(m8((1 - core) * half), half)], rb0, sibling)
        yield
        finish(0, rb0)
        part[pl.ds(at_h, half), :] = part[pl.ds(at_h, half), :] + rb0[...]
        go(1, part.at[pl.ds(m8(at_h + (1 - bit1) * quarter), quarter)], rb1, peer1)
        yield
        finish(1, rb1)
        part[pl.ds(at_q, quarter), :] = part[pl.ds(at_q, quarter), :] + rb1[...]
        go(2, part.at[pl.ds(m8(at_q + (1 - bit2) * eighth), eighth)], rb2, peer2)
        yield
        finish(2, rb2)
        part[pl.ds(at_e, eighth), :] = part[pl.ds(at_e, eighth), :] + rb2[...]
        for o in range(quad - 1):
            go(3, part.at[pl.ds(m8(at_e + z_at[o] * piece), piece)], rb3.at[pl.ds(o * piece, piece)], z_peer[o])
        yield
        finish(3, rb3)
        own = part[pl.ds(at_p, piece), :]
        for o in range(quad - 1):
            own = own + rb3[o * piece : (o + 1) * piece, :]
        if far > 1:
            rb4 = r.rb4[q]
            rb4[at_far] = own
            for device in far_peer:
                go(8, rb4.at[at_far], rb4.at[at_far], device)
            yield
            finish(8, rb4.at[pl.ds(0, far - 1)])
            own = rb4[0]
            for o in range(1, far):
                own = own + rb4[o]
        whole[pl.ds(at_p, piece), :] = own
        for o in range(quad - 1):
            go(4, whole.at[pl.ds(at_p, piece)], whole.at[pl.ds(at_p, piece)], z_peer[o])
        yield
        finish(4, whole.at[pl.ds(0, (quad - 1) * piece)])
        go(5, whole.at[pl.ds(at_e, eighth)], whole.at[pl.ds(at_e, eighth)], peer2)
        yield
        finish(5, whole.at[pl.ds(0, eighth)])
        go(6, whole.at[pl.ds(at_q, quarter)], whole.at[pl.ds(at_q, quarter)], peer1)
        yield
        finish(6, whole.at[pl.ds(0, quarter)])
        go(7, whole.at[pl.ds(at_h, half)], whole.at[pl.ds(at_h, half)], sibling)
        yield
        finish(7, whole.at[pl.ds(0, half)])
        yield

    chunks = [chunk(q) for q in range(5)]

    def go_on(*which):
        for name in which:
            next(chunks[name], None)

    def spread_lanes(ref, value):
        height_of = value.shape[0]
        for q in range(value.shape[1] // 128):
            ref[q * height_of : (q + 1) * height_of, :] = value[:, q * 128 : (q + 1) * 128]

    grad_b, grad_a = r.grad_b, r.grad_a
    grad_b[...] = dot(gpc[...], we[...], NT)
    back_sums(4, grad_b, slope_b, hat_b)
    near_send(4)
    spread_lanes(r.part[E], dot(hbt[...], gpc[...]))
    go_on(E)
    sums_near(4)
    go_on(E)
    g3 = r.g3

    def write_gb(at, grad):
        grad = jnp.where(mask, grad, 0.0)
        three(g3, at, pltpu.roll(grad, SIDE - 1, 0), grad, pltpu.roll(grad, 1, 0))

    back_apply(4, table_b, r.gain_b, inv_b, grad_b, hat_b, write_gb)
    go_on(E)
    for i in range(3):
        spread_lanes(r.part[S0 + i], dot(xt[...], g3[(2 - i) * SIDE : (2 - i) * SIDE + rows, :]))
        go_on(S0 + i)
    acc = None
    for i in range(3):
        part = dot(g3[(2 - i) * SIDE : (2 - i) * SIDE + rows, :], wc[i], NT)
        acc = part if acc is None else acc + part
    grad_a[...] = acc
    back_sums(5, grad_a, slope_a, hat_a)
    near_send(5)
    go_on(S0, S1, E, S2)
    sums_near(5)
    go_on(S0, S1, E, S2)
    gpa = r.gpa

    def write_ga(at, grad):
        gpa[pl.ds(at, SIDE), :] = grad.astype(BF16)

    back_apply(5, table_a, r.gain_a, inv_a, grad_a, hat_a, write_ga)
    spread_lanes(r.part[R], dot(r.ft[...], gpa[...]))
    go_on(R)
    go_on(E, S0, S1, S2)

    hat_c[...] = dot(gpa[...], wr[...], NT)
    go_on(E, S0, S1, S2, R)
    gf = r.gf

    def blend(y, carry):
        for p in range(tiles // group):
            values = []
            for q in range(group):
                lanes = slice((p * group + q) * 128, (p * group + q + 1) * 128)
                terms = [
                    slope_c[pl.ds(block(k, y), SIDE), lanes] * coef[k : k + 1, lanes]
                    + hat_c[pl.ds(block(k, y), SIDE), lanes]
                    for k in range(live)
                ]
                values.append(terms[0] * keep[0])
                for m in range(1, live):
                    values.append(terms[m] * keep[m] + terms[m - 1] * moved[m - 1])
                values.append(terms[live - 1] * moved[live - 1])
            value = jnp.swapaxes(jnp.stack(values), 0, 1)
            gf[pl.ds(y * width, width), p * SIDE : (p + 1) * SIDE, :] = value[0:width].astype(BF16)
        return carry

    for part in range(2):
        lax.fori_loop(part * height // 2, (part + 1) * height // 2, blend, 0)
        go_on(E, S0, S1, S2, R)

    for _ in range(12):
        go_on(E, S0, S1, S2, R)

    for at in range(6):
        wait_bytes(r.near[at].at[pl.ds(0, inner - 1)], near_s.at[at])
        wait_bytes(r.wide[at].at[pl.ds(0, outer - 1)], wide_s.at[at])
    wait_bytes(pool.at[pl.ds(1, len(clip_peers))], r.pool_s.at[0])
    for ref, sem in waits:
        wait_bytes(ref, sem)


def store(gf, vectors, expand, s0, s1, s2, reduce, frames_out, reduce_out, spatial_out, expand_out, *rest):
    ga, ba, gb, bb, gc, bc, sem = rest
    pltpu.make_async_copy(gf, frames_out, sem.at[0]).start()
    depth, width = reduce_out.shape
    for q in range(width // 128):
        pltpu.make_async_copy(
            reduce.at[pl.ds(q * depth, depth)], reduce_out.at[:, pl.ds(q * 128, 128)], sem.at[1]
        ).start()
    depth, width = expand_out.shape
    for q in range(width // 128):
        pltpu.make_async_copy(
            expand.at[pl.ds(q * depth, depth)], expand_out.at[:, pl.ds(q * 128, 128)], sem.at[2]
        ).start()
    for i, part in enumerate((s0, s1, s2)):
        for q in range(part.shape[0] // depth):
            pltpu.make_async_copy(
                part.at[pl.ds(q * depth, depth)],
                spatial_out.at[i, q * 128 // depth, :, pl.ds(q * 128 % depth, 128)],
                sem.at[3 + i],
            ).start()
    for ref, first in ((bc, 0), (gc, 8), (bb, 16), (gb, 18), (ba, 24), (ga, 26)):
        for q in range(ref.shape[0] // 128):
            ref[q * 128 : (q + 1) * 128] = vectors[first + q : first + q + 1, :].reshape(128)
    wait_bytes(gf, sem.at[0])
    wait_bytes(reduce, sem.at[1])
    wait_bytes(expand, sem.at[2])
    for i, part in enumerate((s0, s1, s2)):
        wait_bytes(part, sem.at[3 + i])


def solution(mesh):
    n = mesh.shape["clip"]

    def shards(*args):
        slots, height, width, feat = args[0].shape
        mid = args[1].shape[1]
        live = slots - 1
        rows = live * ROWS
        outer = n // 8
        quad = min(4, outer)
        far = outer // quad
        flat_shape = (height * width, slots * feat // 128, 128)
        hbm = pl.BlockSpec(memory_space=pltpu.HBM)
        vmem = pl.BlockSpec(memory_space=pltpu.VMEM)
        smem = pl.BlockSpec(memory_space=pltpu.SMEM)
        dma = pltpu.SemaphoreType.DMA
        matrix, third = mid * feat // 128, 3 * mid * mid // 128
        sizes = [matrix, third, third, third, matrix]
        scratch = dict(
            f4=pltpu.VMEM((flat_shape[0] + SIDE - width, *flat_shape[1:]), BF16),
            fp=pltpu.VMEM((rows, feat), BF16),
            ft=pltpu.VMEM((feat, rows), BF16),
            wr=pltpu.VMEM((feat, mid), BF16),
            ws=pltpu.VMEM((3, 3, mid, mid), BF16),
            wc=pltpu.VMEM((3, mid, 3 * mid), BF16),
            we=pltpu.VMEM((mid, feat), BF16),
            hat_a=pltpu.VMEM((rows, mid), F32),
            slope_a=pltpu.VMEM((rows, mid), F32),
            grad_a=pltpu.VMEM((rows, mid), F32),
            hat_b=pltpu.VMEM((rows, mid), F32),
            slope_b=pltpu.VMEM((rows, mid), F32),
            grad_b=pltpu.VMEM((rows, mid), F32),
            xp=pltpu.VMEM((rows + 2 * SIDE, 3 * mid), BF16),
            xt=pltpu.VMEM((mid, rows), BF16),
            hb=pltpu.VMEM((rows, mid), BF16),
            hbt=pltpu.VMEM((mid, rows), BF16),
            hat_c=pltpu.VMEM((rows, feat), F32),
            slope_c=pltpu.VMEM((rows, feat), F32),
            gpc=pltpu.VMEM((rows, feat), BF16),
            g3=pltpu.VMEM((rows + 2 * SIDE, 3 * mid), BF16),
            gpa=pltpu.VMEM((rows, mid), BF16),
            table_a=pltpu.VMEM((8, mid), F32),
            table_b=pltpu.VMEM((8, mid), F32),
            table_c=pltpu.VMEM((8, feat), F32),
            coef=pltpu.VMEM((8, feat), F32),
            dense=pltpu.VMEM((8, 128), F32),
            pool=pltpu.VMEM((6, 32, 128), F32),
            slope_sum=pltpu.VMEM((live, 8, 128), F32),
            slope_hat=pltpu.VMEM((live, 8, 128), F32),
            near=[pltpu.VMEM((8, 16 if at in (2, 3) else 8, 128), F32) for at in range(6)],
            wide=[pltpu.VMEM((outer, 16 if at in (2, 3) else 8, 128), F32) for at in range(6)],
            part=[pltpu.VMEM((size, 128), F32) for size in sizes],
            rb0=[pltpu.VMEM((size // 2, 128), F32) for size in sizes],
            rb1=[pltpu.VMEM((size // 4, 128), F32) for size in sizes],
            rb2=[pltpu.VMEM((size // 8, 128), F32) for size in sizes],
            rb3=[pltpu.VMEM(((quad - 1) * size // (8 * quad), 128), F32) for size in sizes],
            rb4=[pltpu.VMEM((far, size // (8 * quad), 128), F32) for size in sizes if far > 1],
            load_sem=dma((5,)),
            near_s=dma((6,)),
            near_r=dma((6,)),
            wide_s=dma((6,)),
            wide_r=dma((6,)),
            pool_s=dma((1,)),
            pool_r=dma((1,)),
            chunk_s=dma((5, 9)),
            chunk_r=dma((5, 9)),
        )
        ins = dict(
            frames=hbm, w_reduce=hbm, w_spatial=hbm, w_expand=hbm,
            gain_a=vmem, bias_a=vmem, gain_b=vmem, bias_b=vmem, gain_c=vmem, bias_c=vmem,
            clip_ids=smem, segment_ids=smem, slot_valid=smem, segment_weight=smem, loss_weight=vmem,
        )
        outs = dict(gf=pltpu.VMEM(flat_shape, BF16), vectors=pltpu.VMEM((32, 128), F32))
        names = (*ins, *outs, *scratch)
        whole = [pltpu.VMEM((size, 128), F32) for size in sizes]
        tiled = args[0].transpose(1, 2, 0, 3).reshape(height, width, slots, feat // 128, 128)
        tiled = tiled.transpose(0, 1, 3, 2, 4).reshape(flat_shape)
        results = pl.pallas_call(
            functools.partial(kernel, (names, len(ins) + len(outs), n, slots, height, width, feat, mid)),
            out_shape=[*outs.values(), *whole],
            in_specs=list(ins.values()),
            out_specs=[vmem] * (len(outs) + len(whole)),
            scratch_shapes=list(scratch.values()),
            compiler_params=pltpu.CompilerParams(
                collective_id=0, has_side_effects=True, vmem_limit_bytes=48 * 1024 * 1024
            ),
            cost_estimate=pl.CostEstimate(flops=5_200_000_000, bytes_accessed=12_000_000, transcendentals=1_500_000),
        )(tiled, *args[1:])
        vector = jax.ShapeDtypeStruct((mid,), F32)
        wide_vector = jax.ShapeDtypeStruct((feat,), F32)
        flat_grad, *rest = pl.pallas_call(
            store,
            out_shape=[
                jax.ShapeDtypeStruct(flat_shape, BF16),
                jax.ShapeDtypeStruct((feat, mid), F32),
                jax.ShapeDtypeStruct((3, 3, mid, mid), F32),
                jax.ShapeDtypeStruct((mid, feat), F32),
                vector, vector, vector, vector, wide_vector, wide_vector,
            ],
            in_specs=[vmem] * 7,
            out_specs=[hbm] * 4 + [vmem] * 6,
            scratch_shapes=[dma((6,))],
            compiler_params=pltpu.CompilerParams(vmem_limit_bytes=8 * 1024 * 1024),
        )(*(pltpu.with_memory_space_constraint(part, pltpu.VMEM) for part in results))
        grad_frames = flat_grad.reshape(height, width, feat // 128, slots, 128).transpose(0, 1, 3, 2, 4)
        return grad_frames.reshape(height, width, slots, feat).transpose(2, 0, 1, 3), *rest

    split = P("clip")
    in_specs = (split,) + (P(),) * 9 + (split,) * 3 + (P(), P())
    out_specs = (split,) + (P(),) * 9
    return jax.shard_map(shards, mesh=mesh, in_specs=in_specs, out_specs=out_specs, check_vma=False)
```

```python
import functools
from types import SimpleNamespace

import jax
import jax.numpy as jnp
from jax import lax
from jax.experimental import pallas as pl
from jax.experimental.pallas import tpu as pltpu
from jax.sharding import PartitionSpec as P

MESH = pl.DeviceIdType.MESH
EPS = 1e-05
F32 = jnp.float32
BF16 = jnp.bfloat16
SIDE = 16
ROWS = SIDE * SIDE
NN = (((1,), (0,)), ((), ()))
NT = (((1,), (1,)), ((), ()))
E, S0, S1, S2, R = range(5)


def dot(a, b, dims=NN):
    return lax.dot_general(a, b, dims, preferred_element_type=F32)


def wait_bytes(ref, sem):
    pltpu.make_async_copy(ref, ref, sem).wait()


def kernel(cfg, *refs):
    names, arrays, n, slots, height, width, feat, mid = cfg
    r = SimpleNamespace(**dict(zip(names, refs[:arrays] + refs[arrays + 5 :], strict=True)), whole=refs[arrays : arrays + 5])
    live = slots - 1
    rows = live * ROWS
    area = height * width
    inner = 8
    outer = n // inner
    quad = min(4, outer)
    far = outer // quad
    me = lax.axis_index("clip")
    low, high = me % inner, me // inner

    def send(src, dst, ssem, rsem, device):
        copy = pltpu.make_async_remote_copy(
            src_ref=src, dst_ref=dst, send_sem=ssem, recv_sem=rsem, device_id=(device,), device_id_type=MESH
        )
        copy.start()

    direct = n <= 32
    peers = [(me + o) % n for o in range(1, n)]
    low_peers = [me - low + (low + o) % inner for o in range(1, inner)]
    high_peers = [low + inner * ((high + o) % outer) for o in range(1, outer)]
    clip_peers = [(me + o) % n for o in (1, n - 1, n // 2, n // 2 - 1, n // 2 + 1)]
    barrier = pltpu.get_barrier_semaphore()
    greeted = peers if direct else low_peers + high_peers + clip_peers
    for device in greeted:
        pl.semaphore_signal(barrier, inc=1, device_id=(device,), device_id_type=MESH)

    load = r.load_sem
    out = r.vectors
    f_load = pltpu.make_async_copy(r.frames, r.f4.at[pl.ds(0, area)], load.at[0])
    wr_load = pltpu.make_async_copy(r.w_reduce, r.wr, load.at[1])
    ws_load = pltpu.make_async_copy(r.w_spatial, r.ws, load.at[2])
    we_load = pltpu.make_async_copy(r.w_expand, r.we, load.at[3])
    f_load.start()
    r.f4[area:] = jnp.zeros((r.f4.shape[0] - area, *r.f4.shape[1:]), BF16)
    wr_load.start()
    ws_load.start()
    we_load.start()
    wc = r.wc
    for i in range(3):
        for j in range(3):
            pltpu.make_async_copy(
                r.w_spatial.at[i, j], wc.at[i, :, pl.ds(j * mid, mid)], load.at[4]
            ).start()

    hbm_names = [
        r.gain_a, r.bias_a, r.gain_b, r.bias_b, r.gain_c, r.bias_c,
        r.clip_ids, r.segment_ids, r.slot_valid, r.segment_weight, r.loss_weight,
    ]
    small_loads = [
        pltpu.make_async_copy(src, dst, load.at[5 + q]) for q, (src, dst) in enumerate(zip(hbm_names, r.small))
    ]
    for copy in small_loads[6:10] + small_loads[:6] + small_loads[10:]:
        copy.start()
    (r.gain_a, r.bias_a, r.gain_b, r.bias_b, r.gain_c, r.bias_c,
     r.clip_ids, r.segment_ids, r.slot_valid, r.segment_weight, r.loss_weight) = r.small

    for ref in (r.fp, r.xp, r.g3, r.hb, r.gpc, r.gpa):
        ref[...] = jnp.zeros(ref.shape, ref.dtype)

    for copy in small_loads[6:10]:
        copy.wait()

    valid, clip, segment = r.slot_valid, r.clip_ids, r.segment_ids
    later, alive = [], 1
    for k in range(live):
        alive = alive * valid[k]
        later.append(1 - alive)

    def kept(values, k):
        return values[k] + later[k] * (values[k + 1] - values[k])

    v = [kept(valid, k).astype(F32) for k in range(live)]
    key = [kept(clip, k).astype(F32) for k in range(live)]
    weight = []
    for k in range(live):
        at = kept(segment, k).astype(F32)
        w0, w1, w2 = (r.segment_weight[q] for q in range(3))
        weight.append(
            v[k] * (w0 * ((1.0 - at) * (2.0 - at) * 0.5) + w1 * (at * (2.0 - at)) + w2 * (at * (at - 1.0) * 0.5))
        )
    n_own = (v[0] + v[1] + v[2]) * float(area)

    def block(k, y):
        return pl.multiple_of(k * ROWS + y * SIDE, SIDE)

    mask = lax.broadcasted_iota(jnp.int32, (SIDE, 256), 0) < width

    def fold(value):
        return jnp.sum(jnp.where(mask, value, 0.0), axis=0, keepdims=True)

    def to_dense(ref, at, row0, value, first):
        for q in range(value.shape[1] // 128):
            ref[at, pl.ds(row0 + first + q, 1), :] = value[:, q * 128 : (q + 1) * 128]

    def row_form(ref, row, dense):
        d = r.dense
        count = dense.shape[0]
        d[0:count, :] = dense
        for q in range(count):
            ref[row : row + 1, q * 128 : (q + 1) * 128] = d[q : q + 1, :]

    def dense_of(ref1):
        d = r.dense
        count = ref1.shape[0] // 128
        for q in range(count):
            d[q : q + 1, :] = ref1[q * 128 : (q + 1) * 128].reshape(1, 128)
        return d[0:count, :]

    near_s, near_r, wide_s, wide_r = r.near_s, r.near_r, r.wide_s, r.wide_r

    def one_stage(at):
        return direct and at not in (2, 3)

    def near_at(at):
        return me if one_stage(at) else low

    def near_send(at):
        buf, mine = r.near[at], near_at(at)
        for device in peers if one_stage(at) else low_peers:
            send(buf.at[mine], buf.at[mine], near_s.at[at], near_r.at[at], device)

    def near_wait(at, sems):
        buf = r.near[at]
        wait_bytes(buf.at[pl.ds(0, buf.shape[0] - 1)], sems.at[at])

    def wide_send(at):
        buf = r.wide[at]
        for device in high_peers:
            send(buf.at[high], buf.at[high], wide_s.at[at], wide_r.at[at], device)

    def wide_wait(at, sems):
        wait_bytes(r.wide[at].at[pl.ds(0, outer - 1)], sems.at[at])

    def combine(buf, counts, group, count):
        n_part = [counts(q) for q in range(group)]
        s_part = [buf[q, 0:count, :] for q in range(group)]
        n_all = sum(n_part[1:], n_part[0])
        s_all = sum(s_part[1:], s_part[0])
        mean = s_all / jnp.maximum(n_all, 1.0)
        spread = jnp.zeros((count, 128), F32)
        for q in range(group):
            gap = s_part[q] / jnp.maximum(n_part[q], 1.0) - mean
            spread = spread + (buf[q, count : 2 * count, :] + n_part[q] * gap * gap)
        return n_all, s_all, mean, spread

    counts0 = r.near[0]
    plane = r.plane

    def near_count(q):
        return counts0[(me - low + q) if direct else q, 4:5, :]

    def wide_count(q):
        return plane[q, 0:1, :] if direct else r.wide[0][q, 4:5, :]

    def stats_near(at, count):
        if one_stage(at):
            return
        near_wait(at, near_r)
        n_all, s_all, _, spread = combine(r.near[at], near_count, inner, count)
        buf = r.wide[at]
        buf[high, 0:count, :] = s_all
        buf[high, count : 2 * count, :] = spread
        if at == 0:
            buf[high, 4:5, :] = n_all
        wide_send(at)

    def stats_wide(at, count, table):
        if one_stage(at):
            near_wait(at, near_r)
            n_all, _, mean, spread = combine(r.near[at], lambda q: counts0[q, 4:5, :], n, count)
            if at == 0:
                for q in range(outer):
                    plane[q, 0:1, :] = sum(counts0[q * inner + m, 4:5, :] for m in range(inner))
        else:
            wide_wait(at, wide_r)
            n_all, _, mean, spread = combine(r.wide[at], wide_count, outer, count)
        row_form(table, 0, mean)
        inverse = lax.rsqrt(spread / n_all + EPS)
        row_form(table, 1, inverse)
        return n_all, inverse

    def total(buf):
        out = buf[0]
        for q in range(1, buf.shape[0]):
            out = out + buf[q]
        return out

    def sums_near(at):
        if not one_stage(at):
            near_wait(at, near_r)
            r.wide[at][high] = total(r.near[at])
            wide_send(at)

    def sums_wide(at):
        if one_stage(at):
            near_wait(at, near_r)
            return total(r.near[at])
        wide_wait(at, wide_r)
        return total(r.wide[at])

    def local_stats(at, ref, channels):
        count = channels // 128
        buf = r.near[at]
        for c in range(channels // 256):
            lanes = slice(c * 256, (c + 1) * 256)
            acc = jnp.zeros((SIDE, 256), F32)
            for k in range(live):
                part = lax.fori_loop(
                    0, height, lambda y, a: a + ref[pl.ds(block(k, y), SIDE), lanes],
                    jnp.zeros((SIDE, 256), F32), unroll=height,
                )
                acc = acc + part * v[k]
            s_own = fold(acc)
            mean = s_own / jnp.maximum(n_own, 1.0)
            acc = jnp.zeros((SIDE, 256), F32)
            for k in range(live):
                def square(y, a):
                    gap = ref[pl.ds(block(k, y), SIDE), lanes] - mean
                    return a + gap * gap

                part = lax.fori_loop(0, height, square, jnp.zeros((SIDE, 256), F32), unroll=height)
                acc = acc + part * v[k]
            to_dense(buf, near_at(at), 0, s_own, 2 * c)
            to_dense(buf, near_at(at), count, fold(acc), 2 * c)
        if at == 0:
            buf[near_at(at), 4:5, :] = jnp.full((1, 128), n_own, F32)

    def norm_silu(ref, slope_ref, table, gain, bias, write):
        centre, inverse = table[0:1, :], table[1:2, :]
        g, b = gain[...].reshape(1, mid), bias[...].reshape(1, mid)
        for k in range(live):
            def step(y, carry):
                at = block(k, y)
                hat = (ref[pl.ds(at, SIDE), :] - centre) * inverse
                u = hat * g + b
                s = 0.5 * jnp.tanh(0.5 * u) + 0.5
                h = u * s
                ref[pl.ds(at, SIDE), :] = hat
                slope_ref[pl.ds(at, SIDE), :] = jnp.where(mask, s + (h - h * s), 0.0)
                write(at, jnp.where(mask, h, 0.0))
                return carry

            lax.fori_loop(0, height, step, 0, unroll=2)

    f_load.wait()
    fp, f4 = r.fp, r.f4
    tiles = feat // 128
    group = SIDE // slots
    short = lax.broadcasted_iota(jnp.int32, (SIDE, 128), 0) < width
    keep = [(1 - later[k]).astype(F32) for k in range(live)]
    moved = [later[k].astype(F32) for k in range(live)]

    def regroup(y, carry):
        for p in range(tiles // group):
            value = f4[pl.ds(y * width, SIDE), p * SIDE : (p + 1) * SIDE, :].astype(F32)
            value = jnp.swapaxes(value, 0, 1)
            for q in range(group):
                for k in range(live):
                    row = value[q * slots + k] * keep[k] + value[q * slots + k + 1] * moved[k]
                    lanes = slice((p * group + q) * 128, (p * group + q + 1) * 128)
                    fp[pl.ds(block(k, y), SIDE), lanes] = jnp.where(short, row, 0.0).astype(BF16)
        return carry

    lax.fori_loop(0, height, regroup, 0)
    wr_load.wait()
    wr = r.wr
    hat_a, slope_a = r.hat_a, r.slope_a
    hat_a[...] = dot(fp[...], wr[...])
    local_stats(0, hat_a, mid)
    pl.semaphore_wait(barrier, len(greeted))
    near_send(0)
    r.ft[...] = fp[...].T
    stats_near(0, mid // 128)
    ws_load.wait()
    we_load.wait()
    wait_bytes(wc, load.at[4])
    ws, we = r.ws, r.we
    for copy in small_loads[:6] + small_loads[10:]:
        copy.wait()
    table_a, table_b, table_c = r.table_a, r.table_b, r.table_c
    n_all, inv_a = stats_wide(0, mid // 128, table_a)
    xp = r.xp

    def three(ref, at, left, middle, right):
        here = pl.ds(at + SIDE, SIDE)
        ref[here, 0:mid] = left.astype(BF16)
        ref[here, mid : 2 * mid] = middle.astype(BF16)
        ref[here, 2 * mid : 3 * mid] = right.astype(BF16)

    def write_a(at, h):
        three(xp, at, pltpu.roll(h, 1, 0), h, pltpu.roll(h, SIDE - 1, 0))

    norm_silu(hat_a, slope_a, table_a, r.gain_a, r.bias_a, write_a)

    hat_b, slope_b, hb = r.hat_b, r.slope_b, r.hb
    acc = None
    for i in range(3):
        part = dot(xp[i * SIDE : i * SIDE + rows, :], ws[i].reshape(3 * mid, mid))
        acc = part if acc is None else acc + part
    hat_b[...] = acc
    local_stats(1, hat_b, mid)
    near_send(1)
    xt = r.xt
    xt[...] = xp[SIDE : SIDE + rows, mid : 2 * mid].T
    stats_near(1, mid // 128)
    _, inv_b = stats_wide(1, mid // 128, table_b)

    def write_b(at, h):
        hb[pl.ds(at, SIDE), :] = h.astype(BF16)

    norm_silu(hat_b, slope_b, table_b, r.gain_b, r.bias_b, write_b)

    hat_c, slope_c = r.hat_c, r.slope_c
    hat_c[...] = dot(hb[...], we[...])
    local_stats(2, hat_c, feat)
    near_send(2)
    hbt = r.hbt
    hbt[...] = hb[...].T
    stats_near(2, feat // 128)
    _, inv_c = stats_wide(2, feat // 128, table_c)

    pool, slope_sum, slope_hat = r.pool, r.slope_sum, r.slope_hat
    for c in range(feat // 256):
        lanes = slice(c * 256, (c + 1) * 256)
        centre, inverse = table_c[0:1, lanes], table_c[1:2, lanes]
        g = r.gain_c[lanes].reshape(1, 256)
        b = r.bias_c[lanes].reshape(1, 256)
        for k in range(live):
            def step(y, carry):
                a0, a1, a2 = carry
                at = block(k, y)
                hat = (hat_c[pl.ds(at, SIDE), lanes] - centre) * inverse
                u = hat * g + b + fp[pl.ds(at, SIDE), lanes].astype(F32)
                s = 0.5 * jnp.tanh(0.5 * u) + 0.5
                h = u * s
                slope = s + (h - h * s)
                hat_c[pl.ds(at, SIDE), lanes] = hat
                slope_c[pl.ds(at, SIDE), lanes] = slope
                return a0 + h, a1 + slope, a2 + slope * hat

            zero = jnp.zeros((SIDE, 256), F32)
            a0, a1, a2 = lax.fori_loop(0, height, step, (zero, zero, zero), unroll=2)
            p_row = (fold(a0) * (1.0 / area)).astype(BF16).astype(F32)
            to_dense(pool, 0, 8 * k, p_row, 2 * c)
            to_dense(slope_sum, k, 0, fold(a1), 2 * c)
            to_dense(slope_hat, k, 0, fold(a2), 2 * c)
    for k in range(live):
        pool[0, 24 + k : 25 + k, :] = jnp.full((1, 128), key[k], F32)
        pool[0, 28 + k : 29 + k, :] = jnp.full((1, 128), weight[k], F32)
    for q, device in enumerate(clip_peers):
        send(pool.at[0], pool.at[q + 1], r.pool_s.at[0], r.pool_r.at[0], device)
    wait_bytes(pool.at[pl.ds(1, len(clip_peers))], r.pool_r.at[0])

    lw = dense_of(r.loss_weight)
    grads = []
    for k in range(live):
        my_key = jnp.full((1, 128), key[k], F32)
        my_weight = jnp.full((1, 128), weight[k], F32)
        mean = jnp.zeros((8, 128), F32)
        den = jnp.zeros((1, 128), F32)
        for q in range(len(clip_peers) + 1):
            for m in range(live):
                match = jnp.where(pool[q, 24 + m : 25 + m, :] == my_key, pool[q, 28 + m : 29 + m, :], 0.0)
                den = den + match
                mean = mean + match * pool[q, 8 * m : 8 * m + 8, :]
        den = jnp.where(den == 0.0, 1.0, den)
        mean = mean / den
        power = jnp.sum(jnp.sum(mean * mean, axis=0, keepdims=True), axis=1, keepdims=True)
        scale = lax.rsqrt(power * (1.0 / feat) + EPS)
        unit = mean * scale
        along = jnp.sum(jnp.sum(unit * lw, axis=0, keepdims=True), axis=1, keepdims=True)
        mean_grad = scale * (lw - unit * (along * (1.0 / feat)))
        grads.append((my_weight / den) * mean_grad * (1.0 / area))

    near3 = r.near[3]
    shift = jnp.zeros((8, 128), F32)
    gain = jnp.zeros((8, 128), F32)
    for k in range(live):
        shift = shift + grads[k] * slope_sum[k]
        gain = gain + grads[k] * slope_hat[k]
    near3[low, 0:8, :] = shift
    near3[low, 8:16, :] = gain
    near_send(3)
    coef = r.coef
    scale_c = dense_of(r.gain_c) * inv_c
    for k in range(live):
        row_form(coef, k, grads[k])
        row_form(coef, 3 + k, grads[k] * scale_c)
    sums_near(3)
    both = sums_wide(3)
    out[0:16, :] = both
    row_form(coef, 6, both[0:8] * scale_c / n_all)
    row_form(coef, 7, both[8:16] * scale_c / n_all)
    gpc = r.gpc
    for k in range(live):
        for c in range(feat // 256):
            lanes = slice(c * 256, (c + 1) * 256)
            c0 = coef[3 + k : 4 + k, lanes]
            c1 = coef[6:7, lanes] * v[k]
            c2 = coef[7:8, lanes] * v[k]

            def step(y, carry):
                at = block(k, y)
                grad = slope_c[pl.ds(at, SIDE), lanes] * c0 - (c1 + hat_c[pl.ds(at, SIDE), lanes] * c2)
                gpc[pl.ds(at, SIDE), lanes] = grad.astype(BF16)
                return carry

            lax.fori_loop(0, height, step, 0, unroll=2)

    def back_sums(at, grad_ref, slope_ref, hat_ref):
        zero = jnp.zeros((SIDE, mid), F32)
        carry = (zero, zero)
        for k in range(live):
            def step(y, c):
                here = pl.ds(block(k, y), SIDE)
                grad = grad_ref[here, :] * slope_ref[here, :]
                grad_ref[here, :] = grad
                return c[0] + grad, c[1] + grad * hat_ref[here, :]

            carry = lax.fori_loop(0, height, step, carry, unroll=2)
        buf = r.near[at]
        to_dense(buf, near_at(at), 0, jnp.sum(carry[0], axis=0, keepdims=True), 0)
        to_dense(buf, near_at(at), 2, jnp.sum(carry[1], axis=0, keepdims=True), 0)

    def back_apply(at, table, gain_ref, inv, grad_ref, hat_ref, write):
        both = sums_wide(at)
        out[8 * at - 16 : 8 * at - 12, :] = both[0:4]
        scale = dense_of(gain_ref) * inv
        row_form(table, 2, scale)
        row_form(table, 3, both[0:2] * scale / n_all)
        row_form(table, 4, both[2:4] * scale / n_all)
        for k in range(live):
            c0, c1, c2 = table[2:3, :], table[3:4, :] * v[k], table[4:5, :] * v[k]

            def step(y, carry):
                at_row = block(k, y)
                here = pl.ds(at_row, SIDE)
                write(at_row, grad_ref[here, :] * c0 - (c1 + hat_ref[here, :] * c2))
                return carry

            lax.fori_loop(0, height, step, 0, unroll=2)

    core, bit_x, bit_y, at_z = me % 2, (me // 2) % 2, (me // 4) % 2, (me // 8) % quad
    at_far = me // (8 * quad)
    bit1 = bit_x + core * (bit_y - bit_x)
    bit2 = bit_y + core * (bit_x - bit_y)
    sibling = me + 1 - 2 * core
    peer1 = me + (1 - 2 * bit1) * (2 + 2 * core)
    peer2 = me + (1 - 2 * bit2) * (4 - 2 * core)
    z_at = [(at_z + o) % quad for o in range(1, quad)]
    z_peer = [me + 8 * (q - at_z) for q in z_at]
    far_peer = [me + 8 * quad * ((at_far + o) % far - at_far) for o in range(1, far)]
    chunk_s, chunk_r = r.chunk_s, r.chunk_r
    waits = []

    def chunk(q):
        part, whole = r.part[q], r.whole[q]
        size = part.shape[0]
        half, quarter, eighth, piece = size // 2, size // 4, size // 8, size // (8 * quad)
        m8 = lambda value: pl.multiple_of(value, 8)
        at_h = m8(core * half)
        at_q = m8(at_h + bit1 * quarter)
        at_e = m8(at_q + bit2 * eighth)
        at_p = m8(at_e + at_z * piece)

        def go(step, src, dst, device):
            send(src, dst, chunk_s.at[q, step], chunk_r.at[q, step], device)

        def finish(step, ref):
            wait_bytes(ref, chunk_r.at[q, step])
            waits.append((ref, chunk_s.at[q, step]))

        rb0, rb1, rb2, rb3 = r.rb0[q], r.rb1[q], r.rb2[q], r.rb3[q]
        go(0, part.at[pl.ds(m8((1 - core) * half), half)], rb0, sibling)
        yield
        finish(0, rb0)
        part[pl.ds(at_h, half), :] = part[pl.ds(at_h, half), :] + rb0[...]
        go(1, part.at[pl.ds(m8(at_h + (1 - bit1) * quarter), quarter)], rb1, peer1)
        yield
        finish(1, rb1)
        part[pl.ds(at_q, quarter), :] = part[pl.ds(at_q, quarter), :] + rb1[...]
        go(2, part.at[pl.ds(m8(at_q + (1 - bit2) * eighth), eighth)], rb2, peer2)
        yield
        finish(2, rb2)
        part[pl.ds(at_e, eighth), :] = part[pl.ds(at_e, eighth), :] + rb2[...]
        for o in range(quad - 1):
            go(3, part.at[pl.ds(m8(at_e + z_at[o] * piece), piece)], rb3.at[pl.ds(o * piece, piece)], z_peer[o])
        yield
        finish(3, rb3)
        own = part[pl.ds(at_p, piece), :]
        for o in range(quad - 1):
            own = own + rb3[o * piece : (o + 1) * piece, :]
        if far > 1:
            rb4 = r.rb4[q]
            rb4[at_far] = own
            for device in far_peer:
                go(8, rb4.at[at_far], rb4.at[at_far], device)
            yield
            finish(8, rb4.at[pl.ds(0, far - 1)])
            own = rb4[0]
            for o in range(1, far):
                own = own + rb4[o]
        whole[pl.ds(at_p, piece), :] = own
        for o in range(quad - 1):
            go(4, whole.at[pl.ds(at_p, piece)], whole.at[pl.ds(at_p, piece)], z_peer[o])
        yield
        finish(4, whole.at[pl.ds(0, (quad - 1) * piece)])
        go(5, whole.at[pl.ds(at_e, eighth)], whole.at[pl.ds(at_e, eighth)], peer2)
        yield
        finish(5, whole.at[pl.ds(0, eighth)])
        go(6, whole.at[pl.ds(at_q, quarter)], whole.at[pl.ds(at_q, quarter)], peer1)
        yield
        finish(6, whole.at[pl.ds(0, quarter)])
        go(7, whole.at[pl.ds(at_h, half)], whole.at[pl.ds(at_h, half)], sibling)
        yield
        finish(7, whole.at[pl.ds(0, half)])
        yield

    chunks = [chunk(q) for q in range(5)]

    def go_on(*which):
        for name in which:
            next(chunks[name], None)

    def spread_lanes(ref, value):
        height_of = value.shape[0]
        for q in range(value.shape[1] // 128):
            ref[q * height_of : (q + 1) * height_of, :] = value[:, q * 128 : (q + 1) * 128]

    grad_b, grad_a = r.grad_b, r.grad_a
    grad_b[...] = dot(gpc[...], we[...], NT)
    back_sums(4, grad_b, slope_b, hat_b)
    near_send(4)
    spread_lanes(r.part[E], dot(hbt[...], gpc[...]))
    go_on(E)
    sums_near(4)
    go_on(E)
    g3 = r.g3

    def write_gb(at, grad):
        grad = jnp.where(mask, grad, 0.0)
        three(g3, at, pltpu.roll(grad, SIDE - 1, 0), grad, pltpu.roll(grad, 1, 0))

    back_apply(4, table_b, r.gain_b, inv_b, grad_b, hat_b, write_gb)
    go_on(E)
    acc = None
    for i in range(3):
        part = dot(g3[(2 - i) * SIDE : (2 - i) * SIDE + rows, :], wc[i], NT)
        acc = part if acc is None else acc + part
    grad_a[...] = acc
    back_sums(5, grad_a, slope_a, hat_a)
    near_send(5)
    for i in range(3):
        spread_lanes(r.part[S0 + i], dot(xt[...], g3[(2 - i) * SIDE : (2 - i) * SIDE + rows, :]))
        go_on(S0 + i)
    go_on(E)
    sums_near(5)
    gpa = r.gpa

    def write_ga(at, grad):
        gpa[pl.ds(at, SIDE), :] = grad.astype(BF16)

    back_apply(5, table_a, r.gain_a, inv_a, grad_a, hat_a, write_ga)
    spread_lanes(r.part[R], dot(r.ft[...], gpa[...]))
    go_on(R)
    go_on(S0, S1, E, S2)

    hat_c[...] = dot(gpa[...], wr[...], NT)
    go_on(E, S0, S1, S2, R)
    gf = r.gf

    def blend(y, carry):
        for p in range(tiles // group):
            values = []
            for q in range(group):
                lanes = slice((p * group + q) * 128, (p * group + q + 1) * 128)
                terms = [
                    slope_c[pl.ds(block(k, y), SIDE), lanes] * coef[k : k + 1, lanes]
                    + hat_c[pl.ds(block(k, y), SIDE), lanes]
                    for k in range(live)
                ]
                values.append(terms[0] * keep[0])
                for m in range(1, live):
                    values.append(terms[m] * keep[m] + terms[m - 1] * moved[m - 1])
                values.append(terms[live - 1] * moved[live - 1])
            value = jnp.swapaxes(jnp.stack(values), 0, 1)
            gf[pl.ds(y * width, width), p * SIDE : (p + 1) * SIDE, :] = value[0:width].astype(BF16)
        return carry

    for part in range(2):
        lax.fori_loop(part * height // 2, (part + 1) * height // 2, blend, 0)
        go_on(E, S0, S1, S2, R)

    for _ in range(12):
        go_on(E, S0, S1, S2, R)

    for at in range(6):
        near_wait(at, near_s)
        if not one_stage(at):
            wide_wait(at, wide_s)
    wait_bytes(pool.at[pl.ds(1, len(clip_peers))], r.pool_s.at[0])
    for ref, sem in waits:
        wait_bytes(ref, sem)


def store(gf, vectors, expand, s0, s1, s2, reduce, frames_out, reduce_out, spatial_out, expand_out, *rest):
    ga, ba, gb, bb, gc, bc, sem = rest
    pltpu.make_async_copy(gf, frames_out, sem.at[0]).start()
    depth, width = reduce_out.shape
    for q in range(width // 128):
        pltpu.make_async_copy(
            reduce.at[pl.ds(q * depth, depth)], reduce_out.at[:, pl.ds(q * 128, 128)], sem.at[1]
        ).start()
    depth, width = expand_out.shape
    for q in range(width // 128):
        pltpu.make_async_copy(
            expand.at[pl.ds(q * depth, depth)], expand_out.at[:, pl.ds(q * 128, 128)], sem.at[2]
        ).start()
    for i, part in enumerate((s0, s1, s2)):
        for q in range(part.shape[0] // depth):
            pltpu.make_async_copy(
                part.at[pl.ds(q * depth, depth)],
                spatial_out.at[i, q * 128 // depth, :, pl.ds(q * 128 % depth, 128)],
                sem.at[3 + i],
            ).start()
    for ref, first in ((bc, 0), (gc, 8), (bb, 16), (gb, 18), (ba, 24), (ga, 26)):
        for q in range(ref.shape[0] // 128):
            ref[q * 128 : (q + 1) * 128] = vectors[first + q : first + q + 1, :].reshape(128)
    wait_bytes(gf, sem.at[0])
    wait_bytes(reduce, sem.at[1])
    wait_bytes(expand, sem.at[2])
    for i, part in enumerate((s0, s1, s2)):
        wait_bytes(part, sem.at[3 + i])


def solution(mesh):
    n = mesh.shape["clip"]

    def shards(*args):
        slots, height, width, feat = args[0].shape
        mid = args[1].shape[1]
        live = slots - 1
        rows = live * ROWS
        outer = n // 8
        quad = min(4, outer)
        far = outer // quad
        flat_shape = (height * width, slots * feat // 128, 128)
        hbm = pl.BlockSpec(memory_space=pltpu.HBM)
        vmem = pl.BlockSpec(memory_space=pltpu.VMEM)
        dma = pltpu.SemaphoreType.DMA
        matrix, third = mid * feat // 128, 3 * mid * mid // 128
        depths = list(enumerate((8, 4, 16, 16, 4, 4)))
        sizes = [matrix, third, third, third, matrix]
        scratch = dict(
            f4=pltpu.VMEM((flat_shape[0] + SIDE - width, *flat_shape[1:]), BF16),
            fp=pltpu.VMEM((rows, feat), BF16),
            ft=pltpu.VMEM((feat, rows), BF16),
            wr=pltpu.VMEM((feat, mid), BF16),
            ws=pltpu.VMEM((3, 3, mid, mid), BF16),
            wc=pltpu.VMEM((3, mid, 3 * mid), BF16),
            we=pltpu.VMEM((mid, feat), BF16),
            hat_a=pltpu.VMEM((rows, mid), F32),
            slope_a=pltpu.VMEM((rows, mid), F32),
            grad_a=pltpu.VMEM((rows, mid), F32),
            hat_b=pltpu.VMEM((rows, mid), F32),
            slope_b=pltpu.VMEM((rows, mid), F32),
            grad_b=pltpu.VMEM((rows, mid), F32),
            xp=pltpu.VMEM((rows + 2 * SIDE, 3 * mid), BF16),
            xt=pltpu.VMEM((mid, rows), BF16),
            hb=pltpu.VMEM((rows, mid), BF16),
            hbt=pltpu.VMEM((mid, rows), BF16),
            hat_c=pltpu.VMEM((rows, feat), F32),
            slope_c=pltpu.VMEM((rows, feat), F32),
            gpc=pltpu.VMEM((rows, feat), BF16),
            g3=pltpu.VMEM((rows + 2 * SIDE, 3 * mid), BF16),
            gpa=pltpu.VMEM((rows, mid), BF16),
            table_a=pltpu.VMEM((8, mid), F32),
            table_b=pltpu.VMEM((8, mid), F32),
            table_c=pltpu.VMEM((8, feat), F32),
            coef=pltpu.VMEM((8, feat), F32),
            dense=pltpu.VMEM((8, 128), F32),
            pool=pltpu.VMEM((6, 32, 128), F32),
            slope_sum=pltpu.VMEM((live, 8, 128), F32),
            slope_hat=pltpu.VMEM((live, 8, 128), F32),
            near=[pltpu.VMEM((n if n <= 32 and at not in (2, 3) else 8, deep, 128), F32) for at, deep in depths],
            wide=[pltpu.VMEM((outer, deep, 128), F32) for at, deep in depths],
            plane=pltpu.VMEM((outer, 8, 128), F32),
            part=[pltpu.VMEM((size, 128), F32) for size in sizes],
            rb0=[pltpu.VMEM((size // 2, 128), F32) for size in sizes],
            rb1=[pltpu.VMEM((size // 4, 128), F32) for size in sizes],
            rb2=[pltpu.VMEM((size // 8, 128), F32) for size in sizes],
            rb3=[pltpu.VMEM(((quad - 1) * size // (8 * quad), 128), F32) for size in sizes],
            rb4=[pltpu.VMEM((far, size // (8 * quad), 128), F32) for size in sizes if far > 1],
            small=[
                *(pltpu.VMEM((c,), F32) for c in (mid, mid, mid, mid, feat, feat)),
                *(pltpu.SMEM((slots,), jnp.int32) for _ in range(3)),
                pltpu.SMEM(args[13].shape, F32),
                pltpu.VMEM((feat,), F32),
            ],
            load_sem=dma((16,)),
            near_s=dma((6,)),
            near_r=dma((6,)),
            wide_s=dma((6,)),
            wide_r=dma((6,)),
            pool_s=dma((1,)),
            pool_r=dma((1,)),
            chunk_s=dma((5, 9)),
            chunk_r=dma((5, 9)),
        )
        ins = dict(
            frames=hbm, w_reduce=hbm, w_spatial=hbm, w_expand=hbm,
            gain_a=hbm, bias_a=hbm, gain_b=hbm, bias_b=hbm, gain_c=hbm, bias_c=hbm,
            clip_ids=hbm, segment_ids=hbm, slot_valid=hbm, segment_weight=hbm, loss_weight=hbm,
        )
        outs = dict(gf=pltpu.VMEM(flat_shape, BF16), vectors=pltpu.VMEM((32, 128), F32))
        names = (*ins, *outs, *scratch)
        whole = [pltpu.VMEM((size, 128), F32) for size in sizes]
        tiled = args[0].transpose(1, 2, 0, 3).reshape(height, width, slots, feat // 128, 128)
        tiled = tiled.transpose(0, 1, 3, 2, 4).reshape(flat_shape)
        results = pl.pallas_call(
            functools.partial(kernel, (names, len(ins) + len(outs), n, slots, height, width, feat, mid)),
            out_shape=[*outs.values(), *whole],
            in_specs=list(ins.values()),
            out_specs=[vmem] * (len(outs) + len(whole)),
            scratch_shapes=list(scratch.values()),
            compiler_params=pltpu.CompilerParams(
                collective_id=0, has_side_effects=True, vmem_limit_bytes=48 * 1024 * 1024
            ),
            cost_estimate=pl.CostEstimate(flops=5_200_000_000, bytes_accessed=12_000_000, transcendentals=1_500_000),
        )(tiled, *args[1:])
        vector = jax.ShapeDtypeStruct((mid,), F32)
        wide_vector = jax.ShapeDtypeStruct((feat,), F32)
        flat_grad, *rest = pl.pallas_call(
            store,
            out_shape=[
                jax.ShapeDtypeStruct(flat_shape, BF16),
                jax.ShapeDtypeStruct((feat, mid), F32),
                jax.ShapeDtypeStruct((3, 3, mid, mid), F32),
                jax.ShapeDtypeStruct((mid, feat), F32),
                vector, vector, vector, vector, wide_vector, wide_vector,
            ],
            in_specs=[vmem] * 7,
            out_specs=[hbm] * 4 + [vmem] * 6,
            scratch_shapes=[dma((6,))],
            compiler_params=pltpu.CompilerParams(vmem_limit_bytes=8 * 1024 * 1024),
        )(*(pltpu.with_memory_space_constraint(part, pltpu.VMEM) for part in results))
        grad_frames = flat_grad.reshape(height, width, feat // 128, slots, 128).transpose(0, 1, 3, 2, 4)
        return grad_frames.reshape(height, width, slots, feat).transpose(2, 0, 1, 3), *rest

    split = P("clip")
    in_specs = (split,) + (P(),) * 9 + (split,) * 3 + (P(), P())
    out_specs = (split,) + (P(),) * 9
    return jax.shard_map(shards, mesh=mesh, in_specs=in_specs, out_specs=out_specs, check_vma=False)
```

```python
import functools
from types import SimpleNamespace

import jax
import jax.numpy as jnp
from jax import lax
from jax.experimental import pallas as pl
from jax.experimental.pallas import tpu as pltpu
from jax.sharding import PartitionSpec as P

MESH = pl.DeviceIdType.MESH
EPS = 1e-05
F32 = jnp.float32
BF16 = jnp.bfloat16
SIDE = 16
ROWS = SIDE * SIDE
NN = (((1,), (0,)), ((), ()))
NT = (((1,), (1,)), ((), ()))
E, S0, S1, S2, R = range(5)


def dot(a, b, dims=NN):
    return lax.dot_general(a, b, dims, preferred_element_type=F32)


def wait_bytes(ref, sem):
    pltpu.make_async_copy(ref, ref, sem).wait()


def kernel(cfg, *refs):
    names, arrays, n, slots, height, width, feat, mid = cfg
    r = SimpleNamespace(**dict(zip(names, refs[:arrays] + refs[arrays + 5 :], strict=True)), whole=refs[arrays : arrays + 5])
    live = slots - 1
    rows = live * ROWS
    area = height * width
    inner = 8
    outer = n // inner
    quad = min(4, outer)
    far = outer // quad
    me = lax.axis_index("clip")
    low, high = me % inner, me // inner

    def send(src, dst, ssem, rsem, device):
        copy = pltpu.make_async_remote_copy(
            src_ref=src, dst_ref=dst, send_sem=ssem, recv_sem=rsem, device_id=(device,), device_id_type=MESH
        )
        copy.start()

    direct = n <= 32
    peers = [(me + o) % n for o in range(1, n)]
    low_peers = [me - low + (low + o) % inner for o in range(1, inner)]
    high_peers = [low + inner * ((high + o) % outer) for o in range(1, outer)]
    clip_peers = [(me + o) % n for o in (1, n - 1, n // 2, n // 2 - 1, n // 2 + 1)]
    barrier = pltpu.get_barrier_semaphore()
    greeted = peers if direct else low_peers + high_peers + clip_peers
    for device in greeted:
        pl.semaphore_signal(barrier, inc=1, device_id=(device,), device_id_type=MESH)

    load = r.load_sem
    out = r.vectors
    f_load = pltpu.make_async_copy(r.frames, r.f4.at[pl.ds(0, area)], load.at[0])
    wr_load = pltpu.make_async_copy(r.w_reduce, r.wr, load.at[1])
    ws_load = pltpu.make_async_copy(r.w_spatial, r.ws, load.at[2])
    we_load = pltpu.make_async_copy(r.w_expand, r.we, load.at[3])
    f_load.start()
    r.f4[area:] = jnp.zeros((r.f4.shape[0] - area, *r.f4.shape[1:]), BF16)
    wr_load.start()
    ws_load.start()
    we_load.start()
    wc = r.wc
    for i in range(3):
        for j in range(3):
            pltpu.make_async_copy(
                r.w_spatial.at[i, j], wc.at[i, :, pl.ds(j * mid, mid)], load.at[4]
            ).start()

    hbm_names = [
        r.gain_a, r.bias_a, r.gain_b, r.bias_b, r.gain_c, r.bias_c,
        r.clip_ids, r.segment_ids, r.slot_valid, r.segment_weight, r.loss_weight,
    ]
    small_loads = [
        pltpu.make_async_copy(src, dst, load.at[5 + q]) for q, (src, dst) in enumerate(zip(hbm_names, r.small))
    ]
    for copy in small_loads[6:10] + small_loads[:6] + small_loads[10:]:
        copy.start()
    (r.gain_a, r.bias_a, r.gain_b, r.bias_b, r.gain_c, r.bias_c,
     r.clip_ids, r.segment_ids, r.slot_valid, r.segment_weight, r.loss_weight) = r.small

    for ref in (r.fp, r.xp, r.g3, r.hb, r.gpc, r.gpa):
        ref[...] = jnp.zeros(ref.shape, ref.dtype)

    for copy in small_loads[6:10]:
        copy.wait()

    valid, clip, segment = r.slot_valid, r.clip_ids, r.segment_ids
    later, alive = [], 1
    for k in range(live):
        alive = alive * valid[k]
        later.append(1 - alive)

    def kept(values, k):
        return values[k] + later[k] * (values[k + 1] - values[k])

    v = [kept(valid, k).astype(F32) for k in range(live)]
    key = [kept(clip, k).astype(F32) for k in range(live)]
    weight = []
    for k in range(live):
        at = kept(segment, k).astype(F32)
        w0, w1, w2 = (r.segment_weight[q] for q in range(3))
        weight.append(
            v[k] * (w0 * ((1.0 - at) * (2.0 - at) * 0.5) + w1 * (at * (2.0 - at)) + w2 * (at * (at - 1.0) * 0.5))
        )
    n_own = (v[0] + v[1] + v[2]) * float(area)

    def block(k, y):
        return pl.multiple_of(k * ROWS + y * SIDE, SIDE)

    mask = lax.broadcasted_iota(jnp.int32, (SIDE, 256), 0) < width

    def fold(value):
        return jnp.sum(jnp.where(mask, value, 0.0), axis=0, keepdims=True)

    def to_dense(ref, at, row0, value, first):
        for q in range(value.shape[1] // 128):
            ref[at, pl.ds(row0 + first + q, 1), :] = value[:, q * 128 : (q + 1) * 128]

    def row_form(ref, row, dense):
        d = r.dense
        count = dense.shape[0]
        d[0:count, :] = dense
        for q in range(count):
            ref[row : row + 1, q * 128 : (q + 1) * 128] = d[q : q + 1, :]

    def dense_of(ref1):
        d = r.dense
        count = ref1.shape[0] // 128
        for q in range(count):
            d[q : q + 1, :] = ref1[q * 128 : (q + 1) * 128].reshape(1, 128)
        return d[0:count, :]

    def by_rows(ref, value):
        def step(k, carry):
            here = pl.ds(pl.multiple_of(k * 256, 256), 256)
            ref[here, :] = value(here)
            return carry

        lax.fori_loop(0, ref.shape[0] // 256, step, 0)

    def moved_rows(here, at):
        return pl.ds(pl.multiple_of(here.start + at, SIDE), 256)

    near_s, near_r, wide_s, wide_r = r.near_s, r.near_r, r.wide_s, r.wide_r

    def one_stage(at):
        return direct and at not in (2, 3)

    def near_at(at):
        return me if one_stage(at) else low

    def near_send(at):
        buf, mine = r.near[at], near_at(at)
        for device in peers if one_stage(at) else low_peers:
            send(buf.at[mine], buf.at[mine], near_s.at[at], near_r.at[at], device)

    def near_wait(at, sems):
        buf = r.near[at]
        wait_bytes(buf.at[pl.ds(0, buf.shape[0] - 1)], sems.at[at])

    def wide_send(at):
        buf = r.wide[at]
        for device in high_peers:
            send(buf.at[high], buf.at[high], wide_s.at[at], wide_r.at[at], device)

    def wide_wait(at, sems):
        wait_bytes(r.wide[at].at[pl.ds(0, outer - 1)], sems.at[at])

    def combine(buf, counts, group, count):
        n_part = [counts(q) for q in range(group)]
        s_part = [buf[q, 0:count, :] for q in range(group)]
        n_all = sum(n_part[1:], n_part[0])
        s_all = sum(s_part[1:], s_part[0])
        mean = s_all / jnp.maximum(n_all, 1.0)
        spread = jnp.zeros((count, 128), F32)
        for q in range(group):
            gap = s_part[q] / jnp.maximum(n_part[q], 1.0) - mean
            spread = spread + (buf[q, count : 2 * count, :] + n_part[q] * gap * gap)
        return n_all, s_all, mean, spread

    counts0 = r.near[0]
    plane = r.plane

    def near_count(q):
        return counts0[(me - low + q) if direct else q, 4:5, :]

    def wide_count(q):
        return plane[q, 0:1, :] if direct else r.wide[0][q, 4:5, :]

    def stats_near(at, count):
        if one_stage(at):
            return
        near_wait(at, near_r)
        n_all, s_all, _, spread = combine(r.near[at], near_count, inner, count)
        buf = r.wide[at]
        buf[high, 0:count, :] = s_all
        buf[high, count : 2 * count, :] = spread
        if at == 0:
            buf[high, 4:5, :] = n_all
        wide_send(at)

    def stats_wide(at, count, table):
        if one_stage(at):
            near_wait(at, near_r)
            n_all, _, mean, spread = combine(r.near[at], lambda q: counts0[q, 4:5, :], n, count)
            if at == 0:
                for q in range(outer):
                    plane[q, 0:1, :] = sum(counts0[q * inner + m, 4:5, :] for m in range(inner))
        else:
            wide_wait(at, wide_r)
            n_all, _, mean, spread = combine(r.wide[at], wide_count, outer, count)
        row_form(table, 0, mean)
        inverse = lax.rsqrt(spread / n_all + EPS)
        row_form(table, 1, inverse)
        return n_all, inverse

    def total(buf):
        out = buf[0]
        for q in range(1, buf.shape[0]):
            out = out + buf[q]
        return out

    def sums_near(at):
        if not one_stage(at):
            near_wait(at, near_r)
            r.wide[at][high] = total(r.near[at])
            wide_send(at)

    def sums_wide(at):
        if one_stage(at):
            near_wait(at, near_r)
            return total(r.near[at])
        wide_wait(at, wide_r)
        return total(r.wide[at])

    def local_stats(at, ref, channels):
        count = channels // 128
        buf = r.near[at]
        for c in range(channels // 256):
            lanes = slice(c * 256, (c + 1) * 256)
            acc = jnp.zeros((SIDE, 256), F32)
            for k in range(live):
                part = lax.fori_loop(
                    0, height, lambda y, a: a + ref[pl.ds(block(k, y), SIDE), lanes],
                    jnp.zeros((SIDE, 256), F32), unroll=height,
                )
                acc = acc + part * v[k]
            s_own = fold(acc)
            mean = s_own / jnp.maximum(n_own, 1.0)
            acc = jnp.zeros((SIDE, 256), F32)
            for k in range(live):
                def square(y, a):
                    gap = ref[pl.ds(block(k, y), SIDE), lanes] - mean
                    return a + gap * gap

                part = lax.fori_loop(0, height, square, jnp.zeros((SIDE, 256), F32), unroll=height)
                acc = acc + part * v[k]
            to_dense(buf, near_at(at), 0, s_own, 2 * c)
            to_dense(buf, near_at(at), count, fold(acc), 2 * c)
        if at == 0:
            buf[near_at(at), 4:5, :] = jnp.full((1, 128), n_own, F32)

    def norm_silu(ref, slope_ref, table, gain, bias, write):
        centre, inverse = table[0:1, :], table[1:2, :]
        g, b = gain[...].reshape(1, mid), bias[...].reshape(1, mid)
        for k in range(live):
            def step(y, carry):
                at = block(k, y)
                hat = (ref[pl.ds(at, SIDE), :] - centre) * inverse
                u = hat * g + b
                s = 0.5 * jnp.tanh(0.5 * u) + 0.5
                h = u * s
                ref[pl.ds(at, SIDE), :] = hat
                slope_ref[pl.ds(at, SIDE), :] = jnp.where(mask, s + (h - h * s), 0.0)
                write(at, jnp.where(mask, h, 0.0))
                return carry

            lax.fori_loop(0, height, step, 0, unroll=7)

    f_load.wait()
    fp, f4 = r.fp, r.f4
    tiles = feat // 128
    group = SIDE // slots
    short = lax.broadcasted_iota(jnp.int32, (SIDE, 128), 0) < width
    keep = [(1 - later[k]).astype(F32) for k in range(live)]
    moved = [later[k].astype(F32) for k in range(live)]

    def regroup(y, carry):
        for p in range(tiles // group):
            value = f4[pl.ds(y * width, SIDE), p * SIDE : (p + 1) * SIDE, :].astype(F32)
            value = jnp.swapaxes(value, 0, 1)
            for q in range(group):
                for k in range(live):
                    row = value[q * slots + k] * keep[k] + value[q * slots + k + 1] * moved[k]
                    lanes = slice((p * group + q) * 128, (p * group + q + 1) * 128)
                    fp[pl.ds(block(k, y), SIDE), lanes] = jnp.where(short, row, 0.0).astype(BF16)
        return carry

    lax.fori_loop(0, height, regroup, 0)
    wr_load.wait()
    wr = r.wr
    hat_a, slope_a = r.hat_a, r.slope_a
    by_rows(hat_a, lambda here: dot(fp[here, :], wr[...]))
    local_stats(0, hat_a, mid)
    pl.semaphore_wait(barrier, len(greeted))
    near_send(0)
    r.ft[...] = fp[...].T
    stats_near(0, mid // 128)
    ws_load.wait()
    we_load.wait()
    wait_bytes(wc, load.at[4])
    ws, we = r.ws, r.we
    for copy in small_loads[:6] + small_loads[10:]:
        copy.wait()
    table_a, table_b, table_c = r.table_a, r.table_b, r.table_c
    n_all, inv_a = stats_wide(0, mid // 128, table_a)
    xp = r.xp

    def three(ref, at, left, middle, right):
        here = pl.ds(at + SIDE, SIDE)
        ref[here, 0:mid] = left.astype(BF16)
        ref[here, mid : 2 * mid] = middle.astype(BF16)
        ref[here, 2 * mid : 3 * mid] = right.astype(BF16)

    def write_a(at, h):
        three(xp, at, pltpu.roll(h, 1, 0), h, pltpu.roll(h, SIDE - 1, 0))

    norm_silu(hat_a, slope_a, table_a, r.gain_a, r.bias_a, write_a)

    hat_b, slope_b, hb = r.hat_b, r.slope_b, r.hb
    by_rows(
        hat_b,
        lambda here: sum(dot(xp[moved_rows(here, i * SIDE), :], ws[i].reshape(3 * mid, mid)) for i in range(3)),
    )
    local_stats(1, hat_b, mid)
    near_send(1)
    xt = r.xt
    xt[...] = xp[SIDE : SIDE + rows, mid : 2 * mid].T
    stats_near(1, mid // 128)
    _, inv_b = stats_wide(1, mid // 128, table_b)

    def write_b(at, h):
        hb[pl.ds(at, SIDE), :] = h.astype(BF16)

    norm_silu(hat_b, slope_b, table_b, r.gain_b, r.bias_b, write_b)

    hat_c, slope_c = r.hat_c, r.slope_c
    by_rows(hat_c, lambda here: dot(hb[here, :], we[...]))
    local_stats(2, hat_c, feat)
    near_send(2)
    hbt = r.hbt
    hbt[...] = hb[...].T
    stats_near(2, feat // 128)
    _, inv_c = stats_wide(2, feat // 128, table_c)

    pool, slope_sum, slope_hat = r.pool, r.slope_sum, r.slope_hat
    for c in range(feat // 256):
        lanes = slice(c * 256, (c + 1) * 256)
        centre, inverse = table_c[0:1, lanes], table_c[1:2, lanes]
        g = r.gain_c[lanes].reshape(1, 256)
        b = r.bias_c[lanes].reshape(1, 256)
        for k in range(live):
            def step(y, carry):
                a0, a1, a2 = carry
                at = block(k, y)
                hat = (hat_c[pl.ds(at, SIDE), lanes] - centre) * inverse
                u = hat * g + b + fp[pl.ds(at, SIDE), lanes].astype(F32)
                s = 0.5 * jnp.tanh(0.5 * u) + 0.5
                h = u * s
                slope = s + (h - h * s)
                hat_c[pl.ds(at, SIDE), lanes] = hat
                slope_c[pl.ds(at, SIDE), lanes] = slope
                return a0 + h, a1 + slope, a2 + slope * hat

            zero = jnp.zeros((SIDE, 256), F32)
            a0, a1, a2 = lax.fori_loop(0, height, step, (zero, zero, zero), unroll=7)
            p_row = (fold(a0) * (1.0 / area)).astype(BF16).astype(F32)
            to_dense(pool, 0, 8 * k, p_row, 2 * c)
            to_dense(slope_sum, k, 0, fold(a1), 2 * c)
            to_dense(slope_hat, k, 0, fold(a2), 2 * c)
    for k in range(live):
        pool[0, 24 + k : 25 + k, :] = jnp.full((1, 128), key[k], F32)
        pool[0, 28 + k : 29 + k, :] = jnp.full((1, 128), weight[k], F32)
    for q, device in enumerate(clip_peers):
        send(pool.at[0], pool.at[q + 1], r.pool_s.at[0], r.pool_r.at[0], device)
    wait_bytes(pool.at[pl.ds(1, len(clip_peers))], r.pool_r.at[0])

    lw = dense_of(r.loss_weight)
    grads = []
    for k in range(live):
        my_key = jnp.full((1, 128), key[k], F32)
        my_weight = jnp.full((1, 128), weight[k], F32)
        mean = jnp.zeros((8, 128), F32)
        den = jnp.zeros((1, 128), F32)
        for q in range(len(clip_peers) + 1):
            for m in range(live):
                match = jnp.where(pool[q, 24 + m : 25 + m, :] == my_key, pool[q, 28 + m : 29 + m, :], 0.0)
                den = den + match
                mean = mean + match * pool[q, 8 * m : 8 * m + 8, :]
        den = jnp.where(den == 0.0, 1.0, den)
        mean = mean / den
        power = jnp.sum(jnp.sum(mean * mean, axis=0, keepdims=True), axis=1, keepdims=True)
        scale = lax.rsqrt(power * (1.0 / feat) + EPS)
        unit = mean * scale
        along = jnp.sum(jnp.sum(unit * lw, axis=0, keepdims=True), axis=1, keepdims=True)
        mean_grad = scale * (lw - unit * (along * (1.0 / feat)))
        grads.append((my_weight / den) * mean_grad * (1.0 / area))

    near3 = r.near[3]
    shift = jnp.zeros((8, 128), F32)
    gain = jnp.zeros((8, 128), F32)
    for k in range(live):
        shift = shift + grads[k] * slope_sum[k]
        gain = gain + grads[k] * slope_hat[k]
    near3[low, 0:8, :] = shift
    near3[low, 8:16, :] = gain
    near_send(3)
    coef = r.coef
    scale_c = dense_of(r.gain_c) * inv_c
    for k in range(live):
        row_form(coef, k, grads[k])
        row_form(coef, 3 + k, grads[k] * scale_c)
    sums_near(3)
    both = sums_wide(3)
    out[0:16, :] = both
    row_form(coef, 6, both[0:8] * scale_c / n_all)
    row_form(coef, 7, both[8:16] * scale_c / n_all)
    gpc = r.gpc
    for k in range(live):
        for c in range(feat // 256):
            lanes = slice(c * 256, (c + 1) * 256)
            c0 = coef[3 + k : 4 + k, lanes]
            c1 = coef[6:7, lanes] * v[k]
            c2 = coef[7:8, lanes] * v[k]

            def step(y, carry):
                at = block(k, y)
                grad = slope_c[pl.ds(at, SIDE), lanes] * c0 - (c1 + hat_c[pl.ds(at, SIDE), lanes] * c2)
                gpc[pl.ds(at, SIDE), lanes] = grad.astype(BF16)
                return carry

            lax.fori_loop(0, height, step, 0, unroll=7)

    def back_sums(at, grad_ref, slope_ref, hat_ref):
        zero = jnp.zeros((SIDE, mid), F32)
        carry = (zero, zero)
        for k in range(live):
            def step(y, c):
                here = pl.ds(block(k, y), SIDE)
                grad = grad_ref[here, :] * slope_ref[here, :]
                grad_ref[here, :] = grad
                return c[0] + grad, c[1] + grad * hat_ref[here, :]

            carry = lax.fori_loop(0, height, step, carry, unroll=7)
        buf = r.near[at]
        to_dense(buf, near_at(at), 0, jnp.sum(carry[0], axis=0, keepdims=True), 0)
        to_dense(buf, near_at(at), 2, jnp.sum(carry[1], axis=0, keepdims=True), 0)

    def back_apply(at, table, gain_ref, inv, grad_ref, hat_ref, write):
        both = sums_wide(at)
        out[8 * at - 16 : 8 * at - 12, :] = both[0:4]
        scale = dense_of(gain_ref) * inv
        row_form(table, 2, scale)
        row_form(table, 3, both[0:2] * scale / n_all)
        row_form(table, 4, both[2:4] * scale / n_all)
        for k in range(live):
            c0, c1, c2 = table[2:3, :], table[3:4, :] * v[k], table[4:5, :] * v[k]

            def step(y, carry):
                at_row = block(k, y)
                here = pl.ds(at_row, SIDE)
                write(at_row, grad_ref[here, :] * c0 - (c1 + hat_ref[here, :] * c2))
                return carry

            lax.fori_loop(0, height, step, 0, unroll=7)

    core, bit_x, bit_y, at_z = me % 2, (me // 2) % 2, (me // 4) % 2, (me // 8) % quad
    at_far = me // (8 * quad)
    bit1 = bit_x + core * (bit_y - bit_x)
    bit2 = bit_y + core * (bit_x - bit_y)
    sibling = me + 1 - 2 * core
    peer1 = me + (1 - 2 * bit1) * (2 + 2 * core)
    peer2 = me + (1 - 2 * bit2) * (4 - 2 * core)
    z_at = [(at_z + o) % quad for o in range(1, quad)]
    z_peer = [me + 8 * (q - at_z) for q in z_at]
    far_peer = [me + 8 * quad * ((at_far + o) % far - at_far) for o in range(1, far)]
    chunk_s, chunk_r = r.chunk_s, r.chunk_r
    waits = []

    def chunk(q):
        part, whole = r.part[q], r.whole[q]
        size = part.shape[0]
        half, quarter, eighth, piece = size // 2, size // 4, size // 8, size // (8 * quad)
        m8 = lambda value: pl.multiple_of(value, 8)
        at_h = m8(core * half)
        at_q = m8(at_h + bit1 * quarter)
        at_e = m8(at_q + bit2 * eighth)
        at_p = m8(at_e + at_z * piece)

        def go(step, src, dst, device):
            send(src, dst, chunk_s.at[q, step], chunk_r.at[q, step], device)

        def finish(step, ref):
            wait_bytes(ref, chunk_r.at[q, step])
            waits.append((ref, chunk_s.at[q, step]))

        rb0, rb1, rb2, rb3 = r.rb0[q], r.rb1[q], r.rb2[q], r.rb3[q]
        go(0, part.at[pl.ds(m8((1 - core) * half), half)], rb0, sibling)
        yield
        finish(0, rb0)
        part[pl.ds(at_h, half), :] = part[pl.ds(at_h, half), :] + rb0[...]
        go(1, part.at[pl.ds(m8(at_h + (1 - bit1) * quarter), quarter)], rb1, peer1)
        yield
        finish(1, rb1)
        part[pl.ds(at_q, quarter), :] = part[pl.ds(at_q, quarter), :] + rb1[...]
        go(2, part.at[pl.ds(m8(at_q + (1 - bit2) * eighth), eighth)], rb2, peer2)
        yield
        finish(2, rb2)
        part[pl.ds(at_e, eighth), :] = part[pl.ds(at_e, eighth), :] + rb2[...]
        for o in range(quad - 1):
            go(3, part.at[pl.ds(m8(at_e + z_at[o] * piece), piece)], rb3.at[pl.ds(o * piece, piece)], z_peer[o])
        yield
        finish(3, rb3)
        own = part[pl.ds(at_p, piece), :]
        for o in range(quad - 1):
            own = own + rb3[o * piece : (o + 1) * piece, :]
        if far > 1:
            rb4 = r.rb4[q]
            rb4[at_far] = own
            for device in far_peer:
                go(8, rb4.at[at_far], rb4.at[at_far], device)
            yield
            finish(8, rb4.at[pl.ds(0, far - 1)])
            own = rb4[0]
            for o in range(1, far):
                own = own + rb4[o]
        whole[pl.ds(at_p, piece), :] = own
        for o in range(quad - 1):
            go(4, whole.at[pl.ds(at_p, piece)], whole.at[pl.ds(at_p, piece)], z_peer[o])
        yield
        finish(4, whole.at[pl.ds(0, (quad - 1) * piece)])
        go(5, whole.at[pl.ds(at_e, eighth)], whole.at[pl.ds(at_e, eighth)], peer2)
        yield
        finish(5, whole.at[pl.ds(0, eighth)])
        go(6, whole.at[pl.ds(at_q, quarter)], whole.at[pl.ds(at_q, quarter)], peer1)
        yield
        finish(6, whole.at[pl.ds(0, quarter)])
        go(7, whole.at[pl.ds(at_h, half)], whole.at[pl.ds(at_h, half)], sibling)
        yield
        finish(7, whole.at[pl.ds(0, half)])
        yield

    chunks = [chunk(q) for q in range(5)]

    def go_on(*which):
        for name in which:
            next(chunks[name], None)

    def spread_lanes(ref, value):
        height_of = value.shape[0]
        for q in range(value.shape[1] // 128):
            ref[q * height_of : (q + 1) * height_of, :] = value[:, q * 128 : (q + 1) * 128]

    grad_b, grad_a = r.grad_b, r.grad_a
    by_rows(grad_b, lambda here: dot(gpc[here, :], we[...], NT))
    back_sums(4, grad_b, slope_b, hat_b)
    near_send(4)

    def expand_part(q, carry):
        lanes = pl.ds(pl.multiple_of(q * 256, 256), 256)
        value = dot(hbt[...], gpc[:, lanes])
        for m in range(2):
            r.part[E][pl.ds(pl.multiple_of((2 * q + m) * mid, mid), mid), :] = value[:, m * 128 : (m + 1) * 128]
        return carry

    lax.fori_loop(0, feat // 256, expand_part, 0)
    go_on(E)
    sums_near(4)
    go_on(E)
    g3 = r.g3

    def write_gb(at, grad):
        grad = jnp.where(mask, grad, 0.0)
        three(g3, at, pltpu.roll(grad, SIDE - 1, 0), grad, pltpu.roll(grad, 1, 0))

    back_apply(4, table_b, r.gain_b, inv_b, grad_b, hat_b, write_gb)
    go_on(E)
    by_rows(
        grad_a, lambda here: sum(dot(g3[moved_rows(here, (2 - i) * SIDE), :], wc[i], NT) for i in range(3))
    )
    back_sums(5, grad_a, slope_a, hat_a)
    near_send(5)
    for i in range(3):
        spread_lanes(r.part[S0 + i], dot(xt[...], g3[(2 - i) * SIDE : (2 - i) * SIDE + rows, :]))
        go_on(S0 + i)
    go_on(E)
    sums_near(5)
    gpa = r.gpa

    def write_ga(at, grad):
        gpa[pl.ds(at, SIDE), :] = grad.astype(BF16)

    back_apply(5, table_a, r.gain_a, inv_a, grad_a, hat_a, write_ga)

    def reduce_part(q, carry):
        here = pl.ds(pl.multiple_of(q * 256, 256), 256)
        value = dot(r.ft[here, :], gpa[...])
        for m in range(mid // 128):
            r.part[R][pl.ds(pl.multiple_of(q * 256 + m * feat, 256), 256), :] = value[:, m * 128 : (m + 1) * 128]
        return carry

    lax.fori_loop(0, feat // 256, reduce_part, 0)
    go_on(R)
    go_on(S0, S1, E, S2)

    by_rows(hat_c, lambda here: dot(gpa[here, :], wr[...], NT))
    go_on(E, S0, S1, S2, R)
    gf = r.gf

    def blend(y, carry):
        for p in range(tiles // group):
            values = []
            for q in range(group):
                lanes = slice((p * group + q) * 128, (p * group + q + 1) * 128)
                terms = [
                    slope_c[pl.ds(block(k, y), SIDE), lanes] * coef[k : k + 1, lanes]
                    + hat_c[pl.ds(block(k, y), SIDE), lanes]
                    for k in range(live)
                ]
                values.append(terms[0] * keep[0])
                for m in range(1, live):
                    values.append(terms[m] * keep[m] + terms[m - 1] * moved[m - 1])
                values.append(terms[live - 1] * moved[live - 1])
            value = jnp.swapaxes(jnp.stack(values), 0, 1)
            gf[pl.ds(y * width, width), p * SIDE : (p + 1) * SIDE, :] = value[0:width].astype(BF16)
        return carry

    for part in range(2):
        lax.fori_loop(part * height // 2, (part + 1) * height // 2, blend, 0)
        go_on(E, S0, S1, S2, R)

    for _ in range(12):
        go_on(E, S0, S1, S2, R)

    for at in range(6):
        near_wait(at, near_s)
        if not one_stage(at):
            wide_wait(at, wide_s)
    wait_bytes(pool.at[pl.ds(1, len(clip_peers))], r.pool_s.at[0])
    for ref, sem in waits:
        wait_bytes(ref, sem)


def store(gf, vectors, expand, s0, s1, s2, reduce, frames_out, reduce_out, spatial_out, expand_out, *rest):
    ga, ba, gb, bb, gc, bc, sem = rest
    pltpu.make_async_copy(gf, frames_out, sem.at[0]).start()
    depth, width = reduce_out.shape
    for q in range(width // 128):
        pltpu.make_async_copy(
            reduce.at[pl.ds(q * depth, depth)], reduce_out.at[:, pl.ds(q * 128, 128)], sem.at[1]
        ).start()
    depth, width = expand_out.shape
    for q in range(width // 128):
        pltpu.make_async_copy(
            expand.at[pl.ds(q * depth, depth)], expand_out.at[:, pl.ds(q * 128, 128)], sem.at[2]
        ).start()
    for i, part in enumerate((s0, s1, s2)):
        for q in range(part.shape[0] // depth):
            pltpu.make_async_copy(
                part.at[pl.ds(q * depth, depth)],
                spatial_out.at[i, q * 128 // depth, :, pl.ds(q * 128 % depth, 128)],
                sem.at[3 + i],
            ).start()
    for ref, first in ((bc, 0), (gc, 8), (bb, 16), (gb, 18), (ba, 24), (ga, 26)):
        for q in range(ref.shape[0] // 128):
            ref[q * 128 : (q + 1) * 128] = vectors[first + q : first + q + 1, :].reshape(128)
    wait_bytes(gf, sem.at[0])
    wait_bytes(reduce, sem.at[1])
    wait_bytes(expand, sem.at[2])
    for i, part in enumerate((s0, s1, s2)):
        wait_bytes(part, sem.at[3 + i])


def solution(mesh):
    n = mesh.shape["clip"]

    def shards(*args):
        slots, height, width, feat = args[0].shape
        mid = args[1].shape[1]
        live = slots - 1
        rows = live * ROWS
        outer = n // 8
        quad = min(4, outer)
        far = outer // quad
        flat_shape = (height * width, slots * feat // 128, 128)
        hbm = pl.BlockSpec(memory_space=pltpu.HBM)
        vmem = pl.BlockSpec(memory_space=pltpu.VMEM)
        dma = pltpu.SemaphoreType.DMA
        matrix, third = mid * feat // 128, 3 * mid * mid // 128
        depths = list(enumerate((8, 4, 16, 16, 4, 4)))
        sizes = [matrix, third, third, third, matrix]
        scratch = dict(
            f4=pltpu.VMEM((flat_shape[0] + SIDE - width, *flat_shape[1:]), BF16),
            fp=pltpu.VMEM((rows, feat), BF16),
            ft=pltpu.VMEM((feat, rows), BF16),
            wr=pltpu.VMEM((feat, mid), BF16),
            ws=pltpu.VMEM((3, 3, mid, mid), BF16),
            wc=pltpu.VMEM((3, mid, 3 * mid), BF16),
            we=pltpu.VMEM((mid, feat), BF16),
            hat_a=pltpu.VMEM((rows, mid), F32),
            slope_a=pltpu.VMEM((rows, mid), F32),
            grad_a=pltpu.VMEM((rows, mid), F32),
            hat_b=pltpu.VMEM((rows, mid), F32),
            slope_b=pltpu.VMEM((rows, mid), F32),
            grad_b=pltpu.VMEM((rows, mid), F32),
            xp=pltpu.VMEM((rows + 2 * SIDE, 3 * mid), BF16),
            xt=pltpu.VMEM((mid, rows), BF16),
            hb=pltpu.VMEM((rows, mid), BF16),
            hbt=pltpu.VMEM((mid, rows), BF16),
            hat_c=pltpu.VMEM((rows, feat), F32),
            slope_c=pltpu.VMEM((rows, feat), F32),
            gpc=pltpu.VMEM((rows, feat), BF16),
            g3=pltpu.VMEM((rows + 2 * SIDE, 3 * mid), BF16),
            gpa=pltpu.VMEM((rows, mid), BF16),
            table_a=pltpu.VMEM((8, mid), F32),
            table_b=pltpu.VMEM((8, mid), F32),
            table_c=pltpu.VMEM((8, feat), F32),
            coef=pltpu.VMEM((8, feat), F32),
            dense=pltpu.VMEM((8, 128), F32),
            pool=pltpu.VMEM((6, 32, 128), F32),
            slope_sum=pltpu.VMEM((live, 8, 128), F32),
            slope_hat=pltpu.VMEM((live, 8, 128), F32),
            near=[pltpu.VMEM((n if n <= 32 and at not in (2, 3) else 8, deep, 128), F32) for at, deep in depths],
            wide=[pltpu.VMEM((outer, deep, 128), F32) for at, deep in depths],
            plane=pltpu.VMEM((outer, 8, 128), F32),
            part=[pltpu.VMEM((size, 128), F32) for size in sizes],
            rb0=[pltpu.VMEM((size // 2, 128), F32) for size in sizes],
            rb1=[pltpu.VMEM((size // 4, 128), F32) for size in sizes],
            rb2=[pltpu.VMEM((size // 8, 128), F32) for size in sizes],
            rb3=[pltpu.VMEM(((quad - 1) * size // (8 * quad), 128), F32) for size in sizes],
            rb4=[pltpu.VMEM((far, size // (8 * quad), 128), F32) for size in sizes if far > 1],
            small=[
                *(pltpu.VMEM((c,), F32) for c in (mid, mid, mid, mid, feat, feat)),
                *(pltpu.SMEM((slots,), jnp.int32) for _ in range(3)),
                pltpu.SMEM(args[13].shape, F32),
                pltpu.VMEM((feat,), F32),
            ],
            load_sem=dma((16,)),
            near_s=dma((6,)),
            near_r=dma((6,)),
            wide_s=dma((6,)),
            wide_r=dma((6,)),
            pool_s=dma((1,)),
            pool_r=dma((1,)),
            chunk_s=dma((5, 9)),
            chunk_r=dma((5, 9)),
        )
        ins = dict(
            frames=hbm, w_reduce=hbm, w_spatial=hbm, w_expand=hbm,
            gain_a=hbm, bias_a=hbm, gain_b=hbm, bias_b=hbm, gain_c=hbm, bias_c=hbm,
            clip_ids=hbm, segment_ids=hbm, slot_valid=hbm, segment_weight=hbm, loss_weight=hbm,
        )
        outs = dict(gf=pltpu.VMEM(flat_shape, BF16), vectors=pltpu.VMEM((32, 128), F32))
        names = (*ins, *outs, *scratch)
        whole = [pltpu.VMEM((size, 128), F32) for size in sizes]
        tiled = args[0].transpose(1, 2, 0, 3).reshape(height, width, slots, feat // 128, 128)
        tiled = tiled.transpose(0, 1, 3, 2, 4).reshape(flat_shape)
        results = pl.pallas_call(
            functools.partial(kernel, (names, len(ins) + len(outs), n, slots, height, width, feat, mid)),
            out_shape=[*outs.values(), *whole],
            in_specs=list(ins.values()),
            out_specs=[vmem] * (len(outs) + len(whole)),
            scratch_shapes=list(scratch.values()),
            compiler_params=pltpu.CompilerParams(
                collective_id=0, has_side_effects=True, vmem_limit_bytes=48 * 1024 * 1024
            ),
            cost_estimate=pl.CostEstimate(flops=5_200_000_000, bytes_accessed=12_000_000, transcendentals=1_500_000),
        )(*(pltpu.with_memory_space_constraint(part, pltpu.HBM) for part in (tiled, *args[1:])))
        vector = jax.ShapeDtypeStruct((mid,), F32)
        wide_vector = jax.ShapeDtypeStruct((feat,), F32)
        flat_grad, *rest = pl.pallas_call(
            store,
            out_shape=[
                jax.ShapeDtypeStruct(flat_shape, BF16),
                jax.ShapeDtypeStruct((feat, mid), F32),
                jax.ShapeDtypeStruct((3, 3, mid, mid), F32),
                jax.ShapeDtypeStruct((mid, feat), F32),
                vector, vector, vector, vector, wide_vector, wide_vector,
            ],
            in_specs=[vmem] * 7,
            out_specs=[hbm] * 4 + [vmem] * 6,
            scratch_shapes=[dma((6,))],
            compiler_params=pltpu.CompilerParams(vmem_limit_bytes=8 * 1024 * 1024),
        )(*(pltpu.with_memory_space_constraint(part, pltpu.VMEM) for part in results))
        grad_frames = flat_grad.reshape(height, width, feat // 128, slots, 128).transpose(0, 1, 3, 2, 4)
        return grad_frames.reshape(height, width, slots, feat).transpose(2, 0, 1, 3), *rest

    split = P("clip")
    in_specs = (split,) + (P(),) * 9 + (split,) * 3 + (P(), P())
    out_specs = (split,) + (P(),) * 9
    return jax.shard_map(shards, mesh=mesh, in_specs=in_specs, out_specs=out_specs, check_vma=False)
```

```python
import functools
from types import SimpleNamespace

import jax
import jax.numpy as jnp
from jax import lax
from jax.experimental import pallas as pl
from jax.experimental.pallas import tpu as pltpu
from jax.sharding import PartitionSpec as P

MESH = pl.DeviceIdType.MESH
EPS = 1e-05
F32 = jnp.float32
BF16 = jnp.bfloat16
SIDE = 16
ROWS = SIDE * SIDE
NN = (((1,), (0,)), ((), ()))
NT = (((1,), (1,)), ((), ()))
E, S0, S1, S2, R = range(5)


def dot(a, b, dims=NN):
    return lax.dot_general(a, b, dims, preferred_element_type=F32)


def wait_bytes(ref, sem):
    pltpu.make_async_copy(ref, ref, sem).wait()


def spread_lanes(ref, value):
    depth = value.shape[0]
    for q in range(value.shape[1] // 128):
        ref[q * depth : (q + 1) * depth, :] = value[:, q * 128 : (q + 1) * 128]


def by_rows(ref, value):
    def step(k, carry):
        here = pl.ds(pl.multiple_of(k * 256, 256), 256)
        ref[here, :] = value(here)
        return carry

    lax.fori_loop(0, ref.shape[0] // 256, step, 0)


def moved_rows(here, at):
    return pl.ds(pl.multiple_of(here.start + at, SIDE), 256)


def block(k, y):
    return pl.multiple_of(k * ROWS + y * SIDE, SIDE)


def to_dense(ref, at, value, first):
    for q in range(value.shape[1] // 128):
        ref[at, pl.ds(first + q, 1), :] = value[:, q * 128 : (q + 1) * 128]


def row_form(ref, row, source, first, count):
    for q in range(count):
        ref[row : row + 1, q * 128 : (q + 1) * 128] = source[first + q : first + q + 1, :]


def three(ref, at, left, middle, right):
    here, wide = pl.ds(at + SIDE, SIDE), middle.shape[1]
    ref[here, 0:wide] = left.astype(BF16)
    ref[here, wide : 2 * wide] = middle.astype(BF16)
    ref[here, 2 * wide : 3 * wide] = right.astype(BF16)


def dense_of(ref1, scratch):
    count = ref1.shape[0] // 128
    for q in range(count):
        scratch[q : q + 1, :] = ref1[q * 128 : (q + 1) * 128].reshape(1, 128)
    return scratch[0:count, :]


class Step:
    def __init__(self, cfg, r):
        self.r, self.sizes = r, cfg
        self.n, self.slots, self.height, self.width, self.feat, self.mid = cfg
        self.live = self.slots - 1
        self.rows = self.live * ROWS
        self.area = self.height * self.width
        self.inner = 8
        self.outer = self.n // 8
        self.quad = min(4, self.outer)
        self.far = self.outer // self.quad
        self.loads = {}
        self.mask = lax.broadcasted_iota(jnp.int32, (SIDE, 256), 0) < self.width

    def load(self, **pairs):
        for name, (src, dst) in pairs.items():
            copy = pltpu.make_async_copy(src, dst, self.r.load_sem.at[len(self.loads)])
            copy.start()
            self.loads[name] = copy

    def loaded(self, **names):
        for name in names:
            self.loads[name].wait()

    def fold(self, value):
        return jnp.sum(jnp.where(self.mask, value, 0.0), axis=0, keepdims=True)

    def slot_facts(self):
        r, live = self.r, self.live
        alive, later = 1, []
        for k in range(live):
            alive = alive * r.valid[k]
            later.append(1 - alive)
        self.keep = [(1 - q).astype(F32) for q in later]
        self.moved = [q.astype(F32) for q in later]
        self.later = later
        self.v = [self.kept(r.valid, k) for k in range(live)]
        self.n_own = (self.v[0] + self.v[1] + self.v[2]) * float(self.area)

    def kept(self, values, k):
        return (values[k] + self.later[k] * (values[k + 1] - values[k])).astype(F32)

    def places(self):
        n = self.n
        self.me = me = lax.axis_index("clip")
        self.low, self.high = low, high = me % self.inner, me // self.inner
        self.direct = n <= 32
        self.peers = [(me + o) % n for o in range(1, n)]
        self.low_peers = [me - low + (low + o) % self.inner for o in range(1, self.inner)]
        self.high_peers = [low + self.inner * ((high + o) % self.outer) for o in range(1, self.outer)]
        self.clip_peers = [(me + o) % n for o in (1, n - 1, n // 2, n // 2 - 1, n // 2 + 1)]

    def greet(self):
        self.greeted = self.peers if self.direct else self.low_peers + self.high_peers + self.clip_peers
        self.barrier = pltpu.get_barrier_semaphore()
        for device in self.greeted:
            pl.semaphore_signal(self.barrier, inc=1, device_id=(device,), device_id_type=MESH)

    def all_here(self):
        pl.semaphore_wait(self.barrier, len(self.greeted))

    def send(self, src, dst, ssem, rsem, device):
        pltpu.make_async_remote_copy(
            src_ref=src, dst_ref=dst, send_sem=ssem, recv_sem=rsem, device_id=(device,), device_id_type=MESH
        ).start()

    def one_stage(self, at):
        return self.direct and at not in (2, 3)

    def near_at(self, at):
        return self.me if self.one_stage(at) else self.low

    def near_send(self, at):
        buf, mine = self.r.near[at], self.near_at(at)
        for device in self.peers if self.one_stage(at) else self.low_peers:
            self.send(buf.at[mine], buf.at[mine], self.r.near_s.at[at], self.r.near_r.at[at], device)

    def near_wait(self, at, sems):
        buf = self.r.near[at]
        wait_bytes(buf.at[pl.ds(0, buf.shape[0] - 1)], sems.at[at])

    def wide_send(self, at):
        buf = self.r.wide[at]
        for device in self.high_peers:
            self.send(buf.at[self.high], buf.at[self.high], self.r.wide_s.at[at], self.r.wide_r.at[at], device)

    def wide_wait(self, at, sems):
        wait_bytes(self.r.wide[at].at[pl.ds(0, self.outer - 1)], sems.at[at])

    def all_sent(self, *rounds):
        for at in rounds:
            self.near_wait(at, self.r.near_s)
            if not self.one_stage(at):
                self.wide_wait(at, self.r.wide_s)

    def near_count(self, q):
        return self.r.near[0][(self.me - self.low + q) if self.direct else q, 4:5, :]

    def wide_count(self, q):
        return self.r.plane[q, 0:1, :] if self.direct else self.r.wide[0][q, 4:5, :]

    def stats_near(self, at, count):
        if self.one_stage(at):
            return
        self.near_wait(at, self.r.near_r)
        n_all, s_all, _, spread = combine(self.r.near[at], self.near_count, self.inner, count)
        buf = self.r.wide[at]
        buf[self.high, 0:count, :] = s_all
        buf[self.high, count : 2 * count, :] = spread
        if at == 0:
            buf[self.high, 4:5, :] = n_all
        self.wide_send(at)

    def stats_wide(self, at, count, table):
        r = self.r
        if self.one_stage(at):
            self.near_wait(at, r.near_r)
            counts = r.near[0]
            n_all, _, mean, spread = combine(r.near[at], lambda q: counts[q, 4:5, :], self.n, count)
            if at == 0:
                for q in range(self.outer):
                    r.plane[q, 0:1, :] = sum(counts[q * self.inner + m, 4:5, :] for m in range(self.inner))
        else:
            self.wide_wait(at, r.wide_r)
            n_all, _, mean, spread = combine(r.wide[at], self.wide_count, self.outer, count)
        inverse = lax.rsqrt(spread / n_all + EPS)
        r.dense[0:count, :] = mean
        row_form(table, 0, r.dense, 0, count)
        r.dense[0:count, :] = inverse
        row_form(table, 1, r.dense, 0, count)
        return n_all, inverse

    def sums_near(self, at):
        if not self.one_stage(at):
            self.near_wait(at, self.r.near_r)
            self.r.wide[at][self.high] = total(self.r.near[at])
            self.wide_send(at)

    def sums_wide(self, at):
        if self.one_stage(at):
            self.near_wait(at, self.r.near_r)
            return total(self.r.near[at])
        self.wide_wait(at, self.r.wide_r)
        return total(self.r.wide[at])

    def local_stats(self, buf, at, ref):
        channels = ref.shape[1]
        count = channels // 128
        for c in range(channels // 256):
            lanes = slice(c * 256, (c + 1) * 256)

            def gather(term):
                acc = jnp.zeros((SIDE, 256), F32)
                for k in range(self.live):
                    part = lax.fori_loop(
                        0, self.height, lambda y, a: a + term(ref[pl.ds(block(k, y), SIDE), lanes]),
                        jnp.zeros((SIDE, 256), F32), unroll=self.height,
                    )
                    acc = acc + part * self.v[k]
                return self.fold(acc)

            s_own = gather(lambda x: x)
            mean = s_own / jnp.maximum(self.n_own, 1.0)
            to_dense(buf, at, s_own, 2 * c)
            to_dense(buf, at, gather(lambda x: (x - mean) * (x - mean)), count + 2 * c)

    def norm_silu(self, ref, slope_ref, table, gain, bias, write):
        centre, inverse = table[0:1, :], table[1:2, :]
        g, b = gain[...].reshape(1, self.mid), bias[...].reshape(1, self.mid)
        for k in range(self.live):
            def step(y, carry):
                at = block(k, y)
                hat = (ref[pl.ds(at, SIDE), :] - centre) * inverse
                u = hat * g + b
                s = 0.5 * jnp.tanh(0.5 * u) + 0.5
                h = u * s
                ref[pl.ds(at, SIDE), :] = hat
                slope_ref[pl.ds(at, SIDE), :] = jnp.where(self.mask, s + (h - h * s), 0.0)
                write(at, jnp.where(self.mask, h, 0.0))
                return carry

            lax.fori_loop(0, self.height, step, 0, unroll=7)


def combine(buf, counts, group, count):
    n_part = [counts(q) for q in range(group)]
    s_part = [buf[q, 0:count, :] for q in range(group)]
    n_all = sum(n_part[1:], n_part[0])
    s_all = sum(s_part[1:], s_part[0])
    mean = s_all / jnp.maximum(n_all, 1.0)
    spread = jnp.zeros((count, 128), F32)
    for q in range(group):
        gap = s_part[q] / jnp.maximum(n_part[q], 1.0) - mean
        spread = spread + (buf[q, count : 2 * count, :] + n_part[q] * gap * gap)
    return n_all, s_all, mean, spread


def total(buf):
    out = buf[0]
    for q in range(1, buf.shape[0]):
        out = out + buf[q]
    return out


def clear(*refs):
    for ref in refs:
        ref[...] = jnp.zeros(ref.shape, ref.dtype)


def prologue(t):
    r, slots, live, width, feat = t.r, t.slots, t.live, t.width, t.feat
    t.load(valid=(r.slot_valid, r.valid), frames=(r.frames, r.f4.at[pl.ds(0, t.area)]), reduce=(r.w_reduce, r.wr))
    r.f4[t.area :] = jnp.zeros((r.f4.shape[0] - t.area, *r.f4.shape[1:]), BF16)
    clear(r.fp)
    t.loaded(valid=0)
    t.slot_facts()
    t.loaded(frames=0)
    fp, f4 = r.fp, r.f4
    tiles = feat // 128
    group = SIDE // slots
    short = lax.broadcasted_iota(jnp.int32, (SIDE, 128), 0) < width

    def regroup(y, carry):
        for p in range(tiles // group):
            value = f4[pl.ds(y * width, SIDE), p * SIDE : (p + 1) * SIDE, :].astype(F32)
            value = jnp.swapaxes(value, 0, 1)
            for q in range(group):
                for k in range(live):
                    row = value[q * slots + k] * t.keep[k] + value[q * slots + k + 1] * t.moved[k]
                    lanes = slice((p * group + q) * 128, (p * group + q + 1) * 128)
                    fp[pl.ds(block(k, y), SIDE), lanes] = jnp.where(short, row, 0.0).astype(BF16)
        return carry

    lax.fori_loop(0, t.height, regroup, 0)
    t.loaded(reduce=0)
    by_rows(r.hat_a, lambda here: dot(fp[here, :], r.wr[...]))
    t.local_stats(r.first, 0, r.hat_a)
    r.first[0, 4:5, :] = jnp.full((1, 128), t.n_own, F32)


def forward(t):
    r, live, mid, feat, rows, area, height = t.r, t.live, t.mid, t.feat, t.rows, t.area, t.height
    t.places()
    t.greet()
    t.load(
        valid=(r.slot_valid, r.valid), clip=(r.clip_ids, r.clip), segment=(r.segment_ids, r.segment),
        share=(r.segment_weight, r.share), spatial=(r.w_spatial, r.ws), expand=(r.w_expand, r.we),
        ga=(r.gain_a, r.ga), ba=(r.bias_a, r.ba), gb=(r.gain_b, r.gb), bb=(r.bias_b, r.bb),
        gc=(r.gain_c, r.gc), bc=(r.bias_c, r.bc), loss=(r.loss_weight, r.loss),
    )
    r.near[0][t.near_at(0)] = r.first[0]
    t.all_here()
    t.near_send(0)
    r.ft[...] = r.fp[...].T
    t.stats_near(0, mid // 128)
    clear(r.xp, r.hb)
    t.loaded(valid=0, clip=0, segment=0, share=0, ga=0, ba=0, gb=0, bb=0, gc=0, bc=0, loss=0, spatial=0, expand=0)
    t.slot_facts()
    key = [t.kept(r.clip, k) for k in range(live)]
    weight = []
    for k in range(live):
        at = t.kept(r.segment, k)
        w0, w1, w2 = (r.share[q] for q in range(3))
        weight.append(
            t.v[k] * (w0 * ((1.0 - at) * (2.0 - at) * 0.5) + w1 * (at * (2.0 - at)) + w2 * (at * (at - 1.0) * 0.5))
        )
    n_all, inv_a = t.stats_wide(0, mid // 128, r.table_a)
    r.facts[0:1, :] = n_all
    r.facts[8 : 8 + mid // 128, :] = inv_a

    xp, hb = r.xp, r.hb

    def write_a(at, h):
        three(xp, at, pltpu.roll(h, 1, 0), h, pltpu.roll(h, SIDE - 1, 0))

    r.hat_a[...] = r.pre_a[...]
    t.norm_silu(r.hat_a, r.slope_a, r.table_a, r.ga, r.ba, write_a)

    by_rows(
        r.hat_b,
        lambda here: sum(dot(xp[moved_rows(here, i * SIDE), :], r.ws[i].reshape(3 * mid, mid)) for i in range(3)),
    )
    t.local_stats(r.near[1], t.near_at(1), r.hat_b)
    t.near_send(1)
    r.xt[...] = xp[SIDE : SIDE + rows, mid : 2 * mid].T
    t.stats_near(1, mid // 128)
    _, inv_b = t.stats_wide(1, mid // 128, r.table_b)
    r.facts[16 : 16 + mid // 128, :] = inv_b

    def write_b(at, h):
        hb[pl.ds(at, SIDE), :] = h.astype(BF16)

    t.norm_silu(r.hat_b, r.slope_b, r.table_b, r.gb, r.bb, write_b)

    hat_c, slope_c, fp, table_c = r.hat_c, r.slope_c, r.fp, r.table_c
    by_rows(hat_c, lambda here: dot(hb[here, :], r.we[...]))
    t.local_stats(r.near[2], t.near_at(2), hat_c)
    t.near_send(2)
    r.hbt[...] = hb[...].T
    t.stats_near(2, feat // 128)
    _, inv_c = t.stats_wide(2, feat // 128, table_c)

    pool, slope_sum, slope_hat = r.pool, r.slope_sum, r.slope_hat
    for c in range(feat // 256):
        lanes = slice(c * 256, (c + 1) * 256)
        centre, inverse = table_c[0:1, lanes], table_c[1:2, lanes]
        g = r.gc[lanes].reshape(1, 256)
        b = r.bc[lanes].reshape(1, 256)
        for k in range(live):
            def step(y, carry):
                a0, a1, a2 = carry
                at = block(k, y)
                hat = (hat_c[pl.ds(at, SIDE), lanes] - centre) * inverse
                u = hat * g + b + fp[pl.ds(at, SIDE), lanes].astype(F32)
                s = 0.5 * jnp.tanh(0.5 * u) + 0.5
                h = u * s
                slope = s + (h - h * s)
                hat_c[pl.ds(at, SIDE), lanes] = hat
                slope_c[pl.ds(at, SIDE), lanes] = slope
                return a0 + h, a1 + slope, a2 + slope * hat

            zero = jnp.zeros((SIDE, 256), F32)
            a0, a1, a2 = lax.fori_loop(0, height, step, (zero, zero, zero), unroll=7)
            p_row = (t.fold(a0) * (1.0 / area)).astype(BF16).astype(F32)
            to_dense(pool, 0, p_row, 8 * k + 2 * c)
            to_dense(slope_sum, k, t.fold(a1), 2 * c)
            to_dense(slope_hat, k, t.fold(a2), 2 * c)
    for k in range(live):
        pool[0, 24 + k : 25 + k, :] = jnp.full((1, 128), key[k], F32)
        pool[0, 28 + k : 29 + k, :] = jnp.full((1, 128), weight[k], F32)
    for q, device in enumerate(t.clip_peers):
        t.send(pool.at[0], pool.at[q + 1], r.pool_s.at[0], r.pool_r.at[0], device)
    wait_bytes(pool.at[pl.ds(1, len(t.clip_peers))], r.pool_r.at[0])

    lw = dense_of(r.loss, r.dense)
    grads = []
    for k in range(live):
        my_key = jnp.full((1, 128), key[k], F32)
        my_weight = jnp.full((1, 128), weight[k], F32)
        mean = jnp.zeros((8, 128), F32)
        den = jnp.zeros((1, 128), F32)
        for q in range(len(t.clip_peers) + 1):
            for m in range(live):
                match = jnp.where(pool[q, 24 + m : 25 + m, :] == my_key, pool[q, 28 + m : 29 + m, :], 0.0)
                den = den + match
                mean = mean + match * pool[q, 8 * m : 8 * m + 8, :]
        den = jnp.where(den == 0.0, 1.0, den)
        mean = mean / den
        power = jnp.sum(jnp.sum(mean * mean, axis=0, keepdims=True), axis=1, keepdims=True)
        scale = lax.rsqrt(power * (1.0 / feat) + EPS)
        unit = mean * scale
        along = jnp.sum(jnp.sum(unit * lw, axis=0, keepdims=True), axis=1, keepdims=True)
        mean_grad = scale * (lw - unit * (along * (1.0 / feat)))
        grads.append((my_weight / den) * mean_grad * (1.0 / area))

    near3 = r.near[3]
    shift = jnp.zeros((8, 128), F32)
    gain = jnp.zeros((8, 128), F32)
    for k in range(live):
        shift = shift + grads[k] * slope_sum[k]
        gain = gain + grads[k] * slope_hat[k]
    near3[t.near_at(3), 0:8, :] = shift
    near3[t.near_at(3), 8:16, :] = gain
    t.near_send(3)
    coef, dense = r.coef, r.dense
    scale_c = dense_of(r.gc, dense) * inv_c
    for k in range(live):
        dense[...] = grads[k]
        row_form(coef, k, dense, 0, feat // 128)
        dense[...] = grads[k] * scale_c
        row_form(coef, 3 + k, dense, 0, feat // 128)
    t.sums_near(3)
    both = t.sums_wide(3)
    r.vectors_c[...] = both
    for q in range(2):
        dense[...] = both[8 * q : 8 * q + 8] * scale_c / n_all
        row_form(coef, 6 + q, dense, 0, feat // 128)
    t.all_sent(0, 1, 2, 3)
    wait_bytes(pool.at[pl.ds(1, len(t.clip_peers))], r.pool_s.at[0])


def backward(t):
    r, live, mid, feat, rows, area, height = t.r, t.live, t.mid, t.feat, t.rows, t.area, t.height
    slots, width, quad, far, v = t.slots, t.width, t.quad, t.far, None
    t.places()
    t.greet()
    t.load(
        valid=(r.slot_valid, r.valid), expand=(r.w_expand, r.we),
        ga=(r.gain_a, r.ga), gb=(r.gain_b, r.gb), reduce=(r.w_reduce, r.wr),
    )
    wc = r.wc
    for i in range(3):
        for j in range(3):
            pltpu.make_async_copy(
                r.w_spatial.at[i, j], wc.at[i, :, pl.ds(j * mid, mid)], r.load_sem.at[15]
            ).start()
    clear(r.g3, r.gpc, r.gpa)
    t.loaded(valid=0)
    t.slot_facts()
    v = t.v
    n_all = r.facts[0:1, :]
    inv_a, inv_b = r.facts[8 : 8 + mid // 128, :], r.facts[16 : 16 + mid // 128, :]
    coef, hat_c, slope_c, out = r.coef, r.hat_c, r.slope_c, r.vectors
    me, send = t.me, t.send
    gpc = r.gpc
    for k in range(live):
        for c in range(feat // 256):
            lanes = slice(c * 256, (c + 1) * 256)
            c0 = coef[3 + k : 4 + k, lanes]
            c1 = coef[6:7, lanes] * v[k]
            c2 = coef[7:8, lanes] * v[k]

            def step(y, carry):
                at = block(k, y)
                grad = slope_c[pl.ds(at, SIDE), lanes] * c0 - (c1 + hat_c[pl.ds(at, SIDE), lanes] * c2)
                gpc[pl.ds(at, SIDE), lanes] = grad.astype(BF16)
                return carry

            lax.fori_loop(0, height, step, 0, unroll=7)

    def back_sums(at, grad_ref, slope_ref, hat_ref):
        zero = jnp.zeros((SIDE, mid), F32)
        carry = (zero, zero)
        for k in range(live):
            def step(y, c):
                here = pl.ds(block(k, y), SIDE)
                grad = grad_ref[here, :] * slope_ref[here, :]
                grad_ref[here, :] = grad
                return c[0] + grad, c[1] + grad * hat_ref[here, :]

            carry = lax.fori_loop(0, height, step, carry, unroll=7)
        buf = r.near[at]
        to_dense(buf, t.near_at(at), jnp.sum(carry[0], axis=0, keepdims=True), 0)
        to_dense(buf, t.near_at(at), jnp.sum(carry[1], axis=0, keepdims=True), 2)

    def back_apply(at, table, gain_ref, inv, grad_ref, hat_ref, write):
        both = t.sums_wide(at)
        out[8 * at - 32 : 8 * at - 28, :] = both[0:4]
        dense = r.dense
        scale = dense_of(gain_ref, dense) * inv
        dense[0:2, :] = scale
        dense[2:4, :] = both[0:2] * scale / n_all
        dense[4:6, :] = both[2:4] * scale / n_all
        for q in range(3):
            row_form(table, q, dense, 2 * q, 2)
        for k in range(live):
            c0, c1, c2 = table[0:1, :], table[1:2, :] * v[k], table[2:3, :] * v[k]

            def step(y, carry):
                at_row = block(k, y)
                here = pl.ds(at_row, SIDE)
                write(at_row, grad_ref[here, :] * c0 - (c1 + hat_ref[here, :] * c2))
                return carry

            lax.fori_loop(0, height, step, 0, unroll=7)

    core, bit_x, bit_y, at_z = me % 2, (me // 2) % 2, (me // 4) % 2, (me // 8) % quad
    at_far = me // (8 * quad)
    bit1 = bit_x + core * (bit_y - bit_x)
    bit2 = bit_y + core * (bit_x - bit_y)
    sibling = me + 1 - 2 * core
    peer1 = me + (1 - 2 * bit1) * (2 + 2 * core)
    peer2 = me + (1 - 2 * bit2) * (4 - 2 * core)
    z_at = [(at_z + o) % quad for o in range(1, quad)]
    z_peer = [me + 8 * (q - at_z) for q in z_at]
    far_peer = [me + 8 * quad * ((at_far + o) % far - at_far) for o in range(1, far)]
    chunk_s, chunk_r = r.chunk_s, r.chunk_r
    waits = []

    def chunk(q):
        part, whole = r.part[q], (r.e, r.s0, r.s1, r.s2, r.r)[q]
        size = part.shape[0]
        half, quarter, eighth, piece = size // 2, size // 4, size // 8, size // (8 * quad)
        m8 = lambda value: pl.multiple_of(value, 8)
        at_h = m8(core * half)
        at_q = m8(at_h + bit1 * quarter)
        at_e = m8(at_q + bit2 * eighth)
        at_p = m8(at_e + at_z * piece)

        def go(step, src, dst, device):
            send(src, dst, chunk_s.at[q, step], chunk_r.at[q, step], device)

        def finish(step, ref):
            wait_bytes(ref, chunk_r.at[q, step])
            waits.append((ref, chunk_s.at[q, step]))

        rb0, rb1, rb2, rb3 = r.rb0[q], r.rb1[q], r.rb2[q], r.rb3[q]
        go(0, part.at[pl.ds(m8((1 - core) * half), half)], rb0, sibling)
        yield
        finish(0, rb0)
        part[pl.ds(at_h, half), :] = part[pl.ds(at_h, half), :] + rb0[...]
        go(1, part.at[pl.ds(m8(at_h + (1 - bit1) * quarter), quarter)], rb1, peer1)
        yield
        finish(1, rb1)
        part[pl.ds(at_q, quarter), :] = part[pl.ds(at_q, quarter), :] + rb1[...]
        go(2, part.at[pl.ds(m8(at_q + (1 - bit2) * eighth), eighth)], rb2, peer2)
        yield
        finish(2, rb2)
        part[pl.ds(at_e, eighth), :] = part[pl.ds(at_e, eighth), :] + rb2[...]
        for o in range(quad - 1):
            go(3, part.at[pl.ds(m8(at_e + z_at[o] * piece), piece)], rb3.at[pl.ds(o * piece, piece)], z_peer[o])
        yield
        finish(3, rb3)
        own = part[pl.ds(at_p, piece), :]
        for o in range(quad - 1):
            own = own + rb3[o * piece : (o + 1) * piece, :]
        if far > 1:
            rb4 = r.rb4[q]
            rb4[at_far] = own
            for device in far_peer:
                go(8, rb4.at[at_far], rb4.at[at_far], device)
            yield
            finish(8, rb4.at[pl.ds(0, far - 1)])
            own = rb4[0]
            for o in range(1, far):
                own = own + rb4[o]
        whole[pl.ds(at_p, piece), :] = own
        for o in range(quad - 1):
            go(4, whole.at[pl.ds(at_p, piece)], whole.at[pl.ds(at_p, piece)], z_peer[o])
        yield
        finish(4, whole.at[pl.ds(0, (quad - 1) * piece)])
        go(5, whole.at[pl.ds(at_e, eighth)], whole.at[pl.ds(at_e, eighth)], peer2)
        yield
        finish(5, whole.at[pl.ds(0, eighth)])
        go(6, whole.at[pl.ds(at_q, quarter)], whole.at[pl.ds(at_q, quarter)], peer1)
        yield
        finish(6, whole.at[pl.ds(0, quarter)])
        go(7, whole.at[pl.ds(at_h, half)], whole.at[pl.ds(at_h, half)], sibling)
        yield
        finish(7, whole.at[pl.ds(0, half)])
        yield

    chunks = [chunk(q) for q in range(5)]

    def go_on(*which):
        for name in which:
            next(chunks[name], None)

    hat_a, slope_a, hat_b, slope_b, hbt, xt = r.hat_a, r.slope_a, r.hat_b, r.slope_b, r.hbt, r.xt
    we, wr, back = r.we, r.wr, r.back
    tiles = feat // 128
    group = SIDE // slots
    keep, moved, mask = t.keep, t.moved, t.mask
    grad_b, grad_a = r.grad_b, r.grad_a
    t.loaded(expand=0, ga=0, gb=0, reduce=0)
    wait_bytes(wc, r.load_sem.at[15])
    by_rows(grad_b, lambda here: dot(gpc[here, :], we[...], NT))
    back_sums(4, grad_b, slope_b, hat_b)
    t.all_here()
    t.near_send(4)

    def expand_part(q, carry):
        lanes = pl.ds(pl.multiple_of(q * 256, 256), 256)
        value = dot(hbt[...], gpc[:, lanes])
        for m in range(2):
            r.part[E][pl.ds(pl.multiple_of((2 * q + m) * mid, mid), mid), :] = value[:, m * 128 : (m + 1) * 128]
        return carry

    lax.fori_loop(0, feat // 256, expand_part, 0)
    go_on(E)
    t.sums_near(4)
    go_on(E)
    g3 = r.g3

    def write_gb(at, grad):
        grad = jnp.where(mask, grad, 0.0)
        three(g3, at, pltpu.roll(grad, SIDE - 1, 0), grad, pltpu.roll(grad, 1, 0))

    back_apply(4, r.table, r.gb, inv_b, grad_b, hat_b, write_gb)
    go_on(E)
    by_rows(
        grad_a, lambda here: sum(dot(g3[moved_rows(here, (2 - i) * SIDE), :], wc[i], NT) for i in range(3))
    )
    back_sums(5, grad_a, slope_a, hat_a)
    t.near_send(5)
    for i in range(3):
        spread_lanes(r.part[S0 + i], dot(xt[...], g3[(2 - i) * SIDE : (2 - i) * SIDE + rows, :]))
        go_on(S0 + i)
    go_on(E)
    t.sums_near(5)
    gpa = r.gpa

    def write_ga(at, grad):
        gpa[pl.ds(at, SIDE), :] = grad.astype(BF16)

    back_apply(5, r.table, r.ga, inv_a, grad_a, hat_a, write_ga)

    def reduce_part(q, carry):
        here = pl.ds(pl.multiple_of(q * 256, 256), 256)
        value = dot(r.ft[here, :], gpa[...])
        for m in range(mid // 128):
            r.part[R][pl.ds(pl.multiple_of(q * 256 + m * feat, 256), 256), :] = value[:, m * 128 : (m + 1) * 128]
        return carry

    lax.fori_loop(0, feat // 256, reduce_part, 0)
    go_on(R)
    go_on(S0, S1, E, S2)

    by_rows(back, lambda here: dot(gpa[here, :], wr[...], NT))
    go_on(E, S0, S1, S2, R)
    gf = r.gf

    def blend(y, carry):
        for p in range(tiles // group):
            values = []
            for q in range(group):
                lanes = slice((p * group + q) * 128, (p * group + q + 1) * 128)
                terms = [
                    slope_c[pl.ds(block(k, y), SIDE), lanes] * coef[k : k + 1, lanes]
                    + back[pl.ds(block(k, y), SIDE), lanes]
                    for k in range(live)
                ]
                values.append(terms[0] * keep[0])
                for m in range(1, live):
                    values.append(terms[m] * keep[m] + terms[m - 1] * moved[m - 1])
                values.append(terms[live - 1] * moved[live - 1])
            value = jnp.swapaxes(jnp.stack(values), 0, 1)
            gf[pl.ds(y * width, width), p * SIDE : (p + 1) * SIDE, :] = value[0:width].astype(BF16)
        return carry

    for part in range(2):
        lax.fori_loop(part * height // 2, (part + 1) * height // 2, blend, 0)
        go_on(E, S0, S1, S2, R)

    for _ in range(12):
        go_on(E, S0, S1, S2, R)

    t.all_sent(4, 5)
    for ref, sem in waits:
        wait_bytes(ref, sem)


def store(gf, vectors_c, vectors, expand, s0, s1, s2, reduce, frames_out, reduce_out, spatial_out, expand_out, *rest):
    ga, ba, gb, bb, gc, bc, sem = rest
    pltpu.make_async_copy(gf, frames_out, sem.at[0]).start()
    depth, width = reduce_out.shape
    for q in range(width // 128):
        pltpu.make_async_copy(
            reduce.at[pl.ds(q * depth, depth)], reduce_out.at[:, pl.ds(q * 128, 128)], sem.at[1]
        ).start()
    depth, width = expand_out.shape
    for q in range(width // 128):
        pltpu.make_async_copy(
            expand.at[pl.ds(q * depth, depth)], expand_out.at[:, pl.ds(q * 128, 128)], sem.at[2]
        ).start()
    for i, part in enumerate((s0, s1, s2)):
        for q in range(part.shape[0] // depth):
            pltpu.make_async_copy(
                part.at[pl.ds(q * depth, depth)],
                spatial_out.at[i, q * 128 // depth, :, pl.ds(q * 128 % depth, 128)],
                sem.at[3 + i],
            ).start()
    for ref, source, first in (
        (bc, vectors_c, 0), (gc, vectors_c, 8), (bb, vectors, 0), (gb, vectors, 2), (ba, vectors, 8), (ga, vectors, 10)
    ):
        for q in range(ref.shape[0] // 128):
            ref[q * 128 : (q + 1) * 128] = source[first + q : first + q + 1, :].reshape(128)
    wait_bytes(gf, sem.at[0])
    wait_bytes(reduce, sem.at[1])
    wait_bytes(expand, sem.at[2])
    for i, part in enumerate((s0, s1, s2)):
        wait_bytes(part, sem.at[3 + i])


def solution(mesh):
    n = mesh.shape["clip"]

    def shards(*args):
        slots, height, width, feat = args[0].shape
        mid = args[1].shape[1]
        rows = (slots - 1) * ROWS
        outer = n // 8
        quad = min(4, outer)
        far = outer // quad
        cfg = (n, slots, height, width, feat, mid)
        flat_shape = (height * width, slots * feat // 128, 128)
        hbm = pl.BlockSpec(memory_space=pltpu.HBM)
        vmem = pl.BlockSpec(memory_space=pltpu.VMEM)
        dma, wide, half = pltpu.SemaphoreType.DMA, F32, BF16
        depths = list(enumerate((8, 4, 16, 16, 4, 4)))
        matrix, third = mid * feat // 128, 3 * mid * mid // 128
        sizes = [matrix, third, third, third, matrix]

        tiled = args[0].transpose(1, 2, 0, 3).reshape(height, width, slots, feat // 128, 128)
        tiled = tiled.transpose(0, 1, 3, 2, 4).reshape(flat_shape)
        given = [pltpu.with_memory_space_constraint(part, pltpu.HBM) for part in (tiled, *args[1:])]
        values = dict(zip(arg_names(), given, strict=True))

        def run(body, outs, scratch, limit, number, **ins):
            names = (*ins, *outs, *scratch)

            def kernel(*refs):
                body(Step(cfg, SimpleNamespace(**dict(zip(names, refs, strict=True)))))

            held = [name in values and values[name] is ins[name] for name in ins]
            results = pl.pallas_call(
                kernel,
                out_shape=list(outs.values()),
                in_specs=[hbm if q else vmem for q in held],
                out_specs=[vmem] * len(outs),
                scratch_shapes=list(scratch.values()),
                compiler_params=pltpu.CompilerParams(
                    collective_id=number, has_side_effects=number is not None, vmem_limit_bytes=limit * 1024 * 1024
                ),
            )(*(part if q else pltpu.with_memory_space_constraint(part, pltpu.VMEM) for q, part in zip(held, ins.values())))
            return dict(zip(outs, results))

        def pick(source, **names):
            return {name: source[name] for name in names}

        vm = pltpu.VMEM
        ints = dict(valid=pltpu.SMEM((slots,), jnp.int32))
        narrow, broad = vm((mid,), F32), vm((feat,), F32)
        first = run(
            prologue,
            dict(fp=vm((rows, feat), half), hat_a=vm((rows, mid), wide), first=vm((1, 8, 128), wide)),
            dict(
                f4=vm((flat_shape[0] + SIDE - width, *flat_shape[1:]), half), wr=vm((feat, mid), half), **ints,
                load_sem=dma((3,)),
            ),
            16,
            None,
            **pick(values, frames=0, w_reduce=0, slot_valid=0),
        )
        small = dict(
            near=[vm((n if n <= 32 and at not in (2, 3) else 8, deep, 128), F32) for at, deep in depths],
            wide=[vm((outer, deep, 128), F32) for at, deep in depths],
            plane=vm((outer, 8, 128), F32),
            dense=vm((8, 128), F32),
            load_sem=dma((16,)),
            near_s=dma((6,)),
            near_r=dma((6,)),
            wide_s=dma((6,)),
            wide_r=dma((6,)),
        )
        square = vm((rows, mid), wide)
        second = run(
            forward,
            dict(
                ft=vm((feat, rows), half), xt=vm((mid, rows), half), hbt=vm((mid, rows), half),
                slope_a=square, hat_b=square, slope_b=square,
                hat_c=vm((rows, feat), wide), slope_c=vm((rows, feat), wide),
                coef=vm((8, feat), wide), facts=vm((24, 128), wide), vectors_c=vm((16, 128), wide), hat_a=square,
            ),
            dict(
                ws=vm((3, 3, mid, mid), half), we=vm((mid, feat), half), **ints,
                clip=pltpu.SMEM((slots,), jnp.int32), segment=pltpu.SMEM((slots,), jnp.int32),
                share=pltpu.SMEM(args[13].shape, F32),
                ga=narrow, ba=narrow, gb=narrow, bb=narrow, gc=broad, bc=broad, loss=broad,
                xp=vm((rows + 2 * SIDE, 3 * mid), half), hb=vm((rows, mid), half),
                table_a=vm((8, mid), wide), table_b=vm((8, mid), wide), table_c=vm((8, feat), wide),
                pool=vm((6, 32, 128), wide), slope_sum=vm((3, 8, 128), wide), slope_hat=vm((3, 8, 128), wide),
                pool_s=dma((1,)), pool_r=dma((1,)), **small,
            ),
            20,
            0,
            fp=first["fp"], pre_a=first["hat_a"], first=first["first"],
            **pick(
                values, w_spatial=0, w_expand=0, gain_a=0, bias_a=0, gain_b=0, bias_b=0, gain_c=0, bias_c=0,
                clip_ids=0, segment_ids=0, slot_valid=0, segment_weight=0, loss_weight=0,
            ),
        )
        third_ = run(
            backward,
            dict(
                gf=vm(flat_shape, half), vectors=vm((16, 128), wide),
                **{name: vm((size, 128), wide) for name, size in zip(dict(e=0, s0=0, s1=0, s2=0, r=0), sizes)},
            ),
            dict(
                wr=vm((feat, mid), half), wc=vm((3, mid, 3 * mid), half), we=vm((mid, feat), half), **ints,
                ga=narrow, gb=narrow, table=vm((8, mid), wide),
                gpc=vm((rows, feat), half), g3=vm((rows + 2 * SIDE, 3 * mid), half), gpa=vm((rows, mid), half),
                grad_a=square, grad_b=square, back=vm((rows, feat), wide),
                part=[vm((size, 128), F32) for size in sizes],
                rb0=[vm((size // 2, 128), F32) for size in sizes],
                rb1=[vm((size // 4, 128), F32) for size in sizes],
                rb2=[vm((size // 8, 128), F32) for size in sizes],
                rb3=[vm(((quad - 1) * size // (8 * quad), 128), F32) for size in sizes],
                rb4=[vm((far, size // (8 * quad), 128), F32) for size in sizes if far > 1],
                chunk_s=dma((5, 9)), chunk_r=dma((5, 9)), **small,
            ),
            30,
            1,
            **pick(
                second, ft=0, xt=0, hbt=0, slope_a=0, hat_b=0, slope_b=0, hat_c=0, slope_c=0, coef=0, facts=0, hat_a=0
            ),
            **pick(values, w_reduce=0, w_spatial=0, w_expand=0, gain_a=0, gain_b=0, slot_valid=0),
        )
        results = [third_["gf"], second["vectors_c"], *list(third_.values())[1:]]
        vector = jax.ShapeDtypeStruct((mid,), F32)
        wide_vector = jax.ShapeDtypeStruct((feat,), F32)
        flat_grad, *rest = pl.pallas_call(
            store,
            out_shape=[
                jax.ShapeDtypeStruct(flat_shape, BF16),
                jax.ShapeDtypeStruct((feat, mid), F32),
                jax.ShapeDtypeStruct((3, 3, mid, mid), F32),
                jax.ShapeDtypeStruct((mid, feat), F32),
                vector, vector, vector, vector, wide_vector, wide_vector,
            ],
            in_specs=[vmem] * 8,
            out_specs=[hbm] * 4 + [vmem] * 6,
            scratch_shapes=[dma((6,))],
            compiler_params=pltpu.CompilerParams(vmem_limit_bytes=8 * 1024 * 1024),
        )(*(pltpu.with_memory_space_constraint(part, pltpu.VMEM) for part in results))
        grad_frames = flat_grad.reshape(height, width, feat // 128, slots, 128).transpose(0, 1, 3, 2, 4)
        return grad_frames.reshape(height, width, slots, feat).transpose(2, 0, 1, 3), *rest

    split = P("clip")
    in_specs = (split,) + (P(),) * 9 + (split,) * 3 + (P(), P())
    out_specs = (split,) + (P(),) * 9
    return jax.shard_map(shards, mesh=mesh, in_specs=in_specs, out_specs=out_specs, check_vma=False)


def arg_names():
    return dict(
        frames=0, w_reduce=0, w_spatial=0, w_expand=0, gain_a=0, bias_a=0, gain_b=0, bias_b=0, gain_c=0, bias_c=0,
        clip_ids=0, segment_ids=0, slot_valid=0, segment_weight=0, loss_weight=0,
    )
```

```python
import functools
from types import SimpleNamespace

import jax
import jax.numpy as jnp
from jax import lax
from jax.experimental import pallas as pl
from jax.experimental.pallas import tpu as pltpu
from jax.sharding import PartitionSpec as P

MESH = pl.DeviceIdType.MESH
EPS = 1e-05
F32 = jnp.float32
BF16 = jnp.bfloat16
SIDE = 16
ROWS = SIDE * SIDE
NN = (((1,), (0,)), ((), ()))
NT = (((1,), (1,)), ((), ()))

ORDER = (
    (),
    (),
    (),
    (),
    (),
    (0,),
    (1, 0),
    (),
    (1, 2, 0, 3),
    (4, 5, 1, 2),
    (0, 6, 3, 7, 4),
    (1, 5, 2),
    (0, 6, 8, 3),
    (),
    (9, 1, 7, 4, 2, 5, 10, 0, 11, 3, 6, 8, 9, 4),
    (1, 2, 7, 10, 5),
    (3, 0, 11),
    (6, 8, 9, 4, 0),
    (1, 7, 2, 10, 5, 3, 11, 4, 6, 1),
    (8,),
    (2, 9, 5),
    (7, 3, 10, 2),
    (11, 4, 6, 8, 3, 9, 5, 10, 7, 4, 11, 6, 5, 8, 9, 10, 6, 7, 11, 8, 9, 7, 10, 8, 11, 9, 10, 11),
)


def dot(a, b, dims=NN):
    return lax.dot_general(a, b, dims, preferred_element_type=F32)


def wait_bytes(ref, sem):
    pltpu.make_async_copy(ref, ref, sem).wait()


def spread_lanes(ref, value):
    depth = value.shape[0]
    for q in range(value.shape[1] // 128):
        ref[q * depth : (q + 1) * depth, :] = value[:, q * 128 : (q + 1) * 128]


def by_rows(ref, value):
    def step(k, carry):
        here = pl.ds(pl.multiple_of(k * 256, 256), 256)
        ref[here, :] = value(here)
        return carry

    lax.fori_loop(0, ref.shape[0] // 256, step, 0)


def moved_rows(here, at):
    return pl.ds(pl.multiple_of(here.start + at, SIDE), 256)


def block(k, y):
    return pl.multiple_of(k * ROWS + y * SIDE, SIDE)


def to_dense(ref, at, value, first):
    for q in range(value.shape[1] // 128):
        ref[at, pl.ds(first + q, 1), :] = value[:, q * 128 : (q + 1) * 128]


def row_form(ref, row, source, first, count):
    for q in range(count):
        ref[row : row + 1, q * 128 : (q + 1) * 128] = source[first + q : first + q + 1, :]


def three(ref, at, left, middle, right):
    here, wide = pl.ds(at + SIDE, SIDE), middle.shape[1]
    ref[here, 0:wide] = left.astype(BF16)
    ref[here, wide : 2 * wide] = middle.astype(BF16)
    ref[here, 2 * wide : 3 * wide] = right.astype(BF16)


def dense_of(ref1, scratch):
    count = ref1.shape[0] // 128
    for q in range(count):
        scratch[q : q + 1, :] = ref1[q * 128 : (q + 1) * 128].reshape(1, 128)
    return scratch[0:count, :]


class Step:
    def __init__(self, cfg, r):
        self.r, self.sizes = r, cfg
        self.n, self.slots, self.height, self.width, self.feat, self.mid = cfg
        self.live = self.slots - 1
        self.rows = self.live * ROWS
        self.area = self.height * self.width
        self.inner = 8
        self.outer = self.n // 8
        self.quad = min(4, self.outer)
        self.far = self.outer // self.quad
        self.loads = {}
        self.mask = lax.broadcasted_iota(jnp.int32, (SIDE, 256), 0) < self.width

    def load(self, **pairs):
        for name, (src, dst) in pairs.items():
            copy = pltpu.make_async_copy(src, dst, self.r.load_sem.at[len(self.loads)])
            copy.start()
            self.loads[name] = copy

    def loaded(self, **names):
        for name in names:
            self.loads[name].wait()

    def fold(self, value):
        return jnp.sum(jnp.where(self.mask, value, 0.0), axis=0, keepdims=True)

    def slot_facts(self):
        r, live = self.r, self.live
        alive, later = 1, []
        for k in range(live):
            alive = alive * r.valid[k]
            later.append(1 - alive)
        self.keep = [(1 - q).astype(F32) for q in later]
        self.moved = [q.astype(F32) for q in later]
        self.later = later
        self.v = [self.kept(r.valid, k) for k in range(live)]
        self.n_own = (self.v[0] + self.v[1] + self.v[2]) * float(self.area)

    def kept(self, values, k):
        return (values[k] + self.later[k] * (values[k + 1] - values[k])).astype(F32)

    def places(self):
        n = self.n
        self.me = me = lax.axis_index("clip")
        self.low, self.high = low, high = me % self.inner, me // self.inner
        self.direct = n <= 32
        self.peers = [(me + o) % n for o in range(1, n)]
        self.low_peers = [me - low + (low + o) % self.inner for o in range(1, self.inner)]
        self.high_peers = [low + self.inner * ((high + o) % self.outer) for o in range(1, self.outer)]
        self.clip_peers = [(me + o) % n for o in (1, n - 1, n // 2, n // 2 - 1, n // 2 + 1)]

    def greet(self):
        self.greeted = self.peers if self.direct else self.low_peers + self.high_peers + self.clip_peers
        self.barrier = pltpu.get_barrier_semaphore()
        for device in self.greeted:
            pl.semaphore_signal(self.barrier, inc=1, device_id=(device,), device_id_type=MESH)

    def all_here(self):
        pl.semaphore_wait(self.barrier, len(self.greeted))

    def send(self, src, dst, ssem, rsem, device):
        pltpu.make_async_remote_copy(
            src_ref=src, dst_ref=dst, send_sem=ssem, recv_sem=rsem, device_id=(device,), device_id_type=MESH
        ).start()

    def one_stage(self, at):
        return self.direct and at not in (2, 3)

    def near_at(self, at):
        return self.me if self.one_stage(at) else self.low

    def near_send(self, at):
        buf, mine = self.r.near[at], self.near_at(at)
        for device in self.peers if self.one_stage(at) else self.low_peers:
            self.send(buf.at[mine], buf.at[mine], self.r.near_s.at[at], self.r.near_r.at[at], device)

    def near_wait(self, at, sems):
        buf = self.r.near[at]
        wait_bytes(buf.at[pl.ds(0, buf.shape[0] - 1)], sems.at[at])

    def wide_send(self, at):
        buf = self.r.wide[at]
        for device in self.high_peers:
            self.send(buf.at[self.high], buf.at[self.high], self.r.wide_s.at[at], self.r.wide_r.at[at], device)

    def wide_wait(self, at, sems):
        wait_bytes(self.r.wide[at].at[pl.ds(0, self.outer - 1)], sems.at[at])

    def all_sent(self, *rounds):
        for at in rounds:
            self.near_wait(at, self.r.near_s)
            if not self.one_stage(at):
                self.wide_wait(at, self.r.wide_s)

    def near_count(self, q):
        return self.r.near[0][(self.me - self.low + q) if self.direct else q, 4:5, :]

    def wide_count(self, q):
        return self.r.plane[q, 0:1, :] if self.direct else self.r.wide[0][q, 4:5, :]

    def stats_near(self, at, count):
        if self.one_stage(at):
            return
        self.near_wait(at, self.r.near_r)
        n_all, s_all, _, spread = combine(self.r.near[at], self.near_count, self.inner, count)
        buf = self.r.wide[at]
        buf[self.high, 0:count, :] = s_all
        buf[self.high, count : 2 * count, :] = spread
        if at == 0:
            buf[self.high, 4:5, :] = n_all
        self.wide_send(at)

    def stats_wide(self, at, count, table):
        r = self.r
        if self.one_stage(at):
            self.near_wait(at, r.near_r)
            counts = r.near[0]
            n_all, _, mean, spread = combine(r.near[at], lambda q: counts[q, 4:5, :], self.n, count)
            if at == 0:
                for q in range(self.outer):
                    r.plane[q, 0:1, :] = sum(counts[q * self.inner + m, 4:5, :] for m in range(self.inner))
        else:
            self.wide_wait(at, r.wide_r)
            n_all, _, mean, spread = combine(r.wide[at], self.wide_count, self.outer, count)
        inverse = lax.rsqrt(spread / n_all + EPS)
        r.dense[0:count, :] = mean
        row_form(table, 0, r.dense, 0, count)
        r.dense[0:count, :] = inverse
        row_form(table, 1, r.dense, 0, count)
        return n_all, inverse

    def sums_near(self, at):
        if not self.one_stage(at):
            self.near_wait(at, self.r.near_r)
            self.r.wide[at][self.high] = total(self.r.near[at])
            self.wide_send(at)

    def sums_wide(self, at):
        if self.one_stage(at):
            self.near_wait(at, self.r.near_r)
            return total(self.r.near[at])
        self.wide_wait(at, self.r.wide_r)
        return total(self.r.wide[at])

    def local_stats(self, buf, at, ref):
        channels = ref.shape[1]
        count = channels // 128
        for c in range(channels // 256):
            lanes = slice(c * 256, (c + 1) * 256)

            def gather(term):
                acc = jnp.zeros((SIDE, 256), F32)
                for k in range(self.live):
                    part = lax.fori_loop(
                        0, self.height, lambda y, a: a + term(ref[pl.ds(block(k, y), SIDE), lanes]),
                        jnp.zeros((SIDE, 256), F32), unroll=self.height,
                    )
                    acc = acc + part * self.v[k]
                return self.fold(acc)

            s_own = gather(lambda x: x)
            mean = s_own / jnp.maximum(self.n_own, 1.0)
            to_dense(buf, at, s_own, 2 * c)
            to_dense(buf, at, gather(lambda x: (x - mean) * (x - mean)), count + 2 * c)

    def norm_silu(self, ref, slope_ref, table, gain, bias, write):
        centre, inverse = table[0:1, :], table[1:2, :]
        g, b = gain[...].reshape(1, self.mid), bias[...].reshape(1, self.mid)
        for k in range(self.live):
            def step(y, carry):
                at = block(k, y)
                hat = (ref[pl.ds(at, SIDE), :] - centre) * inverse
                u = hat * g + b
                s = 0.5 * jnp.tanh(0.5 * u) + 0.5
                h = u * s
                ref[pl.ds(at, SIDE), :] = hat
                slope_ref[pl.ds(at, SIDE), :] = jnp.where(self.mask, s + (h - h * s), 0.0)
                write(at, jnp.where(self.mask, h, 0.0))
                return carry

            lax.fori_loop(0, self.height, step, 0, unroll=7)


def combine(buf, counts, group, count):
    n_part = [counts(q) for q in range(group)]
    s_part = [buf[q, 0:count, :] for q in range(group)]
    n_all = sum(n_part[1:], n_part[0])
    s_all = sum(s_part[1:], s_part[0])
    mean = s_all / jnp.maximum(n_all, 1.0)
    spread = jnp.zeros((count, 128), F32)
    for q in range(group):
        gap = s_part[q] / jnp.maximum(n_part[q], 1.0) - mean
        spread = spread + (buf[q, count : 2 * count, :] + n_part[q] * gap * gap)
    return n_all, s_all, mean, spread


def total(buf):
    out = buf[0]
    for q in range(1, buf.shape[0]):
        out = out + buf[q]
    return out


def clear(*refs):
    for ref in refs:
        ref[...] = jnp.zeros(ref.shape, ref.dtype)


def prologue(t):
    r, slots, live, width, feat = t.r, t.slots, t.live, t.width, t.feat
    t.places()
    t.greet()
    t.load(
        frames=(r.frames, r.f4.at[pl.ds(0, t.area)]), valid=(r.slot_valid, r.valid), reduce=(r.w_reduce, r.wr),
        clip=(r.clip_ids, r.clip), segment=(r.segment_ids, r.segment),
        share=(r.segment_weight, r.share), spatial=(r.w_spatial, r.ws), expand=(r.w_expand, r.we),
        ga=(r.gain_a, r.ga), ba=(r.bias_a, r.ba), gb=(r.gain_b, r.gb), bb=(r.bias_b, r.bb),
        gc=(r.gain_c, r.gc), bc=(r.bias_c, r.bc), loss=(r.loss_weight, r.loss),
    )
    for i in range(3):
        for j in range(3):
            pltpu.make_async_copy(
                r.w_spatial.at[i, j], r.wc.at[i, :, pl.ds(j * t.mid, t.mid)], r.load_sem.at[15]
            ).start()
    r.f4[t.area :] = jnp.zeros((r.f4.shape[0] - t.area, *r.f4.shape[1:]), BF16)
    clear(r.fp)
    t.loaded(valid=0)
    t.slot_facts()
    t.loaded(frames=0)
    fp, f4 = r.fp, r.f4
    tiles = feat // 128
    group = SIDE // slots
    short = lax.broadcasted_iota(jnp.int32, (SIDE, 128), 0) < width

    def regroup(y, carry):
        for p in range(tiles // group):
            value = f4[pl.ds(y * width, SIDE), p * SIDE : (p + 1) * SIDE, :].astype(F32)
            value = jnp.swapaxes(value, 0, 1)
            for q in range(group):
                for k in range(live):
                    row = value[q * slots + k] * t.keep[k] + value[q * slots + k + 1] * t.moved[k]
                    lanes = slice((p * group + q) * 128, (p * group + q + 1) * 128)
                    fp[pl.ds(block(k, y), SIDE), lanes] = jnp.where(short, row, 0.0).astype(BF16)
        return carry

    lax.fori_loop(0, t.height, regroup, 0)
    t.loaded(reduce=0)
    by_rows(r.hat_a, lambda here: dot(fp[here, :], r.wr[...]))
    t.local_stats(r.near[0], t.near_at(0), r.hat_a)
    r.near[0][t.near_at(0), 4:5, :] = jnp.full((1, 128), t.n_own, F32)


def forward(t):
    r, live, mid, feat, rows, area, height = t.r, t.live, t.mid, t.feat, t.rows, t.area, t.height
    t.all_here()
    t.near_send(0)
    r.ft[...] = r.fp[...].T
    t.stats_near(0, mid // 128)
    clear(r.xp, r.hb, r.g3, r.gpc, r.gpa)
    t.loaded(clip=0, segment=0, share=0, ga=0, ba=0, gb=0, bb=0, gc=0, bc=0, loss=0, spatial=0, expand=0)
    key = [t.kept(r.clip, k) for k in range(live)]
    weight = []
    for k in range(live):
        at = t.kept(r.segment, k)
        w0, w1, w2 = (r.share[q] for q in range(3))
        weight.append(
            t.v[k] * (w0 * ((1.0 - at) * (2.0 - at) * 0.5) + w1 * (at * (2.0 - at)) + w2 * (at * (at - 1.0) * 0.5))
        )
    n_all, inv_a = t.stats_wide(0, mid // 128, r.table_a)

    xp, hb = r.xp, r.hb

    def write_a(at, h):
        three(xp, at, pltpu.roll(h, 1, 0), h, pltpu.roll(h, SIDE - 1, 0))

    t.norm_silu(r.hat_a, r.slope_a, r.table_a, r.ga, r.ba, write_a)

    by_rows(
        r.hat_b,
        lambda here: sum(dot(xp[moved_rows(here, i * SIDE), :], r.ws[i].reshape(3 * mid, mid)) for i in range(3)),
    )
    t.local_stats(r.near[1], t.near_at(1), r.hat_b)
    t.near_send(1)
    r.xt[...] = xp[SIDE : SIDE + rows, mid : 2 * mid].T
    t.stats_near(1, mid // 128)
    _, inv_b = t.stats_wide(1, mid // 128, r.table_b)

    def write_b(at, h):
        hb[pl.ds(at, SIDE), :] = h.astype(BF16)

    t.norm_silu(r.hat_b, r.slope_b, r.table_b, r.gb, r.bb, write_b)

    hat_c, slope_c, fp, table_c = r.hat_c, r.slope_c, r.fp, r.table_c
    by_rows(hat_c, lambda here: dot(hb[here, :], r.we[...]))
    t.local_stats(r.near[2], t.near_at(2), hat_c)
    t.near_send(2)
    r.hbt[...] = hb[...].T
    t.stats_near(2, feat // 128)
    _, inv_c = t.stats_wide(2, feat // 128, table_c)

    pool, slope_sum, slope_hat = r.pool, r.slope_sum, r.slope_hat
    for c in range(feat // 256):
        lanes = slice(c * 256, (c + 1) * 256)
        centre, inverse = table_c[0:1, lanes], table_c[1:2, lanes]
        g = r.gc[lanes].reshape(1, 256)
        b = r.bc[lanes].reshape(1, 256)
        for k in range(live):
            def step(y, carry):
                a0, a1, a2 = carry
                at = block(k, y)
                hat = (hat_c[pl.ds(at, SIDE), lanes] - centre) * inverse
                u = hat * g + b + fp[pl.ds(at, SIDE), lanes].astype(F32)
                s = 0.5 * jnp.tanh(0.5 * u) + 0.5
                h = u * s
                slope = s + (h - h * s)
                hat_c[pl.ds(at, SIDE), lanes] = hat
                slope_c[pl.ds(at, SIDE), lanes] = slope
                return a0 + h, a1 + slope, a2 + slope * hat

            zero = jnp.zeros((SIDE, 256), F32)
            a0, a1, a2 = lax.fori_loop(0, height, step, (zero, zero, zero), unroll=7)
            p_row = (t.fold(a0) * (1.0 / area)).astype(BF16).astype(F32)
            to_dense(pool, 0, p_row, 8 * k + 2 * c)
            to_dense(slope_sum, k, t.fold(a1), 2 * c)
            to_dense(slope_hat, k, t.fold(a2), 2 * c)
    for k in range(live):
        pool[0, 24 + k : 25 + k, :] = jnp.full((1, 128), key[k], F32)
        pool[0, 28 + k : 29 + k, :] = jnp.full((1, 128), weight[k], F32)
    for q, device in enumerate(t.clip_peers):
        t.send(pool.at[0], pool.at[q + 1], r.pool_s.at[0], r.pool_r.at[0], device)
    wait_bytes(pool.at[pl.ds(1, len(t.clip_peers))], r.pool_r.at[0])

    lw = dense_of(r.loss, r.dense)
    grads = []
    for k in range(live):
        my_key = jnp.full((1, 128), key[k], F32)
        my_weight = jnp.full((1, 128), weight[k], F32)
        mean = jnp.zeros((8, 128), F32)
        den = jnp.zeros((1, 128), F32)
        for q in range(len(t.clip_peers) + 1):
            for m in range(live):
                match = jnp.where(pool[q, 24 + m : 25 + m, :] == my_key, pool[q, 28 + m : 29 + m, :], 0.0)
                den = den + match
                mean = mean + match * pool[q, 8 * m : 8 * m + 8, :]
        den = jnp.where(den == 0.0, 1.0, den)
        mean = mean / den
        power = jnp.sum(jnp.sum(mean * mean, axis=0, keepdims=True), axis=1, keepdims=True)
        scale = lax.rsqrt(power * (1.0 / feat) + EPS)
        unit = mean * scale
        along = jnp.sum(jnp.sum(unit * lw, axis=0, keepdims=True), axis=1, keepdims=True)
        mean_grad = scale * (lw - unit * (along * (1.0 / feat)))
        grads.append((my_weight / den) * mean_grad * (1.0 / area))

    near3 = r.near[3]
    shift = jnp.zeros((8, 128), F32)
    gain = jnp.zeros((8, 128), F32)
    for k in range(live):
        shift = shift + grads[k] * slope_sum[k]
        gain = gain + grads[k] * slope_hat[k]
    near3[t.near_at(3), 0:8, :] = shift
    near3[t.near_at(3), 8:16, :] = gain
    t.near_send(3)
    coef, dense = r.coef, r.dense
    scale_c = dense_of(r.gc, dense) * inv_c
    for k in range(live):
        dense[...] = grads[k]
        row_form(coef, k, dense, 0, feat // 128)
        dense[...] = grads[k] * scale_c
        row_form(coef, 3 + k, dense, 0, feat // 128)
    t.sums_near(3)
    both = t.sums_wide(3)
    r.vectors_c[...] = both
    for q in range(2):
        dense[...] = both[8 * q : 8 * q + 8] * scale_c / n_all
        row_form(coef, 6 + q, dense, 0, feat // 128)
    return n_all, inv_a, inv_b


def backward(t, n_all, inv_a, inv_b):
    r, live, mid, feat, rows, height = t.r, t.live, t.mid, t.feat, t.rows, t.height
    slots, width, quad, far, v, wc = t.slots, t.width, t.quad, t.far, t.v, r.wc
    coef, hat_c, slope_c, out = r.coef, r.hat_c, r.slope_c, r.vectors
    me, send = t.me, t.send
    gpc = r.gpc
    for k in range(live):
        for c in range(feat // 256):
            lanes = slice(c * 256, (c + 1) * 256)
            c0 = coef[3 + k : 4 + k, lanes]
            c1 = coef[6:7, lanes] * v[k]
            c2 = coef[7:8, lanes] * v[k]

            def step(y, carry):
                at = block(k, y)
                grad = slope_c[pl.ds(at, SIDE), lanes] * c0 - (c1 + hat_c[pl.ds(at, SIDE), lanes] * c2)
                gpc[pl.ds(at, SIDE), lanes] = grad.astype(BF16)
                return carry

            lax.fori_loop(0, height, step, 0, unroll=7)

    def back_sums(at, grad_ref, slope_ref, hat_ref):
        zero = jnp.zeros((SIDE, mid), F32)
        carry = (zero, zero)
        for k in range(live):
            def step(y, c):
                here = pl.ds(block(k, y), SIDE)
                grad = grad_ref[here, :] * slope_ref[here, :]
                grad_ref[here, :] = grad
                return c[0] + grad, c[1] + grad * hat_ref[here, :]

            carry = lax.fori_loop(0, height, step, carry, unroll=7)
        buf = r.near[at]
        to_dense(buf, t.near_at(at), jnp.sum(carry[0], axis=0, keepdims=True), 0)
        to_dense(buf, t.near_at(at), jnp.sum(carry[1], axis=0, keepdims=True), 2)

    def back_apply(at, table, gain_ref, inv, grad_ref, hat_ref, write):
        both = t.sums_wide(at)
        out[8 * at - 32 : 8 * at - 28, :] = both[0:4]
        dense = r.dense
        scale = dense_of(gain_ref, dense) * inv
        dense[0:2, :] = scale
        dense[2:4, :] = both[0:2] * scale / n_all
        dense[4:6, :] = both[2:4] * scale / n_all
        for q in range(3):
            row_form(table, q, dense, 2 * q, 2)
        for k in range(live):
            c0, c1, c2 = table[0:1, :], table[1:2, :] * v[k], table[2:3, :] * v[k]

            def step(y, carry):
                at_row = block(k, y)
                here = pl.ds(at_row, SIDE)
                write(at_row, grad_ref[here, :] * c0 - (c1 + hat_ref[here, :] * c2))
                return carry

            lax.fori_loop(0, height, step, 0, unroll=7)

    core, bit_x, bit_y, at_z = me % 2, (me // 2) % 2, (me // 4) % 2, (me // 8) % quad
    at_far = me // (8 * quad)
    bit1 = bit_x + core * (bit_y - bit_x)
    bit2 = bit_y + core * (bit_x - bit_y)
    sibling = me + 1 - 2 * core
    peer1 = me + (1 - 2 * bit1) * (2 + 2 * core)
    peer2 = me + (1 - 2 * bit2) * (4 - 2 * core)
    z_at = [(at_z + o) % quad for o in range(1, quad)]
    z_peer = [me + 8 * (q - at_z) for q in z_at]
    far_peer = [me + 8 * quad * ((at_far + o) % far - at_far) for o in range(1, far)]
    chunk_s, chunk_r = r.chunk_s, r.chunk_r
    waits, blocks = [], iter(ORDER)
    plan = [(0, q, 2) for q in range(2)] + [(1 + q // 2, q % 2, 2) for q in range(6)] + [(4, q, 4) for q in range(4)]

    def chunk(q):
        name, at, count = plan[q]
        size = r.part[name].shape[0] // count
        part = r.part[name].at[pl.ds(at * size, size)]
        whole = (r.e, r.s0, r.s1, r.s2, r.r)[name].at[pl.ds(at * size, size)]
        half, quarter, eighth, piece = size // 2, size // 4, size // 8, size // (8 * quad)
        m8 = lambda value: pl.multiple_of(value, 8)
        at_h = m8(core * half)
        at_q = m8(at_h + bit1 * quarter)
        at_e = m8(at_q + bit2 * eighth)
        at_p = m8(at_e + at_z * piece)

        def go(step, src, dst, device):
            send(src, dst, chunk_s.at[q, step], chunk_r.at[q, step], device)

        def finish(step, ref):
            wait_bytes(ref, chunk_r.at[q, step])
            waits.append((ref, chunk_s.at[q, step]))

        rb0, rb1, rb2, rb3 = r.rb0[q], r.rb1[q], r.rb2[q], r.rb3[q]
        go(0, part.at[pl.ds(m8((1 - core) * half), half)], rb0, sibling)
        yield
        finish(0, rb0)
        part[pl.ds(at_h, half), :] = part[pl.ds(at_h, half), :] + rb0[...]
        go(1, part.at[pl.ds(m8(at_h + (1 - bit1) * quarter), quarter)], rb1, peer1)
        yield
        finish(1, rb1)
        part[pl.ds(at_q, quarter), :] = part[pl.ds(at_q, quarter), :] + rb1[...]
        go(2, part.at[pl.ds(m8(at_q + (1 - bit2) * eighth), eighth)], rb2, peer2)
        yield
        finish(2, rb2)
        part[pl.ds(at_e, eighth), :] = part[pl.ds(at_e, eighth), :] + rb2[...]
        for o in range(quad - 1):
            go(3, part.at[pl.ds(m8(at_e + z_at[o] * piece), piece)], rb3.at[pl.ds(o * piece, piece)], z_peer[o])
        yield
        finish(3, rb3)
        own = part[pl.ds(at_p, piece), :]
        for o in range(quad - 1):
            own = own + rb3[o * piece : (o + 1) * piece, :]
        if far > 1:
            rb4 = r.rb4[q]
            rb4[at_far] = own
            for device in far_peer:
                go(8, rb4.at[at_far], rb4.at[at_far], device)
            yield
            finish(8, rb4.at[pl.ds(0, far - 1)])
            own = rb4[0]
            for o in range(1, far):
                own = own + rb4[o]
        whole[pl.ds(at_p, piece), :] = own
        for o in range(quad - 1):
            go(4, whole.at[pl.ds(at_p, piece)], whole.at[pl.ds(at_p, piece)], z_peer[o])
        yield
        finish(4, whole.at[pl.ds(0, (quad - 1) * piece)])
        go(5, whole.at[pl.ds(at_e, eighth)], whole.at[pl.ds(at_e, eighth)], peer2)
        yield
        finish(5, whole.at[pl.ds(0, eighth)])
        go(6, whole.at[pl.ds(at_q, quarter)], whole.at[pl.ds(at_q, quarter)], peer1)
        yield
        finish(6, whole.at[pl.ds(0, quarter)])
        go(7, whole.at[pl.ds(at_h, half)], whole.at[pl.ds(at_h, half)], sibling)
        yield
        finish(7, whole.at[pl.ds(0, half)])
        yield

    chunks = [chunk(q) for q in range(len(plan))]

    def go_on(*which):
        for q in which:
            next(chunks[q])

    def go_on_all():
        go_on(*next(blocks))

    hat_a, slope_a, hat_b, slope_b, hbt, xt = r.hat_a, r.slope_a, r.hat_b, r.slope_b, r.hbt, r.xt
    we, wr, back = r.we, r.wr, r.back
    tiles = feat // 128
    group = SIDE // slots
    keep, moved, mask = t.keep, t.moved, t.mask
    grad_b, grad_a = r.grad_b, r.grad_a
    wait_bytes(wc, r.load_sem.at[15])
    go_on_all()
    go_on_all()
    by_rows(grad_b, lambda here: dot(gpc[here, :], we[...], NT))
    back_sums(4, grad_b, slope_b, hat_b)
    t.near_send(4)
    for e in range(2):
        go_on_all()
        for q in range(2):
            first = (2 * e + q) * 256
            spread_lanes(r.part[0].at[pl.ds(2 * first, 512)], dot(hbt[...], gpc[:, first : first + 256]))
        go_on(e)
    go_on_all()
    g3 = r.g3

    def write_gb(at, grad):
        grad = jnp.where(mask, grad, 0.0)
        three(g3, at, pltpu.roll(grad, SIDE - 1, 0), grad, pltpu.roll(grad, 1, 0))

    back_apply(4, r.table, r.gb, inv_b, grad_b, hat_b, write_gb)
    go_on_all()
    by_rows(
        grad_a, lambda here: sum(dot(g3[moved_rows(here, (2 - i) * SIDE), :], wc[i], NT) for i in range(3))
    )
    back_sums(5, grad_a, slope_a, hat_a)
    t.near_send(5)
    for i in range(3):
        go_on_all()
        spread_lanes(r.part[1 + i], dot(xt[...], g3[(2 - i) * SIDE : (2 - i) * SIDE + rows, :]))
        go_on(2 + 2 * i, 3 + 2 * i)
    go_on_all()
    gpa = r.gpa

    def write_ga(at, grad):
        gpa[pl.ds(at, SIDE), :] = grad.astype(BF16)

    back_apply(5, r.table, r.ga, inv_a, grad_a, hat_a, write_ga)
    for q in range(4):
        go_on_all()
        spread_lanes(r.part[4].at[pl.ds(q * 512, 512)], dot(r.ft[q * 256 : (q + 1) * 256, :], gpa[...]))
        go_on(8 + q)

    go_on_all()
    by_rows(back, lambda here: dot(gpa[here, :], wr[...], NT))
    gf = r.gf

    def blend(y, carry):
        for p in range(tiles // group):
            values = []
            for q in range(group):
                lanes = slice((p * group + q) * 128, (p * group + q + 1) * 128)
                terms = [
                    slope_c[pl.ds(block(k, y), SIDE), lanes] * coef[k : k + 1, lanes]
                    + back[pl.ds(block(k, y), SIDE), lanes]
                    for k in range(live)
                ]
                values.append(terms[0] * keep[0])
                for m in range(1, live):
                    values.append(terms[m] * keep[m] + terms[m - 1] * moved[m - 1])
                values.append(terms[live - 1] * moved[live - 1])
            value = jnp.swapaxes(jnp.stack(values), 0, 1)
            gf[pl.ds(y * width, width), p * SIDE : (p + 1) * SIDE, :] = value[0:width].astype(BF16)
        return carry

    for q in range(height // 2):
        go_on_all()
        for y in range(2):
            blend(2 * q + y, 0)
    go_on_all()
    for each in chunks:
        for _ in each:
            pass

    t.all_sent(*range(6))
    wait_bytes(r.pool.at[pl.ds(1, len(t.clip_peers))], r.pool_s.at[0])
    for ref, sem in waits:
        wait_bytes(ref, sem)


def store(gf, vectors_c, vectors, expand, s0, s1, s2, reduce, frames_out, reduce_out, spatial_out, expand_out, *rest):
    ga, ba, gb, bb, gc, bc, sem = rest
    pltpu.make_async_copy(gf, frames_out, sem.at[0]).start()
    depth, width = reduce_out.shape
    for q in range(depth // 256):
        for m in range(width // 128):
            pltpu.make_async_copy(
                reduce.at[pl.ds((q * width // 128 + m) * 256, 256)],
                reduce_out.at[pl.ds(q * 256, 256), pl.ds(m * 128, 128)],
                sem.at[1],
            ).start()
    depth, width = expand_out.shape
    for q in range(width // 128):
        pltpu.make_async_copy(
            expand.at[pl.ds(q * depth, depth)], expand_out.at[:, pl.ds(q * 128, 128)], sem.at[2]
        ).start()
    for i, part in enumerate((s0, s1, s2)):
        for q in range(part.shape[0] // depth):
            pltpu.make_async_copy(
                part.at[pl.ds(q * depth, depth)],
                spatial_out.at[i, q * 128 // depth, :, pl.ds(q * 128 % depth, 128)],
                sem.at[3 + i],
            ).start()
    for ref, source, first in (
        (bc, vectors_c, 0), (gc, vectors_c, 8), (bb, vectors, 0), (gb, vectors, 2), (ba, vectors, 8), (ga, vectors, 10)
    ):
        for q in range(ref.shape[0] // 128):
            ref[q * 128 : (q + 1) * 128] = source[first + q : first + q + 1, :].reshape(128)
    wait_bytes(gf, sem.at[0])
    wait_bytes(reduce, sem.at[1])
    wait_bytes(expand, sem.at[2])
    for i, part in enumerate((s0, s1, s2)):
        wait_bytes(part, sem.at[3 + i])


def solution(mesh):
    n = mesh.shape["clip"]

    def shards(*args):
        slots, height, width, feat = args[0].shape
        mid = args[1].shape[1]
        rows = (slots - 1) * ROWS
        outer = n // 8
        quad = min(4, outer)
        far = outer // quad
        cfg = (n, slots, height, width, feat, mid)
        flat_shape = (height * width, slots * feat // 128, 128)
        hbm = pl.BlockSpec(memory_space=pltpu.HBM)
        vmem = pl.BlockSpec(memory_space=pltpu.VMEM)
        dma = pltpu.SemaphoreType.DMA
        depths = list(enumerate((8, 4, 16, 16, 4, 4)))
        matrix, third = mid * feat // 128, 3 * mid * mid // 128
        sizes = [matrix, third, third, third, matrix]

        tiled = args[0].transpose(1, 2, 0, 3).reshape(height, width, slots, feat // 128, 128)
        tiled = tiled.transpose(0, 1, 3, 2, 4).reshape(flat_shape)
        given = [pltpu.with_memory_space_constraint(part, pltpu.HBM) for part in (tiled, *args[1:])]

        vm = pltpu.VMEM
        narrow, broad, square = vm((mid,), F32), vm((feat,), F32), vm((rows, mid), F32)
        ints = pltpu.SMEM((slots,), jnp.int32)
        plan = [matrix // 2] * 2 + [third // 2] * 6 + [matrix // 4] * 4
        outs = dict(
            gf=vm(flat_shape, BF16), vectors_c=vm((16, 128), F32), vectors=vm((16, 128), F32),
            e=vm((matrix, 128), F32), s0=vm((third, 128), F32), s1=vm((third, 128), F32), s2=vm((third, 128), F32),
            r=vm((matrix, 128), F32),
        )
        scratch = dict(
            f4=vm((flat_shape[0] + SIDE - width, *flat_shape[1:]), BF16),
            fp=vm((rows, feat), BF16), ft=vm((feat, rows), BF16),
            wr=vm((feat, mid), BF16), ws=vm((3, 3, mid, mid), BF16), wc=vm((3, mid, 3 * mid), BF16), we=vm((mid, feat), BF16),
            valid=ints, clip=ints, segment=ints, share=pltpu.SMEM(args[13].shape, F32),
            ga=narrow, ba=narrow, gb=narrow, bb=narrow, gc=broad, bc=broad, loss=broad,
            xp=vm((rows + 2 * SIDE, 3 * mid), BF16), xt=vm((mid, rows), BF16),
            hb=vm((rows, mid), BF16), hbt=vm((mid, rows), BF16),
            hat_a=square, slope_a=square, hat_b=square, slope_b=square, grad_a=square, grad_b=square,
            hat_c=vm((rows, feat), F32), slope_c=vm((rows, feat), F32), back=vm((rows, feat), F32),
            gpc=vm((rows, feat), BF16), g3=vm((rows + 2 * SIDE, 3 * mid), BF16), gpa=vm((rows, mid), BF16),
            table_a=vm((8, mid), F32), table_b=vm((8, mid), F32), table=vm((8, mid), F32),
            table_c=vm((8, feat), F32), coef=vm((8, feat), F32), dense=vm((8, 128), F32),
            pool=vm((6, 32, 128), F32), slope_sum=vm((3, 8, 128), F32), slope_hat=vm((3, 8, 128), F32),
            near=[vm((n if n <= 32 and at not in (2, 3) else 8, deep, 128), F32) for at, deep in depths],
            wide=[vm((outer, deep, 128), F32) for at, deep in depths],
            plane=vm((outer, 8, 128), F32),
            part=[vm((size, 128), F32) for size in sizes],
            rb0=[vm((size // 2, 128), F32) for size in plan],
            rb1=[vm((size // 4, 128), F32) for size in plan],
            rb2=[vm((size // 8, 128), F32) for size in plan],
            rb3=[vm(((quad - 1) * size // (8 * quad), 128), F32) for size in plan],
            rb4=[vm((far, size // (8 * quad), 128), F32) for size in plan if far > 1],
            load_sem=dma((16,)), near_s=dma((6,)), near_r=dma((6,)), wide_s=dma((6,)), wide_r=dma((6,)),
            pool_s=dma((1,)), pool_r=dma((1,)), chunk_s=dma((12, 9)), chunk_r=dma((12, 9)),
        )
        names = (*arg_names(), *outs, *scratch)

        def kernel(*refs):
            t = Step(cfg, SimpleNamespace(**dict(zip(names, refs, strict=True))))
            prologue(t)
            backward(t, *forward(t))

        results = pl.pallas_call(
            kernel,
            out_shape=list(outs.values()),
            in_specs=[hbm] * len(given),
            out_specs=[vmem] * len(outs),
            scratch_shapes=list(scratch.values()),
            compiler_params=pltpu.CompilerParams(
                collective_id=0, has_side_effects=True, vmem_limit_bytes=50 * 1024 * 1024
            ),
        )(*given)
        vector = jax.ShapeDtypeStruct((mid,), F32)
        wide_vector = jax.ShapeDtypeStruct((feat,), F32)
        flat_grad, *rest = pl.pallas_call(
            store,
            out_shape=[
                jax.ShapeDtypeStruct(flat_shape, BF16),
                jax.ShapeDtypeStruct((feat, mid), F32),
                jax.ShapeDtypeStruct((3, 3, mid, mid), F32),
                jax.ShapeDtypeStruct((mid, feat), F32),
                vector, vector, vector, vector, wide_vector, wide_vector,
            ],
            in_specs=[vmem] * 8,
            out_specs=[hbm] * 4 + [vmem] * 6,
            scratch_shapes=[dma((6,))],
            compiler_params=pltpu.CompilerParams(vmem_limit_bytes=8 * 1024 * 1024),
        )(*(pltpu.with_memory_space_constraint(part, pltpu.VMEM) for part in results))
        grad_frames = flat_grad.reshape(height, width, feat // 128, slots, 128).transpose(0, 1, 3, 2, 4)
        return grad_frames.reshape(height, width, slots, feat).transpose(2, 0, 1, 3), *rest

    split = P("clip")
    in_specs = (split,) + (P(),) * 9 + (split,) * 3 + (P(), P())
    out_specs = (split,) + (P(),) * 9
    return jax.shard_map(shards, mesh=mesh, in_specs=in_specs, out_specs=out_specs, check_vma=False)


def arg_names():
    return dict(
        frames=0, w_reduce=0, w_spatial=0, w_expand=0, gain_a=0, bias_a=0, gain_b=0, bias_b=0, gain_c=0, bias_c=0,
        clip_ids=0, segment_ids=0, slot_valid=0, segment_weight=0, loss_weight=0,
    )
```

```python
import functools
from types import SimpleNamespace

import jax
import jax.numpy as jnp
from jax import lax
from jax.experimental import pallas as pl
from jax.experimental.pallas import tpu as pltpu
from jax.sharding import PartitionSpec as P

MESH = pl.DeviceIdType.MESH
EPS = 1e-05
F32 = jnp.float32
BF16 = jnp.bfloat16
SIDE = 16
ROWS = SIDE * SIDE
NN = (((1,), (0,)), ((), ()))
NT = (((1,), (1,)), ((), ()))

ORDER = (
    (),
    (),
    (),
    (0,),
    (),
    (),
    (1, 0),
    (2, 3, 1, 0),
    (),
    (2, 3, 0, 4, 1, 5),
    (6, 7, 2, 3, 0, 4),
    (),
    (5, 1),
    (6, 2, 8, 7, 9, 3, 0),
    (4, 10, 5, 1, 6, 8, 2, 7, 11, 3, 9),
    (4, 0, 5, 10, 1, 6, 8, 2),
    (7, 11, 0, 3, 4, 9, 10, 5),
    (),
    (1, 6),
    (8, 2, 11, 7),
    (3, 9, 1, 4, 10, 5, 2, 6, 8),
    (7, 11, 3),
    (9, 4, 10, 5, 11, 6, 4, 8, 5, 7, 9, 10, 6, 11, 8, 7, 9, 10, 8, 11, 9, 10, 11),
)


def dot(a, b, dims=NN):
    return lax.dot_general(a, b, dims, preferred_element_type=F32)


def wait_bytes(ref, sem):
    pltpu.make_async_copy(ref, ref, sem).wait()


def spread_lanes(ref, value):
    depth = value.shape[0]
    for q in range(value.shape[1] // 128):
        ref[q * depth : (q + 1) * depth, :] = value[:, q * 128 : (q + 1) * 128]


def by_rows(ref, value):
    def step(k, carry):
        here = pl.ds(pl.multiple_of(k * 256, 256), 256)
        ref[here, :] = value(here)
        return carry

    lax.fori_loop(0, ref.shape[0] // 256, step, 0)


def moved_rows(here, at):
    return pl.ds(pl.multiple_of(here.start + at, SIDE), 256)


def block(k, y):
    return pl.multiple_of(k * ROWS + y * SIDE, SIDE)


def to_dense(ref, at, value, first):
    for q in range(value.shape[1] // 128):
        ref[at, pl.ds(first + q, 1), :] = value[:, q * 128 : (q + 1) * 128]


def row_form(ref, row, source, first, count):
    for q in range(count):
        ref[row : row + 1, q * 128 : (q + 1) * 128] = source[first + q : first + q + 1, :]


def three(ref, at, left, middle, right):
    here, wide = pl.ds(at + SIDE, SIDE), middle.shape[1]
    ref[here, 0:wide] = left.astype(BF16)
    ref[here, wide : 2 * wide] = middle.astype(BF16)
    ref[here, 2 * wide : 3 * wide] = right.astype(BF16)


def dense_of(ref1, scratch):
    count = ref1.shape[0] // 128
    for q in range(count):
        scratch[q : q + 1, :] = ref1[q * 128 : (q + 1) * 128].reshape(1, 128)
    return scratch[0:count, :]


class Step:
    def __init__(self, cfg, r):
        self.r, self.sizes = r, cfg
        self.n, self.slots, self.height, self.width, self.feat, self.mid = cfg
        self.live = self.slots - 1
        self.rows = self.live * ROWS
        self.area = self.height * self.width
        self.inner = 8
        self.outer = self.n // 8
        self.quad = min(4, self.outer)
        self.far = self.outer // self.quad
        self.loads = {}
        self.mask = lax.broadcasted_iota(jnp.int32, (SIDE, 256), 0) < self.width

    def load(self, **pairs):
        for name, (src, dst) in pairs.items():
            copy = pltpu.make_async_copy(src, dst, self.r.load_sem.at[len(self.loads)])
            copy.start()
            self.loads[name] = copy

    def loaded(self, **names):
        for name in names:
            self.loads[name].wait()

    def fold(self, value):
        return jnp.sum(jnp.where(self.mask, value, 0.0), axis=0, keepdims=True)

    def slot_facts(self):
        r, live = self.r, self.live
        alive, later = 1, []
        for k in range(live):
            alive = alive * r.valid[k]
            later.append(1 - alive)
        self.keep = [(1 - q).astype(F32) for q in later]
        self.moved = [q.astype(F32) for q in later]
        self.later = later
        self.v = [self.kept(r.valid, k) for k in range(live)]
        self.n_own = (self.v[0] + self.v[1] + self.v[2]) * float(self.area)

    def kept(self, values, k):
        return (values[k] + self.later[k] * (values[k + 1] - values[k])).astype(F32)

    def places(self):
        n = self.n
        self.me = me = lax.axis_index("clip")
        self.low, self.high = low, high = me % self.inner, me // self.inner
        self.direct = n <= 32
        self.peers = [(me + o) % n for o in range(1, n)]
        self.low_peers = [me - low + (low + o) % self.inner for o in range(1, self.inner)]
        self.high_peers = [low + self.inner * ((high + o) % self.outer) for o in range(1, self.outer)]
        self.clip_peers = [(me + o) % n for o in (1, n - 1, n // 2, n // 2 - 1, n // 2 + 1)]

    def greet(self):
        self.greeted = self.peers if self.direct else self.low_peers + self.high_peers + self.clip_peers
        self.barrier = pltpu.get_barrier_semaphore()
        for device in self.greeted:
            pl.semaphore_signal(self.barrier, inc=1, device_id=(device,), device_id_type=MESH)

    def all_here(self):
        pl.semaphore_wait(self.barrier, len(self.greeted))

    def send(self, src, dst, ssem, rsem, device):
        pltpu.make_async_remote_copy(
            src_ref=src, dst_ref=dst, send_sem=ssem, recv_sem=rsem, device_id=(device,), device_id_type=MESH
        ).start()

    def one_stage(self, at):
        return self.direct and at not in (2, 3)

    def near_at(self, at):
        return self.me if self.one_stage(at) else self.low

    def near_send(self, at):
        buf, mine = self.r.near[at], self.near_at(at)
        for device in self.peers if self.one_stage(at) else self.low_peers:
            self.send(buf.at[mine], buf.at[mine], self.r.near_s.at[at], self.r.near_r.at[at], device)

    def near_wait(self, at, sems):
        buf = self.r.near[at]
        wait_bytes(buf.at[pl.ds(0, buf.shape[0] - 1)], sems.at[at])

    def wide_send(self, at):
        buf = self.r.wide[at]
        for device in self.high_peers:
            self.send(buf.at[self.high], buf.at[self.high], self.r.wide_s.at[at], self.r.wide_r.at[at], device)

    def wide_wait(self, at, sems):
        wait_bytes(self.r.wide[at].at[pl.ds(0, self.outer - 1)], sems.at[at])

    def all_sent(self, *rounds):
        for at in rounds:
            self.near_wait(at, self.r.near_s)
            if not self.one_stage(at):
                self.wide_wait(at, self.r.wide_s)

    def near_count(self, q):
        return self.r.near[0][(self.me - self.low + q) if self.direct else q, 4:5, :]

    def wide_count(self, q):
        return self.r.plane[q, 0:1, :] if self.direct else self.r.wide[0][q, 4:5, :]

    def stats_near(self, at, count):
        if self.one_stage(at):
            return
        self.near_wait(at, self.r.near_r)
        n_all, s_all, _, spread = combine(self.r.near[at], self.near_count, self.inner, count)
        buf = self.r.wide[at]
        buf[self.high, 0:count, :] = s_all
        buf[self.high, count : 2 * count, :] = spread
        if at == 0:
            buf[self.high, 4:5, :] = n_all
        self.wide_send(at)

    def stats_wide(self, at, count, table):
        r = self.r
        if self.one_stage(at):
            self.near_wait(at, r.near_r)
            counts = r.near[0]
            n_all, _, mean, spread = combine(r.near[at], lambda q: counts[q, 4:5, :], self.n, count)
            if at == 0:
                for q in range(self.outer):
                    r.plane[q, 0:1, :] = sum(counts[q * self.inner + m, 4:5, :] for m in range(self.inner))
        else:
            self.wide_wait(at, r.wide_r)
            n_all, _, mean, spread = combine(r.wide[at], self.wide_count, self.outer, count)
        inverse = lax.rsqrt(spread / n_all + EPS)
        r.dense[0:count, :] = mean
        row_form(table, 0, r.dense, 0, count)
        r.dense[0:count, :] = inverse
        row_form(table, 1, r.dense, 0, count)
        return n_all, inverse

    def sums_near(self, at):
        if not self.one_stage(at):
            self.near_wait(at, self.r.near_r)
            self.r.wide[at][self.high] = total(self.r.near[at])
            self.wide_send(at)

    def sums_wide(self, at):
        if self.one_stage(at):
            self.near_wait(at, self.r.near_r)
            return total(self.r.near[at])
        self.wide_wait(at, self.r.wide_r)
        return total(self.r.wide[at])

    def local_stats(self, buf, at, ref):
        channels = ref.shape[1]
        count = channels // 128
        for c in range(channels // 256):
            lanes = slice(c * 256, (c + 1) * 256)

            def gather(term):
                acc = jnp.zeros((SIDE, 256), F32)
                for k in range(self.live):
                    part = lax.fori_loop(
                        0, self.height, lambda y, a: a + term(ref[pl.ds(block(k, y), SIDE), lanes]),
                        jnp.zeros((SIDE, 256), F32), unroll=self.height,
                    )
                    acc = acc + part * self.v[k]
                return self.fold(acc)

            s_own = gather(lambda x: x)
            mean = s_own / jnp.maximum(self.n_own, 1.0)
            to_dense(buf, at, s_own, 2 * c)
            to_dense(buf, at, gather(lambda x: (x - mean) * (x - mean)), count + 2 * c)

    def norm_silu(self, ref, slope_ref, table, gain, bias, write):
        centre, scale = table[0:1, :], table[1:2, :] * gain[...].reshape(1, self.mid)
        b = bias[...].reshape(1, self.mid)
        for k in range(self.live):
            def step(y, carry):
                at = block(k, y)
                u = (ref[pl.ds(at, SIDE), :] - centre) * scale + b
                s = 0.5 * jnp.tanh(0.5 * u) + 0.5
                h = u * s
                slope_ref[pl.ds(at, SIDE), :] = jnp.where(self.mask, s + (h - h * s), 0.0)
                write(at, jnp.where(self.mask, h, 0.0))
                return carry

            lax.fori_loop(0, self.height, step, 0, unroll=7)


def combine(buf, counts, group, count):
    n_part = [counts(q) for q in range(group)]
    s_part = [buf[q, 0:count, :] for q in range(group)]
    n_all = sum(n_part[1:], n_part[0])
    s_all = sum(s_part[1:], s_part[0])
    mean = s_all / jnp.maximum(n_all, 1.0)
    spread = jnp.zeros((count, 128), F32)
    for q in range(group):
        gap = s_part[q] / jnp.maximum(n_part[q], 1.0) - mean
        spread = spread + (buf[q, count : 2 * count, :] + n_part[q] * gap * gap)
    return n_all, s_all, mean, spread


def total(buf):
    out = buf[0]
    for q in range(1, buf.shape[0]):
        out = out + buf[q]
    return out


def clear(*refs):
    for ref in refs:
        ref[...] = jnp.zeros(ref.shape, ref.dtype)


def prologue(t):
    r, slots, live, width, feat = t.r, t.slots, t.live, t.width, t.feat
    t.places()
    t.greet()
    t.load(
        frames=(r.frames, r.f4.at[pl.ds(0, t.area)]), valid=(r.slot_valid, r.valid), reduce=(r.w_reduce, r.wr),
        clip=(r.clip_ids, r.clip), segment=(r.segment_ids, r.segment),
        share=(r.segment_weight, r.share), spatial=(r.w_spatial, r.ws), expand=(r.w_expand, r.we),
        ga=(r.gain_a, r.ga), ba=(r.bias_a, r.ba), gb=(r.gain_b, r.gb), bb=(r.bias_b, r.bb),
        gc=(r.gain_c, r.gc), bc=(r.bias_c, r.bc), loss=(r.loss_weight, r.loss),
    )
    for i in range(3):
        for j in range(3):
            pltpu.make_async_copy(
                r.w_spatial.at[i, j], r.wc.at[i, :, pl.ds(j * t.mid, t.mid)], r.load_sem.at[15]
            ).start()
    r.f4[t.area :] = jnp.zeros((r.f4.shape[0] - t.area, *r.f4.shape[1:]), BF16)
    clear(r.fp)
    t.loaded(valid=0)
    t.slot_facts()
    t.loaded(frames=0)
    fp, f4 = r.fp, r.f4
    tiles = feat // 128
    group = SIDE // slots
    short = lax.broadcasted_iota(jnp.int32, (SIDE, 128), 0) < width

    def regroup(y, carry):
        for p in range(tiles // group):
            value = f4[pl.ds(y * width, SIDE), p * SIDE : (p + 1) * SIDE, :].astype(F32)
            value = jnp.swapaxes(value, 0, 1)
            for q in range(group):
                for k in range(live):
                    row = value[q * slots + k] * t.keep[k] + value[q * slots + k + 1] * t.moved[k]
                    lanes = slice((p * group + q) * 128, (p * group + q + 1) * 128)
                    fp[pl.ds(block(k, y), SIDE), lanes] = jnp.where(short, row, 0.0).astype(BF16)
        return carry

    lax.fori_loop(0, t.height, regroup, 0)
    t.loaded(reduce=0)
    by_rows(r.pre_a, lambda here: dot(fp[here, :], r.wr[...]))
    t.local_stats(r.near[0], t.near_at(0), r.pre_a)
    r.near[0][t.near_at(0), 4:5, :] = jnp.full((1, 128), t.n_own, F32)


def forward(t):
    r, live, mid, feat, rows, area, height = t.r, t.live, t.mid, t.feat, t.rows, t.area, t.height
    t.all_here()
    t.near_send(0)
    r.ft[...] = r.fp[...].T
    t.stats_near(0, mid // 128)
    clear(r.xp, r.hb, r.g3, r.gpc, r.gpa)
    t.loaded(clip=0, segment=0, share=0, ga=0, ba=0, gb=0, bb=0, gc=0, bc=0, loss=0, spatial=0, expand=0)
    key = [t.kept(r.clip, k) for k in range(live)]
    weight = []
    for k in range(live):
        at = t.kept(r.segment, k)
        w0, w1, w2 = (r.share[q] for q in range(3))
        weight.append(
            t.v[k] * (w0 * ((1.0 - at) * (2.0 - at) * 0.5) + w1 * (at * (2.0 - at)) + w2 * (at * (at - 1.0) * 0.5))
        )
    n_all, inv_a = t.stats_wide(0, mid // 128, r.table_a)

    xp, hb = r.xp, r.hb

    def write_a(at, h):
        three(xp, at, pltpu.roll(h, 1, 0), h, pltpu.roll(h, SIDE - 1, 0))

    t.norm_silu(r.pre_a, r.slope_a, r.table_a, r.ga, r.ba, write_a)

    by_rows(
        r.pre_b,
        lambda here: sum(dot(xp[moved_rows(here, i * SIDE), :], r.ws[i].reshape(3 * mid, mid)) for i in range(3)),
    )
    t.local_stats(r.near[1], t.near_at(1), r.pre_b)
    t.near_send(1)
    r.xt[...] = xp[SIDE : SIDE + rows, mid : 2 * mid].T
    t.stats_near(1, mid // 128)
    _, inv_b = t.stats_wide(1, mid // 128, r.table_b)

    def write_b(at, h):
        hb[pl.ds(at, SIDE), :] = h.astype(BF16)

    t.norm_silu(r.pre_b, r.slope_b, r.table_b, r.gb, r.bb, write_b)

    pre_c, slope_c, fp, table_c = r.pre_c, r.slope_c, r.fp, r.table_c
    by_rows(pre_c, lambda here: dot(hb[here, :], r.we[...]))
    t.local_stats(r.near[2], t.near_at(2), pre_c)
    t.near_send(2)
    r.hbt[...] = hb[...].T
    t.stats_near(2, feat // 128)
    _, inv_c = t.stats_wide(2, feat // 128, table_c)

    pool, slope_sum, slope_hat = r.pool, r.slope_sum, r.slope_hat
    for c in range(feat // 256):
        lanes = slice(c * 256, (c + 1) * 256)
        centre, inverse = table_c[0:1, lanes], table_c[1:2, lanes]
        g = r.gc[lanes].reshape(1, 256)
        b = r.bc[lanes].reshape(1, 256)
        for k in range(live):
            def step(y, carry):
                a0, a1, a2 = carry
                at = block(k, y)
                hat = (pre_c[pl.ds(at, SIDE), lanes] - centre) * inverse
                u = hat * g + b + fp[pl.ds(at, SIDE), lanes].astype(F32)
                s = 0.5 * jnp.tanh(0.5 * u) + 0.5
                h = u * s
                slope = s + (h - h * s)
                slope_c[pl.ds(at, SIDE), lanes] = slope
                return a0 + h, a1 + slope, a2 + slope * hat

            zero = jnp.zeros((SIDE, 256), F32)
            a0, a1, a2 = lax.fori_loop(0, height, step, (zero, zero, zero), unroll=7)
            p_row = (t.fold(a0) * (1.0 / area)).astype(BF16).astype(F32)
            to_dense(pool, 0, p_row, 8 * k + 2 * c)
            to_dense(slope_sum, k, t.fold(a1), 2 * c)
            to_dense(slope_hat, k, t.fold(a2), 2 * c)
    for k in range(live):
        pool[0, 24 + k : 25 + k, :] = jnp.full((1, 128), key[k], F32)
        pool[0, 28 + k : 29 + k, :] = jnp.full((1, 128), weight[k], F32)
    for q, device in enumerate(t.clip_peers):
        t.send(pool.at[0], pool.at[q + 1], r.pool_s.at[0], r.pool_r.at[0], device)
    wait_bytes(pool.at[pl.ds(1, len(t.clip_peers))], r.pool_r.at[0])

    lw = dense_of(r.loss, r.dense)
    grads = []
    for k in range(live):
        my_key = jnp.full((1, 128), key[k], F32)
        my_weight = jnp.full((1, 128), weight[k], F32)
        mean = jnp.zeros((8, 128), F32)
        den = jnp.zeros((1, 128), F32)
        for q in range(len(t.clip_peers) + 1):
            for m in range(live):
                match = jnp.where(pool[q, 24 + m : 25 + m, :] == my_key, pool[q, 28 + m : 29 + m, :], 0.0)
                den = den + match
                mean = mean + match * pool[q, 8 * m : 8 * m + 8, :]
        den = jnp.where(den == 0.0, 1.0, den)
        mean = mean / den
        power = jnp.sum(jnp.sum(mean * mean, axis=0, keepdims=True), axis=1, keepdims=True)
        scale = lax.rsqrt(power * (1.0 / feat) + EPS)
        unit = mean * scale
        along = jnp.sum(jnp.sum(unit * lw, axis=0, keepdims=True), axis=1, keepdims=True)
        mean_grad = scale * (lw - unit * (along * (1.0 / feat)))
        grads.append((my_weight / den) * mean_grad * (1.0 / area))

    near3 = r.near[3]
    shift = jnp.zeros((8, 128), F32)
    gain = jnp.zeros((8, 128), F32)
    for k in range(live):
        shift = shift + grads[k] * slope_sum[k]
        gain = gain + grads[k] * slope_hat[k]
    near3[t.near_at(3), 0:8, :] = shift
    near3[t.near_at(3), 8:16, :] = gain
    t.near_send(3)
    coef, dense = r.coef, r.dense
    scale_c = dense_of(r.gc, dense) * inv_c
    for k in range(live):
        dense[...] = grads[k]
        row_form(coef, k, dense, 0, feat // 128)
        dense[...] = grads[k] * scale_c
        row_form(coef, 3 + k, dense, 0, feat // 128)
    t.sums_near(3)
    both = t.sums_wide(3)
    r.vectors_c[...] = both
    dense[...] = both[0:8] * scale_c / n_all
    row_form(coef, 6, dense, 0, feat // 128)
    dense[...] = both[8:16] * scale_c * inv_c / n_all
    row_form(coef, 7, dense, 0, feat // 128)
    return n_all, inv_a, inv_b


def backward(t, n_all, inv_a, inv_b):
    r, live, mid, feat, rows, height = t.r, t.live, t.mid, t.feat, t.rows, t.height
    slots, width, quad, far, v, wc = t.slots, t.width, t.quad, t.far, t.v, r.wc
    coef, pre_c, slope_c, out = r.coef, r.pre_c, r.slope_c, r.vectors
    me, send = t.me, t.send
    gpc = r.gpc
    for k in range(live):
        for c in range(feat // 256):
            lanes = slice(c * 256, (c + 1) * 256)
            centre = r.table_c[0:1, lanes]
            c0 = coef[3 + k : 4 + k, lanes]
            c1 = coef[6:7, lanes] * v[k]
            c2 = coef[7:8, lanes] * v[k]

            def step(y, carry):
                at = block(k, y)
                grad = slope_c[pl.ds(at, SIDE), lanes] * c0 - (c1 + (pre_c[pl.ds(at, SIDE), lanes] - centre) * c2)
                gpc[pl.ds(at, SIDE), lanes] = grad.astype(BF16)
                return carry

            lax.fori_loop(0, height, step, 0, unroll=7)

    def back_sums(at, table, inv, grad_ref, slope_ref, pre_ref):
        zero = jnp.zeros((SIDE, mid), F32)
        carry = (zero, zero)
        centre = table[0:1, :]
        for k in range(live):
            def step(y, c):
                here = pl.ds(block(k, y), SIDE)
                grad = grad_ref[here, :] * slope_ref[here, :]
                grad_ref[here, :] = grad
                return c[0] + grad, c[1] + grad * (pre_ref[here, :] - centre)

            carry = lax.fori_loop(0, height, step, carry, unroll=7)
        buf = r.near[at]
        to_dense(buf, t.near_at(at), jnp.sum(carry[0], axis=0, keepdims=True), 0)
        to_dense(buf, t.near_at(at), jnp.sum(carry[1], axis=0, keepdims=True) * table[1:2, :], 2)

    def back_apply(at, table, gain_ref, inv, grad_ref, pre_ref, write):
        both = t.sums_wide(at)
        out[8 * at - 32 : 8 * at - 28, :] = both[0:4]
        dense = r.dense
        scale = dense_of(gain_ref, dense) * inv
        dense[0:2, :] = scale
        dense[2:4, :] = both[0:2] * scale / n_all
        dense[4:6, :] = both[2:4] * scale * inv / n_all
        for q in range(3):
            row_form(table, 2 + q, dense, 2 * q, 2)
        centre = table[0:1, :]
        for k in range(live):
            c0, c1, c2 = table[2:3, :], table[3:4, :] * v[k], table[4:5, :] * v[k]

            def step(y, carry):
                at_row = block(k, y)
                here = pl.ds(at_row, SIDE)
                write(at_row, grad_ref[here, :] * c0 - (c1 + (pre_ref[here, :] - centre) * c2))
                return carry

            lax.fori_loop(0, height, step, 0, unroll=7)

    core, bit_x, bit_y, at_z = me % 2, (me // 2) % 2, (me // 4) % 2, (me // 8) % quad
    at_far = me // (8 * quad)
    bit1 = bit_x + core * (bit_y - bit_x)
    bit2 = bit_y + core * (bit_x - bit_y)
    sibling = me + 1 - 2 * core
    peer1 = me + (1 - 2 * bit1) * (2 + 2 * core)
    peer2 = me + (1 - 2 * bit2) * (4 - 2 * core)
    z_at = [(at_z + o) % quad for o in range(1, quad)]
    z_peer = [me + 8 * (q - at_z) for q in z_at]
    far_peer = [me + 8 * quad * ((at_far + o) % far - at_far) for o in range(1, far)]
    chunk_s, chunk_r = r.chunk_s, r.chunk_r
    waits, blocks = [], iter(ORDER)
    plan = [(0, q, 2) for q in range(2)] + [(1 + q // 2, q % 2, 2) for q in range(6)] + [(4, q, 4) for q in range(4)]

    def chunk(q):
        name, at, count = plan[q]
        size = r.part[name].shape[0] // count
        part = r.part[name].at[pl.ds(at * size, size)]
        whole = (r.e, r.s0, r.s1, r.s2, r.r)[name].at[pl.ds(at * size, size)]
        half, quarter, eighth, piece = size // 2, size // 4, size // 8, size // (8 * quad)
        m8 = lambda value: pl.multiple_of(value, 8)
        at_h = m8(core * half)
        at_q = m8(at_h + bit1 * quarter)
        at_e = m8(at_q + bit2 * eighth)
        at_p = m8(at_e + at_z * piece)

        def go(step, src, dst, device):
            send(src, dst, chunk_s.at[q, step], chunk_r.at[q, step], device)

        def finish(step, ref):
            wait_bytes(ref, chunk_r.at[q, step])
            waits.append((ref, chunk_s.at[q, step]))

        rb0, rb1, rb2, rb3 = r.rb0[q], r.rb1[q], r.rb2[q], r.rb3[q]
        go(0, part.at[pl.ds(m8((1 - core) * half), half)], rb0, sibling)
        yield
        finish(0, rb0)
        part[pl.ds(at_h, half), :] = part[pl.ds(at_h, half), :] + rb0[...]
        go(1, part.at[pl.ds(m8(at_h + (1 - bit1) * quarter), quarter)], rb1, peer1)
        yield
        finish(1, rb1)
        part[pl.ds(at_q, quarter), :] = part[pl.ds(at_q, quarter), :] + rb1[...]
        go(2, part.at[pl.ds(m8(at_q + (1 - bit2) * eighth), eighth)], rb2, peer2)
        yield
        finish(2, rb2)
        part[pl.ds(at_e, eighth), :] = part[pl.ds(at_e, eighth), :] + rb2[...]
        for o in range(quad - 1):
            go(3, part.at[pl.ds(m8(at_e + z_at[o] * piece), piece)], rb3.at[pl.ds(o * piece, piece)], z_peer[o])
        yield
        finish(3, rb3)
        own = part[pl.ds(at_p, piece), :]
        for o in range(quad - 1):
            own = own + rb3[o * piece : (o + 1) * piece, :]
        if far > 1:
            rb4 = r.rb4[q]
            rb4[at_far] = own
            for device in far_peer:
                go(8, rb4.at[at_far], rb4.at[at_far], device)
            yield
            finish(8, rb4.at[pl.ds(0, far - 1)])
            own = rb4[0]
            for o in range(1, far):
                own = own + rb4[o]
        whole[pl.ds(at_p, piece), :] = own
        for o in range(quad - 1):
            go(4, whole.at[pl.ds(at_p, piece)], whole.at[pl.ds(at_p, piece)], z_peer[o])
        yield
        finish(4, whole.at[pl.ds(0, (quad - 1) * piece)])
        go(5, whole.at[pl.ds(at_e, eighth)], whole.at[pl.ds(at_e, eighth)], peer2)
        yield
        finish(5, whole.at[pl.ds(0, eighth)])
        go(6, whole.at[pl.ds(at_q, quarter)], whole.at[pl.ds(at_q, quarter)], peer1)
        yield
        finish(6, whole.at[pl.ds(0, quarter)])
        go(7, whole.at[pl.ds(at_h, half)], whole.at[pl.ds(at_h, half)], sibling)
        yield
        finish(7, whole.at[pl.ds(0, half)])
        yield

    chunks = [chunk(q) for q in range(len(plan))]

    def go_on(*which):
        for q in which:
            next(chunks[q])

    def go_on_all():
        go_on(*next(blocks))

    pre_a, slope_a, pre_b, slope_b, hbt, xt = r.pre_a, r.slope_a, r.pre_b, r.slope_b, r.hbt, r.xt
    we, wr, back = r.we, r.wr, r.back
    tiles = feat // 128
    group = SIDE // slots
    keep, moved, mask = t.keep, t.moved, t.mask
    grad_b, grad_a = r.grad_b, r.grad_a
    wait_bytes(wc, r.load_sem.at[15])
    g3 = r.g3

    def write_gb(at, grad):
        grad = jnp.where(mask, grad, 0.0)
        three(g3, at, pltpu.roll(grad, SIDE - 1, 0), grad, pltpu.roll(grad, 1, 0))

    def expand_part(e):
        go_on_all()
        for q in range(2):
            first = (2 * e + q) * 256
            spread_lanes(r.part[0].at[pl.ds(2 * first, 512)], dot(hbt[...], gpc[:, first : first + 256]))
        go_on(e)

    def spatial_part(i):
        go_on_all()
        spread_lanes(r.part[1 + i], dot(xt[...], g3[(2 - i) * SIDE : (2 - i) * SIDE + rows, :]))
        go_on(2 + 2 * i, 3 + 2 * i)

    go_on_all()
    expand_part(0)
    go_on_all()
    by_rows(grad_b, lambda here: dot(gpc[here, :], we[...], NT))
    back_sums(4, r.table_b, inv_b, grad_b, slope_b, pre_b)
    t.near_send(4)
    expand_part(1)
    go_on_all()
    back_apply(4, r.table_b, r.gb, inv_b, grad_b, pre_b, write_gb)
    spatial_part(0)
    go_on_all()
    by_rows(
        grad_a, lambda here: sum(dot(g3[moved_rows(here, (2 - i) * SIDE), :], wc[i], NT) for i in range(3))
    )
    back_sums(5, r.table_a, inv_a, grad_a, slope_a, pre_a)
    t.near_send(5)
    spatial_part(1)
    spatial_part(2)
    go_on_all()
    gpa = r.gpa

    def write_ga(at, grad):
        gpa[pl.ds(at, SIDE), :] = grad.astype(BF16)

    back_apply(5, r.table_a, r.ga, inv_a, grad_a, pre_a, write_ga)
    for q in range(4):
        go_on_all()
        spread_lanes(r.part[4].at[pl.ds(q * 512, 512)], dot(r.ft[q * 256 : (q + 1) * 256, :], gpa[...]))
        go_on(8 + q)

    go_on_all()
    by_rows(back, lambda here: dot(gpa[here, :], wr[...], NT))
    gf = r.gf

    def blend(y, carry):
        for p in range(tiles // group):
            values = []
            for q in range(group):
                lanes = slice((p * group + q) * 128, (p * group + q + 1) * 128)
                terms = [
                    slope_c[pl.ds(block(k, y), SIDE), lanes] * coef[k : k + 1, lanes]
                    + back[pl.ds(block(k, y), SIDE), lanes]
                    for k in range(live)
                ]
                values.append(terms[0] * keep[0])
                for m in range(1, live):
                    values.append(terms[m] * keep[m] + terms[m - 1] * moved[m - 1])
                values.append(terms[live - 1] * moved[live - 1])
            value = jnp.swapaxes(jnp.stack(values), 0, 1)
            gf[pl.ds(y * width, width), p * SIDE : (p + 1) * SIDE, :] = value[0:width].astype(BF16)
        return carry

    for q in range(height // 2):
        go_on_all()
        for y in range(2):
            blend(2 * q + y, 0)
    go_on_all()
    for each in chunks:
        for _ in each:
            pass

    t.all_sent(*range(6))
    wait_bytes(r.pool.at[pl.ds(1, len(t.clip_peers))], r.pool_s.at[0])
    for ref, sem in waits:
        wait_bytes(ref, sem)


def store(gf, vectors_c, vectors, expand, s0, s1, s2, reduce, frames_out, reduce_out, spatial_out, expand_out, *rest):
    ga, ba, gb, bb, gc, bc, *scratch, sem = rest
    vectors_of = (
        (bc, vectors_c, 0), (gc, vectors_c, 8), (bb, vectors, 0), (gb, vectors, 2), (ba, vectors, 8), (ga, vectors, 10)
    )
    pltpu.make_async_copy(gf, frames_out, sem.at[0]).start()
    for number, (ref, source, first) in enumerate(vectors_of):
        for q in range(ref.shape[0] // 128):
            scratch[number][q * 128 : (q + 1) * 128] = source[first + q : first + q + 1, :].reshape(128)
        pltpu.make_async_copy(scratch[number], ref, sem.at[6 + number]).start()
    depth, width = reduce_out.shape
    for q in range(depth // 256):
        for m in range(width // 128):
            pltpu.make_async_copy(
                reduce.at[pl.ds((q * width // 128 + m) * 256, 256)],
                reduce_out.at[pl.ds(q * 256, 256), pl.ds(m * 128, 128)],
                sem.at[1],
            ).start()
    depth, width = expand_out.shape
    for q in range(width // 128):
        pltpu.make_async_copy(
            expand.at[pl.ds(q * depth, depth)], expand_out.at[:, pl.ds(q * 128, 128)], sem.at[2]
        ).start()
    for i, part in enumerate((s0, s1, s2)):
        for q in range(part.shape[0] // depth):
            pltpu.make_async_copy(
                part.at[pl.ds(q * depth, depth)],
                spatial_out.at[i, q * 128 // depth, :, pl.ds(q * 128 % depth, 128)],
                sem.at[3 + i],
            ).start()
    wait_bytes(gf, sem.at[0])
    wait_bytes(reduce, sem.at[1])
    wait_bytes(expand, sem.at[2])
    for i, part in enumerate((s0, s1, s2)):
        wait_bytes(part, sem.at[3 + i])
    for number in range(6):
        wait_bytes(scratch[number], sem.at[6 + number])


def solution(mesh):
    n = mesh.shape["clip"]

    def shards(*args):
        slots, height, width, feat = args[0].shape
        mid = args[1].shape[1]
        rows = (slots - 1) * ROWS
        outer = n // 8
        quad = min(4, outer)
        far = outer // quad
        cfg = (n, slots, height, width, feat, mid)
        flat_shape = (height * width, slots * feat // 128, 128)
        hbm = pl.BlockSpec(memory_space=pltpu.HBM)
        vmem = pl.BlockSpec(memory_space=pltpu.VMEM)
        dma = pltpu.SemaphoreType.DMA
        depths = list(enumerate((8, 4, 16, 16, 4, 4)))
        matrix, third = mid * feat // 128, 3 * mid * mid // 128
        sizes = [matrix, third, third, third, matrix]

        tiled = args[0].transpose(1, 2, 0, 3).reshape(height, width, slots, feat // 128, 128)
        tiled = tiled.transpose(0, 1, 3, 2, 4).reshape(flat_shape)
        given = [pltpu.with_memory_space_constraint(part, pltpu.HBM) for part in (tiled, *args[1:])]

        vm = pltpu.VMEM
        narrow, broad, square = vm((mid,), F32), vm((feat,), F32), vm((rows, mid), F32)
        ints = pltpu.SMEM((slots,), jnp.int32)
        plan = [matrix // 2] * 2 + [third // 2] * 6 + [matrix // 4] * 4
        outs = dict(
            gf=vm(flat_shape, BF16), vectors_c=vm((16, 128), F32), vectors=vm((16, 128), F32),
            e=vm((matrix, 128), F32), s0=vm((third, 128), F32), s1=vm((third, 128), F32), s2=vm((third, 128), F32),
            r=vm((matrix, 128), F32),
        )
        scratch = dict(
            f4=vm((flat_shape[0] + SIDE - width, *flat_shape[1:]), BF16),
            fp=vm((rows, feat), BF16), ft=vm((feat, rows), BF16),
            wr=vm((feat, mid), BF16), ws=vm((3, 3, mid, mid), BF16), wc=vm((3, mid, 3 * mid), BF16), we=vm((mid, feat), BF16),
            valid=ints, clip=ints, segment=ints, share=pltpu.SMEM(args[13].shape, F32),
            ga=narrow, ba=narrow, gb=narrow, bb=narrow, gc=broad, bc=broad, loss=broad,
            xp=vm((rows + 2 * SIDE, 3 * mid), BF16), xt=vm((mid, rows), BF16),
            hb=vm((rows, mid), BF16), hbt=vm((mid, rows), BF16),
            pre_a=square, slope_a=square, pre_b=square, slope_b=square, grad_a=square, grad_b=square,
            pre_c=vm((rows, feat), F32), slope_c=vm((rows, feat), F32), back=vm((rows, feat), F32),
            gpc=vm((rows, feat), BF16), g3=vm((rows + 2 * SIDE, 3 * mid), BF16), gpa=vm((rows, mid), BF16),
            table_a=vm((8, mid), F32), table_b=vm((8, mid), F32),
            table_c=vm((8, feat), F32), coef=vm((8, feat), F32), dense=vm((8, 128), F32),
            pool=vm((6, 32, 128), F32), slope_sum=vm((3, 8, 128), F32), slope_hat=vm((3, 8, 128), F32),
            near=[vm((n if n <= 32 and at not in (2, 3) else 8, deep, 128), F32) for at, deep in depths],
            wide=[vm((outer, deep, 128), F32) for at, deep in depths],
            plane=vm((outer, 8, 128), F32),
            part=[vm((size, 128), F32) for size in sizes],
            rb0=[vm((size // 2, 128), F32) for size in plan],
            rb1=[vm((size // 4, 128), F32) for size in plan],
            rb2=[vm((size // 8, 128), F32) for size in plan],
            rb3=[vm(((quad - 1) * size // (8 * quad), 128), F32) for size in plan],
            rb4=[vm((far, size // (8 * quad), 128), F32) for size in plan if far > 1],
            load_sem=dma((16,)), near_s=dma((6,)), near_r=dma((6,)), wide_s=dma((6,)), wide_r=dma((6,)),
            pool_s=dma((1,)), pool_r=dma((1,)), chunk_s=dma((12, 9)), chunk_r=dma((12, 9)),
        )
        names = (*arg_names(), *outs, *scratch)

        def kernel(*refs):
            t = Step(cfg, SimpleNamespace(**dict(zip(names, refs, strict=True))))
            prologue(t)
            backward(t, *forward(t))

        results = pl.pallas_call(
            kernel,
            out_shape=list(outs.values()),
            in_specs=[hbm] * len(given),
            out_specs=[vmem] * len(outs),
            scratch_shapes=list(scratch.values()),
            compiler_params=pltpu.CompilerParams(
                collective_id=0, has_side_effects=True, vmem_limit_bytes=50 * 1024 * 1024
            ),
        )(*given)
        vector = jax.ShapeDtypeStruct((mid,), F32)
        wide_vector = jax.ShapeDtypeStruct((feat,), F32)
        flat_grad, *rest = pl.pallas_call(
            store,
            out_shape=[
                jax.ShapeDtypeStruct(flat_shape, BF16),
                jax.ShapeDtypeStruct((feat, mid), F32),
                jax.ShapeDtypeStruct((3, 3, mid, mid), F32),
                jax.ShapeDtypeStruct((mid, feat), F32),
                vector, vector, vector, vector, wide_vector, wide_vector,
            ],
            in_specs=[vmem] * 8,
            out_specs=[hbm] * 10,
            scratch_shapes=[*(vm((c,), F32) for c in (feat, feat, mid, mid, mid, mid)), dma((12,))],
            compiler_params=pltpu.CompilerParams(vmem_limit_bytes=8 * 1024 * 1024),
        )(*(pltpu.with_memory_space_constraint(part, pltpu.VMEM) for part in results))
        grad_frames = flat_grad.reshape(height, width, feat // 128, slots, 128).transpose(0, 1, 3, 2, 4)
        return grad_frames.reshape(height, width, slots, feat).transpose(2, 0, 1, 3), *rest

    split = P("clip")
    in_specs = (split,) + (P(),) * 9 + (split,) * 3 + (P(), P())
    out_specs = (split,) + (P(),) * 9
    return jax.shard_map(shards, mesh=mesh, in_specs=in_specs, out_specs=out_specs, check_vma=False)


def arg_names():
    return dict(
        frames=0, w_reduce=0, w_spatial=0, w_expand=0, gain_a=0, bias_a=0, gain_b=0, bias_b=0, gain_c=0, bias_c=0,
        clip_ids=0, segment_ids=0, slot_valid=0, segment_weight=0, loss_weight=0,
    )
```

```python
import functools
from types import SimpleNamespace

import jax
import jax.numpy as jnp
from jax import lax
from jax.experimental import pallas as pl
from jax.experimental.pallas import tpu as pltpu
from jax.sharding import PartitionSpec as P

MESH = pl.DeviceIdType.MESH
EPS = 1e-05
F32 = jnp.float32
BF16 = jnp.bfloat16
SIDE = 16
ROWS = SIDE * SIDE
NN = (((1,), (0,)), ((), ()))
NT = (((1,), (1,)), ((), ()))

ORDER = (
    (),
    (),
    (),
    (0,),
    (),
    (),
    (1, 0),
    (2, 3, 1, 0),
    (),
    (2, 3, 0, 4, 1, 5),
    (6, 7, 2, 3, 0, 4),
    (),
    (5, 1),
    (6, 2, 8, 7, 9, 3, 0),
    (4, 10, 5, 1, 6, 8, 2, 7, 11, 3, 9),
    (4, 0, 5, 10, 1, 6, 8, 2),
    (7, 11, 0, 3, 4, 9, 10, 5),
    (),
    (1, 6),
    (8, 2, 11, 7),
    (3, 9, 1, 4, 10, 5, 2, 6, 8),
    (7, 11, 3),
    (9, 4, 10, 5, 11, 6, 4, 8, 5, 7, 9, 10, 6, 11, 8, 7, 9, 10, 8, 11, 9, 10, 11),
)


def dot(a, b, dims=NN):
    return lax.dot_general(a, b, dims, preferred_element_type=F32)


def wait_bytes(ref, sem):
    pltpu.make_async_copy(ref, ref, sem).wait()


def spread_lanes(ref, value):
    depth = value.shape[0]
    for q in range(value.shape[1] // 128):
        ref[q * depth : (q + 1) * depth, :] = value[:, q * 128 : (q + 1) * 128]


def by_rows(ref, value):
    def step(k, carry):
        here = pl.ds(pl.multiple_of(k * 256, 256), 256)
        ref[here, :] = value(here)
        return carry

    lax.fori_loop(0, ref.shape[0] // 256, step, 0)


def moved_rows(here, at):
    return pl.ds(pl.multiple_of(here.start + at, SIDE), 256)


def block(k, y):
    return pl.multiple_of(k * ROWS + y * SIDE, SIDE)


def to_dense(ref, at, value, first):
    for q in range(value.shape[1] // 128):
        ref[at, pl.ds(first + q, 1), :] = value[:, q * 128 : (q + 1) * 128]


def row_form(ref, row, source, first, count):
    for q in range(count):
        ref[row : row + 1, q * 128 : (q + 1) * 128] = source[first + q : first + q + 1, :]


def three(ref, at, left, middle, right):
    here, wide = pl.ds(at + SIDE, SIDE), middle.shape[1]
    ref[here, 0:wide] = left.astype(BF16)
    ref[here, wide : 2 * wide] = middle.astype(BF16)
    ref[here, 2 * wide : 3 * wide] = right.astype(BF16)


def dense_of(ref1, scratch):
    count = ref1.shape[0] // 128
    for q in range(count):
        scratch[q : q + 1, :] = ref1[q * 128 : (q + 1) * 128].reshape(1, 128)
    return scratch[0:count, :]


class Step:
    def __init__(self, cfg, r):
        self.r, self.sizes = r, cfg
        self.n, self.slots, self.height, self.width, self.feat, self.mid = cfg
        self.live = self.slots - 1
        self.rows = self.live * ROWS
        self.area = self.height * self.width
        self.inner = 8
        self.outer = self.n // 8
        self.quad = min(4, self.outer)
        self.far = self.outer // self.quad
        self.loads = {}
        self.mask = lax.broadcasted_iota(jnp.int32, (SIDE, 256), 0) < self.width

    def load(self, **pairs):
        for name, (src, dst) in pairs.items():
            copy = pltpu.make_async_copy(src, dst, self.r.load_sem.at[len(self.loads)])
            copy.start()
            self.loads[name] = copy

    def loaded(self, **names):
        for name in names:
            self.loads[name].wait()

    def fold(self, value):
        return jnp.sum(jnp.where(self.mask, value, 0.0), axis=0, keepdims=True)

    def slot_facts(self):
        r, live = self.r, self.live
        alive, later = 1, []
        for k in range(live):
            alive = alive * r.valid[k]
            later.append(1 - alive)
        self.keep = [(1 - q).astype(F32) for q in later]
        self.moved = [q.astype(F32) for q in later]
        self.later = later
        self.v = [self.kept(r.valid, k) for k in range(live)]
        self.n_own = (self.v[0] + self.v[1] + self.v[2]) * float(self.area)

    def kept(self, values, k):
        return (values[k] + self.later[k] * (values[k + 1] - values[k])).astype(F32)

    def places(self):
        n = self.n
        self.me = me = lax.axis_index("clip")
        self.low, self.high = low, high = me % self.inner, me // self.inner
        self.direct = n <= 32
        self.peers = flips(me, n)
        self.low_peers = flips(me, self.inner)
        self.high_peers = flips(me, self.outer, self.inner)
        self.clip_peers = [(me + o) % n for o in (n // 2 - 1, n // 2 + 1, n // 2, n - 1, 1)]

    def greet(self):
        self.greeted = self.peers if self.direct else self.low_peers + self.high_peers + self.clip_peers
        self.barrier = pltpu.get_barrier_semaphore()
        for device in self.greeted:
            pl.semaphore_signal(self.barrier, inc=1, device_id=(device,), device_id_type=MESH)

    def all_here(self):
        pl.semaphore_wait(self.barrier, len(self.greeted))

    def send(self, src, dst, ssem, rsem, device):
        pltpu.make_async_remote_copy(
            src_ref=src, dst_ref=dst, send_sem=ssem, recv_sem=rsem, device_id=(device,), device_id_type=MESH
        ).start()

    def one_stage(self, at):
        return self.direct and at not in (2, 3)

    def near_at(self, at):
        return self.me if self.one_stage(at) else self.low

    def near_send(self, at):
        buf, mine = self.r.near[at], self.near_at(at)
        for device in self.peers if self.one_stage(at) else self.low_peers:
            self.send(buf.at[mine], buf.at[mine], self.r.near_s.at[at], self.r.near_r.at[at], device)

    def near_wait(self, at, sems):
        buf = self.r.near[at]
        wait_bytes(buf.at[pl.ds(0, buf.shape[0] - 1)], sems.at[at])

    def wide_send(self, at):
        buf = self.r.wide[at]
        for device in self.high_peers:
            self.send(buf.at[self.high], buf.at[self.high], self.r.wide_s.at[at], self.r.wide_r.at[at], device)

    def wide_wait(self, at, sems):
        wait_bytes(self.r.wide[at].at[pl.ds(0, self.outer - 1)], sems.at[at])

    def all_sent(self, *rounds):
        for at in rounds:
            self.near_wait(at, self.r.near_s)
            if not self.one_stage(at):
                self.wide_wait(at, self.r.wide_s)

    def near_count(self, q):
        return self.r.near[0][(self.me - self.low + q) if self.direct else q, 4:5, :]

    def wide_count(self, q):
        return self.r.plane[q, 0:1, :] if self.direct else self.r.wide[0][q, 4:5, :]

    def stats_near(self, at, count):
        if self.one_stage(at):
            return
        self.near_wait(at, self.r.near_r)
        n_all, s_all, _, spread = combine(self.r.near[at], self.near_count, self.inner, count)
        buf = self.r.wide[at]
        buf[self.high, 0:count, :] = s_all
        buf[self.high, count : 2 * count, :] = spread
        if at == 0:
            buf[self.high, 4:5, :] = n_all
        self.wide_send(at)

    def stats_wide(self, at, count, table):
        r = self.r
        if self.one_stage(at):
            self.near_wait(at, r.near_r)
            counts = r.near[0]
            n_all, _, mean, spread = combine(r.near[at], lambda q: counts[q, 4:5, :], self.n, count)
            if at == 0:
                for q in range(self.outer):
                    r.plane[q, 0:1, :] = sum(counts[q * self.inner + m, 4:5, :] for m in range(self.inner))
        else:
            self.wide_wait(at, r.wide_r)
            n_all, _, mean, spread = combine(r.wide[at], self.wide_count, self.outer, count)
        inverse = lax.rsqrt(spread / n_all + EPS)
        r.dense[0:count, :] = mean
        row_form(table, 0, r.dense, 0, count)
        r.dense[0:count, :] = inverse
        row_form(table, 1, r.dense, 0, count)
        return n_all, inverse

    def sums_near(self, at):
        if not self.one_stage(at):
            self.near_wait(at, self.r.near_r)
            self.r.wide[at][self.high] = total(self.r.near[at])
            self.wide_send(at)

    def sums_wide(self, at):
        if self.one_stage(at):
            self.near_wait(at, self.r.near_r)
            return total(self.r.near[at])
        self.wide_wait(at, self.r.wide_r)
        return total(self.r.wide[at])

    def local_stats(self, buf, at, ref):
        channels = ref.shape[1]
        count = channels // 128
        for c in range(channels // 256):
            lanes = slice(c * 256, (c + 1) * 256)

            def gather(term):
                acc = jnp.zeros((SIDE, 256), F32)
                for k in range(self.live):
                    part = lax.fori_loop(
                        0, self.height, lambda y, a: a + term(ref[pl.ds(block(k, y), SIDE), lanes]),
                        jnp.zeros((SIDE, 256), F32), unroll=self.height,
                    )
                    acc = acc + part * self.v[k]
                return self.fold(acc)

            s_own = gather(lambda x: x)
            mean = s_own / jnp.maximum(self.n_own, 1.0)
            to_dense(buf, at, s_own, 2 * c)
            to_dense(buf, at, gather(lambda x: (x - mean) * (x - mean)), count + 2 * c)

    def norm_silu(self, ref, slope_ref, table, gain, bias, write):
        centre, scale = table[0:1, :], table[1:2, :] * gain[...].reshape(1, self.mid)
        b = bias[...].reshape(1, self.mid)
        for k in range(self.live):
            def step(y, carry):
                at = block(k, y)
                u = (ref[pl.ds(at, SIDE), :] - centre) * scale + b
                s = 0.5 * jnp.tanh(0.5 * u) + 0.5
                h = u * s
                slope_ref[pl.ds(at, SIDE), :] = jnp.where(self.mask, s + (h - h * s), 0.0)
                write(at, jnp.where(self.mask, h, 0.0))
                return carry

            lax.fori_loop(0, self.height, step, 0, unroll=7)


def flips(index, count, stride=1):
    steps, at = [], 1
    while at < count:
        steps.append(at * stride * (1 - 2 * ((index // (at * stride)) % 2)))
        at *= 2
    return [sum((d for b, d in enumerate(steps) if o >> b & 1), index) for o in reversed(range(1, count))]


def combine(buf, counts, group, count):
    n_part = [counts(q) for q in range(group)]
    s_part = [buf[q, 0:count, :] for q in range(group)]
    n_all = sum(n_part[1:], n_part[0])
    s_all = sum(s_part[1:], s_part[0])
    mean = s_all / jnp.maximum(n_all, 1.0)
    spread = jnp.zeros((count, 128), F32)
    for q in range(group):
        gap = s_part[q] / jnp.maximum(n_part[q], 1.0) - mean
        spread = spread + (buf[q, count : 2 * count, :] + n_part[q] * gap * gap)
    return n_all, s_all, mean, spread


def total(buf):
    out = buf[0]
    for q in range(1, buf.shape[0]):
        out = out + buf[q]
    return out


def clear(*refs):
    for ref in refs:
        ref[...] = jnp.zeros(ref.shape, ref.dtype)


def prologue(t):
    r, slots, live, width, feat = t.r, t.slots, t.live, t.width, t.feat
    t.places()
    t.greet()
    t.load(
        frames=(r.frames, r.f4.at[pl.ds(0, t.area)]), valid=(r.slot_valid, r.valid), reduce=(r.w_reduce, r.wr),
        clip=(r.clip_ids, r.clip), segment=(r.segment_ids, r.segment),
        share=(r.segment_weight, r.share), spatial=(r.w_spatial, r.ws), expand=(r.w_expand, r.we),
        ga=(r.gain_a, r.ga), ba=(r.bias_a, r.ba), gb=(r.gain_b, r.gb), bb=(r.bias_b, r.bb),
        gc=(r.gain_c, r.gc), bc=(r.bias_c, r.bc), loss=(r.loss_weight, r.loss),
    )
    for i in range(3):
        for j in range(3):
            pltpu.make_async_copy(
                r.w_spatial.at[i, j], r.wc.at[i, :, pl.ds(j * t.mid, t.mid)], r.load_sem.at[15]
            ).start()
    r.f4[t.area :] = jnp.zeros((r.f4.shape[0] - t.area, *r.f4.shape[1:]), BF16)
    clear(r.fp)
    t.loaded(valid=0)
    t.slot_facts()
    t.loaded(frames=0)
    fp, f4 = r.fp, r.f4
    tiles = feat // 128
    group = SIDE // slots
    short = lax.broadcasted_iota(jnp.int32, (SIDE, 128), 0) < width

    def regroup(y, carry):
        for p in range(tiles // group):
            value = f4[pl.ds(y * width, SIDE), p * SIDE : (p + 1) * SIDE, :].astype(F32)
            value = jnp.swapaxes(value, 0, 1)
            for q in range(group):
                for k in range(live):
                    row = value[q * slots + k] * t.keep[k] + value[q * slots + k + 1] * t.moved[k]
                    lanes = slice((p * group + q) * 128, (p * group + q + 1) * 128)
                    fp[pl.ds(block(k, y), SIDE), lanes] = jnp.where(short, row, 0.0).astype(BF16)
        return carry

    lax.fori_loop(0, t.height, regroup, 0)
    t.loaded(reduce=0)
    by_rows(r.pre_a, lambda here: dot(fp[here, :], r.wr[...]))
    t.local_stats(r.near[0], t.near_at(0), r.pre_a)
    r.near[0][t.near_at(0), 4:5, :] = jnp.full((1, 128), t.n_own, F32)


def forward(t):
    r, live, mid, feat, rows, area, height = t.r, t.live, t.mid, t.feat, t.rows, t.area, t.height
    t.all_here()
    t.near_send(0)
    r.ft[...] = r.fp[...].T
    t.stats_near(0, mid // 128)
    clear(r.xp, r.hb, r.g3, r.gpc, r.gpa)
    t.loaded(clip=0, segment=0, share=0, ga=0, ba=0, gb=0, bb=0, gc=0, bc=0, loss=0, spatial=0, expand=0)
    key = [t.kept(r.clip, k) for k in range(live)]
    weight = []
    for k in range(live):
        at = t.kept(r.segment, k)
        w0, w1, w2 = (r.share[q] for q in range(3))
        weight.append(
            t.v[k] * (w0 * ((1.0 - at) * (2.0 - at) * 0.5) + w1 * (at * (2.0 - at)) + w2 * (at * (at - 1.0) * 0.5))
        )
    n_all, inv_a = t.stats_wide(0, mid // 128, r.table_a)

    xp, hb = r.xp, r.hb

    def write_a(at, h):
        three(xp, at, pltpu.roll(h, 1, 0), h, pltpu.roll(h, SIDE - 1, 0))

    t.norm_silu(r.pre_a, r.slope_a, r.table_a, r.ga, r.ba, write_a)

    by_rows(
        r.pre_b,
        lambda here: sum(dot(xp[moved_rows(here, i * SIDE), :], r.ws[i].reshape(3 * mid, mid)) for i in range(3)),
    )
    t.local_stats(r.near[1], t.near_at(1), r.pre_b)
    t.near_send(1)
    r.xt[...] = xp[SIDE : SIDE + rows, mid : 2 * mid].T
    t.stats_near(1, mid // 128)
    _, inv_b = t.stats_wide(1, mid // 128, r.table_b)

    def write_b(at, h):
        hb[pl.ds(at, SIDE), :] = h.astype(BF16)

    t.norm_silu(r.pre_b, r.slope_b, r.table_b, r.gb, r.bb, write_b)

    pre_c, slope_c, fp, table_c = r.pre_c, r.slope_c, r.fp, r.table_c
    by_rows(pre_c, lambda here: dot(hb[here, :], r.we[...]))
    t.local_stats(r.near[2], t.near_at(2), pre_c)
    t.near_send(2)
    r.hbt[...] = hb[...].T
    t.stats_near(2, feat // 128)
    _, inv_c = t.stats_wide(2, feat // 128, table_c)

    pool, slope_sum, slope_hat = r.pool, r.slope_sum, r.slope_hat
    for c in range(feat // 256):
        lanes = slice(c * 256, (c + 1) * 256)
        centre, inverse = table_c[0:1, lanes], table_c[1:2, lanes]
        g = r.gc[lanes].reshape(1, 256)
        b = r.bc[lanes].reshape(1, 256)
        for k in range(live):
            def step(y, carry):
                a0, a1, a2 = carry
                at = block(k, y)
                hat = (pre_c[pl.ds(at, SIDE), lanes] - centre) * inverse
                u = hat * g + b + fp[pl.ds(at, SIDE), lanes].astype(F32)
                s = 0.5 * jnp.tanh(0.5 * u) + 0.5
                h = u * s
                slope = s + (h - h * s)
                slope_c[pl.ds(at, SIDE), lanes] = slope
                return a0 + h, a1 + slope, a2 + slope * hat

            zero = jnp.zeros((SIDE, 256), F32)
            a0, a1, a2 = lax.fori_loop(0, height, step, (zero, zero, zero), unroll=7)
            p_row = (t.fold(a0) * (1.0 / area)).astype(BF16).astype(F32)
            to_dense(pool, 0, p_row, 8 * k + 2 * c)
            to_dense(slope_sum, k, t.fold(a1), 2 * c)
            to_dense(slope_hat, k, t.fold(a2), 2 * c)
    for k in range(live):
        pool[0, 24 + k : 25 + k, :] = jnp.full((1, 128), key[k], F32)
        pool[0, 28 + k : 29 + k, :] = jnp.full((1, 128), weight[k], F32)
    for q, device in enumerate(t.clip_peers):
        t.send(pool.at[0], pool.at[q + 1], r.pool_s.at[0], r.pool_r.at[0], device)
    wait_bytes(pool.at[pl.ds(1, len(t.clip_peers))], r.pool_r.at[0])

    lw = dense_of(r.loss, r.dense)
    grads = []
    for k in range(live):
        my_key = jnp.full((1, 128), key[k], F32)
        my_weight = jnp.full((1, 128), weight[k], F32)
        mean = jnp.zeros((8, 128), F32)
        den = jnp.zeros((1, 128), F32)
        for q in range(len(t.clip_peers) + 1):
            for m in range(live):
                match = jnp.where(pool[q, 24 + m : 25 + m, :] == my_key, pool[q, 28 + m : 29 + m, :], 0.0)
                den = den + match
                mean = mean + match * pool[q, 8 * m : 8 * m + 8, :]
        den = jnp.where(den == 0.0, 1.0, den)
        mean = mean / den
        power = jnp.sum(jnp.sum(mean * mean, axis=0, keepdims=True), axis=1, keepdims=True)
        scale = lax.rsqrt(power * (1.0 / feat) + EPS)
        unit = mean * scale
        along = jnp.sum(jnp.sum(unit * lw, axis=0, keepdims=True), axis=1, keepdims=True)
        mean_grad = scale * (lw - unit * (along * (1.0 / feat)))
        grads.append((my_weight / den) * mean_grad * (1.0 / area))

    near3 = r.near[3]
    shift = jnp.zeros((8, 128), F32)
    gain = jnp.zeros((8, 128), F32)
    for k in range(live):
        shift = shift + grads[k] * slope_sum[k]
        gain = gain + grads[k] * slope_hat[k]
    near3[t.near_at(3), 0:8, :] = shift
    near3[t.near_at(3), 8:16, :] = gain
    t.near_send(3)
    coef, dense = r.coef, r.dense
    scale_c = dense_of(r.gc, dense) * inv_c
    for k in range(live):
        dense[...] = grads[k]
        row_form(coef, k, dense, 0, feat // 128)
        dense[...] = grads[k] * scale_c
        row_form(coef, 3 + k, dense, 0, feat // 128)
    t.sums_near(3)
    both = t.sums_wide(3)
    r.vectors_c[...] = both
    dense[...] = both[0:8] * scale_c / n_all
    row_form(coef, 6, dense, 0, feat // 128)
    dense[...] = both[8:16] * scale_c * inv_c / n_all
    row_form(coef, 7, dense, 0, feat // 128)
    return n_all, inv_a, inv_b


def backward(t, n_all, inv_a, inv_b):
    r, live, mid, feat, rows, height = t.r, t.live, t.mid, t.feat, t.rows, t.height
    slots, width, quad, far, v, wc = t.slots, t.width, t.quad, t.far, t.v, r.wc
    coef, pre_c, slope_c, out = r.coef, r.pre_c, r.slope_c, r.vectors
    me, send = t.me, t.send
    gpc = r.gpc
    for k in range(live):
        for c in range(feat // 256):
            lanes = slice(c * 256, (c + 1) * 256)
            centre = r.table_c[0:1, lanes]
            c0 = coef[3 + k : 4 + k, lanes]
            c1 = coef[6:7, lanes] * v[k]
            c2 = coef[7:8, lanes] * v[k]

            def step(y, carry):
                at = block(k, y)
                grad = slope_c[pl.ds(at, SIDE), lanes] * c0 - (c1 + (pre_c[pl.ds(at, SIDE), lanes] - centre) * c2)
                gpc[pl.ds(at, SIDE), lanes] = grad.astype(BF16)
                return carry

            lax.fori_loop(0, height, step, 0, unroll=7)

    def back_sums(at, table, inv, grad_ref, slope_ref, pre_ref):
        zero = jnp.zeros((SIDE, mid), F32)
        carry = (zero, zero)
        centre = table[0:1, :]
        for k in range(live):
            def step(y, c):
                here = pl.ds(block(k, y), SIDE)
                grad = grad_ref[here, :] * slope_ref[here, :]
                grad_ref[here, :] = grad
                return c[0] + grad, c[1] + grad * (pre_ref[here, :] - centre)

            carry = lax.fori_loop(0, height, step, carry, unroll=7)
        buf = r.near[at]
        to_dense(buf, t.near_at(at), jnp.sum(carry[0], axis=0, keepdims=True), 0)
        to_dense(buf, t.near_at(at), jnp.sum(carry[1], axis=0, keepdims=True) * table[1:2, :], 2)

    def back_apply(at, table, gain_ref, inv, grad_ref, pre_ref, write):
        both = t.sums_wide(at)
        out[8 * at - 32 : 8 * at - 28, :] = both[0:4]
        dense = r.dense
        scale = dense_of(gain_ref, dense) * inv
        dense[0:2, :] = scale
        dense[2:4, :] = both[0:2] * scale / n_all
        dense[4:6, :] = both[2:4] * scale * inv / n_all
        for q in range(3):
            row_form(table, 2 + q, dense, 2 * q, 2)
        centre = table[0:1, :]
        for k in range(live):
            c0, c1, c2 = table[2:3, :], table[3:4, :] * v[k], table[4:5, :] * v[k]

            def step(y, carry):
                at_row = block(k, y)
                here = pl.ds(at_row, SIDE)
                write(at_row, grad_ref[here, :] * c0 - (c1 + (pre_ref[here, :] - centre) * c2))
                return carry

            lax.fori_loop(0, height, step, 0, unroll=7)

    core, bit_x, bit_y, at_z = me % 2, (me // 2) % 2, (me // 4) % 2, (me // 8) % quad
    at_far = me // (8 * quad)
    bit1 = bit_x + core * (bit_y - bit_x)
    bit2 = bit_y + core * (bit_x - bit_y)
    sibling = me + 1 - 2 * core
    peer1 = me + (1 - 2 * bit1) * (2 + 2 * core)
    peer2 = me + (1 - 2 * bit2) * (4 - 2 * core)
    z_at = flips(at_z, quad)
    z_peer = [me + 8 * (q - at_z) for q in z_at]
    far_peer = [me + 8 * quad * ((at_far + o) % far - at_far) for o in range(1, far)]
    chunk_s, chunk_r = r.chunk_s, r.chunk_r
    waits, blocks = [], iter(ORDER)
    plan = [(0, q, 2) for q in range(2)] + [(1 + q // 2, q % 2, 2) for q in range(6)] + [(4, q, 4) for q in range(4)]

    def chunk(q):
        name, at, count = plan[q]
        size = r.part[name].shape[0] // count
        part = r.part[name].at[pl.ds(at * size, size)]
        whole = (r.e, r.s0, r.s1, r.s2, r.r)[name].at[pl.ds(at * size, size)]
        half, quarter, eighth, piece = size // 2, size // 4, size // 8, size // (8 * quad)
        m8 = lambda value: pl.multiple_of(value, 8)
        at_h = m8(core * half)
        at_q = m8(at_h + bit1 * quarter)
        at_e = m8(at_q + bit2 * eighth)
        at_p = m8(at_e + at_z * piece)

        def go(step, src, dst, device):
            send(src, dst, chunk_s.at[q, step], chunk_r.at[q, step], device)

        def finish(step, ref):
            wait_bytes(ref, chunk_r.at[q, step])
            waits.append((ref, chunk_s.at[q, step]))

        rb0, rb1, rb2, rb3 = r.rb0[q], r.rb1[q], r.rb2[q], r.rb3[q]
        go(0, part.at[pl.ds(m8((1 - core) * half), half)], rb0, sibling)
        yield
        finish(0, rb0)
        part[pl.ds(at_h, half), :] = part[pl.ds(at_h, half), :] + rb0[...]
        go(1, part.at[pl.ds(m8(at_h + (1 - bit1) * quarter), quarter)], rb1, peer1)
        yield
        finish(1, rb1)
        part[pl.ds(at_q, quarter), :] = part[pl.ds(at_q, quarter), :] + rb1[...]
        go(2, part.at[pl.ds(m8(at_q + (1 - bit2) * eighth), eighth)], rb2, peer2)
        yield
        finish(2, rb2)
        part[pl.ds(at_e, eighth), :] = part[pl.ds(at_e, eighth), :] + rb2[...]
        for o in range(quad - 1):
            go(3, part.at[pl.ds(m8(at_e + z_at[o] * piece), piece)], rb3.at[pl.ds(o * piece, piece)], z_peer[o])
        yield
        finish(3, rb3)
        own = part[pl.ds(at_p, piece), :]
        for o in range(quad - 1):
            own = own + rb3[o * piece : (o + 1) * piece, :]
        if far > 1:
            rb4 = r.rb4[q]
            rb4[at_far] = own
            for device in far_peer:
                go(8, rb4.at[at_far], rb4.at[at_far], device)
            yield
            finish(8, rb4.at[pl.ds(0, far - 1)])
            own = rb4[0]
            for o in range(1, far):
                own = own + rb4[o]
        whole[pl.ds(at_p, piece), :] = own
        for o in range(quad - 1):
            go(4, whole.at[pl.ds(at_p, piece)], whole.at[pl.ds(at_p, piece)], z_peer[o])
        yield
        finish(4, whole.at[pl.ds(0, (quad - 1) * piece)])
        go(5, whole.at[pl.ds(at_e, eighth)], whole.at[pl.ds(at_e, eighth)], peer2)
        yield
        finish(5, whole.at[pl.ds(0, eighth)])
        go(6, whole.at[pl.ds(at_q, quarter)], whole.at[pl.ds(at_q, quarter)], peer1)
        yield
        finish(6, whole.at[pl.ds(0, quarter)])
        go(7, whole.at[pl.ds(at_h, half)], whole.at[pl.ds(at_h, half)], sibling)
        yield
        finish(7, whole.at[pl.ds(0, half)])
        yield

    chunks = [chunk(q) for q in range(len(plan))]

    def go_on(*which):
        for q in which:
            next(chunks[q])

    def go_on_all():
        go_on(*next(blocks))

    pre_a, slope_a, pre_b, slope_b, hbt, xt = r.pre_a, r.slope_a, r.pre_b, r.slope_b, r.hbt, r.xt
    we, wr, back = r.we, r.wr, r.back
    tiles = feat // 128
    group = SIDE // slots
    keep, moved, mask = t.keep, t.moved, t.mask
    grad_b, grad_a = r.grad_b, r.grad_a
    wait_bytes(wc, r.load_sem.at[15])
    g3 = r.g3

    def write_gb(at, grad):
        grad = jnp.where(mask, grad, 0.0)
        three(g3, at, pltpu.roll(grad, SIDE - 1, 0), grad, pltpu.roll(grad, 1, 0))

    def expand_part(e):
        go_on_all()
        for q in range(2):
            first = (2 * e + q) * 256
            spread_lanes(r.part[0].at[pl.ds(2 * first, 512)], dot(hbt[...], gpc[:, first : first + 256]))
        go_on(e)

    def spatial_part(i):
        go_on_all()
        spread_lanes(r.part[1 + i], dot(xt[...], g3[(2 - i) * SIDE : (2 - i) * SIDE + rows, :]))
        go_on(2 + 2 * i, 3 + 2 * i)

    go_on_all()
    expand_part(0)
    go_on_all()
    by_rows(grad_b, lambda here: dot(gpc[here, :], we[...], NT))
    back_sums(4, r.table_b, inv_b, grad_b, slope_b, pre_b)
    t.near_send(4)
    expand_part(1)
    go_on_all()
    back_apply(4, r.table_b, r.gb, inv_b, grad_b, pre_b, write_gb)
    spatial_part(0)
    go_on_all()
    by_rows(
        grad_a, lambda here: sum(dot(g3[moved_rows(here, (2 - i) * SIDE), :], wc[i], NT) for i in range(3))
    )
    back_sums(5, r.table_a, inv_a, grad_a, slope_a, pre_a)
    t.near_send(5)
    spatial_part(1)
    spatial_part(2)
    go_on_all()
    gpa = r.gpa

    def write_ga(at, grad):
        gpa[pl.ds(at, SIDE), :] = grad.astype(BF16)

    back_apply(5, r.table_a, r.ga, inv_a, grad_a, pre_a, write_ga)
    for q in range(4):
        go_on_all()
        spread_lanes(r.part[4].at[pl.ds(q * 512, 512)], dot(r.ft[q * 256 : (q + 1) * 256, :], gpa[...]))
        go_on(8 + q)

    go_on_all()
    by_rows(back, lambda here: dot(gpa[here, :], wr[...], NT))
    gf = r.gf

    def blend(y, carry):
        for p in range(tiles // group):
            values = []
            for q in range(group):
                lanes = slice((p * group + q) * 128, (p * group + q + 1) * 128)
                terms = [
                    slope_c[pl.ds(block(k, y), SIDE), lanes] * coef[k : k + 1, lanes]
                    + back[pl.ds(block(k, y), SIDE), lanes]
                    for k in range(live)
                ]
                values.append(terms[0] * keep[0])
                for m in range(1, live):
                    values.append(terms[m] * keep[m] + terms[m - 1] * moved[m - 1])
                values.append(terms[live - 1] * moved[live - 1])
            value = jnp.swapaxes(jnp.stack(values), 0, 1)
            gf[pl.ds(y * width, width), p * SIDE : (p + 1) * SIDE, :] = value[0:width].astype(BF16)
        return carry

    for q in range(height // 2):
        go_on_all()
        for y in range(2):
            blend(2 * q + y, 0)
    go_on_all()
    for each in chunks:
        for _ in each:
            pass

    t.all_sent(*range(6))
    wait_bytes(r.pool.at[pl.ds(1, len(t.clip_peers))], r.pool_s.at[0])
    for ref, sem in waits:
        wait_bytes(ref, sem)


def store(gf, vectors_c, vectors, expand, s0, s1, s2, reduce, frames_out, reduce_out, spatial_out, expand_out, *rest):
    ga, ba, gb, bb, gc, bc, *scratch, sem = rest
    vectors_of = (
        (bc, vectors_c, 0), (gc, vectors_c, 8), (bb, vectors, 0), (gb, vectors, 2), (ba, vectors, 8), (ga, vectors, 10)
    )
    pltpu.make_async_copy(gf, frames_out, sem.at[0]).start()
    for number, (ref, source, first) in enumerate(vectors_of):
        for q in range(ref.shape[0] // 128):
            scratch[number][q * 128 : (q + 1) * 128] = source[first + q : first + q + 1, :].reshape(128)
        pltpu.make_async_copy(scratch[number], ref, sem.at[6 + number]).start()
    depth, width = reduce_out.shape
    for q in range(depth // 256):
        for m in range(width // 128):
            pltpu.make_async_copy(
                reduce.at[pl.ds((q * width // 128 + m) * 256, 256)],
                reduce_out.at[pl.ds(q * 256, 256), pl.ds(m * 128, 128)],
                sem.at[1],
            ).start()
    depth, width = expand_out.shape
    for q in range(width // 128):
        pltpu.make_async_copy(
            expand.at[pl.ds(q * depth, depth)], expand_out.at[:, pl.ds(q * 128, 128)], sem.at[2]
        ).start()
    for i, part in enumerate((s0, s1, s2)):
        for q in range(part.shape[0] // depth):
            pltpu.make_async_copy(
                part.at[pl.ds(q * depth, depth)],
                spatial_out.at[i, q * 128 // depth, :, pl.ds(q * 128 % depth, 128)],
                sem.at[3 + i],
            ).start()
    wait_bytes(gf, sem.at[0])
    wait_bytes(reduce, sem.at[1])
    wait_bytes(expand, sem.at[2])
    for i, part in enumerate((s0, s1, s2)):
        wait_bytes(part, sem.at[3 + i])
    for number in range(6):
        wait_bytes(scratch[number], sem.at[6 + number])


def solution(mesh):
    n = mesh.shape["clip"]

    def shards(*args):
        slots, height, width, feat = args[0].shape
        mid = args[1].shape[1]
        rows = (slots - 1) * ROWS
        outer = n // 8
        quad = min(4, outer)
        far = outer // quad
        cfg = (n, slots, height, width, feat, mid)
        flat_shape = (height * width, slots * feat // 128, 128)
        hbm = pl.BlockSpec(memory_space=pltpu.HBM)
        vmem = pl.BlockSpec(memory_space=pltpu.VMEM)
        dma = pltpu.SemaphoreType.DMA
        depths = list(enumerate((8, 4, 16, 16, 4, 4)))
        matrix, third = mid * feat // 128, 3 * mid * mid // 128
        sizes = [matrix, third, third, third, matrix]

        tiled = args[0].transpose(1, 2, 0, 3).reshape(height, width, slots, feat // 128, 128)
        tiled = tiled.transpose(0, 1, 3, 2, 4).reshape(flat_shape)
        given = [pltpu.with_memory_space_constraint(part, pltpu.HBM) for part in (tiled, *args[1:])]

        vm = pltpu.VMEM
        narrow, broad, square = vm((mid,), F32), vm((feat,), F32), vm((rows, mid), F32)
        ints = pltpu.SMEM((slots,), jnp.int32)
        plan = [matrix // 2] * 2 + [third // 2] * 6 + [matrix // 4] * 4
        outs = dict(
            gf=vm(flat_shape, BF16), vectors_c=vm((16, 128), F32), vectors=vm((16, 128), F32),
            e=vm((matrix, 128), F32), s0=vm((third, 128), F32), s1=vm((third, 128), F32), s2=vm((third, 128), F32),
            r=vm((matrix, 128), F32),
        )
        scratch = dict(
            f4=vm((flat_shape[0] + SIDE - width, *flat_shape[1:]), BF16),
            fp=vm((rows, feat), BF16), ft=vm((feat, rows), BF16),
            wr=vm((feat, mid), BF16), ws=vm((3, 3, mid, mid), BF16), wc=vm((3, mid, 3 * mid), BF16), we=vm((mid, feat), BF16),
            valid=ints, clip=ints, segment=ints, share=pltpu.SMEM(args[13].shape, F32),
            ga=narrow, ba=narrow, gb=narrow, bb=narrow, gc=broad, bc=broad, loss=broad,
            xp=vm((rows + 2 * SIDE, 3 * mid), BF16), xt=vm((mid, rows), BF16),
            hb=vm((rows, mid), BF16), hbt=vm((mid, rows), BF16),
            pre_a=square, slope_a=square, pre_b=square, slope_b=square, grad_a=square, grad_b=square,
            pre_c=vm((rows, feat), F32), slope_c=vm((rows, feat), F32), back=vm((rows, feat), F32),
            gpc=vm((rows, feat), BF16), g3=vm((rows + 2 * SIDE, 3 * mid), BF16), gpa=vm((rows, mid), BF16),
            table_a=vm((8, mid), F32), table_b=vm((8, mid), F32),
            table_c=vm((8, feat), F32), coef=vm((8, feat), F32), dense=vm((8, 128), F32),
            pool=vm((6, 32, 128), F32), slope_sum=vm((3, 8, 128), F32), slope_hat=vm((3, 8, 128), F32),
            near=[vm((n if n <= 32 and at not in (2, 3) else 8, deep, 128), F32) for at, deep in depths],
            wide=[vm((outer, deep, 128), F32) for at, deep in depths],
            plane=vm((outer, 8, 128), F32),
            part=[vm((size, 128), F32) for size in sizes],
            rb0=[vm((size // 2, 128), F32) for size in plan],
            rb1=[vm((size // 4, 128), F32) for size in plan],
            rb2=[vm((size // 8, 128), F32) for size in plan],
            rb3=[vm(((quad - 1) * size // (8 * quad), 128), F32) for size in plan],
            rb4=[vm((far, size // (8 * quad), 128), F32) for size in plan if far > 1],
            load_sem=dma((16,)), near_s=dma((6,)), near_r=dma((6,)), wide_s=dma((6,)), wide_r=dma((6,)),
            pool_s=dma((1,)), pool_r=dma((1,)), chunk_s=dma((12, 9)), chunk_r=dma((12, 9)),
        )
        names = (*arg_names(), *outs, *scratch)

        def kernel(*refs):
            t = Step(cfg, SimpleNamespace(**dict(zip(names, refs, strict=True))))
            prologue(t)
            backward(t, *forward(t))

        results = pl.pallas_call(
            kernel,
            out_shape=list(outs.values()),
            in_specs=[hbm] * len(given),
            out_specs=[vmem] * len(outs),
            scratch_shapes=list(scratch.values()),
            compiler_params=pltpu.CompilerParams(
                collective_id=0, has_side_effects=True, vmem_limit_bytes=50 * 1024 * 1024
            ),
        )(*given)
        vector = jax.ShapeDtypeStruct((mid,), F32)
        wide_vector = jax.ShapeDtypeStruct((feat,), F32)
        flat_grad, *rest = pl.pallas_call(
            store,
            out_shape=[
                jax.ShapeDtypeStruct(flat_shape, BF16),
                jax.ShapeDtypeStruct((feat, mid), F32),
                jax.ShapeDtypeStruct((3, 3, mid, mid), F32),
                jax.ShapeDtypeStruct((mid, feat), F32),
                vector, vector, vector, vector, wide_vector, wide_vector,
            ],
            in_specs=[vmem] * 8,
            out_specs=[hbm] * 10,
            scratch_shapes=[*(vm((c,), F32) for c in (feat, feat, mid, mid, mid, mid)), dma((12,))],
            compiler_params=pltpu.CompilerParams(vmem_limit_bytes=8 * 1024 * 1024),
        )(*(pltpu.with_memory_space_constraint(part, pltpu.VMEM) for part in results))
        grad_frames = flat_grad.reshape(height, width, feat // 128, slots, 128).transpose(0, 1, 3, 2, 4)
        return grad_frames.reshape(height, width, slots, feat).transpose(2, 0, 1, 3), *rest

    split = P("clip")
    in_specs = (split,) + (P(),) * 9 + (split,) * 3 + (P(), P())
    out_specs = (split,) + (P(),) * 9
    return jax.shard_map(shards, mesh=mesh, in_specs=in_specs, out_specs=out_specs, check_vma=False)


def arg_names():
    return dict(
        frames=0, w_reduce=0, w_spatial=0, w_expand=0, gain_a=0, bias_a=0, gain_b=0, bias_b=0, gain_c=0, bias_c=0,
        clip_ids=0, segment_ids=0, slot_valid=0, segment_weight=0, loss_weight=0,
    )
```

```python
import functools
from types import SimpleNamespace

import jax
import jax.numpy as jnp
from jax import lax
from jax.experimental import pallas as pl
from jax.experimental.pallas import tpu as pltpu
from jax.sharding import PartitionSpec as P

MESH = pl.DeviceIdType.MESH
EPS = 1e-05
F32 = jnp.float32
BF16 = jnp.bfloat16
SIDE = 16
ROWS = SIDE * SIDE
NN = (((1,), (0,)), ((), ()))
NT = (((1,), (1,)), ((), ()))

ORDER = (
    (),
    (),
    (),
    (0,),
    (),
    (),
    (1, 0),
    (2, 3, 1, 0),
    (),
    (2, 3, 0, 4, 1, 5),
    (6, 7, 2, 3, 0, 4),
    (),
    (5, 1),
    (6, 2, 8, 7, 9, 3, 0),
    (4, 10, 5, 1, 6, 8, 2, 7, 11, 3, 9),
    (4, 0, 5, 10, 1, 6, 8, 2),
    (7, 11, 0, 3, 4, 9, 10, 5),
    (),
    (1, 6),
    (8, 2, 11, 7),
    (3, 9, 1, 4, 10, 5, 2, 6, 8),
    (7, 11, 3),
    (9, 4, 10, 5, 11, 6, 4, 8, 5, 7, 9, 10, 6, 11, 8, 7, 9, 10, 8, 11, 9, 10, 11),
)


def dot(a, b, dims=NN):
    return lax.dot_general(a, b, dims, preferred_element_type=F32)


def wait_bytes(ref, sem):
    pltpu.make_async_copy(ref, ref, sem).wait()


def spread_lanes(ref, value):
    depth = value.shape[0]
    for q in range(value.shape[1] // 128):
        ref[q * depth : (q + 1) * depth, :] = value[:, q * 128 : (q + 1) * 128]


def by_rows(ref, value):
    def step(k, carry):
        here = pl.ds(pl.multiple_of(k * 256, 256), 256)
        ref[here, :] = value(here)
        return carry

    lax.fori_loop(0, ref.shape[0] // 256, step, 0)


def moved_rows(here, at):
    return pl.ds(pl.multiple_of(here.start + at, SIDE), 256)


def block(k, y):
    return pl.multiple_of(k * ROWS + y * SIDE, SIDE)


def to_dense(ref, at, value, first):
    for q in range(value.shape[1] // 128):
        ref[at, pl.ds(first + q, 1), :] = value[:, q * 128 : (q + 1) * 128]


def row_form(ref, row, source, first, count):
    for q in range(count):
        ref[row : row + 1, q * 128 : (q + 1) * 128] = source[first + q : first + q + 1, :]


def three(ref, at, left, middle, right):
    here, wide = pl.ds(at + SIDE, SIDE), middle.shape[1]
    ref[here, 0:wide] = left.astype(BF16)
    ref[here, wide : 2 * wide] = middle.astype(BF16)
    ref[here, 2 * wide : 3 * wide] = right.astype(BF16)


def dense_of(ref1, scratch):
    count = ref1.shape[0] // 128
    for q in range(count):
        scratch[q : q + 1, :] = ref1[q * 128 : (q + 1) * 128].reshape(1, 128)
    return scratch[0:count, :]


class Step:
    def __init__(self, cfg, r):
        self.r, self.sizes = r, cfg
        self.n, self.slots, self.height, self.width, self.feat, self.mid = cfg
        self.live = self.slots - 1
        self.rows = self.live * ROWS
        self.area = self.height * self.width
        self.inner = 8
        self.outer = self.n // 8
        self.quad = min(4, self.outer)
        self.far = self.outer // self.quad
        self.loads = {}
        self.mask = lax.broadcasted_iota(jnp.int32, (SIDE, 256), 0) < self.width

    def load(self, **pairs):
        for name, (src, dst) in pairs.items():
            copy = pltpu.make_async_copy(src, dst, self.r.load_sem.at[len(self.loads)])
            copy.start()
            self.loads[name] = copy

    def loaded(self, **names):
        for name in names:
            self.loads[name].wait()

    def fold(self, value):
        return jnp.sum(jnp.where(self.mask, value, 0.0), axis=0, keepdims=True)

    def slot_facts(self):
        r, live = self.r, self.live
        alive, later = 1, []
        for k in range(live):
            alive = alive * r.valid[k]
            later.append(1 - alive)
        self.keep = [(1 - q).astype(F32) for q in later]
        self.moved = [q.astype(F32) for q in later]
        self.later = later
        self.v = [self.kept(r.valid, k) for k in range(live)]
        self.n_own = (self.v[0] + self.v[1] + self.v[2]) * float(self.area)

    def kept(self, values, k):
        return (values[k] + self.later[k] * (values[k + 1] - values[k])).astype(F32)

    def places(self):
        n = self.n
        self.me = me = lax.axis_index("clip")
        self.low, self.high = low, high = me % self.inner, me // self.inner
        self.direct = n <= 8
        self.peers = flips(me, n)
        self.low_peers = flips(me, self.inner)
        self.high_peers = flips(me, self.outer, self.inner)
        self.clip_peers = [(me + o) % n for o in (n // 2 - 1, n // 2 + 1, n // 2, n - 1, 1)]

    def greet(self):
        self.greeted = self.peers if self.direct else self.low_peers + self.high_peers + self.clip_peers
        self.barrier = pltpu.get_barrier_semaphore()
        for device in self.greeted:
            pl.semaphore_signal(self.barrier, inc=1, device_id=(device,), device_id_type=MESH)

    def all_here(self):
        pl.semaphore_wait(self.barrier, len(self.greeted))

    def send(self, src, dst, ssem, rsem, device):
        pltpu.make_async_remote_copy(
            src_ref=src, dst_ref=dst, send_sem=ssem, recv_sem=rsem, device_id=(device,), device_id_type=MESH
        ).start()

    def one_stage(self, at):
        return self.direct and at not in (2, 3)

    def near_at(self, at):
        return self.me if self.one_stage(at) else self.low

    def near_send(self, at):
        buf, mine = self.r.near[at], self.near_at(at)
        for device in self.peers if self.one_stage(at) else self.low_peers:
            self.send(buf.at[mine], buf.at[mine], self.r.near_s.at[at], self.r.near_r.at[at], device)

    def near_wait(self, at, sems):
        buf = self.r.near[at]
        wait_bytes(buf.at[pl.ds(0, buf.shape[0] - 1)], sems.at[at])

    def wide_send(self, at):
        buf = self.r.wide[at]
        for device in self.high_peers:
            self.send(buf.at[self.high], buf.at[self.high], self.r.wide_s.at[at], self.r.wide_r.at[at], device)

    def wide_wait(self, at, sems):
        wait_bytes(self.r.wide[at].at[pl.ds(0, self.outer - 1)], sems.at[at])

    def all_sent(self, *rounds):
        for at in rounds:
            self.near_wait(at, self.r.near_s)
            if not self.one_stage(at):
                self.wide_wait(at, self.r.wide_s)

    def near_count(self, q):
        return self.r.near[0][(self.me - self.low + q) if self.direct else q, 4:5, :]

    def wide_count(self, q):
        return self.r.plane[q, 0:1, :] if self.direct else self.r.wide[0][q, 4:5, :]

    def stats_near(self, at, count):
        if self.one_stage(at):
            return
        self.near_wait(at, self.r.near_r)
        n_all, s_all, _, spread = combine(self.r.near[at], self.near_count, self.inner, count)
        buf = self.r.wide[at]
        buf[self.high, 0:count, :] = s_all
        buf[self.high, count : 2 * count, :] = spread
        if at == 0:
            buf[self.high, 4:5, :] = n_all
        self.wide_send(at)

    def stats_wide(self, at, count, table):
        r = self.r
        if self.one_stage(at):
            self.near_wait(at, r.near_r)
            counts = r.near[0]
            n_all, _, mean, spread = combine(r.near[at], lambda q: counts[q, 4:5, :], self.n, count)
            if at == 0:
                for q in range(self.outer):
                    r.plane[q, 0:1, :] = sum(counts[q * self.inner + m, 4:5, :] for m in range(self.inner))
        else:
            self.wide_wait(at, r.wide_r)
            n_all, _, mean, spread = combine(r.wide[at], self.wide_count, self.outer, count)
        inverse = lax.rsqrt(spread / n_all + EPS)
        r.dense[0:count, :] = mean
        row_form(table, 0, r.dense, 0, count)
        r.dense[0:count, :] = inverse
        row_form(table, 1, r.dense, 0, count)
        return n_all, inverse

    def sums_near(self, at):
        if not self.one_stage(at):
            self.near_wait(at, self.r.near_r)
            self.r.wide[at][self.high] = total(self.r.near[at])
            self.wide_send(at)

    def sums_wide(self, at):
        if self.one_stage(at):
            self.near_wait(at, self.r.near_r)
            return total(self.r.near[at])
        self.wide_wait(at, self.r.wide_r)
        return total(self.r.wide[at])

    def local_stats(self, buf, at, ref):
        channels = ref.shape[1]
        count = channels // 128
        for c in range(channels // 256):
            lanes = slice(c * 256, (c + 1) * 256)

            def gather(term):
                acc = jnp.zeros((SIDE, 256), F32)
                for k in range(self.live):
                    part = lax.fori_loop(
                        0, self.height, lambda y, a: a + term(ref[pl.ds(block(k, y), SIDE), lanes]),
                        jnp.zeros((SIDE, 256), F32), unroll=self.height,
                    )
                    acc = acc + part * self.v[k]
                return self.fold(acc)

            s_own = gather(lambda x: x)
            mean = s_own / jnp.maximum(self.n_own, 1.0)
            to_dense(buf, at, s_own, 2 * c)
            to_dense(buf, at, gather(lambda x: (x - mean) * (x - mean)), count + 2 * c)

    def norm_silu(self, ref, slope_ref, table, gain, bias, write):
        centre, scale = table[0:1, :], table[1:2, :] * gain[...].reshape(1, self.mid)
        b = bias[...].reshape(1, self.mid)
        for k in range(self.live):
            def step(y, carry):
                at = block(k, y)
                u = (ref[pl.ds(at, SIDE), :] - centre) * scale + b
                s = 0.5 * jnp.tanh(0.5 * u) + 0.5
                h = u * s
                slope_ref[pl.ds(at, SIDE), :] = jnp.where(self.mask, s + (h - h * s), 0.0)
                write(at, jnp.where(self.mask, h, 0.0))
                return carry

            lax.fori_loop(0, self.height, step, 0, unroll=7)


def flips(index, count, stride=1):
    steps, at = [], 1
    while at < count:
        steps.append(at * stride * (1 - 2 * ((index // (at * stride)) % 2)))
        at *= 2
    return [sum((d for b, d in enumerate(steps) if o >> b & 1), index) for o in reversed(range(1, count))]


def combine(buf, counts, group, count):
    n_part = [counts(q) for q in range(group)]
    s_part = [buf[q, 0:count, :] for q in range(group)]
    n_all = sum(n_part[1:], n_part[0])
    s_all = sum(s_part[1:], s_part[0])
    mean = s_all / jnp.maximum(n_all, 1.0)
    spread = jnp.zeros((count, 128), F32)
    for q in range(group):
        gap = s_part[q] / jnp.maximum(n_part[q], 1.0) - mean
        spread = spread + (buf[q, count : 2 * count, :] + n_part[q] * gap * gap)
    return n_all, s_all, mean, spread


def total(buf):
    out = buf[0]
    for q in range(1, buf.shape[0]):
        out = out + buf[q]
    return out


def clear(*refs):
    for ref in refs:
        ref[...] = jnp.zeros(ref.shape, ref.dtype)


def prologue(t):
    r, slots, live, width, feat = t.r, t.slots, t.live, t.width, t.feat
    t.places()
    t.greet()
    t.load(
        frames=(r.frames, r.f4.at[pl.ds(0, t.area)]), valid=(r.slot_valid, r.valid), reduce=(r.w_reduce, r.wr),
        clip=(r.clip_ids, r.clip), segment=(r.segment_ids, r.segment),
        share=(r.segment_weight, r.share), spatial=(r.w_spatial, r.ws), expand=(r.w_expand, r.we),
        ga=(r.gain_a, r.ga), ba=(r.bias_a, r.ba), gb=(r.gain_b, r.gb), bb=(r.bias_b, r.bb),
        gc=(r.gain_c, r.gc), bc=(r.bias_c, r.bc), loss=(r.loss_weight, r.loss),
    )
    for i in range(3):
        for j in range(3):
            pltpu.make_async_copy(
                r.w_spatial.at[i, j], r.wc.at[i, :, pl.ds(j * t.mid, t.mid)], r.load_sem.at[15]
            ).start()
    r.f4[t.area :] = jnp.zeros((r.f4.shape[0] - t.area, *r.f4.shape[1:]), BF16)
    clear(r.fp)
    t.loaded(valid=0)
    t.slot_facts()
    t.loaded(frames=0)
    fp, f4 = r.fp, r.f4
    tiles = feat // 128
    group = SIDE // slots
    short = lax.broadcasted_iota(jnp.int32, (SIDE, 128), 0) < width

    def regroup(y, carry):
        for p in range(tiles // group):
            value = f4[pl.ds(y * width, SIDE), p * SIDE : (p + 1) * SIDE, :].astype(F32)
            value = jnp.swapaxes(value, 0, 1)
            for q in range(group):
                for k in range(live):
                    row = value[q * slots + k] * t.keep[k] + value[q * slots + k + 1] * t.moved[k]
                    lanes = slice((p * group + q) * 128, (p * group + q + 1) * 128)
                    fp[pl.ds(block(k, y), SIDE), lanes] = jnp.where(short, row, 0.0).astype(BF16)
        return carry

    lax.fori_loop(0, t.height, regroup, 0)
    t.loaded(reduce=0)
    by_rows(r.pre_a, lambda here: dot(fp[here, :], r.wr[...]))
    t.local_stats(r.near[0], t.near_at(0), r.pre_a)
    r.near[0][t.near_at(0), 4:5, :] = jnp.full((1, 128), t.n_own, F32)


def forward(t):
    r, live, mid, feat, rows, area, height = t.r, t.live, t.mid, t.feat, t.rows, t.area, t.height
    t.all_here()
    t.near_send(0)
    r.ft[...] = r.fp[...].T
    t.stats_near(0, mid // 128)
    clear(r.xp, r.hb, r.g3, r.gpc, r.gpa)
    t.loaded(clip=0, segment=0, share=0, ga=0, ba=0, gb=0, bb=0, gc=0, bc=0, loss=0, spatial=0, expand=0)
    key = [t.kept(r.clip, k) for k in range(live)]
    weight = []
    for k in range(live):
        at = t.kept(r.segment, k)
        w0, w1, w2 = (r.share[q] for q in range(3))
        weight.append(
            t.v[k] * (w0 * ((1.0 - at) * (2.0 - at) * 0.5) + w1 * (at * (2.0 - at)) + w2 * (at * (at - 1.0) * 0.5))
        )
    n_all, inv_a = t.stats_wide(0, mid // 128, r.table_a)

    xp, hb = r.xp, r.hb

    def write_a(at, h):
        three(xp, at, pltpu.roll(h, 1, 0), h, pltpu.roll(h, SIDE - 1, 0))

    t.norm_silu(r.pre_a, r.slope_a, r.table_a, r.ga, r.ba, write_a)

    by_rows(
        r.pre_b,
        lambda here: sum(dot(xp[moved_rows(here, i * SIDE), :], r.ws[i].reshape(3 * mid, mid)) for i in range(3)),
    )
    t.local_stats(r.near[1], t.near_at(1), r.pre_b)
    t.near_send(1)
    r.xt[...] = xp[SIDE : SIDE + rows, mid : 2 * mid].T
    t.stats_near(1, mid // 128)
    _, inv_b = t.stats_wide(1, mid // 128, r.table_b)

    def write_b(at, h):
        hb[pl.ds(at, SIDE), :] = h.astype(BF16)

    t.norm_silu(r.pre_b, r.slope_b, r.table_b, r.gb, r.bb, write_b)

    pre_c, slope_c, fp, table_c = r.pre_c, r.slope_c, r.fp, r.table_c
    by_rows(pre_c, lambda here: dot(hb[here, :], r.we[...]))
    t.local_stats(r.near[2], t.near_at(2), pre_c)
    t.near_send(2)
    r.hbt[...] = hb[...].T
    t.stats_near(2, feat // 128)
    _, inv_c = t.stats_wide(2, feat // 128, table_c)

    pool, slope_sum, slope_hat = r.pool, r.slope_sum, r.slope_hat
    for c in range(feat // 256):
        lanes = slice(c * 256, (c + 1) * 256)
        centre, inverse = table_c[0:1, lanes], table_c[1:2, lanes]
        g = r.gc[lanes].reshape(1, 256)
        b = r.bc[lanes].reshape(1, 256)
        for k in range(live):
            def step(y, carry):
                a0, a1, a2 = carry
                at = block(k, y)
                hat = (pre_c[pl.ds(at, SIDE), lanes] - centre) * inverse
                u = hat * g + b + fp[pl.ds(at, SIDE), lanes].astype(F32)
                s = 0.5 * jnp.tanh(0.5 * u) + 0.5
                h = u * s
                slope = s + (h - h * s)
                slope_c[pl.ds(at, SIDE), lanes] = slope
                return a0 + h, a1 + slope, a2 + slope * hat

            zero = jnp.zeros((SIDE, 256), F32)
            a0, a1, a2 = lax.fori_loop(0, height, step, (zero, zero, zero), unroll=7)
            p_row = (t.fold(a0) * (1.0 / area)).astype(BF16).astype(F32)
            to_dense(pool, 0, p_row, 8 * k + 2 * c)
            to_dense(slope_sum, k, t.fold(a1), 2 * c)
            to_dense(slope_hat, k, t.fold(a2), 2 * c)
    for k in range(live):
        pool[0, 24 + k : 25 + k, :] = jnp.full((1, 128), key[k], F32)
        pool[0, 28 + k : 29 + k, :] = jnp.full((1, 128), weight[k], F32)
    for q, device in enumerate(t.clip_peers):
        t.send(pool.at[0], pool.at[q + 1], r.pool_s.at[0], r.pool_r.at[0], device)
    wait_bytes(pool.at[pl.ds(1, len(t.clip_peers))], r.pool_r.at[0])

    lw = dense_of(r.loss, r.dense)
    grads = []
    for k in range(live):
        my_key = jnp.full((1, 128), key[k], F32)
        my_weight = jnp.full((1, 128), weight[k], F32)
        mean = jnp.zeros((8, 128), F32)
        den = jnp.zeros((1, 128), F32)
        for q in range(len(t.clip_peers) + 1):
            for m in range(live):
                match = jnp.where(pool[q, 24 + m : 25 + m, :] == my_key, pool[q, 28 + m : 29 + m, :], 0.0)
                den = den + match
                mean = mean + match * pool[q, 8 * m : 8 * m + 8, :]
        den = jnp.where(den == 0.0, 1.0, den)
        mean = mean / den
        power = jnp.sum(jnp.sum(mean * mean, axis=0, keepdims=True), axis=1, keepdims=True)
        scale = lax.rsqrt(power * (1.0 / feat) + EPS)
        unit = mean * scale
        along = jnp.sum(jnp.sum(unit * lw, axis=0, keepdims=True), axis=1, keepdims=True)
        mean_grad = scale * (lw - unit * (along * (1.0 / feat)))
        grads.append((my_weight / den) * mean_grad * (1.0 / area))

    near3 = r.near[3]
    shift = jnp.zeros((8, 128), F32)
    gain = jnp.zeros((8, 128), F32)
    for k in range(live):
        shift = shift + grads[k] * slope_sum[k]
        gain = gain + grads[k] * slope_hat[k]
    near3[t.near_at(3), 0:8, :] = shift
    near3[t.near_at(3), 8:16, :] = gain
    t.near_send(3)
    coef, dense = r.coef, r.dense
    scale_c = dense_of(r.gc, dense) * inv_c
    for k in range(live):
        dense[...] = grads[k]
        row_form(coef, k, dense, 0, feat // 128)
        dense[...] = grads[k] * scale_c
        row_form(coef, 3 + k, dense, 0, feat // 128)
    t.sums_near(3)
    both = t.sums_wide(3)
    r.vectors_c[...] = both
    dense[...] = both[0:8] * scale_c / n_all
    row_form(coef, 6, dense, 0, feat // 128)
    dense[...] = both[8:16] * scale_c * inv_c / n_all
    row_form(coef, 7, dense, 0, feat // 128)
    return n_all, inv_a, inv_b


def backward(t, n_all, inv_a, inv_b):
    r, live, mid, feat, rows, height = t.r, t.live, t.mid, t.feat, t.rows, t.height
    slots, width, quad, far, v, wc = t.slots, t.width, t.quad, t.far, t.v, r.wc
    coef, pre_c, slope_c, out = r.coef, r.pre_c, r.slope_c, r.vectors
    me, send = t.me, t.send
    gpc = r.gpc
    for k in range(live):
        for c in range(feat // 256):
            lanes = slice(c * 256, (c + 1) * 256)
            centre = r.table_c[0:1, lanes]
            c0 = coef[3 + k : 4 + k, lanes]
            c1 = coef[6:7, lanes] * v[k]
            c2 = coef[7:8, lanes] * v[k]

            def step(y, carry):
                at = block(k, y)
                grad = slope_c[pl.ds(at, SIDE), lanes] * c0 - (c1 + (pre_c[pl.ds(at, SIDE), lanes] - centre) * c2)
                gpc[pl.ds(at, SIDE), lanes] = grad.astype(BF16)
                return carry

            lax.fori_loop(0, height, step, 0, unroll=7)

    def back_sums(at, table, inv, grad_ref, slope_ref, pre_ref):
        zero = jnp.zeros((SIDE, mid), F32)
        carry = (zero, zero)
        centre = table[0:1, :]
        for k in range(live):
            def step(y, c):
                here = pl.ds(block(k, y), SIDE)
                grad = grad_ref[here, :] * slope_ref[here, :]
                grad_ref[here, :] = grad
                return c[0] + grad, c[1] + grad * (pre_ref[here, :] - centre)

            carry = lax.fori_loop(0, height, step, carry, unroll=7)
        buf = r.near[at]
        to_dense(buf, t.near_at(at), jnp.sum(carry[0], axis=0, keepdims=True), 0)
        to_dense(buf, t.near_at(at), jnp.sum(carry[1], axis=0, keepdims=True) * table[1:2, :], 2)

    def back_apply(at, table, gain_ref, inv, grad_ref, pre_ref, write):
        both = t.sums_wide(at)
        out[8 * at - 32 : 8 * at - 28, :] = both[0:4]
        dense = r.dense
        scale = dense_of(gain_ref, dense) * inv
        dense[0:2, :] = scale
        dense[2:4, :] = both[0:2] * scale / n_all
        dense[4:6, :] = both[2:4] * scale * inv / n_all
        for q in range(3):
            row_form(table, 2 + q, dense, 2 * q, 2)
        centre = table[0:1, :]
        for k in range(live):
            c0, c1, c2 = table[2:3, :], table[3:4, :] * v[k], table[4:5, :] * v[k]

            def step(y, carry):
                at_row = block(k, y)
                here = pl.ds(at_row, SIDE)
                write(at_row, grad_ref[here, :] * c0 - (c1 + (pre_ref[here, :] - centre) * c2))
                return carry

            lax.fori_loop(0, height, step, 0, unroll=7)

    core, bit_x, bit_y, at_z = me % 2, (me // 2) % 2, (me // 4) % 2, (me // 8) % quad
    at_far = me // (8 * quad)
    bit1 = bit_x + core * (bit_y - bit_x)
    bit2 = bit_y + core * (bit_x - bit_y)
    sibling = me + 1 - 2 * core
    peer1 = me + (1 - 2 * bit1) * (2 + 2 * core)
    peer2 = me + (1 - 2 * bit2) * (4 - 2 * core)
    z_at = flips(at_z, quad)
    z_peer = [me + 8 * (q - at_z) for q in z_at]
    far_peer = [me + 8 * quad * ((at_far + o) % far - at_far) for o in range(1, far)]
    chunk_s, chunk_r = r.chunk_s, r.chunk_r
    waits, blocks = [], iter(ORDER)
    plan = [(0, q, 2) for q in range(2)] + [(1 + q // 2, q % 2, 2) for q in range(6)] + [(4, q, 4) for q in range(4)]

    def chunk(q):
        name, at, count = plan[q]
        size = r.part[name].shape[0] // count
        part = r.part[name].at[pl.ds(at * size, size)]
        whole = (r.e, r.s0, r.s1, r.s2, r.r)[name].at[pl.ds(at * size, size)]
        half, quarter, eighth, piece = size // 2, size // 4, size // 8, size // (8 * quad)
        m8 = lambda value: pl.multiple_of(value, 8)
        at_h = m8(core * half)
        at_q = m8(at_h + bit1 * quarter)
        at_e = m8(at_q + bit2 * eighth)
        at_p = m8(at_e + at_z * piece)

        def go(step, src, dst, device):
            send(src, dst, chunk_s.at[q, step], chunk_r.at[q, step], device)

        def finish(step, ref):
            wait_bytes(ref, chunk_r.at[q, step])
            waits.append((ref, chunk_s.at[q, step]))

        rb0, rb1, rb2, rb3 = r.rb0[q], r.rb1[q], r.rb2[q], r.rb3[q]
        go(0, part.at[pl.ds(m8((1 - core) * half), half)], rb0, sibling)
        yield
        finish(0, rb0)
        part[pl.ds(at_h, half), :] = part[pl.ds(at_h, half), :] + rb0[...]
        go(1, part.at[pl.ds(m8(at_h + (1 - bit1) * quarter), quarter)], rb1, peer1)
        yield
        finish(1, rb1)
        part[pl.ds(at_q, quarter), :] = part[pl.ds(at_q, quarter), :] + rb1[...]
        go(2, part.at[pl.ds(m8(at_q + (1 - bit2) * eighth), eighth)], rb2, peer2)
        yield
        finish(2, rb2)
        part[pl.ds(at_e, eighth), :] = part[pl.ds(at_e, eighth), :] + rb2[...]
        for o in range(quad - 1):
            go(3, part.at[pl.ds(m8(at_e + z_at[o] * piece), piece)], rb3.at[pl.ds(o * piece, piece)], z_peer[o])
        yield
        finish(3, rb3)
        own = part[pl.ds(at_p, piece), :]
        for o in range(quad - 1):
            own = own + rb3[o * piece : (o + 1) * piece, :]
        if far > 1:
            rb4 = r.rb4[q]
            rb4[at_far] = own
            for device in far_peer:
                go(8, rb4.at[at_far], rb4.at[at_far], device)
            yield
            finish(8, rb4.at[pl.ds(0, far - 1)])
            own = rb4[0]
            for o in range(1, far):
                own = own + rb4[o]
        whole[pl.ds(at_p, piece), :] = own
        for o in range(quad - 1):
            go(4, whole.at[pl.ds(at_p, piece)], whole.at[pl.ds(at_p, piece)], z_peer[o])
        yield
        finish(4, whole.at[pl.ds(0, (quad - 1) * piece)])
        go(5, whole.at[pl.ds(at_e, eighth)], whole.at[pl.ds(at_e, eighth)], peer2)
        yield
        finish(5, whole.at[pl.ds(0, eighth)])
        go(6, whole.at[pl.ds(at_q, quarter)], whole.at[pl.ds(at_q, quarter)], peer1)
        yield
        finish(6, whole.at[pl.ds(0, quarter)])
        go(7, whole.at[pl.ds(at_h, half)], whole.at[pl.ds(at_h, half)], sibling)
        yield
        finish(7, whole.at[pl.ds(0, half)])
        yield

    chunks = [chunk(q) for q in range(len(plan))]

    def go_on(*which):
        for q in which:
            next(chunks[q])

    def go_on_all():
        go_on(*next(blocks))

    pre_a, slope_a, pre_b, slope_b, hbt, xt = r.pre_a, r.slope_a, r.pre_b, r.slope_b, r.hbt, r.xt
    we, wr, back = r.we, r.wr, r.back
    tiles = feat // 128
    group = SIDE // slots
    keep, moved, mask = t.keep, t.moved, t.mask
    grad_b, grad_a = r.grad_b, r.grad_a
    wait_bytes(wc, r.load_sem.at[15])
    g3 = r.g3

    def write_gb(at, grad):
        grad = jnp.where(mask, grad, 0.0)
        three(g3, at, pltpu.roll(grad, SIDE - 1, 0), grad, pltpu.roll(grad, 1, 0))

    def expand_part(e):
        go_on_all()
        for q in range(2):
            first = (2 * e + q) * 256
            spread_lanes(r.part[0].at[pl.ds(2 * first, 512)], dot(hbt[...], gpc[:, first : first + 256]))
        go_on(e)

    def spatial_part(i):
        go_on_all()
        spread_lanes(r.part[1 + i], dot(xt[...], g3[(2 - i) * SIDE : (2 - i) * SIDE + rows, :]))
        go_on(2 + 2 * i, 3 + 2 * i)

    go_on_all()
    expand_part(0)
    go_on_all()
    by_rows(grad_b, lambda here: dot(gpc[here, :], we[...], NT))
    back_sums(4, r.table_b, inv_b, grad_b, slope_b, pre_b)
    t.near_send(4)
    expand_part(1)
    t.sums_near(4)
    go_on_all()
    back_apply(4, r.table_b, r.gb, inv_b, grad_b, pre_b, write_gb)
    spatial_part(0)
    go_on_all()
    by_rows(
        grad_a, lambda here: sum(dot(g3[moved_rows(here, (2 - i) * SIDE), :], wc[i], NT) for i in range(3))
    )
    back_sums(5, r.table_a, inv_a, grad_a, slope_a, pre_a)
    t.near_send(5)
    spatial_part(1)
    t.sums_near(5)
    spatial_part(2)
    go_on_all()
    gpa = r.gpa

    def write_ga(at, grad):
        gpa[pl.ds(at, SIDE), :] = grad.astype(BF16)

    back_apply(5, r.table_a, r.ga, inv_a, grad_a, pre_a, write_ga)
    for q in range(4):
        go_on_all()
        spread_lanes(r.part[4].at[pl.ds(q * 512, 512)], dot(r.ft[q * 256 : (q + 1) * 256, :], gpa[...]))
        go_on(8 + q)

    go_on_all()
    by_rows(back, lambda here: dot(gpa[here, :], wr[...], NT))
    gf = r.gf

    def blend(y, carry):
        for p in range(tiles // group):
            values = []
            for q in range(group):
                lanes = slice((p * group + q) * 128, (p * group + q + 1) * 128)
                terms = [
                    slope_c[pl.ds(block(k, y), SIDE), lanes] * coef[k : k + 1, lanes]
                    + back[pl.ds(block(k, y), SIDE), lanes]
                    for k in range(live)
                ]
                values.append(terms[0] * keep[0])
                for m in range(1, live):
                    values.append(terms[m] * keep[m] + terms[m - 1] * moved[m - 1])
                values.append(terms[live - 1] * moved[live - 1])
            value = jnp.swapaxes(jnp.stack(values), 0, 1)
            gf[pl.ds(y * width, width), p * SIDE : (p + 1) * SIDE, :] = value[0:width].astype(BF16)
        return carry

    for q in range(height // 2):
        go_on_all()
        for y in range(2):
            blend(2 * q + y, 0)
    go_on_all()
    for each in chunks:
        for _ in each:
            pass

    t.all_sent(*range(6))
    wait_bytes(r.pool.at[pl.ds(1, len(t.clip_peers))], r.pool_s.at[0])
    for ref, sem in waits:
        wait_bytes(ref, sem)


def store(gf, vectors_c, vectors, expand, s0, s1, s2, reduce, frames_out, reduce_out, spatial_out, expand_out, *rest):
    ga, ba, gb, bb, gc, bc, *scratch, sem = rest
    vectors_of = (
        (bc, vectors_c, 0), (gc, vectors_c, 8), (bb, vectors, 0), (gb, vectors, 2), (ba, vectors, 8), (ga, vectors, 10)
    )
    pltpu.make_async_copy(gf, frames_out, sem.at[0]).start()
    for number, (ref, source, first) in enumerate(vectors_of):
        for q in range(ref.shape[0] // 128):
            scratch[number][q * 128 : (q + 1) * 128] = source[first + q : first + q + 1, :].reshape(128)
        pltpu.make_async_copy(scratch[number], ref, sem.at[6 + number]).start()
    depth, width = reduce_out.shape
    for q in range(depth // 256):
        for m in range(width // 128):
            pltpu.make_async_copy(
                reduce.at[pl.ds((q * width // 128 + m) * 256, 256)],
                reduce_out.at[pl.ds(q * 256, 256), pl.ds(m * 128, 128)],
                sem.at[1],
            ).start()
    depth, width = expand_out.shape
    for q in range(width // 128):
        pltpu.make_async_copy(
            expand.at[pl.ds(q * depth, depth)], expand_out.at[:, pl.ds(q * 128, 128)], sem.at[2]
        ).start()
    for i, part in enumerate((s0, s1, s2)):
        for q in range(part.shape[0] // depth):
            pltpu.make_async_copy(
                part.at[pl.ds(q * depth, depth)],
                spatial_out.at[i, q * 128 // depth, :, pl.ds(q * 128 % depth, 128)],
                sem.at[3 + i],
            ).start()
    wait_bytes(gf, sem.at[0])
    wait_bytes(reduce, sem.at[1])
    wait_bytes(expand, sem.at[2])
    for i, part in enumerate((s0, s1, s2)):
        wait_bytes(part, sem.at[3 + i])
    for number in range(6):
        wait_bytes(scratch[number], sem.at[6 + number])


def solution(mesh):
    n = mesh.shape["clip"]

    def shards(*args):
        slots, height, width, feat = args[0].shape
        mid = args[1].shape[1]
        rows = (slots - 1) * ROWS
        outer = n // 8
        quad = min(4, outer)
        far = outer // quad
        cfg = (n, slots, height, width, feat, mid)
        flat_shape = (height * width, slots * feat // 128, 128)
        hbm = pl.BlockSpec(memory_space=pltpu.HBM)
        vmem = pl.BlockSpec(memory_space=pltpu.VMEM)
        dma = pltpu.SemaphoreType.DMA
        depths = list(enumerate((8, 4, 16, 16, 4, 4)))
        matrix, third = mid * feat // 128, 3 * mid * mid // 128
        sizes = [matrix, third, third, third, matrix]

        tiled = args[0].transpose(1, 2, 0, 3).reshape(height, width, slots, feat // 128, 128)
        tiled = tiled.transpose(0, 1, 3, 2, 4).reshape(flat_shape)
        given = [pltpu.with_memory_space_constraint(part, pltpu.HBM) for part in (tiled, *args[1:])]

        vm = pltpu.VMEM
        narrow, broad, square = vm((mid,), F32), vm((feat,), F32), vm((rows, mid), F32)
        ints = pltpu.SMEM((slots,), jnp.int32)
        plan = [matrix // 2] * 2 + [third // 2] * 6 + [matrix // 4] * 4
        outs = dict(
            gf=vm(flat_shape, BF16), vectors_c=vm((16, 128), F32), vectors=vm((16, 128), F32),
            e=vm((matrix, 128), F32), s0=vm((third, 128), F32), s1=vm((third, 128), F32), s2=vm((third, 128), F32),
            r=vm((matrix, 128), F32),
        )
        scratch = dict(
            f4=vm((flat_shape[0] + SIDE - width, *flat_shape[1:]), BF16),
            fp=vm((rows, feat), BF16), ft=vm((feat, rows), BF16),
            wr=vm((feat, mid), BF16), ws=vm((3, 3, mid, mid), BF16), wc=vm((3, mid, 3 * mid), BF16), we=vm((mid, feat), BF16),
            valid=ints, clip=ints, segment=ints, share=pltpu.SMEM(args[13].shape, F32),
            ga=narrow, ba=narrow, gb=narrow, bb=narrow, gc=broad, bc=broad, loss=broad,
            xp=vm((rows + 2 * SIDE, 3 * mid), BF16), xt=vm((mid, rows), BF16),
            hb=vm((rows, mid), BF16), hbt=vm((mid, rows), BF16),
            pre_a=square, slope_a=square, pre_b=square, slope_b=square, grad_a=square, grad_b=square,
            pre_c=vm((rows, feat), F32), slope_c=vm((rows, feat), F32), back=vm((rows, feat), F32),
            gpc=vm((rows, feat), BF16), g3=vm((rows + 2 * SIDE, 3 * mid), BF16), gpa=vm((rows, mid), BF16),
            table_a=vm((8, mid), F32), table_b=vm((8, mid), F32),
            table_c=vm((8, feat), F32), coef=vm((8, feat), F32), dense=vm((8, 128), F32),
            pool=vm((6, 32, 128), F32), slope_sum=vm((3, 8, 128), F32), slope_hat=vm((3, 8, 128), F32),
            near=[vm((n if n <= 8 and at not in (2, 3) else 8, deep, 128), F32) for at, deep in depths],
            wide=[vm((outer, deep, 128), F32) for at, deep in depths],
            plane=vm((outer, 8, 128), F32),
            part=[vm((size, 128), F32) for size in sizes],
            rb0=[vm((size // 2, 128), F32) for size in plan],
            rb1=[vm((size // 4, 128), F32) for size in plan],
            rb2=[vm((size // 8, 128), F32) for size in plan],
            rb3=[vm(((quad - 1) * size // (8 * quad), 128), F32) for size in plan],
            rb4=[vm((far, size // (8 * quad), 128), F32) for size in plan if far > 1],
            load_sem=dma((16,)), near_s=dma((6,)), near_r=dma((6,)), wide_s=dma((6,)), wide_r=dma((6,)),
            pool_s=dma((1,)), pool_r=dma((1,)), chunk_s=dma((12, 9)), chunk_r=dma((12, 9)),
        )
        names = (*arg_names(), *outs, *scratch)

        def kernel(*refs):
            t = Step(cfg, SimpleNamespace(**dict(zip(names, refs, strict=True))))
            prologue(t)
            backward(t, *forward(t))

        results = pl.pallas_call(
            kernel,
            out_shape=list(outs.values()),
            in_specs=[hbm] * len(given),
            out_specs=[vmem] * len(outs),
            scratch_shapes=list(scratch.values()),
            compiler_params=pltpu.CompilerParams(
                collective_id=0, has_side_effects=True, vmem_limit_bytes=50 * 1024 * 1024
            ),
        )(*given)
        vector = jax.ShapeDtypeStruct((mid,), F32)
        wide_vector = jax.ShapeDtypeStruct((feat,), F32)
        flat_grad, *rest = pl.pallas_call(
            store,
            out_shape=[
                jax.ShapeDtypeStruct(flat_shape, BF16),
                jax.ShapeDtypeStruct((feat, mid), F32),
                jax.ShapeDtypeStruct((3, 3, mid, mid), F32),
                jax.ShapeDtypeStruct((mid, feat), F32),
                vector, vector, vector, vector, wide_vector, wide_vector,
            ],
            in_specs=[vmem] * 8,
            out_specs=[hbm] * 10,
            scratch_shapes=[*(vm((c,), F32) for c in (feat, feat, mid, mid, mid, mid)), dma((12,))],
            compiler_params=pltpu.CompilerParams(vmem_limit_bytes=8 * 1024 * 1024),
        )(*(pltpu.with_memory_space_constraint(part, pltpu.VMEM) for part in results))
        grad_frames = flat_grad.reshape(height, width, feat // 128, slots, 128).transpose(0, 1, 3, 2, 4)
        return grad_frames.reshape(height, width, slots, feat).transpose(2, 0, 1, 3), *rest

    split = P("clip")
    in_specs = (split,) + (P(),) * 9 + (split,) * 3 + (P(), P())
    out_specs = (split,) + (P(),) * 9
    return jax.shard_map(shards, mesh=mesh, in_specs=in_specs, out_specs=out_specs, check_vma=False)


def arg_names():
    return dict(
        frames=0, w_reduce=0, w_spatial=0, w_expand=0, gain_a=0, bias_a=0, gain_b=0, bias_b=0, gain_c=0, bias_c=0,
        clip_ids=0, segment_ids=0, slot_valid=0, segment_weight=0, loss_weight=0,
    )
```

```python
import functools
from types import SimpleNamespace

import jax
import jax.numpy as jnp
from jax import lax
from jax.experimental import pallas as pl
from jax.experimental.pallas import tpu as pltpu
from jax.sharding import PartitionSpec as P

MESH = pl.DeviceIdType.MESH
EPS = 1e-05
F32 = jnp.float32
BF16 = jnp.bfloat16
SIDE = 16
ROWS = SIDE * SIDE
NN = (((1,), (0,)), ((), ()))
NT = (((1,), (1,)), ((), ()))

ORDER = (
    (),
    (),
    (),
    (),
    (),
    (0,),
    (1, 0,),
    (),
    (1, 0,),
    (2,),
    (1, 3, 0, 2,),
    (4, 1, 3,),
    (2, 5, 4, 3, 0,),
    (1, 5, 2,),
    (0, 4, 3,),
    (),
    (2, 5, 1,),
    (),
    (4, 3, 2, 5, 4, 1, 3, 5, 4, 2, 5, 0,),
    (4, 3, 1, 5, 4, 2, 3, 0, 5,),
)


def dot(a, b, dims=NN):
    return lax.dot_general(a, b, dims, preferred_element_type=F32)


def wait_bytes(ref, sem):
    pltpu.make_async_copy(ref, ref, sem).wait()


def spread_lanes(ref, value):
    depth = value.shape[0]
    for q in range(value.shape[1] // 128):
        ref[q * depth : (q + 1) * depth, :] = value[:, q * 128 : (q + 1) * 128]


def by_rows(ref, value):
    def step(k, carry):
        here = pl.ds(pl.multiple_of(k * 256, 256), 256)
        ref[here, :] = value(here)
        return carry

    lax.fori_loop(0, ref.shape[0] // 256, step, 0)


def moved_rows(here, at):
    return pl.ds(pl.multiple_of(here.start + at, SIDE), 256)


def block(k, y):
    return pl.multiple_of(k * ROWS + y * SIDE, SIDE)


def to_dense(ref, at, value, first):
    for q in range(value.shape[1] // 128):
        ref[at, pl.ds(first + q, 1), :] = value[:, q * 128 : (q + 1) * 128]


def row_form(ref, row, source, first, count):
    for q in range(count):
        ref[row : row + 1, q * 128 : (q + 1) * 128] = source[first + q : first + q + 1, :]


def three(ref, at, left, middle, right):
    here, wide = pl.ds(at + SIDE, SIDE), middle.shape[1]
    ref[here, 0:wide] = left.astype(BF16)
    ref[here, wide : 2 * wide] = middle.astype(BF16)
    ref[here, 2 * wide : 3 * wide] = right.astype(BF16)


def dense_of(ref1, scratch):
    count = ref1.shape[0] // 128
    for q in range(count):
        scratch[q : q + 1, :] = ref1[q * 128 : (q + 1) * 128].reshape(1, 128)
    return scratch[0:count, :]


class Step:
    def __init__(self, cfg, r):
        self.r, self.sizes = r, cfg
        self.n, self.slots, self.height, self.width, self.feat, self.mid = cfg
        self.live = self.slots - 1
        self.rows = self.live * ROWS
        self.area = self.height * self.width
        self.inner = 8
        self.outer = self.n // 8
        self.quad = min(4, self.outer)
        self.far = self.outer // self.quad
        self.loads = {}
        self.mask = lax.broadcasted_iota(jnp.int32, (SIDE, 256), 0) < self.width

    def load(self, **pairs):
        for name, (src, dst) in pairs.items():
            copy = pltpu.make_async_copy(src, dst, self.r.load_sem.at[len(self.loads)])
            copy.start()
            self.loads[name] = copy

    def loaded(self, **names):
        for name in names:
            self.loads[name].wait()

    def fold(self, value):
        return jnp.sum(jnp.where(self.mask, value, 0.0), axis=0, keepdims=True)

    def slot_facts(self):
        r, live = self.r, self.live
        alive, later = 1, []
        for k in range(live):
            alive = alive * r.valid[k]
            later.append(1 - alive)
        self.keep = [(1 - q).astype(F32) for q in later]
        self.moved = [q.astype(F32) for q in later]
        self.later = later
        self.v = [self.kept(r.valid, k) for k in range(live)]
        self.n_own = (self.v[0] + self.v[1] + self.v[2]) * float(self.area)

    def kept(self, values, k):
        return (values[k] + self.later[k] * (values[k + 1] - values[k])).astype(F32)

    def places(self):
        n = self.n
        self.me = me = lax.axis_index("clip")
        self.low, self.high = low, high = me % self.inner, me // self.inner
        self.direct = n <= 32
        self.peers = flips(me, n)
        self.low_peers = flips(me, self.inner)
        self.high_peers = flips(me, self.outer, self.inner)
        self.clip_peers = [(me + o) % n for o in (n // 2 - 1, n // 2 + 1, n // 2, n - 1, 1)]

    def greet(self):
        self.greeted = self.peers if self.direct else self.low_peers + self.high_peers + self.clip_peers
        self.barrier = pltpu.get_barrier_semaphore()
        for device in self.greeted:
            pl.semaphore_signal(self.barrier, inc=1, device_id=(device,), device_id_type=MESH)

    def all_here(self):
        pl.semaphore_wait(self.barrier, len(self.greeted))

    def send(self, src, dst, ssem, rsem, device):
        pltpu.make_async_remote_copy(
            src_ref=src, dst_ref=dst, send_sem=ssem, recv_sem=rsem, device_id=(device,), device_id_type=MESH
        ).start()

    def one_stage(self, at):
        return self.direct and at not in (2, 3)

    def near_at(self, at):
        return self.me if self.one_stage(at) else self.low

    def near_send(self, at):
        buf, mine = self.r.near[at], self.near_at(at)
        for device in self.peers if self.one_stage(at) else self.low_peers:
            self.send(buf.at[mine], buf.at[mine], self.r.near_s.at[at], self.r.near_r.at[at], device)

    def near_wait(self, at, sems):
        buf = self.r.near[at]
        wait_bytes(buf.at[pl.ds(0, buf.shape[0] - 1)], sems.at[at])

    def wide_send(self, at):
        buf = self.r.wide[at]
        for device in self.high_peers:
            self.send(buf.at[self.high], buf.at[self.high], self.r.wide_s.at[at], self.r.wide_r.at[at], device)

    def wide_wait(self, at, sems):
        wait_bytes(self.r.wide[at].at[pl.ds(0, self.outer - 1)], sems.at[at])

    def all_sent(self, *rounds):
        for at in rounds:
            self.near_wait(at, self.r.near_s)
            if not self.one_stage(at):
                self.wide_wait(at, self.r.wide_s)

    def near_count(self, q):
        return self.r.near[0][(self.me - self.low + q) if self.direct else q, 4:5, :]

    def wide_count(self, q):
        return self.r.plane[q, 0:1, :] if self.direct else self.r.wide[0][q, 4:5, :]

    def stats_near(self, at, count):
        if self.one_stage(at):
            return
        self.near_wait(at, self.r.near_r)
        n_all, s_all, _, spread = combine(self.r.near[at], self.near_count, self.inner, count)
        buf = self.r.wide[at]
        buf[self.high, 0:count, :] = s_all
        buf[self.high, count : 2 * count, :] = spread
        if at == 0:
            buf[self.high, 4:5, :] = n_all
        self.wide_send(at)

    def stats_wide(self, at, count, table):
        r = self.r
        if self.one_stage(at):
            self.near_wait(at, r.near_r)
            counts = r.near[0]
            n_all, _, mean, spread = combine(r.near[at], lambda q: counts[q, 4:5, :], self.n, count)
            if at == 0:
                for q in range(self.outer):
                    r.plane[q, 0:1, :] = sum(counts[q * self.inner + m, 4:5, :] for m in range(self.inner))
        else:
            self.wide_wait(at, r.wide_r)
            n_all, _, mean, spread = combine(r.wide[at], self.wide_count, self.outer, count)
        inverse = lax.rsqrt(spread / n_all + EPS)
        r.dense[0:count, :] = mean
        row_form(table, 0, r.dense, 0, count)
        r.dense[0:count, :] = inverse
        row_form(table, 1, r.dense, 0, count)
        return n_all, inverse

    def sums_near(self, at):
        if not self.one_stage(at):
            self.near_wait(at, self.r.near_r)
            self.r.wide[at][self.high] = total(self.r.near[at])
            self.wide_send(at)

    def sums_wide(self, at):
        if self.one_stage(at):
            self.near_wait(at, self.r.near_r)
            return total(self.r.near[at])
        self.wide_wait(at, self.r.wide_r)
        return total(self.r.wide[at])

    def local_stats(self, buf, at, ref):
        channels = ref.shape[1]
        count = channels // 128
        for c in range(channels // 256):
            lanes = slice(c * 256, (c + 1) * 256)

            def gather(term):
                acc = jnp.zeros((SIDE, 256), F32)
                for k in range(self.live):
                    part = lax.fori_loop(
                        0, self.height, lambda y, a: a + term(ref[pl.ds(block(k, y), SIDE), lanes]),
                        jnp.zeros((SIDE, 256), F32), unroll=self.height,
                    )
                    acc = acc + part * self.v[k]
                return self.fold(acc)

            s_own = gather(lambda x: x)
            mean = s_own / jnp.maximum(self.n_own, 1.0)
            to_dense(buf, at, s_own, 2 * c)
            to_dense(buf, at, gather(lambda x: (x - mean) * (x - mean)), count + 2 * c)

    def norm_silu(self, ref, slope_ref, table, gain, bias, write):
        centre, scale = table[0:1, :], table[1:2, :] * gain[...].reshape(1, self.mid)
        b = bias[...].reshape(1, self.mid)
        for k in range(self.live):
            def step(y, carry):
                at = block(k, y)
                u = (ref[pl.ds(at, SIDE), :] - centre) * scale + b
                s = 0.5 * jnp.tanh(0.5 * u) + 0.5
                h = u * s
                slope_ref[pl.ds(at, SIDE), :] = jnp.where(self.mask, s + (h - h * s), 0.0)
                write(at, jnp.where(self.mask, h, 0.0))
                return carry

            lax.fori_loop(0, self.height, step, 0, unroll=7)


def flips(index, count, stride=1):
    steps, at = [], 1
    while at < count:
        steps.append(at * stride * (1 - 2 * ((index // (at * stride)) % 2)))
        at *= 2
    return [sum((d for b, d in enumerate(steps) if o >> b & 1), index) for o in reversed(range(1, count))]


def combine(buf, counts, group, count):
    n_part = [counts(q) for q in range(group)]
    s_part = [buf[q, 0:count, :] for q in range(group)]
    n_all = sum(n_part[1:], n_part[0])
    s_all = sum(s_part[1:], s_part[0])
    mean = s_all / jnp.maximum(n_all, 1.0)
    spread = jnp.zeros((count, 128), F32)
    for q in range(group):
        gap = s_part[q] / jnp.maximum(n_part[q], 1.0) - mean
        spread = spread + (buf[q, count : 2 * count, :] + n_part[q] * gap * gap)
    return n_all, s_all, mean, spread


def total(buf):
    out = buf[0]
    for q in range(1, buf.shape[0]):
        out = out + buf[q]
    return out


def clear(*refs):
    for ref in refs:
        ref[...] = jnp.zeros(ref.shape, ref.dtype)


def prologue(t):
    r, slots, live, width, feat = t.r, t.slots, t.live, t.width, t.feat
    t.places()
    t.greet()
    t.load(
        frames=(r.frames, r.f4.at[pl.ds(0, t.area)]), valid=(r.slot_valid, r.valid), reduce=(r.w_reduce, r.wr),
        clip=(r.clip_ids, r.clip), segment=(r.segment_ids, r.segment),
        share=(r.segment_weight, r.share), spatial=(r.w_spatial, r.ws), expand=(r.w_expand, r.we),
        ga=(r.gain_a, r.ga), ba=(r.bias_a, r.ba), gb=(r.gain_b, r.gb), bb=(r.bias_b, r.bb),
        gc=(r.gain_c, r.gc), bc=(r.bias_c, r.bc), loss=(r.loss_weight, r.loss),
    )
    for i in range(3):
        for j in range(3):
            pltpu.make_async_copy(
                r.w_spatial.at[i, j], r.wc.at[i, :, pl.ds(j * t.mid, t.mid)], r.load_sem.at[15]
            ).start()
    r.f4[t.area :] = jnp.zeros((r.f4.shape[0] - t.area, *r.f4.shape[1:]), BF16)
    clear(r.fp)
    t.loaded(valid=0)
    t.slot_facts()
    t.loaded(frames=0)
    fp, f4 = r.fp, r.f4
    tiles = feat // 128
    group = SIDE // slots
    short = lax.broadcasted_iota(jnp.int32, (SIDE, 128), 0) < width

    def regroup(y, carry):
        for p in range(tiles // group):
            value = f4[pl.ds(y * width, SIDE), p * SIDE : (p + 1) * SIDE, :].astype(F32)
            value = jnp.swapaxes(value, 0, 1)
            for q in range(group):
                for k in range(live):
                    row = value[q * slots + k] * t.keep[k] + value[q * slots + k + 1] * t.moved[k]
                    lanes = slice((p * group + q) * 128, (p * group + q + 1) * 128)
                    fp[pl.ds(block(k, y), SIDE), lanes] = jnp.where(short, row, 0.0).astype(BF16)
        return carry

    lax.fori_loop(0, t.height, regroup, 0)
    t.loaded(reduce=0)
    by_rows(r.pre_a, lambda here: dot(fp[here, :], r.wr[...]))
    t.local_stats(r.near[0], t.near_at(0), r.pre_a)
    r.near[0][t.near_at(0), 4:5, :] = jnp.full((1, 128), t.n_own, F32)


def forward(t):
    r, live, mid, feat, rows, area, height = t.r, t.live, t.mid, t.feat, t.rows, t.area, t.height
    t.all_here()
    t.near_send(0)
    r.ft[...] = r.fp[...].T
    t.stats_near(0, mid // 128)
    clear(r.xp, r.hb, r.g3, r.gpc, r.gpa)
    t.loaded(clip=0, segment=0, share=0, ga=0, ba=0, gb=0, bb=0, gc=0, bc=0, loss=0, spatial=0, expand=0)
    key = [t.kept(r.clip, k) for k in range(live)]
    weight = []
    for k in range(live):
        at = t.kept(r.segment, k)
        w0, w1, w2 = (r.share[q] for q in range(3))
        weight.append(
            t.v[k] * (w0 * ((1.0 - at) * (2.0 - at) * 0.5) + w1 * (at * (2.0 - at)) + w2 * (at * (at - 1.0) * 0.5))
        )
    n_all, inv_a = t.stats_wide(0, mid // 128, r.table_a)

    xp, hb = r.xp, r.hb

    def write_a(at, h):
        three(xp, at, pltpu.roll(h, 1, 0), h, pltpu.roll(h, SIDE - 1, 0))

    t.norm_silu(r.pre_a, r.slope_a, r.table_a, r.ga, r.ba, write_a)

    by_rows(
        r.pre_b,
        lambda here: sum(dot(xp[moved_rows(here, i * SIDE), :], r.ws[i].reshape(3 * mid, mid)) for i in range(3)),
    )
    t.local_stats(r.near[1], t.near_at(1), r.pre_b)
    t.near_send(1)
    r.xt[...] = xp[SIDE : SIDE + rows, mid : 2 * mid].T
    t.stats_near(1, mid // 128)
    _, inv_b = t.stats_wide(1, mid // 128, r.table_b)

    def write_b(at, h):
        hb[pl.ds(at, SIDE), :] = h.astype(BF16)

    t.norm_silu(r.pre_b, r.slope_b, r.table_b, r.gb, r.bb, write_b)

    pre_c, slope_c, fp, table_c = r.pre_c, r.slope_c, r.fp, r.table_c
    by_rows(pre_c, lambda here: dot(hb[here, :], r.we[...]))
    t.local_stats(r.near[2], t.near_at(2), pre_c)
    t.near_send(2)
    r.hbt[...] = hb[...].T
    t.stats_near(2, feat // 128)
    _, inv_c = t.stats_wide(2, feat // 128, table_c)

    pool, slope_sum, slope_hat = r.pool, r.slope_sum, r.slope_hat
    for c in range(feat // 256):
        lanes = slice(c * 256, (c + 1) * 256)
        centre, inverse = table_c[0:1, lanes], table_c[1:2, lanes]
        g = r.gc[lanes].reshape(1, 256)
        b = r.bc[lanes].reshape(1, 256)
        for k in range(live):
            def step(y, carry):
                a0, a1, a2 = carry
                at = block(k, y)
                hat = (pre_c[pl.ds(at, SIDE), lanes] - centre) * inverse
                u = hat * g + b + fp[pl.ds(at, SIDE), lanes].astype(F32)
                s = 0.5 * jnp.tanh(0.5 * u) + 0.5
                h = u * s
                slope = s + (h - h * s)
                slope_c[pl.ds(at, SIDE), lanes] = slope
                return a0 + h, a1 + slope, a2 + slope * hat

            zero = jnp.zeros((SIDE, 256), F32)
            a0, a1, a2 = lax.fori_loop(0, height, step, (zero, zero, zero), unroll=7)
            p_row = (t.fold(a0) * (1.0 / area)).astype(BF16).astype(F32)
            to_dense(pool, 0, p_row, 8 * k + 2 * c)
            to_dense(slope_sum, k, t.fold(a1), 2 * c)
            to_dense(slope_hat, k, t.fold(a2), 2 * c)
    for k in range(live):
        pool[0, 24 + k : 25 + k, :] = jnp.full((1, 128), key[k], F32)
        pool[0, 28 + k : 29 + k, :] = jnp.full((1, 128), weight[k], F32)
    for q, device in enumerate(t.clip_peers):
        t.send(pool.at[0], pool.at[q + 1], r.pool_s.at[0], r.pool_r.at[0], device)
    wait_bytes(pool.at[pl.ds(1, len(t.clip_peers))], r.pool_r.at[0])

    lw = dense_of(r.loss, r.dense)
    grads = []
    for k in range(live):
        my_key = jnp.full((1, 128), key[k], F32)
        my_weight = jnp.full((1, 128), weight[k], F32)
        mean = jnp.zeros((8, 128), F32)
        den = jnp.zeros((1, 128), F32)
        for q in range(len(t.clip_peers) + 1):
            for m in range(live):
                match = jnp.where(pool[q, 24 + m : 25 + m, :] == my_key, pool[q, 28 + m : 29 + m, :], 0.0)
                den = den + match
                mean = mean + match * pool[q, 8 * m : 8 * m + 8, :]
        den = jnp.where(den == 0.0, 1.0, den)
        mean = mean / den
        power = jnp.sum(jnp.sum(mean * mean, axis=0, keepdims=True), axis=1, keepdims=True)
        scale = lax.rsqrt(power * (1.0 / feat) + EPS)
        unit = mean * scale
        along = jnp.sum(jnp.sum(unit * lw, axis=0, keepdims=True), axis=1, keepdims=True)
        mean_grad = scale * (lw - unit * (along * (1.0 / feat)))
        grads.append((my_weight / den) * mean_grad * (1.0 / area))

    near3 = r.near[3]
    shift = jnp.zeros((8, 128), F32)
    gain = jnp.zeros((8, 128), F32)
    for k in range(live):
        shift = shift + grads[k] * slope_sum[k]
        gain = gain + grads[k] * slope_hat[k]
    near3[t.near_at(3), 0:8, :] = shift
    near3[t.near_at(3), 8:16, :] = gain
    t.near_send(3)
    coef, dense = r.coef, r.dense
    scale_c = dense_of(r.gc, dense) * inv_c
    for k in range(live):
        dense[...] = grads[k]
        row_form(coef, k, dense, 0, feat // 128)
        dense[...] = grads[k] * scale_c
        row_form(coef, 3 + k, dense, 0, feat // 128)
    t.sums_near(3)
    both = t.sums_wide(3)
    r.vectors_c[...] = both
    dense[...] = both[0:8] * scale_c / n_all
    row_form(coef, 6, dense, 0, feat // 128)
    dense[...] = both[8:16] * scale_c * inv_c / n_all
    row_form(coef, 7, dense, 0, feat // 128)
    return n_all, inv_a, inv_b


def backward(t, n_all, inv_a, inv_b):
    r, live, mid, feat, rows, height = t.r, t.live, t.mid, t.feat, t.rows, t.height
    slots, width, quad, far, v, wc = t.slots, t.width, t.quad, t.far, t.v, r.wc
    coef, pre_c, slope_c, out = r.coef, r.pre_c, r.slope_c, r.vectors
    me, send = t.me, t.send
    gpc = r.gpc
    for k in range(live):
        for c in range(feat // 256):
            lanes = slice(c * 256, (c + 1) * 256)
            centre = r.table_c[0:1, lanes]
            c0 = coef[3 + k : 4 + k, lanes]
            c1 = coef[6:7, lanes] * v[k]
            c2 = coef[7:8, lanes] * v[k]

            def step(y, carry):
                at = block(k, y)
                grad = slope_c[pl.ds(at, SIDE), lanes] * c0 - (c1 + (pre_c[pl.ds(at, SIDE), lanes] - centre) * c2)
                gpc[pl.ds(at, SIDE), lanes] = grad.astype(BF16)
                return carry

            lax.fori_loop(0, height, step, 0, unroll=7)

    def back_sums(at, table, inv, grad_ref, slope_ref, pre_ref):
        zero = jnp.zeros((SIDE, mid), F32)
        carry = (zero, zero)
        centre = table[0:1, :]
        for k in range(live):
            def step(y, c):
                here = pl.ds(block(k, y), SIDE)
                grad = grad_ref[here, :] * slope_ref[here, :]
                grad_ref[here, :] = grad
                return c[0] + grad, c[1] + grad * (pre_ref[here, :] - centre)

            carry = lax.fori_loop(0, height, step, carry, unroll=7)
        buf = r.near[at]
        to_dense(buf, t.near_at(at), jnp.sum(carry[0], axis=0, keepdims=True), 0)
        to_dense(buf, t.near_at(at), jnp.sum(carry[1], axis=0, keepdims=True) * table[1:2, :], 2)

    def back_apply(at, table, gain_ref, inv, grad_ref, pre_ref, write):
        both = t.sums_wide(at)
        out[8 * at - 32 : 8 * at - 28, :] = both[0:4]
        dense = r.dense
        scale = dense_of(gain_ref, dense) * inv
        dense[0:2, :] = scale
        dense[2:4, :] = both[0:2] * scale / n_all
        dense[4:6, :] = both[2:4] * scale * inv / n_all
        for q in range(3):
            row_form(table, 2 + q, dense, 2 * q, 2)
        centre = table[0:1, :]
        for k in range(live):
            c0, c1, c2 = table[2:3, :], table[3:4, :] * v[k], table[4:5, :] * v[k]

            def step(y, carry):
                at_row = block(k, y)
                here = pl.ds(at_row, SIDE)
                write(at_row, grad_ref[here, :] * c0 - (c1 + (pre_ref[here, :] - centre) * c2))
                return carry

            lax.fori_loop(0, height, step, 0, unroll=7)

    core, bit_x, bit_y, at_z = me % 2, (me // 2) % 2, (me // 4) % 2, (me // 8) % quad
    at_far = me // (8 * quad)
    bit1 = bit_x + core * (bit_y - bit_x)
    bit2 = bit_y + core * (bit_x - bit_y)
    sibling = me + 1 - 2 * core
    peer1 = me + (1 - 2 * bit1) * (2 + 2 * core)
    peer2 = me + (1 - 2 * bit2) * (4 - 2 * core)
    z_at = flips(at_z, quad)
    z_peer = [me + 8 * (q - at_z) for q in z_at]
    far_peer = [me + 8 * quad * ((at_far + o) % far - at_far) for o in range(1, far)]
    chunk_s, chunk_r = r.chunk_s, r.chunk_r
    blocks = iter(ORDER)
    plan = [(q, 0, 1) for q in range(4)] + [(4, q, 2) for q in range(2)]

    def chunk(q):
        name, at, count = plan[q]
        size = r.part[name].shape[0] // count
        part = r.part[name].at[pl.ds(at * size, size)]
        whole = (r.e, r.s0, r.s1, r.s2, r.r)[name].at[pl.ds(at * size, size)]
        half, quarter, eighth, piece = size // 2, size // 4, size // 8, size // (8 * quad)
        m8 = lambda value: pl.multiple_of(value, 8)
        at_h = m8(core * half)
        at_q = m8(at_h + bit1 * quarter)
        at_e = m8(at_q + bit2 * eighth)
        at_p = m8(at_e + at_z * piece)

        def go(step, src, dst, device):
            send(src, dst, chunk_s.at[q, step // 4], chunk_r.at[q, step], device)

        def finish(step, ref):
            wait_bytes(ref, chunk_r.at[q, step])

        rb0, rb1, rb2, rb3 = r.rb0[q], r.rb1[q], r.rb2[q], r.rb3[q]
        go(0, part.at[pl.ds(m8((1 - core) * half), half)], rb0, sibling)
        yield
        finish(0, rb0)
        part[pl.ds(at_h, half), :] = part[pl.ds(at_h, half), :] + rb0[...]
        go(1, part.at[pl.ds(m8(at_h + (1 - bit1) * quarter), quarter)], rb1, peer1)
        yield
        finish(1, rb1)
        part[pl.ds(at_q, quarter), :] = part[pl.ds(at_q, quarter), :] + rb1[...]
        go(2, part.at[pl.ds(m8(at_q + (1 - bit2) * eighth), eighth)], rb2, peer2)
        yield
        finish(2, rb2)
        part[pl.ds(at_e, eighth), :] = part[pl.ds(at_e, eighth), :] + rb2[...]
        for o in range(quad - 1):
            go(3, part.at[pl.ds(m8(at_e + z_at[o] * piece), piece)], rb3.at[pl.ds(o * piece, piece)], z_peer[o])
        yield
        finish(3, rb3)
        own = part[pl.ds(at_p, piece), :]
        for o in range(quad - 1):
            own = own + rb3[o * piece : (o + 1) * piece, :]
        if far > 1:
            rb4 = r.rb4[q]
            rb4[at_far] = own
            for device in far_peer:
                go(8, rb4.at[at_far], rb4.at[at_far], device)
            yield
            finish(8, rb4.at[pl.ds(0, far - 1)])
            own = rb4[0]
            for o in range(1, far):
                own = own + rb4[o]
        whole[pl.ds(at_p, piece), :] = own
        for o in range(quad - 1):
            go(4, whole.at[pl.ds(at_p, piece)], whole.at[pl.ds(at_p, piece)], z_peer[o])
        yield
        finish(4, whole.at[pl.ds(0, (quad - 1) * piece)])
        go(5, whole.at[pl.ds(at_e, eighth)], whole.at[pl.ds(at_e, eighth)], peer2)
        yield
        finish(5, whole.at[pl.ds(0, eighth)])
        go(6, whole.at[pl.ds(at_q, quarter)], whole.at[pl.ds(at_q, quarter)], peer1)
        yield
        finish(6, whole.at[pl.ds(0, quarter)])
        go(7, whole.at[pl.ds(at_h, half)], whole.at[pl.ds(at_h, half)], sibling)
        yield
        finish(7, whole.at[pl.ds(0, half)])
        yield

    chunks = [chunk(q) for q in range(len(plan))]

    def go_on(*which):
        for q in which:
            next(chunks[q])

    def go_on_all():
        go_on(*next(blocks))

    pre_a, slope_a, pre_b, slope_b, hbt, xt = r.pre_a, r.slope_a, r.pre_b, r.slope_b, r.hbt, r.xt
    we, wr, back = r.we, r.wr, r.back
    tiles = feat // 128
    group = SIDE // slots
    keep, moved, mask = t.keep, t.moved, t.mask
    grad_b, grad_a = r.grad_b, r.grad_a
    wait_bytes(wc, r.load_sem.at[15])
    g3 = r.g3

    def write_gb(at, grad):
        grad = jnp.where(mask, grad, 0.0)
        three(g3, at, pltpu.roll(grad, SIDE - 1, 0), grad, pltpu.roll(grad, 1, 0))

    def spatial_part(i):
        go_on_all()
        spread_lanes(r.part[1 + i], dot(xt[...], g3[(2 - i) * SIDE : (2 - i) * SIDE + rows, :]))
        go_on(1 + i)

    go_on_all()
    go_on_all()
    by_rows(grad_b, lambda here: dot(gpc[here, :], we[...], NT))
    back_sums(4, r.table_b, inv_b, grad_b, slope_b, pre_b)
    t.near_send(4)
    go_on_all()
    for q in range(feat // 256):
        lanes = slice(q * 256, (q + 1) * 256)
        spread_lanes(r.part[0].at[pl.ds(2 * mid * q, 2 * mid)], dot(hbt[...], gpc[:, lanes]))
    go_on(0)
    t.sums_near(4)
    go_on_all()
    back_apply(4, r.table_b, r.gb, inv_b, grad_b, pre_b, write_gb)
    spatial_part(0)
    go_on_all()
    by_rows(
        grad_a, lambda here: sum(dot(g3[moved_rows(here, (2 - i) * SIDE), :], wc[i], NT) for i in range(3))
    )
    back_sums(5, r.table_a, inv_a, grad_a, slope_a, pre_a)
    t.near_send(5)
    spatial_part(1)
    t.sums_near(5)
    spatial_part(2)
    go_on_all()
    gpa = r.gpa

    def write_ga(at, grad):
        gpa[pl.ds(at, SIDE), :] = grad.astype(BF16)

    back_apply(5, r.table_a, r.ga, inv_a, grad_a, pre_a, write_ga)
    for q in range(2):
        go_on_all()
        for m in range(2 * q, 2 * q + 2):
            spread_lanes(r.part[4].at[pl.ds(m * 512, 512)], dot(r.ft[m * 256 : (m + 1) * 256, :], gpa[...]))
        go_on(4 + q)

    go_on_all()
    by_rows(back, lambda here: dot(gpa[here, :], wr[...], NT))
    gf = r.gf

    def blend(y, carry):
        for p in range(tiles // group):
            values = []
            for q in range(group):
                lanes = slice((p * group + q) * 128, (p * group + q + 1) * 128)
                terms = [
                    slope_c[pl.ds(block(k, y), SIDE), lanes] * coef[k : k + 1, lanes]
                    + back[pl.ds(block(k, y), SIDE), lanes]
                    for k in range(live)
                ]
                values.append(terms[0] * keep[0])
                for m in range(1, live):
                    values.append(terms[m] * keep[m] + terms[m - 1] * moved[m - 1])
                values.append(terms[live - 1] * moved[live - 1])
            value = jnp.swapaxes(jnp.stack(values), 0, 1)
            gf[pl.ds(y * width, width), p * SIDE : (p + 1) * SIDE, :] = value[0:width].astype(BF16)
        return carry

    for q in range(height // 2):
        go_on_all()
        for y in range(2):
            blend(2 * q + y, 0)
    go_on_all()
    for each in chunks:
        for _ in each:
            pass

    t.all_sent(*range(6))
    wait_bytes(r.pool.at[pl.ds(1, len(t.clip_peers))], r.pool_s.at[0])
    for q, (name, _, count) in enumerate(plan):
        piece = r.part[name].shape[0] // count // (8 * quad)
        for m, pieces in enumerate((8 * quad - 1, 8 * quad - 1, far - 1)):
            if pieces:
                wait_bytes(r.part[0].at[pl.ds(0, pieces * piece)], chunk_s.at[q, m])


def store(gf, vectors_c, vectors, expand, s0, s1, s2, reduce, frames_out, reduce_out, spatial_out, expand_out, *rest):
    ga, ba, gb, bb, gc, bc, *scratch, sem = rest
    vectors_of = (
        (bc, vectors_c, 0), (gc, vectors_c, 8), (bb, vectors, 0), (gb, vectors, 2), (ba, vectors, 8), (ga, vectors, 10)
    )
    pltpu.make_async_copy(gf, frames_out, sem.at[0]).start()
    for number, (ref, source, first) in enumerate(vectors_of):
        for q in range(ref.shape[0] // 128):
            scratch[number][q * 128 : (q + 1) * 128] = source[first + q : first + q + 1, :].reshape(128)
        pltpu.make_async_copy(scratch[number], ref, sem.at[6 + number]).start()
    depth, width = reduce_out.shape
    for q in range(depth // 256):
        for m in range(width // 128):
            pltpu.make_async_copy(
                reduce.at[pl.ds((q * width // 128 + m) * 256, 256)],
                reduce_out.at[pl.ds(q * 256, 256), pl.ds(m * 128, 128)],
                sem.at[1],
            ).start()
    depth, width = expand_out.shape
    for q in range(width // 128):
        pltpu.make_async_copy(
            expand.at[pl.ds(q * depth, depth)], expand_out.at[:, pl.ds(q * 128, 128)], sem.at[2]
        ).start()
    for i, part in enumerate((s0, s1, s2)):
        for q in range(part.shape[0] // depth):
            pltpu.make_async_copy(
                part.at[pl.ds(q * depth, depth)],
                spatial_out.at[i, q * 128 // depth, :, pl.ds(q * 128 % depth, 128)],
                sem.at[3 + i],
            ).start()
    wait_bytes(gf, sem.at[0])
    wait_bytes(reduce, sem.at[1])
    wait_bytes(expand, sem.at[2])
    for i, part in enumerate((s0, s1, s2)):
        wait_bytes(part, sem.at[3 + i])
    for number in range(6):
        wait_bytes(scratch[number], sem.at[6 + number])


def solution(mesh):
    n = mesh.shape["clip"]

    def shards(*args):
        slots, height, width, feat = args[0].shape
        mid = args[1].shape[1]
        rows = (slots - 1) * ROWS
        outer = n // 8
        quad = min(4, outer)
        far = outer // quad
        cfg = (n, slots, height, width, feat, mid)
        flat_shape = (height * width, slots * feat // 128, 128)
        hbm = pl.BlockSpec(memory_space=pltpu.HBM)
        vmem = pl.BlockSpec(memory_space=pltpu.VMEM)
        dma = pltpu.SemaphoreType.DMA
        depths = list(enumerate((8, 4, 16, 16, 4, 4)))
        matrix, third = mid * feat // 128, 3 * mid * mid // 128
        sizes = [matrix, third, third, third, matrix]

        tiled = args[0].transpose(1, 2, 0, 3).reshape(height, width, slots, feat // 128, 128)
        tiled = tiled.transpose(0, 1, 3, 2, 4).reshape(flat_shape)
        given = [pltpu.with_memory_space_constraint(part, pltpu.HBM) for part in (tiled, *args[1:])]

        vm = pltpu.VMEM
        narrow, broad, square = vm((mid,), F32), vm((feat,), F32), vm((rows, mid), F32)
        ints = pltpu.SMEM((slots,), jnp.int32)
        plan = [matrix] + [third] * 3 + [matrix // 2] * 2
        outs = dict(
            gf=vm(flat_shape, BF16), vectors_c=vm((16, 128), F32), vectors=vm((16, 128), F32),
            e=vm((matrix, 128), F32), s0=vm((third, 128), F32), s1=vm((third, 128), F32), s2=vm((third, 128), F32),
            r=vm((matrix, 128), F32),
        )
        scratch = dict(
            f4=vm((flat_shape[0] + SIDE - width, *flat_shape[1:]), BF16),
            fp=vm((rows, feat), BF16), ft=vm((feat, rows), BF16),
            wr=vm((feat, mid), BF16), ws=vm((3, 3, mid, mid), BF16), wc=vm((3, mid, 3 * mid), BF16), we=vm((mid, feat), BF16),
            valid=ints, clip=ints, segment=ints, share=pltpu.SMEM(args[13].shape, F32),
            ga=narrow, ba=narrow, gb=narrow, bb=narrow, gc=broad, bc=broad, loss=broad,
            xp=vm((rows + 2 * SIDE, 3 * mid), BF16), xt=vm((mid, rows), BF16),
            hb=vm((rows, mid), BF16), hbt=vm((mid, rows), BF16),
            pre_a=square, slope_a=square, pre_b=square, slope_b=square, grad_a=square, grad_b=square,
            pre_c=vm((rows, feat), F32), slope_c=vm((rows, feat), F32), back=vm((rows, feat), F32),
            gpc=vm((rows, feat), BF16), g3=vm((rows + 2 * SIDE, 3 * mid), BF16), gpa=vm((rows, mid), BF16),
            table_a=vm((8, mid), F32), table_b=vm((8, mid), F32),
            table_c=vm((8, feat), F32), coef=vm((8, feat), F32), dense=vm((8, 128), F32),
            pool=vm((6, 32, 128), F32), slope_sum=vm((3, 8, 128), F32), slope_hat=vm((3, 8, 128), F32),
            near=[vm((n if n <= 32 and at not in (2, 3) else 8, deep, 128), F32) for at, deep in depths],
            wide=[vm((outer, deep, 128), F32) for at, deep in depths],
            plane=vm((outer, 8, 128), F32),
            part=[vm((size, 128), F32) for size in sizes],
            rb0=[vm((size // 2, 128), F32) for size in plan],
            rb1=[vm((size // 4, 128), F32) for size in plan],
            rb2=[vm((size // 8, 128), F32) for size in plan],
            rb3=[vm(((quad - 1) * size // (8 * quad), 128), F32) for size in plan],
            rb4=[vm((far, size // (8 * quad), 128), F32) for size in plan if far > 1],
            load_sem=dma((16,)), near_s=dma((6,)), near_r=dma((6,)), wide_s=dma((6,)), wide_r=dma((6,)),
            pool_s=dma((1,)), pool_r=dma((1,)), chunk_s=dma((6, 3)), chunk_r=dma((6, 9)),
        )
        names = (*arg_names(), *outs, *scratch)

        def kernel(*refs):
            t = Step(cfg, SimpleNamespace(**dict(zip(names, refs, strict=True))))
            prologue(t)
            backward(t, *forward(t))

        results = pl.pallas_call(
            kernel,
            out_shape=list(outs.values()),
            in_specs=[hbm] * len(given),
            out_specs=[vmem] * len(outs),
            scratch_shapes=list(scratch.values()),
            compiler_params=pltpu.CompilerParams(
                collective_id=0, has_side_effects=True, vmem_limit_bytes=50 * 1024 * 1024
            ),
        )(*given)
        vector = jax.ShapeDtypeStruct((mid,), F32)
        wide_vector = jax.ShapeDtypeStruct((feat,), F32)
        flat_grad, *rest = pl.pallas_call(
            store,
            out_shape=[
                jax.ShapeDtypeStruct(flat_shape, BF16),
                jax.ShapeDtypeStruct((feat, mid), F32),
                jax.ShapeDtypeStruct((3, 3, mid, mid), F32),
                jax.ShapeDtypeStruct((mid, feat), F32),
                vector, vector, vector, vector, wide_vector, wide_vector,
            ],
            in_specs=[vmem] * 8,
            out_specs=[hbm] * 10,
            scratch_shapes=[*(vm((c,), F32) for c in (feat, feat, mid, mid, mid, mid)), dma((12,))],
            compiler_params=pltpu.CompilerParams(vmem_limit_bytes=8 * 1024 * 1024),
        )(*(pltpu.with_memory_space_constraint(part, pltpu.VMEM) for part in results))
        grad_frames = flat_grad.reshape(height, width, feat // 128, slots, 128).transpose(0, 1, 3, 2, 4)
        return grad_frames.reshape(height, width, slots, feat).transpose(2, 0, 1, 3), *rest

    split = P("clip")
    in_specs = (split,) + (P(),) * 9 + (split,) * 3 + (P(), P())
    out_specs = (split,) + (P(),) * 9
    return jax.shard_map(shards, mesh=mesh, in_specs=in_specs, out_specs=out_specs, check_vma=False)


def arg_names():
    return dict(
        frames=0, w_reduce=0, w_spatial=0, w_expand=0, gain_a=0, bias_a=0, gain_b=0, bias_b=0, gain_c=0, bias_c=0,
        clip_ids=0, segment_ids=0, slot_valid=0, segment_weight=0, loss_weight=0,
    )
```

```python
import functools
from types import SimpleNamespace

import jax
import jax.numpy as jnp
from jax import lax
from jax.experimental import pallas as pl
from jax.experimental.pallas import tpu as pltpu
from jax.sharding import PartitionSpec as P

MESH = pl.DeviceIdType.MESH
EPS = 1e-05
F32 = jnp.float32
BF16 = jnp.bfloat16
SIDE = 16
ROWS = SIDE * SIDE
NN = (((1,), (0,)), ((), ()))
NT = (((1,), (1,)), ((), ()))

ORDER = (
    (),
    (),
    (),
    (),
    (),
    (),
    (0, 1,),
    (2, 0,),
    (1,),
    (2, 0, 1, 3,),
    (2, 4,),
    (),
    (),
    (0,),
    (1, 3, 5, 2, 4,),
    (6, 3, 8,),
    (1, 0, 5, 7, 4, 8, 1, 3, 6, 7, 8, 2, 0,),
    (4, 7, 3,),
    (6, 2, 8, 1, 5, 0, 4, 7, 3, 6, 8, 5, 7, 1, 6, 4,),
    (5, 6, 0, 3,),
    (7,),
    (8, 2, 4, 5, 7, 8, 6, 3, 5,),
    (7, 8, 6, 5, 4, 2,),
)


def dot(a, b, dims=NN):
    return lax.dot_general(a, b, dims, preferred_element_type=F32)


def wait_bytes(ref, sem):
    pltpu.make_async_copy(ref, ref, sem).wait()


def spread_lanes(ref, value):
    depth = value.shape[0]
    for q in range(value.shape[1] // 128):
        ref[q * depth : (q + 1) * depth, :] = value[:, q * 128 : (q + 1) * 128]


def by_rows(ref, value):
    for k in range(ref.shape[0] // 256):
        ref[k * 256 : (k + 1) * 256, :] = value(slice(k * 256, (k + 1) * 256))


def moved_rows(here, at):
    return slice(here.start + at, here.stop + at)


def block(k, y):
    return pl.multiple_of(k * ROWS + y * SIDE, SIDE)


def to_dense(ref, at, value, first):
    for q in range(value.shape[1] // 128):
        ref[at, pl.ds(first + q, 1), :] = value[:, q * 128 : (q + 1) * 128]


def row_form(ref, row, source, first, count):
    for q in range(count):
        ref[row : row + 1, q * 128 : (q + 1) * 128] = source[first + q : first + q + 1, :]


def three(ref, at, left, middle, right):
    here, wide = pl.ds(at + SIDE, SIDE), middle.shape[1]
    ref[here, 0:wide] = left.astype(BF16)
    ref[here, wide : 2 * wide] = middle.astype(BF16)
    ref[here, 2 * wide : 3 * wide] = right.astype(BF16)


def dense_of(ref1, scratch):
    count = ref1.shape[0] // 128
    for q in range(count):
        scratch[q : q + 1, :] = ref1[q * 128 : (q + 1) * 128].reshape(1, 128)
    return scratch[0:count, :]


class Step:
    def __init__(self, cfg, r):
        self.r, self.sizes = r, cfg
        self.n, self.slots, self.height, self.width, self.feat, self.mid = cfg
        self.live = self.slots - 1
        self.rows = self.live * ROWS
        self.area = self.height * self.width
        self.inner = 8
        self.outer = self.n // 8
        self.quad = min(4, self.outer)
        self.far = self.outer // self.quad
        self.loads = {}
        self.mask = lax.broadcasted_iota(jnp.int32, (SIDE, 256), 0) < self.width

    def load(self, **pairs):
        for name, (src, dst) in pairs.items():
            copy = pltpu.make_async_copy(src, dst, self.r.load_sem.at[len(self.loads)])
            copy.start()
            self.loads[name] = copy

    def loaded(self, **names):
        for name in names:
            self.loads[name].wait()

    def fold(self, value):
        return jnp.sum(jnp.where(self.mask, value, 0.0), axis=0, keepdims=True)

    def slot_facts(self):
        r, live = self.r, self.live
        alive, later = 1, []
        for k in range(live):
            alive = alive * r.valid[k]
            later.append(1 - alive)
        self.keep = [(1 - q).astype(F32) for q in later]
        self.moved = [q.astype(F32) for q in later]
        self.later = later
        self.v = [self.kept(r.valid, k) for k in range(live)]
        self.n_own = (self.v[0] + self.v[1] + self.v[2]) * float(self.area)

    def kept(self, values, k):
        return (values[k] + self.later[k] * (values[k + 1] - values[k])).astype(F32)

    def places(self):
        n = self.n
        self.me = me = lax.axis_index("clip")
        self.low, self.high = low, high = me % self.inner, me // self.inner
        self.direct = n <= 32
        self.peers = flips(me, n)
        self.low_peers = flips(me, self.inner)
        self.high_peers = flips(me, self.outer, self.inner)
        self.clip_peers = [(me + o) % n for o in (n // 2 - 1, n // 2 + 1, n // 2, n - 1, 1)]

    def greet(self):
        self.greeted = self.peers if self.direct else self.low_peers + self.high_peers + self.clip_peers
        self.barrier = pltpu.get_barrier_semaphore()
        for device in self.greeted:
            pl.semaphore_signal(self.barrier, inc=1, device_id=(device,), device_id_type=MESH)

    def all_here(self):
        pl.semaphore_wait(self.barrier, len(self.greeted))

    def send(self, src, dst, ssem, rsem, device):
        pltpu.make_async_remote_copy(
            src_ref=src, dst_ref=dst, send_sem=ssem, recv_sem=rsem, device_id=(device,), device_id_type=MESH
        ).start()

    def one_stage(self, at):
        return self.direct and at not in (2, 3)

    def near_at(self, at):
        return self.me if self.one_stage(at) else self.low

    def near_send(self, at):
        buf, mine = self.r.near[at], self.near_at(at)
        for device in self.peers if self.one_stage(at) else self.low_peers:
            self.send(buf.at[mine], buf.at[mine], self.r.near_s.at[at], self.r.near_r.at[at], device)

    def near_wait(self, at, sems):
        buf = self.r.near[at]
        wait_bytes(buf.at[pl.ds(0, buf.shape[0] - 1)], sems.at[at])

    def wide_send(self, at):
        buf = self.r.wide[at]
        for device in self.high_peers:
            self.send(buf.at[self.high], buf.at[self.high], self.r.wide_s.at[at], self.r.wide_r.at[at], device)

    def wide_wait(self, at, sems):
        wait_bytes(self.r.wide[at].at[pl.ds(0, self.outer - 1)], sems.at[at])

    def all_sent(self, *rounds):
        for at in rounds:
            self.near_wait(at, self.r.near_s)
            if not self.one_stage(at):
                self.wide_wait(at, self.r.wide_s)

    def near_count(self, q):
        return self.r.near[0][(self.me - self.low + q) if self.direct else q, 4:5, :]

    def wide_count(self, q):
        return self.r.plane[q, 0:1, :] if self.direct else self.r.wide[0][q, 4:5, :]

    def stats_near(self, at, count):
        if self.one_stage(at):
            return
        self.near_wait(at, self.r.near_r)
        n_all, s_all, _, spread = combine(self.r.near[at], self.near_count, self.inner, count)
        buf = self.r.wide[at]
        buf[self.high, 0:count, :] = s_all
        buf[self.high, count : 2 * count, :] = spread
        if at == 0:
            buf[self.high, 4:5, :] = n_all
        self.wide_send(at)

    def stats_wide(self, at, count, table):
        r = self.r
        if self.one_stage(at):
            self.near_wait(at, r.near_r)
            counts = r.near[0]
            n_all, _, mean, spread = combine(r.near[at], lambda q: counts[q, 4:5, :], self.n, count)
            if at == 0:
                for q in range(self.outer):
                    r.plane[q, 0:1, :] = sum(counts[q * self.inner + m, 4:5, :] for m in range(self.inner))
        else:
            self.wide_wait(at, r.wide_r)
            n_all, _, mean, spread = combine(r.wide[at], self.wide_count, self.outer, count)
        inverse = lax.rsqrt(spread / n_all + EPS)
        r.dense[0:count, :] = mean
        row_form(table, 0, r.dense, 0, count)
        r.dense[0:count, :] = inverse
        row_form(table, 1, r.dense, 0, count)
        return n_all, inverse

    def sums_near(self, at):
        if not self.one_stage(at):
            self.near_wait(at, self.r.near_r)
            self.r.wide[at][self.high] = total(self.r.near[at])
            self.wide_send(at)

    def sums_wide(self, at):
        if self.one_stage(at):
            self.near_wait(at, self.r.near_r)
            return total(self.r.near[at])
        self.wide_wait(at, self.r.wide_r)
        return total(self.r.wide[at])

    def local_stats(self, buf, at, ref):
        channels = ref.shape[1]
        count = channels // 128
        for c in range(channels // 256):
            lanes = slice(c * 256, (c + 1) * 256)

            def gather(term):
                acc = jnp.zeros((SIDE, 256), F32)
                for k in range(self.live):
                    part = lax.fori_loop(
                        0, self.height, lambda y, a: a + term(ref[pl.ds(block(k, y), SIDE), lanes]),
                        jnp.zeros((SIDE, 256), F32), unroll=self.height,
                    )
                    acc = acc + part * self.v[k]
                return self.fold(acc)

            s_own = gather(lambda x: x)
            mean = s_own / jnp.maximum(self.n_own, 1.0)
            to_dense(buf, at, s_own, 2 * c)
            to_dense(buf, at, gather(lambda x: (x - mean) * (x - mean)), count + 2 * c)

    def norm_silu(self, ref, slope_ref, table, gain, bias, write):
        centre, scale = table[0:1, :], table[1:2, :] * gain[...].reshape(1, self.mid)
        b = bias[...].reshape(1, self.mid)
        for k in range(self.live):
            def step(y, carry):
                at = block(k, y)
                u = (ref[pl.ds(at, SIDE), :] - centre) * scale + b
                s = 0.5 * jnp.tanh(0.5 * u) + 0.5
                h = u * s
                slope_ref[pl.ds(at, SIDE), :] = jnp.where(self.mask, s + (h - h * s), 0.0)
                write(at, jnp.where(self.mask, h, 0.0))
                return carry

            lax.fori_loop(0, self.height, step, 0, unroll=14)


def flips(index, count, stride=1):
    steps, at = [], 1
    while at < count:
        steps.append(at * stride * (1 - 2 * ((index // (at * stride)) % 2)))
        at *= 2
    return [sum((d for b, d in enumerate(steps) if o >> b & 1), index) for o in reversed(range(1, count))]


def combine(buf, counts, group, count):
    n_part = [counts(q) for q in range(group)]
    s_part = [buf[q, 0:count, :] for q in range(group)]
    n_all = sum(n_part[1:], n_part[0])
    s_all = sum(s_part[1:], s_part[0])
    mean = s_all / jnp.maximum(n_all, 1.0)
    spread = jnp.zeros((count, 128), F32)
    for q in range(group):
        gap = s_part[q] / jnp.maximum(n_part[q], 1.0) - mean
        spread = spread + (buf[q, count : 2 * count, :] + n_part[q] * gap * gap)
    return n_all, s_all, mean, spread


def total(buf):
    out = buf[0]
    for q in range(1, buf.shape[0]):
        out = out + buf[q]
    return out


def clear(*refs):
    for ref in refs:
        ref[...] = jnp.zeros(ref.shape, ref.dtype)


def prologue(t):
    r, slots, live, width, feat = t.r, t.slots, t.live, t.width, t.feat
    t.places()
    t.greet()
    t.load(
        frames=(r.frames, r.f4.at[pl.ds(0, t.area)]), valid=(r.slot_valid, r.valid), reduce=(r.w_reduce, r.wr),
        clip=(r.clip_ids, r.clip), segment=(r.segment_ids, r.segment),
        share=(r.segment_weight, r.share), spatial=(r.w_spatial, r.ws), expand=(r.w_expand, r.we),
        ga=(r.gain_a, r.ga), ba=(r.bias_a, r.ba), gb=(r.gain_b, r.gb), bb=(r.bias_b, r.bb),
        gc=(r.gain_c, r.gc), bc=(r.bias_c, r.bc), loss=(r.loss_weight, r.loss),
    )
    for i in range(3):
        for j in range(3):
            pltpu.make_async_copy(
                r.w_spatial.at[i, j], r.wc.at[i, :, pl.ds(j * t.mid, t.mid)], r.load_sem.at[15]
            ).start()
    r.f4[t.area :] = jnp.zeros((r.f4.shape[0] - t.area, *r.f4.shape[1:]), BF16)
    clear(r.fp)
    t.loaded(valid=0)
    t.slot_facts()
    t.loaded(frames=0)
    fp, f4 = r.fp, r.f4
    tiles = feat // 128
    group = SIDE // slots
    short = lax.broadcasted_iota(jnp.int32, (SIDE, 128), 0) < width

    def regroup(y, carry):
        for p in range(tiles // group):
            value = f4[pl.ds(y * width, SIDE), p * SIDE : (p + 1) * SIDE, :].astype(F32)
            value = jnp.swapaxes(value, 0, 1)
            for q in range(group):
                for k in range(live):
                    row = value[q * slots + k] * t.keep[k] + value[q * slots + k + 1] * t.moved[k]
                    lanes = slice((p * group + q) * 128, (p * group + q + 1) * 128)
                    fp[pl.ds(block(k, y), SIDE), lanes] = jnp.where(short, row, 0.0).astype(BF16)
        return carry

    lax.fori_loop(0, t.height, regroup, 0)
    t.loaded(reduce=0)
    by_rows(r.pre_a, lambda here: dot(fp[here, :], r.wr[...]))
    t.local_stats(r.near[0], t.near_at(0), r.pre_a)
    r.near[0][t.near_at(0), 4:5, :] = jnp.full((1, 128), t.n_own, F32)


def forward(t):
    r, live, mid, feat, rows, area, height = t.r, t.live, t.mid, t.feat, t.rows, t.area, t.height
    t.all_here()
    t.near_send(0)
    r.ft[...] = r.fp[...].T
    t.stats_near(0, mid // 128)
    clear(r.xp, r.hb, r.g3, r.gpc, r.gpa)
    t.loaded(clip=0, segment=0, share=0, ga=0, ba=0, gb=0, bb=0, gc=0, bc=0, loss=0, spatial=0, expand=0)
    key = [t.kept(r.clip, k) for k in range(live)]
    weight = []
    for k in range(live):
        at = t.kept(r.segment, k)
        w0, w1, w2 = (r.share[q] for q in range(3))
        weight.append(
            t.v[k] * (w0 * ((1.0 - at) * (2.0 - at) * 0.5) + w1 * (at * (2.0 - at)) + w2 * (at * (at - 1.0) * 0.5))
        )
    n_all, inv_a = t.stats_wide(0, mid // 128, r.table_a)

    xp, hb = r.xp, r.hb

    def write_a(at, h):
        three(xp, at, pltpu.roll(h, 1, 0), h, pltpu.roll(h, SIDE - 1, 0))

    t.norm_silu(r.pre_a, r.slope_a, r.table_a, r.ga, r.ba, write_a)

    by_rows(
        r.pre_b,
        lambda here: sum(dot(xp[moved_rows(here, i * SIDE), :], r.ws[i].reshape(3 * mid, mid)) for i in range(3)),
    )
    t.local_stats(r.near[1], t.near_at(1), r.pre_b)
    t.near_send(1)
    r.xt[...] = xp[SIDE : SIDE + rows, mid : 2 * mid].T
    t.stats_near(1, mid // 128)
    _, inv_b = t.stats_wide(1, mid // 128, r.table_b)

    def write_b(at, h):
        hb[pl.ds(at, SIDE), :] = h.astype(BF16)

    t.norm_silu(r.pre_b, r.slope_b, r.table_b, r.gb, r.bb, write_b)

    pre_c, slope_c, fp, table_c = r.pre_c, r.slope_c, r.fp, r.table_c
    by_rows(pre_c, lambda here: dot(hb[here, :], r.we[...]))
    t.local_stats(r.near[2], t.near_at(2), pre_c)
    t.near_send(2)
    r.hbt[...] = hb[...].T
    t.stats_near(2, feat // 128)
    _, inv_c = t.stats_wide(2, feat // 128, table_c)

    pool, slope_sum, slope_hat = r.pool, r.slope_sum, r.slope_hat
    for c in range(feat // 256):
        lanes = slice(c * 256, (c + 1) * 256)
        centre, inverse = table_c[0:1, lanes], table_c[1:2, lanes]
        g = r.gc[lanes].reshape(1, 256)
        b = r.bc[lanes].reshape(1, 256)
        for k in range(live):
            def step(y, carry):
                a0, a1, a2 = carry
                at = block(k, y)
                hat = (pre_c[pl.ds(at, SIDE), lanes] - centre) * inverse
                u = hat * g + b + fp[pl.ds(at, SIDE), lanes].astype(F32)
                s = 0.5 * jnp.tanh(0.5 * u) + 0.5
                h = u * s
                slope = s + (h - h * s)
                slope_c[pl.ds(at, SIDE), lanes] = slope
                return a0 + h, a1 + slope, a2 + slope * hat

            zero = jnp.zeros((SIDE, 256), F32)
            a0, a1, a2 = lax.fori_loop(0, height, step, (zero, zero, zero), unroll=14)
            p_row = (t.fold(a0) * (1.0 / area)).astype(BF16).astype(F32)
            to_dense(pool, 0, p_row, 8 * k + 2 * c)
            to_dense(slope_sum, k, t.fold(a1), 2 * c)
            to_dense(slope_hat, k, t.fold(a2), 2 * c)
    for k in range(live):
        pool[0, 24 + k : 25 + k, :] = jnp.full((1, 128), key[k], F32)
        pool[0, 28 + k : 29 + k, :] = jnp.full((1, 128), weight[k], F32)
    for q, device in enumerate(t.clip_peers):
        t.send(pool.at[0], pool.at[q + 1], r.pool_s.at[0], r.pool_r.at[0], device)
    wait_bytes(pool.at[pl.ds(1, len(t.clip_peers))], r.pool_r.at[0])

    lw = dense_of(r.loss, r.dense)
    grads = []
    for k in range(live):
        my_key = jnp.full((1, 128), key[k], F32)
        my_weight = jnp.full((1, 128), weight[k], F32)
        mean = jnp.zeros((8, 128), F32)
        den = jnp.zeros((1, 128), F32)
        for q in range(len(t.clip_peers) + 1):
            for m in range(live):
                match = jnp.where(pool[q, 24 + m : 25 + m, :] == my_key, pool[q, 28 + m : 29 + m, :], 0.0)
                den = den + match
                mean = mean + match * pool[q, 8 * m : 8 * m + 8, :]
        den = jnp.where(den == 0.0, 1.0, den)
        mean = mean / den
        power = jnp.sum(jnp.sum(mean * mean, axis=0, keepdims=True), axis=1, keepdims=True)
        scale = lax.rsqrt(power * (1.0 / feat) + EPS)
        unit = mean * scale
        along = jnp.sum(jnp.sum(unit * lw, axis=0, keepdims=True), axis=1, keepdims=True)
        mean_grad = scale * (lw - unit * (along * (1.0 / feat)))
        grads.append((my_weight / den) * mean_grad * (1.0 / area))

    near3 = r.near[3]
    shift = jnp.zeros((8, 128), F32)
    gain = jnp.zeros((8, 128), F32)
    for k in range(live):
        shift = shift + grads[k] * slope_sum[k]
        gain = gain + grads[k] * slope_hat[k]
    near3[t.near_at(3), 0:8, :] = shift
    near3[t.near_at(3), 8:16, :] = gain
    t.near_send(3)
    coef, dense = r.coef, r.dense
    scale_c = dense_of(r.gc, dense) * inv_c
    for k in range(live):
        dense[...] = grads[k]
        row_form(coef, k, dense, 0, feat // 128)
        dense[...] = grads[k] * scale_c
        row_form(coef, 3 + k, dense, 0, feat // 128)
    t.sums_near(3)
    both = t.sums_wide(3)
    r.vectors_c[...] = both
    dense[...] = both[0:8] * scale_c / n_all
    row_form(coef, 6, dense, 0, feat // 128)
    dense[...] = both[8:16] * scale_c * inv_c / n_all
    row_form(coef, 7, dense, 0, feat // 128)
    return n_all, inv_a, inv_b


def backward(t, n_all, inv_a, inv_b):
    r, live, mid, feat, rows, height = t.r, t.live, t.mid, t.feat, t.rows, t.height
    slots, width, quad, far, v, wc = t.slots, t.width, t.quad, t.far, t.v, r.wc
    coef, pre_c, slope_c, out = r.coef, r.pre_c, r.slope_c, r.vectors
    me, send = t.me, t.send
    gpc = r.gpc
    for k in range(live):
        for c in range(feat // 256):
            lanes = slice(c * 256, (c + 1) * 256)
            centre = r.table_c[0:1, lanes]
            c0 = coef[3 + k : 4 + k, lanes]
            c1 = coef[6:7, lanes] * v[k]
            c2 = coef[7:8, lanes] * v[k]

            def step(y, carry):
                at = block(k, y)
                grad = slope_c[pl.ds(at, SIDE), lanes] * c0 - (c1 + (pre_c[pl.ds(at, SIDE), lanes] - centre) * c2)
                gpc[pl.ds(at, SIDE), lanes] = grad.astype(BF16)
                return carry

            lax.fori_loop(0, height, step, 0, unroll=14)

    def back_sums(at, table, inv, grad_ref, slope_ref, pre_ref):
        zero = jnp.zeros((SIDE, mid), F32)
        carry = (zero, zero)
        centre = table[0:1, :]
        for k in range(live):
            def step(y, c):
                here = pl.ds(block(k, y), SIDE)
                grad = grad_ref[here, :] * slope_ref[here, :]
                grad_ref[here, :] = grad
                return c[0] + grad, c[1] + grad * (pre_ref[here, :] - centre)

            carry = lax.fori_loop(0, height, step, carry, unroll=14)
        buf = r.near[at]
        to_dense(buf, t.near_at(at), jnp.sum(carry[0], axis=0, keepdims=True), 0)
        to_dense(buf, t.near_at(at), jnp.sum(carry[1], axis=0, keepdims=True) * table[1:2, :], 2)

    def back_apply(at, table, gain_ref, inv, grad_ref, pre_ref, write):
        both = t.sums_wide(at)
        out[8 * at - 32 : 8 * at - 28, :] = both[0:4]
        dense = r.dense
        scale = dense_of(gain_ref, dense) * inv
        dense[0:2, :] = scale
        dense[2:4, :] = both[0:2] * scale / n_all
        dense[4:6, :] = both[2:4] * scale * inv / n_all
        for q in range(3):
            row_form(table, 2 + q, dense, 2 * q, 2)
        centre = table[0:1, :]
        for k in range(live):
            c0, c1, c2 = table[2:3, :], table[3:4, :] * v[k], table[4:5, :] * v[k]

            def step(y, carry):
                at_row = block(k, y)
                here = pl.ds(at_row, SIDE)
                write(at_row, grad_ref[here, :] * c0 - (c1 + (pre_ref[here, :] - centre) * c2))
                return carry

            lax.fori_loop(0, height, step, 0, unroll=14)

    core, bit_x, bit_y, at_z = me % 2, (me // 2) % 2, (me // 4) % 2, (me // 8) % quad
    at_far = me // (8 * quad)
    bit1 = bit_x + core * (bit_y - bit_x)
    bit2 = bit_y + core * (bit_x - bit_y)
    sibling = me + 1 - 2 * core
    peer1 = me + (1 - 2 * bit1) * (2 + 2 * core)
    peer2 = me + (1 - 2 * bit2) * (4 - 2 * core)
    z_at = flips(at_z, quad)
    z_peer = [me + 8 * (q - at_z) for q in z_at]
    far_peer = [me + 8 * quad * ((at_far + o) % far - at_far) for o in range(1, far)]
    chunk_s, chunk_r = r.chunk_s, r.chunk_r
    blocks = iter(ORDER)
    plan = [(0, q, 2) for q in range(2)] + [(1 + q, 0, 1) for q in range(3)] + [(4, q, 4) for q in range(4)]

    def chunk(q):
        name, at, count = plan[q]
        size = r.part[name].shape[0] // count
        part = r.part[name].at[pl.ds(at * size, size)]
        whole = (r.e, r.s0, r.s1, r.s2, r.r)[name].at[pl.ds(at * size, size)]
        half, quarter, eighth, piece = size // 2, size // 4, size // 8, size // (8 * quad)
        m8 = lambda value: pl.multiple_of(value, 8)
        at_h = m8(core * half)
        at_q = m8(at_h + bit1 * quarter)
        at_e = m8(at_q + bit2 * eighth)
        at_p = m8(at_e + at_z * piece)

        def go(step, src, dst, device):
            send(src, dst, chunk_s.at[q, step // 4], chunk_r.at[q, step], device)

        def finish(step, ref):
            wait_bytes(ref, chunk_r.at[q, step])

        rb0, rb1, rb2, rb3 = r.rb0[q], r.rb1[q], r.rb2[q], r.rb3[q]
        go(0, part.at[pl.ds(m8((1 - core) * half), half)], rb0, sibling)
        yield
        finish(0, rb0)
        part[pl.ds(at_h, half), :] = part[pl.ds(at_h, half), :] + rb0[...]
        go(1, part.at[pl.ds(m8(at_h + (1 - bit1) * quarter), quarter)], rb1, peer1)
        yield
        finish(1, rb1)
        part[pl.ds(at_q, quarter), :] = part[pl.ds(at_q, quarter), :] + rb1[...]
        go(2, part.at[pl.ds(m8(at_q + (1 - bit2) * eighth), eighth)], rb2, peer2)
        yield
        finish(2, rb2)
        part[pl.ds(at_e, eighth), :] = part[pl.ds(at_e, eighth), :] + rb2[...]
        for o in range(quad - 1):
            go(3, part.at[pl.ds(m8(at_e + z_at[o] * piece), piece)], rb3.at[pl.ds(o * piece, piece)], z_peer[o])
        yield
        finish(3, rb3)
        own = part[pl.ds(at_p, piece), :]
        for o in range(quad - 1):
            own = own + rb3[o * piece : (o + 1) * piece, :]
        if far > 1:
            rb4 = r.rb4[q]
            rb4[at_far] = own
            for device in far_peer:
                go(8, rb4.at[at_far], rb4.at[at_far], device)
            yield
            finish(8, rb4.at[pl.ds(0, far - 1)])
            own = rb4[0]
            for o in range(1, far):
                own = own + rb4[o]
        whole[pl.ds(at_p, piece), :] = own
        for o in range(quad - 1):
            go(4, whole.at[pl.ds(at_p, piece)], whole.at[pl.ds(at_p, piece)], z_peer[o])
        yield
        finish(4, whole.at[pl.ds(0, (quad - 1) * piece)])
        go(5, whole.at[pl.ds(at_e, eighth)], whole.at[pl.ds(at_e, eighth)], peer2)
        yield
        finish(5, whole.at[pl.ds(0, eighth)])
        go(6, whole.at[pl.ds(at_q, quarter)], whole.at[pl.ds(at_q, quarter)], peer1)
        yield
        finish(6, whole.at[pl.ds(0, quarter)])
        go(7, whole.at[pl.ds(at_h, half)], whole.at[pl.ds(at_h, half)], sibling)
        yield
        finish(7, whole.at[pl.ds(0, half)])
        yield

    chunks = [chunk(q) for q in range(len(plan))]

    def go_on(*which):
        for q in which:
            next(chunks[q])

    def go_on_all():
        go_on(*next(blocks))

    pre_a, slope_a, pre_b, slope_b, hbt, xt = r.pre_a, r.slope_a, r.pre_b, r.slope_b, r.hbt, r.xt
    we, wr, back = r.we, r.wr, r.back
    tiles = feat // 128
    group = SIDE // slots
    keep, moved, mask = t.keep, t.moved, t.mask
    grad_b, grad_a = r.grad_b, r.grad_a
    wait_bytes(wc, r.load_sem.at[15])
    g3 = r.g3

    def write_gb(at, grad):
        grad = jnp.where(mask, grad, 0.0)
        three(g3, at, pltpu.roll(grad, SIDE - 1, 0), grad, pltpu.roll(grad, 1, 0))

    def spatial_part(i):
        go_on_all()
        spread_lanes(r.part[1 + i], dot(xt[...], g3[(2 - i) * SIDE : (2 - i) * SIDE + rows, :]))
        go_on(2 + i)

    go_on_all()
    go_on_all()
    by_rows(grad_b, lambda here: dot(gpc[here, :], we[...], NT))
    back_sums(4, r.table_b, inv_b, grad_b, slope_b, pre_b)
    t.near_send(4)
    for e in range(2):
        go_on_all()
        for q in range(2 * e, 2 * e + 2):
            lanes = slice(q * 256, (q + 1) * 256)
            spread_lanes(r.part[0].at[pl.ds(2 * mid * q, 2 * mid)], dot(hbt[...], gpc[:, lanes]))
        go_on(e)
    t.sums_near(4)
    go_on_all()
    back_apply(4, r.table_b, r.gb, inv_b, grad_b, pre_b, write_gb)
    spatial_part(0)
    go_on_all()
    by_rows(
        grad_a, lambda here: sum(dot(g3[moved_rows(here, (2 - i) * SIDE), :], wc[i], NT) for i in range(3))
    )
    back_sums(5, r.table_a, inv_a, grad_a, slope_a, pre_a)
    t.near_send(5)
    spatial_part(1)
    t.sums_near(5)
    spatial_part(2)
    go_on_all()
    gpa = r.gpa

    def write_ga(at, grad):
        gpa[pl.ds(at, SIDE), :] = grad.astype(BF16)

    back_apply(5, r.table_a, r.ga, inv_a, grad_a, pre_a, write_ga)
    for q in range(4):
        go_on_all()
        spread_lanes(r.part[4].at[pl.ds(q * 512, 512)], dot(r.ft[q * 256 : (q + 1) * 256, :], gpa[...]))
        go_on(5 + q)

    go_on_all()
    by_rows(back, lambda here: dot(gpa[here, :], wr[...], NT))
    gf = r.gf

    def blend(y, carry):
        for p in range(tiles // group):
            values = []
            for q in range(group):
                lanes = slice((p * group + q) * 128, (p * group + q + 1) * 128)
                terms = [
                    slope_c[pl.ds(block(k, y), SIDE), lanes] * coef[k : k + 1, lanes]
                    + back[pl.ds(block(k, y), SIDE), lanes]
                    for k in range(live)
                ]
                values.append(terms[0] * keep[0])
                for m in range(1, live):
                    values.append(terms[m] * keep[m] + terms[m - 1] * moved[m - 1])
                values.append(terms[live - 1] * moved[live - 1])
            value = jnp.swapaxes(jnp.stack(values), 0, 1)
            gf[pl.ds(y * width, width), p * SIDE : (p + 1) * SIDE, :] = value[0:width].astype(BF16)
        return carry

    for q in range(height // 2):
        go_on_all()
        for y in range(2):
            blend(2 * q + y, 0)
    go_on_all()
    for each in chunks:
        for _ in each:
            pass

    t.all_sent(*range(6))
    wait_bytes(r.pool.at[pl.ds(1, len(t.clip_peers))], r.pool_s.at[0])
    for q, (name, _, count) in enumerate(plan):
        piece = r.part[name].shape[0] // count // (8 * quad)
        for m, pieces in enumerate((8 * quad - 1, 8 * quad - 1, far - 1)):
            if pieces:
                wait_bytes(r.part[0].at[pl.ds(0, pieces * piece)], chunk_s.at[q, m])


def store(gf, vectors_c, vectors, expand, s0, s1, s2, reduce, frames_out, reduce_out, spatial_out, expand_out, *rest):
    ga, ba, gb, bb, gc, bc, *scratch, sem = rest
    vectors_of = (
        (bc, vectors_c, 0), (gc, vectors_c, 8), (bb, vectors, 0), (gb, vectors, 2), (ba, vectors, 8), (ga, vectors, 10)
    )
    pltpu.make_async_copy(gf, frames_out, sem.at[0]).start()
    for number, (ref, source, first) in enumerate(vectors_of):
        for q in range(ref.shape[0] // 128):
            scratch[number][q * 128 : (q + 1) * 128] = source[first + q : first + q + 1, :].reshape(128)
        pltpu.make_async_copy(scratch[number], ref, sem.at[6 + number]).start()
    depth, width = reduce_out.shape
    for q in range(depth // 256):
        for m in range(width // 128):
            pltpu.make_async_copy(
                reduce.at[pl.ds((q * width // 128 + m) * 256, 256)],
                reduce_out.at[pl.ds(q * 256, 256), pl.ds(m * 128, 128)],
                sem.at[1],
            ).start()
    depth, width = expand_out.shape
    for q in range(width // 128):
        pltpu.make_async_copy(
            expand.at[pl.ds(q * depth, depth)], expand_out.at[:, pl.ds(q * 128, 128)], sem.at[2]
        ).start()
    for i, part in enumerate((s0, s1, s2)):
        for q in range(part.shape[0] // depth):
            pltpu.make_async_copy(
                part.at[pl.ds(q * depth, depth)],
                spatial_out.at[i, q * 128 // depth, :, pl.ds(q * 128 % depth, 128)],
                sem.at[3 + i],
            ).start()
    wait_bytes(gf, sem.at[0])
    wait_bytes(reduce, sem.at[1])
    wait_bytes(expand, sem.at[2])
    for i, part in enumerate((s0, s1, s2)):
        wait_bytes(part, sem.at[3 + i])
    for number in range(6):
        wait_bytes(scratch[number], sem.at[6 + number])


def solution(mesh):
    n = mesh.shape["clip"]

    def shards(*args):
        slots, height, width, feat = args[0].shape
        mid = args[1].shape[1]
        rows = (slots - 1) * ROWS
        outer = n // 8
        quad = min(4, outer)
        far = outer // quad
        cfg = (n, slots, height, width, feat, mid)
        flat_shape = (height * width, slots * feat // 128, 128)
        hbm = pl.BlockSpec(memory_space=pltpu.HBM)
        vmem = pl.BlockSpec(memory_space=pltpu.VMEM)
        dma = pltpu.SemaphoreType.DMA
        depths = list(enumerate((8, 4, 16, 16, 4, 4)))
        matrix, third = mid * feat // 128, 3 * mid * mid // 128
        sizes = [matrix, third, third, third, matrix]

        tiled = args[0].transpose(1, 2, 0, 3).reshape(height, width, slots, feat // 128, 128)
        tiled = tiled.transpose(0, 1, 3, 2, 4).reshape(flat_shape)
        given = [pltpu.with_memory_space_constraint(part, pltpu.HBM) for part in (tiled, *args[1:])]

        vm = pltpu.VMEM
        narrow, broad, square = vm((mid,), F32), vm((feat,), F32), vm((rows, mid), F32)
        ints = pltpu.SMEM((slots,), jnp.int32)
        plan = [matrix // 2] * 2 + [third] * 3 + [matrix // 4] * 4
        outs = dict(
            gf=vm(flat_shape, BF16), vectors_c=vm((16, 128), F32), vectors=vm((16, 128), F32),
            e=vm((matrix, 128), F32), s0=vm((third, 128), F32), s1=vm((third, 128), F32), s2=vm((third, 128), F32),
            r=vm((matrix, 128), F32),
        )
        scratch = dict(
            f4=vm((flat_shape[0] + SIDE - width, *flat_shape[1:]), BF16),
            fp=vm((rows, feat), BF16), ft=vm((feat, rows), BF16),
            wr=vm((feat, mid), BF16), ws=vm((3, 3, mid, mid), BF16), wc=vm((3, mid, 3 * mid), BF16), we=vm((mid, feat), BF16),
            valid=ints, clip=ints, segment=ints, share=pltpu.SMEM(args[13].shape, F32),
            ga=narrow, ba=narrow, gb=narrow, bb=narrow, gc=broad, bc=broad, loss=broad,
            xp=vm((rows + 2 * SIDE, 3 * mid), BF16), xt=vm((mid, rows), BF16),
            hb=vm((rows, mid), BF16), hbt=vm((mid, rows), BF16),
            pre_a=square, slope_a=square, pre_b=square, slope_b=square, grad_a=square, grad_b=square,
            pre_c=vm((rows, feat), F32), slope_c=vm((rows, feat), F32), back=vm((rows, feat), F32),
            gpc=vm((rows, feat), BF16), g3=vm((rows + 2 * SIDE, 3 * mid), BF16), gpa=vm((rows, mid), BF16),
            table_a=vm((8, mid), F32), table_b=vm((8, mid), F32),
            table_c=vm((8, feat), F32), coef=vm((8, feat), F32), dense=vm((8, 128), F32),
            pool=vm((6, 32, 128), F32), slope_sum=vm((3, 8, 128), F32), slope_hat=vm((3, 8, 128), F32),
            near=[vm((n if n <= 32 and at not in (2, 3) else 8, deep, 128), F32) for at, deep in depths],
            wide=[vm((outer, deep, 128), F32) for at, deep in depths],
            plane=vm((outer, 8, 128), F32),
            part=[vm((size, 128), F32) for size in sizes],
            rb0=[vm((size // 2, 128), F32) for size in plan],
            rb1=[vm((size // 4, 128), F32) for size in plan],
            rb2=[vm((size // 8, 128), F32) for size in plan],
            rb3=[vm(((quad - 1) * size // (8 * quad), 128), F32) for size in plan],
            rb4=[vm((far, size // (8 * quad), 128), F32) for size in plan if far > 1],
            load_sem=dma((16,)), near_s=dma((6,)), near_r=dma((6,)), wide_s=dma((6,)), wide_r=dma((6,)),
            pool_s=dma((1,)), pool_r=dma((1,)), chunk_s=dma((9, 3)), chunk_r=dma((9, 9)),
        )
        names = (*arg_names(), *outs, *scratch)

        def kernel(*refs):
            t = Step(cfg, SimpleNamespace(**dict(zip(names, refs, strict=True))))
            prologue(t)
            backward(t, *forward(t))

        results = pl.pallas_call(
            kernel,
            out_shape=list(outs.values()),
            in_specs=[hbm] * len(given),
            out_specs=[vmem] * len(outs),
            scratch_shapes=list(scratch.values()),
            compiler_params=pltpu.CompilerParams(
                collective_id=0, has_side_effects=True, vmem_limit_bytes=50 * 1024 * 1024
            ),
        )(*given)
        vector = jax.ShapeDtypeStruct((mid,), F32)
        wide_vector = jax.ShapeDtypeStruct((feat,), F32)
        flat_grad, *rest = pl.pallas_call(
            store,
            out_shape=[
                jax.ShapeDtypeStruct(flat_shape, BF16),
                jax.ShapeDtypeStruct((feat, mid), F32),
                jax.ShapeDtypeStruct((3, 3, mid, mid), F32),
                jax.ShapeDtypeStruct((mid, feat), F32),
                vector, vector, vector, vector, wide_vector, wide_vector,
            ],
            in_specs=[vmem] * 8,
            out_specs=[hbm] * 10,
            scratch_shapes=[*(vm((c,), F32) for c in (feat, feat, mid, mid, mid, mid)), dma((12,))],
            compiler_params=pltpu.CompilerParams(vmem_limit_bytes=8 * 1024 * 1024),
        )(*(pltpu.with_memory_space_constraint(part, pltpu.VMEM) for part in results))
        grad_frames = flat_grad.reshape(height, width, feat // 128, slots, 128).transpose(0, 1, 3, 2, 4)
        return grad_frames.reshape(height, width, slots, feat).transpose(2, 0, 1, 3), *rest

    split = P("clip")
    in_specs = (split,) + (P(),) * 9 + (split,) * 3 + (P(), P())
    out_specs = (split,) + (P(),) * 9
    return jax.shard_map(shards, mesh=mesh, in_specs=in_specs, out_specs=out_specs, check_vma=False)


def arg_names():
    return dict(
        frames=0, w_reduce=0, w_spatial=0, w_expand=0, gain_a=0, bias_a=0, gain_b=0, bias_b=0, gain_c=0, bias_c=0,
        clip_ids=0, segment_ids=0, slot_valid=0, segment_weight=0, loss_weight=0,
    )
```

```python
import functools
from types import SimpleNamespace

import jax
import jax.numpy as jnp
from jax import lax
from jax.experimental import pallas as pl
from jax.experimental.pallas import tpu as pltpu
from jax.sharding import PartitionSpec as P

MESH = pl.DeviceIdType.MESH
EPS = 1e-05
F32 = jnp.float32
BF16 = jnp.bfloat16
SIDE = 16
ROWS = SIDE * SIDE
NN = (((1,), (0,)), ((), ()))
NT = (((1,), (1,)), ((), ()))

ORDER = (
    (),
    (),
    (),
    (),
    (),
    (),
    (0, 1,),
    (2, 0,),
    (1,),
    (2, 0, 1, 3,),
    (2, 4,),
    (),
    (),
    (0,),
    (1, 3, 5, 2, 4,),
    (6, 3, 8,),
    (1, 0, 5, 7, 4, 8, 1, 3, 6, 7, 8, 2, 0,),
    (4, 7, 3,),
    (6, 2, 8, 1, 5, 0, 4, 7, 3, 6, 8, 5, 7, 1, 6, 4,),
    (5, 6, 0, 3,),
    (7,),
    (8, 2, 4, 5, 7, 8, 6, 3, 5,),
    (7, 8, 6, 5, 4, 2,),
)


def dot(a, b, dims=NN):
    return lax.dot_general(a, b, dims, preferred_element_type=F32)


def wait_bytes(ref, sem):
    pltpu.make_async_copy(ref, ref, sem).wait()


def spread_lanes(ref, value):
    depth = value.shape[0]
    for q in range(value.shape[1] // 128):
        ref[q * depth : (q + 1) * depth, :] = value[:, q * 128 : (q + 1) * 128]


def by_rows(ref, value):
    def step(k, carry):
        here = pl.ds(pl.multiple_of(k * 256, 256), 256)
        ref[here, :] = value(here)
        return carry

    lax.fori_loop(0, ref.shape[0] // 256, step, 0)


def moved_rows(here, at):
    return pl.ds(pl.multiple_of(here.start + at, SIDE), 256)


def add_rows(into, first, values):
    rows = values.shape[0]
    block_rows = max(q for q in (8, 16, 24, 32, 48, 64) if rows % q == 0)

    def step(q, carry):
        at = pl.multiple_of(q * block_rows, 8)
        here = pl.ds(pl.multiple_of(first + at, 8), block_rows)
        into[here, :] = into[here, :] + values[pl.ds(at, block_rows), :]
        return carry

    lax.fori_loop(0, rows // block_rows, step, 0)


def block(k, y):
    return pl.multiple_of(k * ROWS + y * SIDE, SIDE)


def to_dense(ref, at, value, first):
    for q in range(value.shape[1] // 128):
        ref[at, pl.ds(first + q, 1), :] = value[:, q * 128 : (q + 1) * 128]


def row_form(ref, row, source, first, count):
    for q in range(count):
        ref[row : row + 1, q * 128 : (q + 1) * 128] = source[first + q : first + q + 1, :]


def three(ref, at, left, middle, right):
    here, wide = pl.ds(at + SIDE, SIDE), middle.shape[1]
    ref[here, 0:wide] = left.astype(BF16)
    ref[here, wide : 2 * wide] = middle.astype(BF16)
    ref[here, 2 * wide : 3 * wide] = right.astype(BF16)


def dense_of(ref1, scratch):
    count = ref1.shape[0] // 128
    for q in range(count):
        scratch[q : q + 1, :] = ref1[q * 128 : (q + 1) * 128].reshape(1, 128)
    return scratch[0:count, :]


class Step:
    def __init__(self, cfg, r):
        self.r, self.sizes = r, cfg
        self.n, self.slots, self.height, self.width, self.feat, self.mid = cfg
        self.live = self.slots - 1
        self.rows = self.live * ROWS
        self.area = self.height * self.width
        self.inner = 8
        self.outer = self.n // 8
        self.quad = min(4, self.outer)
        self.far = self.outer // self.quad
        self.loads = {}
        self.mask = lax.broadcasted_iota(jnp.int32, (SIDE, 256), 0) < self.width

    def load(self, **pairs):
        for name, (src, dst) in pairs.items():
            copy = pltpu.make_async_copy(src, dst, self.r.load_sem.at[len(self.loads)])
            copy.start()
            self.loads[name] = copy

    def loaded(self, **names):
        for name in names:
            self.loads[name].wait()

    def fold(self, value):
        return jnp.sum(jnp.where(self.mask, value, 0.0), axis=0, keepdims=True)

    def slot_facts(self):
        r, live = self.r, self.live
        alive, later = 1, []
        for k in range(live):
            alive = alive * r.valid[k]
            later.append(1 - alive)
        self.keep = [(1 - q).astype(F32) for q in later]
        self.moved = [q.astype(F32) for q in later]
        self.later = later
        self.v = [self.kept(r.valid, k) for k in range(live)]
        for k in range(live):
            r.vs[k] = self.v[k]
        self.n_own = (self.v[0] + self.v[1] + self.v[2]) * float(self.area)

    def kept(self, values, k):
        return (values[k] + self.later[k] * (values[k + 1] - values[k])).astype(F32)

    def places(self):
        n = self.n
        self.me = me = lax.axis_index("clip")
        self.low, self.high = low, high = me % self.inner, me // self.inner
        self.direct = n <= 32
        self.peers = flips(me, n)
        self.low_peers = flips(me, self.inner)
        self.high_peers = flips(me, self.outer, self.inner)
        self.clip_peers = [(me + o) % n for o in (n // 2 - 1, n // 2 + 1, n // 2, n - 1, 1)]

    def greet(self):
        self.greeted = self.peers if self.direct else self.low_peers + self.high_peers + self.clip_peers
        self.barrier = pltpu.get_barrier_semaphore()
        for device in self.greeted:
            pl.semaphore_signal(self.barrier, inc=1, device_id=(device,), device_id_type=MESH)

    def all_here(self):
        pl.semaphore_wait(self.barrier, len(self.greeted))

    def send(self, src, dst, ssem, rsem, device):
        pltpu.make_async_remote_copy(
            src_ref=src, dst_ref=dst, send_sem=ssem, recv_sem=rsem, device_id=(device,), device_id_type=MESH
        ).start()

    def one_stage(self, at):
        return self.direct and at not in (2, 3)

    def near_at(self, at):
        return self.me if self.one_stage(at) else self.low

    def near_send(self, at):
        buf, mine = self.r.near[at], self.near_at(at)
        for device in self.peers if self.one_stage(at) else self.low_peers:
            self.send(buf.at[mine], buf.at[mine], self.r.near_s.at[at], self.r.near_r.at[at], device)

    def near_wait(self, at, sems):
        buf = self.r.near[at]
        wait_bytes(buf.at[pl.ds(0, buf.shape[0] - 1)], sems.at[at])

    def wide_send(self, at):
        buf = self.r.wide[at]
        for device in self.high_peers:
            self.send(buf.at[self.high], buf.at[self.high], self.r.wide_s.at[at], self.r.wide_r.at[at], device)

    def wide_wait(self, at, sems):
        wait_bytes(self.r.wide[at].at[pl.ds(0, self.outer - 1)], sems.at[at])

    def all_sent(self, *rounds):
        for at in rounds:
            self.near_wait(at, self.r.near_s)
            if not self.one_stage(at):
                self.wide_wait(at, self.r.wide_s)

    def near_count(self, q):
        return self.r.near[0][(self.me - self.low + q) if self.direct else q, 4:5, :]

    def wide_count(self, q):
        return self.r.plane[q, 0:1, :] if self.direct else self.r.wide[0][q, 4:5, :]

    def stats_near(self, at, count):
        if self.one_stage(at):
            return
        self.near_wait(at, self.r.near_r)
        n_all, s_all, _, spread = combine(self.r.near[at], self.near_count, self.inner, count)
        buf = self.r.wide[at]
        buf[self.high, 0:count, :] = s_all
        buf[self.high, count : 2 * count, :] = spread
        if at == 0:
            buf[self.high, 4:5, :] = n_all
        self.wide_send(at)

    def stats_wide(self, at, count, table):
        r = self.r
        if self.one_stage(at):
            self.near_wait(at, r.near_r)
            counts = r.near[0]
            n_all, _, mean, spread = combine(r.near[at], lambda q: counts[q, 4:5, :], self.n, count)
            if at == 0:
                for q in range(self.outer):
                    r.plane[q, 0:1, :] = sum(counts[q * self.inner + m, 4:5, :] for m in range(self.inner))
        else:
            self.wide_wait(at, r.wide_r)
            n_all, _, mean, spread = combine(r.wide[at], self.wide_count, self.outer, count)
        inverse = lax.rsqrt(spread / n_all + EPS)
        r.dense[0:count, :] = mean
        row_form(table, 0, r.dense, 0, count)
        r.dense[0:count, :] = inverse
        row_form(table, 1, r.dense, 0, count)
        return n_all, inverse

    def sums_near(self, at):
        if not self.one_stage(at):
            self.near_wait(at, self.r.near_r)
            self.r.wide[at][self.high] = total(self.r.near[at])
            self.wide_send(at)

    def sums_wide(self, at):
        if self.one_stage(at):
            self.near_wait(at, self.r.near_r)
            return total(self.r.near[at])
        self.wide_wait(at, self.r.wide_r)
        return total(self.r.wide[at])

    def local_stats(self, buf, at, ref):
        channels = ref.shape[1]
        count = channels // 128
        zero = jnp.zeros((SIDE, 256), F32)

        def columns(c, carry):
            lanes = pl.ds(pl.multiple_of(c * 256, 256), 256)

            def gather(term):
                def slot(k, acc):
                    part = lax.fori_loop(
                        0, self.height, lambda y, a: a + term(ref[pl.ds(block(k, y), SIDE), lanes]), zero, unroll=7
                    )
                    return acc + part * self.r.vs[k]

                return self.fold(lax.fori_loop(0, self.live, slot, zero))

            s_own = gather(lambda x: x)
            mean = s_own / jnp.maximum(self.n_own, 1.0)
            to_dense(buf, at, s_own, 2 * c)
            to_dense(buf, at, gather(lambda x: (x - mean) * (x - mean)), count + 2 * c)
            return carry

        lax.fori_loop(0, channels // 256, columns, 0)

    def norm_silu(self, ref, slope_ref, table, gain, bias, write):
        centre, scale = table[0:1, :], table[1:2, :] * gain[...].reshape(1, self.mid)
        b = bias[...].reshape(1, self.mid)

        def slot(k, carry):
            def step(y, inside):
                at = block(k, y)
                u = (ref[pl.ds(at, SIDE), :] - centre) * scale + b
                s = 0.5 * jnp.tanh(0.5 * u) + 0.5
                h = u * s
                slope_ref[pl.ds(at, SIDE), :] = jnp.where(self.mask, s + (h - h * s), 0.0)
                write(at, jnp.where(self.mask, h, 0.0))
                return inside

            return lax.fori_loop(0, self.height, step, carry, unroll=7)

        lax.fori_loop(0, self.live, slot, 0)


def flips(index, count, stride=1):
    steps, at = [], 1
    while at < count:
        steps.append(at * stride * (1 - 2 * ((index // (at * stride)) % 2)))
        at *= 2
    return [sum((d for b, d in enumerate(steps) if o >> b & 1), index) for o in reversed(range(1, count))]


def combine(buf, counts, group, count):
    n_part = [counts(q) for q in range(group)]
    s_part = [buf[q, 0:count, :] for q in range(group)]
    n_all = sum(n_part[1:], n_part[0])
    s_all = sum(s_part[1:], s_part[0])
    mean = s_all / jnp.maximum(n_all, 1.0)
    spread = jnp.zeros((count, 128), F32)
    for q in range(group):
        gap = s_part[q] / jnp.maximum(n_part[q], 1.0) - mean
        spread = spread + (buf[q, count : 2 * count, :] + n_part[q] * gap * gap)
    return n_all, s_all, mean, spread


def total(buf):
    out = buf[0]
    for q in range(1, buf.shape[0]):
        out = out + buf[q]
    return out


def clear(*refs):
    for ref in refs:
        ref[...] = jnp.zeros(ref.shape, ref.dtype)


def prologue(t):
    r, slots, live, width, feat = t.r, t.slots, t.live, t.width, t.feat
    t.places()
    t.greet()
    t.load(
        frames=(r.frames, r.f4.at[pl.ds(0, t.area)]), valid=(r.slot_valid, r.valid), reduce=(r.w_reduce, r.wr),
        clip=(r.clip_ids, r.clip), segment=(r.segment_ids, r.segment),
        share=(r.segment_weight, r.share), spatial=(r.w_spatial, r.ws), expand=(r.w_expand, r.we),
        ga=(r.gain_a, r.ga), ba=(r.bias_a, r.ba), gb=(r.gain_b, r.gb), bb=(r.bias_b, r.bb),
        gc=(r.gain_c, r.gc), bc=(r.bias_c, r.bc), loss=(r.loss_weight, r.loss),
    )
    for i in range(3):
        for j in range(3):
            pltpu.make_async_copy(
                r.w_spatial.at[i, j], r.wc.at[i, :, pl.ds(j * t.mid, t.mid)], r.load_sem.at[15]
            ).start()
    r.f4[t.area :] = jnp.zeros((r.f4.shape[0] - t.area, *r.f4.shape[1:]), BF16)
    clear(r.fp)
    t.loaded(valid=0)
    t.slot_facts()
    t.loaded(frames=0)
    fp, f4 = r.fp, r.f4
    tiles = feat // 128
    group = SIDE // slots
    short = lax.broadcasted_iota(jnp.int32, (SIDE, 128), 0) < width

    def regroup(y, carry):
        for p in range(tiles // group):
            value = f4[pl.ds(y * width, SIDE), p * SIDE : (p + 1) * SIDE, :].astype(F32)
            value = jnp.swapaxes(value, 0, 1)
            for q in range(group):
                for k in range(live):
                    row = value[q * slots + k] * t.keep[k] + value[q * slots + k + 1] * t.moved[k]
                    lanes = slice((p * group + q) * 128, (p * group + q + 1) * 128)
                    fp[pl.ds(block(k, y), SIDE), lanes] = jnp.where(short, row, 0.0).astype(BF16)
        return carry

    lax.fori_loop(0, t.height, regroup, 0)
    t.loaded(reduce=0)
    by_rows(r.pre_a, lambda here: dot(fp[here, :], r.wr[...]))
    t.local_stats(r.near[0], t.near_at(0), r.pre_a)
    r.near[0][t.near_at(0), 4:5, :] = jnp.full((1, 128), t.n_own, F32)


def forward(t):
    r, live, mid, feat, rows, area, height = t.r, t.live, t.mid, t.feat, t.rows, t.area, t.height
    t.all_here()
    t.near_send(0)
    r.ft[...] = r.fp[...].T
    t.stats_near(0, mid // 128)
    clear(r.xp, r.hb, r.g3, r.gpc, r.gpa)
    t.loaded(clip=0, segment=0, share=0, ga=0, ba=0, gb=0, bb=0, gc=0, bc=0, loss=0, spatial=0, expand=0)
    key = [t.kept(r.clip, k) for k in range(live)]
    weight = []
    for k in range(live):
        at = t.kept(r.segment, k)
        w0, w1, w2 = (r.share[q] for q in range(3))
        weight.append(
            t.v[k] * (w0 * ((1.0 - at) * (2.0 - at) * 0.5) + w1 * (at * (2.0 - at)) + w2 * (at * (at - 1.0) * 0.5))
        )
    n_all, inv_a = t.stats_wide(0, mid // 128, r.table_a)

    xp, hb = r.xp, r.hb

    def write_a(at, h):
        three(xp, at, pltpu.roll(h, 1, 0), h, pltpu.roll(h, SIDE - 1, 0))

    t.norm_silu(r.pre_a, r.slope_a, r.table_a, r.ga, r.ba, write_a)

    by_rows(
        r.pre_b,
        lambda here: sum(dot(xp[moved_rows(here, i * SIDE), :], r.ws[i].reshape(3 * mid, mid)) for i in range(3)),
    )
    t.local_stats(r.near[1], t.near_at(1), r.pre_b)
    t.near_send(1)
    r.xt[...] = xp[SIDE : SIDE + rows, mid : 2 * mid].T
    t.stats_near(1, mid // 128)
    _, inv_b = t.stats_wide(1, mid // 128, r.table_b)

    def write_b(at, h):
        hb[pl.ds(at, SIDE), :] = h.astype(BF16)

    t.norm_silu(r.pre_b, r.slope_b, r.table_b, r.gb, r.bb, write_b)

    pre_c, slope_c, fp, table_c = r.pre_c, r.slope_c, r.fp, r.table_c
    by_rows(pre_c, lambda here: dot(hb[here, :], r.we[...]))
    t.local_stats(r.near[2], t.near_at(2), pre_c)
    t.near_send(2)
    r.hbt[...] = hb[...].T
    t.stats_near(2, feat // 128)
    _, inv_c = t.stats_wide(2, feat // 128, table_c)

    pool, slope_sum, slope_hat = r.pool, r.slope_sum, r.slope_hat
    dense = r.dense
    for row, vector in ((2, r.gc), (3, r.bc)):
        dense_of(vector, dense)
        row_form(table_c, row, dense, 0, feat // 128)

    def columns(c, carry):
        lanes = pl.ds(pl.multiple_of(c * 256, 256), 256)
        centre, inverse, g, b = (table_c[q : q + 1, lanes] for q in range(4))

        def slot(k, inside):
            def step(y, sums):
                a0, a1, a2 = sums
                at = block(k, y)
                hat = (pre_c[pl.ds(at, SIDE), lanes] - centre) * inverse
                u = hat * g + b + fp[pl.ds(at, SIDE), lanes].astype(F32)
                s = 0.5 * jnp.tanh(0.5 * u) + 0.5
                h = u * s
                slope = s + (h - h * s)
                slope_c[pl.ds(at, SIDE), lanes] = slope
                return a0 + h, a1 + slope, a2 + slope * hat

            zero = jnp.zeros((SIDE, 256), F32)
            a0, a1, a2 = lax.fori_loop(0, height, step, (zero, zero, zero), unroll=7)
            p_row = (t.fold(a0) * (1.0 / area)).astype(BF16).astype(F32)
            to_dense(pool, 0, p_row, 8 * k + 2 * c)
            to_dense(slope_sum, k, t.fold(a1), 2 * c)
            to_dense(slope_hat, k, t.fold(a2), 2 * c)
            return inside

        return lax.fori_loop(0, live, slot, carry)

    lax.fori_loop(0, feat // 256, columns, 0)
    for k in range(live):
        pool[0, 24 + k : 25 + k, :] = jnp.full((1, 128), key[k], F32)
        pool[0, 28 + k : 29 + k, :] = jnp.full((1, 128), weight[k], F32)
    for q, device in enumerate(t.clip_peers):
        t.send(pool.at[0], pool.at[q + 1], r.pool_s.at[0], r.pool_r.at[0], device)
    wait_bytes(pool.at[pl.ds(1, len(t.clip_peers))], r.pool_r.at[0])

    lw = dense_of(r.loss, r.dense)
    grads = []
    for k in range(live):
        my_key = jnp.full((1, 128), key[k], F32)
        my_weight = jnp.full((1, 128), weight[k], F32)
        mean = jnp.zeros((8, 128), F32)
        den = jnp.zeros((1, 128), F32)
        for q in range(len(t.clip_peers) + 1):
            for m in range(live):
                match = jnp.where(pool[q, 24 + m : 25 + m, :] == my_key, pool[q, 28 + m : 29 + m, :], 0.0)
                den = den + match
                mean = mean + match * pool[q, 8 * m : 8 * m + 8, :]
        den = jnp.where(den == 0.0, 1.0, den)
        mean = mean / den
        power = jnp.sum(jnp.sum(mean * mean, axis=0, keepdims=True), axis=1, keepdims=True)
        scale = lax.rsqrt(power * (1.0 / feat) + EPS)
        unit = mean * scale
        along = jnp.sum(jnp.sum(unit * lw, axis=0, keepdims=True), axis=1, keepdims=True)
        mean_grad = scale * (lw - unit * (along * (1.0 / feat)))
        grads.append((my_weight / den) * mean_grad * (1.0 / area))

    near3 = r.near[3]
    shift = jnp.zeros((8, 128), F32)
    gain = jnp.zeros((8, 128), F32)
    for k in range(live):
        shift = shift + grads[k] * slope_sum[k]
        gain = gain + grads[k] * slope_hat[k]
    near3[t.near_at(3), 0:8, :] = shift
    near3[t.near_at(3), 8:16, :] = gain
    t.near_send(3)
    coef, dense = r.coef, r.dense
    scale_c = dense_of(r.gc, dense) * inv_c
    for k in range(live):
        dense[...] = grads[k]
        row_form(coef, k, dense, 0, feat // 128)
        dense[...] = grads[k] * scale_c
        row_form(coef, 3 + k, dense, 0, feat // 128)
    t.sums_near(3)
    both = t.sums_wide(3)
    r.vectors_c[...] = both
    dense[...] = both[0:8] * scale_c / n_all
    row_form(coef, 6, dense, 0, feat // 128)
    dense[...] = both[8:16] * scale_c * inv_c / n_all
    row_form(coef, 7, dense, 0, feat // 128)
    return n_all, inv_a, inv_b


def backward(t, n_all, inv_a, inv_b):
    r, live, mid, feat, rows, height = t.r, t.live, t.mid, t.feat, t.rows, t.height
    slots, width, quad, far, v, wc = t.slots, t.width, t.quad, t.far, t.v, r.wc
    coef, pre_c, slope_c, out = r.coef, r.pre_c, r.slope_c, r.vectors
    me, send = t.me, t.send
    gpc = r.gpc

    def slot_grad(k, carry):
        def columns(c, inside):
            lanes = pl.ds(pl.multiple_of(c * 256, 256), 256)
            centre = r.table_c[0:1, lanes]
            c0 = coef[pl.ds(3 + k, 1), lanes]
            c1 = coef[6:7, lanes] * r.vs[k]
            c2 = coef[7:8, lanes] * r.vs[k]

            def step(y, last):
                at = block(k, y)
                grad = slope_c[pl.ds(at, SIDE), lanes] * c0 - (c1 + (pre_c[pl.ds(at, SIDE), lanes] - centre) * c2)
                gpc[pl.ds(at, SIDE), lanes] = grad.astype(BF16)
                return last

            return lax.fori_loop(0, height, step, inside, unroll=7)

        return lax.fori_loop(0, feat // 256, columns, carry)

    lax.fori_loop(0, live, slot_grad, 0)

    def back_sums(at, table, inv, grad_ref, slope_ref, pre_ref):
        zero = jnp.zeros((SIDE, mid), F32)
        carry = (zero, zero)
        centre = table[0:1, :]

        def slot(k, sums):
            def step(y, c):
                here = pl.ds(block(k, y), SIDE)
                grad = grad_ref[here, :] * slope_ref[here, :]
                grad_ref[here, :] = grad
                return c[0] + grad, c[1] + grad * (pre_ref[here, :] - centre)

            return lax.fori_loop(0, height, step, sums, unroll=7)

        carry = lax.fori_loop(0, live, slot, carry)
        buf = r.near[at]
        to_dense(buf, t.near_at(at), jnp.sum(carry[0], axis=0, keepdims=True), 0)
        to_dense(buf, t.near_at(at), jnp.sum(carry[1], axis=0, keepdims=True) * table[1:2, :], 2)

    def back_apply(at, table, gain_ref, inv, grad_ref, pre_ref, write):
        both = t.sums_wide(at)
        out[8 * at - 32 : 8 * at - 28, :] = both[0:4]
        dense = r.dense
        scale = dense_of(gain_ref, dense) * inv
        dense[0:2, :] = scale
        dense[2:4, :] = both[0:2] * scale / n_all
        dense[4:6, :] = both[2:4] * scale * inv / n_all
        for q in range(3):
            row_form(table, 2 + q, dense, 2 * q, 2)
        centre = table[0:1, :]

        def slot(k, carry):
            c0, c1, c2 = table[2:3, :], table[3:4, :] * r.vs[k], table[4:5, :] * r.vs[k]

            def step(y, inside):
                at_row = block(k, y)
                here = pl.ds(at_row, SIDE)
                write(at_row, grad_ref[here, :] * c0 - (c1 + (pre_ref[here, :] - centre) * c2))
                return inside

            return lax.fori_loop(0, height, step, carry, unroll=7)

        lax.fori_loop(0, live, slot, 0)

    core, bit_x, bit_y, at_z = me % 2, (me // 2) % 2, (me // 4) % 2, (me // 8) % quad
    at_far = me // (8 * quad)
    bit1 = bit_x + core * (bit_y - bit_x)
    bit2 = bit_y + core * (bit_x - bit_y)
    sibling = me + 1 - 2 * core
    peer1 = me + (1 - 2 * bit1) * (2 + 2 * core)
    peer2 = me + (1 - 2 * bit2) * (4 - 2 * core)
    z_at = flips(at_z, quad)
    z_peer = [me + 8 * (q - at_z) for q in z_at]
    far_peer = [me + 8 * quad * ((at_far + o) % far - at_far) for o in range(1, far)]
    chunk_s, chunk_r = r.chunk_s, r.chunk_r
    blocks = iter(ORDER)
    plan = [(0, q, 2) for q in range(2)] + [(1 + q, 0, 1) for q in range(3)] + [(4, q, 4) for q in range(4)]

    def chunk(q):
        name, at, count = plan[q]
        size = r.part[name].shape[0] // count
        part = r.part[name].at[pl.ds(at * size, size)]
        whole = (r.e, r.s0, r.s1, r.s2, r.r)[name].at[pl.ds(at * size, size)]
        half, quarter, eighth, piece = size // 2, size // 4, size // 8, size // (8 * quad)
        m8 = lambda value: pl.multiple_of(value, 8)
        at_h = m8(core * half)
        at_q = m8(at_h + bit1 * quarter)
        at_e = m8(at_q + bit2 * eighth)
        at_p = m8(at_e + at_z * piece)

        def go(step, src, dst, device):
            send(src, dst, chunk_s.at[q, step // 4], chunk_r.at[q, step], device)

        def finish(step, ref):
            wait_bytes(ref, chunk_r.at[q, step])

        rb0, rb1, rb2, rb3 = r.rb0[q], r.rb1[q], r.rb2[q], r.rb3[q]
        go(0, part.at[pl.ds(m8((1 - core) * half), half)], rb0, sibling)
        yield
        finish(0, rb0)
        add_rows(part, at_h, rb0)
        go(1, part.at[pl.ds(m8(at_h + (1 - bit1) * quarter), quarter)], rb1, peer1)
        yield
        finish(1, rb1)
        add_rows(part, at_q, rb1)
        go(2, part.at[pl.ds(m8(at_q + (1 - bit2) * eighth), eighth)], rb2, peer2)
        yield
        finish(2, rb2)
        add_rows(part, at_e, rb2)
        for o in range(quad - 1):
            go(3, part.at[pl.ds(m8(at_e + z_at[o] * piece), piece)], rb3.at[pl.ds(o * piece, piece)], z_peer[o])
        yield
        finish(3, rb3)
        own = part[pl.ds(at_p, piece), :]
        for o in range(quad - 1):
            own = own + rb3[o * piece : (o + 1) * piece, :]
        if far > 1:
            rb4 = r.rb4[q]
            rb4[at_far] = own
            for device in far_peer:
                go(8, rb4.at[at_far], rb4.at[at_far], device)
            yield
            finish(8, rb4.at[pl.ds(0, far - 1)])
            own = rb4[0]
            for o in range(1, far):
                own = own + rb4[o]
        whole[pl.ds(at_p, piece), :] = own
        for o in range(quad - 1):
            go(4, whole.at[pl.ds(at_p, piece)], whole.at[pl.ds(at_p, piece)], z_peer[o])
        yield
        finish(4, whole.at[pl.ds(0, (quad - 1) * piece)])
        go(5, whole.at[pl.ds(at_e, eighth)], whole.at[pl.ds(at_e, eighth)], peer2)
        yield
        finish(5, whole.at[pl.ds(0, eighth)])
        go(6, whole.at[pl.ds(at_q, quarter)], whole.at[pl.ds(at_q, quarter)], peer1)
        yield
        finish(6, whole.at[pl.ds(0, quarter)])
        go(7, whole.at[pl.ds(at_h, half)], whole.at[pl.ds(at_h, half)], sibling)
        yield
        finish(7, whole.at[pl.ds(0, half)])
        yield

    chunks = [chunk(q) for q in range(len(plan))]

    def go_on(*which):
        for q in which:
            next(chunks[q])

    def go_on_all():
        go_on(*next(blocks))

    pre_a, slope_a, pre_b, slope_b, hbt, xt = r.pre_a, r.slope_a, r.pre_b, r.slope_b, r.hbt, r.xt
    we, wr, back = r.we, r.wr, r.back
    tiles = feat // 128
    group = SIDE // slots
    keep, moved, mask = t.keep, t.moved, t.mask
    grad_b, grad_a = r.grad_b, r.grad_a
    wait_bytes(wc, r.load_sem.at[15])
    g3 = r.g3

    def write_gb(at, grad):
        grad = jnp.where(mask, grad, 0.0)
        three(g3, at, pltpu.roll(grad, SIDE - 1, 0), grad, pltpu.roll(grad, 1, 0))

    def expand_part(q, carry):
        value = dot(hbt[...], gpc[:, pl.ds(pl.multiple_of(q * 256, 256), 256)])
        for m in range(2):
            r.part[0][pl.ds(pl.multiple_of((2 * q + m) * mid, mid), mid), :] = value[:, m * 128 : (m + 1) * 128]
        return carry

    def spatial_part(i):
        go_on_all()

        def columns(j, carry):
            lanes = pl.ds(pl.multiple_of(j * mid, mid), mid)
            value = dot(xt[...], g3[(2 - i) * SIDE : (2 - i) * SIDE + rows, lanes])
            for m in range(2):
                r.part[1 + i][pl.ds(pl.multiple_of((2 * j + m) * mid, mid), mid), :] = value[:, m * 128 : (m + 1) * 128]
            return carry

        lax.fori_loop(0, 3, columns, 0)
        go_on(2 + i)

    go_on_all()
    go_on_all()
    by_rows(grad_b, lambda here: dot(gpc[here, :], we[...], NT))
    back_sums(4, r.table_b, inv_b, grad_b, slope_b, pre_b)
    t.near_send(4)
    for e in range(2):
        go_on_all()
        lax.fori_loop(2 * e, 2 * e + 2, expand_part, 0)
        go_on(e)
    t.sums_near(4)
    go_on_all()
    back_apply(4, r.table_b, r.gb, inv_b, grad_b, pre_b, write_gb)
    spatial_part(0)
    go_on_all()
    by_rows(
        grad_a, lambda here: sum(dot(g3[moved_rows(here, (2 - i) * SIDE), :], wc[i], NT) for i in range(3))
    )
    back_sums(5, r.table_a, inv_a, grad_a, slope_a, pre_a)
    t.near_send(5)
    spatial_part(1)
    t.sums_near(5)
    spatial_part(2)
    go_on_all()
    gpa = r.gpa

    def write_ga(at, grad):
        gpa[pl.ds(at, SIDE), :] = grad.astype(BF16)

    back_apply(5, r.table_a, r.ga, inv_a, grad_a, pre_a, write_ga)
    for q in range(4):
        go_on_all()
        spread_lanes(r.part[4].at[pl.ds(q * 512, 512)], dot(r.ft[q * 256 : (q + 1) * 256, :], gpa[...]))
        go_on(5 + q)

    go_on_all()
    by_rows(back, lambda here: dot(gpa[here, :], wr[...], NT))
    gf = r.gf

    def blend(y, carry):
        for p in range(tiles // group):
            values = []
            for q in range(group):
                lanes = slice((p * group + q) * 128, (p * group + q + 1) * 128)
                terms = [
                    slope_c[pl.ds(block(k, y), SIDE), lanes] * coef[k : k + 1, lanes]
                    + back[pl.ds(block(k, y), SIDE), lanes]
                    for k in range(live)
                ]
                values.append(terms[0] * keep[0])
                for m in range(1, live):
                    values.append(terms[m] * keep[m] + terms[m - 1] * moved[m - 1])
                values.append(terms[live - 1] * moved[live - 1])
            value = jnp.swapaxes(jnp.stack(values), 0, 1)
            gf[pl.ds(y * width, width), p * SIDE : (p + 1) * SIDE, :] = value[0:width].astype(BF16)
        return carry

    for q in range(height // 2):
        go_on_all()
        lax.fori_loop(2 * q, 2 * q + 2, blend, 0)
    go_on_all()
    for each in chunks:
        for _ in each:
            pass

    t.all_sent(*range(6))
    wait_bytes(r.pool.at[pl.ds(1, len(t.clip_peers))], r.pool_s.at[0])
    for q, (name, _, count) in enumerate(plan):
        piece = r.part[name].shape[0] // count // (8 * quad)
        for m, pieces in enumerate((8 * quad - 1, 8 * quad - 1, far - 1)):
            if pieces:
                wait_bytes(r.part[0].at[pl.ds(0, pieces * piece)], chunk_s.at[q, m])


def store(gf, vectors_c, vectors, expand, s0, s1, s2, reduce, frames_out, reduce_out, spatial_out, expand_out, *rest):
    ga, ba, gb, bb, gc, bc, *scratch, sem = rest
    vectors_of = (
        (bc, vectors_c, 0), (gc, vectors_c, 8), (bb, vectors, 0), (gb, vectors, 2), (ba, vectors, 8), (ga, vectors, 10)
    )
    pltpu.make_async_copy(gf, frames_out, sem.at[0]).start()
    for number, (ref, source, first) in enumerate(vectors_of):
        for q in range(ref.shape[0] // 128):
            scratch[number][q * 128 : (q + 1) * 128] = source[first + q : first + q + 1, :].reshape(128)
        pltpu.make_async_copy(scratch[number], ref, sem.at[6 + number]).start()
    depth, width = reduce_out.shape
    for q in range(depth // 256):
        for m in range(width // 128):
            pltpu.make_async_copy(
                reduce.at[pl.ds((q * width // 128 + m) * 256, 256)],
                reduce_out.at[pl.ds(q * 256, 256), pl.ds(m * 128, 128)],
                sem.at[1],
            ).start()
    depth, width = expand_out.shape
    for q in range(width // 128):
        pltpu.make_async_copy(
            expand.at[pl.ds(q * depth, depth)], expand_out.at[:, pl.ds(q * 128, 128)], sem.at[2]
        ).start()
    for i, part in enumerate((s0, s1, s2)):
        for q in range(part.shape[0] // depth):
            pltpu.make_async_copy(
                part.at[pl.ds(q * depth, depth)],
                spatial_out.at[i, q * 128 // depth, :, pl.ds(q * 128 % depth, 128)],
                sem.at[3 + i],
            ).start()
    wait_bytes(gf, sem.at[0])
    wait_bytes(reduce, sem.at[1])
    wait_bytes(expand, sem.at[2])
    for i, part in enumerate((s0, s1, s2)):
        wait_bytes(part, sem.at[3 + i])
    for number in range(6):
        wait_bytes(scratch[number], sem.at[6 + number])


def solution(mesh):
    n = mesh.shape["clip"]

    def shards(*args):
        slots, height, width, feat = args[0].shape
        mid = args[1].shape[1]
        rows = (slots - 1) * ROWS
        outer = n // 8
        quad = min(4, outer)
        far = outer // quad
        cfg = (n, slots, height, width, feat, mid)
        flat_shape = (height * width, slots * feat // 128, 128)
        hbm = pl.BlockSpec(memory_space=pltpu.HBM)
        vmem = pl.BlockSpec(memory_space=pltpu.VMEM)
        dma = pltpu.SemaphoreType.DMA
        depths = list(enumerate((8, 4, 16, 16, 4, 4)))
        matrix, third = mid * feat // 128, 3 * mid * mid // 128
        sizes = [matrix, third, third, third, matrix]

        tiled = args[0].transpose(1, 2, 0, 3).reshape(height, width, slots, feat // 128, 128)
        tiled = tiled.transpose(0, 1, 3, 2, 4).reshape(flat_shape)
        given = [pltpu.with_memory_space_constraint(part, pltpu.HBM) for part in (tiled, *args[1:])]

        vm = pltpu.VMEM
        narrow, broad, square = vm((mid,), F32), vm((feat,), F32), vm((rows, mid), F32)
        ints = pltpu.SMEM((slots,), jnp.int32)
        plan = [matrix // 2] * 2 + [third] * 3 + [matrix // 4] * 4
        outs = dict(
            gf=vm(flat_shape, BF16), vectors_c=vm((16, 128), F32), vectors=vm((16, 128), F32),
            e=vm((matrix, 128), F32), s0=vm((third, 128), F32), s1=vm((third, 128), F32), s2=vm((third, 128), F32),
            r=vm((matrix, 128), F32),
        )
        scratch = dict(
            f4=vm((flat_shape[0] + SIDE - width, *flat_shape[1:]), BF16),
            fp=vm((rows, feat), BF16), ft=vm((feat, rows), BF16),
            wr=vm((feat, mid), BF16), ws=vm((3, 3, mid, mid), BF16), wc=vm((3, mid, 3 * mid), BF16), we=vm((mid, feat), BF16),
            valid=ints, vs=pltpu.SMEM((slots,), F32), clip=ints, segment=ints, share=pltpu.SMEM(args[13].shape, F32),
            ga=narrow, ba=narrow, gb=narrow, bb=narrow, gc=broad, bc=broad, loss=broad,
            xp=vm((rows + 2 * SIDE, 3 * mid), BF16), xt=vm((mid, rows), BF16),
            hb=vm((rows, mid), BF16), hbt=vm((mid, rows), BF16),
            pre_a=square, slope_a=square, pre_b=square, slope_b=square, grad_a=square, grad_b=square,
            pre_c=vm((rows, feat), F32), slope_c=vm((rows, feat), F32), back=vm((rows, feat), F32),
            gpc=vm((rows, feat), BF16), g3=vm((rows + 2 * SIDE, 3 * mid), BF16), gpa=vm((rows, mid), BF16),
            table_a=vm((8, mid), F32), table_b=vm((8, mid), F32),
            table_c=vm((8, feat), F32), coef=vm((8, feat), F32), dense=vm((8, 128), F32),
            pool=vm((6, 32, 128), F32), slope_sum=vm((3, 8, 128), F32), slope_hat=vm((3, 8, 128), F32),
            near=[vm((n if n <= 32 and at not in (2, 3) else 8, deep, 128), F32) for at, deep in depths],
            wide=[vm((outer, deep, 128), F32) for at, deep in depths],
            plane=vm((outer, 8, 128), F32),
            part=[vm((size, 128), F32) for size in sizes],
            rb0=[vm((size // 2, 128), F32) for size in plan],
            rb1=[vm((size // 4, 128), F32) for size in plan],
            rb2=[vm((size // 8, 128), F32) for size in plan],
            rb3=[vm(((quad - 1) * size // (8 * quad), 128), F32) for size in plan],
            rb4=[vm((far, size // (8 * quad), 128), F32) for size in plan if far > 1],
            load_sem=dma((16,)), near_s=dma((6,)), near_r=dma((6,)), wide_s=dma((6,)), wide_r=dma((6,)),
            pool_s=dma((1,)), pool_r=dma((1,)), chunk_s=dma((9, 3)), chunk_r=dma((9, 9)),
        )
        names = (*arg_names(), *outs, *scratch)

        def kernel(*refs):
            t = Step(cfg, SimpleNamespace(**dict(zip(names, refs, strict=True))))
            prologue(t)
            backward(t, *forward(t))

        results = pl.pallas_call(
            kernel,
            out_shape=list(outs.values()),
            in_specs=[hbm] * len(given),
            out_specs=[vmem] * len(outs),
            scratch_shapes=list(scratch.values()),
            compiler_params=pltpu.CompilerParams(
                collective_id=0, has_side_effects=True, vmem_limit_bytes=50 * 1024 * 1024
            ),
        )(*given)
        vector = jax.ShapeDtypeStruct((mid,), F32)
        wide_vector = jax.ShapeDtypeStruct((feat,), F32)
        flat_grad, *rest = pl.pallas_call(
            store,
            out_shape=[
                jax.ShapeDtypeStruct(flat_shape, BF16),
                jax.ShapeDtypeStruct((feat, mid), F32),
                jax.ShapeDtypeStruct((3, 3, mid, mid), F32),
                jax.ShapeDtypeStruct((mid, feat), F32),
                vector, vector, vector, vector, wide_vector, wide_vector,
            ],
            in_specs=[vmem] * 8,
            out_specs=[hbm] * 10,
            scratch_shapes=[*(vm((c,), F32) for c in (feat, feat, mid, mid, mid, mid)), dma((12,))],
            compiler_params=pltpu.CompilerParams(vmem_limit_bytes=8 * 1024 * 1024),
        )(*(pltpu.with_memory_space_constraint(part, pltpu.VMEM) for part in results))
        grad_frames = flat_grad.reshape(height, width, feat // 128, slots, 128).transpose(0, 1, 3, 2, 4)
        return grad_frames.reshape(height, width, slots, feat).transpose(2, 0, 1, 3), *rest

    split = P("clip")
    in_specs = (split,) + (P(),) * 9 + (split,) * 3 + (P(), P())
    out_specs = (split,) + (P(),) * 9
    return jax.shard_map(shards, mesh=mesh, in_specs=in_specs, out_specs=out_specs, check_vma=False)


def arg_names():
    return dict(
        frames=0, w_reduce=0, w_spatial=0, w_expand=0, gain_a=0, bias_a=0, gain_b=0, bias_b=0, gain_c=0, bias_c=0,
        clip_ids=0, segment_ids=0, slot_valid=0, segment_weight=0, loss_weight=0,
    )
```

```python
import functools
from types import SimpleNamespace

import jax
import jax.numpy as jnp
from jax import lax
from jax.experimental import pallas as pl
from jax.experimental.pallas import tpu as pltpu
from jax.sharding import PartitionSpec as P

MESH = pl.DeviceIdType.MESH
EPS = 1e-05
F32 = jnp.float32
BF16 = jnp.bfloat16
SIDE = 16
ROWS = SIDE * SIDE
NN = (((1,), (0,)), ((), ()))
NT = (((1,), (1,)), ((), ()))

ORDER = (
    (),
    (),
    (),
    (),
    (),
    (),
    (0, 1,),
    (2, 0,),
    (1,),
    (2, 0, 1, 3,),
    (2, 4,),
    (),
    (),
    (0,),
    (1, 3, 5, 2, 4,),
    (6, 3, 8,),
    (1, 0, 5, 7, 4, 8, 1, 3, 6, 7, 8, 2, 0,),
    (4, 7, 3,),
    (6, 2, 8, 1, 5, 0, 4, 7, 3, 6, 8, 5, 7, 1, 6, 4,),
    (5, 6, 0, 3,),
    (7,),
    (8, 2, 4, 5, 7, 8, 6, 3, 5,),
    (7, 8, 6, 5, 4, 2,),
)


def dot(a, b, dims=NN):
    return lax.dot_general(a, b, dims, preferred_element_type=F32)


def wait_bytes(ref, sem):
    pltpu.make_async_copy(ref, ref, sem).wait()


def by_rows(ref, value):
    for k in range(ref.shape[0] // 256):
        ref[k * 256 : (k + 1) * 256, :] = value(slice(k * 256, (k + 1) * 256))


def moved_rows(here, at):
    return slice(here.start + at, here.stop + at)


def block(k, y):
    return pl.multiple_of(k * ROWS + y * SIDE, SIDE)


def to_dense(ref, at, value, first):
    for q in range(value.shape[1] // 128):
        ref[at, pl.ds(first + q, 1), :] = value[:, q * 128 : (q + 1) * 128]


def row_form(ref, row, source, first, count):
    for q in range(count):
        ref[row : row + 1, q * 128 : (q + 1) * 128] = source[first + q : first + q + 1, :]


def three(ref, at, left, middle, right):
    here, wide = pl.ds(at + SIDE, SIDE), middle.shape[1]
    ref[here, 0:wide] = left.astype(BF16)
    ref[here, wide : 2 * wide] = middle.astype(BF16)
    ref[here, 2 * wide : 3 * wide] = right.astype(BF16)


def dense_of(ref1, scratch):
    count = ref1.shape[0] // 128
    for q in range(count):
        scratch[q : q + 1, :] = ref1[q * 128 : (q + 1) * 128].reshape(1, 128)
    return scratch[0:count, :]


class Step:
    def __init__(self, cfg, r):
        self.r, self.sizes = r, cfg
        self.n, self.slots, self.height, self.width, self.feat, self.mid = cfg
        self.live = self.slots - 1
        self.rows = self.live * ROWS
        self.area = self.height * self.width
        self.inner = 8
        self.outer = self.n // 8
        self.quad = min(4, self.outer)
        self.far = self.outer // self.quad
        self.loads = {}
        self.mask = lax.broadcasted_iota(jnp.int32, (SIDE, 256), 0) < self.width

    def load(self, **pairs):
        for name, (src, dst) in pairs.items():
            copy = pltpu.make_async_copy(src, dst, self.r.load_sem.at[len(self.loads)])
            copy.start()
            self.loads[name] = copy

    def loaded(self, **names):
        for name in names:
            self.loads[name].wait()

    def fold(self, value):
        return jnp.sum(jnp.where(self.mask, value, 0.0), axis=0, keepdims=True)

    def slot_facts(self):
        r, live = self.r, self.live
        alive, later = 1, []
        for k in range(live):
            alive = alive * r.valid[k]
            later.append(1 - alive)
        self.keep = [(1 - q).astype(F32) for q in later]
        self.moved = [q.astype(F32) for q in later]
        self.later = later
        self.v = [self.kept(r.valid, k) for k in range(live)]
        self.n_own = (self.v[0] + self.v[1] + self.v[2]) * float(self.area)

    def kept(self, values, k):
        return (values[k] + self.later[k] * (values[k + 1] - values[k])).astype(F32)

    def places(self):
        n = self.n
        self.me = me = lax.axis_index("clip")
        self.low, self.high = low, high = me % self.inner, me // self.inner
        self.direct = n <= 32
        self.peers = flips(me, n)
        self.low_peers = flips(me, self.inner)
        self.high_peers = flips(me, self.outer, self.inner)
        self.clip_peers = [(me + o) % n for o in (n // 2 - 1, n // 2 + 1, n // 2, n - 1, 1)]

    def greet(self):
        self.greeted = self.peers if self.direct else self.low_peers + self.high_peers + self.clip_peers
        self.barrier = pltpu.get_barrier_semaphore()
        for device in self.greeted:
            pl.semaphore_signal(self.barrier, inc=1, device_id=(device,), device_id_type=MESH)

    def all_here(self):
        pl.semaphore_wait(self.barrier, len(self.greeted))

    def send(self, src, dst, ssem, rsem, device):
        pltpu.make_async_remote_copy(
            src_ref=src, dst_ref=dst, send_sem=ssem, recv_sem=rsem, device_id=(device,), device_id_type=MESH
        ).start()

    def one_stage(self, at):
        return self.direct and at not in (2, 3)

    def near_at(self, at):
        return self.me if self.one_stage(at) else self.low

    def near_send(self, at):
        buf, mine = self.r.near[at], self.near_at(at)
        for device in self.peers if self.one_stage(at) else self.low_peers:
            self.send(buf.at[mine], buf.at[mine], self.r.near_s.at[at], self.r.near_r.at[at], device)

    def near_wait(self, at, sems):
        buf = self.r.near[at]
        wait_bytes(buf.at[pl.ds(0, buf.shape[0] - 1)], sems.at[at])

    def wide_send(self, at):
        buf = self.r.wide[at]
        for device in self.high_peers:
            self.send(buf.at[self.high], buf.at[self.high], self.r.wide_s.at[at], self.r.wide_r.at[at], device)

    def wide_wait(self, at, sems):
        wait_bytes(self.r.wide[at].at[pl.ds(0, self.outer - 1)], sems.at[at])

    def all_sent(self, *rounds):
        for at in rounds:
            self.near_wait(at, self.r.near_s)
            if not self.one_stage(at):
                self.wide_wait(at, self.r.wide_s)

    def near_count(self, q):
        return self.r.near[0][(self.me - self.low + q) if self.direct else q, 4:5, :]

    def wide_count(self, q):
        return self.r.plane[q, 0:1, :] if self.direct else self.r.wide[0][q, 4:5, :]

    def stats_near(self, at, count):
        if self.one_stage(at):
            return
        self.near_wait(at, self.r.near_r)
        n_all, s_all, _, spread = combine(self.r.near[at], self.near_count, self.inner, count)
        buf = self.r.wide[at]
        buf[self.high, 0:count, :] = s_all
        buf[self.high, count : 2 * count, :] = spread
        if at == 0:
            buf[self.high, 4:5, :] = n_all
        self.wide_send(at)

    def stats_wide(self, at, count, table):
        r = self.r
        if self.one_stage(at):
            self.near_wait(at, r.near_r)
            counts = r.near[0]
            n_all, _, mean, spread = combine(r.near[at], lambda q: counts[q, 4:5, :], self.n, count)
            if at == 0:
                for q in range(self.outer):
                    r.plane[q, 0:1, :] = sum(counts[q * self.inner + m, 4:5, :] for m in range(self.inner))
        else:
            self.wide_wait(at, r.wide_r)
            n_all, _, mean, spread = combine(r.wide[at], self.wide_count, self.outer, count)
        inverse = lax.rsqrt(spread / n_all + EPS)
        r.dense[0:count, :] = mean
        row_form(table, 0, r.dense, 0, count)
        r.dense[0:count, :] = inverse
        row_form(table, 1, r.dense, 0, count)
        return n_all, inverse

    def sums_near(self, at):
        if not self.one_stage(at):
            self.near_wait(at, self.r.near_r)
            self.r.wide[at][self.high] = total(self.r.near[at])
            self.wide_send(at)

    def sums_wide(self, at):
        if self.one_stage(at):
            self.near_wait(at, self.r.near_r)
            return total(self.r.near[at])
        self.wide_wait(at, self.r.wide_r)
        return total(self.r.wide[at])

    def local_stats(self, buf, at, ref):
        channels = ref.shape[1]
        count = channels // 128
        for c in range(channels // 256):
            lanes = slice(c * 256, (c + 1) * 256)

            def gather(term):
                acc = jnp.zeros((SIDE, 256), F32)
                for k in range(self.live):
                    part = lax.fori_loop(
                        0, self.height, lambda y, a: a + term(ref[pl.ds(block(k, y), SIDE), lanes]),
                        jnp.zeros((SIDE, 256), F32), unroll=self.height,
                    )
                    acc = acc + part * self.v[k]
                return self.fold(acc)

            s_own = gather(lambda x: x)
            mean = s_own / jnp.maximum(self.n_own, 1.0)
            to_dense(buf, at, s_own, 2 * c)
            to_dense(buf, at, gather(lambda x: (x - mean) * (x - mean)), count + 2 * c)

    def norm_silu(self, ref, slope_ref, table, gain, bias, write):
        centre, scale = table[0:1, :], table[1:2, :] * gain[...].reshape(1, self.mid)
        b = bias[...].reshape(1, self.mid)
        for k in range(self.live):
            def step(y, carry):
                at = block(k, y)
                u = (ref[pl.ds(at, SIDE), :] - centre) * scale + b
                s = 0.5 * jnp.tanh(0.5 * u) + 0.5
                h = u * s
                slope_ref[pl.ds(at, SIDE), :] = jnp.where(self.mask, s + (h - h * s), 0.0)
                write(at, jnp.where(self.mask, h, 0.0))
                return carry

            lax.fori_loop(0, self.height, step, 0, unroll=self.height)


def flips(index, count, stride=1):
    steps, at = [], 1
    while at < count:
        steps.append(at * stride * (1 - 2 * ((index // (at * stride)) % 2)))
        at *= 2
    return [sum((d for b, d in enumerate(steps) if o >> b & 1), index) for o in reversed(range(1, count))]


def combine(buf, counts, group, count):
    n_part = [counts(q) for q in range(group)]
    s_part = [buf[q, 0:count, :] for q in range(group)]
    n_all = sum(n_part[1:], n_part[0])
    s_all = sum(s_part[1:], s_part[0])
    mean = s_all / jnp.maximum(n_all, 1.0)
    spread = jnp.zeros((count, 128), F32)
    for q in range(group):
        gap = s_part[q] / jnp.maximum(n_part[q], 1.0) - mean
        spread = spread + (buf[q, count : 2 * count, :] + n_part[q] * gap * gap)
    return n_all, s_all, mean, spread


def total(buf):
    out = buf[0]
    for q in range(1, buf.shape[0]):
        out = out + buf[q]
    return out


def clear(*refs):
    for ref in refs:
        ref[...] = jnp.zeros(ref.shape, ref.dtype)


def prologue(t):
    r, slots, live, width, feat = t.r, t.slots, t.live, t.width, t.feat
    t.places()
    t.greet()
    t.load(
        frames=(r.frames, r.f4.at[pl.ds(0, t.area)]), valid=(r.slot_valid, r.valid), reduce=(r.w_reduce, r.wr)
    )
    r.f4[t.area :] = jnp.zeros((r.f4.shape[0] - t.area, *r.f4.shape[1:]), BF16)
    clear(r.fp)
    t.loaded(valid=0)
    t.slot_facts()
    t.loaded(frames=0)
    t.load(
        clip=(r.clip_ids, r.clip), segment=(r.segment_ids, r.segment),
        share=(r.segment_weight, r.share), spatial=(r.w_spatial, r.ws), expand=(r.w_expand, r.we),
        ga=(r.gain_a, r.ga), ba=(r.bias_a, r.ba), gb=(r.gain_b, r.gb), bb=(r.bias_b, r.bb),
        gc=(r.gain_c, r.gc), bc=(r.bias_c, r.bc), loss=(r.loss_weight, r.loss),
    )
    for i in range(3):
        for j in range(3):
            pltpu.make_async_copy(
                r.w_spatial.at[i, j], r.wc.at[i, :, pl.ds(j * t.mid, t.mid)], r.load_sem.at[15]
            ).start()
    fp, f4 = r.fp, r.f4
    tiles = feat // 128
    group = SIDE // slots
    short = lax.broadcasted_iota(jnp.int32, (SIDE, 128), 0) < width

    def regroup(y, carry):
        for p in range(tiles // group):
            value = f4[pl.ds(y * width, SIDE), p * SIDE : (p + 1) * SIDE, :].astype(F32)
            value = jnp.swapaxes(value, 0, 1)
            for q in range(group):
                for k in range(live):
                    row = value[q * slots + k] * t.keep[k] + value[q * slots + k + 1] * t.moved[k]
                    lanes = slice((p * group + q) * 128, (p * group + q + 1) * 128)
                    fp[pl.ds(block(k, y), SIDE), lanes] = jnp.where(short, row, 0.0).astype(BF16)
        return carry

    lax.fori_loop(0, t.height, regroup, 0)
    t.loaded(reduce=0)
    by_rows(r.pre_a, lambda here: dot(fp[here, :], r.wr[...]))
    t.local_stats(r.near[0], t.near_at(0), r.pre_a)
    r.near[0][t.near_at(0), 4:5, :] = jnp.full((1, 128), t.n_own, F32)


def forward(t):
    r, live, mid, feat, rows, area, height = t.r, t.live, t.mid, t.feat, t.rows, t.area, t.height

    def turn(q):
        lanes = slice(q * feat // 4, (q + 1) * feat // 4)
        r.ft[lanes, :] = r.fp[:, lanes].T

    t.all_here()
    t.near_send(0)
    turn(0)
    t.stats_near(0, mid // 128)
    clear(r.xp, r.hb, r.g3, r.gpc, r.gpa)
    t.loaded(clip=0, segment=0, share=0, ga=0, ba=0, gb=0, bb=0, gc=0, bc=0, loss=0, spatial=0, expand=0)
    key = [t.kept(r.clip, k) for k in range(live)]
    weight = []
    for k in range(live):
        at = t.kept(r.segment, k)
        w0, w1, w2 = (r.share[q] for q in range(3))
        weight.append(
            t.v[k] * (w0 * ((1.0 - at) * (2.0 - at) * 0.5) + w1 * (at * (2.0 - at)) + w2 * (at * (at - 1.0) * 0.5))
        )
    n_all, inv_a = t.stats_wide(0, mid // 128, r.table_a)

    xp, hb = r.xp, r.hb

    def write_a(at, h):
        three(xp, at, pltpu.roll(h, 1, 0), h, pltpu.roll(h, SIDE - 1, 0))

    t.norm_silu(r.pre_a, r.slope_a, r.table_a, r.ga, r.ba, write_a)

    by_rows(
        r.pre_b,
        lambda here: sum(dot(xp[moved_rows(here, i * SIDE), :], r.ws[i].reshape(3 * mid, mid)) for i in range(3)),
    )
    t.local_stats(r.near[1], t.near_at(1), r.pre_b)
    t.near_send(1)
    r.xt[...] = xp[SIDE : SIDE + rows, mid : 2 * mid].T
    t.stats_near(1, mid // 128)
    _, inv_b = t.stats_wide(1, mid // 128, r.table_b)

    def write_b(at, h):
        hb[pl.ds(at, SIDE), :] = h.astype(BF16)

    t.norm_silu(r.pre_b, r.slope_b, r.table_b, r.gb, r.bb, write_b)

    pre_c, slope_c, fp, table_c = r.pre_c, r.slope_c, r.fp, r.table_c
    by_rows(pre_c, lambda here: dot(hb[here, :], r.we[...]))
    t.local_stats(r.near[2], t.near_at(2), pre_c)
    t.near_send(2)
    r.hbt[...] = hb[...].T
    t.stats_near(2, feat // 128)
    turn(1)
    _, inv_c = t.stats_wide(2, feat // 128, table_c)

    pool, slope_sum, slope_hat = r.pool, r.slope_sum, r.slope_hat
    for c in range(feat // 256):
        lanes = slice(c * 256, (c + 1) * 256)
        centre, inverse = table_c[0:1, lanes], table_c[1:2, lanes]
        g = r.gc[lanes].reshape(1, 256)
        b = r.bc[lanes].reshape(1, 256)
        for k in range(live):
            def step(y, carry):
                a0, a1, a2 = carry
                at = block(k, y)
                hat = (pre_c[pl.ds(at, SIDE), lanes] - centre) * inverse
                u = hat * g + b + fp[pl.ds(at, SIDE), lanes].astype(F32)
                s = 0.5 * jnp.tanh(0.5 * u) + 0.5
                h = u * s
                slope = s + (h - h * s)
                slope_c[pl.ds(at, SIDE), lanes] = slope
                return a0 + h, a1 + slope, a2 + slope * hat

            zero = jnp.zeros((SIDE, 256), F32)
            a0, a1, a2 = lax.fori_loop(0, height, step, (zero, zero, zero), unroll=height)
            p_row = (t.fold(a0) * (1.0 / area)).astype(BF16).astype(F32)
            to_dense(pool, 0, p_row, 8 * k + 2 * c)
            to_dense(slope_sum, k, t.fold(a1), 2 * c)
            to_dense(slope_hat, k, t.fold(a2), 2 * c)
    for k in range(live):
        pool[0, 24 + k : 25 + k, :] = jnp.full((1, 128), key[k], F32)
        pool[0, 28 + k : 29 + k, :] = jnp.full((1, 128), weight[k], F32)
    for q, device in enumerate(t.clip_peers):
        t.send(pool.at[0], pool.at[q + 1], r.pool_s.at[0], r.pool_r.at[0], device)
    turn(2)
    wait_bytes(pool.at[pl.ds(1, len(t.clip_peers))], r.pool_r.at[0])

    lw = dense_of(r.loss, r.dense)
    grads = []
    for k in range(live):
        my_key = jnp.full((1, 128), key[k], F32)
        my_weight = jnp.full((1, 128), weight[k], F32)
        mean = jnp.zeros((8, 128), F32)
        den = jnp.zeros((1, 128), F32)
        for q in range(len(t.clip_peers) + 1):
            for m in range(live):
                match = jnp.where(pool[q, 24 + m : 25 + m, :] == my_key, pool[q, 28 + m : 29 + m, :], 0.0)
                den = den + match
                mean = mean + match * pool[q, 8 * m : 8 * m + 8, :]
        den = jnp.where(den == 0.0, 1.0, den)
        mean = mean / den
        power = jnp.sum(jnp.sum(mean * mean, axis=0, keepdims=True), axis=1, keepdims=True)
        along = jnp.sum(jnp.sum(mean * lw, axis=0, keepdims=True), axis=1, keepdims=True)
        scale = lax.rsqrt(power * (1.0 / feat) + EPS)
        mean_grad = scale * (lw - (mean * scale) * (scale * along * (1.0 / feat)))
        grads.append((my_weight / den) * mean_grad * (1.0 / area))

    near3 = r.near[3]
    shift = jnp.zeros((8, 128), F32)
    gain = jnp.zeros((8, 128), F32)
    for k in range(live):
        shift = shift + grads[k] * slope_sum[k]
        gain = gain + grads[k] * slope_hat[k]
    near3[t.near_at(3), 0:8, :] = shift
    near3[t.near_at(3), 8:16, :] = gain
    t.near_send(3)
    coef, dense = r.coef, r.dense
    scale_c = dense_of(r.gc, dense) * inv_c
    for k in range(live):
        dense[...] = grads[k]
        row_form(coef, k, dense, 0, feat // 128)
        dense[...] = grads[k] * scale_c
        row_form(coef, 3 + k, dense, 0, feat // 128)
    t.sums_near(3)
    turn(3)
    both = t.sums_wide(3)
    r.vectors_c[...] = both
    dense[...] = both[0:8] * scale_c / n_all
    row_form(coef, 6, dense, 0, feat // 128)
    dense[...] = both[8:16] * scale_c * inv_c / n_all
    row_form(coef, 7, dense, 0, feat // 128)
    return n_all, inv_a, inv_b


def backward(t, n_all, inv_a, inv_b):
    r, live, mid, feat, rows, height = t.r, t.live, t.mid, t.feat, t.rows, t.height
    slots, width, quad, far, v, wc = t.slots, t.width, t.quad, t.far, t.v, r.wc
    coef, pre_c, slope_c, out = r.coef, r.pre_c, r.slope_c, r.vectors
    me, send = t.me, t.send
    gpc = r.gpc
    for k in range(live):
        for c in range(feat // 256):
            lanes = slice(c * 256, (c + 1) * 256)
            centre = r.table_c[0:1, lanes]
            c0 = coef[3 + k : 4 + k, lanes]
            c1 = coef[6:7, lanes] * v[k]
            c2 = coef[7:8, lanes] * v[k]

            def step(y, carry):
                at = block(k, y)
                grad = slope_c[pl.ds(at, SIDE), lanes] * c0 - (c1 + (pre_c[pl.ds(at, SIDE), lanes] - centre) * c2)
                gpc[pl.ds(at, SIDE), lanes] = grad.astype(BF16)
                return carry

            lax.fori_loop(0, height, step, 0, unroll=height)

    def back_sums(at, table, inv, grad_ref, slope_ref, pre_ref):
        zero = jnp.zeros((SIDE, mid), F32)
        carry = (zero, zero)
        centre = table[0:1, :]
        for k in range(live):
            def step(y, c):
                here = pl.ds(block(k, y), SIDE)
                grad = grad_ref[here, :] * slope_ref[here, :]
                grad_ref[here, :] = grad
                return c[0] + grad, c[1] + grad * (pre_ref[here, :] - centre)

            carry = lax.fori_loop(0, height, step, carry, unroll=height)
        buf = r.near[at]
        to_dense(buf, t.near_at(at), jnp.sum(carry[0], axis=0, keepdims=True), 0)
        to_dense(buf, t.near_at(at), jnp.sum(carry[1], axis=0, keepdims=True) * table[1:2, :], 2)

    def back_apply(at, table, gain_ref, inv, grad_ref, pre_ref, write):
        both = t.sums_wide(at)
        out[8 * at - 32 : 8 * at - 28, :] = both[0:4]
        dense = r.dense
        scale = dense_of(gain_ref, dense) * inv
        dense[0:2, :] = scale
        dense[2:4, :] = both[0:2] * scale / n_all
        dense[4:6, :] = both[2:4] * scale * inv / n_all
        for q in range(3):
            row_form(table, 2 + q, dense, 2 * q, 2)
        centre = table[0:1, :]
        for k in range(live):
            c0, c1, c2 = table[2:3, :], table[3:4, :] * v[k], table[4:5, :] * v[k]

            def step(y, carry):
                at_row = block(k, y)
                here = pl.ds(at_row, SIDE)
                write(at_row, grad_ref[here, :] * c0 - (c1 + (pre_ref[here, :] - centre) * c2))
                return carry

            lax.fori_loop(0, height, step, 0, unroll=height)

    core, bit_x, bit_y, at_z = me % 2, (me // 2) % 2, (me // 4) % 2, (me // 8) % quad
    at_far = me // (8 * quad)
    bit1 = bit_x + core * (bit_y - bit_x)
    bit2 = bit_y + core * (bit_x - bit_y)
    sibling = me + 1 - 2 * core
    peer1 = me + (1 - 2 * bit1) * (2 + 2 * core)
    peer2 = me + (1 - 2 * bit2) * (4 - 2 * core)
    z_at = flips(at_z, quad)
    z_peer = [me + 8 * (q - at_z) for q in z_at]
    far_peer = [me + 8 * quad * ((at_far + o) % far - at_far) for o in range(1, far)]
    chunk_s, chunk_r = r.chunk_s, r.chunk_r
    blocks = iter(ORDER)
    plan = [(0, q, 2) for q in range(2)] + [(1 + q, 0, 1) for q in range(3)] + [(4, q, 4) for q in range(4)]

    def chunk(q):
        name, at, count = plan[q]
        size = r.part[name].shape[0] // count
        part = r.part[name].at[pl.ds(at * size, size)]
        whole = (r.e, r.s0, r.s1, r.s2, r.r)[name].at[pl.ds(at * size, size)]
        half, quarter, eighth, piece = size // 2, size // 4, size // 8, size // (8 * quad)
        m8 = lambda value: pl.multiple_of(value, 8)
        at_h = m8(core * half)
        at_q = m8(at_h + bit1 * quarter)
        at_e = m8(at_q + bit2 * eighth)
        at_p = m8(at_e + at_z * piece)

        def go(step, src, dst, device):
            send(src, dst, chunk_s.at[q, step // 4], chunk_r.at[q, step], device)

        def finish(step, ref):
            wait_bytes(ref, chunk_r.at[q, step])

        rb0, rb1, rb2, rb3 = r.rb0[q], r.rb1[q], r.rb2[q], r.rb3[q]
        go(0, part.at[pl.ds(m8((1 - core) * half), half)], rb0, sibling)
        yield
        finish(0, rb0)
        part[pl.ds(at_h, half), :] = part[pl.ds(at_h, half), :] + rb0[...]
        go(1, part.at[pl.ds(m8(at_h + (1 - bit1) * quarter), quarter)], rb1, peer1)
        yield
        finish(1, rb1)
        part[pl.ds(at_q, quarter), :] = part[pl.ds(at_q, quarter), :] + rb1[...]
        go(2, part.at[pl.ds(m8(at_q + (1 - bit2) * eighth), eighth)], rb2, peer2)
        yield
        finish(2, rb2)
        part[pl.ds(at_e, eighth), :] = part[pl.ds(at_e, eighth), :] + rb2[...]
        for o in range(quad - 1):
            go(3, part.at[pl.ds(m8(at_e + z_at[o] * piece), piece)], rb3.at[pl.ds(o * piece, piece)], z_peer[o])
        yield
        finish(3, rb3)
        own = part[pl.ds(at_p, piece), :]
        for o in range(quad - 1):
            own = own + rb3[o * piece : (o + 1) * piece, :]
        if far > 1:
            rb4 = r.rb4[q]
            rb4[at_far] = own
            for device in far_peer:
                go(8, rb4.at[at_far], rb4.at[at_far], device)
            yield
            finish(8, rb4.at[pl.ds(0, far - 1)])
            own = rb4[0]
            for o in range(1, far):
                own = own + rb4[o]
        whole[pl.ds(at_p, piece), :] = own
        for o in range(quad - 1):
            go(4, whole.at[pl.ds(at_p, piece)], whole.at[pl.ds(at_p, piece)], z_peer[o])
        yield
        finish(4, whole.at[pl.ds(0, (quad - 1) * piece)])
        go(5, whole.at[pl.ds(at_e, eighth)], whole.at[pl.ds(at_e, eighth)], peer2)
        yield
        finish(5, whole.at[pl.ds(0, eighth)])
        go(6, whole.at[pl.ds(at_q, quarter)], whole.at[pl.ds(at_q, quarter)], peer1)
        yield
        finish(6, whole.at[pl.ds(0, quarter)])
        go(7, whole.at[pl.ds(at_h, half)], whole.at[pl.ds(at_h, half)], sibling)
        yield
        finish(7, whole.at[pl.ds(0, half)])
        yield

    chunks = [chunk(q) for q in range(len(plan))]

    def go_on(*which):
        for q in which:
            next(chunks[q])

    def go_on_all():
        go_on(*next(blocks))

    pre_a, slope_a, pre_b, slope_b, hbt, xt = r.pre_a, r.slope_a, r.pre_b, r.slope_b, r.hbt, r.xt
    we, wr, back = r.we, r.wr, r.back
    tiles = feat // 128
    group = SIDE // slots
    keep, moved, mask = t.keep, t.moved, t.mask
    grad_b, grad_a = r.grad_b, r.grad_a
    wait_bytes(wc, r.load_sem.at[15])
    g3 = r.g3

    def write_gb(at, grad):
        grad = jnp.where(mask, grad, 0.0)
        three(g3, at, pltpu.roll(grad, SIDE - 1, 0), grad, pltpu.roll(grad, 1, 0))

    def spatial_part(i):
        go_on_all()
        value = dot(xt[...], g3[(2 - i) * SIDE : (2 - i) * SIDE + rows, :])
        for j in range(3):
            r.part[1 + i][j * mid : (j + 1) * mid, :] = value[:, j * mid : (j + 1) * mid]
        go_on(2 + i)

    go_on_all()
    go_on_all()
    by_rows(grad_b, lambda here: dot(gpc[here, :], we[...], NT))
    back_sums(4, r.table_b, inv_b, grad_b, slope_b, pre_b)
    t.near_send(4)
    for e in range(2):
        go_on_all()
        for q in range(2 * e, 2 * e + 2):
            lanes = slice(q * 256, (q + 1) * 256)
            r.part[0][e * mid : (e + 1) * mid, q % 2 * 256 : (q % 2 + 1) * 256] = dot(hbt[...], gpc[:, lanes])
        go_on(e)
    t.sums_near(4)
    go_on_all()
    back_apply(4, r.table_b, r.gb, inv_b, grad_b, pre_b, write_gb)
    spatial_part(0)
    go_on_all()
    by_rows(
        grad_a, lambda here: sum(dot(g3[moved_rows(here, (2 - i) * SIDE), :], wc[i], NT) for i in range(3))
    )
    back_sums(5, r.table_a, inv_a, grad_a, slope_a, pre_a)
    t.near_send(5)
    spatial_part(1)
    t.sums_near(5)
    spatial_part(2)
    go_on_all()
    gpa = r.gpa

    def write_ga(at, grad):
        gpa[pl.ds(at, SIDE), :] = grad.astype(BF16)

    back_apply(5, r.table_a, r.ga, inv_a, grad_a, pre_a, write_ga)
    for q in range(4):
        go_on_all()
        r.part[4][q * 256 : (q + 1) * 256, :] = dot(r.ft[q * 256 : (q + 1) * 256, :], gpa[...])
        go_on(5 + q)

    go_on_all()
    by_rows(back, lambda here: dot(gpa[here, :], wr[...], NT))
    gf = r.gf

    def blend(y, carry):
        for p in range(tiles // group):
            values = []
            for q in range(group):
                lanes = slice((p * group + q) * 128, (p * group + q + 1) * 128)
                terms = [
                    slope_c[pl.ds(block(k, y), SIDE), lanes] * coef[k : k + 1, lanes]
                    + back[pl.ds(block(k, y), SIDE), lanes]
                    for k in range(live)
                ]
                values.append(terms[0] * keep[0])
                for m in range(1, live):
                    values.append(terms[m] * keep[m] + terms[m - 1] * moved[m - 1])
                values.append(terms[live - 1] * moved[live - 1])
            value = jnp.swapaxes(jnp.stack(values), 0, 1)
            gf[pl.ds(y * width, width), p * SIDE : (p + 1) * SIDE, :] = value[0:width].astype(BF16)
        return carry

    for q in range(height // 2):
        go_on_all()
        for y in range(2):
            blend(2 * q + y, 0)
    go_on_all()
    for each in chunks:
        for _ in each:
            pass

    t.all_sent(*range(6))
    wait_bytes(r.pool.at[pl.ds(1, len(t.clip_peers))], r.pool_s.at[0])
    for q, (name, _, count) in enumerate(plan):
        part = r.part[name]
        piece = part.shape[0] // count // (8 * quad)
        for m, pieces in enumerate((8 * quad - 1, 8 * quad - 1, far - 1)):
            if pieces:
                wait_bytes(part.at[pl.ds(0, pieces * piece)], chunk_s.at[q, m])


def store(gf, vectors_c, vectors, expand, s0, s1, s2, reduce, frames_out, reduce_out, spatial_out, expand_out, *rest):
    ga, ba, gb, bb, gc, bc, *scratch, sem = rest
    vectors_of = (
        (bc, vectors_c, 0), (gc, vectors_c, 8), (bb, vectors, 0), (gb, vectors, 2), (ba, vectors, 8), (ga, vectors, 10)
    )
    pltpu.make_async_copy(gf, frames_out, sem.at[0]).start()
    pltpu.make_async_copy(reduce, reduce_out, sem.at[1]).start()
    depth, width = expand_out.shape
    for q in range(2):
        pltpu.make_async_copy(
            expand.at[pl.ds(q * depth, depth)], expand_out.at[:, pl.ds(q * width // 2, width // 2)], sem.at[2]
        ).start()
    for i, part in enumerate((s0, s1, s2)):
        for j in range(3):
            pltpu.make_async_copy(part.at[pl.ds(j * depth, depth)], spatial_out.at[i, j], sem.at[3 + i]).start()
    for number, (ref, source, first) in enumerate(vectors_of):
        for q in range(ref.shape[0] // 128):
            scratch[number][q * 128 : (q + 1) * 128] = source[first + q : first + q + 1, :].reshape(128)
        pltpu.make_async_copy(scratch[number], ref, sem.at[6 + number]).start()
    wait_bytes(gf, sem.at[0])
    wait_bytes(reduce, sem.at[1])
    wait_bytes(expand, sem.at[2])
    for i, part in enumerate((s0, s1, s2)):
        wait_bytes(part, sem.at[3 + i])
    for number in range(6):
        wait_bytes(scratch[number], sem.at[6 + number])


def solution(mesh):
    n = mesh.shape["clip"]

    def shards(*args):
        slots, height, width, feat = args[0].shape
        mid = args[1].shape[1]
        rows = (slots - 1) * ROWS
        outer = n // 8
        quad = min(4, outer)
        far = outer // quad
        cfg = (n, slots, height, width, feat, mid)
        flat_shape = (height * width, slots * feat // 128, 128)
        hbm = pl.BlockSpec(memory_space=pltpu.HBM)
        vmem = pl.BlockSpec(memory_space=pltpu.VMEM)
        dma = pltpu.SemaphoreType.DMA
        depths = list(enumerate((8, 4, 16, 16, 4, 4)))
        sizes = [(2 * mid, feat // 2)] + [(3 * mid, mid)] * 3 + [(feat, mid)]

        tiled = args[0].transpose(1, 2, 0, 3).reshape(height, width, slots, feat // 128, 128)
        tiled = tiled.transpose(0, 1, 3, 2, 4).reshape(flat_shape)
        given = [pltpu.with_memory_space_constraint(part, pltpu.HBM) for part in (tiled, *args[1:])]

        vm = pltpu.VMEM
        narrow, broad, square = vm((mid,), F32), vm((feat,), F32), vm((rows, mid), F32)
        ints = pltpu.SMEM((slots,), jnp.int32)
        plan = [(mid, feat // 2)] * 2 + [(3 * mid, mid)] * 3 + [(feat // 4, mid)] * 4
        outs = dict(
            gf=vm(flat_shape, BF16), vectors_c=vm((16, 128), F32), vectors=vm((16, 128), F32),
            **{name: vm(size, F32) for name, size in zip(dict(e=0, s0=0, s1=0, s2=0, r=0), sizes)},
        )
        scratch = dict(
            f4=vm((flat_shape[0] + SIDE - width, *flat_shape[1:]), BF16),
            fp=vm((rows, feat), BF16), ft=vm((feat, rows), BF16),
            wr=vm((feat, mid), BF16), ws=vm((3, 3, mid, mid), BF16), wc=vm((3, mid, 3 * mid), BF16), we=vm((mid, feat), BF16),
            valid=ints, clip=ints, segment=ints, share=pltpu.SMEM(args[13].shape, F32),
            ga=narrow, ba=narrow, gb=narrow, bb=narrow, gc=broad, bc=broad, loss=broad,
            xp=vm((rows + 2 * SIDE, 3 * mid), BF16), xt=vm((mid, rows), BF16),
            hb=vm((rows, mid), BF16), hbt=vm((mid, rows), BF16),
            pre_a=square, slope_a=square, pre_b=square, slope_b=square, grad_a=square, grad_b=square,
            pre_c=vm((rows, feat), F32), slope_c=vm((rows, feat), F32), back=vm((rows, feat), F32),
            gpc=vm((rows, feat), BF16), g3=vm((rows + 2 * SIDE, 3 * mid), BF16), gpa=vm((rows, mid), BF16),
            table_a=vm((8, mid), F32), table_b=vm((8, mid), F32),
            table_c=vm((8, feat), F32), coef=vm((8, feat), F32), dense=vm((8, 128), F32),
            pool=vm((6, 32, 128), F32), slope_sum=vm((3, 8, 128), F32), slope_hat=vm((3, 8, 128), F32),
            near=[vm((n if n <= 32 and at not in (2, 3) else 8, deep, 128), F32) for at, deep in depths],
            wide=[vm((outer, deep, 128), F32) for at, deep in depths],
            plane=vm((outer, 8, 128), F32),
            part=[vm(size, F32) for size in sizes],
            rb0=[vm((size // 2, lanes), F32) for size, lanes in plan],
            rb1=[vm((size // 4, lanes), F32) for size, lanes in plan],
            rb2=[vm((size // 8, lanes), F32) for size, lanes in plan],
            rb3=[vm(((quad - 1) * size // (8 * quad), lanes), F32) for size, lanes in plan],
            rb4=[vm((far, size // (8 * quad), lanes), F32) for size, lanes in plan if far > 1],
            load_sem=dma((16,)), near_s=dma((6,)), near_r=dma((6,)), wide_s=dma((6,)), wide_r=dma((6,)),
            pool_s=dma((1,)), pool_r=dma((1,)), chunk_s=dma((9, 3)), chunk_r=dma((9, 9)),
        )
        names = (*arg_names(), *outs, *scratch)

        def kernel(*refs):
            t = Step(cfg, SimpleNamespace(**dict(zip(names, refs, strict=True))))
            prologue(t)
            backward(t, *forward(t))

        results = pl.pallas_call(
            kernel,
            out_shape=list(outs.values()),
            in_specs=[hbm] * len(given),
            out_specs=[vmem] * len(outs),
            scratch_shapes=list(scratch.values()),
            compiler_params=pltpu.CompilerParams(
                collective_id=0, has_side_effects=True, vmem_limit_bytes=50 * 1024 * 1024
            ),
        )(*given)
        vector = jax.ShapeDtypeStruct((mid,), F32)
        wide_vector = jax.ShapeDtypeStruct((feat,), F32)
        flat_grad, *rest = pl.pallas_call(
            store,
            out_shape=[
                jax.ShapeDtypeStruct(flat_shape, BF16),
                jax.ShapeDtypeStruct((feat, mid), F32),
                jax.ShapeDtypeStruct((3, 3, mid, mid), F32),
                jax.ShapeDtypeStruct((mid, feat), F32),
                vector, vector, vector, vector, wide_vector, wide_vector,
            ],
            in_specs=[vmem] * 8,
            out_specs=[hbm] * 10,
            scratch_shapes=[*(vm((c,), F32) for c in (feat, feat, mid, mid, mid, mid)), dma((12,))],
            compiler_params=pltpu.CompilerParams(vmem_limit_bytes=8 * 1024 * 1024),
        )(*(pltpu.with_memory_space_constraint(part, pltpu.VMEM) for part in results))
        grad_frames = flat_grad.reshape(height, width, feat // 128, slots, 128).transpose(0, 1, 3, 2, 4)
        return grad_frames.reshape(height, width, slots, feat).transpose(2, 0, 1, 3), *rest

    split = P("clip")
    in_specs = (split,) + (P(),) * 9 + (split,) * 3 + (P(), P())
    out_specs = (split,) + (P(),) * 9
    return jax.shard_map(shards, mesh=mesh, in_specs=in_specs, out_specs=out_specs, check_vma=False)


def arg_names():
    return dict(
        frames=0, w_reduce=0, w_spatial=0, w_expand=0, gain_a=0, bias_a=0, gain_b=0, bias_b=0, gain_c=0, bias_c=0,
        clip_ids=0, segment_ids=0, slot_valid=0, segment_weight=0, loss_weight=0,
    )
```

```python
import functools
from types import SimpleNamespace

import jax
import jax.numpy as jnp
from jax import lax
from jax.experimental import pallas as pl
from jax.experimental.pallas import tpu as pltpu
from jax.sharding import PartitionSpec as P

MESH = pl.DeviceIdType.MESH
EPS = 1e-05
F32 = jnp.float32
BF16 = jnp.bfloat16
SIDE = 16
ROWS = SIDE * SIDE
NN = (((1,), (0,)), ((), ()))
NT = (((1,), (1,)), ((), ()))

ORDER = (
    (),
    (),
    (),
    (),
    (),
    (),
    (0, 1,),
    (2, 0,),
    (1,),
    (2, 0, 1, 3,),
    (2, 4,),
    (),
    (),
    (0,),
    (1, 3, 5, 2, 4,),
    (6, 3, 8,),
    (1, 0, 5, 7, 4, 8, 1, 3, 6, 7, 8, 2, 0,),
    (4, 7, 3,),
    (6, 2, 8, 1, 5, 0, 4, 7, 3, 6, 8, 5, 7, 1, 6, 4,),
    (5, 6, 0, 3,),
    (7,),
    (8, 2, 4, 5, 7, 8, 6, 3, 5,),
    (7, 8, 6, 5, 4, 2,),
)


def dot(a, b, dims=NN):
    return lax.dot_general(a, b, dims, preferred_element_type=F32)


def wait_bytes(ref, sem):
    pltpu.make_async_copy(ref, ref, sem).wait()


def by_rows(ref, value):
    for k in range(ref.shape[0] // 256):
        ref[k * 256 : (k + 1) * 256, :] = value(slice(k * 256, (k + 1) * 256))


def moved_rows(here, at):
    return slice(here.start + at, here.stop + at)


def block(k, y):
    return pl.multiple_of(k * ROWS + y * SIDE, SIDE)


def to_dense(ref, at, value, first):
    for q in range(value.shape[1] // 128):
        ref[at, pl.ds(first + q, 1), :] = value[:, q * 128 : (q + 1) * 128]


def row_form(ref, row, source, first, count):
    for q in range(count):
        ref[row : row + 1, q * 128 : (q + 1) * 128] = source[first + q : first + q + 1, :]


def three(ref, at, left, middle, right):
    here, wide = pl.ds(at + SIDE, SIDE), middle.shape[1]
    ref[here, 0:wide] = left.astype(BF16)
    ref[here, wide : 2 * wide] = middle.astype(BF16)
    ref[here, 2 * wide : 3 * wide] = right.astype(BF16)


def dense_of(ref1, scratch):
    count = ref1.shape[0] // 128
    for q in range(count):
        scratch[q : q + 1, :] = ref1[q * 128 : (q + 1) * 128].reshape(1, 128)
    return scratch[0:count, :]


class Step:
    def __init__(self, cfg, r):
        self.r, self.sizes = r, cfg
        self.n, self.slots, self.height, self.width, self.feat, self.mid = cfg
        self.live = self.slots - 1
        self.rows = self.live * ROWS
        self.area = self.height * self.width
        self.inner = 8
        self.outer = self.n // 8
        self.quad = min(4, self.outer)
        self.far = self.outer // self.quad
        self.loads = {}
        self.mask = lax.broadcasted_iota(jnp.int32, (SIDE, 256), 0) < self.width

    def load(self, **pairs):
        for name, (src, dst) in pairs.items():
            copy = pltpu.make_async_copy(src, dst, self.r.load_sem.at[len(self.loads)])
            copy.start()
            self.loads[name] = copy

    def loaded(self, **names):
        for name in names:
            self.loads[name].wait()

    def fold(self, value):
        return jnp.sum(jnp.where(self.mask, value, 0.0), axis=0, keepdims=True)

    def slot_facts(self):
        r, live = self.r, self.live
        alive, later = 1, []
        for k in range(live):
            alive = alive * r.valid[k]
            later.append(1 - alive)
        self.keep = [(1 - q).astype(F32) for q in later]
        self.moved = [q.astype(F32) for q in later]
        self.later = later
        self.v = [self.kept(r.valid, k) for k in range(live)]
        self.n_own = (self.v[0] + self.v[1] + self.v[2]) * float(self.area)

    def kept(self, values, k):
        return (values[k] + self.later[k] * (values[k + 1] - values[k])).astype(F32)

    def places(self):
        n = self.n
        self.me = me = lax.axis_index("clip")
        self.low, self.high = low, high = me % self.inner, me // self.inner
        self.direct = n <= 32
        self.peers = flips(me, n)
        self.low_peers = flips(me, self.inner)
        self.high_peers = flips(me, self.outer, self.inner)
        self.clip_peers = [(me + o) % n for o in (n // 2 - 1, n // 2 + 1, n // 2, n - 1, 1)]

    def greet(self):
        self.greeted = self.peers if self.direct else self.low_peers + self.high_peers + self.clip_peers
        self.barrier = pltpu.get_barrier_semaphore()
        for device in self.greeted:
            pl.semaphore_signal(self.barrier, inc=1, device_id=(device,), device_id_type=MESH)

    def all_here(self):
        pl.semaphore_wait(self.barrier, len(self.greeted))

    def send(self, src, dst, ssem, rsem, device):
        pltpu.make_async_remote_copy(
            src_ref=src, dst_ref=dst, send_sem=ssem, recv_sem=rsem, device_id=(device,), device_id_type=MESH
        ).start()

    def one_stage(self, at):
        return self.direct and at not in (2, 3)

    def near_at(self, at):
        return self.me if self.one_stage(at) else self.low

    def near_send(self, at):
        buf, mine = self.r.near[at], self.near_at(at)
        for device in self.peers if self.one_stage(at) else self.low_peers:
            self.send(buf.at[mine], buf.at[mine], self.r.near_s.at[at], self.r.near_r.at[at], device)

    def near_wait(self, at, sems):
        buf = self.r.near[at]
        wait_bytes(buf.at[pl.ds(0, buf.shape[0] - 1)], sems.at[at])

    def wide_send(self, at):
        buf = self.r.wide[at]
        for device in self.high_peers:
            self.send(buf.at[self.high], buf.at[self.high], self.r.wide_s.at[at], self.r.wide_r.at[at], device)

    def wide_wait(self, at, sems):
        wait_bytes(self.r.wide[at].at[pl.ds(0, self.outer - 1)], sems.at[at])

    def all_sent(self, *rounds):
        for at in rounds:
            self.near_wait(at, self.r.near_s)
            if not self.one_stage(at):
                self.wide_wait(at, self.r.wide_s)

    def near_count(self, q):
        return self.r.near[0][(self.me - self.low + q) if self.direct else q, 4:5, :]

    def wide_count(self, q):
        return self.r.plane[q, 0:1, :] if self.direct else self.r.wide[0][q, 4:5, :]

    def stats_near(self, at, count):
        if self.one_stage(at):
            return
        self.near_wait(at, self.r.near_r)
        n_all, s_all, _, spread = combine(self.r.near[at], self.near_count, self.inner, count)
        buf = self.r.wide[at]
        buf[self.high, 0:count, :] = s_all
        buf[self.high, count : 2 * count, :] = spread
        if at == 0:
            buf[self.high, 4:5, :] = n_all
        self.wide_send(at)

    def stats_wide(self, at, count, table):
        r = self.r
        if self.one_stage(at):
            self.near_wait(at, r.near_r)
            counts = r.near[0]
            n_all, _, mean, spread = combine(r.near[at], lambda q: counts[q, 4:5, :], self.n, count)
            if at == 0:
                for q in range(self.outer):
                    r.plane[q, 0:1, :] = sum(counts[q * self.inner + m, 4:5, :] for m in range(self.inner))
        else:
            self.wide_wait(at, r.wide_r)
            n_all, _, mean, spread = combine(r.wide[at], self.wide_count, self.outer, count)
        inverse = lax.rsqrt(spread / n_all + EPS)
        r.dense[0:count, :] = mean
        row_form(table, 0, r.dense, 0, count)
        r.dense[0:count, :] = inverse
        row_form(table, 1, r.dense, 0, count)
        return n_all, inverse

    def sums_near(self, at):
        if not self.one_stage(at):
            self.near_wait(at, self.r.near_r)
            self.r.wide[at][self.high] = total(self.r.near[at])
            self.wide_send(at)

    def sums_wide(self, at):
        if self.one_stage(at):
            self.near_wait(at, self.r.near_r)
            return total(self.r.near[at])
        self.wide_wait(at, self.r.wide_r)
        return total(self.r.wide[at])

    def local_stats(self, buf, at, ref):
        channels = ref.shape[1]
        count = channels // 128
        for c in range(channels // 256):
            lanes = slice(c * 256, (c + 1) * 256)

            def gather(term):
                acc = jnp.zeros((SIDE, 256), F32)
                for k in range(self.live):
                    part = lax.fori_loop(
                        0, self.height, lambda y, a: a + term(ref[pl.ds(block(k, y), SIDE), lanes]),
                        jnp.zeros((SIDE, 256), F32), unroll=self.height,
                    )
                    acc = acc + part * self.v[k]
                return self.fold(acc)

            s_own = gather(lambda x: x)
            mean = s_own / jnp.maximum(self.n_own, 1.0)
            to_dense(buf, at, s_own, 2 * c)
            to_dense(buf, at, gather(lambda x: (x - mean) * (x - mean)), count + 2 * c)

    def norm_silu(self, ref, slope_ref, table, gain, bias, write):
        centre, scale = table[0:1, :], table[1:2, :] * gain[...].reshape(1, self.mid)
        b = bias[...].reshape(1, self.mid)
        for k in range(self.live):
            def step(y, carry):
                at = block(k, y)
                u = (ref[pl.ds(at, SIDE), :] - centre) * scale + b
                s = 0.5 * jnp.tanh(0.5 * u) + 0.5
                h = u * s
                slope_ref[pl.ds(at, SIDE), :] = jnp.where(self.mask, s + (h - h * s), 0.0)
                write(at, jnp.where(self.mask, h, 0.0))
                return carry

            lax.fori_loop(0, self.height, step, 0, unroll=self.height)


def flips(index, count, stride=1):
    steps, at = [], 1
    while at < count:
        steps.append(at * stride * (1 - 2 * ((index // (at * stride)) % 2)))
        at *= 2
    return [sum((d for b, d in enumerate(steps) if o >> b & 1), index) for o in reversed(range(1, count))]


def combine(buf, counts, group, count):
    n_part = [counts(q) for q in range(group)]
    s_part = [buf[q, 0:count, :] for q in range(group)]
    n_all = sum(n_part[1:], n_part[0])
    s_all = sum(s_part[1:], s_part[0])
    mean = s_all / jnp.maximum(n_all, 1.0)
    spread = jnp.zeros((count, 128), F32)
    for q in range(group):
        gap = s_part[q] / jnp.maximum(n_part[q], 1.0) - mean
        spread = spread + (buf[q, count : 2 * count, :] + n_part[q] * gap * gap)
    return n_all, s_all, mean, spread


def total(buf):
    out = buf[0]
    for q in range(1, buf.shape[0]):
        out = out + buf[q]
    return out


def clear(*refs):
    for ref in refs:
        ref[...] = jnp.zeros(ref.shape, ref.dtype)


def prologue(t):
    r, slots, live, width, feat = t.r, t.slots, t.live, t.width, t.feat
    t.places()
    t.greet()
    t.load(
        frames=(r.frames, r.f4.at[pl.ds(0, t.area)]), valid=(r.slot_valid, r.valid), reduce=(r.w_reduce, r.wr)
    )
    r.f4[t.area :] = jnp.zeros((r.f4.shape[0] - t.area, *r.f4.shape[1:]), BF16)
    clear(r.fp)
    t.loaded(valid=0)
    t.slot_facts()
    t.loaded(frames=0)
    t.load(
        clip=(r.clip_ids, r.clip), segment=(r.segment_ids, r.segment),
        share=(r.segment_weight, r.share), spatial=(r.w_spatial, r.ws), expand=(r.w_expand, r.we),
        ga=(r.gain_a, r.ga), ba=(r.bias_a, r.ba), gb=(r.gain_b, r.gb), bb=(r.bias_b, r.bb),
        gc=(r.gain_c, r.gc), bc=(r.bias_c, r.bc), loss=(r.loss_weight, r.loss),
    )
    for i in range(3):
        for j in range(3):
            pltpu.make_async_copy(
                r.w_spatial.at[i, j], r.wc.at[i, :, pl.ds(j * t.mid, t.mid)], r.load_sem.at[15]
            ).start()
    fp, f4 = r.fp, r.f4
    tiles = feat // 128
    group = SIDE // slots
    short = lax.broadcasted_iota(jnp.int32, (SIDE, 128), 0) < width

    def regroup(y, carry):
        for p in range(tiles // group):
            value = f4[pl.ds(y * width, SIDE), p * SIDE : (p + 1) * SIDE, :].astype(F32)
            value = jnp.swapaxes(value, 0, 1)
            for q in range(group):
                for k in range(live):
                    row = value[q * slots + k] * t.keep[k] + value[q * slots + k + 1] * t.moved[k]
                    lanes = slice((p * group + q) * 128, (p * group + q + 1) * 128)
                    fp[pl.ds(block(k, y), SIDE), lanes] = jnp.where(short, row, 0.0).astype(BF16)
        return carry

    lax.fori_loop(0, t.height, regroup, 0)
    t.loaded(reduce=0)
    by_rows(r.pre_a, lambda here: dot(fp[here, :], r.wr[...]))
    t.local_stats(r.near[0], t.near_at(0), r.pre_a)
    r.near[0][t.near_at(0), 4:5, :] = jnp.full((1, 128), t.n_own, F32)


def forward(t):
    r, live, mid, feat, rows, area, height = t.r, t.live, t.mid, t.feat, t.rows, t.area, t.height

    def turn(q):
        lanes = slice(q * feat // 4, (q + 1) * feat // 4)
        r.ft[lanes, :] = r.fp[:, lanes].T

    t.all_here()
    t.near_send(0)
    turn(0)
    t.stats_near(0, mid // 128)
    clear(r.xp, r.hb, r.g3, r.gpc, r.gpa)
    t.loaded(clip=0, segment=0, share=0, ga=0, ba=0, gb=0, bb=0, gc=0, bc=0, loss=0, spatial=0, expand=0)
    key = [t.kept(r.clip, k) for k in range(live)]
    weight = []
    for k in range(live):
        at = t.kept(r.segment, k)
        w0, w1, w2 = (r.share[q] for q in range(3))
        weight.append(
            t.v[k] * (w0 * ((1.0 - at) * (2.0 - at) * 0.5) + w1 * (at * (2.0 - at)) + w2 * (at * (at - 1.0) * 0.5))
        )
    n_all, inv_a = t.stats_wide(0, mid // 128, r.table_a)

    xp, hb = r.xp, r.hb

    def write_a(at, h):
        three(xp, at, pltpu.roll(h, 1, 0), h, pltpu.roll(h, SIDE - 1, 0))

    t.norm_silu(r.pre_a, r.slope_a, r.table_a, r.ga, r.ba, write_a)

    by_rows(
        r.pre_b,
        lambda here: sum(dot(xp[moved_rows(here, i * SIDE), :], r.ws[i].reshape(3 * mid, mid)) for i in range(3)),
    )
    t.local_stats(r.near[1], t.near_at(1), r.pre_b)
    t.near_send(1)
    r.xt[...] = xp[SIDE : SIDE + rows, mid : 2 * mid].T
    t.stats_near(1, mid // 128)
    _, inv_b = t.stats_wide(1, mid // 128, r.table_b)

    def write_b(at, h):
        hb[pl.ds(at, SIDE), :] = h.astype(BF16)

    t.norm_silu(r.pre_b, r.slope_b, r.table_b, r.gb, r.bb, write_b)

    pre_c, slope_c, fp, table_c = r.pre_c, r.slope_c, r.fp, r.table_c
    by_rows(pre_c, lambda here: dot(hb[here, :], r.we[...]))
    t.local_stats(r.near[2], t.near_at(2), pre_c)
    t.near_send(2)
    r.hbt[...] = hb[...].T
    t.stats_near(2, feat // 128)
    turn(1)
    _, inv_c = t.stats_wide(2, feat // 128, table_c)

    pool, slope_sum, slope_hat = r.pool, r.slope_sum, r.slope_hat
    for c in range(feat // 256):
        lanes = slice(c * 256, (c + 1) * 256)
        centre, inverse = table_c[0:1, lanes], table_c[1:2, lanes]
        g = r.gc[lanes].reshape(1, 256)
        b = r.bc[lanes].reshape(1, 256)
        for k in range(live):
            def step(y, carry):
                a0, a1, a2 = carry
                at = block(k, y)
                hat = (pre_c[pl.ds(at, SIDE), lanes] - centre) * inverse
                u = hat * g + b + fp[pl.ds(at, SIDE), lanes].astype(F32)
                s = 0.5 * jnp.tanh(0.5 * u) + 0.5
                h = u * s
                slope = s + (h - h * s)
                slope_c[pl.ds(at, SIDE), lanes] = slope
                return a0 + h, a1 + slope, a2 + slope * hat

            zero = jnp.zeros((SIDE, 256), F32)
            a0, a1, a2 = lax.fori_loop(0, height, step, (zero, zero, zero), unroll=height)
            p_row = (t.fold(a0) * (1.0 / area)).astype(BF16).astype(F32)
            to_dense(pool, 0, p_row, 8 * k + 2 * c)
            to_dense(slope_sum, k, t.fold(a1), 2 * c)
            to_dense(slope_hat, k, t.fold(a2), 2 * c)
    for k in range(live):
        pool[0, 24 + k : 25 + k, :] = jnp.full((1, 128), key[k], F32)
        pool[0, 28 + k : 29 + k, :] = jnp.full((1, 128), weight[k], F32)
    for q, device in enumerate(t.clip_peers):
        t.send(pool.at[0], pool.at[q + 1], r.pool_s.at[0], r.pool_r.at[0], device)
    turn(2)
    wait_bytes(pool.at[pl.ds(1, len(t.clip_peers))], r.pool_r.at[0])

    lw = dense_of(r.loss, r.dense)
    grads = []
    for k in range(live):
        my_key = jnp.full((1, 128), key[k], F32)
        my_weight = jnp.full((1, 128), weight[k], F32)
        mean = jnp.zeros((8, 128), F32)
        den = jnp.zeros((1, 128), F32)
        for q in range(len(t.clip_peers) + 1):
            for m in range(live):
                match = jnp.where(pool[q, 24 + m : 25 + m, :] == my_key, pool[q, 28 + m : 29 + m, :], 0.0)
                den = den + match
                mean = mean + match * pool[q, 8 * m : 8 * m + 8, :]
        den = jnp.where(den == 0.0, 1.0, den)
        mean = mean / den
        power = jnp.sum(jnp.sum(mean * mean, axis=0, keepdims=True), axis=1, keepdims=True)
        along = jnp.sum(jnp.sum(mean * lw, axis=0, keepdims=True), axis=1, keepdims=True)
        scale = lax.rsqrt(power * (1.0 / feat) + EPS)
        mean_grad = scale * (lw - (mean * scale) * (scale * along * (1.0 / feat)))
        grads.append((my_weight / den) * mean_grad * (1.0 / area))

    near3 = r.near[3]
    shift = jnp.zeros((8, 128), F32)
    gain = jnp.zeros((8, 128), F32)
    for k in range(live):
        shift = shift + grads[k] * slope_sum[k]
        gain = gain + grads[k] * slope_hat[k]
    near3[t.near_at(3), 0:8, :] = shift
    near3[t.near_at(3), 8:16, :] = gain
    t.near_send(3)
    coef, dense = r.coef, r.dense
    scale_c = dense_of(r.gc, dense) * inv_c
    for k in range(live):
        dense[...] = grads[k]
        row_form(coef, k, dense, 0, feat // 128)
        dense[...] = grads[k] * scale_c
        row_form(coef, 3 + k, dense, 0, feat // 128)
    t.sums_near(3)
    turn(3)
    both = t.sums_wide(3)
    r.vectors_c[...] = both
    dense[...] = both[0:8] * scale_c / n_all
    row_form(coef, 6, dense, 0, feat // 128)
    dense[...] = both[8:16] * scale_c * inv_c / n_all
    row_form(coef, 7, dense, 0, feat // 128)
    return n_all, inv_a, inv_b


def backward(t, n_all, inv_a, inv_b):
    r, live, mid, feat, rows, height = t.r, t.live, t.mid, t.feat, t.rows, t.height
    slots, width, quad, far, v, wc = t.slots, t.width, t.quad, t.far, t.v, r.wc
    coef, pre_c, slope_c, out = r.coef, r.pre_c, r.slope_c, r.vectors
    me, send = t.me, t.send
    gpc = r.gpc
    for k in range(live):
        for c in range(feat // 256):
            lanes = slice(c * 256, (c + 1) * 256)
            centre = r.table_c[0:1, lanes]
            c0 = coef[3 + k : 4 + k, lanes]
            c1 = coef[6:7, lanes] * v[k]
            c2 = coef[7:8, lanes] * v[k]

            def step(y, carry):
                at = block(k, y)
                grad = slope_c[pl.ds(at, SIDE), lanes] * c0 - (c1 + (pre_c[pl.ds(at, SIDE), lanes] - centre) * c2)
                gpc[pl.ds(at, SIDE), lanes] = grad.astype(BF16)
                return carry

            lax.fori_loop(0, height, step, 0, unroll=height)

    def back_sums(at, table, inv, grad_ref, slope_ref, pre_ref):
        zero = jnp.zeros((SIDE, mid), F32)
        carry = (zero, zero)
        centre = table[0:1, :]
        for k in range(live):
            def step(y, c):
                here = pl.ds(block(k, y), SIDE)
                grad = grad_ref[here, :] * slope_ref[here, :]
                grad_ref[here, :] = grad
                return c[0] + grad, c[1] + grad * (pre_ref[here, :] - centre)

            carry = lax.fori_loop(0, height, step, carry, unroll=height)
        buf = r.near[at]
        to_dense(buf, t.near_at(at), jnp.sum(carry[0], axis=0, keepdims=True), 0)
        to_dense(buf, t.near_at(at), jnp.sum(carry[1], axis=0, keepdims=True) * table[1:2, :], 2)

    def back_apply(at, table, gain_ref, inv, grad_ref, pre_ref, write):
        both = t.sums_wide(at)
        out[8 * at - 32 : 8 * at - 28, :] = both[0:4]
        dense = r.dense
        scale = dense_of(gain_ref, dense) * inv
        dense[0:2, :] = scale
        dense[2:4, :] = both[0:2] * scale / n_all
        dense[4:6, :] = both[2:4] * scale * inv / n_all
        for q in range(3):
            row_form(table, 2 + q, dense, 2 * q, 2)
        centre = table[0:1, :]
        for k in range(live):
            c0, c1, c2 = table[2:3, :], table[3:4, :] * v[k], table[4:5, :] * v[k]

            def step(y, carry):
                at_row = block(k, y)
                here = pl.ds(at_row, SIDE)
                write(at_row, grad_ref[here, :] * c0 - (c1 + (pre_ref[here, :] - centre) * c2))
                return carry

            lax.fori_loop(0, height, step, 0, unroll=height)

    core, bit_x, bit_y, at_z = me % 2, (me // 2) % 2, (me // 4) % 2, (me // 8) % quad
    at_far = me // (8 * quad)
    bit1 = bit_x + core * (bit_y - bit_x)
    bit2 = bit_y + core * (bit_x - bit_y)
    sibling = me + 1 - 2 * core
    peer1 = me + (1 - 2 * bit1) * (2 + 2 * core)
    peer2 = me + (1 - 2 * bit2) * (4 - 2 * core)
    z_at = flips(at_z, quad)
    z_peer = [me + 8 * (q - at_z) for q in z_at]
    far_peer = [me + 8 * quad * ((at_far + o) % far - at_far) for o in range(1, far)]
    chunk_s, chunk_r = r.chunk_s, r.chunk_r
    blocks = iter(ORDER)
    plan = [(0, q, 2) for q in range(2)] + [(1 + q, 0, 1) for q in range(3)] + [(4, q, 4) for q in range(4)]

    def chunk(q):
        name, at, count = plan[q]
        size = r.part[name].shape[0] // count
        part = r.part[name].at[pl.ds(at * size, size)]
        whole = (r.e, r.s0, r.s1, r.s2, r.r)[name].at[pl.ds(at * size, size)]
        half, quarter, eighth, piece = size // 2, size // 4, size // 8, size // (8 * quad)
        m8 = lambda value: pl.multiple_of(value, 8)
        at_h = m8(core * half)
        at_q = m8(at_h + bit1 * quarter)
        at_e = m8(at_q + bit2 * eighth)
        at_p = m8(at_e + at_z * piece)

        def go(step, src, dst, device):
            size = src.shape[0]
            parts = 2 if size % 16 == 0 and size >= 64 else 1
            for m in range(parts):
                here = pl.ds(m * size // parts, size // parts)
                send(src.at[here], dst.at[here], chunk_s.at[q, step // 4], chunk_r.at[q, step], device)

        def finish(step, ref):
            wait_bytes(ref, chunk_r.at[q, step])

        rb0, rb1, rb2, rb3 = r.rb0[q], r.rb1[q], r.rb2[q], r.rb3[q]
        go(0, part.at[pl.ds(m8((1 - core) * half), half)], rb0, sibling)
        yield
        finish(0, rb0)
        part[pl.ds(at_h, half), :] = part[pl.ds(at_h, half), :] + rb0[...]
        go(1, part.at[pl.ds(m8(at_h + (1 - bit1) * quarter), quarter)], rb1, peer1)
        yield
        finish(1, rb1)
        part[pl.ds(at_q, quarter), :] = part[pl.ds(at_q, quarter), :] + rb1[...]
        go(2, part.at[pl.ds(m8(at_q + (1 - bit2) * eighth), eighth)], rb2, peer2)
        yield
        finish(2, rb2)
        part[pl.ds(at_e, eighth), :] = part[pl.ds(at_e, eighth), :] + rb2[...]
        for o in range(quad - 1):
            go(3, part.at[pl.ds(m8(at_e + z_at[o] * piece), piece)], rb3.at[pl.ds(o * piece, piece)], z_peer[o])
        yield
        finish(3, rb3)
        own = part[pl.ds(at_p, piece), :]
        for o in range(quad - 1):
            own = own + rb3[o * piece : (o + 1) * piece, :]
        if far > 1:
            rb4 = r.rb4[q]
            rb4[at_far] = own
            for device in far_peer:
                go(8, rb4.at[at_far], rb4.at[at_far], device)
            yield
            finish(8, rb4.at[pl.ds(0, far - 1)])
            own = rb4[0]
            for o in range(1, far):
                own = own + rb4[o]
        whole[pl.ds(at_p, piece), :] = own
        for o in range(quad - 1):
            go(4, whole.at[pl.ds(at_p, piece)], whole.at[pl.ds(at_p, piece)], z_peer[o])
        yield
        finish(4, whole.at[pl.ds(0, (quad - 1) * piece)])
        go(5, whole.at[pl.ds(at_e, eighth)], whole.at[pl.ds(at_e, eighth)], peer2)
        yield
        finish(5, whole.at[pl.ds(0, eighth)])
        go(6, whole.at[pl.ds(at_q, quarter)], whole.at[pl.ds(at_q, quarter)], peer1)
        yield
        finish(6, whole.at[pl.ds(0, quarter)])
        go(7, whole.at[pl.ds(at_h, half)], whole.at[pl.ds(at_h, half)], sibling)
        yield
        finish(7, whole.at[pl.ds(0, half)])
        yield

    chunks = [chunk(q) for q in range(len(plan))]

    def go_on(*which):
        for q in which:
            next(chunks[q])

    def go_on_all():
        go_on(*next(blocks))

    pre_a, slope_a, pre_b, slope_b, hbt, xt = r.pre_a, r.slope_a, r.pre_b, r.slope_b, r.hbt, r.xt
    we, wr, back = r.we, r.wr, r.back
    tiles = feat // 128
    group = SIDE // slots
    keep, moved, mask = t.keep, t.moved, t.mask
    grad_b, grad_a = r.grad_b, r.grad_a
    wait_bytes(wc, r.load_sem.at[15])
    g3 = r.g3

    def write_gb(at, grad):
        grad = jnp.where(mask, grad, 0.0)
        three(g3, at, pltpu.roll(grad, SIDE - 1, 0), grad, pltpu.roll(grad, 1, 0))

    def spatial_part(i):
        go_on_all()
        value = dot(xt[...], g3[(2 - i) * SIDE : (2 - i) * SIDE + rows, :])
        for j in range(3):
            r.part[1 + i][j * mid : (j + 1) * mid, :] = value[:, j * mid : (j + 1) * mid]
        go_on(2 + i)

    go_on_all()
    go_on_all()
    by_rows(grad_b, lambda here: dot(gpc[here, :], we[...], NT))
    back_sums(4, r.table_b, inv_b, grad_b, slope_b, pre_b)
    t.near_send(4)
    for e in range(2):
        go_on_all()
        for q in range(2 * e, 2 * e + 2):
            lanes = slice(q * 256, (q + 1) * 256)
            r.part[0][e * mid : (e + 1) * mid, q % 2 * 256 : (q % 2 + 1) * 256] = dot(hbt[...], gpc[:, lanes])
        go_on(e)
    t.sums_near(4)
    go_on_all()
    back_apply(4, r.table_b, r.gb, inv_b, grad_b, pre_b, write_gb)
    spatial_part(0)
    go_on_all()
    by_rows(
        grad_a, lambda here: sum(dot(g3[moved_rows(here, (2 - i) * SIDE), :], wc[i], NT) for i in range(3))
    )
    back_sums(5, r.table_a, inv_a, grad_a, slope_a, pre_a)
    t.near_send(5)
    spatial_part(1)
    t.sums_near(5)
    spatial_part(2)
    go_on_all()
    gpa = r.gpa

    def write_ga(at, grad):
        gpa[pl.ds(at, SIDE), :] = grad.astype(BF16)

    back_apply(5, r.table_a, r.ga, inv_a, grad_a, pre_a, write_ga)
    for q in range(4):
        go_on_all()
        r.part[4][q * 256 : (q + 1) * 256, :] = dot(r.ft[q * 256 : (q + 1) * 256, :], gpa[...])
        go_on(5 + q)

    go_on_all()
    by_rows(back, lambda here: dot(gpa[here, :], wr[...], NT))
    gf = r.gf

    def blend(y, carry):
        for p in range(tiles // group):
            values = []
            for q in range(group):
                lanes = slice((p * group + q) * 128, (p * group + q + 1) * 128)
                terms = [
                    slope_c[pl.ds(block(k, y), SIDE), lanes] * coef[k : k + 1, lanes]
                    + back[pl.ds(block(k, y), SIDE), lanes]
                    for k in range(live)
                ]
                values.append(terms[0] * keep[0])
                for m in range(1, live):
                    values.append(terms[m] * keep[m] + terms[m - 1] * moved[m - 1])
                values.append(terms[live - 1] * moved[live - 1])
            value = jnp.swapaxes(jnp.stack(values), 0, 1)
            gf[pl.ds(y * width, width), p * SIDE : (p + 1) * SIDE, :] = value[0:width].astype(BF16)
        return carry

    for q in range(height // 2):
        go_on_all()
        for y in range(2):
            blend(2 * q + y, 0)
    go_on_all()
    for each in chunks:
        for _ in each:
            pass

    t.all_sent(*range(6))
    wait_bytes(r.pool.at[pl.ds(1, len(t.clip_peers))], r.pool_s.at[0])
    for q, (name, _, count) in enumerate(plan):
        part = r.part[name]
        piece = part.shape[0] // count // (8 * quad)
        for m, pieces in enumerate((8 * quad - 1, 8 * quad - 1, far - 1)):
            if pieces:
                wait_bytes(part.at[pl.ds(0, pieces * piece)], chunk_s.at[q, m])


def store(gf, vectors_c, vectors, expand, s0, s1, s2, reduce, frames_out, reduce_out, spatial_out, expand_out, *rest):
    ga, ba, gb, bb, gc, bc, *scratch, sem = rest
    vectors_of = (
        (bc, vectors_c, 0), (gc, vectors_c, 8), (bb, vectors, 0), (gb, vectors, 2), (ba, vectors, 8), (ga, vectors, 10)
    )
    pltpu.make_async_copy(gf, frames_out, sem.at[0]).start()
    pltpu.make_async_copy(reduce, reduce_out, sem.at[1]).start()
    depth, width = expand_out.shape
    for q in range(2):
        pltpu.make_async_copy(
            expand.at[pl.ds(q * depth, depth)], expand_out.at[:, pl.ds(q * width // 2, width // 2)], sem.at[2]
        ).start()
    for i, part in enumerate((s0, s1, s2)):
        for j in range(3):
            pltpu.make_async_copy(part.at[pl.ds(j * depth, depth)], spatial_out.at[i, j], sem.at[3 + i]).start()
    for number, (ref, source, first) in enumerate(vectors_of):
        for q in range(ref.shape[0] // 128):
            scratch[number][q * 128 : (q + 1) * 128] = source[first + q : first + q + 1, :].reshape(128)
        pltpu.make_async_copy(scratch[number], ref, sem.at[6 + number]).start()
    wait_bytes(gf, sem.at[0])
    wait_bytes(reduce, sem.at[1])
    wait_bytes(expand, sem.at[2])
    for i, part in enumerate((s0, s1, s2)):
        wait_bytes(part, sem.at[3 + i])
    for number in range(6):
        wait_bytes(scratch[number], sem.at[6 + number])


def solution(mesh):
    n = mesh.shape["clip"]

    def shards(*args):
        slots, height, width, feat = args[0].shape
        mid = args[1].shape[1]
        rows = (slots - 1) * ROWS
        outer = n // 8
        quad = min(4, outer)
        far = outer // quad
        cfg = (n, slots, height, width, feat, mid)
        flat_shape = (height * width, slots * feat // 128, 128)
        hbm = pl.BlockSpec(memory_space=pltpu.HBM)
        vmem = pl.BlockSpec(memory_space=pltpu.VMEM)
        dma = pltpu.SemaphoreType.DMA
        depths = list(enumerate((8, 4, 16, 16, 4, 4)))
        sizes = [(2 * mid, feat // 2)] + [(3 * mid, mid)] * 3 + [(feat, mid)]

        tiled = args[0].transpose(1, 2, 0, 3).reshape(height, width, slots, feat // 128, 128)
        tiled = tiled.transpose(0, 1, 3, 2, 4).reshape(flat_shape)
        given = [pltpu.with_memory_space_constraint(part, pltpu.HBM) for part in (tiled, *args[1:])]

        vm = pltpu.VMEM
        narrow, broad, square = vm((mid,), F32), vm((feat,), F32), vm((rows, mid), F32)
        ints = pltpu.SMEM((slots,), jnp.int32)
        plan = [(mid, feat // 2)] * 2 + [(3 * mid, mid)] * 3 + [(feat // 4, mid)] * 4
        outs = dict(
            gf=vm(flat_shape, BF16), vectors_c=vm((16, 128), F32), vectors=vm((16, 128), F32),
            **{name: vm(size, F32) for name, size in zip(dict(e=0, s0=0, s1=0, s2=0, r=0), sizes)},
        )
        scratch = dict(
            f4=vm((flat_shape[0] + SIDE - width, *flat_shape[1:]), BF16),
            fp=vm((rows, feat), BF16), ft=vm((feat, rows), BF16),
            wr=vm((feat, mid), BF16), ws=vm((3, 3, mid, mid), BF16), wc=vm((3, mid, 3 * mid), BF16), we=vm((mid, feat), BF16),
            valid=ints, clip=ints, segment=ints, share=pltpu.SMEM(args[13].shape, F32),
            ga=narrow, ba=narrow, gb=narrow, bb=narrow, gc=broad, bc=broad, loss=broad,
            xp=vm((rows + 2 * SIDE, 3 * mid), BF16), xt=vm((mid, rows), BF16),
            hb=vm((rows, mid), BF16), hbt=vm((mid, rows), BF16),
            pre_a=square, slope_a=square, pre_b=square, slope_b=square, grad_a=square, grad_b=square,
            pre_c=vm((rows, feat), F32), slope_c=vm((rows, feat), F32), back=vm((rows, feat), F32),
            gpc=vm((rows, feat), BF16), g3=vm((rows + 2 * SIDE, 3 * mid), BF16), gpa=vm((rows, mid), BF16),
            table_a=vm((8, mid), F32), table_b=vm((8, mid), F32),
            table_c=vm((8, feat), F32), coef=vm((8, feat), F32), dense=vm((8, 128), F32),
            pool=vm((6, 32, 128), F32), slope_sum=vm((3, 8, 128), F32), slope_hat=vm((3, 8, 128), F32),
            near=[vm((n if n <= 32 and at not in (2, 3) else 8, deep, 128), F32) for at, deep in depths],
            wide=[vm((outer, deep, 128), F32) for at, deep in depths],
            plane=vm((outer, 8, 128), F32),
            part=[vm(size, F32) for size in sizes],
            rb0=[vm((size // 2, lanes), F32) for size, lanes in plan],
            rb1=[vm((size // 4, lanes), F32) for size, lanes in plan],
            rb2=[vm((size // 8, lanes), F32) for size, lanes in plan],
            rb3=[vm(((quad - 1) * size // (8 * quad), lanes), F32) for size, lanes in plan],
            rb4=[vm((far, size // (8 * quad), lanes), F32) for size, lanes in plan if far > 1],
            load_sem=dma((16,)), near_s=dma((6,)), near_r=dma((6,)), wide_s=dma((6,)), wide_r=dma((6,)),
            pool_s=dma((1,)), pool_r=dma((1,)), chunk_s=dma((9, 3)), chunk_r=dma((9, 9)),
        )
        names = (*arg_names(), *outs, *scratch)

        def kernel(*refs):
            t = Step(cfg, SimpleNamespace(**dict(zip(names, refs, strict=True))))
            prologue(t)
            backward(t, *forward(t))

        results = pl.pallas_call(
            kernel,
            out_shape=list(outs.values()),
            in_specs=[hbm] * len(given),
            out_specs=[vmem] * len(outs),
            scratch_shapes=list(scratch.values()),
            compiler_params=pltpu.CompilerParams(
                collective_id=0, has_side_effects=True, vmem_limit_bytes=50 * 1024 * 1024
            ),
        )(*given)
        vector = jax.ShapeDtypeStruct((mid,), F32)
        wide_vector = jax.ShapeDtypeStruct((feat,), F32)
        flat_grad, *rest = pl.pallas_call(
            store,
            out_shape=[
                jax.ShapeDtypeStruct(flat_shape, BF16),
                jax.ShapeDtypeStruct((feat, mid), F32),
                jax.ShapeDtypeStruct((3, 3, mid, mid), F32),
                jax.ShapeDtypeStruct((mid, feat), F32),
                vector, vector, vector, vector, wide_vector, wide_vector,
            ],
            in_specs=[vmem] * 8,
            out_specs=[hbm] * 10,
            scratch_shapes=[*(vm((c,), F32) for c in (feat, feat, mid, mid, mid, mid)), dma((12,))],
            compiler_params=pltpu.CompilerParams(vmem_limit_bytes=8 * 1024 * 1024),
        )(*(pltpu.with_memory_space_constraint(part, pltpu.VMEM) for part in results))
        grad_frames = flat_grad.reshape(height, width, feat // 128, slots, 128).transpose(0, 1, 3, 2, 4)
        return grad_frames.reshape(height, width, slots, feat).transpose(2, 0, 1, 3), *rest

    split = P("clip")
    in_specs = (split,) + (P(),) * 9 + (split,) * 3 + (P(), P())
    out_specs = (split,) + (P(),) * 9
    return jax.shard_map(shards, mesh=mesh, in_specs=in_specs, out_specs=out_specs, check_vma=False)


def arg_names():
    return dict(
        frames=0, w_reduce=0, w_spatial=0, w_expand=0, gain_a=0, bias_a=0, gain_b=0, bias_b=0, gain_c=0, bias_c=0,
        clip_ids=0, segment_ids=0, slot_valid=0, segment_weight=0, loss_weight=0,
    )
```

```python
import functools
from types import SimpleNamespace

import jax
import jax.numpy as jnp
from jax import lax
from jax.experimental import pallas as pl
from jax.experimental.pallas import tpu as pltpu
from jax.sharding import PartitionSpec as P

MESH = pl.DeviceIdType.MESH
EPS = 1e-05
F32 = jnp.float32
BF16 = jnp.bfloat16
SIDE = 16
ROWS = SIDE * SIDE
NN = (((1,), (0,)), ((), ()))
NT = (((1,), (1,)), ((), ()))

ORDER = (
    (),
    (),
    (),
    (),
    (),
    (),
    (0, 1,),
    (2, 0,),
    (1,),
    (2, 0, 1, 3,),
    (2, 4,),
    (),
    (),
    (0,),
    (1, 3, 5, 2, 4,),
    (6, 3, 8,),
    (1, 0, 5, 7, 4, 8, 1, 3, 6, 7, 8, 2, 0,),
    (4, 7, 3,),
    (6, 2, 8, 1, 5, 0, 4, 7, 3, 6, 8, 5, 7, 1, 6, 4,),
    (5, 6, 0, 3,),
    (7,),
    (8, 2, 4, 5, 7, 8, 6, 3, 5,),
    (7, 8, 6, 5, 4, 2,),
)


def dot(a, b, dims=NN):
    return lax.dot_general(a, b, dims, preferred_element_type=F32)


def wait_bytes(ref, sem):
    pltpu.make_async_copy(ref, ref, sem).wait()


def by_rows(ref, value):
    for k in range(ref.shape[0] // 256):
        ref[k * 256 : (k + 1) * 256, :] = value(slice(k * 256, (k + 1) * 256))


def moved_rows(here, at):
    return slice(here.start + at, here.stop + at)


def block(k, y):
    return pl.multiple_of(k * ROWS + y * SIDE, SIDE)


def to_dense(ref, at, value, first):
    for q in range(value.shape[1] // 128):
        ref[at, pl.ds(first + q, 1), :] = value[:, q * 128 : (q + 1) * 128]


def row_form(ref, row, source, first, count, lane=0):
    for q in range(count):
        ref[row : row + 1, (lane + q) * 128 : (lane + q + 1) * 128] = source[first + q : first + q + 1, :]


def three(ref, at, left, middle, right):
    here, wide = pl.ds(at + SIDE, SIDE), middle.shape[1]
    ref[here, 0:wide] = left.astype(BF16)
    ref[here, wide : 2 * wide] = middle.astype(BF16)
    ref[here, 2 * wide : 3 * wide] = right.astype(BF16)


def dense_of(ref1, scratch):
    count = ref1.shape[0] // 128
    for q in range(count):
        scratch[q : q + 1, :] = ref1[q * 128 : (q + 1) * 128].reshape(1, 128)
    return scratch[0:count, :]


class Step:
    def __init__(self, cfg, r):
        self.r, self.sizes = r, cfg
        self.n, self.slots, self.height, self.width, self.feat, self.mid = cfg
        self.live = self.slots - 1
        self.rows = self.live * ROWS
        self.area = self.height * self.width
        self.inner = 8
        self.outer = self.n // 8
        self.quad = min(4, self.outer)
        self.far = self.outer // self.quad
        self.loads = {}
        self.mask = lax.broadcasted_iota(jnp.int32, (SIDE, 256), 0) < self.width

    def load(self, **pairs):
        for name, (src, dst) in pairs.items():
            copy = pltpu.make_async_copy(src, dst, self.r.load_sem.at[len(self.loads)])
            copy.start()
            self.loads[name] = copy

    def loaded(self, **names):
        for name in names:
            self.loads[name].wait()

    def fold(self, value):
        return jnp.sum(jnp.where(self.mask, value, 0.0), axis=0, keepdims=True)

    def slot_facts(self):
        r, live = self.r, self.live
        alive, later = 1, []
        for k in range(live):
            alive = alive * r.valid[k]
            later.append(1 - alive)
        self.keep = [(1 - q).astype(F32) for q in later]
        self.moved = [q.astype(F32) for q in later]
        self.later = later
        self.v = [self.kept(r.valid, k) for k in range(live)]
        self.n_own = (self.v[0] + self.v[1] + self.v[2]) * float(self.area)

    def kept(self, values, k):
        return (values[k] + self.later[k] * (values[k + 1] - values[k])).astype(F32)

    def places(self):
        n = self.n
        self.me = me = lax.axis_index("clip")
        self.low, self.high = low, high = me % self.inner, me // self.inner
        self.direct = n <= 32
        self.peers = flips(me, n)
        self.low_peers = flips(me, self.inner)
        self.high_peers = flips(me, self.outer, self.inner)
        self.clip_peers = [(me + o) % n for o in (n // 2 - 1, n // 2 + 1, n // 2, n - 1, 1)]

    def greet(self):
        self.greeted = self.peers if self.direct else self.low_peers + self.high_peers + self.clip_peers
        self.barrier = pltpu.get_barrier_semaphore()
        for device in self.greeted:
            pl.semaphore_signal(self.barrier, inc=1, device_id=(device,), device_id_type=MESH)

    def all_here(self):
        pl.semaphore_wait(self.barrier, len(self.greeted))

    def send(self, src, dst, ssem, rsem, device):
        pltpu.make_async_remote_copy(
            src_ref=src, dst_ref=dst, send_sem=ssem, recv_sem=rsem, device_id=(device,), device_id_type=MESH
        ).start()

    def one_stage(self, at):
        return self.direct and at != 3

    def near_at(self, at):
        return self.me if self.one_stage(at) else self.low

    def near_send(self, at):
        buf, mine = self.r.near[at], self.near_at(at)
        for device in self.peers if self.one_stage(at) else self.low_peers:
            self.send(buf.at[mine], buf.at[mine], self.r.near_s.at[at], self.r.near_r.at[at], device)

    def near_wait(self, at, sems):
        buf = self.r.near[at]
        wait_bytes(buf.at[pl.ds(0, buf.shape[0] - 1)], sems.at[at])

    def wide_send(self, at):
        buf = self.r.wide[at]
        for device in self.high_peers:
            self.send(buf.at[self.high], buf.at[self.high], self.r.wide_s.at[at], self.r.wide_r.at[at], device)

    def wide_wait(self, at, sems):
        wait_bytes(self.r.wide[at].at[pl.ds(0, self.outer - 1)], sems.at[at])

    def all_sent(self, *rounds):
        for at in rounds:
            self.near_wait(at, self.r.near_s)
            if not self.one_stage(at):
                self.wide_wait(at, self.r.wide_s)

    def stats_near(self, at, count):
        if self.one_stage(at):
            return
        self.near_wait(at, self.r.near_r)
        n_all, s_all, _, spread = combine(self.r.near[at], lambda q: self.r.near[0][q, 4:5, :], self.inner, count)
        buf = self.r.wide[at]
        buf[self.high, 0:count, :] = s_all
        buf[self.high, count : 2 * count, :] = spread
        if at == 0:
            buf[self.high, 4:5, :] = n_all
        self.wide_send(at)

    def stats_wide(self, at, count, table, first=0):
        r = self.r
        if self.one_stage(at):
            self.near_wait(at, r.near_r)
            counts = r.near[0]
            n_all, _, mean, spread = combine(r.near[at], lambda q: counts[q, 4:5, :], self.n, count)
        else:
            self.wide_wait(at, r.wide_r)
            n_all, _, mean, spread = combine(r.wide[at], lambda q: r.wide[0][q, 4:5, :], self.outer, count)
        inverse = lax.rsqrt(spread / n_all + EPS)
        r.dense[0:count, :] = mean
        row_form(table, 0, r.dense, 0, count, first)
        r.dense[0:count, :] = inverse
        row_form(table, 1, r.dense, 0, count, first)
        return n_all, inverse

    def sums_near(self, at):
        if not self.one_stage(at):
            self.near_wait(at, self.r.near_r)
            self.r.wide[at][self.high] = total(self.r.near[at])
            self.wide_send(at)

    def sums_wide(self, at):
        if self.one_stage(at):
            self.near_wait(at, self.r.near_r)
            return total(self.r.near[at])
        self.wide_wait(at, self.r.wide_r)
        return total(self.r.wide[at])

    def local_stats(self, buf, at, ref, first=0, channels=None):
        channels = channels or ref.shape[1]
        count = channels // 128
        for c in range(channels // 256):
            lanes = slice(first + c * 256, first + (c + 1) * 256)

            def gather(term):
                acc = jnp.zeros((SIDE, 256), F32)
                for k in range(self.live):
                    part = lax.fori_loop(
                        0, self.height, lambda y, a: a + term(ref[pl.ds(block(k, y), SIDE), lanes]),
                        jnp.zeros((SIDE, 256), F32), unroll=self.height,
                    )
                    acc = acc + part * self.v[k]
                return self.fold(acc)

            s_own = gather(lambda x: x)
            mean = s_own / jnp.maximum(self.n_own, 1.0)
            to_dense(buf, at, s_own, 2 * c)
            to_dense(buf, at, gather(lambda x: (x - mean) * (x - mean)), count + 2 * c)

    def norm_silu(self, ref, slope_ref, table, gain, bias, write):
        centre, scale = table[0:1, :], table[1:2, :] * gain[...].reshape(1, self.mid)
        b = bias[...].reshape(1, self.mid)
        for k in range(self.live):
            def step(y, carry):
                at = block(k, y)
                u = (ref[pl.ds(at, SIDE), :] - centre) * scale + b
                s = 0.5 * jnp.tanh(0.5 * u) + 0.5
                h = u * s
                slope_ref[pl.ds(at, SIDE), :] = jnp.where(self.mask, s + (h - h * s), 0.0)
                write(at, jnp.where(self.mask, h, 0.0))
                return carry

            lax.fori_loop(0, self.height, step, 0, unroll=self.height)


def flips(index, count, stride=1):
    steps, at = [], 1
    while at < count:
        steps.append(at * stride * (1 - 2 * ((index // (at * stride)) % 2)))
        at *= 2
    return [sum((d for b, d in enumerate(steps) if o >> b & 1), index) for o in reversed(range(1, count))]


def combine(buf, counts, group, count):
    n_part = [counts(q) for q in range(group)]
    s_part = [buf[q, 0:count, :] for q in range(group)]
    n_all = sum(n_part[1:], n_part[0])
    s_all = sum(s_part[1:], s_part[0])
    mean = s_all / jnp.maximum(n_all, 1.0)
    spread = jnp.zeros((count, 128), F32)
    for q in range(group):
        gap = s_part[q] / jnp.maximum(n_part[q], 1.0) - mean
        spread = spread + (buf[q, count : 2 * count, :] + n_part[q] * gap * gap)
    return n_all, s_all, mean, spread


def total(buf):
    out = buf[0]
    for q in range(1, buf.shape[0]):
        out = out + buf[q]
    return out


def clear(*refs):
    for ref in refs:
        ref[...] = jnp.zeros(ref.shape, ref.dtype)


def prologue(t):
    r, slots, live, width, feat = t.r, t.slots, t.live, t.width, t.feat
    t.places()
    t.greet()
    t.load(
        frames=(r.frames, r.f4.at[pl.ds(0, t.area)]), valid=(r.slot_valid, r.valid), reduce=(r.w_reduce, r.wr)
    )
    r.f4[t.area :] = jnp.zeros((r.f4.shape[0] - t.area, *r.f4.shape[1:]), BF16)
    clear(r.fp)
    t.loaded(valid=0)
    t.slot_facts()
    t.loaded(frames=0)
    t.load(
        clip=(r.clip_ids, r.clip), segment=(r.segment_ids, r.segment),
        share=(r.segment_weight, r.share), spatial=(r.w_spatial, r.ws), expand=(r.w_expand, r.we),
        ga=(r.gain_a, r.ga), ba=(r.bias_a, r.ba), gb=(r.gain_b, r.gb), bb=(r.bias_b, r.bb),
        gc=(r.gain_c, r.gc), bc=(r.bias_c, r.bc), loss=(r.loss_weight, r.loss),
    )
    for i in range(3):
        for j in range(3):
            pltpu.make_async_copy(
                r.w_spatial.at[i, j], r.wc.at[i, :, pl.ds(j * t.mid, t.mid)], r.load_sem.at[15]
            ).start()
    fp, f4 = r.fp, r.f4
    tiles = feat // 128
    group = SIDE // slots
    short = lax.broadcasted_iota(jnp.int32, (SIDE, 128), 0) < width

    def regroup(y, carry):
        for p in range(tiles // group):
            value = f4[pl.ds(y * width, SIDE), p * SIDE : (p + 1) * SIDE, :].astype(F32)
            value = jnp.swapaxes(value, 0, 1)
            for q in range(group):
                for k in range(live):
                    row = value[q * slots + k] * t.keep[k] + value[q * slots + k + 1] * t.moved[k]
                    lanes = slice((p * group + q) * 128, (p * group + q + 1) * 128)
                    fp[pl.ds(block(k, y), SIDE), lanes] = jnp.where(short, row, 0.0).astype(BF16)
        return carry

    lax.fori_loop(0, t.height, regroup, 0)
    t.loaded(reduce=0)
    by_rows(r.pre_a, lambda here: dot(fp[here, :], r.wr[...]))
    t.local_stats(r.near[0], t.near_at(0), r.pre_a)
    r.near[0][t.near_at(0), 4:5, :] = jnp.full((1, 128), t.n_own, F32)


def forward(t):
    r, live, mid, feat, rows, area, height = t.r, t.live, t.mid, t.feat, t.rows, t.area, t.height

    def turn(q):
        lanes = slice(q * feat // 4, (q + 1) * feat // 4)
        r.ft[lanes, :] = r.fp[:, lanes].T

    t.all_here()
    t.near_send(0)
    turn(0)
    t.stats_near(0, mid // 128)
    clear(r.xp, r.hb, r.g3, r.gpc, r.gpa)
    t.loaded(clip=0, segment=0, share=0, ga=0, ba=0, gb=0, bb=0, gc=0, bc=0, loss=0, spatial=0, expand=0)
    key = [t.kept(r.clip, k) for k in range(live)]
    weight = []
    for k in range(live):
        at = t.kept(r.segment, k)
        w0, w1, w2 = (r.share[q] for q in range(3))
        weight.append(
            t.v[k] * (w0 * ((1.0 - at) * (2.0 - at) * 0.5) + w1 * (at * (2.0 - at)) + w2 * (at * (at - 1.0) * 0.5))
        )
    n_all, inv_a = t.stats_wide(0, mid // 128, r.table_a)

    xp, hb = r.xp, r.hb

    def write_a(at, h):
        three(xp, at, pltpu.roll(h, 1, 0), h, pltpu.roll(h, SIDE - 1, 0))

    t.norm_silu(r.pre_a, r.slope_a, r.table_a, r.ga, r.ba, write_a)

    by_rows(
        r.pre_b,
        lambda here: sum(dot(xp[moved_rows(here, i * SIDE), :], r.ws[i].reshape(3 * mid, mid)) for i in range(3)),
    )
    t.local_stats(r.near[1], t.near_at(1), r.pre_b)
    t.near_send(1)
    r.xt[...] = xp[SIDE : SIDE + rows, mid : 2 * mid].T
    t.stats_near(1, mid // 128)
    _, inv_b = t.stats_wide(1, mid // 128, r.table_b)

    def write_b(at, h):
        hb[pl.ds(at, SIDE), :] = h.astype(BF16)

    t.norm_silu(r.pre_b, r.slope_b, r.table_b, r.gb, r.bb, write_b)

    pre_c, slope_c, fp, table_c = r.pre_c, r.slope_c, r.fp, r.table_c
    half = feat // 2
    rounds = (2, 6)
    for h, at in enumerate(rounds):
        lanes = slice(h * half, (h + 1) * half)
        for k in range(live):
            here = slice(k * ROWS, (k + 1) * ROWS)
            pre_c[here, lanes] = dot(hb[here, :], r.we[:, lanes])
        t.local_stats(r.near[at], t.near_at(at), pre_c, h * half, half)
        t.near_send(at)
    r.hbt[...] = hb[...].T
    for at in rounds:
        t.stats_near(at, half // 128)
    turn(1)

    pool, slope_sum, slope_hat = r.pool, r.slope_sum, r.slope_hat
    for c in range(feat // 256):
        if c * 256 % half == 0:
            h = c * 256 // half
            _, inv_half = t.stats_wide(rounds[h], half // 128, table_c, h * half // 128)
            r.inv_c[h * half // 128 : (h + 1) * half // 128, :] = inv_half
        lanes = slice(c * 256, (c + 1) * 256)
        centre, inverse = table_c[0:1, lanes], table_c[1:2, lanes]
        g = r.gc[lanes].reshape(1, 256)
        b = r.bc[lanes].reshape(1, 256)
        for k in range(live):
            def step(y, carry):
                a0, a1, a2 = carry
                at = block(k, y)
                hat = (pre_c[pl.ds(at, SIDE), lanes] - centre) * inverse
                u = hat * g + b + fp[pl.ds(at, SIDE), lanes].astype(F32)
                s = 0.5 * jnp.tanh(0.5 * u) + 0.5
                h = u * s
                slope = s + (h - h * s)
                slope_c[pl.ds(at, SIDE), lanes] = slope
                return a0 + h, a1 + slope, a2 + slope * hat

            zero = jnp.zeros((SIDE, 256), F32)
            a0, a1, a2 = lax.fori_loop(0, height, step, (zero, zero, zero), unroll=height)
            p_row = (t.fold(a0) * (1.0 / area)).astype(BF16).astype(F32)
            to_dense(pool, 0, p_row, 8 * k + 2 * c)
            to_dense(slope_sum, k, t.fold(a1), 2 * c)
            to_dense(slope_hat, k, t.fold(a2), 2 * c)
    for k in range(live):
        pool[0, 24 + k : 25 + k, :] = jnp.full((1, 128), key[k], F32)
        pool[0, 28 + k : 29 + k, :] = jnp.full((1, 128), weight[k], F32)
    for q, device in enumerate(t.clip_peers):
        t.send(pool.at[0], pool.at[q + 1], r.pool_s.at[0], r.pool_r.at[0], device)
    turn(2)
    wait_bytes(pool.at[pl.ds(1, len(t.clip_peers))], r.pool_r.at[0])

    lw = dense_of(r.loss, r.dense)
    grads = []
    for k in range(live):
        my_key = jnp.full((1, 128), key[k], F32)
        my_weight = jnp.full((1, 128), weight[k], F32)
        mean = jnp.zeros((8, 128), F32)
        den = jnp.zeros((1, 128), F32)
        for q in range(len(t.clip_peers) + 1):
            for m in range(live):
                match = jnp.where(pool[q, 24 + m : 25 + m, :] == my_key, pool[q, 28 + m : 29 + m, :], 0.0)
                den = den + match
                mean = mean + match * pool[q, 8 * m : 8 * m + 8, :]
        den = jnp.where(den == 0.0, 1.0, den)
        mean = mean / den
        power = jnp.sum(jnp.sum(mean * mean, axis=0, keepdims=True), axis=1, keepdims=True)
        along = jnp.sum(jnp.sum(mean * lw, axis=0, keepdims=True), axis=1, keepdims=True)
        scale = lax.rsqrt(power * (1.0 / feat) + EPS)
        mean_grad = scale * (lw - (mean * scale) * (scale * along * (1.0 / feat)))
        grads.append((my_weight / den) * mean_grad * (1.0 / area))

    inv_c = r.inv_c[...]
    near3 = r.near[3]
    shift = jnp.zeros((8, 128), F32)
    gain = jnp.zeros((8, 128), F32)
    for k in range(live):
        shift = shift + grads[k] * slope_sum[k]
        gain = gain + grads[k] * slope_hat[k]
    near3[t.near_at(3), 0:8, :] = shift
    near3[t.near_at(3), 8:16, :] = gain
    t.near_send(3)
    coef, dense = r.coef, r.dense
    scale_c = dense_of(r.gc, dense) * inv_c
    for k in range(live):
        dense[...] = grads[k]
        row_form(coef, k, dense, 0, feat // 128)
        dense[...] = grads[k] * scale_c
        row_form(coef, 3 + k, dense, 0, feat // 128)
    t.sums_near(3)
    turn(3)
    both = t.sums_wide(3)
    r.vectors_c[...] = both
    dense[...] = both[0:8] * scale_c / n_all
    row_form(coef, 6, dense, 0, feat // 128)
    dense[...] = both[8:16] * scale_c * inv_c / n_all
    row_form(coef, 7, dense, 0, feat // 128)
    return n_all, inv_a, inv_b


def backward(t, n_all, inv_a, inv_b):
    r, live, mid, feat, rows, height = t.r, t.live, t.mid, t.feat, t.rows, t.height
    slots, width, quad, far, v, wc = t.slots, t.width, t.quad, t.far, t.v, r.wc
    coef, pre_c, slope_c, out = r.coef, r.pre_c, r.slope_c, r.vectors
    me, send = t.me, t.send
    gpc = r.gpc
    for k in range(live):
        for c in range(feat // 256):
            lanes = slice(c * 256, (c + 1) * 256)
            centre = r.table_c[0:1, lanes]
            c0 = coef[3 + k : 4 + k, lanes]
            c1 = coef[6:7, lanes] * v[k]
            c2 = coef[7:8, lanes] * v[k]

            def step(y, carry):
                at = block(k, y)
                grad = slope_c[pl.ds(at, SIDE), lanes] * c0 - (c1 + (pre_c[pl.ds(at, SIDE), lanes] - centre) * c2)
                gpc[pl.ds(at, SIDE), lanes] = grad.astype(BF16)
                return carry

            lax.fori_loop(0, height, step, 0, unroll=height)

    def back_sums(at, table, inv, grad_ref, slope_ref, pre_ref):
        zero = jnp.zeros((SIDE, mid), F32)
        carry = (zero, zero)
        centre = table[0:1, :]
        for k in range(live):
            def step(y, c):
                here = pl.ds(block(k, y), SIDE)
                grad = grad_ref[here, :] * slope_ref[here, :]
                grad_ref[here, :] = grad
                return c[0] + grad, c[1] + grad * (pre_ref[here, :] - centre)

            carry = lax.fori_loop(0, height, step, carry, unroll=height)
        buf = r.near[at]
        to_dense(buf, t.near_at(at), jnp.sum(carry[0], axis=0, keepdims=True), 0)
        to_dense(buf, t.near_at(at), jnp.sum(carry[1], axis=0, keepdims=True) * table[1:2, :], 2)

    def back_apply(at, table, gain_ref, inv, grad_ref, pre_ref, write):
        both = t.sums_wide(at)
        out[8 * at - 32 : 8 * at - 28, :] = both[0:4]
        dense = r.dense
        scale = dense_of(gain_ref, dense) * inv
        dense[0:2, :] = scale
        dense[2:4, :] = both[0:2] * scale / n_all
        dense[4:6, :] = both[2:4] * scale * inv / n_all
        for q in range(3):
            row_form(table, 2 + q, dense, 2 * q, 2)
        centre = table[0:1, :]
        for k in range(live):
            c0, c1, c2 = table[2:3, :], table[3:4, :] * v[k], table[4:5, :] * v[k]

            def step(y, carry):
                at_row = block(k, y)
                here = pl.ds(at_row, SIDE)
                write(at_row, grad_ref[here, :] * c0 - (c1 + (pre_ref[here, :] - centre) * c2))
                return carry

            lax.fori_loop(0, height, step, 0, unroll=height)

    core, bit_x, bit_y, at_z = me % 2, (me // 2) % 2, (me // 4) % 2, (me // 8) % quad
    at_far = me // (8 * quad)
    bit1 = bit_x + core * (bit_y - bit_x)
    bit2 = bit_y + core * (bit_x - bit_y)
    sibling = me + 1 - 2 * core
    peer1 = me + (1 - 2 * bit1) * (2 + 2 * core)
    peer2 = me + (1 - 2 * bit2) * (4 - 2 * core)
    z_at = flips(at_z, quad)
    z_peer = [me + 8 * (q - at_z) for q in z_at]
    far_peer = [me + 8 * quad * ((at_far + o) % far - at_far) for o in range(1, far)]
    chunk_s, chunk_r = r.chunk_s, r.chunk_r
    blocks = iter(ORDER)
    plan = [(0, q, 2) for q in range(2)] + [(1 + q, 0, 1) for q in range(3)] + [(4, q, 4) for q in range(4)]

    def chunk(q):
        name, at, count = plan[q]
        size = r.part[name].shape[0] // count
        part = r.part[name].at[pl.ds(at * size, size)]
        whole = (r.e, r.s0, r.s1, r.s2, r.r)[name].at[pl.ds(at * size, size)]
        half, quarter, eighth, piece = size // 2, size // 4, size // 8, size // (8 * quad)
        m8 = lambda value: pl.multiple_of(value, 8)
        at_h = m8(core * half)
        at_q = m8(at_h + bit1 * quarter)
        at_e = m8(at_q + bit2 * eighth)
        at_p = m8(at_e + at_z * piece)

        def go(step, src, dst, device):
            send(src, dst, chunk_s.at[q, step // 4], chunk_r.at[q, step], device)

        def finish(step, ref):
            wait_bytes(ref, chunk_r.at[q, step])

        rb0, rb1, rb2, rb3 = r.rb0[q], r.rb1[q], r.rb2[q], r.rb3[q]
        go(0, part.at[pl.ds(m8((1 - core) * half), half)], rb0, sibling)
        yield
        finish(0, rb0)
        part[pl.ds(at_h, half), :] = part[pl.ds(at_h, half), :] + rb0[...]
        go(1, part.at[pl.ds(m8(at_h + (1 - bit1) * quarter), quarter)], rb1, peer1)
        yield
        finish(1, rb1)
        part[pl.ds(at_q, quarter), :] = part[pl.ds(at_q, quarter), :] + rb1[...]
        go(2, part.at[pl.ds(m8(at_q + (1 - bit2) * eighth), eighth)], rb2, peer2)
        yield
        finish(2, rb2)
        part[pl.ds(at_e, eighth), :] = part[pl.ds(at_e, eighth), :] + rb2[...]
        for o in range(quad - 1):
            go(3, part.at[pl.ds(m8(at_e + z_at[o] * piece), piece)], rb3.at[pl.ds(o * piece, piece)], z_peer[o])
        yield
        finish(3, rb3)
        own = part[pl.ds(at_p, piece), :]
        for o in range(quad - 1):
            own = own + rb3[o * piece : (o + 1) * piece, :]
        if far > 1:
            rb4 = r.rb4[q]
            rb4[at_far] = own
            for device in far_peer:
                go(8, rb4.at[at_far], rb4.at[at_far], device)
            yield
            finish(8, rb4.at[pl.ds(0, far - 1)])
            own = rb4[0]
            for o in range(1, far):
                own = own + rb4[o]
        whole[pl.ds(at_p, piece), :] = own
        for o in range(quad - 1):
            go(4, whole.at[pl.ds(at_p, piece)], whole.at[pl.ds(at_p, piece)], z_peer[o])
        yield
        finish(4, whole.at[pl.ds(0, (quad - 1) * piece)])
        go(5, whole.at[pl.ds(at_e, eighth)], whole.at[pl.ds(at_e, eighth)], peer2)
        yield
        finish(5, whole.at[pl.ds(0, eighth)])
        go(6, whole.at[pl.ds(at_q, quarter)], whole.at[pl.ds(at_q, quarter)], peer1)
        yield
        finish(6, whole.at[pl.ds(0, quarter)])
        go(7, whole.at[pl.ds(at_h, half)], whole.at[pl.ds(at_h, half)], sibling)
        yield
        finish(7, whole.at[pl.ds(0, half)])
        yield

    chunks = [chunk(q) for q in range(len(plan))]

    def go_on(*which):
        for q in which:
            next(chunks[q])

    def go_on_all():
        go_on(*next(blocks))

    pre_a, slope_a, pre_b, slope_b, hbt, xt = r.pre_a, r.slope_a, r.pre_b, r.slope_b, r.hbt, r.xt
    we, wr, back = r.we, r.wr, r.back
    tiles = feat // 128
    group = SIDE // slots
    keep, moved, mask = t.keep, t.moved, t.mask
    grad_b, grad_a = r.grad_b, r.grad_a
    wait_bytes(wc, r.load_sem.at[15])
    g3 = r.g3

    def write_gb(at, grad):
        grad = jnp.where(mask, grad, 0.0)
        three(g3, at, pltpu.roll(grad, SIDE - 1, 0), grad, pltpu.roll(grad, 1, 0))

    def spatial_part(i):
        go_on_all()
        value = dot(xt[...], g3[(2 - i) * SIDE : (2 - i) * SIDE + rows, :])
        for j in range(3):
            r.part[1 + i][j * mid : (j + 1) * mid, :] = value[:, j * mid : (j + 1) * mid]
        go_on(2 + i)

    go_on_all()
    go_on_all()
    by_rows(grad_b, lambda here: dot(gpc[here, :], we[...], NT))
    back_sums(4, r.table_b, inv_b, grad_b, slope_b, pre_b)
    t.near_send(4)
    for e in range(2):
        go_on_all()
        for q in range(2 * e, 2 * e + 2):
            lanes = slice(q * 256, (q + 1) * 256)
            r.part[0][e * mid : (e + 1) * mid, q % 2 * 256 : (q % 2 + 1) * 256] = dot(hbt[...], gpc[:, lanes])
        go_on(e)
    t.sums_near(4)
    go_on_all()
    back_apply(4, r.table_b, r.gb, inv_b, grad_b, pre_b, write_gb)
    spatial_part(0)
    go_on_all()
    by_rows(
        grad_a, lambda here: sum(dot(g3[moved_rows(here, (2 - i) * SIDE), :], wc[i], NT) for i in range(3))
    )
    back_sums(5, r.table_a, inv_a, grad_a, slope_a, pre_a)
    t.near_send(5)
    spatial_part(1)
    t.sums_near(5)
    spatial_part(2)
    go_on_all()
    gpa = r.gpa

    def write_ga(at, grad):
        gpa[pl.ds(at, SIDE), :] = grad.astype(BF16)

    back_apply(5, r.table_a, r.ga, inv_a, grad_a, pre_a, write_ga)
    for q in range(4):
        go_on_all()
        r.part[4][q * 256 : (q + 1) * 256, :] = dot(r.ft[q * 256 : (q + 1) * 256, :], gpa[...])
        go_on(5 + q)

    go_on_all()
    by_rows(back, lambda here: dot(gpa[here, :], wr[...], NT))
    gf = r.gf

    def blend(y, carry):
        for p in range(tiles // group):
            values = []
            for q in range(group):
                lanes = slice((p * group + q) * 128, (p * group + q + 1) * 128)
                terms = [
                    slope_c[pl.ds(block(k, y), SIDE), lanes] * coef[k : k + 1, lanes]
                    + back[pl.ds(block(k, y), SIDE), lanes]
                    for k in range(live)
                ]
                values.append(terms[0] * keep[0])
                for m in range(1, live):
                    values.append(terms[m] * keep[m] + terms[m - 1] * moved[m - 1])
                values.append(terms[live - 1] * moved[live - 1])
            value = jnp.swapaxes(jnp.stack(values), 0, 1)
            gf[pl.ds(y * width, width), p * SIDE : (p + 1) * SIDE, :] = value[0:width].astype(BF16)
        return carry

    for q in range(height // 2):
        go_on_all()
        for y in range(2):
            blend(2 * q + y, 0)
    go_on_all()
    for each in chunks:
        for _ in each:
            pass

    t.all_sent(*range(7))
    wait_bytes(r.pool.at[pl.ds(1, len(t.clip_peers))], r.pool_s.at[0])
    for q, (name, _, count) in enumerate(plan):
        part = r.part[name]
        piece = part.shape[0] // count // (8 * quad)
        for m, pieces in enumerate((8 * quad - 1, 8 * quad - 1, far - 1)):
            if pieces:
                wait_bytes(part.at[pl.ds(0, pieces * piece)], chunk_s.at[q, m])


def store(gf, vectors_c, vectors, expand, s0, s1, s2, reduce, frames_out, reduce_out, spatial_out, expand_out, *rest):
    ga, ba, gb, bb, gc, bc, *scratch, sem = rest
    vectors_of = (
        (bc, vectors_c, 0), (gc, vectors_c, 8), (bb, vectors, 0), (gb, vectors, 2), (ba, vectors, 8), (ga, vectors, 10)
    )
    pltpu.make_async_copy(gf, frames_out, sem.at[0]).start()
    pltpu.make_async_copy(reduce, reduce_out, sem.at[1]).start()
    depth, width = expand_out.shape
    for q in range(2):
        pltpu.make_async_copy(
            expand.at[pl.ds(q * depth, depth)], expand_out.at[:, pl.ds(q * width // 2, width // 2)], sem.at[2]
        ).start()
    for i, part in enumerate((s0, s1, s2)):
        for j in range(3):
            pltpu.make_async_copy(part.at[pl.ds(j * depth, depth)], spatial_out.at[i, j], sem.at[3 + i]).start()
    for number, (ref, source, first) in enumerate(vectors_of):
        for q in range(ref.shape[0] // 128):
            scratch[number][q * 128 : (q + 1) * 128] = source[first + q : first + q + 1, :].reshape(128)
        pltpu.make_async_copy(scratch[number], ref, sem.at[6 + number]).start()
    wait_bytes(gf, sem.at[0])
    wait_bytes(reduce, sem.at[1])
    wait_bytes(expand, sem.at[2])
    for i, part in enumerate((s0, s1, s2)):
        wait_bytes(part, sem.at[3 + i])
    for number in range(6):
        wait_bytes(scratch[number], sem.at[6 + number])


def solution(mesh):
    n = mesh.shape["clip"]

    def shards(*args):
        slots, height, width, feat = args[0].shape
        mid = args[1].shape[1]
        rows = (slots - 1) * ROWS
        outer = n // 8
        quad = min(4, outer)
        far = outer // quad
        cfg = (n, slots, height, width, feat, mid)
        flat_shape = (height * width, slots * feat // 128, 128)
        hbm = pl.BlockSpec(memory_space=pltpu.HBM)
        vmem = pl.BlockSpec(memory_space=pltpu.VMEM)
        dma = pltpu.SemaphoreType.DMA
        depths = list(enumerate((8, 4, 8, 16, 4, 4, 8)))
        sizes = [(2 * mid, feat // 2)] + [(3 * mid, mid)] * 3 + [(feat, mid)]

        tiled = args[0].transpose(1, 2, 0, 3).reshape(height, width, slots, feat // 128, 128)
        tiled = tiled.transpose(0, 1, 3, 2, 4).reshape(flat_shape)
        given = [pltpu.with_memory_space_constraint(part, pltpu.HBM) for part in (tiled, *args[1:])]

        vm = pltpu.VMEM
        narrow, broad, square = vm((mid,), F32), vm((feat,), F32), vm((rows, mid), F32)
        ints = pltpu.SMEM((slots,), jnp.int32)
        plan = [(mid, feat // 2)] * 2 + [(3 * mid, mid)] * 3 + [(feat // 4, mid)] * 4
        outs = dict(
            gf=vm(flat_shape, BF16), vectors_c=vm((16, 128), F32), vectors=vm((16, 128), F32),
            **{name: vm(size, F32) for name, size in zip(dict(e=0, s0=0, s1=0, s2=0, r=0), sizes)},
        )
        scratch = dict(
            f4=vm((flat_shape[0] + SIDE - width, *flat_shape[1:]), BF16),
            fp=vm((rows, feat), BF16), ft=vm((feat, rows), BF16),
            wr=vm((feat, mid), BF16), ws=vm((3, 3, mid, mid), BF16), wc=vm((3, mid, 3 * mid), BF16), we=vm((mid, feat), BF16),
            valid=ints, clip=ints, segment=ints, share=pltpu.SMEM(args[13].shape, F32),
            ga=narrow, ba=narrow, gb=narrow, bb=narrow, gc=broad, bc=broad, loss=broad,
            xp=vm((rows + 2 * SIDE, 3 * mid), BF16), xt=vm((mid, rows), BF16),
            hb=vm((rows, mid), BF16), hbt=vm((mid, rows), BF16),
            pre_a=square, slope_a=square, pre_b=square, slope_b=square, grad_a=square, grad_b=square,
            pre_c=vm((rows, feat), F32), slope_c=vm((rows, feat), F32), back=vm((rows, feat), F32),
            gpc=vm((rows, feat), BF16), g3=vm((rows + 2 * SIDE, 3 * mid), BF16), gpa=vm((rows, mid), BF16),
            table_a=vm((8, mid), F32), table_b=vm((8, mid), F32),
            table_c=vm((8, feat), F32), coef=vm((8, feat), F32), dense=vm((8, 128), F32), inv_c=vm((8, 128), F32),
            pool=vm((6, 32, 128), F32), slope_sum=vm((3, 8, 128), F32), slope_hat=vm((3, 8, 128), F32),
            near=[vm((n if n <= 32 and at != 3 else 8, deep, 128), F32) for at, deep in depths],
            wide=[vm((outer, deep, 128), F32) for at, deep in depths],
            part=[vm(size, F32) for size in sizes],
            rb0=[vm((size // 2, lanes), F32) for size, lanes in plan],
            rb1=[vm((size // 4, lanes), F32) for size, lanes in plan],
            rb2=[vm((size // 8, lanes), F32) for size, lanes in plan],
            rb3=[vm(((quad - 1) * size // (8 * quad), lanes), F32) for size, lanes in plan],
            rb4=[vm((far, size // (8 * quad), lanes), F32) for size, lanes in plan if far > 1],
            load_sem=dma((16,)), near_s=dma((7,)), near_r=dma((7,)), wide_s=dma((7,)), wide_r=dma((7,)),
            pool_s=dma((1,)), pool_r=dma((1,)), chunk_s=dma((9, 3)), chunk_r=dma((9, 9)),
        )
        names = (*arg_names(), *outs, *scratch)

        def kernel(*refs):
            t = Step(cfg, SimpleNamespace(**dict(zip(names, refs, strict=True))))
            prologue(t)
            backward(t, *forward(t))

        results = pl.pallas_call(
            kernel,
            out_shape=list(outs.values()),
            in_specs=[hbm] * len(given),
            out_specs=[vmem] * len(outs),
            scratch_shapes=list(scratch.values()),
            compiler_params=pltpu.CompilerParams(
                collective_id=0, has_side_effects=True, vmem_limit_bytes=50 * 1024 * 1024
            ),
        )(*given)
        vector = jax.ShapeDtypeStruct((mid,), F32)
        wide_vector = jax.ShapeDtypeStruct((feat,), F32)
        flat_grad, *rest = pl.pallas_call(
            store,
            out_shape=[
                jax.ShapeDtypeStruct(flat_shape, BF16),
                jax.ShapeDtypeStruct((feat, mid), F32),
                jax.ShapeDtypeStruct((3, 3, mid, mid), F32),
                jax.ShapeDtypeStruct((mid, feat), F32),
                vector, vector, vector, vector, wide_vector, wide_vector,
            ],
            in_specs=[vmem] * 8,
            out_specs=[hbm] * 10,
            scratch_shapes=[*(vm((c,), F32) for c in (feat, feat, mid, mid, mid, mid)), dma((12,))],
            compiler_params=pltpu.CompilerParams(vmem_limit_bytes=8 * 1024 * 1024),
        )(*(pltpu.with_memory_space_constraint(part, pltpu.VMEM) for part in results))
        grad_frames = flat_grad.reshape(height, width, feat // 128, slots, 128).transpose(0, 1, 3, 2, 4)
        return grad_frames.reshape(height, width, slots, feat).transpose(2, 0, 1, 3), *rest

    split = P("clip")
    in_specs = (split,) + (P(),) * 9 + (split,) * 3 + (P(), P())
    out_specs = (split,) + (P(),) * 9
    return jax.shard_map(shards, mesh=mesh, in_specs=in_specs, out_specs=out_specs, check_vma=False)


def arg_names():
    return dict(
        frames=0, w_reduce=0, w_spatial=0, w_expand=0, gain_a=0, bias_a=0, gain_b=0, bias_b=0, gain_c=0, bias_c=0,
        clip_ids=0, segment_ids=0, slot_valid=0, segment_weight=0, loss_weight=0,
    )
```

```python
import functools
from types import SimpleNamespace

import jax
import jax.numpy as jnp
from jax import lax
from jax.experimental import pallas as pl
from jax.experimental.pallas import tpu as pltpu
from jax.sharding import PartitionSpec as P

MESH = pl.DeviceIdType.MESH
EPS = 1e-05
F32 = jnp.float32
BF16 = jnp.bfloat16
SIDE = 16
ROWS = SIDE * SIDE
NN = (((1,), (0,)), ((), ()))
NT = (((1,), (1,)), ((), ()))

ORDER = (
    (),
    (),
    (),
    (),
    (),
    (),
    (0, 1,),
    (2, 0,),
    (1,),
    (2, 0, 1, 3,),
    (2, 4,),
    (),
    (),
    (0,),
    (1, 3, 5, 2, 4,),
    (6, 3, 8,),
    (1, 0, 5, 7, 4, 8, 1, 3, 6, 7, 8, 2, 0,),
    (4, 7, 3,),
    (6, 2, 8, 1, 5, 0, 4, 7, 3, 6, 8, 5, 7, 1, 6, 4,),
    (5, 6, 0, 3,),
    (7,),
    (8, 2, 4, 5, 7, 8, 6, 3, 5,),
    (7, 8, 6, 5, 4, 2,),
)


def dot(a, b, dims=NN):
    return lax.dot_general(a, b, dims, preferred_element_type=F32)


def wait_bytes(ref, sem):
    pltpu.make_async_copy(ref, ref, sem).wait()


def by_rows(ref, value):
    for k in range(ref.shape[0] // 256):
        ref[k * 256 : (k + 1) * 256, :] = value(slice(k * 256, (k + 1) * 256))


def moved_rows(here, at):
    return slice(here.start + at, here.stop + at)


def block(k, y):
    return pl.multiple_of(k * ROWS + y * SIDE, SIDE)


def to_dense(ref, at, value, first):
    for q in range(value.shape[1] // 128):
        ref[at, pl.ds(first + q, 1), :] = value[:, q * 128 : (q + 1) * 128]


def row_form(ref, row, source, first, count, lane=0):
    for q in range(count):
        ref[row : row + 1, (lane + q) * 128 : (lane + q + 1) * 128] = source[first + q : first + q + 1, :]


def three(ref, at, left, middle, right):
    here, wide = pl.ds(at + SIDE, SIDE), middle.shape[1]
    ref[here, 0:wide] = left.astype(BF16)
    ref[here, wide : 2 * wide] = middle.astype(BF16)
    ref[here, 2 * wide : 3 * wide] = right.astype(BF16)


def dense_of(ref1, scratch):
    count = ref1.shape[0] // 128
    for q in range(count):
        scratch[q : q + 1, :] = ref1[q * 128 : (q + 1) * 128].reshape(1, 128)
    return scratch[0:count, :]


class Step:
    def __init__(self, cfg, r):
        self.r, self.sizes = r, cfg
        self.n, self.slots, self.height, self.width, self.feat, self.mid = cfg
        self.live = self.slots - 1
        self.rows = self.live * ROWS
        self.area = self.height * self.width
        self.inner = 8
        self.outer = self.n // 8
        self.quad = min(4, self.outer)
        self.far = self.outer // self.quad
        self.loads = {}
        self.mask = lax.broadcasted_iota(jnp.int32, (SIDE, 256), 0) < self.width

    def load(self, **pairs):
        for name, (src, dst) in pairs.items():
            copy = pltpu.make_async_copy(src, dst, self.r.load_sem.at[len(self.loads)])
            copy.start()
            self.loads[name] = copy

    def loaded(self, **names):
        for name in names:
            self.loads[name].wait()

    def fold(self, value):
        return jnp.sum(jnp.where(self.mask, value, 0.0), axis=0, keepdims=True)

    def slot_facts(self):
        r, live = self.r, self.live
        alive, later = 1, []
        for k in range(live):
            alive = alive * r.valid[k]
            later.append(1 - alive)
        self.keep = [(1 - q).astype(F32) for q in later]
        self.moved = [q.astype(F32) for q in later]
        self.later = later
        self.v = [self.kept(r.valid, k) for k in range(live)]
        self.n_own = (self.v[0] + self.v[1] + self.v[2]) * float(self.area)

    def kept(self, values, k):
        return (values[k] + self.later[k] * (values[k + 1] - values[k])).astype(F32)

    def places(self):
        n = self.n
        self.me = me = lax.axis_index("clip")
        self.low, self.high = low, high = me % self.inner, me // self.inner
        self.direct = n <= 32
        self.peers = flips(me, n)
        self.low_peers = flips(me, self.inner)
        self.high_peers = flips(me, self.outer, self.inner)
        self.clip_peers = [(me + o) % n for o in (n // 2 - 1, n // 2 + 1, n // 2, n - 1, 1)]

    def greet(self):
        self.greeted = self.peers if self.direct else self.low_peers + self.high_peers + self.clip_peers
        self.barrier = pltpu.get_barrier_semaphore()
        for device in self.greeted:
            pl.semaphore_signal(self.barrier, inc=1, device_id=(device,), device_id_type=MESH)

    def all_here(self):
        pl.semaphore_wait(self.barrier, len(self.greeted))

    def send(self, src, dst, ssem, rsem, device):
        pltpu.make_async_remote_copy(
            src_ref=src, dst_ref=dst, send_sem=ssem, recv_sem=rsem, device_id=(device,), device_id_type=MESH
        ).start()

    def one_stage(self, at):
        return self.direct and at not in (2, 3, 6)

    def near_at(self, at):
        return self.me if self.one_stage(at) else self.low

    def near_send(self, at):
        buf, mine = self.r.near[at], self.near_at(at)
        for device in self.peers if self.one_stage(at) else self.low_peers:
            self.send(buf.at[mine], buf.at[mine], self.r.near_s.at[at], self.r.near_r.at[at], device)

    def near_wait(self, at, sems):
        buf = self.r.near[at]
        wait_bytes(buf.at[pl.ds(0, buf.shape[0] - 1)], sems.at[at])

    def wide_send(self, at):
        buf = self.r.wide[at]
        for device in self.high_peers:
            self.send(buf.at[self.high], buf.at[self.high], self.r.wide_s.at[at], self.r.wide_r.at[at], device)

    def wide_wait(self, at, sems):
        wait_bytes(self.r.wide[at].at[pl.ds(0, self.outer - 1)], sems.at[at])

    def all_sent(self, *rounds):
        for at in rounds:
            self.near_wait(at, self.r.near_s)
            if not self.one_stage(at):
                self.wide_wait(at, self.r.wide_s)

    def near_count(self, q):
        return self.r.near[0][(self.me - self.low + q) if self.direct else q, 4:5, :]

    def wide_count(self, q):
        return self.r.plane[q, 0:1, :] if self.direct else self.r.wide[0][q, 4:5, :]

    def stats_near(self, at, count):
        if self.one_stage(at):
            return
        self.near_wait(at, self.r.near_r)
        n_all, s_all, _, spread = combine(self.r.near[at], self.near_count, self.inner, count)
        buf = self.r.wide[at]
        buf[self.high, 0:count, :] = s_all
        buf[self.high, count : 2 * count, :] = spread
        if at == 0:
            buf[self.high, 4:5, :] = n_all
        self.wide_send(at)

    def stats_wide(self, at, count, table, first=0):
        r = self.r
        if self.one_stage(at):
            self.near_wait(at, r.near_r)
            counts = r.near[0]
            n_all, _, mean, spread = combine(r.near[at], lambda q: counts[q, 4:5, :], self.n, count)
        else:
            self.wide_wait(at, r.wide_r)
            n_all, _, mean, spread = combine(r.wide[at], self.wide_count, self.outer, count)
        if at == 0 and self.direct:
            counts = r.near[0]
            for q in range(self.outer):
                r.plane[q, 0:1, :] = sum(counts[q * self.inner + m, 4:5, :] for m in range(self.inner))
        inverse = lax.rsqrt(spread / n_all + EPS)
        r.dense[0:count, :] = mean
        row_form(table, 0, r.dense, 0, count, first)
        r.dense[0:count, :] = inverse
        row_form(table, 1, r.dense, 0, count, first)
        return n_all, inverse

    def sums_near(self, at):
        if not self.one_stage(at):
            self.near_wait(at, self.r.near_r)
            self.r.wide[at][self.high] = total(self.r.near[at])
            self.wide_send(at)

    def sums_wide(self, at):
        if self.one_stage(at):
            self.near_wait(at, self.r.near_r)
            return total(self.r.near[at])
        self.wide_wait(at, self.r.wide_r)
        return total(self.r.wide[at])

    def local_stats(self, buf, at, ref, first=0, channels=None):
        channels = channels or ref.shape[1]
        count = channels // 128
        for c in range(channels // 256):
            lanes = slice(first + c * 256, first + (c + 1) * 256)

            def gather(term):
                acc = jnp.zeros((SIDE, 256), F32)
                for k in range(self.live):
                    part = lax.fori_loop(
                        0, self.height, lambda y, a: a + term(ref[pl.ds(block(k, y), SIDE), lanes]),
                        jnp.zeros((SIDE, 256), F32), unroll=self.height,
                    )
                    acc = acc + part * self.v[k]
                return self.fold(acc)

            s_own = gather(lambda x: x)
            mean = s_own / jnp.maximum(self.n_own, 1.0)
            to_dense(buf, at, s_own, 2 * c)
            to_dense(buf, at, gather(lambda x: (x - mean) * (x - mean)), count + 2 * c)

    def norm_silu(self, ref, slope_ref, table, gain, bias, write):
        centre, scale = table[0:1, :], table[1:2, :] * gain[...].reshape(1, self.mid)
        b = bias[...].reshape(1, self.mid)
        for k in range(self.live):
            def step(y, carry):
                at = block(k, y)
                u = (ref[pl.ds(at, SIDE), :] - centre) * scale + b
                s = 0.5 * jnp.tanh(0.5 * u) + 0.5
                h = u * s
                slope_ref[pl.ds(at, SIDE), :] = jnp.where(self.mask, s + (h - h * s), 0.0)
                write(at, jnp.where(self.mask, h, 0.0))
                return carry

            lax.fori_loop(0, self.height, step, 0, unroll=self.height)


def flips(index, count, stride=1):
    steps, at = [], 1
    while at < count:
        steps.append(at * stride * (1 - 2 * ((index // (at * stride)) % 2)))
        at *= 2
    return [sum((d for b, d in enumerate(steps) if o >> b & 1), index) for o in reversed(range(1, count))]


def combine(buf, counts, group, count):
    n_part = [counts(q) for q in range(group)]
    s_part = [buf[q, 0:count, :] for q in range(group)]
    n_all = sum(n_part[1:], n_part[0])
    s_all = sum(s_part[1:], s_part[0])
    mean = s_all / jnp.maximum(n_all, 1.0)
    spread = jnp.zeros((count, 128), F32)
    for q in range(group):
        gap = s_part[q] / jnp.maximum(n_part[q], 1.0) - mean
        spread = spread + (buf[q, count : 2 * count, :] + n_part[q] * gap * gap)
    return n_all, s_all, mean, spread


def total(buf):
    out = buf[0]
    for q in range(1, buf.shape[0]):
        out = out + buf[q]
    return out


def clear(*refs):
    for ref in refs:
        ref[...] = jnp.zeros(ref.shape, ref.dtype)


def prologue(t):
    r, slots, live, width, feat = t.r, t.slots, t.live, t.width, t.feat
    t.places()
    t.greet()
    t.load(
        frames=(r.frames, r.f4.at[pl.ds(0, t.area)]), valid=(r.slot_valid, r.valid), reduce=(r.w_reduce, r.wr)
    )
    r.f4[t.area :] = jnp.zeros((r.f4.shape[0] - t.area, *r.f4.shape[1:]), BF16)
    clear(r.fp)
    t.loaded(valid=0)
    t.slot_facts()
    t.loaded(frames=0)
    t.load(
        clip=(r.clip_ids, r.clip), segment=(r.segment_ids, r.segment),
        share=(r.segment_weight, r.share), spatial=(r.w_spatial, r.ws), expand=(r.w_expand, r.we),
        ga=(r.gain_a, r.ga), ba=(r.bias_a, r.ba), gb=(r.gain_b, r.gb), bb=(r.bias_b, r.bb),
        gc=(r.gain_c, r.gc), bc=(r.bias_c, r.bc), loss=(r.loss_weight, r.loss),
    )
    for i in range(3):
        for j in range(3):
            pltpu.make_async_copy(
                r.w_spatial.at[i, j], r.wc.at[i, :, pl.ds(j * t.mid, t.mid)], r.load_sem.at[15]
            ).start()
    fp, f4 = r.fp, r.f4
    tiles = feat // 128
    group = SIDE // slots
    short = lax.broadcasted_iota(jnp.int32, (SIDE, 128), 0) < width

    def regroup(y, carry):
        for p in range(tiles // group):
            value = f4[pl.ds(y * width, SIDE), p * SIDE : (p + 1) * SIDE, :].astype(F32)
            value = jnp.swapaxes(value, 0, 1)
            for q in range(group):
                for k in range(live):
                    row = value[q * slots + k] * t.keep[k] + value[q * slots + k + 1] * t.moved[k]
                    lanes = slice((p * group + q) * 128, (p * group + q + 1) * 128)
                    fp[pl.ds(block(k, y), SIDE), lanes] = jnp.where(short, row, 0.0).astype(BF16)
        return carry

    lax.fori_loop(0, t.height, regroup, 0)
    t.loaded(reduce=0)
    by_rows(r.pre_a, lambda here: dot(fp[here, :], r.wr[...]))
    t.local_stats(r.near[0], t.near_at(0), r.pre_a)
    r.near[0][t.near_at(0), 4:5, :] = jnp.full((1, 128), t.n_own, F32)


def forward(t):
    r, live, mid, feat, rows, area, height = t.r, t.live, t.mid, t.feat, t.rows, t.area, t.height

    def turn(q):
        lanes = slice(q * feat // 4, (q + 1) * feat // 4)
        r.ft[lanes, :] = r.fp[:, lanes].T

    t.all_here()
    t.near_send(0)
    turn(0)
    t.stats_near(0, mid // 128)
    clear(r.xp, r.hb, r.g3, r.gpc, r.gpa)
    t.loaded(clip=0, segment=0, share=0, ga=0, ba=0, gb=0, bb=0, gc=0, bc=0, loss=0, spatial=0, expand=0)
    key = [t.kept(r.clip, k) for k in range(live)]
    weight = []
    for k in range(live):
        at = t.kept(r.segment, k)
        w0, w1, w2 = (r.share[q] for q in range(3))
        weight.append(
            t.v[k] * (w0 * ((1.0 - at) * (2.0 - at) * 0.5) + w1 * (at * (2.0 - at)) + w2 * (at * (at - 1.0) * 0.5))
        )
    n_all, inv_a = t.stats_wide(0, mid // 128, r.table_a)

    xp, hb = r.xp, r.hb

    def write_a(at, h):
        three(xp, at, pltpu.roll(h, 1, 0), h, pltpu.roll(h, SIDE - 1, 0))

    t.norm_silu(r.pre_a, r.slope_a, r.table_a, r.ga, r.ba, write_a)

    by_rows(
        r.pre_b,
        lambda here: sum(dot(xp[moved_rows(here, i * SIDE), :], r.ws[i].reshape(3 * mid, mid)) for i in range(3)),
    )
    t.local_stats(r.near[1], t.near_at(1), r.pre_b)
    t.near_send(1)
    r.xt[...] = xp[SIDE : SIDE + rows, mid : 2 * mid].T
    t.stats_near(1, mid // 128)
    _, inv_b = t.stats_wide(1, mid // 128, r.table_b)

    def write_b(at, h):
        hb[pl.ds(at, SIDE), :] = h.astype(BF16)

    t.norm_silu(r.pre_b, r.slope_b, r.table_b, r.gb, r.bb, write_b)

    pre_c, slope_c, fp, table_c = r.pre_c, r.slope_c, r.fp, r.table_c
    half = feat // 2
    rounds = (2, 6)
    for h, at in enumerate(rounds):
        lanes = slice(h * half, (h + 1) * half)
        for k in range(live):
            here = slice(k * ROWS, (k + 1) * ROWS)
            pre_c[here, lanes] = dot(hb[here, :], r.we[:, lanes])
        t.local_stats(r.near[at], t.near_at(at), pre_c, h * half, half)
        t.near_send(at)
    r.hbt[...] = hb[...].T
    for at in rounds:
        t.stats_near(at, half // 128)
    turn(1)

    pool, slope_sum, slope_hat = r.pool, r.slope_sum, r.slope_hat
    for c in range(feat // 256):
        if c * 256 % half == 0:
            h = c * 256 // half
            _, inv_half = t.stats_wide(rounds[h], half // 128, table_c, h * half // 128)
            r.inv_c[h * half // 128 : (h + 1) * half // 128, :] = inv_half
        lanes = slice(c * 256, (c + 1) * 256)
        centre, inverse = table_c[0:1, lanes], table_c[1:2, lanes]
        g = r.gc[lanes].reshape(1, 256)
        b = r.bc[lanes].reshape(1, 256)
        for k in range(live):
            def step(y, carry):
                a0, a1, a2 = carry
                at = block(k, y)
                hat = (pre_c[pl.ds(at, SIDE), lanes] - centre) * inverse
                u = hat * g + b + fp[pl.ds(at, SIDE), lanes].astype(F32)
                s = 0.5 * jnp.tanh(0.5 * u) + 0.5
                h = u * s
                slope = s + (h - h * s)
                slope_c[pl.ds(at, SIDE), lanes] = slope
                return a0 + h, a1 + slope, a2 + slope * hat

            zero = jnp.zeros((SIDE, 256), F32)
            a0, a1, a2 = lax.fori_loop(0, height, step, (zero, zero, zero), unroll=height)
            p_row = (t.fold(a0) * (1.0 / area)).astype(BF16).astype(F32)
            to_dense(pool, 0, p_row, 8 * k + 2 * c)
            to_dense(slope_sum, k, t.fold(a1), 2 * c)
            to_dense(slope_hat, k, t.fold(a2), 2 * c)
    for k in range(live):
        pool[0, 24 + k : 25 + k, :] = jnp.full((1, 128), key[k], F32)
        pool[0, 28 + k : 29 + k, :] = jnp.full((1, 128), weight[k], F32)
    for q, device in enumerate(t.clip_peers):
        t.send(pool.at[0], pool.at[q + 1], r.pool_s.at[0], r.pool_r.at[0], device)
    turn(2)
    wait_bytes(pool.at[pl.ds(1, len(t.clip_peers))], r.pool_r.at[0])

    lw = dense_of(r.loss, r.dense)
    grads = []
    for k in range(live):
        my_key = jnp.full((1, 128), key[k], F32)
        my_weight = jnp.full((1, 128), weight[k], F32)
        mean = jnp.zeros((8, 128), F32)
        den = jnp.zeros((1, 128), F32)
        for q in range(len(t.clip_peers) + 1):
            for m in range(live):
                match = jnp.where(pool[q, 24 + m : 25 + m, :] == my_key, pool[q, 28 + m : 29 + m, :], 0.0)
                den = den + match
                mean = mean + match * pool[q, 8 * m : 8 * m + 8, :]
        den = jnp.where(den == 0.0, 1.0, den)
        mean = mean / den
        power = jnp.sum(jnp.sum(mean * mean, axis=0, keepdims=True), axis=1, keepdims=True)
        along = jnp.sum(jnp.sum(mean * lw, axis=0, keepdims=True), axis=1, keepdims=True)
        scale = lax.rsqrt(power * (1.0 / feat) + EPS)
        mean_grad = scale * (lw - (mean * scale) * (scale * along * (1.0 / feat)))
        grads.append((my_weight / den) * mean_grad * (1.0 / area))

    inv_c = r.inv_c[...]
    near3 = r.near[3]
    shift = jnp.zeros((8, 128), F32)
    gain = jnp.zeros((8, 128), F32)
    for k in range(live):
        shift = shift + grads[k] * slope_sum[k]
        gain = gain + grads[k] * slope_hat[k]
    near3[t.near_at(3), 0:8, :] = shift
    near3[t.near_at(3), 8:16, :] = gain
    t.near_send(3)
    coef, dense = r.coef, r.dense
    scale_c = dense_of(r.gc, dense) * inv_c
    for k in range(live):
        dense[...] = grads[k]
        row_form(coef, k, dense, 0, feat // 128)
        dense[...] = grads[k] * scale_c
        row_form(coef, 3 + k, dense, 0, feat // 128)
    t.sums_near(3)
    turn(3)
    both = t.sums_wide(3)
    r.vectors_c[...] = both
    dense[...] = both[0:8] * scale_c / n_all
    row_form(coef, 6, dense, 0, feat // 128)
    dense[...] = both[8:16] * scale_c * inv_c / n_all
    row_form(coef, 7, dense, 0, feat // 128)
    return n_all, inv_a, inv_b


def backward(t, n_all, inv_a, inv_b):
    r, live, mid, feat, rows, height = t.r, t.live, t.mid, t.feat, t.rows, t.height
    slots, width, quad, far, v, wc = t.slots, t.width, t.quad, t.far, t.v, r.wc
    coef, pre_c, slope_c, out = r.coef, r.pre_c, r.slope_c, r.vectors
    me, send = t.me, t.send
    gpc = r.gpc
    for k in range(live):
        for c in range(feat // 256):
            lanes = slice(c * 256, (c + 1) * 256)
            centre = r.table_c[0:1, lanes]
            c0 = coef[3 + k : 4 + k, lanes]
            c1 = coef[6:7, lanes] * v[k]
            c2 = coef[7:8, lanes] * v[k]

            def step(y, carry):
                at = block(k, y)
                grad = slope_c[pl.ds(at, SIDE), lanes] * c0 - (c1 + (pre_c[pl.ds(at, SIDE), lanes] - centre) * c2)
                gpc[pl.ds(at, SIDE), lanes] = grad.astype(BF16)
                return carry

            lax.fori_loop(0, height, step, 0, unroll=height)

    def back_sums(at, table, inv, grad_ref, slope_ref, pre_ref):
        zero = jnp.zeros((SIDE, mid), F32)
        carry = (zero, zero)
        centre = table[0:1, :]
        for k in range(live):
            def step(y, c):
                here = pl.ds(block(k, y), SIDE)
                grad = grad_ref[here, :] * slope_ref[here, :]
                grad_ref[here, :] = grad
                return c[0] + grad, c[1] + grad * (pre_ref[here, :] - centre)

            carry = lax.fori_loop(0, height, step, carry, unroll=height)
        buf = r.near[at]
        to_dense(buf, t.near_at(at), jnp.sum(carry[0], axis=0, keepdims=True), 0)
        to_dense(buf, t.near_at(at), jnp.sum(carry[1], axis=0, keepdims=True) * table[1:2, :], 2)

    def back_apply(at, table, gain_ref, inv, grad_ref, pre_ref, write):
        both = t.sums_wide(at)
        out[8 * at - 32 : 8 * at - 28, :] = both[0:4]
        dense = r.dense
        scale = dense_of(gain_ref, dense) * inv
        dense[0:2, :] = scale
        dense[2:4, :] = both[0:2] * scale / n_all
        dense[4:6, :] = both[2:4] * scale * inv / n_all
        for q in range(3):
            row_form(table, 2 + q, dense, 2 * q, 2)
        centre = table[0:1, :]
        for k in range(live):
            c0, c1, c2 = table[2:3, :], table[3:4, :] * v[k], table[4:5, :] * v[k]

            def step(y, carry):
                at_row = block(k, y)
                here = pl.ds(at_row, SIDE)
                write(at_row, grad_ref[here, :] * c0 - (c1 + (pre_ref[here, :] - centre) * c2))
                return carry

            lax.fori_loop(0, height, step, 0, unroll=height)

    core, bit_x, bit_y, at_z = me % 2, (me // 2) % 2, (me // 4) % 2, (me // 8) % quad
    at_far = me // (8 * quad)
    bit1 = bit_x + core * (bit_y - bit_x)
    bit2 = bit_y + core * (bit_x - bit_y)
    sibling = me + 1 - 2 * core
    peer1 = me + (1 - 2 * bit1) * (2 + 2 * core)
    peer2 = me + (1 - 2 * bit2) * (4 - 2 * core)
    z_at = flips(at_z, quad)
    z_peer = [me + 8 * (q - at_z) for q in z_at]
    far_peer = [me + 8 * quad * ((at_far + o) % far - at_far) for o in range(1, far)]
    chunk_s, chunk_r = r.chunk_s, r.chunk_r
    blocks = iter(ORDER)
    plan = [(0, q, 2) for q in range(2)] + [(1 + q, 0, 1) for q in range(3)] + [(4, q, 4) for q in range(4)]

    def chunk(q):
        name, at, count = plan[q]
        size = r.part[name].shape[0] // count
        part = r.part[name].at[pl.ds(at * size, size)]
        whole = (r.e, r.s0, r.s1, r.s2, r.r)[name].at[pl.ds(at * size, size)]
        half, quarter, eighth, piece = size // 2, size // 4, size // 8, size // (8 * quad)
        m8 = lambda value: pl.multiple_of(value, 8)
        at_h = m8(core * half)
        at_q = m8(at_h + bit1 * quarter)
        at_e = m8(at_q + bit2 * eighth)
        at_p = m8(at_e + at_z * piece)

        def go(step, src, dst, device):
            send(src, dst, chunk_s.at[q, step // 4], chunk_r.at[q, step], device)

        def finish(step, ref):
            wait_bytes(ref, chunk_r.at[q, step])

        rb0, rb1, rb2, rb3 = r.rb0[q], r.rb1[q], r.rb2[q], r.rb3[q]
        go(0, part.at[pl.ds(m8((1 - core) * half), half)], rb0, sibling)
        yield
        finish(0, rb0)
        part[pl.ds(at_h, half), :] = part[pl.ds(at_h, half), :] + rb0[...]
        go(1, part.at[pl.ds(m8(at_h + (1 - bit1) * quarter), quarter)], rb1, peer1)
        yield
        finish(1, rb1)
        part[pl.ds(at_q, quarter), :] = part[pl.ds(at_q, quarter), :] + rb1[...]
        go(2, part.at[pl.ds(m8(at_q + (1 - bit2) * eighth), eighth)], rb2, peer2)
        yield
        finish(2, rb2)
        part[pl.ds(at_e, eighth), :] = part[pl.ds(at_e, eighth), :] + rb2[...]
        for o in range(quad - 1):
            go(3, part.at[pl.ds(m8(at_e + z_at[o] * piece), piece)], rb3.at[pl.ds(o * piece, piece)], z_peer[o])
        yield
        finish(3, rb3)
        own = part[pl.ds(at_p, piece), :]
        for o in range(quad - 1):
            own = own + rb3[o * piece : (o + 1) * piece, :]
        if far > 1:
            rb4 = r.rb4[q]
            rb4[at_far] = own
            for device in far_peer:
                go(8, rb4.at[at_far], rb4.at[at_far], device)
            yield
            finish(8, rb4.at[pl.ds(0, far - 1)])
            own = rb4[0]
            for o in range(1, far):
                own = own + rb4[o]
        whole[pl.ds(at_p, piece), :] = own
        for o in range(quad - 1):
            go(4, whole.at[pl.ds(at_p, piece)], whole.at[pl.ds(at_p, piece)], z_peer[o])
        yield
        finish(4, whole.at[pl.ds(0, (quad - 1) * piece)])
        go(5, whole.at[pl.ds(at_e, eighth)], whole.at[pl.ds(at_e, eighth)], peer2)
        yield
        finish(5, whole.at[pl.ds(0, eighth)])
        go(6, whole.at[pl.ds(at_q, quarter)], whole.at[pl.ds(at_q, quarter)], peer1)
        yield
        finish(6, whole.at[pl.ds(0, quarter)])
        go(7, whole.at[pl.ds(at_h, half)], whole.at[pl.ds(at_h, half)], sibling)
        yield
        finish(7, whole.at[pl.ds(0, half)])
        yield

    chunks = [chunk(q) for q in range(len(plan))]

    def go_on(*which):
        for q in which:
            next(chunks[q])

    def go_on_all():
        go_on(*next(blocks))

    pre_a, slope_a, pre_b, slope_b, hbt, xt = r.pre_a, r.slope_a, r.pre_b, r.slope_b, r.hbt, r.xt
    we, wr, back = r.we, r.wr, r.back
    tiles = feat // 128
    group = SIDE // slots
    keep, moved, mask = t.keep, t.moved, t.mask
    grad_b, grad_a = r.grad_b, r.grad_a
    wait_bytes(wc, r.load_sem.at[15])
    g3 = r.g3

    def write_gb(at, grad):
        grad = jnp.where(mask, grad, 0.0)
        three(g3, at, pltpu.roll(grad, SIDE - 1, 0), grad, pltpu.roll(grad, 1, 0))

    def spatial_part(i):
        go_on_all()
        value = dot(xt[...], g3[(2 - i) * SIDE : (2 - i) * SIDE + rows, :])
        for j in range(3):
            r.part[1 + i][j * mid : (j + 1) * mid, :] = value[:, j * mid : (j + 1) * mid]
        go_on(2 + i)

    go_on_all()
    go_on_all()
    by_rows(grad_b, lambda here: dot(gpc[here, :], we[...], NT))
    back_sums(4, r.table_b, inv_b, grad_b, slope_b, pre_b)
    t.near_send(4)
    for e in range(2):
        go_on_all()
        for q in range(2 * e, 2 * e + 2):
            lanes = slice(q * 256, (q + 1) * 256)
            r.part[0][e * mid : (e + 1) * mid, q % 2 * 256 : (q % 2 + 1) * 256] = dot(hbt[...], gpc[:, lanes])
        go_on(e)
    t.sums_near(4)
    go_on_all()
    back_apply(4, r.table_b, r.gb, inv_b, grad_b, pre_b, write_gb)
    spatial_part(0)
    go_on_all()
    by_rows(
        grad_a, lambda here: sum(dot(g3[moved_rows(here, (2 - i) * SIDE), :], wc[i], NT) for i in range(3))
    )
    back_sums(5, r.table_a, inv_a, grad_a, slope_a, pre_a)
    t.near_send(5)
    spatial_part(1)
    t.sums_near(5)
    spatial_part(2)
    go_on_all()
    gpa = r.gpa

    def write_ga(at, grad):
        gpa[pl.ds(at, SIDE), :] = grad.astype(BF16)

    back_apply(5, r.table_a, r.ga, inv_a, grad_a, pre_a, write_ga)
    for q in range(4):
        go_on_all()
        r.part[4][q * 256 : (q + 1) * 256, :] = dot(r.ft[q * 256 : (q + 1) * 256, :], gpa[...])
        go_on(5 + q)

    go_on_all()
    by_rows(back, lambda here: dot(gpa[here, :], wr[...], NT))
    gf = r.gf

    def blend(y, carry):
        for p in range(tiles // group):
            values = []
            for q in range(group):
                lanes = slice((p * group + q) * 128, (p * group + q + 1) * 128)
                terms = [
                    slope_c[pl.ds(block(k, y), SIDE), lanes] * coef[k : k + 1, lanes]
                    + back[pl.ds(block(k, y), SIDE), lanes]
                    for k in range(live)
                ]
                values.append(terms[0] * keep[0])
                for m in range(1, live):
                    values.append(terms[m] * keep[m] + terms[m - 1] * moved[m - 1])
                values.append(terms[live - 1] * moved[live - 1])
            value = jnp.swapaxes(jnp.stack(values), 0, 1)
            gf[pl.ds(y * width, width), p * SIDE : (p + 1) * SIDE, :] = value[0:width].astype(BF16)
        return carry

    for q in range(height // 2):
        go_on_all()
        for y in range(2):
            blend(2 * q + y, 0)
    go_on_all()
    for each in chunks:
        for _ in each:
            pass

    t.all_sent(*range(7))
    wait_bytes(r.pool.at[pl.ds(1, len(t.clip_peers))], r.pool_s.at[0])
    for q, (name, _, count) in enumerate(plan):
        part = r.part[name]
        piece = part.shape[0] // count // (8 * quad)
        for m, pieces in enumerate((8 * quad - 1, 8 * quad - 1, far - 1)):
            if pieces:
                wait_bytes(part.at[pl.ds(0, pieces * piece)], chunk_s.at[q, m])


def store(gf, vectors_c, vectors, expand, s0, s1, s2, reduce, frames_out, reduce_out, spatial_out, expand_out, *rest):
    ga, ba, gb, bb, gc, bc, *scratch, sem = rest
    vectors_of = (
        (bc, vectors_c, 0), (gc, vectors_c, 8), (bb, vectors, 0), (gb, vectors, 2), (ba, vectors, 8), (ga, vectors, 10)
    )
    pltpu.make_async_copy(gf, frames_out, sem.at[0]).start()
    pltpu.make_async_copy(reduce, reduce_out, sem.at[1]).start()
    depth, width = expand_out.shape
    for q in range(2):
        pltpu.make_async_copy(
            expand.at[pl.ds(q * depth, depth)], expand_out.at[:, pl.ds(q * width // 2, width // 2)], sem.at[2]
        ).start()
    for i, part in enumerate((s0, s1, s2)):
        for j in range(3):
            pltpu.make_async_copy(part.at[pl.ds(j * depth, depth)], spatial_out.at[i, j], sem.at[3 + i]).start()
    for number, (ref, source, first) in enumerate(vectors_of):
        for q in range(ref.shape[0] // 128):
            scratch[number][q * 128 : (q + 1) * 128] = source[first + q : first + q + 1, :].reshape(128)
        pltpu.make_async_copy(scratch[number], ref, sem.at[6 + number]).start()
    wait_bytes(gf, sem.at[0])
    wait_bytes(reduce, sem.at[1])
    wait_bytes(expand, sem.at[2])
    for i, part in enumerate((s0, s1, s2)):
        wait_bytes(part, sem.at[3 + i])
    for number in range(6):
        wait_bytes(scratch[number], sem.at[6 + number])


def solution(mesh):
    n = mesh.shape["clip"]

    def shards(*args):
        slots, height, width, feat = args[0].shape
        mid = args[1].shape[1]
        rows = (slots - 1) * ROWS
        outer = n // 8
        quad = min(4, outer)
        far = outer // quad
        cfg = (n, slots, height, width, feat, mid)
        flat_shape = (height * width, slots * feat // 128, 128)
        hbm = pl.BlockSpec(memory_space=pltpu.HBM)
        vmem = pl.BlockSpec(memory_space=pltpu.VMEM)
        dma = pltpu.SemaphoreType.DMA
        depths = list(enumerate((5, 4, 8, 16, 4, 4, 8)))
        sizes = [(2 * mid, feat // 2)] + [(3 * mid, mid)] * 3 + [(feat, mid)]

        tiled = args[0].transpose(1, 2, 0, 3).reshape(height, width, slots, feat // 128, 128)
        tiled = tiled.transpose(0, 1, 3, 2, 4).reshape(flat_shape)
        given = [pltpu.with_memory_space_constraint(part, pltpu.HBM) for part in (tiled, *args[1:])]

        vm = pltpu.VMEM
        narrow, broad, square = vm((mid,), F32), vm((feat,), F32), vm((rows, mid), F32)
        ints = pltpu.SMEM((slots,), jnp.int32)
        plan = [(mid, feat // 2)] * 2 + [(3 * mid, mid)] * 3 + [(feat // 4, mid)] * 4
        outs = dict(
            gf=vm(flat_shape, BF16), vectors_c=vm((16, 128), F32), vectors=vm((16, 128), F32),
            **{name: vm(size, F32) for name, size in zip(dict(e=0, s0=0, s1=0, s2=0, r=0), sizes)},
        )
        scratch = dict(
            f4=vm((flat_shape[0] + SIDE - width, *flat_shape[1:]), BF16),
            fp=vm((rows, feat), BF16), ft=vm((feat, rows), BF16),
            wr=vm((feat, mid), BF16), ws=vm((3, 3, mid, mid), BF16), wc=vm((3, mid, 3 * mid), BF16), we=vm((mid, feat), BF16),
            valid=ints, clip=ints, segment=ints, share=pltpu.SMEM(args[13].shape, F32),
            ga=narrow, ba=narrow, gb=narrow, bb=narrow, gc=broad, bc=broad, loss=broad,
            xp=vm((rows + 2 * SIDE, 3 * mid), BF16), xt=vm((mid, rows), BF16),
            hb=vm((rows, mid), BF16), hbt=vm((mid, rows), BF16),
            pre_a=square, slope_a=square, pre_b=square, slope_b=square, grad_a=square, grad_b=square,
            pre_c=vm((rows, feat), F32), slope_c=vm((rows, feat), F32), back=vm((rows, feat), F32),
            gpc=vm((rows, feat), BF16), g3=vm((rows + 2 * SIDE, 3 * mid), BF16), gpa=vm((rows, mid), BF16),
            table_a=vm((8, mid), F32), table_b=vm((8, mid), F32),
            table_c=vm((8, feat), F32), coef=vm((8, feat), F32), dense=vm((8, 128), F32), inv_c=vm((8, 128), F32),
            pool=vm((6, 32, 128), F32), slope_sum=vm((3, 8, 128), F32), slope_hat=vm((3, 8, 128), F32),
            near=[vm((n if n <= 32 and at not in (2, 3, 6) else 8, deep, 128), F32) for at, deep in depths],
            wide=[vm((outer, deep, 128), F32) for at, deep in depths],
            plane=vm((outer, 8, 128), F32),
            part=[vm(size, F32) for size in sizes],
            rb0=[vm((size // 2, lanes), F32) for size, lanes in plan],
            rb1=[vm((size // 4, lanes), F32) for size, lanes in plan],
            rb2=[vm((size // 8, lanes), F32) for size, lanes in plan],
            rb3=[vm(((quad - 1) * size // (8 * quad), lanes), F32) for size, lanes in plan],
            rb4=[vm((far, size // (8 * quad), lanes), F32) for size, lanes in plan if far > 1],
            load_sem=dma((16,)), near_s=dma((7,)), near_r=dma((7,)), wide_s=dma((7,)), wide_r=dma((7,)),
            pool_s=dma((1,)), pool_r=dma((1,)), chunk_s=dma((9, 3)), chunk_r=dma((9, 9)),
        )
        names = (*arg_names(), *outs, *scratch)

        def kernel(*refs):
            t = Step(cfg, SimpleNamespace(**dict(zip(names, refs, strict=True))))
            prologue(t)
            backward(t, *forward(t))

        results = pl.pallas_call(
            kernel,
            out_shape=list(outs.values()),
            in_specs=[hbm] * len(given),
            out_specs=[vmem] * len(outs),
            scratch_shapes=list(scratch.values()),
            compiler_params=pltpu.CompilerParams(
                collective_id=0, has_side_effects=True, vmem_limit_bytes=50 * 1024 * 1024
            ),
        )(*given)
        vector = jax.ShapeDtypeStruct((mid,), F32)
        wide_vector = jax.ShapeDtypeStruct((feat,), F32)
        flat_grad, *rest = pl.pallas_call(
            store,
            out_shape=[
                jax.ShapeDtypeStruct(flat_shape, BF16),
                jax.ShapeDtypeStruct((feat, mid), F32),
                jax.ShapeDtypeStruct((3, 3, mid, mid), F32),
                jax.ShapeDtypeStruct((mid, feat), F32),
                vector, vector, vector, vector, wide_vector, wide_vector,
            ],
            in_specs=[vmem] * 8,
            out_specs=[hbm] * 10,
            scratch_shapes=[*(vm((c,), F32) for c in (feat, feat, mid, mid, mid, mid)), dma((12,))],
            compiler_params=pltpu.CompilerParams(vmem_limit_bytes=8 * 1024 * 1024),
        )(*(pltpu.with_memory_space_constraint(part, pltpu.VMEM) for part in results))
        grad_frames = flat_grad.reshape(height, width, feat // 128, slots, 128).transpose(0, 1, 3, 2, 4)
        return grad_frames.reshape(height, width, slots, feat).transpose(2, 0, 1, 3), *rest

    split = P("clip")
    in_specs = (split,) + (P(),) * 9 + (split,) * 3 + (P(), P())
    out_specs = (split,) + (P(),) * 9
    return jax.shard_map(shards, mesh=mesh, in_specs=in_specs, out_specs=out_specs, check_vma=False)


def arg_names():
    return dict(
        frames=0, w_reduce=0, w_spatial=0, w_expand=0, gain_a=0, bias_a=0, gain_b=0, bias_b=0, gain_c=0, bias_c=0,
        clip_ids=0, segment_ids=0, slot_valid=0, segment_weight=0, loss_weight=0,
    )
```

```python
import functools
from types import SimpleNamespace

import jax
import jax.numpy as jnp
from jax import lax
from jax.experimental import pallas as pl
from jax.experimental.pallas import tpu as pltpu
from jax.sharding import PartitionSpec as P

MESH = pl.DeviceIdType.MESH
EPS = 1e-05
F32 = jnp.float32
BF16 = jnp.bfloat16
SIDE = 16
ROWS = SIDE * SIDE
NN = (((1,), (0,)), ((), ()))
NT = (((1,), (1,)), ((), ()))

ORDER = (
    (),
    (),
    (),
    (),
    (),
    (0, 1,),
    (),
    (1,),
    (0,),
    (2, 1,),
    (3, 0,),
    (),
    (1, 2, 6, 0, 3, 5,),
    (2, 1, 6, 4,),
    (3, 0,),
    (6, 5, 2, 7, 4, 3, 8, 0, 5, 7,),
    (2, 4, 8, 1, 7, 3, 5, 6, 2, 8, 4, 5, 3, 8, 7, 6, 2, 5, 4, 7, 8, 6, 4, 3,),
    (7, 0,),
    (5, 1, 8,),
    (6, 4, 7, 0, 3,),
    (8, 5,),
    (7, 2, 4,),
    (8, 6, 1,),
)


def dot(a, b, dims=NN):
    return lax.dot_general(a, b, dims, preferred_element_type=F32)


def wait_bytes(ref, sem):
    pltpu.make_async_copy(ref, ref, sem).wait()


def by_rows(ref, value):
    for k in range(ref.shape[0] // 256):
        ref[k * 256 : (k + 1) * 256, :] = value(slice(k * 256, (k + 1) * 256))


def moved_rows(here, at):
    return slice(here.start + at, here.stop + at)


def block(k, y):
    return pl.multiple_of(k * ROWS + y * SIDE, SIDE)


def to_dense(ref, at, value, first):
    for q in range(value.shape[1] // 128):
        ref[at, pl.ds(first + q, 1), :] = value[:, q * 128 : (q + 1) * 128]


def row_form(ref, row, source, first, count, lane=0):
    for q in range(count):
        ref[row : row + 1, (lane + q) * 128 : (lane + q + 1) * 128] = source[first + q : first + q + 1, :]


def three(ref, at, left, middle, right):
    here, wide = pl.ds(at + SIDE, SIDE), middle.shape[1]
    ref[here, 0:wide] = left.astype(BF16)
    ref[here, wide : 2 * wide] = middle.astype(BF16)
    ref[here, 2 * wide : 3 * wide] = right.astype(BF16)


def dense_of(ref1, scratch):
    count = ref1.shape[0] // 128
    for q in range(count):
        scratch[q : q + 1, :] = ref1[q * 128 : (q + 1) * 128].reshape(1, 128)
    return scratch[0:count, :]


class Step:
    def __init__(self, cfg, r):
        self.r, self.sizes = r, cfg
        self.n, self.slots, self.height, self.width, self.feat, self.mid = cfg
        self.live = self.slots - 1
        self.rows = self.live * ROWS
        self.area = self.height * self.width
        self.inner = 8
        self.outer = self.n // 8
        self.quad = min(4, self.outer)
        self.far = self.outer // self.quad
        self.loads = {}
        self.mask = lax.broadcasted_iota(jnp.int32, (SIDE, 256), 0) < self.width

    def load(self, **pairs):
        for name, (src, dst) in pairs.items():
            copy = pltpu.make_async_copy(src, dst, self.r.load_sem.at[len(self.loads)])
            copy.start()
            self.loads[name] = copy

    def loaded(self, **names):
        for name in names:
            self.loads[name].wait()

    def fold(self, value):
        return jnp.sum(jnp.where(self.mask, value, 0.0), axis=0, keepdims=True)

    def slot_facts(self):
        r, live = self.r, self.live
        alive, later = 1, []
        for k in range(live):
            alive = alive * r.valid[k]
            later.append(1 - alive)
        self.keep = [(1 - q).astype(F32) for q in later]
        self.moved = [q.astype(F32) for q in later]
        self.later = later
        self.v = [self.kept(r.valid, k) for k in range(live)]
        self.n_own = (self.v[0] + self.v[1] + self.v[2]) * float(self.area)

    def kept(self, values, k):
        return (values[k] + self.later[k] * (values[k + 1] - values[k])).astype(F32)

    def places(self):
        n = self.n
        self.me = me = lax.axis_index("clip")
        self.low, self.high = low, high = me % self.inner, me // self.inner
        self.direct = n <= 32
        self.peers = flips(me, n)
        self.low_peers = flips(me, self.inner)
        self.high_peers = flips(me, self.outer, self.inner)
        self.clip_peers = [(me + o) % n for o in (n // 2 - 1, n // 2 + 1, n // 2, n - 1, 1)]

    def greet(self):
        self.greeted = self.peers if self.direct else self.low_peers + self.high_peers + self.clip_peers
        self.barrier = pltpu.get_barrier_semaphore()
        for device in self.greeted:
            pl.semaphore_signal(self.barrier, inc=1, device_id=(device,), device_id_type=MESH)

    def all_here(self):
        pl.semaphore_wait(self.barrier, len(self.greeted))

    def send(self, src, dst, ssem, rsem, device):
        pltpu.make_async_remote_copy(
            src_ref=src, dst_ref=dst, send_sem=ssem, recv_sem=rsem, device_id=(device,), device_id_type=MESH
        ).start()

    def one_stage(self, at):
        return self.direct and at not in (2, 3, 6)

    def near_at(self, at):
        return self.me if self.one_stage(at) else self.low

    def near_send(self, at):
        buf, mine = self.r.near[at], self.near_at(at)
        for device in self.peers if self.one_stage(at) else self.low_peers:
            self.send(buf.at[mine], buf.at[mine], self.r.near_s.at[at], self.r.near_r.at[at], device)

    def near_wait(self, at, sems):
        buf = self.r.near[at]
        wait_bytes(buf.at[pl.ds(0, buf.shape[0] - 1)], sems.at[at])

    def wide_send(self, at):
        buf = self.r.wide[at]
        for device in self.high_peers:
            self.send(buf.at[self.high], buf.at[self.high], self.r.wide_s.at[at], self.r.wide_r.at[at], device)

    def wide_wait(self, at, sems):
        wait_bytes(self.r.wide[at].at[pl.ds(0, self.outer - 1)], sems.at[at])

    def all_sent(self, *rounds):
        for at in rounds:
            self.near_wait(at, self.r.near_s)
            if not self.one_stage(at):
                self.wide_wait(at, self.r.wide_s)

    def near_count(self, q):
        return self.r.near[0][(self.me - self.low + q) if self.direct else q, 4:5, :]

    def wide_count(self, q):
        return self.r.plane[q, 0:1, :] if self.direct else self.r.wide[0][q, 4:5, :]

    def stats_near(self, at, count):
        if self.one_stage(at):
            return
        self.near_wait(at, self.r.near_r)
        n_all, s_all, _, spread = combine(self.r.near[at], self.near_count, self.inner, count)
        buf = self.r.wide[at]
        buf[self.high, 0:count, :] = s_all
        buf[self.high, count : 2 * count, :] = spread
        if at == 0:
            buf[self.high, 4:5, :] = n_all
        self.wide_send(at)

    def stats_wide(self, at, count, table, first=0):
        r = self.r
        if self.one_stage(at):
            self.near_wait(at, r.near_r)
            counts = r.near[0]
            n_all, _, mean, spread = combine(r.near[at], lambda q: counts[q, 4:5, :], self.n, count)
        else:
            self.wide_wait(at, r.wide_r)
            n_all, _, mean, spread = combine(r.wide[at], self.wide_count, self.outer, count)
        if at == 0 and self.direct:
            counts = r.near[0]
            for q in range(self.outer):
                r.plane[q, 0:1, :] = sum(counts[q * self.inner + m, 4:5, :] for m in range(self.inner))
        inverse = lax.rsqrt(spread / n_all + EPS)
        r.dense[0:count, :] = mean
        row_form(table, 0, r.dense, 0, count, first)
        r.dense[0:count, :] = inverse
        row_form(table, 1, r.dense, 0, count, first)
        return n_all, inverse

    def sums_near(self, at):
        if not self.one_stage(at):
            self.near_wait(at, self.r.near_r)
            self.r.wide[at][self.high] = total(self.r.near[at])
            self.wide_send(at)

    def sums_wide(self, at):
        if self.one_stage(at):
            self.near_wait(at, self.r.near_r)
            return total(self.r.near[at])
        self.wide_wait(at, self.r.wide_r)
        return total(self.r.wide[at])

    def local_stats(self, buf, at, ref, first=0, channels=None):
        channels = channels or ref.shape[1]
        count = channels // 128
        for c in range(channels // 256):
            lanes = slice(first + c * 256, first + (c + 1) * 256)

            def gather(term):
                acc = jnp.zeros((SIDE, 256), F32)
                for k in range(self.live):
                    part = lax.fori_loop(
                        0, self.height, lambda y, a: a + term(ref[pl.ds(block(k, y), SIDE), lanes]),
                        jnp.zeros((SIDE, 256), F32), unroll=self.height,
                    )
                    acc = acc + part * self.v[k]
                return self.fold(acc)

            s_own = gather(lambda x: x)
            mean = s_own / jnp.maximum(self.n_own, 1.0)
            to_dense(buf, at, s_own, 2 * c)
            to_dense(buf, at, gather(lambda x: (x - mean) * (x - mean)), count + 2 * c)

    def norm_silu(self, ref, slope_ref, table, gain, bias, write):
        centre, scale = table[0:1, :], table[1:2, :] * gain[...].reshape(1, self.mid)
        b = bias[...].reshape(1, self.mid)
        for k in range(self.live):
            def step(y, carry):
                at = block(k, y)
                u = (ref[pl.ds(at, SIDE), :] - centre) * scale + b
                s = 0.5 * jnp.tanh(0.5 * u) + 0.5
                h = u * s
                slope_ref[pl.ds(at, SIDE), :] = jnp.where(self.mask, s + (h - h * s), 0.0)
                write(at, jnp.where(self.mask, h, 0.0))
                return carry

            lax.fori_loop(0, self.height, step, 0, unroll=self.height)


def flips(index, count, stride=1):
    steps, at = [], 1
    while at < count:
        steps.append(at * stride * (1 - 2 * ((index // (at * stride)) % 2)))
        at *= 2
    return [sum((d for b, d in enumerate(steps) if o >> b & 1), index) for o in reversed(range(1, count))]


def combine(buf, counts, group, count):
    n_part = [counts(q) for q in range(group)]
    s_part = [buf[q, 0:count, :] for q in range(group)]
    n_all = sum(n_part[1:], n_part[0])
    s_all = sum(s_part[1:], s_part[0])
    mean = s_all / jnp.maximum(n_all, 1.0)
    spread = jnp.zeros((count, 128), F32)
    for q in range(group):
        gap = s_part[q] / jnp.maximum(n_part[q], 1.0) - mean
        spread = spread + (buf[q, count : 2 * count, :] + n_part[q] * gap * gap)
    return n_all, s_all, mean, spread


def total(buf):
    out = buf[0]
    for q in range(1, buf.shape[0]):
        out = out + buf[q]
    return out


def clear(*refs):
    for ref in refs:
        ref[...] = jnp.zeros(ref.shape, ref.dtype)


def prologue(t):
    r, slots, live, width, feat = t.r, t.slots, t.live, t.width, t.feat
    t.places()
    t.greet()
    t.load(
        frames=(r.frames, r.f4.at[pl.ds(0, t.area)]), valid=(r.slot_valid, r.valid), reduce=(r.w_reduce, r.wr)
    )
    r.f4[t.area :] = jnp.zeros((r.f4.shape[0] - t.area, *r.f4.shape[1:]), BF16)
    clear(r.fp)
    t.loaded(valid=0)
    t.slot_facts()
    t.loaded(frames=0)
    t.load(
        clip=(r.clip_ids, r.clip), segment=(r.segment_ids, r.segment),
        share=(r.segment_weight, r.share), spatial=(r.w_spatial, r.ws), expand=(r.w_expand, r.we),
        ga=(r.gain_a, r.ga), ba=(r.bias_a, r.ba), gb=(r.gain_b, r.gb), bb=(r.bias_b, r.bb),
        gc=(r.gain_c, r.gc), bc=(r.bias_c, r.bc), loss=(r.loss_weight, r.loss),
    )
    for i in range(3):
        for j in range(3):
            pltpu.make_async_copy(
                r.w_spatial.at[i, j], r.wc.at[i, :, pl.ds(j * t.mid, t.mid)], r.load_sem.at[15]
            ).start()
    fp, f4 = r.fp, r.f4
    tiles = feat // 128
    group = SIDE // slots
    short = lax.broadcasted_iota(jnp.int32, (SIDE, 128), 0) < width

    def regroup(y, carry):
        for p in range(tiles // group):
            value = f4[pl.ds(y * width, SIDE), p * SIDE : (p + 1) * SIDE, :].astype(F32)
            value = jnp.swapaxes(value, 0, 1)
            for q in range(group):
                for k in range(live):
                    row = value[q * slots + k] * t.keep[k] + value[q * slots + k + 1] * t.moved[k]
                    lanes = slice((p * group + q) * 128, (p * group + q + 1) * 128)
                    fp[pl.ds(block(k, y), SIDE), lanes] = jnp.where(short, row, 0.0).astype(BF16)
        return carry

    lax.fori_loop(0, t.height, regroup, 0)
    t.loaded(reduce=0)
    by_rows(r.pre_a, lambda here: dot(fp[here, :], r.wr[...]))
    t.local_stats(r.near[0], t.near_at(0), r.pre_a)
    r.near[0][t.near_at(0), 4:5, :] = jnp.full((1, 128), t.n_own, F32)


def forward(t):
    r, live, mid, feat, rows, area, height = t.r, t.live, t.mid, t.feat, t.rows, t.area, t.height

    def turn(q):
        lanes = slice(q * feat // 4, (q + 1) * feat // 4)
        r.ft[lanes, :] = r.fp[:, lanes].T

    t.all_here()
    t.near_send(0)
    turn(0)
    t.stats_near(0, mid // 128)
    clear(r.xp, r.hb, r.g3, r.gpc, r.gpa)
    t.loaded(clip=0, segment=0, share=0, ga=0, ba=0, gb=0, bb=0, gc=0, bc=0, loss=0, spatial=0, expand=0)
    key = [t.kept(r.clip, k) for k in range(live)]
    weight = []
    for k in range(live):
        at = t.kept(r.segment, k)
        w0, w1, w2 = (r.share[q] for q in range(3))
        weight.append(
            t.v[k] * (w0 * ((1.0 - at) * (2.0 - at) * 0.5) + w1 * (at * (2.0 - at)) + w2 * (at * (at - 1.0) * 0.5))
        )
    n_all, inv_a = t.stats_wide(0, mid // 128, r.table_a)

    xp, hb = r.xp, r.hb

    def write_a(at, h):
        three(xp, at, pltpu.roll(h, 1, 0), h, pltpu.roll(h, SIDE - 1, 0))

    t.norm_silu(r.pre_a, r.slope_a, r.table_a, r.ga, r.ba, write_a)

    by_rows(
        r.pre_b,
        lambda here: sum(dot(xp[moved_rows(here, i * SIDE), :], r.ws[i].reshape(3 * mid, mid)) for i in range(3)),
    )
    t.local_stats(r.near[1], t.near_at(1), r.pre_b)
    t.near_send(1)
    r.xt[...] = xp[SIDE : SIDE + rows, mid : 2 * mid].T
    t.stats_near(1, mid // 128)
    _, inv_b = t.stats_wide(1, mid // 128, r.table_b)

    def write_b(at, h):
        hb[pl.ds(at, SIDE), :] = h.astype(BF16)

    t.norm_silu(r.pre_b, r.slope_b, r.table_b, r.gb, r.bb, write_b)

    pre_c, slope_c, fp, table_c = r.pre_c, r.slope_c, r.fp, r.table_c
    half = feat // 2
    rounds = (2, 6)
    for h, at in enumerate(rounds):
        lanes = slice(h * half, (h + 1) * half)
        for k in range(live):
            here = slice(k * ROWS, (k + 1) * ROWS)
            pre_c[here, lanes] = dot(hb[here, :], r.we[:, lanes])
        t.local_stats(r.near[at], t.near_at(at), pre_c, h * half, half)
        t.near_send(at)
    r.hbt[...] = hb[...].T
    for at in rounds:
        t.stats_near(at, half // 128)
    turn(1)

    pool, slope_sum, slope_hat = r.pool, r.slope_sum, r.slope_hat
    for c in range(feat // 256):
        if c * 256 % half == 0:
            h = c * 256 // half
            _, inv_half = t.stats_wide(rounds[h], half // 128, table_c, h * half // 128)
            r.inv_c[h * half // 128 : (h + 1) * half // 128, :] = inv_half
        lanes = slice(c * 256, (c + 1) * 256)
        centre, inverse = table_c[0:1, lanes], table_c[1:2, lanes]
        g = r.gc[lanes].reshape(1, 256)
        b = r.bc[lanes].reshape(1, 256)
        for k in range(live):
            def step(y, carry):
                a0, a1, a2 = carry
                at = block(k, y)
                hat = (pre_c[pl.ds(at, SIDE), lanes] - centre) * inverse
                u = hat * g + b + fp[pl.ds(at, SIDE), lanes].astype(F32)
                s = 0.5 * jnp.tanh(0.5 * u) + 0.5
                h = u * s
                slope = s + (h - h * s)
                slope_c[pl.ds(at, SIDE), lanes] = slope
                return a0 + h, a1 + slope, a2 + slope * hat

            zero = jnp.zeros((SIDE, 256), F32)
            a0, a1, a2 = lax.fori_loop(0, height, step, (zero, zero, zero), unroll=height)
            p_row = (t.fold(a0) * (1.0 / area)).astype(BF16).astype(F32)
            to_dense(pool[h], 0, p_row, 4 * k + 2 * (c - 2 * h))
            to_dense(slope_sum, k, t.fold(a1), 2 * c)
            to_dense(slope_hat, k, t.fold(a2), 2 * c)
        if (c + 1) * 256 % half == 0:
            for k in range(live):
                pool[h][0, 12 + k : 13 + k, :] = jnp.full((1, 128), (key, weight)[h][k], F32)
            for q, device in enumerate(t.clip_peers):
                t.send(pool[h].at[0], pool[h].at[q + 1], r.pool_s.at[h], r.pool_r.at[h], device)
    turn(2)
    for h in range(2):
        wait_bytes(pool[h].at[pl.ds(1, len(t.clip_peers))], r.pool_r.at[h])

    lw = dense_of(r.loss, r.dense)
    grads = []
    for k in range(live):
        my_key = jnp.full((1, 128), key[k], F32)
        my_weight = jnp.full((1, 128), weight[k], F32)
        parts = [jnp.zeros((4, 128), F32)] * 2
        den = jnp.zeros((1, 128), F32)
        for q in range(len(t.clip_peers) + 1):
            for m in range(live):
                match = jnp.where(pool[0][q, 12 + m : 13 + m, :] == my_key, pool[1][q, 12 + m : 13 + m, :], 0.0)
                den = den + match
                parts = [parts[h] + match * pool[h][q, 4 * m : 4 * m + 4, :] for h in range(2)]
        den = jnp.where(den == 0.0, 1.0, den)
        for h in range(2):
            r.clip_mean[k, 4 * h : 4 * h + 4, :] = parts[h] / den
        mean = r.clip_mean[k]
        power = jnp.sum(jnp.sum(mean * mean, axis=0, keepdims=True), axis=1, keepdims=True)
        along = jnp.sum(jnp.sum(mean * lw, axis=0, keepdims=True), axis=1, keepdims=True)
        scale = lax.rsqrt(power * (1.0 / feat) + EPS)
        mean_grad = scale * (lw - (mean * scale) * (scale * along * (1.0 / feat)))
        grads.append((my_weight / den) * mean_grad * (1.0 / area))

    inv_c = r.inv_c[...]
    near3 = r.near[3]
    shift = jnp.zeros((8, 128), F32)
    gain = jnp.zeros((8, 128), F32)
    for k in range(live):
        shift = shift + grads[k] * slope_sum[k]
        gain = gain + grads[k] * slope_hat[k]
    near3[t.near_at(3), 0:8, :] = shift
    near3[t.near_at(3), 8:16, :] = gain
    t.near_send(3)
    coef, dense = r.coef, r.dense
    scale_c = dense_of(r.gc, dense) * inv_c
    for k in range(live):
        dense[...] = grads[k]
        row_form(coef, k, dense, 0, feat // 128)
        dense[...] = grads[k] * scale_c
        row_form(coef, 3 + k, dense, 0, feat // 128)
    t.sums_near(3)
    turn(3)
    both = t.sums_wide(3)
    r.vectors_c[...] = both
    dense[...] = both[0:8] * scale_c / n_all
    row_form(coef, 6, dense, 0, feat // 128)
    dense[...] = both[8:16] * scale_c * inv_c / n_all
    row_form(coef, 7, dense, 0, feat // 128)
    return n_all, inv_a, inv_b


def backward(t, n_all, inv_a, inv_b):
    r, live, mid, feat, rows, height = t.r, t.live, t.mid, t.feat, t.rows, t.height
    slots, width, quad, far, v, wc = t.slots, t.width, t.quad, t.far, t.v, r.wc
    coef, pre_c, slope_c, out = r.coef, r.pre_c, r.slope_c, r.vectors
    me, send = t.me, t.send
    gpc = r.gpc
    for k in range(live):
        for c in range(feat // 256):
            lanes = slice(c * 256, (c + 1) * 256)
            centre = r.table_c[0:1, lanes]
            c0 = coef[3 + k : 4 + k, lanes]
            c1 = coef[6:7, lanes] * v[k]
            c2 = coef[7:8, lanes] * v[k]

            def step(y, carry):
                at = block(k, y)
                grad = slope_c[pl.ds(at, SIDE), lanes] * c0 - (c1 + (pre_c[pl.ds(at, SIDE), lanes] - centre) * c2)
                gpc[pl.ds(at, SIDE), lanes] = grad.astype(BF16)
                return carry

            lax.fori_loop(0, height, step, 0, unroll=height)

    def back_sums(at, table, inv, grad_ref, slope_ref, pre_ref):
        zero = jnp.zeros((SIDE, mid), F32)
        carry = (zero, zero)
        centre = table[0:1, :]
        for k in range(live):
            def step(y, c):
                here = pl.ds(block(k, y), SIDE)
                grad = grad_ref[here, :] * slope_ref[here, :]
                grad_ref[here, :] = grad
                return c[0] + grad, c[1] + grad * (pre_ref[here, :] - centre)

            carry = lax.fori_loop(0, height, step, carry, unroll=height)
        buf = r.near[at]
        to_dense(buf, t.near_at(at), jnp.sum(carry[0], axis=0, keepdims=True), 0)
        to_dense(buf, t.near_at(at), jnp.sum(carry[1], axis=0, keepdims=True) * table[1:2, :], 2)

    def back_apply(at, table, gain_ref, inv, grad_ref, pre_ref, write):
        both = t.sums_wide(at)
        out[8 * at - 32 : 8 * at - 28, :] = both[0:4]
        dense = r.dense
        scale = dense_of(gain_ref, dense) * inv
        dense[0:2, :] = scale
        dense[2:4, :] = both[0:2] * scale / n_all
        dense[4:6, :] = both[2:4] * scale * inv / n_all
        for q in range(3):
            row_form(table, 2 + q, dense, 2 * q, 2)
        centre = table[0:1, :]
        for k in range(live):
            c0, c1, c2 = table[2:3, :], table[3:4, :] * v[k], table[4:5, :] * v[k]

            def step(y, carry):
                at_row = block(k, y)
                here = pl.ds(at_row, SIDE)
                write(at_row, grad_ref[here, :] * c0 - (c1 + (pre_ref[here, :] - centre) * c2))
                return carry

            lax.fori_loop(0, height, step, 0, unroll=height)

    core, bit_x, bit_y, at_z = me % 2, (me // 2) % 2, (me // 4) % 2, (me // 8) % quad
    at_far = me // (8 * quad)
    bit1 = bit_x + core * (bit_y - bit_x)
    bit2 = bit_y + core * (bit_x - bit_y)
    sibling = me + 1 - 2 * core
    peer1 = me + (1 - 2 * bit1) * (2 + 2 * core)
    peer2 = me + (1 - 2 * bit2) * (4 - 2 * core)
    z_at = flips(at_z, quad)
    z_peer = [me + 8 * (q - at_z) for q in z_at]
    far_peer = [me + 8 * quad * ((at_far + o) % far - at_far) for o in range(1, far)]
    chunk_s, chunk_r = r.chunk_s, r.chunk_r
    blocks = iter(ORDER)
    plan = [(0, q, 2) for q in range(2)] + [(1 + q, 0, 1) for q in range(3)] + [(4, q, 4) for q in range(4)]

    def chunk(q):
        name, at, count = plan[q]
        size = r.part[name].shape[0] // count
        part = r.part[name].at[pl.ds(at * size, size)]
        whole = (r.e, r.s0, r.s1, r.s2, r.r)[name].at[pl.ds(at * size, size)]
        half, quarter, eighth, piece = size // 2, size // 4, size // 8, size // (8 * quad)
        m8 = lambda value: pl.multiple_of(value, 8)
        at_h = m8(core * half)
        at_q = m8(at_h + bit1 * quarter)
        at_e = m8(at_q + bit2 * eighth)
        at_p = m8(at_e + at_z * piece)

        def go(step, src, dst, device):
            send(src, dst, chunk_s.at[q, step // 4], chunk_r.at[q, step], device)

        def finish(step, ref):
            wait_bytes(ref, chunk_r.at[q, step])

        rb0, rb1, rb2, rb3 = r.rb0[q], r.rb1[q], r.rb2[q], r.rb3[q]
        go(0, part.at[pl.ds(m8((1 - core) * half), half)], rb0, sibling)
        yield
        finish(0, rb0)
        part[pl.ds(at_h, half), :] = part[pl.ds(at_h, half), :] + rb0[...]
        go(1, part.at[pl.ds(m8(at_h + (1 - bit1) * quarter), quarter)], rb1, peer1)
        yield
        finish(1, rb1)
        part[pl.ds(at_q, quarter), :] = part[pl.ds(at_q, quarter), :] + rb1[...]
        go(2, part.at[pl.ds(m8(at_q + (1 - bit2) * eighth), eighth)], rb2, peer2)
        yield
        finish(2, rb2)
        part[pl.ds(at_e, eighth), :] = part[pl.ds(at_e, eighth), :] + rb2[...]
        for o in range(quad - 1):
            go(3, part.at[pl.ds(m8(at_e + z_at[o] * piece), piece)], rb3.at[pl.ds(o * piece, piece)], z_peer[o])
        yield
        finish(3, rb3)
        own = part[pl.ds(at_p, piece), :]
        for o in range(quad - 1):
            own = own + rb3[o * piece : (o + 1) * piece, :]
        if far > 1:
            rb4 = r.rb4[q]
            rb4[at_far] = own
            for device in far_peer:
                go(8, rb4.at[at_far], rb4.at[at_far], device)
            yield
            finish(8, rb4.at[pl.ds(0, far - 1)])
            own = rb4[0]
            for o in range(1, far):
                own = own + rb4[o]
        whole[pl.ds(at_p, piece), :] = own
        for o in range(quad - 1):
            go(4, whole.at[pl.ds(at_p, piece)], whole.at[pl.ds(at_p, piece)], z_peer[o])
        yield
        finish(4, whole.at[pl.ds(0, (quad - 1) * piece)])
        go(5, whole.at[pl.ds(at_e, eighth)], whole.at[pl.ds(at_e, eighth)], peer2)
        yield
        finish(5, whole.at[pl.ds(0, eighth)])
        go(6, whole.at[pl.ds(at_q, quarter)], whole.at[pl.ds(at_q, quarter)], peer1)
        yield
        finish(6, whole.at[pl.ds(0, quarter)])
        go(7, whole.at[pl.ds(at_h, half)], whole.at[pl.ds(at_h, half)], sibling)
        yield
        finish(7, whole.at[pl.ds(0, half)])
        yield

    chunks = [chunk(q) for q in range(len(plan))]

    def go_on(*which):
        for q in which:
            next(chunks[q])

    def go_on_all():
        go_on(*next(blocks))

    pre_a, slope_a, pre_b, slope_b, hbt, xt = r.pre_a, r.slope_a, r.pre_b, r.slope_b, r.hbt, r.xt
    we, wr, back = r.we, r.wr, r.back
    tiles = feat // 128
    group = SIDE // slots
    keep, moved, mask = t.keep, t.moved, t.mask
    grad_b, grad_a = r.grad_b, r.grad_a
    wait_bytes(wc, r.load_sem.at[15])
    g3 = r.g3

    def write_gb(at, grad):
        grad = jnp.where(mask, grad, 0.0)
        three(g3, at, pltpu.roll(grad, SIDE - 1, 0), grad, pltpu.roll(grad, 1, 0))

    def spatial_part(i):
        go_on_all()
        value = dot(xt[...], g3[(2 - i) * SIDE : (2 - i) * SIDE + rows, :])
        for j in range(3):
            r.part[1 + i][j * mid : (j + 1) * mid, :] = value[:, j * mid : (j + 1) * mid]
        go_on(2 + i)

    go_on_all()
    go_on_all()
    by_rows(grad_b, lambda here: dot(gpc[here, :], we[...], NT))
    back_sums(4, r.table_b, inv_b, grad_b, slope_b, pre_b)
    t.near_send(4)
    for e in range(2):
        go_on_all()
        for q in range(2 * e, 2 * e + 2):
            lanes = slice(q * 256, (q + 1) * 256)
            r.part[0][e * mid : (e + 1) * mid, q % 2 * 256 : (q % 2 + 1) * 256] = dot(hbt[...], gpc[:, lanes])
        go_on(e)
    t.sums_near(4)
    go_on_all()
    back_apply(4, r.table_b, r.gb, inv_b, grad_b, pre_b, write_gb)
    go_on_all()
    by_rows(
        grad_a, lambda here: sum(dot(g3[moved_rows(here, (2 - i) * SIDE), :], wc[i], NT) for i in range(3))
    )
    back_sums(5, r.table_a, inv_a, grad_a, slope_a, pre_a)
    t.near_send(5)
    spatial_part(0)
    spatial_part(1)
    t.sums_near(5)
    spatial_part(2)
    go_on_all()
    gpa = r.gpa

    def write_ga(at, grad):
        gpa[pl.ds(at, SIDE), :] = grad.astype(BF16)

    back_apply(5, r.table_a, r.ga, inv_a, grad_a, pre_a, write_ga)
    for q in range(4):
        go_on_all()
        r.part[4][q * 256 : (q + 1) * 256, :] = dot(r.ft[q * 256 : (q + 1) * 256, :], gpa[...])
        go_on(5 + q)

    go_on_all()
    by_rows(back, lambda here: dot(gpa[here, :], wr[...], NT))
    gf = r.gf

    def blend(y, carry):
        for p in range(tiles // group):
            values = []
            for q in range(group):
                lanes = slice((p * group + q) * 128, (p * group + q + 1) * 128)
                terms = [
                    slope_c[pl.ds(block(k, y), SIDE), lanes] * coef[k : k + 1, lanes]
                    + back[pl.ds(block(k, y), SIDE), lanes]
                    for k in range(live)
                ]
                values.append(terms[0] * keep[0])
                for m in range(1, live):
                    values.append(terms[m] * keep[m] + terms[m - 1] * moved[m - 1])
                values.append(terms[live - 1] * moved[live - 1])
            value = jnp.swapaxes(jnp.stack(values), 0, 1)
            gf[pl.ds(y * width, width), p * SIDE : (p + 1) * SIDE, :] = value[0:width].astype(BF16)
        return carry

    for q in range(height // 2):
        go_on_all()
        for y in range(2):
            blend(2 * q + y, 0)
    go_on_all()
    for each in chunks:
        for _ in each:
            pass

    t.all_sent(*range(7))
    for h in range(2):
        wait_bytes(r.pool[h].at[pl.ds(1, len(t.clip_peers))], r.pool_s.at[h])
    for q, (name, _, count) in enumerate(plan):
        part = r.part[name]
        piece = part.shape[0] // count // (8 * quad)
        for m, pieces in enumerate((8 * quad - 1, 8 * quad - 1, far - 1)):
            if pieces:
                wait_bytes(part.at[pl.ds(0, pieces * piece)], chunk_s.at[q, m])


def store(gf, vectors_c, vectors, expand, s0, s1, s2, reduce, frames_out, reduce_out, spatial_out, expand_out, *rest):
    ga, ba, gb, bb, gc, bc, *scratch, sem = rest
    vectors_of = (
        (bc, vectors_c, 0), (gc, vectors_c, 8), (bb, vectors, 0), (gb, vectors, 2), (ba, vectors, 8), (ga, vectors, 10)
    )
    pltpu.make_async_copy(gf, frames_out, sem.at[0]).start()
    pltpu.make_async_copy(reduce, reduce_out, sem.at[1]).start()
    depth, width = expand_out.shape
    for q in range(2):
        pltpu.make_async_copy(
            expand.at[pl.ds(q * depth, depth)], expand_out.at[:, pl.ds(q * width // 2, width // 2)], sem.at[2]
        ).start()
    for i, part in enumerate((s0, s1, s2)):
        for j in range(3):
            pltpu.make_async_copy(part.at[pl.ds(j * depth, depth)], spatial_out.at[i, j], sem.at[3 + i]).start()
    for number, (ref, source, first) in enumerate(vectors_of):
        for q in range(ref.shape[0] // 128):
            scratch[number][q * 128 : (q + 1) * 128] = source[first + q : first + q + 1, :].reshape(128)
        pltpu.make_async_copy(scratch[number], ref, sem.at[6 + number]).start()
    wait_bytes(gf, sem.at[0])
    wait_bytes(reduce, sem.at[1])
    wait_bytes(expand, sem.at[2])
    for i, part in enumerate((s0, s1, s2)):
        wait_bytes(part, sem.at[3 + i])
    for number in range(6):
        wait_bytes(scratch[number], sem.at[6 + number])


def solution(mesh):
    n = mesh.shape["clip"]

    def shards(*args):
        slots, height, width, feat = args[0].shape
        mid = args[1].shape[1]
        rows = (slots - 1) * ROWS
        outer = n // 8
        quad = min(4, outer)
        far = outer // quad
        cfg = (n, slots, height, width, feat, mid)
        flat_shape = (height * width, slots * feat // 128, 128)
        hbm = pl.BlockSpec(memory_space=pltpu.HBM)
        vmem = pl.BlockSpec(memory_space=pltpu.VMEM)
        dma = pltpu.SemaphoreType.DMA
        depths = list(enumerate((5, 4, 8, 16, 4, 4, 8)))
        sizes = [(2 * mid, feat // 2)] + [(3 * mid, mid)] * 3 + [(feat, mid)]

        tiled = args[0].transpose(1, 2, 0, 3).reshape(height, width, slots, feat // 128, 128)
        tiled = tiled.transpose(0, 1, 3, 2, 4).reshape(flat_shape)
        given = [pltpu.with_memory_space_constraint(part, pltpu.HBM) for part in (tiled, *args[1:])]

        vm = pltpu.VMEM
        narrow, broad, square = vm((mid,), F32), vm((feat,), F32), vm((rows, mid), F32)
        ints = pltpu.SMEM((slots,), jnp.int32)
        plan = [(mid, feat // 2)] * 2 + [(3 * mid, mid)] * 3 + [(feat // 4, mid)] * 4
        outs = dict(
            gf=vm(flat_shape, BF16), vectors_c=vm((16, 128), F32), vectors=vm((16, 128), F32),
            **{name: vm(size, F32) for name, size in zip(dict(e=0, s0=0, s1=0, s2=0, r=0), sizes)},
        )
        scratch = dict(
            f4=vm((flat_shape[0] + SIDE - width, *flat_shape[1:]), BF16),
            fp=vm((rows, feat), BF16), ft=vm((feat, rows), BF16),
            wr=vm((feat, mid), BF16), ws=vm((3, 3, mid, mid), BF16), wc=vm((3, mid, 3 * mid), BF16), we=vm((mid, feat), BF16),
            valid=ints, clip=ints, segment=ints, share=pltpu.SMEM(args[13].shape, F32),
            ga=narrow, ba=narrow, gb=narrow, bb=narrow, gc=broad, bc=broad, loss=broad,
            xp=vm((rows + 2 * SIDE, 3 * mid), BF16), xt=vm((mid, rows), BF16),
            hb=vm((rows, mid), BF16), hbt=vm((mid, rows), BF16),
            pre_a=square, slope_a=square, pre_b=square, slope_b=square, grad_a=square, grad_b=square,
            pre_c=vm((rows, feat), F32), slope_c=vm((rows, feat), F32), back=vm((rows, feat), F32),
            gpc=vm((rows, feat), BF16), g3=vm((rows + 2 * SIDE, 3 * mid), BF16), gpa=vm((rows, mid), BF16),
            table_a=vm((8, mid), F32), table_b=vm((8, mid), F32),
            table_c=vm((8, feat), F32), coef=vm((8, feat), F32), dense=vm((8, 128), F32), inv_c=vm((8, 128), F32),
            pool=[vm((6, 16, 128), F32)] * 2, clip_mean=vm((3, 8, 128), F32), slope_sum=vm((3, 8, 128), F32), slope_hat=vm((3, 8, 128), F32),
            near=[vm((n if n <= 32 and at not in (2, 3, 6) else 8, deep, 128), F32) for at, deep in depths],
            wide=[vm((outer, deep, 128), F32) for at, deep in depths],
            plane=vm((outer, 8, 128), F32),
            part=[vm(size, F32) for size in sizes],
            rb0=[vm((size // 2, lanes), F32) for size, lanes in plan],
            rb1=[vm((size // 4, lanes), F32) for size, lanes in plan],
            rb2=[vm((size // 8, lanes), F32) for size, lanes in plan],
            rb3=[vm(((quad - 1) * size // (8 * quad), lanes), F32) for size, lanes in plan],
            rb4=[vm((far, size // (8 * quad), lanes), F32) for size, lanes in plan if far > 1],
            load_sem=dma((16,)), near_s=dma((7,)), near_r=dma((7,)), wide_s=dma((7,)), wide_r=dma((7,)),
            pool_s=dma((2,)), pool_r=dma((2,)), chunk_s=dma((9, 3)), chunk_r=dma((9, 9)),
        )
        names = (*arg_names(), *outs, *scratch)

        def kernel(*refs):
            t = Step(cfg, SimpleNamespace(**dict(zip(names, refs, strict=True))))
            prologue(t)
            backward(t, *forward(t))

        results = pl.pallas_call(
            kernel,
            out_shape=list(outs.values()),
            in_specs=[hbm] * len(given),
            out_specs=[vmem] * len(outs),
            scratch_shapes=list(scratch.values()),
            compiler_params=pltpu.CompilerParams(
                collective_id=0, has_side_effects=True, vmem_limit_bytes=50 * 1024 * 1024
            ),
        )(*given)
        vector = jax.ShapeDtypeStruct((mid,), F32)
        wide_vector = jax.ShapeDtypeStruct((feat,), F32)
        flat_grad, *rest = pl.pallas_call(
            store,
            out_shape=[
                jax.ShapeDtypeStruct(flat_shape, BF16),
                jax.ShapeDtypeStruct((feat, mid), F32),
                jax.ShapeDtypeStruct((3, 3, mid, mid), F32),
                jax.ShapeDtypeStruct((mid, feat), F32),
                vector, vector, vector, vector, wide_vector, wide_vector,
            ],
            in_specs=[vmem] * 8,
            out_specs=[hbm] * 10,
            scratch_shapes=[*(vm((c,), F32) for c in (feat, feat, mid, mid, mid, mid)), dma((12,))],
            compiler_params=pltpu.CompilerParams(vmem_limit_bytes=8 * 1024 * 1024),
        )(*(pltpu.with_memory_space_constraint(part, pltpu.VMEM) for part in results))
        grad_frames = flat_grad.reshape(height, width, feat // 128, slots, 128).transpose(0, 1, 3, 2, 4)
        return grad_frames.reshape(height, width, slots, feat).transpose(2, 0, 1, 3), *rest

    split = P("clip")
    in_specs = (split,) + (P(),) * 9 + (split,) * 3 + (P(), P())
    out_specs = (split,) + (P(),) * 9
    return jax.shard_map(shards, mesh=mesh, in_specs=in_specs, out_specs=out_specs, check_vma=False)


def arg_names():
    return dict(
        frames=0, w_reduce=0, w_spatial=0, w_expand=0, gain_a=0, bias_a=0, gain_b=0, bias_b=0, gain_c=0, bias_c=0,
        clip_ids=0, segment_ids=0, slot_valid=0, segment_weight=0, loss_weight=0,
    )
```

```python
import functools
from types import SimpleNamespace

import jax
import jax.numpy as jnp
from jax import lax
from jax.experimental import pallas as pl
from jax.experimental.pallas import tpu as pltpu
from jax.sharding import PartitionSpec as P

MESH = pl.DeviceIdType.MESH
EPS = 1e-05
F32 = jnp.float32
BF16 = jnp.bfloat16
SIDE = 16
ROWS = SIDE * SIDE
NN = (((1,), (0,)), ((), ()))
NT = (((1,), (1,)), ((), ()))

ORDER = (
    (),
    (),
    (),
    (),
    (),
    (),
    (0, 1,),
    (2, 0,),
    (1,),
    (2, 0, 1, 3,),
    (2, 4,),
    (),
    (),
    (0,),
    (1, 3, 5, 2, 4,),
    (6, 3, 8,),
    (1, 0, 5, 7, 4, 8, 1, 3, 6, 7, 8, 2, 0,),
    (4, 7, 3,),
    (6, 2, 8, 1, 5, 0, 4, 7, 3, 6, 8, 5, 7, 1, 6, 4,),
    (5, 6, 0, 3,),
    (7,),
    (8, 2, 4, 5, 7, 8, 6, 3, 5,),
    (7, 8, 6, 5, 4, 2,),
)


def dot(a, b, dims=NN):
    return lax.dot_general(a, b, dims, preferred_element_type=F32)


def wait_bytes(ref, sem):
    pltpu.make_async_copy(ref, ref, sem).wait()


def by_rows(ref, value):
    for k in range(ref.shape[0] // 256):
        ref[k * 256 : (k + 1) * 256, :] = value(slice(k * 256, (k + 1) * 256))


def moved_rows(here, at):
    return slice(here.start + at, here.stop + at)


def block(k, y):
    return pl.multiple_of(k * ROWS + y * SIDE, SIDE)


def to_dense(ref, at, value, first):
    for q in range(value.shape[1] // 128):
        ref[at, pl.ds(first + q, 1), :] = value[:, q * 128 : (q + 1) * 128]


def row_form(ref, row, source, first, count, lane=0):
    for q in range(count):
        ref[row : row + 1, (lane + q) * 128 : (lane + q + 1) * 128] = source[first + q : first + q + 1, :]


def three(ref, at, left, middle, right):
    here, wide = pl.ds(at + SIDE, SIDE), middle.shape[1]
    ref[here, 0:wide] = left.astype(BF16)
    ref[here, wide : 2 * wide] = middle.astype(BF16)
    ref[here, 2 * wide : 3 * wide] = right.astype(BF16)


def dense_of(ref1, scratch):
    count = ref1.shape[0] // 128
    for q in range(count):
        scratch[q : q + 1, :] = ref1[q * 128 : (q + 1) * 128].reshape(1, 128)
    return scratch[0:count, :]


class Step:
    def __init__(self, cfg, r):
        self.r, self.sizes = r, cfg
        self.n, self.slots, self.height, self.width, self.feat, self.mid = cfg
        self.live = self.slots - 1
        self.rows = self.live * ROWS
        self.area = self.height * self.width
        self.inner = 8
        self.outer = self.n // 8
        self.quad = min(4, self.outer)
        self.far = self.outer // self.quad
        self.loads = {}
        self.mask = lax.broadcasted_iota(jnp.int32, (SIDE, 256), 0) < self.width

    def load(self, **pairs):
        for name, (src, dst) in pairs.items():
            copy = pltpu.make_async_copy(src, dst, self.r.load_sem.at[len(self.loads)])
            copy.start()
            self.loads[name] = copy

    def loaded(self, **names):
        for name in names:
            self.loads[name].wait()

    def fold(self, value):
        return jnp.sum(jnp.where(self.mask, value, 0.0), axis=0, keepdims=True)

    def slot_facts(self):
        r, live = self.r, self.live
        alive, later = 1, []
        for k in range(live):
            alive = alive * r.valid[k]
            later.append(1 - alive)
        self.keep = [(1 - q).astype(F32) for q in later]
        self.moved = [q.astype(F32) for q in later]
        self.later = later
        self.v = [self.kept(r.valid, k) for k in range(live)]
        self.n_own = (self.v[0] + self.v[1] + self.v[2]) * float(self.area)

    def kept(self, values, k):
        return (values[k] + self.later[k] * (values[k + 1] - values[k])).astype(F32)

    def places(self):
        n = self.n
        self.me = me = lax.axis_index("clip")
        self.low, self.high = low, high = me % self.inner, me // self.inner
        self.direct = n <= 32
        self.peers = flips(me, n)
        self.low_peers = flips(me, self.inner)
        self.high_peers = flips(me, self.outer, self.inner)
        self.clip_peers = [(me + o) % n for o in (n // 2 - 1, n // 2 + 1, n // 2, n - 1, 1)]

    def greet(self):
        self.greeted = self.peers if self.direct else self.low_peers + self.high_peers + self.clip_peers
        self.barrier = pltpu.get_barrier_semaphore()
        for device in self.greeted:
            pl.semaphore_signal(self.barrier, inc=1, device_id=(device,), device_id_type=MESH)

    def all_here(self):
        pl.semaphore_wait(self.barrier, len(self.greeted))

    def send(self, src, dst, ssem, rsem, device):
        pltpu.make_async_remote_copy(
            src_ref=src, dst_ref=dst, send_sem=ssem, recv_sem=rsem, device_id=(device,), device_id_type=MESH
        ).start()

    def one_stage(self, at):
        return self.direct and at not in (2, 3, 6)

    def near_at(self, at):
        return self.me if self.one_stage(at) else self.low

    def near_send(self, at):
        buf, mine = self.r.near[at], self.near_at(at)
        for device in self.peers if self.one_stage(at) else self.low_peers:
            self.send(buf.at[mine], buf.at[mine], self.r.near_s.at[at], self.r.near_r.at[at], device)

    def near_wait(self, at, sems):
        buf = self.r.near[at]
        wait_bytes(buf.at[pl.ds(0, buf.shape[0] - 1)], sems.at[at])

    def wide_send(self, at):
        buf = self.r.wide[at]
        for device in self.high_peers:
            self.send(buf.at[self.high], buf.at[self.high], self.r.wide_s.at[at], self.r.wide_r.at[at], device)

    def wide_wait(self, at, sems):
        wait_bytes(self.r.wide[at].at[pl.ds(0, self.outer - 1)], sems.at[at])

    def all_sent(self, *rounds):
        for at in rounds:
            self.near_wait(at, self.r.near_s)
            if not self.one_stage(at):
                self.wide_wait(at, self.r.wide_s)

    def near_count(self, q):
        return self.r.near[0][(self.me - self.low + q) if self.direct else q, 4:5, :]

    def wide_count(self, q):
        return self.r.plane[q, 0:1, :] if self.direct else self.r.wide[0][q, 4:5, :]

    def stats_near(self, at, count):
        if self.one_stage(at):
            return
        self.near_wait(at, self.r.near_r)
        n_all, s_all, _, spread = combine(self.r.near[at], self.near_count, self.inner, count)
        buf = self.r.wide[at]
        buf[self.high, 0:count, :] = s_all
        buf[self.high, count : 2 * count, :] = spread
        if at == 0:
            buf[self.high, 4:5, :] = n_all
        self.wide_send(at)

    def stats_wide(self, at, count, table, first=0):
        r = self.r
        if self.one_stage(at):
            self.near_wait(at, r.near_r)
            counts = r.near[0]
            n_all, _, mean, spread = combine(r.near[at], lambda q: counts[q, 4:5, :], self.n, count)
        else:
            self.wide_wait(at, r.wide_r)
            n_all, _, mean, spread = combine(r.wide[at], self.wide_count, self.outer, count)
        if at == 0 and self.direct:
            counts = r.near[0]
            for q in range(self.outer):
                r.plane[q, 0:1, :] = sum(counts[q * self.inner + m, 4:5, :] for m in range(self.inner))
        inverse = lax.rsqrt(spread / n_all + EPS)
        r.dense[0:count, :] = mean
        row_form(table, 0, r.dense, 0, count, first)
        r.dense[0:count, :] = inverse
        row_form(table, 1, r.dense, 0, count, first)
        return n_all, inverse

    def sums_near(self, at):
        if not self.one_stage(at):
            self.near_wait(at, self.r.near_r)
            self.r.wide[at][self.high] = total(self.r.near[at])
            self.wide_send(at)

    def sums_wide(self, at):
        if self.one_stage(at):
            self.near_wait(at, self.r.near_r)
            return total(self.r.near[at])
        self.wide_wait(at, self.r.wide_r)
        return total(self.r.wide[at])

    def local_stats(self, buf, at, ref, first=0, channels=None):
        channels = channels or ref.shape[1]
        count = channels // 128
        for c in range(channels // 256):
            lanes = slice(first + c * 256, first + (c + 1) * 256)

            def gather(term):
                acc = jnp.zeros((SIDE, 256), F32)
                for k in range(self.live):
                    part = lax.fori_loop(
                        0, self.height, lambda y, a: a + term(ref[pl.ds(block(k, y), SIDE), lanes]),
                        jnp.zeros((SIDE, 256), F32), unroll=self.height,
                    )
                    acc = acc + part * self.v[k]
                return self.fold(acc)

            s_own = gather(lambda x: x)
            mean = s_own / jnp.maximum(self.n_own, 1.0)
            to_dense(buf, at, s_own, 2 * c)
            to_dense(buf, at, gather(lambda x: (x - mean) * (x - mean)), count + 2 * c)

    def norm_silu(self, ref, slope_ref, table, gain, bias, write):
        centre, scale = table[0:1, :], table[1:2, :] * gain[...].reshape(1, self.mid)
        b = bias[...].reshape(1, self.mid)
        for k in range(self.live):
            def step(y, carry):
                at = block(k, y)
                u = (ref[pl.ds(at, SIDE), :] - centre) * scale + b
                s = 0.5 * jnp.tanh(0.5 * u) + 0.5
                h = u * s
                slope_ref[pl.ds(at, SIDE), :] = jnp.where(self.mask, s + (h - h * s), 0.0)
                write(at, jnp.where(self.mask, h, 0.0))
                return carry

            lax.fori_loop(0, self.height, step, 0, unroll=self.height)


def flips(index, count, stride=1):
    steps, at = [], 1
    while at < count:
        steps.append(at * stride * (1 - 2 * ((index // (at * stride)) % 2)))
        at *= 2
    return [sum((d for b, d in enumerate(steps) if o >> b & 1), index) for o in reversed(range(1, count))]


def combine(buf, counts, group, count):
    n_part = [counts(q) for q in range(group)]
    s_part = [buf[q, 0:count, :] for q in range(group)]
    n_all = sum(n_part[1:], n_part[0])
    s_all = sum(s_part[1:], s_part[0])
    mean = s_all / jnp.maximum(n_all, 1.0)
    spread = jnp.zeros((count, 128), F32)
    for q in range(group):
        gap = s_part[q] / jnp.maximum(n_part[q], 1.0) - mean
        spread = spread + (buf[q, count : 2 * count, :] + n_part[q] * gap * gap)
    return n_all, s_all, mean, spread


def total(buf):
    out = buf[0]
    for q in range(1, buf.shape[0]):
        out = out + buf[q]
    return out


def clear(*refs):
    for ref in refs:
        ref[...] = jnp.zeros(ref.shape, ref.dtype)


def prologue(t):
    r, slots, live, width, feat = t.r, t.slots, t.live, t.width, t.feat
    t.load(
        frames=(r.frames, r.f4.at[pl.ds(0, t.area)]), valid=(r.slot_valid, r.valid), reduce=(r.w_reduce, r.wr)
    )
    t.places()
    t.greet()
    r.f4[t.area :] = jnp.zeros((r.f4.shape[0] - t.area, *r.f4.shape[1:]), BF16)
    clear(r.fp)
    t.loaded(valid=0)
    t.slot_facts()
    t.loaded(frames=0)
    fp, f4 = r.fp, r.f4
    tiles = feat // 128
    group = SIDE // slots
    short = lax.broadcasted_iota(jnp.int32, (SIDE, 128), 0) < width

    def regroup(y, carry):
        for p in range(tiles // group):
            value = f4[pl.ds(y * width, SIDE), p * SIDE : (p + 1) * SIDE, :].astype(F32)
            value = jnp.swapaxes(value, 0, 1)
            for q in range(group):
                for k in range(live):
                    row = value[q * slots + k] * t.keep[k] + value[q * slots + k + 1] * t.moved[k]
                    lanes = slice((p * group + q) * 128, (p * group + q + 1) * 128)
                    fp[pl.ds(block(k, y), SIDE), lanes] = jnp.where(short, row, 0.0).astype(BF16)
        return carry

    lax.fori_loop(0, t.height, regroup, 0)
    t.loaded(reduce=0)
    by_rows(r.pre_a, lambda here: dot(fp[here, :], r.wr[...]))
    t.local_stats(r.near[0], t.near_at(0), r.pre_a)
    r.near[0][t.near_at(0), 4:5, :] = jnp.full((1, 128), t.n_own, F32)


def forward(t):
    r, live, mid, feat, rows, area, height = t.r, t.live, t.mid, t.feat, t.rows, t.area, t.height

    def turn(q):
        lanes = slice(q * feat // 4, (q + 1) * feat // 4)
        r.ft[lanes, :] = r.fp[:, lanes].T

    t.all_here()
    t.near_send(0)
    t.load(
        clip=(r.clip_ids, r.clip), segment=(r.segment_ids, r.segment),
        share=(r.segment_weight, r.share), spatial=(r.w_spatial, r.ws), expand=(r.w_expand, r.we),
        ga=(r.gain_a, r.ga), ba=(r.bias_a, r.ba), gb=(r.gain_b, r.gb), bb=(r.bias_b, r.bb),
        gc=(r.gain_c, r.gc), bc=(r.bias_c, r.bc), loss=(r.loss_weight, r.loss),
    )
    for i in range(3):
        for j in range(3):
            pltpu.make_async_copy(
                r.w_spatial.at[i, j], r.wc.at[i, :, pl.ds(j * mid, mid)], r.load_sem.at[15]
            ).start()
    turn(0)
    t.stats_near(0, mid // 128)
    clear(r.xp, r.hb, r.g3, r.gpc, r.gpa)
    t.loaded(clip=0, segment=0, share=0, ga=0, ba=0, gb=0, bb=0, gc=0, bc=0, loss=0, spatial=0, expand=0)
    key = [t.kept(r.clip, k) for k in range(live)]
    weight = []
    for k in range(live):
        at = t.kept(r.segment, k)
        w0, w1, w2 = (r.share[q] for q in range(3))
        weight.append(
            t.v[k] * (w0 * ((1.0 - at) * (2.0 - at) * 0.5) + w1 * (at * (2.0 - at)) + w2 * (at * (at - 1.0) * 0.5))
        )
    n_all, inv_a = t.stats_wide(0, mid // 128, r.table_a)

    xp, hb = r.xp, r.hb

    def write_a(at, h):
        three(xp, at, pltpu.roll(h, 1, 0), h, pltpu.roll(h, SIDE - 1, 0))

    t.norm_silu(r.pre_a, r.slope_a, r.table_a, r.ga, r.ba, write_a)

    by_rows(
        r.pre_b,
        lambda here: sum(dot(xp[moved_rows(here, i * SIDE), :], r.ws[i].reshape(3 * mid, mid)) for i in range(3)),
    )
    t.local_stats(r.near[1], t.near_at(1), r.pre_b)
    t.near_send(1)
    r.xt[...] = xp[SIDE : SIDE + rows, mid : 2 * mid].T
    t.stats_near(1, mid // 128)
    _, inv_b = t.stats_wide(1, mid // 128, r.table_b)

    def write_b(at, h):
        hb[pl.ds(at, SIDE), :] = h.astype(BF16)

    t.norm_silu(r.pre_b, r.slope_b, r.table_b, r.gb, r.bb, write_b)

    pre_c, slope_c, fp, table_c = r.pre_c, r.slope_c, r.fp, r.table_c
    half = feat // 2
    rounds = (2, 6)
    for h, at in enumerate(rounds):
        lanes = slice(h * half, (h + 1) * half)
        for k in range(live):
            here = slice(k * ROWS, (k + 1) * ROWS)
            pre_c[here, lanes] = dot(hb[here, :], r.we[:, lanes])
        t.local_stats(r.near[at], t.near_at(at), pre_c, h * half, half)
        t.near_send(at)
    r.hbt[...] = hb[...].T
    for at in rounds:
        t.stats_near(at, half // 128)
    turn(1)

    pool, slope_sum, slope_hat = r.pool, r.slope_sum, r.slope_hat
    for c in range(feat // 256):
        if c * 256 % half == 0:
            h = c * 256 // half
            _, inv_half = t.stats_wide(rounds[h], half // 128, table_c, h * half // 128)
            r.inv_c[h * half // 128 : (h + 1) * half // 128, :] = inv_half
        lanes = slice(c * 256, (c + 1) * 256)
        centre, inverse = table_c[0:1, lanes], table_c[1:2, lanes]
        g = r.gc[lanes].reshape(1, 256)
        b = r.bc[lanes].reshape(1, 256)
        for k in range(live):
            def step(y, carry):
                a0, a1, a2 = carry
                at = block(k, y)
                hat = (pre_c[pl.ds(at, SIDE), lanes] - centre) * inverse
                u = hat * g + b + fp[pl.ds(at, SIDE), lanes].astype(F32)
                s = 0.5 * jnp.tanh(0.5 * u) + 0.5
                h = u * s
                slope = s + (h - h * s)
                slope_c[pl.ds(at, SIDE), lanes] = slope
                return a0 + h, a1 + slope, a2 + slope * hat

            zero = jnp.zeros((SIDE, 256), F32)
            a0, a1, a2 = lax.fori_loop(0, height, step, (zero, zero, zero), unroll=height)
            p_row = (t.fold(a0) * (1.0 / area)).astype(BF16).astype(F32)
            to_dense(pool, 0, p_row, 8 * k + 2 * c)
            to_dense(slope_sum, k, t.fold(a1), 2 * c)
            to_dense(slope_hat, k, t.fold(a2), 2 * c)
    for k in range(live):
        pool[0, 24 + k : 25 + k, :] = jnp.full((1, 128), key[k], F32)
        pool[0, 28 + k : 29 + k, :] = jnp.full((1, 128), weight[k], F32)
    for q, device in enumerate(t.clip_peers):
        t.send(pool.at[0], pool.at[q + 1], r.pool_s.at[0], r.pool_r.at[0], device)
    turn(2)
    wait_bytes(pool.at[pl.ds(1, len(t.clip_peers))], r.pool_r.at[0])

    lw = dense_of(r.loss, r.dense)
    grads = []
    for k in range(live):
        my_key = jnp.full((1, 128), key[k], F32)
        my_weight = jnp.full((1, 128), weight[k], F32)
        mean = jnp.zeros((8, 128), F32)
        den = jnp.zeros((1, 128), F32)
        for q in range(len(t.clip_peers) + 1):
            for m in range(live):
                match = jnp.where(pool[q, 24 + m : 25 + m, :] == my_key, pool[q, 28 + m : 29 + m, :], 0.0)
                den = den + match
                mean = mean + match * pool[q, 8 * m : 8 * m + 8, :]
        den = jnp.where(den == 0.0, 1.0, den)
        mean = mean / den
        power = jnp.sum(jnp.sum(mean * mean, axis=0, keepdims=True), axis=1, keepdims=True)
        along = jnp.sum(jnp.sum(mean * lw, axis=0, keepdims=True), axis=1, keepdims=True)
        scale = lax.rsqrt(power * (1.0 / feat) + EPS)
        mean_grad = scale * (lw - (mean * scale) * (scale * along * (1.0 / feat)))
        grads.append((my_weight / den) * mean_grad * (1.0 / area))

    inv_c = r.inv_c[...]
    near3 = r.near[3]
    shift = jnp.zeros((8, 128), F32)
    gain = jnp.zeros((8, 128), F32)
    for k in range(live):
        shift = shift + grads[k] * slope_sum[k]
        gain = gain + grads[k] * slope_hat[k]
    near3[t.near_at(3), 0:8, :] = shift
    near3[t.near_at(3), 8:16, :] = gain
    t.near_send(3)
    coef, dense = r.coef, r.dense
    scale_c = dense_of(r.gc, dense) * inv_c
    for k in range(live):
        dense[...] = grads[k]
        row_form(coef, k, dense, 0, feat // 128)
        dense[...] = grads[k] * scale_c
        row_form(coef, 3 + k, dense, 0, feat // 128)
    t.sums_near(3)
    turn(3)
    both = t.sums_wide(3)
    r.vectors_c[...] = both
    dense[...] = both[0:8] * scale_c / n_all
    row_form(coef, 6, dense, 0, feat // 128)
    dense[...] = both[8:16] * scale_c * inv_c / n_all
    row_form(coef, 7, dense, 0, feat // 128)
    return n_all, inv_a, inv_b


def backward(t, n_all, inv_a, inv_b):
    r, live, mid, feat, rows, height = t.r, t.live, t.mid, t.feat, t.rows, t.height
    slots, width, quad, far, v, wc = t.slots, t.width, t.quad, t.far, t.v, r.wc
    coef, pre_c, slope_c, out = r.coef, r.pre_c, r.slope_c, r.vectors
    me, send = t.me, t.send
    gpc = r.gpc
    for k in range(live):
        for c in range(feat // 256):
            lanes = slice(c * 256, (c + 1) * 256)
            centre = r.table_c[0:1, lanes]
            c0 = coef[3 + k : 4 + k, lanes]
            c1 = coef[6:7, lanes] * v[k]
            c2 = coef[7:8, lanes] * v[k]

            def step(y, carry):
                at = block(k, y)
                grad = slope_c[pl.ds(at, SIDE), lanes] * c0 - (c1 + (pre_c[pl.ds(at, SIDE), lanes] - centre) * c2)
                gpc[pl.ds(at, SIDE), lanes] = grad.astype(BF16)
                return carry

            lax.fori_loop(0, height, step, 0, unroll=height)

    def back_sums(at, table, inv, grad_ref, slope_ref, pre_ref):
        zero = jnp.zeros((SIDE, mid), F32)
        carry = (zero, zero)
        centre = table[0:1, :]
        for k in range(live):
            def step(y, c):
                here = pl.ds(block(k, y), SIDE)
                grad = grad_ref[here, :] * slope_ref[here, :]
                grad_ref[here, :] = grad
                return c[0] + grad, c[1] + grad * (pre_ref[here, :] - centre)

            carry = lax.fori_loop(0, height, step, carry, unroll=height)
        buf = r.near[at]
        to_dense(buf, t.near_at(at), jnp.sum(carry[0], axis=0, keepdims=True), 0)
        to_dense(buf, t.near_at(at), jnp.sum(carry[1], axis=0, keepdims=True) * table[1:2, :], 2)

    def back_apply(at, table, gain_ref, inv, grad_ref, pre_ref, write):
        both = t.sums_wide(at)
        out[8 * at - 32 : 8 * at - 28, :] = both[0:4]
        dense = r.dense
        scale = dense_of(gain_ref, dense) * inv
        dense[0:2, :] = scale
        dense[2:4, :] = both[0:2] * scale / n_all
        dense[4:6, :] = both[2:4] * scale * inv / n_all
        for q in range(3):
            row_form(table, 2 + q, dense, 2 * q, 2)
        centre = table[0:1, :]
        for k in range(live):
            c0, c1, c2 = table[2:3, :], table[3:4, :] * v[k], table[4:5, :] * v[k]

            def step(y, carry):
                at_row = block(k, y)
                here = pl.ds(at_row, SIDE)
                write(at_row, grad_ref[here, :] * c0 - (c1 + (pre_ref[here, :] - centre) * c2))
                return carry

            lax.fori_loop(0, height, step, 0, unroll=height)

    core, bit_x, bit_y, at_z = me % 2, (me // 2) % 2, (me // 4) % 2, (me // 8) % quad
    at_far = me // (8 * quad)
    bit1 = bit_x + core * (bit_y - bit_x)
    bit2 = bit_y + core * (bit_x - bit_y)
    sibling = me + 1 - 2 * core
    peer1 = me + (1 - 2 * bit1) * (2 + 2 * core)
    peer2 = me + (1 - 2 * bit2) * (4 - 2 * core)
    z_at = flips(at_z, quad)
    z_peer = [me + 8 * (q - at_z) for q in z_at]
    far_peer = [me + 8 * quad * ((at_far + o) % far - at_far) for o in range(1, far)]
    chunk_s, chunk_r = r.chunk_s, r.chunk_r
    blocks = iter(ORDER)
    plan = [(0, q, 2) for q in range(2)] + [(1 + q, 0, 1) for q in range(3)] + [(4, q, 4) for q in range(4)]

    def chunk(q):
        name, at, count = plan[q]
        size = r.part[name].shape[0] // count
        part = r.part[name].at[pl.ds(at * size, size)]
        whole = (r.e, r.s0, r.s1, r.s2, r.r)[name].at[pl.ds(at * size, size)]
        half, quarter, eighth, piece = size // 2, size // 4, size // 8, size // (8 * quad)
        m8 = lambda value: pl.multiple_of(value, 8)
        at_h = m8(core * half)
        at_q = m8(at_h + bit1 * quarter)
        at_e = m8(at_q + bit2 * eighth)
        at_p = m8(at_e + at_z * piece)

        def go(step, src, dst, device):
            send(src, dst, chunk_s.at[q, step // 4], chunk_r.at[q, step], device)

        def finish(step, ref):
            wait_bytes(ref, chunk_r.at[q, step])

        rb0, rb1, rb2, rb3 = r.rb0[q], r.rb1[q], r.rb2[q], r.rb3[q]
        go(0, part.at[pl.ds(m8((1 - core) * half), half)], rb0, sibling)
        yield
        finish(0, rb0)
        part[pl.ds(at_h, half), :] = part[pl.ds(at_h, half), :] + rb0[...]
        go(1, part.at[pl.ds(m8(at_h + (1 - bit1) * quarter), quarter)], rb1, peer1)
        yield
        finish(1, rb1)
        part[pl.ds(at_q, quarter), :] = part[pl.ds(at_q, quarter), :] + rb1[...]
        go(2, part.at[pl.ds(m8(at_q + (1 - bit2) * eighth), eighth)], rb2, peer2)
        yield
        finish(2, rb2)
        part[pl.ds(at_e, eighth), :] = part[pl.ds(at_e, eighth), :] + rb2[...]
        for o in range(quad - 1):
            go(3, part.at[pl.ds(m8(at_e + z_at[o] * piece), piece)], rb3.at[pl.ds(o * piece, piece)], z_peer[o])
        yield
        finish(3, rb3)
        own = part[pl.ds(at_p, piece), :]
        for o in range(quad - 1):
            own = own + rb3[o * piece : (o + 1) * piece, :]
        if far > 1:
            rb4 = r.rb4[q]
            rb4[at_far] = own
            for device in far_peer:
                go(8, rb4.at[at_far], rb4.at[at_far], device)
            yield
            finish(8, rb4.at[pl.ds(0, far - 1)])
            own = rb4[0]
            for o in range(1, far):
                own = own + rb4[o]
        whole[pl.ds(at_p, piece), :] = own
        for o in range(quad - 1):
            go(4, whole.at[pl.ds(at_p, piece)], whole.at[pl.ds(at_p, piece)], z_peer[o])
        yield
        finish(4, whole.at[pl.ds(0, (quad - 1) * piece)])
        go(5, whole.at[pl.ds(at_e, eighth)], whole.at[pl.ds(at_e, eighth)], peer2)
        yield
        finish(5, whole.at[pl.ds(0, eighth)])
        go(6, whole.at[pl.ds(at_q, quarter)], whole.at[pl.ds(at_q, quarter)], peer1)
        yield
        finish(6, whole.at[pl.ds(0, quarter)])
        go(7, whole.at[pl.ds(at_h, half)], whole.at[pl.ds(at_h, half)], sibling)
        yield
        finish(7, whole.at[pl.ds(0, half)])
        yield

    chunks = [chunk(q) for q in range(len(plan))]

    def go_on(*which):
        for q in which:
            next(chunks[q])

    def go_on_all():
        go_on(*next(blocks))

    pre_a, slope_a, pre_b, slope_b, hbt, xt = r.pre_a, r.slope_a, r.pre_b, r.slope_b, r.hbt, r.xt
    we, wr, back = r.we, r.wr, r.back
    tiles = feat // 128
    group = SIDE // slots
    keep, moved, mask = t.keep, t.moved, t.mask
    grad_b, grad_a = r.grad_b, r.grad_a
    wait_bytes(wc, r.load_sem.at[15])
    g3 = r.g3

    def write_gb(at, grad):
        grad = jnp.where(mask, grad, 0.0)
        three(g3, at, pltpu.roll(grad, SIDE - 1, 0), grad, pltpu.roll(grad, 1, 0))

    def spatial_part(i):
        go_on_all()
        value = dot(xt[...], g3[(2 - i) * SIDE : (2 - i) * SIDE + rows, :])
        for j in range(3):
            r.part[1 + i][j * mid : (j + 1) * mid, :] = value[:, j * mid : (j + 1) * mid]
        go_on(2 + i)

    go_on_all()
    go_on_all()
    by_rows(grad_b, lambda here: dot(gpc[here, :], we[...], NT))
    back_sums(4, r.table_b, inv_b, grad_b, slope_b, pre_b)
    t.near_send(4)
    for e in range(2):
        go_on_all()
        for q in range(2 * e, 2 * e + 2):
            lanes = slice(q * 256, (q + 1) * 256)
            r.part[0][e * mid : (e + 1) * mid, q % 2 * 256 : (q % 2 + 1) * 256] = dot(hbt[...], gpc[:, lanes])
        go_on(e)
    t.sums_near(4)
    go_on_all()
    back_apply(4, r.table_b, r.gb, inv_b, grad_b, pre_b, write_gb)
    spatial_part(0)
    go_on_all()
    by_rows(
        grad_a, lambda here: sum(dot(g3[moved_rows(here, (2 - i) * SIDE), :], wc[i], NT) for i in range(3))
    )
    back_sums(5, r.table_a, inv_a, grad_a, slope_a, pre_a)
    t.near_send(5)
    spatial_part(1)
    t.sums_near(5)
    spatial_part(2)
    go_on_all()
    gpa = r.gpa

    def write_ga(at, grad):
        gpa[pl.ds(at, SIDE), :] = grad.astype(BF16)

    back_apply(5, r.table_a, r.ga, inv_a, grad_a, pre_a, write_ga)
    for q in range(4):
        go_on_all()
        r.part[4][q * 256 : (q + 1) * 256, :] = dot(r.ft[q * 256 : (q + 1) * 256, :], gpa[...])
        go_on(5 + q)

    go_on_all()
    by_rows(back, lambda here: dot(gpa[here, :], wr[...], NT))
    gf = r.gf

    def blend(y, carry):
        for p in range(tiles // group):
            values = []
            for q in range(group):
                lanes = slice((p * group + q) * 128, (p * group + q + 1) * 128)
                terms = [
                    slope_c[pl.ds(block(k, y), SIDE), lanes] * coef[k : k + 1, lanes]
                    + back[pl.ds(block(k, y), SIDE), lanes]
                    for k in range(live)
                ]
                values.append(terms[0] * keep[0])
                for m in range(1, live):
                    values.append(terms[m] * keep[m] + terms[m - 1] * moved[m - 1])
                values.append(terms[live - 1] * moved[live - 1])
            value = jnp.swapaxes(jnp.stack(values), 0, 1)
            gf[pl.ds(y * width, width), p * SIDE : (p + 1) * SIDE, :] = value[0:width].astype(BF16)
        return carry

    for q in range(height // 2):
        go_on_all()
        for y in range(2):
            blend(2 * q + y, 0)
    t.all_sent(*range(7))
    wait_bytes(r.pool.at[pl.ds(1, len(t.clip_peers))], r.pool_s.at[0])
    go_on_all()
    for each in chunks:
        for _ in each:
            pass

    for q, (name, _, count) in enumerate(plan):
        part = r.part[name]
        piece = part.shape[0] // count // (8 * quad)
        for m, pieces in enumerate((8 * quad - 1, 8 * quad - 1, far - 1)):
            if pieces:
                wait_bytes(part.at[pl.ds(0, pieces * piece)], chunk_s.at[q, m])


def store(gf, vectors_c, vectors, expand, s0, s1, s2, reduce, frames_out, reduce_out, spatial_out, expand_out, *rest):
    ga, ba, gb, bb, gc, bc, *scratch, sem = rest
    vectors_of = (
        (bc, vectors_c, 0), (gc, vectors_c, 8), (bb, vectors, 0), (gb, vectors, 2), (ba, vectors, 8), (ga, vectors, 10)
    )
    pltpu.make_async_copy(gf, frames_out, sem.at[0]).start()
    pltpu.make_async_copy(reduce, reduce_out, sem.at[1]).start()
    depth, width = expand_out.shape
    for q in range(2):
        pltpu.make_async_copy(
            expand.at[pl.ds(q * depth, depth)], expand_out.at[:, pl.ds(q * width // 2, width // 2)], sem.at[2]
        ).start()
    for i, part in enumerate((s0, s1, s2)):
        for j in range(3):
            pltpu.make_async_copy(part.at[pl.ds(j * depth, depth)], spatial_out.at[i, j], sem.at[3 + i]).start()
    for number, (ref, source, first) in enumerate(vectors_of):
        for q in range(ref.shape[0] // 128):
            scratch[number][q * 128 : (q + 1) * 128] = source[first + q : first + q + 1, :].reshape(128)
        pltpu.make_async_copy(scratch[number], ref, sem.at[6 + number]).start()
    wait_bytes(gf, sem.at[0])
    wait_bytes(reduce, sem.at[1])
    wait_bytes(expand, sem.at[2])
    for i, part in enumerate((s0, s1, s2)):
        wait_bytes(part, sem.at[3 + i])
    for number in range(6):
        wait_bytes(scratch[number], sem.at[6 + number])


def solution(mesh):
    n = mesh.shape["clip"]

    def shards(*args):
        slots, height, width, feat = args[0].shape
        mid = args[1].shape[1]
        rows = (slots - 1) * ROWS
        outer = n // 8
        quad = min(4, outer)
        far = outer // quad
        cfg = (n, slots, height, width, feat, mid)
        flat_shape = (height * width, slots * feat // 128, 128)
        hbm = pl.BlockSpec(memory_space=pltpu.HBM)
        vmem = pl.BlockSpec(memory_space=pltpu.VMEM)
        dma = pltpu.SemaphoreType.DMA
        depths = list(enumerate((5, 4, 8, 16, 4, 4, 8)))
        sizes = [(2 * mid, feat // 2)] + [(3 * mid, mid)] * 3 + [(feat, mid)]

        tiled = args[0].transpose(1, 2, 0, 3).reshape(height, width, slots, feat // 128, 128)
        tiled = tiled.transpose(0, 1, 3, 2, 4).reshape(flat_shape)
        given = [pltpu.with_memory_space_constraint(part, pltpu.HBM) for part in (tiled, *args[1:])]

        vm = pltpu.VMEM
        narrow, broad, square = vm((mid,), F32), vm((feat,), F32), vm((rows, mid), F32)
        ints = pltpu.SMEM((slots,), jnp.int32)
        plan = [(mid, feat // 2)] * 2 + [(3 * mid, mid)] * 3 + [(feat // 4, mid)] * 4
        outs = dict(
            gf=vm(flat_shape, BF16), vectors_c=vm((16, 128), F32), vectors=vm((16, 128), F32),
            **{name: vm(size, F32) for name, size in zip(dict(e=0, s0=0, s1=0, s2=0, r=0), sizes)},
        )
        scratch = dict(
            f4=vm((flat_shape[0] + SIDE - width, *flat_shape[1:]), BF16),
            fp=vm((rows, feat), BF16), ft=vm((feat, rows), BF16),
            wr=vm((feat, mid), BF16), ws=vm((3, 3, mid, mid), BF16), wc=vm((3, mid, 3 * mid), BF16), we=vm((mid, feat), BF16),
            valid=ints, clip=ints, segment=ints, share=pltpu.SMEM(args[13].shape, F32),
            ga=narrow, ba=narrow, gb=narrow, bb=narrow, gc=broad, bc=broad, loss=broad,
            xp=vm((rows + 2 * SIDE, 3 * mid), BF16), xt=vm((mid, rows), BF16),
            hb=vm((rows, mid), BF16), hbt=vm((mid, rows), BF16),
            pre_a=square, slope_a=square, pre_b=square, slope_b=square, grad_a=square, grad_b=square,
            pre_c=vm((rows, feat), F32), slope_c=vm((rows, feat), F32), back=vm((rows, feat), F32),
            gpc=vm((rows, feat), BF16), g3=vm((rows + 2 * SIDE, 3 * mid), BF16), gpa=vm((rows, mid), BF16),
            table_a=vm((8, mid), F32), table_b=vm((8, mid), F32),
            table_c=vm((8, feat), F32), coef=vm((8, feat), F32), dense=vm((8, 128), F32), inv_c=vm((8, 128), F32),
            pool=vm((6, 32, 128), F32), slope_sum=vm((3, 8, 128), F32), slope_hat=vm((3, 8, 128), F32),
            near=[vm((n if n <= 32 and at not in (2, 3, 6) else 8, deep, 128), F32) for at, deep in depths],
            wide=[vm((outer, deep, 128), F32) for at, deep in depths],
            plane=vm((outer, 8, 128), F32),
            part=[vm(size, F32) for size in sizes],
            rb0=[vm((size // 2, lanes), F32) for size, lanes in plan],
            rb1=[vm((size // 4, lanes), F32) for size, lanes in plan],
            rb2=[vm((size // 8, lanes), F32) for size, lanes in plan],
            rb3=[vm(((quad - 1) * size // (8 * quad), lanes), F32) for size, lanes in plan],
            rb4=[vm((far, size // (8 * quad), lanes), F32) for size, lanes in plan if far > 1],
            load_sem=dma((16,)), near_s=dma((7,)), near_r=dma((7,)), wide_s=dma((7,)), wide_r=dma((7,)),
            pool_s=dma((1,)), pool_r=dma((1,)), chunk_s=dma((9, 3)), chunk_r=dma((9, 9)),
        )
        names = (*arg_names(), *outs, *scratch)

        def kernel(*refs):
            t = Step(cfg, SimpleNamespace(**dict(zip(names, refs, strict=True))))
            prologue(t)
            backward(t, *forward(t))

        results = pl.pallas_call(
            kernel,
            out_shape=list(outs.values()),
            in_specs=[hbm] * len(given),
            out_specs=[vmem] * len(outs),
            scratch_shapes=list(scratch.values()),
            compiler_params=pltpu.CompilerParams(
                collective_id=0, has_side_effects=True, vmem_limit_bytes=50 * 1024 * 1024
            ),
        )(*given)
        vector = jax.ShapeDtypeStruct((mid,), F32)
        wide_vector = jax.ShapeDtypeStruct((feat,), F32)
        flat_grad, *rest = pl.pallas_call(
            store,
            out_shape=[
                jax.ShapeDtypeStruct(flat_shape, BF16),
                jax.ShapeDtypeStruct((feat, mid), F32),
                jax.ShapeDtypeStruct((3, 3, mid, mid), F32),
                jax.ShapeDtypeStruct((mid, feat), F32),
                vector, vector, vector, vector, wide_vector, wide_vector,
            ],
            in_specs=[vmem] * 8,
            out_specs=[hbm] * 10,
            scratch_shapes=[*(vm((c,), F32) for c in (feat, feat, mid, mid, mid, mid)), dma((12,))],
            compiler_params=pltpu.CompilerParams(vmem_limit_bytes=8 * 1024 * 1024),
        )(*(pltpu.with_memory_space_constraint(part, pltpu.VMEM) for part in results))
        grad_frames = flat_grad.reshape(height, width, feat // 128, slots, 128).transpose(0, 1, 3, 2, 4)
        return grad_frames.reshape(height, width, slots, feat).transpose(2, 0, 1, 3), *rest

    split = P("clip")
    in_specs = (split,) + (P(),) * 9 + (split,) * 3 + (P(), P())
    out_specs = (split,) + (P(),) * 9
    return jax.shard_map(shards, mesh=mesh, in_specs=in_specs, out_specs=out_specs, check_vma=False)


def arg_names():
    return dict(
        frames=0, w_reduce=0, w_spatial=0, w_expand=0, gain_a=0, bias_a=0, gain_b=0, bias_b=0, gain_c=0, bias_c=0,
        clip_ids=0, segment_ids=0, slot_valid=0, segment_weight=0, loss_weight=0,
    )
```

```python
import functools
from types import SimpleNamespace

import jax
import jax.numpy as jnp
from jax import lax
from jax.experimental import pallas as pl
from jax.experimental.pallas import tpu as pltpu
from jax.sharding import PartitionSpec as P

MESH = pl.DeviceIdType.MESH
EPS = 1e-05
F32 = jnp.float32
BF16 = jnp.bfloat16
SIDE = 16
ROWS = SIDE * SIDE
NN = (((1,), (0,)), ((), ()))
NT = (((1,), (1,)), ((), ()))

ORDER = (
    (),
    (),
    (),
    (),
    (),
    (),
    (0, 1,),
    (2, 0,),
    (1,),
    (2, 0, 1, 3,),
    (2, 4,),
    (),
    (),
    (0,),
    (1, 3, 5, 2, 4,),
    (6, 3, 8,),
    (1, 0, 5, 7, 4, 8, 1, 3, 6, 7, 8, 2, 0,),
    (4, 7, 3,),
    (6, 2, 8, 1, 5, 0, 4, 7, 3, 6, 8, 5, 7, 1, 6, 4,),
    (5, 6, 0, 3,),
    (7,),
    (8, 2, 4, 5, 7, 8, 6, 3, 5,),
    (7, 8, 6, 5, 4, 2,),
)


def dot(a, b, dims=NN):
    return lax.dot_general(a, b, dims, preferred_element_type=F32)


def wait_bytes(ref, sem):
    pltpu.make_async_copy(ref, ref, sem).wait()


def by_rows(ref, value):
    for k in range(ref.shape[0] // 256):
        ref[k * 256 : (k + 1) * 256, :] = value(slice(k * 256, (k + 1) * 256))


def moved_rows(here, at):
    return slice(here.start + at, here.stop + at)


def block(k, y):
    return pl.multiple_of(k * ROWS + y * SIDE, SIDE)


def to_dense(ref, at, value, first):
    for q in range(value.shape[1] // 128):
        ref[at, pl.ds(first + q, 1), :] = value[:, q * 128 : (q + 1) * 128]


def row_form(ref, row, source, first, count, lane=0):
    for q in range(count):
        ref[row : row + 1, (lane + q) * 128 : (lane + q + 1) * 128] = source[first + q : first + q + 1, :]


def three(ref, at, left, middle, right):
    here, wide = pl.ds(at + SIDE, SIDE), middle.shape[1]
    ref[here, 0:wide] = left.astype(BF16)
    ref[here, wide : 2 * wide] = middle.astype(BF16)
    ref[here, 2 * wide : 3 * wide] = right.astype(BF16)


def dense_of(ref1, scratch):
    count = ref1.shape[0] // 128
    for q in range(count):
        scratch[q : q + 1, :] = ref1[q * 128 : (q + 1) * 128].reshape(1, 128)
    return scratch[0:count, :]


class Step:
    def __init__(self, cfg, r):
        self.r, self.sizes = r, cfg
        self.n, self.slots, self.height, self.width, self.feat, self.mid = cfg
        self.live = self.slots - 1
        self.rows = self.live * ROWS
        self.area = self.height * self.width
        self.inner = 8
        self.outer = self.n // 8
        self.quad = min(4, self.outer)
        self.far = self.outer // self.quad
        self.loads = {}
        self.mask = lax.broadcasted_iota(jnp.int32, (SIDE, 256), 0) < self.width

    def load(self, **pairs):
        for name, (src, dst) in pairs.items():
            copy = pltpu.make_async_copy(src, dst, self.r.load_sem.at[len(self.loads)])
            copy.start()
            self.loads[name] = copy

    def loaded(self, **names):
        for name in names:
            self.loads[name].wait()

    def fold(self, value):
        return jnp.sum(jnp.where(self.mask, value, 0.0), axis=0, keepdims=True)

    def slot_facts(self):
        r, live = self.r, self.live
        alive, later = 1, []
        for k in range(live):
            alive = alive * r.valid[k]
            later.append(1 - alive)
        self.keep = [(1 - q).astype(F32) for q in later]
        self.moved = [q.astype(F32) for q in later]
        self.later = later
        self.v = [self.kept(r.valid, k) for k in range(live)]
        self.n_own = (self.v[0] + self.v[1] + self.v[2]) * float(self.area)

    def kept(self, values, k):
        return (values[k] + self.later[k] * (values[k + 1] - values[k])).astype(F32)

    def places(self):
        n = self.n
        self.me = me = lax.axis_index("clip")
        self.low, self.high = low, high = me % self.inner, me // self.inner
        self.direct = n <= 32
        self.peers = flips(me, n)
        self.low_peers = flips(me, self.inner)
        self.high_peers = flips(me, self.outer, self.inner)
        self.clip_peers = [(me + o) % n for o in (n // 2 - 1, n // 2 + 1, n // 2, n - 1, 1)]

    def greet(self):
        self.greeted = self.peers if self.direct else self.low_peers + self.high_peers + self.clip_peers
        self.barrier = pltpu.get_barrier_semaphore()
        for device in self.greeted:
            pl.semaphore_signal(self.barrier, inc=1, device_id=(device,), device_id_type=MESH)

    def all_here(self):
        pl.semaphore_wait(self.barrier, len(self.greeted))

    def send(self, src, dst, ssem, rsem, device):
        pltpu.make_async_remote_copy(
            src_ref=src, dst_ref=dst, send_sem=ssem, recv_sem=rsem, device_id=(device,), device_id_type=MESH
        ).start()

    def one_stage(self, at):
        return self.direct and at not in (2, 3, 6)

    def near_at(self, at):
        return self.me if self.one_stage(at) else self.low

    def near_send(self, at):
        buf, mine = self.r.near[at], self.near_at(at)
        for device in self.peers if self.one_stage(at) else self.low_peers:
            self.send(buf.at[mine], buf.at[mine], self.r.near_s.at[at], self.r.near_r.at[at], device)

    def near_wait(self, at, sems):
        buf = self.r.near[at]
        wait_bytes(buf.at[pl.ds(0, buf.shape[0] - 1)], sems.at[at])

    def wide_send(self, at):
        buf = self.r.wide[at]
        for device in self.high_peers:
            self.send(buf.at[self.high], buf.at[self.high], self.r.wide_s.at[at], self.r.wide_r.at[at], device)

    def wide_wait(self, at, sems):
        wait_bytes(self.r.wide[at].at[pl.ds(0, self.outer - 1)], sems.at[at])

    def all_sent(self, *rounds):
        for at in rounds:
            self.near_wait(at, self.r.near_s)
            if not self.one_stage(at):
                self.wide_wait(at, self.r.wide_s)

    def near_count(self, q):
        return self.r.near[0][(self.me - self.low + q) if self.direct else q, 4:5, :]

    def wide_count(self, q):
        return self.r.plane[q, 0:1, :] if self.direct else self.r.wide[0][q, 4:5, :]

    def stats_near(self, at, count):
        if self.one_stage(at):
            return
        self.near_wait(at, self.r.near_r)
        n_all, s_all, _, spread = combine(self.r.near[at], self.near_count, self.inner, count)
        buf = self.r.wide[at]
        buf[self.high, 0:count, :] = s_all
        buf[self.high, count : 2 * count, :] = spread
        if at == 0:
            buf[self.high, 4:5, :] = n_all
        self.wide_send(at)

    def stats_wide(self, at, count, table, first=0):
        r = self.r
        if self.one_stage(at):
            self.near_wait(at, r.near_r)
            counts = r.near[0]
            n_all, _, mean, spread = combine(r.near[at], lambda q: counts[q, 4:5, :], self.n, count)
        else:
            self.wide_wait(at, r.wide_r)
            n_all, _, mean, spread = combine(r.wide[at], self.wide_count, self.outer, count)
        if at == 0 and self.direct:
            counts = r.near[0]
            for q in range(self.outer):
                r.plane[q, 0:1, :] = sum(counts[q * self.inner + m, 4:5, :] for m in range(self.inner))
        inverse = lax.rsqrt(spread / n_all + EPS)
        r.dense[0:count, :] = mean
        row_form(table, 0, r.dense, 0, count, first)
        r.dense[0:count, :] = inverse
        row_form(table, 1, r.dense, 0, count, first)
        return n_all, inverse

    def sums_near(self, at):
        if not self.one_stage(at):
            self.near_wait(at, self.r.near_r)
            self.r.wide[at][self.high] = total(self.r.near[at])
            self.wide_send(at)

    def sums_wide(self, at):
        if self.one_stage(at):
            self.near_wait(at, self.r.near_r)
            return total(self.r.near[at])
        self.wide_wait(at, self.r.wide_r)
        return total(self.r.wide[at])

    def local_stats(self, buf, at, ref, first=0, channels=None):
        channels = channels or ref.shape[1]
        count = channels // 128
        for c in range(channels // 256):
            lanes = slice(first + c * 256, first + (c + 1) * 256)

            def gather(term):
                acc = jnp.zeros((SIDE, 256), F32)
                for k in range(self.live):
                    part = lax.fori_loop(
                        0, self.height, lambda y, a: a + term(ref[pl.ds(block(k, y), SIDE), lanes]),
                        jnp.zeros((SIDE, 256), F32), unroll=self.height,
                    )
                    acc = acc + part * self.v[k]
                return self.fold(acc)

            s_own = gather(lambda x: x)
            mean = s_own / jnp.maximum(self.n_own, 1.0)
            to_dense(buf, at, s_own, 2 * c)
            to_dense(buf, at, gather(lambda x: (x - mean) * (x - mean)), count + 2 * c)

    def norm_silu(self, ref, slope_ref, table, gain, bias, write):
        centre, scale = table[0:1, :], table[1:2, :] * gain[...].reshape(1, self.mid)
        b = bias[...].reshape(1, self.mid)
        for k in range(self.live):
            def step(y, carry):
                at = block(k, y)
                u = (ref[pl.ds(at, SIDE), :] - centre) * scale + b
                s = 0.5 * jnp.tanh(0.5 * u) + 0.5
                h = u * s
                slope_ref[pl.ds(at, SIDE), :] = jnp.where(self.mask, s + (h - h * s), 0.0)
                write(at, jnp.where(self.mask, h, 0.0))
                return carry

            lax.fori_loop(0, self.height, step, 0, unroll=self.height)


def flips(index, count, stride=1):
    steps, at = [], 1
    while at < count:
        steps.append(at * stride * (1 - 2 * ((index // (at * stride)) % 2)))
        at *= 2
    return [sum((d for b, d in enumerate(steps) if o >> b & 1), index) for o in reversed(range(1, count))]


def combine(buf, counts, group, count):
    n_part = [counts(q) for q in range(group)]
    s_part = [buf[q, 0:count, :] for q in range(group)]
    n_all, s_all = tree(n_part), tree(s_part)
    mean = s_all / jnp.maximum(n_all, 1.0)
    spread = []
    for q in range(group):
        gap = s_part[q] / jnp.maximum(n_part[q], 1.0) - mean
        spread.append(buf[q, count : 2 * count, :] + n_part[q] * gap * gap)
    return n_all, s_all, mean, tree(spread)


def tree(values):
    while len(values) > 1:
        values = [sum(values[q + 1 : q + 2], values[q]) for q in range(0, len(values), 2)]
    return values[0]


def total(buf):
    return tree([buf[q] for q in range(buf.shape[0])])


def clear(*refs):
    for ref in refs:
        ref[...] = jnp.zeros(ref.shape, ref.dtype)


def prologue(t):
    r, slots, live, width, feat = t.r, t.slots, t.live, t.width, t.feat
    t.load(
        frames=(r.frames, r.f4.at[pl.ds(0, t.area)]), valid=(r.slot_valid, r.valid), reduce=(r.w_reduce, r.wr)
    )
    t.places()
    t.greet()
    r.f4[t.area :] = jnp.zeros((r.f4.shape[0] - t.area, *r.f4.shape[1:]), BF16)
    clear(r.fp)
    t.loaded(valid=0)
    t.slot_facts()
    t.loaded(frames=0)
    fp, f4 = r.fp, r.f4
    tiles = feat // 128
    group = SIDE // slots
    short = lax.broadcasted_iota(jnp.int32, (SIDE, 128), 0) < width

    def regroup(y, carry):
        for p in range(tiles // group):
            value = f4[pl.ds(y * width, SIDE), p * SIDE : (p + 1) * SIDE, :].astype(F32)
            value = jnp.swapaxes(value, 0, 1)
            for q in range(group):
                for k in range(live):
                    row = value[q * slots + k] * t.keep[k] + value[q * slots + k + 1] * t.moved[k]
                    lanes = slice((p * group + q) * 128, (p * group + q + 1) * 128)
                    fp[pl.ds(block(k, y), SIDE), lanes] = jnp.where(short, row, 0.0).astype(BF16)
        return carry

    lax.fori_loop(0, t.height, regroup, 0)
    t.loaded(reduce=0)
    by_rows(r.pre_a, lambda here: dot(fp[here, :], r.wr[...]))
    t.local_stats(r.near[0], t.near_at(0), r.pre_a)
    r.near[0][t.near_at(0), 4:5, :] = jnp.full((1, 128), t.n_own, F32)


def forward(t):
    r, live, mid, feat, rows, area, height = t.r, t.live, t.mid, t.feat, t.rows, t.area, t.height

    def turn(q):
        lanes = slice(q * feat // 4, (q + 1) * feat // 4)
        r.ft[lanes, :] = r.fp[:, lanes].T

    t.all_here()
    t.near_send(0)
    t.load(
        clip=(r.clip_ids, r.clip), segment=(r.segment_ids, r.segment),
        share=(r.segment_weight, r.share), spatial=(r.w_spatial, r.ws), expand=(r.w_expand, r.we),
        ga=(r.gain_a, r.ga), ba=(r.bias_a, r.ba), gb=(r.gain_b, r.gb), bb=(r.bias_b, r.bb),
        gc=(r.gain_c, r.gc), bc=(r.bias_c, r.bc), loss=(r.loss_weight, r.loss),
    )
    for i in range(3):
        for j in range(3):
            pltpu.make_async_copy(
                r.w_spatial.at[i, j], r.wc.at[i, :, pl.ds(j * mid, mid)], r.load_sem.at[15]
            ).start()
    turn(0)
    t.stats_near(0, mid // 128)
    clear(r.xp, r.hb, r.g3, r.gpc, r.gpa)
    t.loaded(clip=0, segment=0, share=0, ga=0, ba=0, gb=0, bb=0, gc=0, bc=0, loss=0, spatial=0, expand=0)
    key = [t.kept(r.clip, k) for k in range(live)]
    weight = []
    for k in range(live):
        at = t.kept(r.segment, k)
        w0, w1, w2 = (r.share[q] for q in range(3))
        weight.append(
            t.v[k] * (w0 * ((1.0 - at) * (2.0 - at) * 0.5) + w1 * (at * (2.0 - at)) + w2 * (at * (at - 1.0) * 0.5))
        )
    n_all, inv_a = t.stats_wide(0, mid // 128, r.table_a)

    xp, hb = r.xp, r.hb

    def write_a(at, h):
        three(xp, at, pltpu.roll(h, 1, 0), h, pltpu.roll(h, SIDE - 1, 0))

    t.norm_silu(r.pre_a, r.slope_a, r.table_a, r.ga, r.ba, write_a)

    by_rows(
        r.pre_b,
        lambda here: sum(dot(xp[moved_rows(here, i * SIDE), :], r.ws[i].reshape(3 * mid, mid)) for i in range(3)),
    )
    t.local_stats(r.near[1], t.near_at(1), r.pre_b)
    t.near_send(1)
    r.xt[...] = xp[SIDE : SIDE + rows, mid : 2 * mid].T
    t.stats_near(1, mid // 128)
    _, inv_b = t.stats_wide(1, mid // 128, r.table_b)

    def write_b(at, h):
        hb[pl.ds(at, SIDE), :] = h.astype(BF16)

    t.norm_silu(r.pre_b, r.slope_b, r.table_b, r.gb, r.bb, write_b)

    pre_c, slope_c, fp, table_c = r.pre_c, r.slope_c, r.fp, r.table_c
    half = feat // 2
    rounds = (2, 6)
    for h, at in enumerate(rounds):
        lanes = slice(h * half, (h + 1) * half)
        for k in range(live):
            here = slice(k * ROWS, (k + 1) * ROWS)
            pre_c[here, lanes] = dot(hb[here, :], r.we[:, lanes])
        t.local_stats(r.near[at], t.near_at(at), pre_c, h * half, half)
        t.near_send(at)
    r.hbt[...] = hb[...].T
    for at in rounds:
        t.stats_near(at, half // 128)
    turn(1)

    pool, slope_sum, slope_hat = r.pool, r.slope_sum, r.slope_hat
    for c in range(feat // 256):
        if c * 256 % half == 0:
            h = c * 256 // half
            _, inv_half = t.stats_wide(rounds[h], half // 128, table_c, h * half // 128)
            r.inv_c[h * half // 128 : (h + 1) * half // 128, :] = inv_half
        lanes = slice(c * 256, (c + 1) * 256)
        centre, inverse = table_c[0:1, lanes], table_c[1:2, lanes]
        g = r.gc[lanes].reshape(1, 256)
        b = r.bc[lanes].reshape(1, 256)
        for k in range(live):
            def step(y, carry):
                a0, a1, a2 = carry
                at = block(k, y)
                hat = (pre_c[pl.ds(at, SIDE), lanes] - centre) * inverse
                u = hat * g + b + fp[pl.ds(at, SIDE), lanes].astype(F32)
                s = 0.5 * jnp.tanh(0.5 * u) + 0.5
                h = u * s
                slope = s + (h - h * s)
                slope_c[pl.ds(at, SIDE), lanes] = slope
                return a0 + h, a1 + slope, a2 + slope * hat

            zero = jnp.zeros((SIDE, 256), F32)
            a0, a1, a2 = lax.fori_loop(0, height, step, (zero, zero, zero), unroll=height)
            p_row = (t.fold(a0) * (1.0 / area)).astype(BF16).astype(F32)
            to_dense(pool[h], 0, p_row, 4 * k + 2 * (c - 2 * h))
            to_dense(slope_sum, k, t.fold(a1), 2 * c)
            to_dense(slope_hat, k, t.fold(a2), 2 * c)
        if (c + 1) * 256 % half == 0:
            for k in range(live):
                pool[h][0, 12 + k : 13 + k, :] = jnp.full((1, 128), (key, weight)[h][k], F32)
            for q, device in enumerate(t.clip_peers):
                t.send(pool[h].at[0], pool[h].at[q + 1], r.pool_s.at[h], r.pool_r.at[h], device)
    turn(2)
    for h in range(2):
        wait_bytes(pool[h].at[pl.ds(1, len(t.clip_peers))], r.pool_r.at[h])

    lw = dense_of(r.loss, r.dense)
    grads = []
    for k in range(live):
        my_key = jnp.full((1, 128), key[k], F32)
        my_weight = jnp.full((1, 128), weight[k], F32)
        parts = [jnp.zeros((4, 128), F32)] * 2
        den = jnp.zeros((1, 128), F32)
        for q in range(len(t.clip_peers) + 1):
            for m in range(live):
                match = jnp.where(pool[0][q, 12 + m : 13 + m, :] == my_key, pool[1][q, 12 + m : 13 + m, :], 0.0)
                den = den + match
                parts = [parts[h] + match * pool[h][q, 4 * m : 4 * m + 4, :] for h in range(2)]
        den = jnp.where(den == 0.0, 1.0, den)
        for h in range(2):
            r.clip_mean[k, 4 * h : 4 * h + 4, :] = parts[h] / den
        mean = r.clip_mean[k]
        power = jnp.sum(jnp.sum(mean * mean, axis=0, keepdims=True), axis=1, keepdims=True)
        along = jnp.sum(jnp.sum(mean * lw, axis=0, keepdims=True), axis=1, keepdims=True)
        scale = lax.rsqrt(power * (1.0 / feat) + EPS)
        mean_grad = scale * (lw - (mean * scale) * (scale * along * (1.0 / feat)))
        grads.append((my_weight / den) * mean_grad * (1.0 / area))

    inv_c = r.inv_c[...]
    near3 = r.near[3]
    shift = jnp.zeros((8, 128), F32)
    gain = jnp.zeros((8, 128), F32)
    for k in range(live):
        shift = shift + grads[k] * slope_sum[k]
        gain = gain + grads[k] * slope_hat[k]
    near3[t.near_at(3), 0:8, :] = shift
    near3[t.near_at(3), 8:16, :] = gain
    t.near_send(3)
    coef, dense = r.coef, r.dense
    scale_c = dense_of(r.gc, dense) * inv_c
    for k in range(live):
        dense[...] = grads[k]
        row_form(coef, k, dense, 0, feat // 128)
        dense[...] = grads[k] * scale_c
        row_form(coef, 3 + k, dense, 0, feat // 128)
    t.sums_near(3)
    turn(3)
    both = t.sums_wide(3)
    r.vectors_c[...] = both
    dense[...] = both[0:8] * scale_c / n_all
    row_form(coef, 6, dense, 0, feat // 128)
    dense[...] = both[8:16] * scale_c * inv_c / n_all
    row_form(coef, 7, dense, 0, feat // 128)
    return n_all, inv_a, inv_b


def backward(t, n_all, inv_a, inv_b):
    r, live, mid, feat, rows, height = t.r, t.live, t.mid, t.feat, t.rows, t.height
    slots, width, quad, far, v, wc = t.slots, t.width, t.quad, t.far, t.v, r.wc
    coef, pre_c, slope_c, out = r.coef, r.pre_c, r.slope_c, r.vectors
    me, send = t.me, t.send
    gpc = r.gpc
    for k in range(live):
        for c in range(feat // 256):
            lanes = slice(c * 256, (c + 1) * 256)
            centre = r.table_c[0:1, lanes]
            c0 = coef[3 + k : 4 + k, lanes]
            c1 = coef[6:7, lanes] * v[k]
            c2 = coef[7:8, lanes] * v[k]

            def step(y, carry):
                at = block(k, y)
                grad = slope_c[pl.ds(at, SIDE), lanes] * c0 - (c1 + (pre_c[pl.ds(at, SIDE), lanes] - centre) * c2)
                gpc[pl.ds(at, SIDE), lanes] = grad.astype(BF16)
                return carry

            lax.fori_loop(0, height, step, 0, unroll=height)

    def back_sums(at, table, inv, grad_ref, slope_ref, pre_ref):
        zero = jnp.zeros((SIDE, mid), F32)
        carry = (zero, zero)
        centre = table[0:1, :]
        for k in range(live):
            def step(y, c):
                here = pl.ds(block(k, y), SIDE)
                grad = grad_ref[here, :] * slope_ref[here, :]
                grad_ref[here, :] = grad
                return c[0] + grad, c[1] + grad * (pre_ref[here, :] - centre)

            carry = lax.fori_loop(0, height, step, carry, unroll=height)
        buf = r.near[at]
        to_dense(buf, t.near_at(at), jnp.sum(carry[0], axis=0, keepdims=True), 0)
        to_dense(buf, t.near_at(at), jnp.sum(carry[1], axis=0, keepdims=True) * table[1:2, :], 2)

    def back_apply(at, table, gain_ref, inv, grad_ref, pre_ref, write):
        both = t.sums_wide(at)
        out[8 * at - 32 : 8 * at - 28, :] = both[0:4]
        dense = r.dense
        scale = dense_of(gain_ref, dense) * inv
        dense[0:2, :] = scale
        dense[2:4, :] = both[0:2] * scale / n_all
        dense[4:6, :] = both[2:4] * scale * inv / n_all
        for q in range(3):
            row_form(table, 2 + q, dense, 2 * q, 2)
        centre = table[0:1, :]
        for k in range(live):
            c0, c1, c2 = table[2:3, :], table[3:4, :] * v[k], table[4:5, :] * v[k]

            def step(y, carry):
                at_row = block(k, y)
                here = pl.ds(at_row, SIDE)
                write(at_row, grad_ref[here, :] * c0 - (c1 + (pre_ref[here, :] - centre) * c2))
                return carry

            lax.fori_loop(0, height, step, 0, unroll=height)

    core, bit_x, bit_y, at_z = me % 2, (me // 2) % 2, (me // 4) % 2, (me // 8) % quad
    at_far = me // (8 * quad)
    bit1 = bit_x + core * (bit_y - bit_x)
    bit2 = bit_y + core * (bit_x - bit_y)
    sibling = me + 1 - 2 * core
    peer1 = me + (1 - 2 * bit1) * (2 + 2 * core)
    peer2 = me + (1 - 2 * bit2) * (4 - 2 * core)
    z_at = flips(at_z, quad)
    z_peer = [me + 8 * (q - at_z) for q in z_at]
    far_peer = [me + 8 * quad * ((at_far + o) % far - at_far) for o in range(1, far)]
    chunk_s, chunk_r = r.chunk_s, r.chunk_r
    blocks = iter(ORDER)
    plan = [(0, q, 2) for q in range(2)] + [(1 + q, 0, 1) for q in range(3)] + [(4, q, 4) for q in range(4)]

    def chunk(q):
        name, at, count = plan[q]
        size = r.part[name].shape[0] // count
        part = r.part[name].at[pl.ds(at * size, size)]
        whole = (r.e, r.s0, r.s1, r.s2, r.r)[name].at[pl.ds(at * size, size)]
        half, quarter, eighth, piece = size // 2, size // 4, size // 8, size // (8 * quad)
        m8 = lambda value: pl.multiple_of(value, 8)
        at_h = m8(core * half)
        at_q = m8(at_h + bit1 * quarter)
        at_e = m8(at_q + bit2 * eighth)
        at_p = m8(at_e + at_z * piece)

        def go(step, src, dst, device):
            send(src, dst, chunk_s.at[q, step // 4], chunk_r.at[q, step], device)

        def finish(step, ref):
            wait_bytes(ref, chunk_r.at[q, step])

        rb0, rb1, rb2, rb3 = r.rb0[q], r.rb1[q], r.rb2[q], r.rb3[q]
        go(0, part.at[pl.ds(m8((1 - core) * half), half)], rb0, sibling)
        yield
        finish(0, rb0)
        part[pl.ds(at_h, half), :] = part[pl.ds(at_h, half), :] + rb0[...]
        go(1, part.at[pl.ds(m8(at_h + (1 - bit1) * quarter), quarter)], rb1, peer1)
        yield
        finish(1, rb1)
        part[pl.ds(at_q, quarter), :] = part[pl.ds(at_q, quarter), :] + rb1[...]
        go(2, part.at[pl.ds(m8(at_q + (1 - bit2) * eighth), eighth)], rb2, peer2)
        yield
        finish(2, rb2)
        part[pl.ds(at_e, eighth), :] = part[pl.ds(at_e, eighth), :] + rb2[...]
        for o in range(quad - 1):
            go(3, part.at[pl.ds(m8(at_e + z_at[o] * piece), piece)], rb3.at[pl.ds(o * piece, piece)], z_peer[o])
        yield
        finish(3, rb3)
        own = part[pl.ds(at_p, piece), :]
        for o in range(quad - 1):
            own = own + rb3[o * piece : (o + 1) * piece, :]
        if far > 1:
            rb4 = r.rb4[q]
            rb4[at_far] = own
            for device in far_peer:
                go(8, rb4.at[at_far], rb4.at[at_far], device)
            yield
            finish(8, rb4.at[pl.ds(0, far - 1)])
            own = rb4[0]
            for o in range(1, far):
                own = own + rb4[o]
        whole[pl.ds(at_p, piece), :] = own
        for o in range(quad - 1):
            go(4, whole.at[pl.ds(at_p, piece)], whole.at[pl.ds(at_p, piece)], z_peer[o])
        yield
        finish(4, whole.at[pl.ds(0, (quad - 1) * piece)])
        go(5, whole.at[pl.ds(at_e, eighth)], whole.at[pl.ds(at_e, eighth)], peer2)
        yield
        finish(5, whole.at[pl.ds(0, eighth)])
        go(6, whole.at[pl.ds(at_q, quarter)], whole.at[pl.ds(at_q, quarter)], peer1)
        yield
        finish(6, whole.at[pl.ds(0, quarter)])
        go(7, whole.at[pl.ds(at_h, half)], whole.at[pl.ds(at_h, half)], sibling)
        yield
        finish(7, whole.at[pl.ds(0, half)])
        yield

    chunks = [chunk(q) for q in range(len(plan))]

    def go_on(*which):
        for q in which:
            next(chunks[q])

    def go_on_all():
        go_on(*next(blocks))

    pre_a, slope_a, pre_b, slope_b, hbt, xt = r.pre_a, r.slope_a, r.pre_b, r.slope_b, r.hbt, r.xt
    we, wr, back = r.we, r.wr, r.back
    tiles = feat // 128
    group = SIDE // slots
    keep, moved, mask = t.keep, t.moved, t.mask
    grad_b, grad_a = r.grad_b, r.grad_a
    wait_bytes(wc, r.load_sem.at[15])
    g3 = r.g3

    def write_gb(at, grad):
        grad = jnp.where(mask, grad, 0.0)
        three(g3, at, pltpu.roll(grad, SIDE - 1, 0), grad, pltpu.roll(grad, 1, 0))

    def spatial_part(i):
        go_on_all()
        value = dot(xt[...], g3[(2 - i) * SIDE : (2 - i) * SIDE + rows, :])
        for j in range(3):
            r.part[1 + i][j * mid : (j + 1) * mid, :] = value[:, j * mid : (j + 1) * mid]
        go_on(2 + i)

    go_on_all()
    go_on_all()
    by_rows(grad_b, lambda here: dot(gpc[here, :], we[...], NT))
    back_sums(4, r.table_b, inv_b, grad_b, slope_b, pre_b)
    t.near_send(4)
    for e in range(2):
        go_on_all()
        for q in range(2 * e, 2 * e + 2):
            lanes = slice(q * 256, (q + 1) * 256)
            r.part[0][e * mid : (e + 1) * mid, q % 2 * 256 : (q % 2 + 1) * 256] = dot(hbt[...], gpc[:, lanes])
        go_on(e)
    t.sums_near(4)
    go_on_all()
    back_apply(4, r.table_b, r.gb, inv_b, grad_b, pre_b, write_gb)
    spatial_part(0)
    go_on_all()
    by_rows(
        grad_a, lambda here: sum(dot(g3[moved_rows(here, (2 - i) * SIDE), :], wc[i], NT) for i in range(3))
    )
    back_sums(5, r.table_a, inv_a, grad_a, slope_a, pre_a)
    t.near_send(5)
    spatial_part(1)
    t.sums_near(5)
    spatial_part(2)
    go_on_all()
    gpa = r.gpa

    def write_ga(at, grad):
        gpa[pl.ds(at, SIDE), :] = grad.astype(BF16)

    back_apply(5, r.table_a, r.ga, inv_a, grad_a, pre_a, write_ga)
    for q in range(4):
        go_on_all()
        r.part[4][q * 256 : (q + 1) * 256, :] = dot(r.ft[q * 256 : (q + 1) * 256, :], gpa[...])
        go_on(5 + q)

    go_on_all()
    by_rows(back, lambda here: dot(gpa[here, :], wr[...], NT))
    gf = r.gf

    def blend(y, carry):
        for p in range(tiles // group):
            values = []
            for q in range(group):
                lanes = slice((p * group + q) * 128, (p * group + q + 1) * 128)
                terms = [
                    slope_c[pl.ds(block(k, y), SIDE), lanes] * coef[k : k + 1, lanes]
                    + back[pl.ds(block(k, y), SIDE), lanes]
                    for k in range(live)
                ]
                values.append(terms[0] * keep[0])
                for m in range(1, live):
                    values.append(terms[m] * keep[m] + terms[m - 1] * moved[m - 1])
                values.append(terms[live - 1] * moved[live - 1])
            value = jnp.swapaxes(jnp.stack(values), 0, 1)
            gf[pl.ds(y * width, width), p * SIDE : (p + 1) * SIDE, :] = value[0:width].astype(BF16)
        return carry

    for q in range(height // 2):
        go_on_all()
        for y in range(2):
            blend(2 * q + y, 0)
    t.all_sent(*range(7))
    for h in range(2):
        wait_bytes(r.pool[h].at[pl.ds(1, len(t.clip_peers))], r.pool_s.at[h])
    go_on_all()
    for each in chunks:
        for _ in each:
            pass

    for q, (name, _, count) in enumerate(plan):
        part = r.part[name]
        piece = part.shape[0] // count // (8 * quad)
        for m, pieces in enumerate((8 * quad - 1, 8 * quad - 1, far - 1)):
            if pieces:
                wait_bytes(part.at[pl.ds(0, pieces * piece)], chunk_s.at[q, m])


def store(gf, vectors_c, vectors, expand, s0, s1, s2, reduce, frames_out, reduce_out, spatial_out, expand_out, *rest):
    ga, ba, gb, bb, gc, bc, *scratch, sem = rest
    vectors_of = (
        (bc, vectors_c, 0), (gc, vectors_c, 8), (bb, vectors, 0), (gb, vectors, 2), (ba, vectors, 8), (ga, vectors, 10)
    )
    pltpu.make_async_copy(gf, frames_out, sem.at[0]).start()
    pltpu.make_async_copy(reduce, reduce_out, sem.at[1]).start()
    depth, width = expand_out.shape
    for q in range(2):
        pltpu.make_async_copy(
            expand.at[pl.ds(q * depth, depth)], expand_out.at[:, pl.ds(q * width // 2, width // 2)], sem.at[2]
        ).start()
    for i, part in enumerate((s0, s1, s2)):
        for j in range(3):
            pltpu.make_async_copy(part.at[pl.ds(j * depth, depth)], spatial_out.at[i, j], sem.at[3 + i]).start()
    for number, (ref, source, first) in enumerate(vectors_of):
        for q in range(ref.shape[0] // 128):
            scratch[number][q * 128 : (q + 1) * 128] = source[first + q : first + q + 1, :].reshape(128)
        pltpu.make_async_copy(scratch[number], ref, sem.at[6 + number]).start()
    wait_bytes(gf, sem.at[0])
    wait_bytes(reduce, sem.at[1])
    wait_bytes(expand, sem.at[2])
    for i, part in enumerate((s0, s1, s2)):
        wait_bytes(part, sem.at[3 + i])
    for number in range(6):
        wait_bytes(scratch[number], sem.at[6 + number])


def solution(mesh):
    n = mesh.shape["clip"]

    def shards(*args):
        slots, height, width, feat = args[0].shape
        mid = args[1].shape[1]
        rows = (slots - 1) * ROWS
        outer = n // 8
        quad = min(4, outer)
        far = outer // quad
        cfg = (n, slots, height, width, feat, mid)
        flat_shape = (height * width, slots * feat // 128, 128)
        hbm = pl.BlockSpec(memory_space=pltpu.HBM)
        vmem = pl.BlockSpec(memory_space=pltpu.VMEM)
        dma = pltpu.SemaphoreType.DMA
        depths = list(enumerate((5, 4, 8, 16, 4, 4, 8)))
        sizes = [(2 * mid, feat // 2)] + [(3 * mid, mid)] * 3 + [(feat, mid)]

        tiled = args[0].transpose(1, 2, 0, 3).reshape(height, width, slots, feat // 128, 128)
        tiled = tiled.transpose(0, 1, 3, 2, 4).reshape(flat_shape)
        given = [pltpu.with_memory_space_constraint(part, pltpu.HBM) for part in (tiled, *args[1:])]

        vm = pltpu.VMEM
        narrow, broad, square = vm((mid,), F32), vm((feat,), F32), vm((rows, mid), F32)
        ints = pltpu.SMEM((slots,), jnp.int32)
        plan = [(mid, feat // 2)] * 2 + [(3 * mid, mid)] * 3 + [(feat // 4, mid)] * 4
        outs = dict(
            gf=vm(flat_shape, BF16), vectors_c=vm((16, 128), F32), vectors=vm((16, 128), F32),
            **{name: vm(size, F32) for name, size in zip(dict(e=0, s0=0, s1=0, s2=0, r=0), sizes)},
        )
        scratch = dict(
            f4=vm((flat_shape[0] + SIDE - width, *flat_shape[1:]), BF16),
            fp=vm((rows, feat), BF16), ft=vm((feat, rows), BF16),
            wr=vm((feat, mid), BF16), ws=vm((3, 3, mid, mid), BF16), wc=vm((3, mid, 3 * mid), BF16), we=vm((mid, feat), BF16),
            valid=ints, clip=ints, segment=ints, share=pltpu.SMEM(args[13].shape, F32),
            ga=narrow, ba=narrow, gb=narrow, bb=narrow, gc=broad, bc=broad, loss=broad,
            xp=vm((rows + 2 * SIDE, 3 * mid), BF16), xt=vm((mid, rows), BF16),
            hb=vm((rows, mid), BF16), hbt=vm((mid, rows), BF16),
            pre_a=square, slope_a=square, pre_b=square, slope_b=square, grad_a=square, grad_b=square,
            pre_c=vm((rows, feat), F32), slope_c=vm((rows, feat), F32), back=vm((rows, feat), F32),
            gpc=vm((rows, feat), BF16), g3=vm((rows + 2 * SIDE, 3 * mid), BF16), gpa=vm((rows, mid), BF16),
            table_a=vm((8, mid), F32), table_b=vm((8, mid), F32),
            table_c=vm((8, feat), F32), coef=vm((8, feat), F32), dense=vm((8, 128), F32), inv_c=vm((8, 128), F32),
            pool=[vm((6, 16, 128), F32)] * 2, clip_mean=vm((3, 8, 128), F32), slope_sum=vm((3, 8, 128), F32), slope_hat=vm((3, 8, 128), F32),
            near=[vm((n if n <= 32 and at not in (2, 3, 6) else 8, deep, 128), F32) for at, deep in depths],
            wide=[vm((outer, deep, 128), F32) for at, deep in depths],
            plane=vm((outer, 8, 128), F32),
            part=[vm(size, F32) for size in sizes],
            rb0=[vm((size // 2, lanes), F32) for size, lanes in plan],
            rb1=[vm((size // 4, lanes), F32) for size, lanes in plan],
            rb2=[vm((size // 8, lanes), F32) for size, lanes in plan],
            rb3=[vm(((quad - 1) * size // (8 * quad), lanes), F32) for size, lanes in plan],
            rb4=[vm((far, size // (8 * quad), lanes), F32) for size, lanes in plan if far > 1],
            load_sem=dma((16,)), near_s=dma((7,)), near_r=dma((7,)), wide_s=dma((7,)), wide_r=dma((7,)),
            pool_s=dma((2,)), pool_r=dma((2,)), chunk_s=dma((9, 3)), chunk_r=dma((9, 9)),
        )
        names = (*arg_names(), *outs, *scratch)

        def kernel(*refs):
            t = Step(cfg, SimpleNamespace(**dict(zip(names, refs, strict=True))))
            prologue(t)
            backward(t, *forward(t))

        results = pl.pallas_call(
            kernel,
            out_shape=list(outs.values()),
            in_specs=[hbm] * len(given),
            out_specs=[vmem] * len(outs),
            scratch_shapes=list(scratch.values()),
            compiler_params=pltpu.CompilerParams(
                collective_id=0, has_side_effects=True, vmem_limit_bytes=50 * 1024 * 1024
            ),
        )(*given)
        vector = jax.ShapeDtypeStruct((mid,), F32)
        wide_vector = jax.ShapeDtypeStruct((feat,), F32)
        flat_grad, *rest = pl.pallas_call(
            store,
            out_shape=[
                jax.ShapeDtypeStruct(flat_shape, BF16),
                jax.ShapeDtypeStruct((feat, mid), F32),
                jax.ShapeDtypeStruct((3, 3, mid, mid), F32),
                jax.ShapeDtypeStruct((mid, feat), F32),
                vector, vector, vector, vector, wide_vector, wide_vector,
            ],
            in_specs=[vmem] * 8,
            out_specs=[hbm] * 10,
            scratch_shapes=[*(vm((c,), F32) for c in (feat, feat, mid, mid, mid, mid)), dma((12,))],
            compiler_params=pltpu.CompilerParams(vmem_limit_bytes=8 * 1024 * 1024),
        )(*(pltpu.with_memory_space_constraint(part, pltpu.VMEM) for part in results))
        grad_frames = flat_grad.reshape(height, width, feat // 128, slots, 128).transpose(0, 1, 3, 2, 4)
        return grad_frames.reshape(height, width, slots, feat).transpose(2, 0, 1, 3), *rest

    split = P("clip")
    in_specs = (split,) + (P(),) * 9 + (split,) * 3 + (P(), P())
    out_specs = (split,) + (P(),) * 9
    return jax.shard_map(shards, mesh=mesh, in_specs=in_specs, out_specs=out_specs, check_vma=False)


def arg_names():
    return dict(
        frames=0, w_reduce=0, w_spatial=0, w_expand=0, gain_a=0, bias_a=0, gain_b=0, bias_b=0, gain_c=0, bias_c=0,
        clip_ids=0, segment_ids=0, slot_valid=0, segment_weight=0, loss_weight=0,
    )
```

```python
import functools
from types import SimpleNamespace

import jax
import jax.numpy as jnp
from jax import lax
from jax.experimental import pallas as pl
from jax.experimental.pallas import tpu as pltpu
from jax.sharding import PartitionSpec as P

MESH = pl.DeviceIdType.MESH
EPS = 1e-05
F32 = jnp.float32
BF16 = jnp.bfloat16
SIDE = 16
ROWS = SIDE * SIDE
NN = (((1,), (0,)), ((), ()))
NT = (((1,), (1,)), ((), ()))

ORDER = (
    (),
    (),
    (),
    (),
    (),
    (),
    (0, 1,),
    (2, 0,),
    (1,),
    (2, 0, 1, 3,),
    (2, 4,),
    (),
    (),
    (0,),
    (1, 3, 5, 2, 4,),
    (6, 3, 8,),
    (1, 0, 5, 7, 4, 8, 1, 3, 6, 7, 8, 2, 0,),
    (4, 7, 3,),
    (6, 2, 8, 1, 5, 0, 4, 7, 3, 6, 8, 5, 7, 1, 6, 4,),
    (5, 6, 0, 3,),
    (7,),
    (8, 2, 4, 5, 7, 8, 6, 3, 5,),
    (7, 8, 6, 5, 4, 2,),
)


def dot(a, b, dims=NN):
    return lax.dot_general(a, b, dims, preferred_element_type=F32)


def wait_bytes(ref, sem):
    pltpu.make_async_copy(ref, ref, sem).wait()


def by_rows(ref, value):
    for k in range(ref.shape[0] // 256):
        ref[k * 256 : (k + 1) * 256, :] = value(slice(k * 256, (k + 1) * 256))


def moved_rows(here, at):
    return slice(here.start + at, here.stop + at)


def block(k, y):
    return pl.multiple_of(k * ROWS + y * SIDE, SIDE)


def to_dense(ref, at, value, first):
    for q in range(value.shape[1] // 128):
        ref[at, pl.ds(first + q, 1), :] = value[:, q * 128 : (q + 1) * 128]


def row_form(ref, row, source, first, count, lane=0):
    for q in range(count):
        ref[row : row + 1, (lane + q) * 128 : (lane + q + 1) * 128] = source[first + q : first + q + 1, :]


def three(ref, at, left, middle, right):
    here, wide = pl.ds(at + SIDE, SIDE), middle.shape[1]
    ref[here, 0:wide] = left.astype(BF16)
    ref[here, wide : 2 * wide] = middle.astype(BF16)
    ref[here, 2 * wide : 3 * wide] = right.astype(BF16)


def dense_of(ref1, scratch):
    count = ref1.shape[0] // 128
    for q in range(count):
        scratch[q : q + 1, :] = ref1[q * 128 : (q + 1) * 128].reshape(1, 128)
    return scratch[0:count, :]


class Step:
    def __init__(self, cfg, r):
        self.r, self.sizes = r, cfg
        self.n, self.slots, self.height, self.width, self.feat, self.mid = cfg
        self.live = self.slots - 1
        self.rows = self.live * ROWS
        self.area = self.height * self.width
        self.inner = 8
        self.outer = self.n // 8
        self.quad = min(4, self.outer)
        self.far = self.outer // self.quad
        self.loads = {}
        self.mask = lax.broadcasted_iota(jnp.int32, (SIDE, 256), 0) < self.width

    def load(self, **pairs):
        for name, (src, dst) in pairs.items():
            copy = pltpu.make_async_copy(src, dst, self.r.load_sem.at[len(self.loads)])
            copy.start()
            self.loads[name] = copy

    def loaded(self, **names):
        for name in names:
            self.loads[name].wait()

    def fold(self, value):
        return jnp.sum(jnp.where(self.mask, value, 0.0), axis=0, keepdims=True)

    def slot_facts(self):
        r, live = self.r, self.live
        alive, later = 1, []
        for k in range(live):
            alive = alive * r.valid[k]
            later.append(1 - alive)
        self.keep = [(1 - q).astype(F32) for q in later]
        self.moved = [q.astype(F32) for q in later]
        self.later = later
        self.v = [self.kept(r.valid, k) for k in range(live)]
        self.n_own = (self.v[0] + self.v[1] + self.v[2]) * float(self.area)

    def kept(self, values, k):
        return (values[k] + self.later[k] * (values[k + 1] - values[k])).astype(F32)

    def places(self):
        n = self.n
        self.me = me = lax.axis_index("clip")
        self.low, self.high = low, high = me % self.inner, me // self.inner
        self.direct = n <= 32
        self.peers = flips(me, n)
        self.low_peers = flips(me, self.inner)
        self.high_peers = flips(me, self.outer, self.inner)
        self.clip_peers = [(me + o) % n for o in (n // 2 - 1, n // 2 + 1, n // 2, n - 1, 1)]

    def greet(self):
        self.greeted = self.peers if self.direct else self.low_peers + self.high_peers + self.clip_peers
        self.barrier = pltpu.get_barrier_semaphore()
        for device in self.greeted:
            pl.semaphore_signal(self.barrier, inc=1, device_id=(device,), device_id_type=MESH)

    def all_here(self):
        pl.semaphore_wait(self.barrier, len(self.greeted))

    def send(self, src, dst, ssem, rsem, device):
        pltpu.make_async_remote_copy(
            src_ref=src, dst_ref=dst, send_sem=ssem, recv_sem=rsem, device_id=(device,), device_id_type=MESH
        ).start()

    def one_stage(self, at):
        return self.direct and at not in (2, 3, 6)

    def near_at(self, at):
        return self.me if self.one_stage(at) else self.low

    def near_send(self, at):
        buf, mine = self.r.near[at], self.near_at(at)
        for device in self.peers if self.one_stage(at) else self.low_peers:
            self.send(buf.at[mine], buf.at[mine], self.r.near_s.at[at], self.r.near_r.at[at], device)

    def near_wait(self, at, sems):
        buf = self.r.near[at]
        wait_bytes(buf.at[pl.ds(0, buf.shape[0] - 1)], sems.at[at])

    def wide_send(self, at):
        buf = self.r.wide[at]
        for device in self.high_peers:
            self.send(buf.at[self.high], buf.at[self.high], self.r.wide_s.at[at], self.r.wide_r.at[at], device)

    def wide_wait(self, at, sems):
        wait_bytes(self.r.wide[at].at[pl.ds(0, self.outer - 1)], sems.at[at])

    def all_sent(self, *rounds):
        for at in rounds:
            self.near_wait(at, self.r.near_s)
            if not self.one_stage(at):
                self.wide_wait(at, self.r.wide_s)

    def near_count(self, q):
        return self.r.near[0][(self.me - self.low + q) if self.direct else q, 4:5, :]

    def wide_count(self, q):
        return self.r.plane[q, 0:1, :] if self.direct else self.r.wide[0][q, 4:5, :]

    def stats_near(self, at, count):
        if self.one_stage(at):
            return
        self.near_wait(at, self.r.near_r)
        n_all, s_all, _, spread = combine(self.r.near[at], self.near_count, self.inner, count)
        buf = self.r.wide[at]
        buf[self.high, 0:count, :] = s_all
        buf[self.high, count : 2 * count, :] = spread
        if at == 0:
            buf[self.high, 4:5, :] = n_all
        self.wide_send(at)

    def stats_wide(self, at, count, table, first=0):
        r = self.r
        if self.one_stage(at):
            self.near_wait(at, r.near_r)
            counts = r.near[0]
            n_all, _, mean, spread = combine(r.near[at], lambda q: counts[q, 4:5, :], self.n, count)
        else:
            self.wide_wait(at, r.wide_r)
            n_all, _, mean, spread = combine(r.wide[at], self.wide_count, self.outer, count)
        if at == 0 and self.direct:
            counts = r.near[0]
            for q in range(self.outer):
                r.plane[q, 0:1, :] = sum(counts[q * self.inner + m, 4:5, :] for m in range(self.inner))
        inverse = lax.rsqrt(spread / n_all + EPS)
        r.dense[0:count, :] = mean
        row_form(table, 0, r.dense, 0, count, first)
        r.dense[0:count, :] = inverse
        row_form(table, 1, r.dense, 0, count, first)
        return n_all, inverse

    def sums_near(self, at):
        if not self.one_stage(at):
            self.near_wait(at, self.r.near_r)
            self.r.wide[at][self.high] = total(self.r.near[at])
            self.wide_send(at)

    def sums_wide(self, at):
        if self.one_stage(at):
            self.near_wait(at, self.r.near_r)
            return total(self.r.near[at])
        self.wide_wait(at, self.r.wide_r)
        return total(self.r.wide[at])

    def local_stats(self, buf, at, ref, first=0, channels=None):
        channels = channels or ref.shape[1]
        count = channels // 128
        for c in range(channels // 256):
            lanes = slice(first + c * 256, first + (c + 1) * 256)

            def gather(term):
                acc = jnp.zeros((SIDE, 256), F32)
                for k in range(self.live):
                    part = lax.fori_loop(
                        0, self.height, lambda y, a: a + term(ref[pl.ds(block(k, y), SIDE), lanes]),
                        jnp.zeros((SIDE, 256), F32), unroll=self.height,
                    )
                    acc = acc + part * self.v[k]
                return self.fold(acc)

            s_own = gather(lambda x: x)
            mean = s_own / jnp.maximum(self.n_own, 1.0)
            to_dense(buf, at, s_own, 2 * c)
            to_dense(buf, at, gather(lambda x: (x - mean) * (x - mean)), count + 2 * c)

    def norm_silu(self, ref, slope_ref, table, gain, bias, write):
        centre, scale = table[0:1, :], table[1:2, :] * gain[...].reshape(1, self.mid)
        b = bias[...].reshape(1, self.mid)
        for k in range(self.live):
            def step(y, carry):
                at = block(k, y)
                u = (ref[pl.ds(at, SIDE), :] - centre) * scale + b
                s = 0.5 * jnp.tanh(0.5 * u) + 0.5
                h = u * s
                slope_ref[pl.ds(at, SIDE), :] = jnp.where(self.mask, s + (h - h * s), 0.0)
                write(at, jnp.where(self.mask, h, 0.0))
                return carry

            lax.fori_loop(0, self.height, step, 0, unroll=self.height)


def flips(index, count, stride=1):
    steps, at = [], 1
    while at < count:
        steps.append(at * stride * (1 - 2 * ((index // (at * stride)) % 2)))
        at *= 2
    return [sum((d for b, d in enumerate(steps) if o >> b & 1), index) for o in reversed(range(1, count))]


def combine(buf, counts, group, count):
    n_part = [counts(q) for q in range(group)]
    s_part = [buf[q, 0:count, :] for q in range(group)]
    n_all = sum(n_part[1:], n_part[0])
    s_all = sum(s_part[1:], s_part[0])
    mean = s_all / jnp.maximum(n_all, 1.0)
    spread = jnp.zeros((count, 128), F32)
    for q in range(group):
        gap = s_part[q] / jnp.maximum(n_part[q], 1.0) - mean
        spread = spread + (buf[q, count : 2 * count, :] + n_part[q] * gap * gap)
    return n_all, s_all, mean, spread


def total(buf):
    out = buf[0]
    for q in range(1, buf.shape[0]):
        out = out + buf[q]
    return out


def clear(*refs):
    for ref in refs:
        ref[...] = jnp.zeros(ref.shape, ref.dtype)


def prologue(t):
    r, slots, live, width, feat = t.r, t.slots, t.live, t.width, t.feat
    early = (t.height // 2 + 1) * t.width
    t.places()
    t.greet()
    t.load(
        frames=(r.frames.at[pl.ds(0, early)], r.f4.at[pl.ds(0, early)]), valid=(r.slot_valid, r.valid), reduce=(r.w_reduce, r.wr),
        rest=(r.frames.at[pl.ds(early, t.area - early)], r.f4.at[pl.ds(early, t.area - early)]),
    )
    r.f4[t.area :] = jnp.zeros((r.f4.shape[0] - t.area, *r.f4.shape[1:]), BF16)
    clear(r.fp)
    t.loaded(valid=0)
    t.slot_facts()
    t.loaded(frames=0)
    t.load(
        clip=(r.clip_ids, r.clip), segment=(r.segment_ids, r.segment),
        share=(r.segment_weight, r.share), spatial=(r.w_spatial, r.ws), expand=(r.w_expand, r.we),
        ga=(r.gain_a, r.ga), ba=(r.bias_a, r.ba), gb=(r.gain_b, r.gb), bb=(r.bias_b, r.bb),
        gc=(r.gain_c, r.gc), bc=(r.bias_c, r.bc), loss=(r.loss_weight, r.loss),
    )
    for i in range(3):
        for j in range(3):
            pltpu.make_async_copy(
                r.w_spatial.at[i, j], r.wc.at[i, :, pl.ds(j * t.mid, t.mid)], r.load_sem.at[16]
            ).start()
    fp, f4 = r.fp, r.f4
    tiles = feat // 128
    group = SIDE // slots
    short = lax.broadcasted_iota(jnp.int32, (SIDE, 128), 0) < width

    def regroup(y, carry):
        for p in range(tiles // group):
            value = f4[pl.ds(y * width, SIDE), p * SIDE : (p + 1) * SIDE, :].astype(F32)
            value = jnp.swapaxes(value, 0, 1)
            for q in range(group):
                for k in range(live):
                    row = value[q * slots + k] * t.keep[k] + value[q * slots + k + 1] * t.moved[k]
                    lanes = slice((p * group + q) * 128, (p * group + q + 1) * 128)
                    fp[pl.ds(block(k, y), SIDE), lanes] = jnp.where(short, row, 0.0).astype(BF16)
        return carry

    lax.fori_loop(0, t.height // 2, regroup, 0)
    t.loaded(rest=0)
    lax.fori_loop(t.height // 2, t.height, regroup, 0)
    t.loaded(reduce=0)
    by_rows(r.pre_a, lambda here: dot(fp[here, :], r.wr[...]))
    t.local_stats(r.near[0], t.near_at(0), r.pre_a)
    r.near[0][t.near_at(0), 4:5, :] = jnp.full((1, 128), t.n_own, F32)


def forward(t):
    r, live, mid, feat, rows, area, height = t.r, t.live, t.mid, t.feat, t.rows, t.area, t.height

    def turn(q):
        lanes = slice(q * feat // 4, (q + 1) * feat // 4)
        r.ft[lanes, :] = r.fp[:, lanes].T

    t.all_here()
    t.near_send(0)
    turn(0)
    t.stats_near(0, mid // 128)
    clear(r.xp, r.hb, r.g3, r.gpc, r.gpa)
    t.loaded(clip=0, segment=0, share=0, ga=0, ba=0, gb=0, bb=0, gc=0, bc=0, loss=0, spatial=0, expand=0)
    key = [t.kept(r.clip, k) for k in range(live)]
    weight = []
    for k in range(live):
        at = t.kept(r.segment, k)
        w0, w1, w2 = (r.share[q] for q in range(3))
        weight.append(
            t.v[k] * (w0 * ((1.0 - at) * (2.0 - at) * 0.5) + w1 * (at * (2.0 - at)) + w2 * (at * (at - 1.0) * 0.5))
        )
    n_all, inv_a = t.stats_wide(0, mid // 128, r.table_a)

    xp, hb = r.xp, r.hb

    def write_a(at, h):
        three(xp, at, pltpu.roll(h, 1, 0), h, pltpu.roll(h, SIDE - 1, 0))

    t.norm_silu(r.pre_a, r.slope_a, r.table_a, r.ga, r.ba, write_a)

    by_rows(
        r.pre_b,
        lambda here: sum(dot(xp[moved_rows(here, i * SIDE), :], r.ws[i].reshape(3 * mid, mid)) for i in range(3)),
    )
    t.local_stats(r.near[1], t.near_at(1), r.pre_b)
    t.near_send(1)
    r.xt[...] = xp[SIDE : SIDE + rows, mid : 2 * mid].T
    t.stats_near(1, mid // 128)
    _, inv_b = t.stats_wide(1, mid // 128, r.table_b)

    def write_b(at, h):
        hb[pl.ds(at, SIDE), :] = h.astype(BF16)

    t.norm_silu(r.pre_b, r.slope_b, r.table_b, r.gb, r.bb, write_b)

    pre_c, slope_c, fp, table_c = r.pre_c, r.slope_c, r.fp, r.table_c
    half = feat // 2
    rounds = (2, 6)
    for h, at in enumerate(rounds):
        lanes = slice(h * half, (h + 1) * half)
        for k in range(live):
            here = slice(k * ROWS, (k + 1) * ROWS)
            pre_c[here, lanes] = dot(hb[here, :], r.we[:, lanes])
        t.local_stats(r.near[at], t.near_at(at), pre_c, h * half, half)
        t.near_send(at)
    r.hbt[...] = hb[...].T
    for at in rounds:
        t.stats_near(at, half // 128)
    turn(1)

    pool, slope_sum, slope_hat = r.pool, r.slope_sum, r.slope_hat
    for c in range(feat // 256):
        if c * 256 % half == 0:
            h = c * 256 // half
            _, inv_half = t.stats_wide(rounds[h], half // 128, table_c, h * half // 128)
            r.inv_c[h * half // 128 : (h + 1) * half // 128, :] = inv_half
        lanes = slice(c * 256, (c + 1) * 256)
        centre, inverse = table_c[0:1, lanes], table_c[1:2, lanes]
        g = r.gc[lanes].reshape(1, 256)
        b = r.bc[lanes].reshape(1, 256)
        for k in range(live):
            def step(y, carry):
                a0, a1, a2 = carry
                at = block(k, y)
                hat = (pre_c[pl.ds(at, SIDE), lanes] - centre) * inverse
                u = hat * g + b + fp[pl.ds(at, SIDE), lanes].astype(F32)
                s = 0.5 * jnp.tanh(0.5 * u) + 0.5
                h = u * s
                slope = s + (h - h * s)
                slope_c[pl.ds(at, SIDE), lanes] = slope
                return a0 + h, a1 + slope, a2 + slope * hat

            zero = jnp.zeros((SIDE, 256), F32)
            a0, a1, a2 = lax.fori_loop(0, height, step, (zero, zero, zero), unroll=height)
            p_row = (t.fold(a0) * (1.0 / area)).astype(BF16).astype(F32)
            to_dense(pool, 0, p_row, 8 * k + 2 * c)
            to_dense(slope_sum, k, t.fold(a1), 2 * c)
            to_dense(slope_hat, k, t.fold(a2), 2 * c)
    for k in range(live):
        pool[0, 24 + k : 25 + k, :] = jnp.full((1, 128), key[k], F32)
        pool[0, 28 + k : 29 + k, :] = jnp.full((1, 128), weight[k], F32)
    for q, device in enumerate(t.clip_peers):
        t.send(pool.at[0], pool.at[q + 1], r.pool_s.at[0], r.pool_r.at[0], device)
    turn(2)
    wait_bytes(pool.at[pl.ds(1, len(t.clip_peers))], r.pool_r.at[0])

    lw = dense_of(r.loss, r.dense)
    grads = []
    for k in range(live):
        my_key = jnp.full((1, 128), key[k], F32)
        my_weight = jnp.full((1, 128), weight[k], F32)
        mean = jnp.zeros((8, 128), F32)
        den = jnp.zeros((1, 128), F32)
        for q in range(len(t.clip_peers) + 1):
            for m in range(live):
                match = jnp.where(pool[q, 24 + m : 25 + m, :] == my_key, pool[q, 28 + m : 29 + m, :], 0.0)
                den = den + match
                mean = mean + match * pool[q, 8 * m : 8 * m + 8, :]
        den = jnp.where(den == 0.0, 1.0, den)
        mean = mean / den
        power = jnp.sum(jnp.sum(mean * mean, axis=0, keepdims=True), axis=1, keepdims=True)
        along = jnp.sum(jnp.sum(mean * lw, axis=0, keepdims=True), axis=1, keepdims=True)
        scale = lax.rsqrt(power * (1.0 / feat) + EPS)
        mean_grad = scale * (lw - (mean * scale) * (scale * along * (1.0 / feat)))
        grads.append((my_weight / den) * mean_grad * (1.0 / area))

    inv_c = r.inv_c[...]
    near3 = r.near[3]
    shift = jnp.zeros((8, 128), F32)
    gain = jnp.zeros((8, 128), F32)
    for k in range(live):
        shift = shift + grads[k] * slope_sum[k]
        gain = gain + grads[k] * slope_hat[k]
    near3[t.near_at(3), 0:8, :] = shift
    near3[t.near_at(3), 8:16, :] = gain
    t.near_send(3)
    coef, dense = r.coef, r.dense
    scale_c = dense_of(r.gc, dense) * inv_c
    for k in range(live):
        dense[...] = grads[k]
        row_form(coef, k, dense, 0, feat // 128)
        dense[...] = grads[k] * scale_c
        row_form(coef, 3 + k, dense, 0, feat // 128)
    t.sums_near(3)
    turn(3)
    both = t.sums_wide(3)
    r.vectors_c[...] = both
    dense[...] = both[0:8] * scale_c / n_all
    row_form(coef, 6, dense, 0, feat // 128)
    dense[...] = both[8:16] * scale_c * inv_c / n_all
    row_form(coef, 7, dense, 0, feat // 128)
    return n_all, inv_a, inv_b


def backward(t, n_all, inv_a, inv_b):
    r, live, mid, feat, rows, height = t.r, t.live, t.mid, t.feat, t.rows, t.height
    slots, width, quad, far, v, wc = t.slots, t.width, t.quad, t.far, t.v, r.wc
    coef, pre_c, slope_c, out = r.coef, r.pre_c, r.slope_c, r.vectors
    me, send = t.me, t.send
    gpc = r.gpc
    for k in range(live):
        for c in range(feat // 256):
            lanes = slice(c * 256, (c + 1) * 256)
            centre = r.table_c[0:1, lanes]
            c0 = coef[3 + k : 4 + k, lanes]
            c1 = coef[6:7, lanes] * v[k]
            c2 = coef[7:8, lanes] * v[k]

            def step(y, carry):
                at = block(k, y)
                grad = slope_c[pl.ds(at, SIDE), lanes] * c0 - (c1 + (pre_c[pl.ds(at, SIDE), lanes] - centre) * c2)
                gpc[pl.ds(at, SIDE), lanes] = grad.astype(BF16)
                return carry

            lax.fori_loop(0, height, step, 0, unroll=height)

    def back_sums(at, table, inv, grad_ref, slope_ref, pre_ref):
        zero = jnp.zeros((SIDE, mid), F32)
        carry = (zero, zero)
        centre = table[0:1, :]
        for k in range(live):
            def step(y, c):
                here = pl.ds(block(k, y), SIDE)
                grad = grad_ref[here, :] * slope_ref[here, :]
                grad_ref[here, :] = grad
                return c[0] + grad, c[1] + grad * (pre_ref[here, :] - centre)

            carry = lax.fori_loop(0, height, step, carry, unroll=height)
        buf = r.near[at]
        to_dense(buf, t.near_at(at), jnp.sum(carry[0], axis=0, keepdims=True), 0)
        to_dense(buf, t.near_at(at), jnp.sum(carry[1], axis=0, keepdims=True) * table[1:2, :], 2)

    def back_apply(at, table, gain_ref, inv, grad_ref, pre_ref, write):
        both = t.sums_wide(at)
        out[8 * at - 32 : 8 * at - 28, :] = both[0:4]
        dense = r.dense
        scale = dense_of(gain_ref, dense) * inv
        dense[0:2, :] = scale
        dense[2:4, :] = both[0:2] * scale / n_all
        dense[4:6, :] = both[2:4] * scale * inv / n_all
        for q in range(3):
            row_form(table, 2 + q, dense, 2 * q, 2)
        centre = table[0:1, :]
        for k in range(live):
            c0, c1, c2 = table[2:3, :], table[3:4, :] * v[k], table[4:5, :] * v[k]

            def step(y, carry):
                at_row = block(k, y)
                here = pl.ds(at_row, SIDE)
                write(at_row, grad_ref[here, :] * c0 - (c1 + (pre_ref[here, :] - centre) * c2))
                return carry

            lax.fori_loop(0, height, step, 0, unroll=height)

    core, bit_x, bit_y, at_z = me % 2, (me // 2) % 2, (me // 4) % 2, (me // 8) % quad
    at_far = me // (8 * quad)
    bit1 = bit_x + core * (bit_y - bit_x)
    bit2 = bit_y + core * (bit_x - bit_y)
    sibling = me + 1 - 2 * core
    peer1 = me + (1 - 2 * bit1) * (2 + 2 * core)
    peer2 = me + (1 - 2 * bit2) * (4 - 2 * core)
    z_at = flips(at_z, quad)
    z_peer = [me + 8 * (q - at_z) for q in z_at]
    far_peer = [me + 8 * quad * ((at_far + o) % far - at_far) for o in range(1, far)]
    chunk_s, chunk_r = r.chunk_s, r.chunk_r
    blocks = iter(ORDER)
    plan = [(0, q, 2) for q in range(2)] + [(1 + q, 0, 1) for q in range(3)] + [(4, q, 4) for q in range(4)]

    def chunk(q):
        name, at, count = plan[q]
        size = r.part[name].shape[0] // count
        part = r.part[name].at[pl.ds(at * size, size)]
        whole = (r.e, r.s0, r.s1, r.s2, r.r)[name].at[pl.ds(at * size, size)]
        half, quarter, eighth, piece = size // 2, size // 4, size // 8, size // (8 * quad)
        m8 = lambda value: pl.multiple_of(value, 8)
        at_h = m8(core * half)
        at_q = m8(at_h + bit1 * quarter)
        at_e = m8(at_q + bit2 * eighth)
        at_p = m8(at_e + at_z * piece)

        def go(step, src, dst, device):
            send(src, dst, chunk_s.at[q, step // 4], chunk_r.at[q, step], device)

        def finish(step, ref):
            wait_bytes(ref, chunk_r.at[q, step])

        rb0, rb1, rb2, rb3 = r.rb0[q], r.rb1[q], r.rb2[q], r.rb3[q]
        go(0, part.at[pl.ds(m8((1 - core) * half), half)], rb0, sibling)
        yield
        finish(0, rb0)
        part[pl.ds(at_h, half), :] = part[pl.ds(at_h, half), :] + rb0[...]
        go(1, part.at[pl.ds(m8(at_h + (1 - bit1) * quarter), quarter)], rb1, peer1)
        yield
        finish(1, rb1)
        part[pl.ds(at_q, quarter), :] = part[pl.ds(at_q, quarter), :] + rb1[...]
        go(2, part.at[pl.ds(m8(at_q + (1 - bit2) * eighth), eighth)], rb2, peer2)
        yield
        finish(2, rb2)
        part[pl.ds(at_e, eighth), :] = part[pl.ds(at_e, eighth), :] + rb2[...]
        for o in range(quad - 1):
            go(3, part.at[pl.ds(m8(at_e + z_at[o] * piece), piece)], rb3.at[pl.ds(o * piece, piece)], z_peer[o])
        yield
        finish(3, rb3)
        own = part[pl.ds(at_p, piece), :]
        for o in range(quad - 1):
            own = own + rb3[o * piece : (o + 1) * piece, :]
        if far > 1:
            rb4 = r.rb4[q]
            rb4[at_far] = own
            for device in far_peer:
                go(8, rb4.at[at_far], rb4.at[at_far], device)
            yield
            finish(8, rb4.at[pl.ds(0, far - 1)])
            own = rb4[0]
            for o in range(1, far):
                own = own + rb4[o]
        whole[pl.ds(at_p, piece), :] = own
        for o in range(quad - 1):
            go(4, whole.at[pl.ds(at_p, piece)], whole.at[pl.ds(at_p, piece)], z_peer[o])
        yield
        finish(4, whole.at[pl.ds(0, (quad - 1) * piece)])
        go(5, whole.at[pl.ds(at_e, eighth)], whole.at[pl.ds(at_e, eighth)], peer2)
        yield
        finish(5, whole.at[pl.ds(0, eighth)])
        go(6, whole.at[pl.ds(at_q, quarter)], whole.at[pl.ds(at_q, quarter)], peer1)
        yield
        finish(6, whole.at[pl.ds(0, quarter)])
        go(7, whole.at[pl.ds(at_h, half)], whole.at[pl.ds(at_h, half)], sibling)
        yield
        finish(7, whole.at[pl.ds(0, half)])
        yield

    chunks = [chunk(q) for q in range(len(plan))]

    def go_on(*which):
        for q in which:
            next(chunks[q])

    def go_on_all():
        go_on(*next(blocks))

    pre_a, slope_a, pre_b, slope_b, hbt, xt = r.pre_a, r.slope_a, r.pre_b, r.slope_b, r.hbt, r.xt
    we, wr, back = r.we, r.wr, r.back
    tiles = feat // 128
    group = SIDE // slots
    keep, moved, mask = t.keep, t.moved, t.mask
    grad_b, grad_a = r.grad_b, r.grad_a
    wait_bytes(wc, r.load_sem.at[16])
    g3 = r.g3

    def write_gb(at, grad):
        grad = jnp.where(mask, grad, 0.0)
        three(g3, at, pltpu.roll(grad, SIDE - 1, 0), grad, pltpu.roll(grad, 1, 0))

    def spatial_part(i):
        go_on_all()
        value = dot(xt[...], g3[(2 - i) * SIDE : (2 - i) * SIDE + rows, :])
        for j in range(3):
            r.part[1 + i][j * mid : (j + 1) * mid, :] = value[:, j * mid : (j + 1) * mid]
        go_on(2 + i)

    go_on_all()
    go_on_all()
    by_rows(grad_b, lambda here: dot(gpc[here, :], we[...], NT))
    back_sums(4, r.table_b, inv_b, grad_b, slope_b, pre_b)
    t.near_send(4)
    for e in range(2):
        go_on_all()
        for q in range(2 * e, 2 * e + 2):
            lanes = slice(q * 256, (q + 1) * 256)
            r.part[0][e * mid : (e + 1) * mid, q % 2 * 256 : (q % 2 + 1) * 256] = dot(hbt[...], gpc[:, lanes])
        go_on(e)
    t.sums_near(4)
    go_on_all()
    back_apply(4, r.table_b, r.gb, inv_b, grad_b, pre_b, write_gb)
    spatial_part(0)
    go_on_all()
    by_rows(
        grad_a, lambda here: sum(dot(g3[moved_rows(here, (2 - i) * SIDE), :], wc[i], NT) for i in range(3))
    )
    back_sums(5, r.table_a, inv_a, grad_a, slope_a, pre_a)
    t.near_send(5)
    spatial_part(1)
    t.sums_near(5)
    spatial_part(2)
    go_on_all()
    gpa = r.gpa

    def write_ga(at, grad):
        gpa[pl.ds(at, SIDE), :] = grad.astype(BF16)

    back_apply(5, r.table_a, r.ga, inv_a, grad_a, pre_a, write_ga)
    for q in range(4):
        go_on_all()
        r.part[4][q * 256 : (q + 1) * 256, :] = dot(r.ft[q * 256 : (q + 1) * 256, :], gpa[...])
        go_on(5 + q)

    go_on_all()
    by_rows(back, lambda here: dot(gpa[here, :], wr[...], NT))
    gf = r.gf

    def blend(y, carry):
        for p in range(tiles // group):
            values = []
            for q in range(group):
                lanes = slice((p * group + q) * 128, (p * group + q + 1) * 128)
                terms = [
                    slope_c[pl.ds(block(k, y), SIDE), lanes] * coef[k : k + 1, lanes]
                    + back[pl.ds(block(k, y), SIDE), lanes]
                    for k in range(live)
                ]
                values.append(terms[0] * keep[0])
                for m in range(1, live):
                    values.append(terms[m] * keep[m] + terms[m - 1] * moved[m - 1])
                values.append(terms[live - 1] * moved[live - 1])
            value = jnp.swapaxes(jnp.stack(values), 0, 1)
            gf[pl.ds(y * width, width), p * SIDE : (p + 1) * SIDE, :] = value[0:width].astype(BF16)
        return carry

    for q in range(height // 2):
        go_on_all()
        for y in range(2):
            blend(2 * q + y, 0)
    go_on_all()
    for each in chunks:
        for _ in each:
            pass

    t.all_sent(*range(7))
    wait_bytes(r.pool.at[pl.ds(1, len(t.clip_peers))], r.pool_s.at[0])
    for q, (name, _, count) in enumerate(plan):
        part = r.part[name]
        piece = part.shape[0] // count // (8 * quad)
        for m, pieces in enumerate((8 * quad - 1, 8 * quad - 1, far - 1)):
            if pieces:
                wait_bytes(part.at[pl.ds(0, pieces * piece)], chunk_s.at[q, m])


def store(gf, vectors_c, vectors, expand, s0, s1, s2, reduce, frames_out, reduce_out, spatial_out, expand_out, *rest):
    ga, ba, gb, bb, gc, bc, *scratch, sem = rest
    vectors_of = (
        (bc, vectors_c, 0), (gc, vectors_c, 8), (bb, vectors, 0), (gb, vectors, 2), (ba, vectors, 8), (ga, vectors, 10)
    )
    pltpu.make_async_copy(gf, frames_out, sem.at[0]).start()
    pltpu.make_async_copy(reduce, reduce_out, sem.at[1]).start()
    depth, width = expand_out.shape
    for q in range(2):
        pltpu.make_async_copy(
            expand.at[pl.ds(q * depth, depth)], expand_out.at[:, pl.ds(q * width // 2, width // 2)], sem.at[2]
        ).start()
    for i, part in enumerate((s0, s1, s2)):
        for j in range(3):
            pltpu.make_async_copy(part.at[pl.ds(j * depth, depth)], spatial_out.at[i, j], sem.at[3 + i]).start()
    for number, (ref, source, first) in enumerate(vectors_of):
        for q in range(ref.shape[0] // 128):
            scratch[number][q * 128 : (q + 1) * 128] = source[first + q : first + q + 1, :].reshape(128)
        pltpu.make_async_copy(scratch[number], ref, sem.at[6 + number]).start()
    wait_bytes(gf, sem.at[0])
    wait_bytes(reduce, sem.at[1])
    wait_bytes(expand, sem.at[2])
    for i, part in enumerate((s0, s1, s2)):
        wait_bytes(part, sem.at[3 + i])
    for number in range(6):
        wait_bytes(scratch[number], sem.at[6 + number])


def solution(mesh):
    n = mesh.shape["clip"]

    def shards(*args):
        slots, height, width, feat = args[0].shape
        mid = args[1].shape[1]
        rows = (slots - 1) * ROWS
        outer = n // 8
        quad = min(4, outer)
        far = outer // quad
        cfg = (n, slots, height, width, feat, mid)
        flat_shape = (height * width, slots * feat // 128, 128)
        hbm = pl.BlockSpec(memory_space=pltpu.HBM)
        vmem = pl.BlockSpec(memory_space=pltpu.VMEM)
        dma = pltpu.SemaphoreType.DMA
        depths = list(enumerate((5, 4, 8, 16, 4, 4, 8)))
        sizes = [(2 * mid, feat // 2)] + [(3 * mid, mid)] * 3 + [(feat, mid)]

        tiled = args[0].transpose(1, 2, 0, 3).reshape(height, width, slots, feat // 128, 128)
        tiled = tiled.transpose(0, 1, 3, 2, 4).reshape(flat_shape)
        given = [pltpu.with_memory_space_constraint(part, pltpu.HBM) for part in (tiled, *args[1:])]

        vm = pltpu.VMEM
        narrow, broad, square = vm((mid,), F32), vm((feat,), F32), vm((rows, mid), F32)
        ints = pltpu.SMEM((slots,), jnp.int32)
        plan = [(mid, feat // 2)] * 2 + [(3 * mid, mid)] * 3 + [(feat // 4, mid)] * 4
        outs = dict(
            gf=vm(flat_shape, BF16), vectors_c=vm((16, 128), F32), vectors=vm((16, 128), F32),
            **{name: vm(size, F32) for name, size in zip(dict(e=0, s0=0, s1=0, s2=0, r=0), sizes)},
        )
        scratch = dict(
            f4=vm((flat_shape[0] + SIDE - width, *flat_shape[1:]), BF16),
            fp=vm((rows, feat), BF16), ft=vm((feat, rows), BF16),
            wr=vm((feat, mid), BF16), ws=vm((3, 3, mid, mid), BF16), wc=vm((3, mid, 3 * mid), BF16), we=vm((mid, feat), BF16),
            valid=ints, clip=ints, segment=ints, share=pltpu.SMEM(args[13].shape, F32),
            ga=narrow, ba=narrow, gb=narrow, bb=narrow, gc=broad, bc=broad, loss=broad,
            xp=vm((rows + 2 * SIDE, 3 * mid), BF16), xt=vm((mid, rows), BF16),
            hb=vm((rows, mid), BF16), hbt=vm((mid, rows), BF16),
            pre_a=square, slope_a=square, pre_b=square, slope_b=square, grad_a=square, grad_b=square,
            pre_c=vm((rows, feat), F32), slope_c=vm((rows, feat), F32), back=vm((rows, feat), F32),
            gpc=vm((rows, feat), BF16), g3=vm((rows + 2 * SIDE, 3 * mid), BF16), gpa=vm((rows, mid), BF16),
            table_a=vm((8, mid), F32), table_b=vm((8, mid), F32),
            table_c=vm((8, feat), F32), coef=vm((8, feat), F32), dense=vm((8, 128), F32), inv_c=vm((8, 128), F32),
            pool=vm((6, 32, 128), F32), slope_sum=vm((3, 8, 128), F32), slope_hat=vm((3, 8, 128), F32),
            near=[vm((n if n <= 32 and at not in (2, 3, 6) else 8, deep, 128), F32) for at, deep in depths],
            wide=[vm((outer, deep, 128), F32) for at, deep in depths],
            plane=vm((outer, 8, 128), F32),
            part=[vm(size, F32) for size in sizes],
            rb0=[vm((size // 2, lanes), F32) for size, lanes in plan],
            rb1=[vm((size // 4, lanes), F32) for size, lanes in plan],
            rb2=[vm((size // 8, lanes), F32) for size, lanes in plan],
            rb3=[vm(((quad - 1) * size // (8 * quad), lanes), F32) for size, lanes in plan],
            rb4=[vm((far, size // (8 * quad), lanes), F32) for size, lanes in plan if far > 1],
            load_sem=dma((17,)), near_s=dma((7,)), near_r=dma((7,)), wide_s=dma((7,)), wide_r=dma((7,)),
            pool_s=dma((1,)), pool_r=dma((1,)), chunk_s=dma((9, 3)), chunk_r=dma((9, 9)),
        )
        names = (*arg_names(), *outs, *scratch)

        def kernel(*refs):
            t = Step(cfg, SimpleNamespace(**dict(zip(names, refs, strict=True))))
            prologue(t)
            backward(t, *forward(t))

        results = pl.pallas_call(
            kernel,
            out_shape=list(outs.values()),
            in_specs=[hbm] * len(given),
            out_specs=[vmem] * len(outs),
            scratch_shapes=list(scratch.values()),
            compiler_params=pltpu.CompilerParams(
                collective_id=0, has_side_effects=True, vmem_limit_bytes=50 * 1024 * 1024
            ),
        )(*given)
        vector = jax.ShapeDtypeStruct((mid,), F32)
        wide_vector = jax.ShapeDtypeStruct((feat,), F32)
        flat_grad, *rest = pl.pallas_call(
            store,
            out_shape=[
                jax.ShapeDtypeStruct(flat_shape, BF16),
                jax.ShapeDtypeStruct((feat, mid), F32),
                jax.ShapeDtypeStruct((3, 3, mid, mid), F32),
                jax.ShapeDtypeStruct((mid, feat), F32),
                vector, vector, vector, vector, wide_vector, wide_vector,
            ],
            in_specs=[vmem] * 8,
            out_specs=[hbm] * 10,
            scratch_shapes=[*(vm((c,), F32) for c in (feat, feat, mid, mid, mid, mid)), dma((12,))],
            compiler_params=pltpu.CompilerParams(vmem_limit_bytes=8 * 1024 * 1024),
        )(*(pltpu.with_memory_space_constraint(part, pltpu.VMEM) for part in results))
        grad_frames = flat_grad.reshape(height, width, feat // 128, slots, 128).transpose(0, 1, 3, 2, 4)
        return grad_frames.reshape(height, width, slots, feat).transpose(2, 0, 1, 3), *rest

    split = P("clip")
    in_specs = (split,) + (P(),) * 9 + (split,) * 3 + (P(), P())
    out_specs = (split,) + (P(),) * 9
    return jax.shard_map(shards, mesh=mesh, in_specs=in_specs, out_specs=out_specs, check_vma=False)


def arg_names():
    return dict(
        frames=0, w_reduce=0, w_spatial=0, w_expand=0, gain_a=0, bias_a=0, gain_b=0, bias_b=0, gain_c=0, bias_c=0,
        clip_ids=0, segment_ids=0, slot_valid=0, segment_weight=0, loss_weight=0,
    )
```
